32 devices in a mesh: tile: 16 (over z, y, x), frame: 2 (over core).
Axes of the slice: x: 2, y: 2, z: 4, core: 2. Of those that a mesh axis runs over, the one named last changes fastest.
Arguments:
- latents: bfloat16 [64, 2, 104, 384], P('tile', 'frame'), may hold values from -80 to 80
- row_video: int32 [64], replicated, may hold values from 0 to 1, never falling along the last dimension, each value on 1 to 48 neighbouring positions
- video_cols: int32 [2], replicated, may hold values from 52 to 104, as said below
- first_gain: float32 [384], replicated, may hold values from 0.5 to 1.5
- first_shift: float32 [384], replicated, may hold values from -3 to 3
- conv_weight: bfloat16 [3, 3, 3, 384, 384], replicated, may hold values from -0.0625 to 0.0625
- conv_bias: float32 [384], replicated, may hold values from -3 to 3
- second_gain: float32 [384], replicated, may hold values from 0.5 to 1.5
- second_shift: float32 [384], replicated, may hold values from -3 to 3
- triple_weight: bfloat16 [384, 1152], replicated, may hold values from -0.55 to 0.55
- triple_bias: float32 [1152], replicated, may hold values from -3 to 3
- output_weight: bfloat16 [384, 384], replicated, may hold values from -0.3125 to 0.3125
- output_bias: float32 [384], replicated, may hold values from -3 to 3
- upsample_weight: bfloat16 [3, 3, 384, 192], replicated, may hold values from -0.109375 to 0.109375
- upsample_bias: float32 [192], replicated, may hold values from -3 to 3
Outputs:
- decoded: bfloat16 [128, 2, 208, 192], P('tile', 'frame')
The draws below stay inside these ranges and needn't reach their ends.
Inputs may be any that keep to these rules, and one draw needn't show every extreme that they name: `row_video`: video numbers never fall along the rows; every video has 1 to 48 rows. `video_cols`: one video has all 104 columns.
All inputs are finite; a program needn't handle non-finite values.
Results may differ from the reference program's by a relative error of at most 0.013.
The reference program's roundings to bfloat16 on the way count: a program that leaves them out, or rounds other values in their place, can miss the bound.
Values may be sent and summed in bfloat16 or wider, within the bound.
No kernel may reach another device: no remote copies, remote signals or barrier semaphores. Data moves between devices by JAX's collectives and lax.ppermute only.
A program may use at most 128 MiB of HBM per device.

```python
import math
import jax
import jax.numpy as jnp
import numpy as np
from jax import lax

CH = 384
CH_OUT = 192
GROUPS = 32
WIDTH = 104
ROWS_DEV = 4
ROWS = 64
FRAMES = 2
VIDEOS = 2
MOST_ROWS = 48
MIN_COLS = 52


def draw_latents(key, part):
    subkeys = jax.random.split(jax.random.fold_in(key, 11), 3)
    normal_part = jnp.clip(jax.random.normal(subkeys[0], (ROWS, FRAMES, WIDTH, CH), jnp.float32), -4.0, 4.0)
    cell_scale = jnp.exp(jax.random.uniform(subkeys[1], (ROWS, FRAMES, WIDTH, 1), jnp.float32, -1.15, 1.15))
    channel_scale = jnp.exp(jax.random.uniform(subkeys[2], (CH,), jnp.float32, -0.69, 0.69))
    height = jnp.arange(ROWS, dtype=jnp.float32) / (ROWS - 1) - 0.5
    rising = (3.0 ** height)[:, None, None, None]
    drawn = normal_part * cell_scale * channel_scale * rising
    return drawn.astype(jnp.bfloat16)


def draw_triple_weight(key, part):
    subkeys = jax.random.split(jax.random.fold_in(key, 23), 4)
    spread = CH ** (-0.5)
    query_part = 1.7 * spread * jnp.clip(jax.random.normal(subkeys[0], (CH, CH), jnp.float32), -4.0, 4.0)
    key_part = 1.7 * spread * jnp.clip(jax.random.normal(subkeys[1], (CH, CH), jnp.float32), -4.0, 4.0)
    value_part = spread * jnp.clip(jax.random.normal(subkeys[3], (CH, CH), jnp.float32), -4.0, 4.0)
    joined = jnp.concatenate([query_part, key_part, value_part], axis=1)
    return jnp.clip(joined, -0.546, 0.546).astype(jnp.bfloat16)


def draw_video_cols(key, part):
    subkeys = jax.random.split(jax.random.fold_in(key, 37), 2)
    columns = jax.random.randint(subkeys[0], (VIDEOS,), MIN_COLS, WIDTH + 1)
    chosen = jax.random.randint(subkeys[1], (), 0, VIDEOS)
    return jnp.where(jnp.arange(VIDEOS) == chosen, WIDTH, columns).astype(jnp.int32)


def split_up(amount, total, reach, slope):
    weights = [(1 << 20) // math.isqrt(rank ** slope) + 1 for rank in range(2, amount + 1)]
    spare, given = total - reach - (amount - 1), [1] * (amount - 1)
    while spare > 0:
        free = [i for i in range(amount - 1) if given[i] < reach]
        mass, budget = sum([weights[i] for i in free]), spare
        for i in free:
            addition = min(reach - given[i], max(1, budget * weights[i] // mass), spare)
            given[i] = given[i] + addition
            spare = spare - addition
    return np.array([reach] + given)


def uneven(own_key, number_of, total, reach, skew):
    if number_of == 2:
        one = jax.random.randint(own_key, (), max(1, total - reach), min(reach, total - 1) + 1)
        return jnp.stack([one, total - one])
    tallies = jnp.asarray(split_up(number_of, total, reach, skew), jnp.int32)
    couples = (number_of - 1) // 2
    giver, receiver = tallies[1:1 + 2 * couples:2], tallies[2:2 + 2 * couples:2]
    slack = jnp.minimum(giver - 1, reach - receiver)
    shifted = jax.random.randint(jax.random.fold_in(own_key, 1), (couples,), 0, 1 << 20) % (slack + 1)
    tallies = tallies.at[1:1 + 2 * couples:2].set(giver - shifted).at[2:2 + 2 * couples:2].set(receiver + shifted)
    return tallies[jax.random.permutation(jax.random.fold_in(own_key, 2), number_of)]


def centred(key, dims, scale, limit, held_as=jnp.bfloat16):
    values = scale * jax.random.normal(key, dims, jnp.float32)
    return jnp.clip(values, min=-limit, max=limit).astype(held_as)


def setup_inputs(seed: int = 0) -> dict:
    seeds = jax.random.split(jax.random.key(seed), 16)
    return {
        "latents": draw_latents(jax.random.fold_in(seeds[15], 71), 0),
        "row_video": jnp.searchsorted(jnp.cumsum(uneven(seeds[1], VIDEOS, ROWS, MOST_ROWS, 1)), jnp.arange(ROWS), side="right").astype(jnp.int32),
        "video_cols": draw_video_cols(jax.random.fold_in(seeds[15], 71), 0),
        "first_gain": jnp.clip(1.0 + 0.1 * jax.random.normal(seeds[3], (CH,), jnp.float32), 0.5, 1.5),
        "first_shift": centred(seeds[4], (CH,), 0.5, 3.0, jnp.float32),
        "conv_weight": centred(seeds[5], (3, 3, 3, CH, CH), (27 * CH) ** -0.5, 0.0625),
        "conv_bias": centred(seeds[6], (CH,), 0.5, 3.0, jnp.float32),
        "second_gain": jnp.clip(1.0 + 0.1 * jax.random.normal(seeds[7], (CH,), jnp.float32), 0.5, 1.5),
        "second_shift": centred(seeds[8], (CH,), 0.5, 3.0, jnp.float32),
        "triple_weight": draw_triple_weight(jax.random.fold_in(seeds[15], 71), 0),
        "triple_bias": centred(seeds[10], (3 * CH,), 0.5, 3.0, jnp.float32),
        "output_weight": centred(seeds[11], (CH, CH), CH ** -0.5, 0.3125),
        "output_bias": centred(seeds[12], (CH,), 0.5, 3.0, jnp.float32),
        "upsample_weight": centred(seeds[13], (3, 3, CH, CH_OUT), (9 * CH) ** -0.5, 0.109375),
        "upsample_bias": centred(seeds[14], (CH_OUT,), 0.5, 3.0, jnp.float32),
    }


EPSILON = 1e-05
MASKED = -1e+30
HIGHEST = lax.Precision.HIGHEST

def video_tables(row_video, video_cols):
    matches = row_video[:, None] == jnp.arange(VIDEOS, dtype=jnp.int32)[None, :]
    widths = lax.optimization_barrier(jnp.sum(jnp.where(matches, video_cols[None, :], 0), axis=1))
    return (matches.astype(jnp.float32), widths)

def group_norm(values, norm_gain, norm_shift, onehot, valid_mask, counts):
    channels = values.shape[3]
    per_group = channels // GROUPS
    member = (jnp.arange(channels, dtype=jnp.int32)[:, None] // per_group == jnp.arange(GROUPS, dtype=jnp.int32)[None, :]).astype(jnp.float32)
    mask_four = valid_mask.astype(jnp.float32)[:, None, :, None]
    masked = values * mask_four
    group_sum = jnp.einsum('rfwc,cg,rv->fvg', masked, member, onehot, precision=HIGHEST)
    group_mean = group_sum / counts
    mean_full = jnp.einsum('fvg,rv,cg->rfc', group_mean, onehot, member, precision=HIGHEST)
    centered = (values - mean_full[:, :, None, :]) * mask_four
    variance = jnp.einsum('rfwc,cg,rv->fvg', centered * centered, member, onehot, precision=HIGHEST) / counts
    scale_full = jnp.einsum('fvg,rv,cg->rfc', lax.rsqrt(variance + EPSILON), onehot, member, precision=HIGHEST)
    return centered * scale_full[:, :, None, :] * norm_gain + norm_shift

def causal_conv(hidden, conv_weight, row_video):
    row_count, frame_count, col_count, channels = hidden.shape
    padded = jnp.pad(hidden, ((1, 1), (2, 0), (1, 1), (0, 0)))
    labels = jnp.pad(row_video, 1, constant_values=-1)
    total = jnp.zeros((row_count * frame_count * col_count, conv_weight.shape[-1]), jnp.float32)
    for row_tap in range(3):
        same = (labels[row_tap:row_tap + row_count] == row_video).astype(hidden.dtype)[:, None, None, None]
        for time_tap in range(3):
            for col_tap in range(3):
                window = padded[row_tap:row_tap + row_count, time_tap:time_tap + frame_count, col_tap:col_tap + col_count] * same
                total = total + jnp.dot(window.reshape(-1, channels), conv_weight[time_tap, row_tap, col_tap], preferred_element_type=jnp.float32)
    return total.reshape(row_count, frame_count, col_count, -1)

def attend_all(queries, keys_all, values_all, row_video, valid_mask):
    row_count, frame_count, col_count, channels = queries.shape
    blocks = row_count // ROWS_DEV
    key_labels = jnp.repeat(row_video, col_count)
    key_valid = valid_mask.reshape(-1)
    scale = CH ** (-0.5)
    zero = jnp.zeros((), jnp.int32)

    def one_block(index):
        frame_index = (index // blocks).astype(jnp.int32)
        first_row = (index % blocks * ROWS_DEV).astype(jnp.int32)
        query_block = lax.dynamic_slice(queries, (first_row, frame_index, zero, zero), (ROWS_DEV, 1, col_count, channels)).reshape(-1, channels)
        key_frame = lax.dynamic_slice(keys_all, (zero, frame_index, zero, zero), (row_count, 1, col_count, channels)).reshape(-1, channels)
        value_frame = lax.dynamic_slice(values_all, (zero, frame_index, zero, zero), (row_count, 1, col_count, channels)).reshape(-1, channels)
        query_labels = jnp.repeat(lax.dynamic_slice(row_video, (first_row,), (ROWS_DEV,)), col_count)
        scores = jnp.dot(query_block, key_frame.T, preferred_element_type=jnp.float32) * scale
        allowed = (query_labels[:, None] == key_labels[None, :]) & key_valid[None, :]
        scores = jnp.where(allowed, scores, MASKED)
        largest = lax.optimization_barrier(jnp.max(scores, axis=1, keepdims=True))
        weights = jnp.where(allowed, jnp.exp(scores - largest), 0.0)
        denominator = lax.optimization_barrier(jnp.sum(weights, axis=1, keepdims=True))
        mixed = jnp.dot(weights.astype(jnp.bfloat16), value_frame, preferred_element_type=jnp.float32) / denominator
        return mixed.astype(jnp.bfloat16).reshape(ROWS_DEV, col_count, channels)
    results = lax.map(one_block, jnp.arange(frame_count * blocks, dtype=jnp.int32))
    results = results.reshape(frame_count, row_count, col_count, channels)
    return jnp.transpose(results, (1, 0, 2, 3))

def upsample_conv(values, weight, row_video):
    row_count, frame_count, col_count, channels = values.shape
    doubled = jnp.repeat(jnp.repeat(values, 2, axis=0), 2, axis=2)
    up_labels = jnp.repeat(row_video, 2)
    padded = jnp.pad(doubled, ((1, 1), (0, 0), (1, 1), (0, 0)))
    labels = jnp.pad(up_labels, 1, constant_values=-1)
    total = jnp.zeros((4 * row_count * frame_count * col_count, weight.shape[-1]), jnp.float32)
    for row_tap in range(3):
        same = (labels[row_tap:row_tap + 2 * row_count] == up_labels).astype(values.dtype)[:, None, None, None]
        for col_tap in range(3):
            window = padded[row_tap:row_tap + 2 * row_count, :, col_tap:col_tap + 2 * col_count] * same
            total = total + jnp.dot(window.reshape(-1, channels), weight[row_tap, col_tap], preferred_element_type=jnp.float32)
    return total.reshape(2 * row_count, frame_count, 2 * col_count, -1)

def reference(latents, row_video, video_cols, first_gain, first_shift, conv_weight, conv_bias, second_gain, second_shift, triple_weight, triple_bias, output_weight, output_bias, upsample_weight, upsample_bias):
    onehot, row_widths = video_tables(row_video, video_cols)
    valid_mask = jnp.arange(WIDTH, dtype=jnp.int32)[None, :] < row_widths[:, None]
    mask_four = valid_mask[:, None, :, None]
    counts = (lax.optimization_barrier(jnp.sum(onehot, axis=0)) * video_cols.astype(jnp.float32) * (CH // GROUPS))[None, :, None]
    source = latents.astype(jnp.float32)
    first_normed = group_norm(source, first_gain, first_shift, onehot, valid_mask, counts)
    hidden = jnp.where(mask_four, jax.nn.silu(first_normed), 0.0).astype(jnp.bfloat16)
    branch = causal_conv(hidden, conv_weight, row_video)
    after_conv = jnp.where(mask_four, source + branch + conv_bias, 0.0).astype(jnp.bfloat16)
    second_normed = jnp.where(mask_four, group_norm(after_conv.astype(jnp.float32), second_gain, second_shift, onehot, valid_mask, counts), 0.0).astype(jnp.bfloat16)
    triple = (jnp.dot(second_normed.reshape(-1, CH), triple_weight, preferred_element_type=jnp.float32) + triple_bias).astype(jnp.bfloat16)
    triple = triple.reshape(ROWS, FRAMES, WIDTH, 3 * CH)
    mixed = attend_all(triple[..., :CH], triple[..., CH:2 * CH], triple[..., 2 * CH:], row_video, valid_mask)
    attended = jnp.dot(mixed.reshape(-1, CH), output_weight, preferred_element_type=jnp.float32).reshape(ROWS, FRAMES, WIDTH, CH)
    after_attention = jnp.where(mask_four, after_conv.astype(jnp.float32) + attended + output_bias, 0.0).astype(jnp.bfloat16)
    decoded = upsample_conv(after_attention, upsample_weight, row_video)
    up_valid = jnp.arange(2 * WIDTH, dtype=jnp.int32)[None, :] < 2 * jnp.repeat(row_widths, 2)[:, None]
    return jnp.where(up_valid[:, None, :, None], decoded + upsample_bias, 0.0).astype(jnp.bfloat16)
```

```python
import functools
import math

import jax
import jax.numpy as jnp
from jax import lax
from jax.experimental import pallas as pl
from jax.experimental.pallas import tpu as pltpu
from jax.sharding import PartitionSpec as P

GROUPS = 32
EPSILON = 1e-05
MASKED = -1e30
LOWEST = -5e29
HIGHEST = lax.Precision.HIGHEST
BOTH = ("tile", "frame")
SLOTS = 8
LANES = 128
KEY_BLOCK = 512
VMEM_BYTES = 40 * 1024 * 1024
F32 = jnp.float32
BF16 = jnp.bfloat16

SMEM_SPEC = pl.BlockSpec(memory_space=pltpu.SMEM)
VMEM_SPEC = pl.BlockSpec(memory_space=pltpu.VMEM)


def cost(macs, nbytes, exps=0):
    return pl.CostEstimate(flops=2 * macs, bytes_accessed=nbytes, transcendentals=exps)


def params():
    return pltpu.CompilerParams(vmem_limit_bytes=VMEM_BYTES)


def member_matrix(channels):
    per_group = channels // GROUPS
    group = lax.broadcasted_iota(jnp.int32, (LANES, channels), 0) * per_group
    channel = lax.broadcasted_iota(jnp.int32, (LANES, channels), 1)
    return jnp.where((channel >= group) & (channel < group + per_group), 1.0, 0.0).astype(F32)


def to_groups(values, member):
    return lax.dot_general(
        values, member, (((1,), (1,)), ((), ())), precision=HIGHEST, preferred_element_type=F32
    )


def to_channels(values, member):
    return jnp.dot(values, member, precision=HIGHEST, preferred_element_type=F32)


def row_label(video_ref, row):
    rows = video_ref.shape[0]
    inside = (row >= 0) & (row < rows)
    return jnp.where(inside, video_ref[jnp.clip(row, 0, rows - 1)], -1)


def row_width(cols_ref, label):
    return jnp.where(label >= 0, cols_ref[jnp.maximum(label, 0)], 0)


def pick(table, label, videos):
    chosen = table[0:1]
    for video in range(1, videos):
        chosen = jnp.where(label == video, table[video : video + 1], chosen)
    return chosen


def norm_tables(stats_ref, gain_ref):
    member = member_matrix(gain_ref.shape[1])
    counts = jnp.maximum(stats_ref[0], 1.0)
    scale = lax.rsqrt(stats_ref[2] / counts + EPSILON)
    return to_channels(stats_ref[1], member), to_channels(scale, member) * gain_ref[...]


def write_stats(out_ref, rows, labels, widths, videos, channels):
    member = member_matrix(channels)
    per_group = channels // GROUPS
    cols = rows[0].shape[0]
    slot = lax.broadcasted_iota(jnp.int32, (SLOTS, 1), 0)
    column = lax.broadcasted_iota(jnp.int32, (cols, 1), 0)
    sums = jnp.zeros((SLOTS, channels), F32)
    counts = jnp.zeros((SLOTS, 1), F32)
    for index, row in enumerate(rows):
        sums = jnp.where(slot == index, jnp.sum(row, axis=0, keepdims=True), sums)
        counts = jnp.where(slot == index, (widths[index] * per_group).astype(F32), counts)
    means = to_groups(sums, member) / jnp.maximum(counts, 1.0)
    means_wide = to_channels(means, member)
    squares = jnp.zeros((SLOTS, channels), F32)
    for index, row in enumerate(rows):
        centered = jnp.where(column < widths[index], row - means_wide[index : index + 1], 0.0)
        squares = jnp.where(
            slot == index, jnp.sum(centered * centered, axis=0, keepdims=True), squares
        )
    spreads = to_groups(squares, member)
    out_ref[...] = jnp.zeros(out_ref.shape, F32)
    for video in range(videos):
        total = jnp.zeros((1, LANES), F32)
        count = jnp.zeros((1, LANES), F32)
        for index in range(len(rows)):
            mine = labels[index] == video
            row_count = counts[index : index + 1]
            total = total + jnp.where(mine, means[index : index + 1] * row_count, 0.0)
            count = count + jnp.where(mine, row_count, 0.0)
        mean = total / jnp.maximum(count, 1.0)
        spread = jnp.zeros((1, LANES), F32)
        for index in range(len(rows)):
            off = means[index : index + 1] - mean
            part = spreads[index : index + 1] + counts[index : index + 1] * off * off
            spread = spread + jnp.where(labels[index] == video, part, 0.0)
        out_ref[0, video : video + 1, :] = count
        out_ref[1, video : video + 1, :] = mean
        out_ref[2, video : video + 1, :] = spread


def place_of(place_ref, video_ref, cols_ref, row_count, rim):
    first = place_ref[0] * row_count
    labels = [row_label(video_ref, first + r) for r in range(-rim, row_count + rim)]
    return labels, [row_width(cols_ref, label) for label in labels]


def build_columns(columns_ref, row_refs):
    padded = columns_ref.shape[0] // len(row_refs)
    for index, row in enumerate(row_refs):
        cells = row().astype(F32)
        count, channels = cells.shape
        cells = jnp.concatenate([cells, jnp.zeros((padded - count, channels), F32)], axis=0)
        start = index * padded
        columns_ref[start : start + padded, 0:channels] = pltpu.roll(cells, 1, 0).astype(BF16)
        columns_ref[start : start + padded, channels : 2 * channels] = cells.astype(BF16)
        columns_ref[start : start + padded, 2 * channels : 3 * channels] = pltpu.roll(
            cells, padded - 1, 0
        ).astype(BF16)


def stats_kernel(place_ref, video_ref, cols_ref, latents_ref, out_ref):
    row_count, cols, channels = latents_ref.shape
    labels, widths = place_of(place_ref, video_ref, cols_ref, row_count, 0)
    column = lax.broadcasted_iota(jnp.int32, (cols, 1), 0)
    rows = [
        jnp.where(column < widths[r], latents_ref[r].astype(F32), 0.0) for r in range(row_count)
    ]
    write_stats(out_ref, rows, labels, widths, cols_ref.shape[0], channels)


def hidden_kernel(
    place_ref, video_ref, cols_ref, before_ref, latents_ref, after_ref, stats_ref, gain_ref,
    shift_ref, out_ref,
):
    row_count, cols, _ = latents_ref.shape
    labels, widths = place_of(place_ref, video_ref, cols_ref, row_count, 1)
    means, scales = norm_tables(stats_ref, gain_ref)
    videos = cols_ref.shape[0]
    column = lax.broadcasted_iota(jnp.int32, (cols, 1), 0)
    for r in range(row_count + 2):
        if r == 0:
            source = before_ref[0]
        elif r == row_count + 1:
            source = after_ref[0]
        else:
            source = latents_ref[r - 1]
        mean = pick(means, labels[r], videos)
        scale = pick(scales, labels[r], videos)
        normed = (source.astype(F32) - mean) * scale + shift_ref[...]
        active = normed / (1.0 + jnp.exp(-normed))
        out_ref[r] = jnp.where(column < widths[r], active, 0.0).astype(BF16)


def conv_kernel(
    last, place_ref, video_ref, cols_ref, hidden_ref, weight_ref, *rest
):
    if last:
        partial_ref, latents_ref, bias_ref, out_ref, stats_ref, columns_ref, total_ref = rest
    else:
        if len(rest) == 4:
            partial_ref, out_ref, columns_ref, total_ref = rest
        else:
            partial_ref = None
            out_ref, columns_ref, total_ref = rest
    tap = pl.program_id(0)
    near_rows = hidden_ref.shape[0]
    row_count = near_rows - 2
    padded = columns_ref.shape[0] // near_rows
    labels, widths = place_of(place_ref, video_ref, cols_ref, row_count, 1)

    @pl.when(tap == 0)
    def _():
        build_columns(
            columns_ref, [functools.partial(hidden_ref.__getitem__, r) for r in range(near_rows)]
        )
        if partial_ref is None:
            total_ref[...] = jnp.zeros(total_ref.shape, F32)
        else:
            total_ref[...] = partial_ref[...]

    start = pl.multiple_of(tap * padded, 16)
    product = jnp.dot(
        columns_ref[pl.ds(start, row_count * padded), :], weight_ref[0], preferred_element_type=F32
    )
    for r in range(row_count):
        lo, hi = r * padded, (r + 1) * padded
        near = jnp.where(tap == 0, labels[r], jnp.where(tap == 1, labels[r + 1], labels[r + 2]))
        total_ref[lo:hi, :] += jnp.where(near == labels[r + 1], product[lo:hi], 0.0)

    @pl.when(tap == 2)
    def _():
        if not last:
            out_ref[...] = total_ref[...]
            return
        cols = latents_ref.shape[1]
        column = lax.broadcasted_iota(jnp.int32, (cols, 1), 0)
        rows = []
        for r in range(row_count):
            branch = total_ref[r * padded : r * padded + cols, :]
            value = latents_ref[r].astype(F32) + branch + bias_ref[...]
            value = jnp.where(column < widths[r + 1], value, 0.0).astype(BF16)
            out_ref[r] = value
            rows.append(value.astype(F32))
        write_stats(
            stats_ref, rows, labels[1:-1], widths[1:-1], cols_ref.shape[0], latents_ref.shape[2]
        )


def normed_pair(pair, labels, means, scales, shift_ref, videos):
    cols = pair.shape[0] // 2
    halves = []
    for half in range(2):
        values = pair[half * cols : (half + 1) * cols]
        mean = pick(means, labels[half], videos)
        scale = pick(scales, labels[half], videos)
        halves.append((values - mean) * scale + shift_ref[...])
    return halves


def query_kernel(
    place_ref, video_ref, cols_ref, own_ref, stats_ref, gain_ref, shift_ref, weight_ref, bias_ref,
    queries_ref, constant_ref,
):
    pairs, double, channels = own_ref.shape
    cols = double // 2
    row_count = 2 * pairs
    labels, widths = place_of(place_ref, video_ref, cols_ref, row_count, 0)
    means, scales = norm_tables(stats_ref, gain_ref)
    videos = cols_ref.shape[0]
    column = lax.broadcasted_iota(jnp.int32, (cols, 1), 0)
    rows = []
    for pair in range(pairs):
        halves = normed_pair(
            own_ref[pair].astype(F32), labels[2 * pair : 2 * pair + 2], means, scales, shift_ref,
            videos,
        )
        for half in range(2):
            rows.append(jnp.where(column < widths[2 * pair + half], halves[half], 0.0))
    cells = jnp.concatenate(rows, axis=0).astype(BF16)
    queries = (
        jnp.dot(cells, weight_ref[:, 0:channels], preferred_element_type=F32)
        + bias_ref[:, 0:channels]
    ).astype(BF16)
    factor = channels ** (-0.5) * math.log2(math.e)
    turned = lax.dot_general(
        queries, weight_ref[:, channels : 2 * channels], (((1,), (1,)), ((), ())),
        preferred_element_type=F32,
    )
    queries_ref[...] = (turned * factor).astype(BF16)
    constant = jnp.sum(
        queries.astype(F32) * bias_ref[:, channels : 2 * channels], axis=1, keepdims=True
    )
    constant_ref[...] = jnp.broadcast_to(constant * factor, constant_ref.shape)


def attend_kernel(
    place_ref, video_ref, cols_ref, own_ref, stats_ref, gain_ref, shift_ref, weight_ref, bias_ref,
    out_weight_ref, out_bias_ref, queries_ref, constant_ref, codes_ref, canvas_ref, out_ref,
    keys_ref, total_ref,
):
    pairs, double, channels = own_ref.shape
    cols = double // 2
    row_count = 2 * pairs
    rows = video_ref.shape[0]
    labels, widths = place_of(place_ref, video_ref, cols_ref, row_count, 0)
    means, scales = norm_tables(stats_ref, gain_ref)
    videos = cols_ref.shape[0]
    lowest, highest = labels[0], labels[-1]

    def count(row, carried):
        below, upto = carried
        label = video_ref[row]
        return (
            below + (label < lowest).astype(jnp.int32),
            upto + (label <= highest).astype(jnp.int32),
        )

    first_row, end_row = lax.fori_loop(0, rows, count, (jnp.int32(0), jnp.int32(0)))
    first_block = (first_row * cols) // KEY_BLOCK
    end_block = (end_row * cols + KEY_BLOCK - 1) // KEY_BLOCK
    first_pair = (first_block * KEY_BLOCK) // double
    end_pair = jnp.minimum((end_block * KEY_BLOCK + double - 1) // double, rows // 2)

    def normalise(pair, carried):
        near = [video_ref[2 * pair], video_ref[2 * pair + 1]]
        halves = normed_pair(
            canvas_ref[pair].astype(F32), near, means, scales, shift_ref, videos
        )
        start = pl.multiple_of(pair * double, 16)
        keys_ref[pl.ds(start, double), :] = jnp.concatenate(halves, axis=0).astype(BF16)
        return carried

    lax.fori_loop(first_pair, end_pair, normalise, jnp.int32(0))

    query_label = jnp.concatenate(
        [jnp.zeros((cols, 1), F32) + labels[r].astype(F32) for r in range(row_count)], axis=0
    )
    queries = queries_ref[...]
    constant = constant_ref[:, 0:1]
    total_ref[...] = jnp.zeros(total_ref.shape, F32)

    def step(block, carried):
        largest, denominator = carried
        start = pl.multiple_of(block * KEY_BLOCK, KEY_BLOCK)
        keys = keys_ref[pl.ds(start, KEY_BLOCK), :]
        scores = lax.dot_general(
            queries, keys, (((1,), (1,)), ((), ())), preferred_element_type=F32
        )
        scores = jnp.where(codes_ref[:, pl.ds(start, KEY_BLOCK)] == query_label, scores, MASKED)
        peak = jnp.maximum(largest, jnp.max(scores, axis=1, keepdims=True) + constant)
        weights = jnp.exp2(scores - (peak - constant))
        factor = jnp.exp2(largest - peak)
        denominator = denominator * factor + jnp.sum(weights, axis=1, keepdims=True)
        total_ref[...] = total_ref[...] * factor + jnp.dot(
            weights.astype(BF16), keys, preferred_element_type=F32
        )
        return peak, denominator

    cells = row_count * cols
    _, denominator = lax.fori_loop(
        first_block, end_block, step,
        (jnp.full((cells, 1), LOWEST, F32), jnp.zeros((cells, 1), F32)),
    )
    mean_cell = (total_ref[...] / denominator).astype(BF16)
    mixed = (
        jnp.dot(mean_cell, weight_ref[:, 2 * channels :], preferred_element_type=F32)
        + bias_ref[:, 2 * channels :]
    ).astype(BF16)
    attended = jnp.dot(mixed, out_weight_ref[...], preferred_element_type=F32) + out_bias_ref[...]
    column = lax.broadcasted_iota(jnp.int32, (cols, 1), 0)
    for pair in range(pairs):
        before = own_ref[pair].astype(F32)
        halves = []
        for half in range(2):
            r = 2 * pair + half
            value = before[half * cols : (half + 1) * cols] + attended[r * cols : (r + 1) * cols]
            halves.append(jnp.where(column < widths[r], value, 0.0))
        out_ref[pair] = jnp.concatenate(halves, axis=0).astype(BF16)


def upsample_kernel(
    place_ref, video_ref, cols_ref, before_ref, own_ref, after_ref, weight_ref, bias_ref, out_ref,
    columns_ref, wide_ref,
):
    row_count, cols, channels = own_ref.shape
    near_rows = row_count + 2
    padded = columns_ref.shape[0] // near_rows
    labels, widths = place_of(place_ref, video_ref, cols_ref, row_count, 1)
    parts_out = wide_ref.shape[0]
    out_channels = out_ref.shape[-1]
    sources = [functools.partial(before_ref.__getitem__, 0)]
    sources += [functools.partial(own_ref.__getitem__, r) for r in range(row_count)]
    sources += [functools.partial(after_ref.__getitem__, 0)]
    build_columns(columns_ref, sources)
    span = row_count * padded
    column = lax.broadcasted_iota(jnp.int32, (2 * cols, 1), 0)
    for down in range(2):
        for right in range(2):
            lanes = slice(right * channels, (right + 2) * channels)
            parts = [
                jnp.dot(
                    columns_ref[(down + tap) * padded : (down + tap) * padded + span, lanes],
                    weight_ref[down, tap, right],
                    preferred_element_type=F32,
                )
                for tap in range(2)
            ]
            rim = parts[down]
            same = parts[1 - down]
            for r in range(row_count):
                lo, hi = r * padded, r * padded + cols
                near = labels[r + 2 * down]
                value = same[lo:hi] + jnp.where(near == labels[r + 1], rim[lo:hi], 0.0)
                for part in range(parts_out):
                    wide_ref[part, 2 * r + down, pl.ds(right, cols, 2), :] = value[
                        :, part * LANES : (part + 1) * LANES
                    ]
    for r in range(2 * row_count):
        valid = column < 2 * widths[r // 2 + 1]
        for part in range(parts_out):
            lo, hi = part * LANES, min((part + 1) * LANES, out_channels)
            value = wide_ref[part, r, :, 0 : hi - lo] + bias_ref[:, lo:hi]
            out_ref[r, :, lo:hi] = jnp.where(valid, value, 0.0).astype(BF16)


def merge_stats(mine, other):
    count = mine[0] + other[0]
    safe = jnp.maximum(count, 1.0)
    off = other[1] - mine[1]
    mean = mine[1] + off * (other[0] / safe)
    spread = mine[2] + other[2] + off * off * (mine[0] * other[0] / safe)
    return jnp.stack([count, mean, spread])


def combined_weight(weight):
    wide = jnp.pad(weight.astype(F32), ((0, 0),) * 3 + ((0, -weight.shape[-1] % LANES),))
    rows = jnp.stack(
        [
            jnp.stack([wide[0], wide[1] + wide[2]]),
            jnp.stack([wide[0] + wide[1], wide[2]]),
        ]
    )
    left = jnp.concatenate([rows[:, :, 0], rows[:, :, 1] + rows[:, :, 2]], axis=2)
    right = jnp.concatenate([rows[:, :, 0] + rows[:, :, 1], rows[:, :, 2]], axis=2)
    return jnp.stack([left, right], axis=2).astype(BF16)


def shards(
    tiles,
    frames,
    latents,
    row_video,
    video_cols,
    first_gain,
    first_shift,
    conv_weight,
    conv_bias,
    second_gain,
    second_shift,
    triple_weight,
    triple_bias,
    output_weight,
    output_bias,
    upsample_weight,
    upsample_bias,
):
    row_count, frame_count, cols, channels = latents.shape
    assert frame_count == 1 and row_count % 2 == 0
    out_channels = upsample_weight.shape[-1]
    rows = row_count * tiles
    cells = row_count * cols
    padded = -(-(cols + 1) // 16) * 16
    near_rows = row_count + 2
    assert (rows * cols) % KEY_BLOCK == 0
    source = latents.reshape(row_count, cols, channels)
    tile = lax.axis_index("tile")
    frame = lax.axis_index("frame")
    place = jnp.reshape(tile, (1,)).astype(jnp.int32)
    turned_place = jnp.reshape(tile // 2 * 2 + frame % 2, (1,)).astype(jnp.int32)

    def number(t, f):
        return t * frames + f

    def turned(t, f):
        return number(t // 2 * 2 + f % 2, f // 2 * 2 + t % 2)

    every = [(t, f) for t in range(tiles) for f in range(frames)]
    turn = [(number(t, f), turned(t, f)) for t, f in every]
    up = [(i, i + 1) for i in range(tiles - 1)]
    down = [(i + 1, i) for i in range(tiles - 1)]

    def row(vector):
        return vector.reshape(1, -1)

    before = lax.ppermute(source[row_count - 1 :], "tile", up)
    after = lax.ppermute(source[:1], "tile", down)
    stats_shape = jax.ShapeDtypeStruct((3, SLOTS, LANES), F32)
    stats = pl.pallas_call(
        stats_kernel,
        out_shape=stats_shape,
        in_specs=[SMEM_SPEC] * 3 + [VMEM_SPEC],
        out_specs=VMEM_SPEC,
        compiler_params=params(),
        cost_estimate=cost(cells * channels * 2, 2 * cells * channels),
        name="first_stats",
    )(place, row_video, video_cols, source)
    bit = 1
    while bit < tiles:
        other = lax.ppermute(stats, "tile", [(i, i ^ bit) for i in range(tiles)])
        stats = merge_stats(stats, other)
        bit *= 2
    hidden = pl.pallas_call(
        hidden_kernel,
        out_shape=jax.ShapeDtypeStruct((near_rows, cols, channels), BF16),
        in_specs=[SMEM_SPEC] * 3 + [VMEM_SPEC] * 6,
        out_specs=VMEM_SPEC,
        compiler_params=params(),
        cost_estimate=cost(cells * channels * 10, 5 * cells * channels, cells * channels),
        name="hidden",
    )(
        place, row_video, video_cols, before, source, after, stats, row(first_gain),
        row(first_shift),
    )

    weights = conv_weight.reshape(9, 3 * channels, channels)
    taps = min(3, frames)
    earlier = [
        lax.ppermute(hidden, "frame", [(i, i + by) for i in range(frames - by)])
        for by in range(1, taps)
    ]
    total = None
    for back, context in enumerate([hidden] + earlier):
        last = back == taps - 1
        time_tap = 2 - back

        def whole(shape):
            return pl.BlockSpec(shape, lambda b, n=len(shape): (0,) * n)

        in_specs = [SMEM_SPEC] * 3 + [
            whole((near_rows, cols, channels)),
            pl.BlockSpec((1, 3 * channels, channels), lambda b, a=time_tap: (3 * a + b, 0, 0)),
        ]
        operands = [place, row_video, video_cols, context, weights]
        if total is not None:
            in_specs.append(whole((row_count * padded, channels)))
            operands.append(total)
        if last:
            in_specs += [whole((row_count, cols, channels)), whole((1, channels))]
            operands += [source, row(conv_bias)]
            out_shape = (jax.ShapeDtypeStruct((row_count, cols, channels), BF16), stats_shape)
            out_specs = (whole((row_count, cols, channels)), whole((3, SLOTS, LANES)))
        else:
            out_shape = jax.ShapeDtypeStruct((row_count * padded, channels), F32)
            out_specs = whole((row_count * padded, channels))
        total = pl.pallas_call(
            functools.partial(conv_kernel, last),
            grid=(3,),
            out_shape=out_shape,
            in_specs=in_specs,
            out_specs=out_specs,
            scratch_shapes=[
                pltpu.VMEM((near_rows * padded, 3 * channels), BF16),
                pltpu.VMEM((row_count * padded, channels), F32),
            ],
            compiler_params=params(),
            cost_estimate=cost(9 * cells * channels * channels, 18 * channels * channels),
            name="conv_last" if last else "conv_part",
        )(*operands)
    after_conv, stats = total

    own = lax.ppermute(after_conv, BOTH, turn)
    stats = lax.ppermute(stats, BOTH, turn)
    groups = [
        [number(t, 2 * j + c) for t in range(side, tiles, 2) for c in range(2)]
        for side in range(2)
        for j in range(frames // 2)
    ]
    canvas = lax.all_gather(own, BOTH, axis=0, tiled=True, axis_index_groups=groups)
    stats = merge_stats(
        stats, lax.ppermute(stats, BOTH, [(number(t, f), number(t, f ^ 1)) for t, f in every])
    )
    bit = 2
    while bit < tiles:
        other = lax.ppermute(
            stats, BOTH, [(number(t, f), number(t ^ bit, f)) for t, f in every]
        )
        stats = merge_stats(stats, other)
        bit *= 2
    own_pairs = own.reshape(row_count // 2, 2 * cols, channels)
    queries, constant = pl.pallas_call(
        query_kernel,
        out_shape=(
            jax.ShapeDtypeStruct((cells, channels), BF16),
            jax.ShapeDtypeStruct((cells, LANES), F32),
        ),
        in_specs=[SMEM_SPEC] * 3 + [VMEM_SPEC] * 6,
        out_specs=(VMEM_SPEC, VMEM_SPEC),
        compiler_params=params(),
        cost_estimate=cost(2 * cells * channels * channels, 4 * cells * channels),
        name="queries",
    )(
        turned_place, row_video, video_cols, own_pairs, stats, row(second_gain),
        row(second_shift), triple_weight, row(triple_bias),
    )
    widths = jnp.sum(
        jnp.where(
            row_video[:, None] == jnp.arange(video_cols.shape[0], dtype=jnp.int32)[None, :],
            video_cols[None, :],
            0,
        ),
        axis=1,
    )
    valid = jnp.arange(cols, dtype=jnp.int32)[None, :] < widths[:, None]
    codes = jnp.where(valid, row_video[:, None], -1).astype(F32).reshape(1, rows * cols)
    attended = pl.pallas_call(
        attend_kernel,
        out_shape=jax.ShapeDtypeStruct((row_count // 2, 2 * cols, channels), BF16),
        in_specs=[SMEM_SPEC] * 3 + [VMEM_SPEC] * 12,
        out_specs=VMEM_SPEC,
        scratch_shapes=[
            pltpu.VMEM((rows * cols, channels), BF16),
            pltpu.VMEM((cells, channels), F32),
        ],
        compiler_params=params(),
        cost_estimate=cost(
            2 * cells * rows * cols * channels, 2 * rows * cols * channels, cells * rows * cols
        ),
        name="attend",
    )(
        turned_place, row_video, video_cols, own_pairs, stats, row(second_gain),
        row(second_shift), triple_weight, row(triple_bias), output_weight, row(output_bias),
        queries, constant, codes, canvas.reshape(rows // 2, 2 * cols, channels),
    )
    attended = attended.reshape(row_count, cols, channels)

    places = {turned(t, f): (t, f) for t, f in every}
    assert all(places[turned(t, f)] == (t, f) for t, f in every)
    back_up = [(turned(t, f), number(t + 1, f)) for t, f in every if t + 1 < tiles]
    back_down = [(turned(t, f), number(t - 1, f)) for t, f in every if t > 0]
    before = lax.ppermute(attended[row_count - 1 :], BOTH, back_up)
    after = lax.ppermute(attended[:1], BOTH, back_down)
    home = lax.ppermute(attended, BOTH, turn)
    decoded = pl.pallas_call(
        upsample_kernel,
        out_shape=jax.ShapeDtypeStruct((2 * row_count, 2 * cols, out_channels), BF16),
        in_specs=[SMEM_SPEC] * 3 + [VMEM_SPEC] * 5,
        out_specs=VMEM_SPEC,
        scratch_shapes=[
            pltpu.VMEM((near_rows * padded, 3 * channels), BF16),
            pltpu.VMEM((-(-out_channels // LANES), 2 * row_count, 2 * cols, LANES), F32),
        ],
        compiler_params=params(),
        cost_estimate=cost(16 * cells * channels * out_channels, 8 * cells * out_channels),
        name="upsample",
    )(
        place, row_video, video_cols, before, home, after, combined_weight(upsample_weight),
        row(upsample_bias),
    )
    return decoded.reshape(2 * row_count, 1, 2 * cols, out_channels)


def solution(mesh):
    sizes = dict(mesh.shape)
    in_specs = (P("tile", "frame", None, None),) + (P(),) * 14
    out_specs = P("tile", "frame", None, None)
    body = functools.partial(shards, sizes["tile"], sizes["frame"])
    return jax.shard_map(body, mesh=mesh, in_specs=in_specs, out_specs=out_specs, check_vma=False)
```

```python
import functools
import math

import jax
import jax.numpy as jnp
from jax import lax
from jax.experimental import pallas as pl
from jax.experimental.pallas import tpu as pltpu
from jax.sharding import PartitionSpec as P

GROUPS = 32
EPSILON = 1e-05
MASKED = -1e30
LOWEST = -5e29
HIGHEST = lax.Precision.HIGHEST
SLOTS = 8
LANES = 128
CHUNKS = 2
VMEM_BYTES = 40 * 1024 * 1024
CONV_VMEM_BYTES = 56 * 1024 * 1024
F32 = jnp.float32
BF16 = jnp.bfloat16

SMEM_SPEC = pl.BlockSpec(memory_space=pltpu.SMEM)
VMEM_SPEC = pl.BlockSpec(memory_space=pltpu.VMEM)


def cost(macs, nbytes, exps=0):
    return pl.CostEstimate(flops=2 * macs, bytes_accessed=nbytes, transcendentals=exps)


def params():
    return pltpu.CompilerParams(vmem_limit_bytes=VMEM_BYTES)


def member_matrix(channels):
    per_group = channels // GROUPS
    group = lax.broadcasted_iota(jnp.int32, (LANES, channels), 0) * per_group
    channel = lax.broadcasted_iota(jnp.int32, (LANES, channels), 1)
    return jnp.where((channel >= group) & (channel < group + per_group), 1.0, 0.0).astype(F32)


def to_groups(values, member):
    return lax.dot_general(
        values, member, (((1,), (1,)), ((), ())), precision=HIGHEST, preferred_element_type=F32
    )


def to_channels(values, member):
    return jnp.dot(values, member, precision=HIGHEST, preferred_element_type=F32)


class Info:
    def __init__(self, ref, rows):
        self.ref, self.rows = ref, rows
        self.videos = ref.shape[0] - 1 - rows

    def tile(self):
        return self.ref[0]

    def label(self, row):
        inside = (row >= 0) & (row < self.rows)
        return jnp.where(inside, self.ref[1 + jnp.clip(row, 0, self.rows - 1)], -1)

    def width(self, label):
        return jnp.where(label >= 0, self.ref[1 + self.rows + jnp.maximum(label, 0)], 0)

    def window(self, first, count):
        labels = [self.label(first + r) for r in range(count)]
        return labels, [self.width(label) for label in labels]


def pick(table, label, videos):
    chosen = table[0:1]
    for video in range(1, videos):
        chosen = jnp.where(label == video, table[video : video + 1], chosen)
    return chosen


def norm_tables(stats_ref, gain_ref):
    member = member_matrix(gain_ref.shape[1])
    counts = jnp.maximum(stats_ref[0], 1.0)
    scale = lax.rsqrt(stats_ref[2] / counts + EPSILON)
    return to_channels(stats_ref[1], member), to_channels(scale, member) * gain_ref[...]


def write_stats(out_ref, rows, labels, widths, videos, channels):
    member = member_matrix(channels)
    per_group = channels // GROUPS
    cols = rows[0].shape[0]
    slot = lax.broadcasted_iota(jnp.int32, (SLOTS, 1), 0)
    column = lax.broadcasted_iota(jnp.int32, (cols, 1), 0)
    sums = jnp.zeros((SLOTS, channels), F32)
    counts = jnp.zeros((SLOTS, 1), F32)
    for index, row in enumerate(rows):
        sums = jnp.where(slot == index, jnp.sum(row, axis=0, keepdims=True), sums)
        counts = jnp.where(slot == index, (widths[index] * per_group).astype(F32), counts)
    means = to_groups(sums, member) / jnp.maximum(counts, 1.0)
    means_wide = to_channels(means, member)
    squares = jnp.zeros((SLOTS, channels), F32)
    for index, row in enumerate(rows):
        centered = jnp.where(column < widths[index], row - means_wide[index : index + 1], 0.0)
        squares = jnp.where(
            slot == index, jnp.sum(centered * centered, axis=0, keepdims=True), squares
        )
    spreads = to_groups(squares, member)
    out_ref[...] = jnp.zeros(out_ref.shape, F32)
    for video in range(videos):
        total = jnp.zeros((1, LANES), F32)
        count = jnp.zeros((1, LANES), F32)
        for index in range(len(rows)):
            mine = labels[index] == video
            row_count = counts[index : index + 1]
            total = total + jnp.where(mine, means[index : index + 1] * row_count, 0.0)
            count = count + jnp.where(mine, row_count, 0.0)
        mean = total / jnp.maximum(count, 1.0)
        spread = jnp.zeros((1, LANES), F32)
        for index in range(len(rows)):
            off = means[index : index + 1] - mean
            part = spreads[index : index + 1] + counts[index : index + 1] * off * off
            spread = spread + jnp.where(labels[index] == video, part, 0.0)
        out_ref[0, video : video + 1, :] = count
        out_ref[1, video : video + 1, :] = mean
        out_ref[2, video : video + 1, :] = spread


def build_columns(columns_ref, row_refs):
    padded = columns_ref.shape[0] // len(row_refs)
    for index, row in enumerate(row_refs):
        cells = row().astype(F32)
        count, channels = cells.shape
        cells = jnp.concatenate([cells, jnp.zeros((padded - count, channels), F32)], axis=0)
        start = index * padded
        columns_ref[start : start + padded, 0:channels] = pltpu.roll(cells, 1, 0).astype(BF16)
        columns_ref[start : start + padded, channels : 2 * channels] = cells.astype(BF16)
        columns_ref[start : start + padded, 2 * channels : 3 * channels] = pltpu.roll(
            cells, padded - 1, 0
        ).astype(BF16)


def stats_kernel(rows, info_ref, latents_ref, out_ref):
    info = Info(info_ref, rows)
    row_count, cols, channels = latents_ref.shape
    labels, widths = info.window(info.tile() * row_count, row_count)
    column = lax.broadcasted_iota(jnp.int32, (cols, 1), 0)
    cells = [
        jnp.where(column < widths[r], latents_ref[r].astype(F32), 0.0) for r in range(row_count)
    ]
    write_stats(out_ref, cells, labels, widths, info.videos, channels)


def hidden_kernel(
    rows, info_ref, before_ref, latents_ref, after_ref, stats_ref, gain_ref, shift_ref, out_ref
):
    info = Info(info_ref, rows)
    row_count, cols, _ = latents_ref.shape
    labels, widths = info.window(info.tile() * row_count - 1, row_count + 2)
    means, scales = norm_tables(stats_ref, gain_ref)
    column = lax.broadcasted_iota(jnp.int32, (cols, 1), 0)
    for r in range(row_count + 2):
        if r == 0:
            source = before_ref[0]
        elif r == row_count + 1:
            source = after_ref[0]
        else:
            source = latents_ref[r - 1]
        mean = pick(means, labels[r], info.videos)
        scale = pick(scales, labels[r], info.videos)
        normed = (source.astype(F32) - mean) * scale + shift_ref[...]
        active = normed / (1.0 + jnp.exp(-normed))
        out_ref[r] = jnp.where(column < widths[r], active, 0.0).astype(BF16)


def conv_kernel(rows, taps, info_ref, *rest):
    hidden_refs, rest = rest[:taps], rest[taps:]
    weight_ref, latents_ref, bias_ref, own_ref, *rest = rest
    row_count, cols, channels = latents_ref.shape
    pair_refs, rest = rest[: row_count // 2], rest[row_count // 2 :]
    edge_ref, stats_ref, columns_ref, total_ref = rest
    info = Info(info_ref, rows)
    step = pl.program_id(0)
    tap = lax.rem(step, 3)
    near_rows = row_count + 2
    padded = columns_ref.shape[0] // near_rows
    labels, widths = info.window(info.tile() * row_count - 1, near_rows)

    for back, hidden_ref in enumerate(hidden_refs):

        @pl.when(step == 3 * back)
        def _():
            build_columns(
                columns_ref,
                [functools.partial(hidden_ref.__getitem__, r) for r in range(near_rows)],
            )

    start = pl.multiple_of(tap * padded, 16)
    product = jnp.dot(
        columns_ref[pl.ds(start, row_count * padded), :], weight_ref[0], preferred_element_type=F32
    )
    for r in range(row_count):
        lo, hi = r * padded, (r + 1) * padded
        near = jnp.where(tap == 0, labels[r], jnp.where(tap == 1, labels[r + 1], labels[r + 2]))
        part = jnp.where(near == labels[r + 1], product[lo:hi], 0.0)
        total_ref[lo:hi, :] = jnp.where(step == 0, part, total_ref[lo:hi, :] + part)

    @pl.when(step == 3 * taps - 1)
    def _():
        column = lax.broadcasted_iota(jnp.int32, (cols, 1), 0)
        cells = []
        for r in range(row_count):
            branch = total_ref[r * padded : r * padded + cols, :]
            value = latents_ref[r].astype(F32) + branch + bias_ref[...]
            value = jnp.where(column < widths[r + 1], value, 0.0).astype(BF16)
            cells.append(value.astype(F32))
        for pair, pair_ref in enumerate(pair_refs):
            both = jnp.concatenate(cells[2 * pair : 2 * pair + 2], axis=0).astype(BF16)
            own_ref[pair] = both
            pair_ref[0] = both
        odd = lax.rem(info.tile(), 2) == 1
        edge_ref[0] = jnp.where(odd, cells[-1], cells[0]).astype(BF16)
        write_stats(stats_ref, cells, labels[1:-1], widths[1:-1], info.videos, channels)


def split_rows(pairs_ref):
    cols = pairs_ref.shape[1] // 2
    cells = []
    for pair in range(pairs_ref.shape[0]):
        both = pairs_ref[pair].astype(F32)
        cells += [both[:cols], both[cols:]]
    return cells


def query_kernel(
    rows, info_ref, own_ref, other_ref, edge_ref, other_edge_ref, stats_ref, gain_ref, shift_ref,
    weight_ref, bias_ref, queries_ref, constant_ref,
):
    info = Info(info_ref, rows)
    pairs, double, channels = own_ref.shape
    cols = double // 2
    row_count = 2 * pairs
    odd = lax.rem(info.tile(), 2)
    labels, widths = info.window((info.tile() - odd) * row_count - 1, 2 * row_count + 2)
    means, scales = norm_tables(stats_ref, gain_ref)
    column = lax.broadcasted_iota(jnp.int32, (cols, 1), 0)
    own, other = split_rows(own_ref), split_rows(other_ref)
    edge, other_edge = edge_ref[0].astype(F32), other_edge_ref[0].astype(F32)
    even_order = [edge] + own + other + [other_edge]
    odd_order = [other_edge] + other + own + [edge]
    cells = []
    for r in range(2 * row_count + 2):
        values = jnp.where(odd == 1, odd_order[r], even_order[r])
        mean = pick(means, labels[r], info.videos)
        scale = pick(scales, labels[r], info.videos)
        normed = (values - mean) * scale + shift_ref[...]
        cells.append(jnp.where(column < widths[r], normed, 0.0))
    cells = jnp.concatenate(cells, axis=0).astype(BF16)
    queries = (
        jnp.dot(cells, weight_ref[:, 0:channels], preferred_element_type=F32)
        + bias_ref[:, 0:channels]
    ).astype(BF16)
    factor = channels ** (-0.5) * math.log2(math.e)
    turned = lax.dot_general(
        queries, weight_ref[:, channels : 2 * channels], (((1,), (1,)), ((), ())),
        preferred_element_type=F32,
    )
    queries_ref[...] = (turned * factor).astype(BF16)
    constant = jnp.sum(
        queries.astype(F32) * bias_ref[:, channels : 2 * channels], axis=1, keepdims=True
    )
    constant_ref[...] = jnp.broadcast_to(constant * factor, constant_ref.shape)


def attend_kernel(rows, chunk, chunks, info_ref, *rest):
    stats_ref, gain_ref, shift_ref, queries_ref, constant_ref, codes_ref, canvas_ref, *rest = rest
    first, last = chunk == 0, chunk == chunks - 1
    if not first:
        old_peak_ref, old_sum_ref, old_total_ref, *rest = rest
    out_refs, (keys_ref, total_ref) = rest[:3], rest[3:]
    info = Info(info_ref, rows)
    pairs, double, channels = canvas_ref.shape
    cols = double // 2
    block = codes_ref.shape[-1]
    per_block = block // double
    row_count = 2 * chunks
    cells = queries_ref.shape[0]
    odd = lax.rem(info.tile(), 2)
    first_row = (info.tile() - odd) * row_count
    labels = [info.label(first_row - 1 + r) for r in range(2 * row_count + 2)]
    lowest, highest = labels[1], labels[-2]
    means, scales = norm_tables(stats_ref, gain_ref)

    def pair_labels(pair):
        row = (2 * pair + odd) * row_count + 2 * chunk
        return [info.label(row), info.label(row + 1)]

    def count(pair, carried):
        below, upto = carried
        upper, lower = pair_labels(pair)
        return (
            below + (lower < lowest).astype(jnp.int32),
            upto + (upper <= highest).astype(jnp.int32),
        )

    first_pair, end_pair = lax.fori_loop(0, pairs, count, (jnp.int32(0), jnp.int32(0)))
    first_block = first_pair // per_block
    end_block = (end_pair + per_block - 1) // per_block

    def normalise(pair, carried):
        near = pair_labels(pair)
        both = canvas_ref[pair].astype(F32)
        halves = []
        for half in range(2):
            mean = pick(means, near[half], info.videos)
            scale = pick(scales, near[half], info.videos)
            halves.append((both[half * cols : (half + 1) * cols] - mean) * scale + shift_ref[...])
        start = pl.multiple_of(pair * double, 16)
        keys_ref[pl.ds(start, double), :] = jnp.concatenate(halves, axis=0).astype(BF16)
        return carried

    lax.fori_loop(first_block * per_block, end_block * per_block, normalise, jnp.int32(0))

    query_label = jnp.concatenate(
        [jnp.zeros((cols, 1), F32) + label.astype(F32) for label in labels], axis=0
    )
    constant = constant_ref[:, 0:1]
    if first:
        total_ref[...] = jnp.zeros(total_ref.shape, F32)
        state = (jnp.full((cells, 1), LOWEST, F32), jnp.zeros((cells, 1), F32))
    else:
        total_ref[...] = old_total_ref[...]
        state = (old_peak_ref[:, 0:1], old_sum_ref[:, 0:1])

    def step(index, carried):
        largest, denominator = carried
        start = pl.multiple_of(index * block, 16)
        keys = keys_ref[pl.ds(start, block), :]
        scores = lax.dot_general(
            queries_ref[...], keys, (((1,), (1,)), ((), ())), preferred_element_type=F32
        )
        scores = jnp.where(codes_ref[chunk, index] == query_label, scores, MASKED)
        peak = jnp.maximum(largest, jnp.max(scores, axis=1, keepdims=True) + constant)
        weights = jnp.exp2(scores - (peak - constant))
        factor = jnp.exp2(largest - peak)
        denominator = denominator * factor + jnp.sum(weights, axis=1, keepdims=True)
        total_ref[...] = total_ref[...] * factor + jnp.dot(
            weights.astype(BF16), keys, preferred_element_type=F32
        )
        return peak, denominator

    peak, denominator = lax.fori_loop(first_block, end_block, step, state)
    if not last:
        peak_ref, sum_ref, out_total_ref = out_refs
        peak_ref[...] = jnp.broadcast_to(peak, peak_ref.shape)
        sum_ref[...] = jnp.broadcast_to(denominator, sum_ref.shape)
        out_total_ref[...] = total_ref[...]
        return
    mean_ref, level_ref, sent_ref = out_refs
    some = denominator > 0.0
    safe = jnp.where(some, denominator, 1.0)
    total_ref[...] = total_ref[...] / safe
    level = jnp.where(some, peak + jnp.log2(safe), LOWEST)
    needed = row_count + 2
    span = row_count * cols
    mine = pl.multiple_of(odd * span, 16)
    yours = pl.multiple_of((1 - odd) * span, 16)
    mean_ref[...] = total_ref[pl.ds(mine, needed * cols), :]
    level_mine = jnp.where(odd == 1, level[span:], level[: needed * cols])
    level_yours = jnp.where(odd == 1, level[: needed * cols], level[span:])
    level_ref[...] = jnp.broadcast_to(level_mine, level_ref.shape)
    lane = lax.broadcasted_iota(jnp.int32, (cols, channels), 1)
    packed = jnp.zeros((cols, channels), F32)
    for r in range(needed):
        sent_ref[r] = total_ref[pl.ds(yours + r * cols, cols), :].astype(BF16)
        left = level_yours[r * cols : (r + 1) * cols]
        for part in range(3):
            rounded = left.astype(BF16).astype(F32)
            packed = jnp.where(lane == 3 * r + part, rounded, packed)
            left = left - rounded
    sent_ref[needed] = packed.astype(BF16)


def finish_kernel(
    rows, info_ref, mean_ref, level_ref, received_ref, own_ref, other_ref, edge_ref, triple_ref,
    triple_bias_ref, output_ref, output_bias_ref, weight_ref, bias_ref, out_ref, columns_ref,
    wide_ref,
):
    info = Info(info_ref, rows)
    pairs, double, channels = own_ref.shape
    cols = double // 2
    row_count = 2 * pairs
    near_rows = row_count + 2
    padded = columns_ref.shape[0] // near_rows
    parts_out = wide_ref.shape[0]
    out_channels = out_ref.shape[-1]
    odd = lax.rem(info.tile(), 2) == 1
    labels, widths = info.window(info.tile() * row_count - 1, near_rows)
    means = []
    levels = received_ref[near_rows].astype(F32)
    for r in range(near_rows):
        mine = level_ref[r * cols : (r + 1) * cols, 0:1]
        yours = (levels[:, 3 * r : 3 * r + 1] + levels[:, 3 * r + 1 : 3 * r + 2]) + levels[
            :, 3 * r + 2 : 3 * r + 3
        ]
        peak = jnp.maximum(mine, yours)
        weight, other_weight = jnp.exp2(mine - peak), jnp.exp2(yours - peak)
        share = weight / (weight + other_weight)
        received = received_ref[r].astype(F32)
        means.append(
            mean_ref[r * cols : (r + 1) * cols, :] * share + received * (1.0 - share)
        )
    mean_cell = jnp.concatenate(means, axis=0).astype(BF16)
    mixed = (
        jnp.dot(mean_cell, triple_ref[:, 2 * channels :], preferred_element_type=F32)
        + triple_bias_ref[:, 2 * channels :]
    ).astype(BF16)
    attended = jnp.dot(mixed, output_ref[...], preferred_element_type=F32) + output_bias_ref[...]
    own, other = split_rows(own_ref), split_rows(other_ref)
    edge = edge_ref[0].astype(F32)
    residual = (
        [jnp.where(odd, other[-1], edge)] + own + [jnp.where(odd, edge, other[0])]
    )
    column = lax.broadcasted_iota(jnp.int32, (cols, 1), 0)
    sources = []
    for r in range(near_rows):
        value = residual[r] + attended[r * cols : (r + 1) * cols]
        value = jnp.where(column < widths[r], value, 0.0).astype(BF16)
        sources.append(lambda value=value: value)
    build_columns(columns_ref, sources)
    span = row_count * padded
    wide_column = lax.broadcasted_iota(jnp.int32, (2 * cols, 1), 0)
    for down in range(2):
        for right in range(2):
            lanes = slice(right * channels, (right + 2) * channels)
            products = [
                jnp.dot(
                    columns_ref[(down + tap) * padded : (down + tap) * padded + span, lanes],
                    weight_ref[down, tap, right],
                    preferred_element_type=F32,
                )
                for tap in range(2)
            ]
            rim, same = products[down], products[1 - down]
            for r in range(row_count):
                lo, hi = r * padded, r * padded + cols
                near = labels[r + 2 * down]
                value = same[lo:hi] + jnp.where(near == labels[r + 1], rim[lo:hi], 0.0)
                for part in range(parts_out):
                    wide_ref[part, 2 * r + down, pl.ds(right, cols, 2), :] = value[
                        :, part * LANES : (part + 1) * LANES
                    ]
    for r in range(2 * row_count):
        valid = wide_column < 2 * widths[r // 2 + 1]
        for part in range(parts_out):
            lo, hi = part * LANES, min((part + 1) * LANES, out_channels)
            value = wide_ref[part, r, :, 0 : hi - lo] + bias_ref[:, lo:hi]
            out_ref[r, :, lo:hi] = jnp.where(valid, value, 0.0).astype(BF16)


def merge_stats(mine, other):
    count = mine[0] + other[0]
    safe = jnp.maximum(count, 1.0)
    off = other[1] - mine[1]
    mean = mine[1] + off * (other[0] / safe)
    spread = mine[2] + other[2] + off * off * (mine[0] * other[0] / safe)
    return jnp.stack([count, mean, spread])


def combined_weight(weight):
    wide = jnp.pad(weight.astype(F32), ((0, 0),) * 3 + ((0, -weight.shape[-1] % LANES),))
    rows = jnp.stack(
        [
            jnp.stack([wide[0], wide[1] + wide[2]]),
            jnp.stack([wide[0] + wide[1], wide[2]]),
        ]
    )
    left = jnp.concatenate([rows[:, :, 0], rows[:, :, 1] + rows[:, :, 2]], axis=2)
    right = jnp.concatenate([rows[:, :, 0] + rows[:, :, 1], rows[:, :, 2]], axis=2)
    return jnp.stack([left, right], axis=2).astype(BF16)


def shards(
    tiles,
    frames,
    latents,
    row_video,
    video_cols,
    first_gain,
    first_shift,
    conv_weight,
    conv_bias,
    second_gain,
    second_shift,
    triple_weight,
    triple_bias,
    output_weight,
    output_bias,
    upsample_weight,
    upsample_bias,
):
    row_count, frame_count, cols, channels = latents.shape
    assert frame_count == 1 and row_count == 2 * CHUNKS and tiles % 4 == 0
    out_channels = upsample_weight.shape[-1]
    rows = row_count * tiles
    cells = row_count * cols
    padded = -(-(cols + 1) // 16) * 16
    near_rows = row_count + 2
    halves = tiles // 2
    source = latents.reshape(row_count, cols, channels)
    tile = lax.axis_index("tile").astype(jnp.int32)
    info = jnp.concatenate([jnp.reshape(tile, (1,)), row_video, video_cols])

    def row(vector):
        return vector.reshape(1, -1)

    def shape(*dims, dtype=BF16):
        return jax.ShapeDtypeStruct(dims, dtype)

    def call(kernel, operands, out_shape, scratch=(), **kwargs):
        many = isinstance(out_shape, tuple)
        return pl.pallas_call(
            kernel,
            out_shape=out_shape,
            in_specs=[SMEM_SPEC] + [VMEM_SPEC] * len(operands),
            out_specs=(VMEM_SPEC,) * len(out_shape) if many else VMEM_SPEC,
            scratch_shapes=list(scratch),
            compiler_params=params(),
            **kwargs,
        )(info, *operands)

    before = lax.ppermute(source[row_count - 1 :], "tile", [(i, i + 1) for i in range(tiles - 1)])
    after = lax.ppermute(source[:1], "tile", [(i + 1, i) for i in range(tiles - 1)])
    stats_shape = shape(3, SLOTS, LANES, dtype=F32)
    stats = call(
        functools.partial(stats_kernel, rows), [source], stats_shape,
        cost_estimate=cost(cells * channels * 2, 2 * cells * channels), name="first_stats",
    )
    stats, before, after = lax.optimization_barrier((stats, before, after))

    def over_tiles(stats):
        bit = 1
        while bit < tiles:
            other = lax.ppermute(stats, "tile", [(i, i ^ bit) for i in range(tiles)])
            stats = merge_stats(stats, other)
            bit *= 2
        return stats

    stats = over_tiles(stats)
    hidden = call(
        functools.partial(hidden_kernel, rows),
        [before, source, after, stats, row(first_gain), row(first_shift)],
        shape(near_rows, cols, channels),
        cost_estimate=cost(cells * channels * 10, 5 * cells * channels, cells * channels),
        name="hidden",
    )

    taps = min(3, frames)
    context = [hidden] + [
        lax.ppermute(hidden, "frame", [(i, i + by) for i in range(frames - by)])
        for by in range(1, taps)
    ]

    def whole(*dims):
        return pl.BlockSpec(dims, lambda step: (0,) * len(dims))

    pair_dims = (1, 2 * cols, channels)
    own, *rest = pl.pallas_call(
        functools.partial(conv_kernel, rows, taps),
        grid=(3 * taps,),
        out_shape=(
            [shape(CHUNKS, 2 * cols, channels)]
            + [shape(*pair_dims)] * CHUNKS
            + [shape(1, cols, channels), stats_shape]
        ),
        in_specs=(
            [SMEM_SPEC]
            + [whole(near_rows, cols, channels)] * taps
            + [
                pl.BlockSpec(
                    (1, 3 * channels, channels),
                    lambda step: (3 * (2 - step // 3) + lax.rem(step, 3), 0, 0),
                ),
                whole(row_count, cols, channels),
                whole(1, channels),
            ]
        ),
        out_specs=(
            [whole(CHUNKS, 2 * cols, channels)]
            + [whole(*pair_dims)] * CHUNKS
            + [whole(1, cols, channels), whole(3, SLOTS, LANES)]
        ),
        scratch_shapes=[
            pltpu.VMEM((near_rows * padded, 3 * channels), BF16),
            pltpu.VMEM((row_count * padded, channels), F32),
        ],
        compiler_params=pltpu.CompilerParams(vmem_limit_bytes=CONV_VMEM_BYTES),
        cost_estimate=cost(
            9 * taps * cells * channels * channels, 18 * taps * channels * channels
        ),
        name="conv",
    )(info, *context, conv_weight.reshape(9, 3 * channels, channels), source, row(conv_bias))
    pieces, edge, stats = rest[:CHUNKS], rest[CHUNKS], rest[CHUNKS + 1]

    groups = [list(range(side, tiles, 2)) for side in range(2)]
    canvas = [
        lax.all_gather(piece, "tile", axis=0, tiled=True, axis_index_groups=groups)
        for piece in pieces
    ]
    neighbour = [(i, i ^ 1) for i in range(tiles)]
    outer = [(i, i - 1 if i % 2 == 0 else i + 1) for i in range(tiles)]
    outer = [(i, j) for i, j in outer if 0 <= j < tiles]
    stats = over_tiles(stats)
    far_edge = lax.ppermute(edge, "tile", outer)
    other = lax.ppermute(own, "tile", neighbour)
    other_edge = lax.ppermute(far_edge, "tile", neighbour)
    gain, shift = row(second_gain), row(second_shift)
    query_cells = (2 * row_count + 2) * cols
    queries, constant = call(
        functools.partial(query_kernel, rows),
        [
            own, other, far_edge, other_edge, stats, gain, shift, triple_weight, row(triple_bias)
        ],
        (shape(query_cells, channels), shape(query_cells, LANES, dtype=F32)),
        cost_estimate=cost(2 * query_cells * channels * channels, 4 * query_cells * channels),
        name="queries",
    )
    widths = jnp.sum(
        jnp.where(
            row_video[:, None] == jnp.arange(video_cols.shape[0], dtype=jnp.int32)[None, :],
            video_cols[None, :],
            0,
        ),
        axis=1,
    )
    valid = jnp.arange(cols, dtype=jnp.int32)[None, :] < widths[:, None]
    codes = jnp.where(valid, row_video[:, None], -2).astype(F32)
    codes = codes.reshape(halves, 2, CHUNKS, 2 * cols)
    codes = lax.dynamic_index_in_dim(codes, tile % 2, axis=1, keepdims=False)
    codes = jnp.transpose(codes, (1, 0, 2)).reshape(CHUNKS, halves // 2, 1, 4 * cols)
    state = []
    for chunk in range(CHUNKS):
        last = chunk == CHUNKS - 1
        if last:
            outs = (
                shape(near_rows * cols, channels, dtype=F32),
                shape(near_rows * cols, LANES, dtype=F32),
                shape(near_rows + 1, cols, channels),
            )
        else:
            outs = (
                shape(query_cells, LANES, dtype=F32),
                shape(query_cells, LANES, dtype=F32),
                shape(query_cells, channels, dtype=F32),
            )
        keys = halves * 2 * cols
        state = call(
            functools.partial(attend_kernel, rows, chunk, CHUNKS),
            [stats, gain, shift, queries, constant, codes, canvas[chunk], *state],
            outs,
            scratch=[
                pltpu.VMEM((keys, channels), BF16),
                pltpu.VMEM((query_cells, channels), F32),
            ],
            cost_estimate=cost(
                2 * query_cells * keys * channels, 2 * keys * channels, query_cells * keys
            ),
            name="attend_last" if last else "attend_part",
        )
    mean, level, sent = state

    received = lax.ppermute(sent, "tile", neighbour)
    decoded = call(
        functools.partial(finish_kernel, rows),
        [
            mean, level, received, own, other, far_edge, triple_weight, row(triple_bias),
            output_weight, row(output_bias), combined_weight(upsample_weight), row(upsample_bias),
        ],
        shape(2 * row_count, 2 * cols, out_channels),
        scratch=[
            pltpu.VMEM((near_rows * padded, 3 * channels), BF16),
            pltpu.VMEM((-(-out_channels // LANES), 2 * row_count, 2 * cols, LANES), F32),
        ],
        cost_estimate=cost(16 * cells * channels * out_channels, 8 * cells * out_channels),
        name="finish",
    )
    return decoded.reshape(2 * row_count, 1, 2 * cols, out_channels)


def solution(mesh):
    sizes = dict(mesh.shape)
    in_specs = (P("tile", "frame", None, None),) + (P(),) * 14
    out_specs = P("tile", "frame", None, None)
    body = functools.partial(shards, sizes["tile"], sizes["frame"])
    return jax.shard_map(body, mesh=mesh, in_specs=in_specs, out_specs=out_specs, check_vma=False)
```

```python
import functools
import math

import jax
import jax.numpy as jnp
from jax import lax
from jax.experimental import pallas as pl
from jax.experimental.pallas import tpu as pltpu
from jax.sharding import PartitionSpec as P

GROUPS = 32
EPSILON = 1e-05
MASKED = -1e30
LOWEST = -5e29
HIGHEST = lax.Precision.HIGHEST
SLOTS = 8
LANES = 128
VMEM_BYTES = 24 * 1024 * 1024
CONV_VMEM_BYTES = 56 * 1024 * 1024
F32 = jnp.float32
BF16 = jnp.bfloat16

SMEM_SPEC = pl.BlockSpec(memory_space=pltpu.SMEM)
VMEM_SPEC = pl.BlockSpec(memory_space=pltpu.VMEM)
HBM_SPEC = pl.BlockSpec(memory_space=pltpu.HBM)


def cost(macs, nbytes, exps=0):
    return pl.CostEstimate(flops=2 * macs, bytes_accessed=nbytes, transcendentals=exps)


def params():
    return pltpu.CompilerParams(vmem_limit_bytes=VMEM_BYTES)


def member_matrix(channels):
    per_group = channels // GROUPS
    group = lax.broadcasted_iota(jnp.int32, (LANES, channels), 0) * per_group
    channel = lax.broadcasted_iota(jnp.int32, (LANES, channels), 1)
    return jnp.where((channel >= group) & (channel < group + per_group), 1.0, 0.0).astype(F32)


def to_groups(values, member):
    return lax.dot_general(
        values, member, (((1,), (1,)), ((), ())), precision=HIGHEST, preferred_element_type=F32
    )


def to_channels(values, member):
    return jnp.dot(values, member, precision=HIGHEST, preferred_element_type=F32)


class Info:
    def __init__(self, ref, rows):
        self.ref, self.rows = ref, rows
        self.videos = ref.shape[0] - 1 - rows

    def tile(self):
        return self.ref[0]

    def label(self, row):
        inside = (row >= 0) & (row < self.rows)
        return jnp.where(inside, self.ref[1 + jnp.clip(row, 0, self.rows - 1)], -1)

    def width(self, label):
        return jnp.where(label >= 0, self.ref[1 + self.rows + jnp.maximum(label, 0)], 0)

    def window(self, first, count):
        labels = [self.label(first + r) for r in range(count)]
        return labels, [self.width(label) for label in labels]


def pick(table, label, videos):
    chosen = table[0:1]
    for video in range(1, videos):
        chosen = jnp.where(label == video, table[video : video + 1], chosen)
    return chosen


def norm_tables(stats_ref, gain_ref):
    member = member_matrix(gain_ref.shape[1])
    counts = jnp.maximum(stats_ref[0], 1.0)
    scale = lax.rsqrt(stats_ref[2] / counts + EPSILON)
    return to_channels(stats_ref[1], member), to_channels(scale, member) * gain_ref[...]


def write_stats(out_ref, rows, labels, widths, videos, channels):
    member = member_matrix(channels)
    per_group = channels // GROUPS
    cols = rows[0].shape[0]
    slot = lax.broadcasted_iota(jnp.int32, (SLOTS, 1), 0)
    column = lax.broadcasted_iota(jnp.int32, (cols, 1), 0)
    sums = jnp.zeros((SLOTS, channels), F32)
    counts = jnp.zeros((SLOTS, 1), F32)
    for index, row in enumerate(rows):
        sums = jnp.where(slot == index, jnp.sum(row, axis=0, keepdims=True), sums)
        counts = jnp.where(slot == index, (widths[index] * per_group).astype(F32), counts)
    means = to_groups(sums, member) / jnp.maximum(counts, 1.0)
    means_wide = to_channels(means, member)
    squares = jnp.zeros((SLOTS, channels), F32)
    for index, row in enumerate(rows):
        centered = jnp.where(column < widths[index], row - means_wide[index : index + 1], 0.0)
        squares = jnp.where(
            slot == index, jnp.sum(centered * centered, axis=0, keepdims=True), squares
        )
    spreads = to_groups(squares, member)
    out_ref[...] = jnp.zeros(out_ref.shape, F32)
    for video in range(videos):
        total = jnp.zeros((1, LANES), F32)
        count = jnp.zeros((1, LANES), F32)
        for index in range(len(rows)):
            mine = labels[index] == video
            row_count = counts[index : index + 1]
            total = total + jnp.where(mine, means[index : index + 1] * row_count, 0.0)
            count = count + jnp.where(mine, row_count, 0.0)
        mean = total / jnp.maximum(count, 1.0)
        spread = jnp.zeros((1, LANES), F32)
        for index in range(len(rows)):
            off = means[index : index + 1] - mean
            part = spreads[index : index + 1] + counts[index : index + 1] * off * off
            spread = spread + jnp.where(labels[index] == video, part, 0.0)
        out_ref[0, video : video + 1, :] = count
        out_ref[1, video : video + 1, :] = mean
        out_ref[2, video : video + 1, :] = spread


def build_columns(columns_ref, row_refs):
    padded = columns_ref.shape[0] // len(row_refs)
    for index, row in enumerate(row_refs):
        cells = row().astype(F32)
        count, channels = cells.shape
        cells = jnp.concatenate([cells, jnp.zeros((padded - count, channels), F32)], axis=0)
        start = index * padded
        columns_ref[start : start + padded, 0:channels] = pltpu.roll(cells, 1, 0).astype(BF16)
        columns_ref[start : start + padded, channels : 2 * channels] = cells.astype(BF16)
        columns_ref[start : start + padded, 2 * channels : 3 * channels] = pltpu.roll(
            cells, padded - 1, 0
        ).astype(BF16)


def stats_kernel(rows, info_ref, latents_ref, out_ref):
    info = Info(info_ref, rows)
    row_count, cols, channels = latents_ref.shape
    labels, widths = info.window(info.tile() * row_count, row_count)
    column = lax.broadcasted_iota(jnp.int32, (cols, 1), 0)
    cells = [
        jnp.where(column < widths[r], latents_ref[r].astype(F32), 0.0) for r in range(row_count)
    ]
    write_stats(out_ref, cells, labels, widths, info.videos, channels)


def hidden_kernel(
    rows, info_ref, before_ref, latents_ref, after_ref, stats_ref, gain_ref, shift_ref, out_ref
):
    info = Info(info_ref, rows)
    row_count, cols, _ = latents_ref.shape
    labels, widths = info.window(info.tile() * row_count - 1, row_count + 2)
    means, scales = norm_tables(stats_ref, gain_ref)
    column = lax.broadcasted_iota(jnp.int32, (cols, 1), 0)
    for r in range(row_count + 2):
        if r == 0:
            source = before_ref[0]
        elif r == row_count + 1:
            source = after_ref[0]
        else:
            source = latents_ref[r - 1]
        mean = pick(means, labels[r], info.videos)
        scale = pick(scales, labels[r], info.videos)
        normed = (source.astype(F32) - mean) * scale + shift_ref[...]
        active = normed / (1.0 + jnp.exp(-normed))
        out_ref[r] = jnp.where(column < widths[r], active, 0.0).astype(BF16)


def conv_kernel(rows, taps, info_ref, *rest):
    hidden_refs, rest = rest[:taps], rest[taps:]
    latents_ref, bias_ref, weight_ref, own_ref, stats_ref, columns_ref, held_ref, sems = rest
    row_count, cols, channels = latents_ref.shape
    info = Info(info_ref, rows)
    near_rows = row_count + 2
    padded = columns_ref.shape[1] // near_rows
    copies = [
        pltpu.make_async_copy(
            weight_ref.at[3 * (2 - step // 3) + step % 3], held_ref.at[step], sems.at[step]
        )
        for step in range(3 * taps)
    ]
    for copy in copies:
        copy.start()
    labels, widths = info.window(info.tile() * row_count - 1, near_rows)
    total = [0.0] * row_count
    for back, hidden_ref in enumerate(hidden_refs):
        build_columns(
            columns_ref.at[back],
            [functools.partial(hidden_ref.__getitem__, r) for r in range(near_rows)],
        )
    for back in range(taps):
        for tap in range(3):
            copies[3 * back + tap].wait()
            product = jnp.dot(
                columns_ref[back, tap * padded : (tap + row_count) * padded, :],
                held_ref[3 * back + tap],
                preferred_element_type=F32,
            )
            for r in range(row_count):
                part = product[r * padded : r * padded + cols]
                if tap != 1:
                    part = jnp.where(labels[r + tap] == labels[r + 1], part, 0.0)
                total[r] = total[r] + part
    column = lax.broadcasted_iota(jnp.int32, (cols, 1), 0)
    cells = []
    for r in range(row_count):
        value = latents_ref[r].astype(F32) + total[r] + bias_ref[...]
        value = jnp.where(column < widths[r + 1], value, 0.0).astype(BF16)
        cells.append(value.astype(F32))
    for pair in range(row_count // 2):
        own_ref[pair] = jnp.concatenate(cells[2 * pair : 2 * pair + 2], axis=0).astype(BF16)
    write_stats(stats_ref, cells, labels[1:-1], widths[1:-1], info.videos, channels)


def split_rows(pairs_ref):
    cols = pairs_ref.shape[1] // 2
    cells = []
    for pair in range(pairs_ref.shape[0]):
        both = pairs_ref[pair].astype(F32)
        cells += [both[:cols], both[cols:]]
    return cells


def query_kernel(
    rows, info_ref, own_ref, other_ref, stats_ref, gain_ref, shift_ref, weight_ref, bias_ref,
    *out_refs,
):
    info = Info(info_ref, rows)
    pairs, double, channels = own_ref.shape
    cols = double // 2
    row_count = 2 * pairs
    span = row_count * cols
    means, scales = norm_tables(stats_ref, gain_ref)
    column = lax.broadcasted_iota(jnp.int32, (cols, 1), 0)
    cells = []
    for tile, pairs_ref in ((info.tile(), own_ref), (info.tile() ^ 1, other_ref)):
        labels, widths = info.window(tile * row_count, row_count)
        for r, values in enumerate(split_rows(pairs_ref)):
            mean = pick(means, labels[r], info.videos)
            scale = pick(scales, labels[r], info.videos)
            normed = (values - mean) * scale + shift_ref[...]
            cells.append(jnp.where(column < widths[r], normed, 0.0))
    cells = jnp.concatenate(cells, axis=0).astype(BF16)
    queries = (
        jnp.dot(cells, weight_ref[:, 0:channels], preferred_element_type=F32)
        + bias_ref[:, 0:channels]
    ).astype(BF16)
    factor = channels ** (-0.5) * math.log2(math.e)
    turned = lax.dot_general(
        queries, weight_ref[:, channels : 2 * channels], (((1,), (1,)), ((), ())),
        preferred_element_type=F32,
    )
    turned = (turned * factor).astype(BF16)
    constant = jnp.sum(
        queries.astype(F32) * bias_ref[:, channels : 2 * channels], axis=1, keepdims=True
    )
    constant = jnp.broadcast_to(constant * factor, (2 * span, LANES))
    for side in range(2):
        out_refs[2 * side][...] = turned[side * span : (side + 1) * span]
        out_refs[2 * side + 1][...] = constant[side * span : (side + 1) * span]


def attend_kernel(rows, masks, yours, first, last, info_ref, *rest):
    stats_ref, gain_ref, shift_ref, queries_ref, constant_ref, *rest = rest
    block_refs, rest = rest[: len(masks)], rest[len(masks) :]
    if not first:
        old_peak_ref, old_sum_ref, old_total_ref, *rest = rest
    if last:
        *out_refs, keys_ref, peak_ref, sum_ref, total_ref = rest
    else:
        peak_ref, sum_ref, total_ref, keys_ref = rest
    info = Info(info_ref, rows)
    pairs, double, channels = block_refs[0].shape
    cols = double // 2
    row_count = 2 * pairs
    span = row_count * cols
    tile = info.tile()
    labels = info.window((tile ^ 1 if yours else tile) * row_count, row_count)[0]
    means, scales = norm_tables(stats_ref, gain_ref)
    if first:
        peak_ref[...] = jnp.full(peak_ref.shape, LOWEST, F32)
        sum_ref[...] = jnp.zeros(sum_ref.shape, F32)
        total_ref[...] = jnp.zeros(total_ref.shape, F32)
    else:
        peak_ref[...] = old_peak_ref[...]
        sum_ref[...] = old_sum_ref[...]
        total_ref[...] = old_total_ref[...]
    query_label = jnp.concatenate(
        [jnp.zeros((cols, 1), F32) + label.astype(F32) for label in labels], axis=0
    )
    position = lax.broadcasted_iota(jnp.int32, (1, span), 1)

    for mask, block_ref in zip(masks, block_refs):
        near, widths = info.window((tile ^ (2 * mask)) * row_count, row_count)

        @pl.when((near[-1] >= labels[0]) & (near[0] <= labels[-1]))
        def _(near=near, widths=widths, block_ref=block_ref):
            code = jnp.full((1, span), -2.0, F32)
            for r in range(row_count):
                inside = (position >= r * cols) & (position < r * cols + widths[r])
                code = jnp.where(inside, near[r].astype(F32), code)
            for pair in range(pairs):
                both = block_ref[pair].astype(F32)
                halves = []
                for half in range(2):
                    label = near[2 * pair + half]
                    mean = pick(means, label, info.videos)
                    scale = pick(scales, label, info.videos)
                    values = both[half * cols : (half + 1) * cols]
                    halves.append((values - mean) * scale + shift_ref[...])
                keys_ref[pair * double : (pair + 1) * double, :] = jnp.concatenate(
                    halves, axis=0
                ).astype(BF16)
            constant = constant_ref[:, 0:1]
            largest = peak_ref[:, 0:1]
            scores = lax.dot_general(
                queries_ref[...], keys_ref[...], (((1,), (1,)), ((), ())),
                preferred_element_type=F32,
            )
            scores = jnp.where(code == query_label, scores, MASKED)
            peak = jnp.maximum(largest, jnp.max(scores, axis=1, keepdims=True) + constant)
            weights = jnp.exp2(scores - (peak - constant))
            factor = jnp.exp2(largest - peak)
            peak_ref[...] = jnp.broadcast_to(peak, peak_ref.shape)
            sums = sum_ref[:, 0:1] * factor + jnp.sum(weights, axis=1, keepdims=True)
            sum_ref[...] = jnp.broadcast_to(sums, sum_ref.shape)
            total_ref[...] = total_ref[...] * factor + jnp.dot(
                weights.astype(BF16), keys_ref[...], preferred_element_type=F32
            )

    if not last:
        return
    denominator = sum_ref[:, 0:1]
    some = denominator > 0.0
    safe = jnp.where(some, denominator, 1.0)
    mean = total_ref[...] / safe
    level = jnp.where(some, peak_ref[:, 0:1] + jnp.log2(safe), LOWEST)
    if not yours:
        mean_ref, level_ref = out_refs
        mean_ref[...] = mean
        level_ref[...] = jnp.broadcast_to(level, level_ref.shape)
        return
    (sent_ref,) = out_refs
    sent_ref[0:span, :] = mean.astype(BF16)
    slots = sent_ref.shape[0] - span
    slot = lax.broadcasted_iota(jnp.int32, (slots, 1), 0)
    packed = jnp.zeros((slots, LANES), F32)
    for r in range(row_count):
        left = level[r * cols : (r + 1) * cols]
        left = jnp.sum(jnp.where(diagonal(cols), left, 0.0), axis=0, keepdims=True)
        for part in range(3):
            rounded = left.astype(BF16).astype(F32)
            packed = jnp.where(slot == 3 * r + part, rounded, packed)
            left = left - rounded
    sent_ref[span:, 0:LANES] = packed.astype(BF16)
    sent_ref[span:, LANES:] = jnp.zeros((slots, channels - LANES), BF16)


def diagonal(cols):
    return lax.broadcasted_iota(jnp.int32, (cols, LANES), 0) == lax.broadcasted_iota(
        jnp.int32, (cols, LANES), 1
    )


def finish_kernel(
    rows, info_ref, mean_ref, level_ref, received_ref, own_ref, triple_ref, triple_bias_ref,
    output_ref, output_bias_ref, out_ref, first_ref, last_ref,
):
    info = Info(info_ref, rows)
    row_count, cols, channels = out_ref.shape
    span = row_count * cols
    _, widths = info.window(info.tile() * row_count, row_count)
    received = received_ref[0:span, :].astype(F32)
    levels = received_ref[span:, 0:LANES].astype(F32)
    yours = []
    for r in range(row_count):
        level = levels[3 * r : 3 * r + 1] + levels[3 * r + 1 : 3 * r + 2]
        level = level + levels[3 * r + 2 : 3 * r + 3]
        yours.append(jnp.sum(jnp.where(diagonal(cols), level, 0.0), axis=1, keepdims=True))
    yours = jnp.concatenate(yours, axis=0)
    mine = level_ref[:, 0:1]
    peak = jnp.maximum(mine, yours)
    weight, other_weight = jnp.exp2(mine - peak), jnp.exp2(yours - peak)
    share = weight / (weight + other_weight)
    mean_cell = (mean_ref[...] * share + received * (1.0 - share)).astype(BF16)
    mixed = (
        jnp.dot(mean_cell, triple_ref[:, 2 * channels :], preferred_element_type=F32)
        + triple_bias_ref[:, 2 * channels :]
    ).astype(BF16)
    attended = jnp.dot(mixed, output_ref[...], preferred_element_type=F32) + output_bias_ref[...]
    column = lax.broadcasted_iota(jnp.int32, (cols, 1), 0)
    for r, before in enumerate(split_rows(own_ref)):
        value = before + attended[r * cols : (r + 1) * cols]
        value = jnp.where(column < widths[r], value, 0.0).astype(BF16)
        out_ref[r] = value
        if r == 0:
            first_ref[0] = value
        if r == row_count - 1:
            last_ref[0] = value


def fold_kernel(weight_ref, out_ref):
    channels = weight_ref.shape[-1]
    wide = [[weight_ref[a, b].astype(F32) for b in range(3)] for a in range(3)]

    def both(upper, lower):
        return [x + y for x, y in zip(upper, lower)]

    phases = [[wide[0], both(wide[1], wide[2])], [both(wide[0], wide[1]), wide[2]]]
    for down in range(2):
        for tap in range(2):
            left, middle, right = phases[down][tap]
            out_ref[down, tap, 0, :, 0:channels] = left.astype(BF16)
            out_ref[down, tap, 0, :, channels:] = (middle + right).astype(BF16)
            out_ref[down, tap, 1, :, 0:channels] = (left + middle).astype(BF16)
            out_ref[down, tap, 1, :, channels:] = right.astype(BF16)


def upsample_kernel(
    rows, info_ref, before_ref, own_ref, after_ref, weight_ref, bias_ref, out_ref, columns_ref,
    wide_ref,
):
    info = Info(info_ref, rows)
    row_count, cols, channels = own_ref.shape
    near_rows = row_count + 2
    padded = columns_ref.shape[0] // near_rows
    parts_out = wide_ref.shape[0]
    out_channels = out_ref.shape[-1]
    labels, widths = info.window(info.tile() * row_count - 1, near_rows)
    sources = [functools.partial(before_ref.__getitem__, 0)]
    sources += [functools.partial(own_ref.__getitem__, r) for r in range(row_count)]
    sources += [functools.partial(after_ref.__getitem__, 0)]
    build_columns(columns_ref, sources)
    span = row_count * padded
    wide_column = lax.broadcasted_iota(jnp.int32, (2 * cols, 1), 0)
    for down in range(2):
        for right in range(2):
            lanes = slice(right * channels, (right + 2) * channels)
            products = [
                lax.dot_general(
                    columns_ref[(down + tap) * padded : (down + tap) * padded + span, lanes],
                    weight_ref[down, tap, right],
                    (((1,), (1,)), ((), ())),
                    preferred_element_type=F32,
                )
                for tap in range(2)
            ]
            rim, same = products[down], products[1 - down]
            for r in range(row_count):
                lo, hi = r * padded, r * padded + cols
                near = labels[r + 2 * down]
                value = same[lo:hi] + jnp.where(near == labels[r + 1], rim[lo:hi], 0.0)
                for part in range(parts_out):
                    part_lo, part_hi = part * LANES, min((part + 1) * LANES, out_channels)
                    piece = value[:, part_lo:part_hi]
                    if part_hi - part_lo < LANES:
                        missing = LANES - (part_hi - part_lo)
                        piece = jnp.concatenate([piece, jnp.zeros((cols, missing), F32)], axis=1)
                    wide_ref[part, 2 * r + down, pl.ds(right, cols, 2), :] = piece
    for r in range(2 * row_count):
        valid = wide_column < 2 * widths[r // 2 + 1]
        for part in range(parts_out):
            lo, hi = part * LANES, min((part + 1) * LANES, out_channels)
            value = wide_ref[part, r, :, 0 : hi - lo] + bias_ref[:, lo:hi]
            out_ref[r, :, lo:hi] = jnp.where(valid, value, 0.0).astype(BF16)


def merge_stats(mine, other):
    count = mine[0] + other[0]
    safe = jnp.maximum(count, 1.0)
    off = other[1] - mine[1]
    mean = mine[1] + off * (other[0] / safe)
    spread = mine[2] + other[2] + off * off * (mine[0] * other[0] / safe)
    return jnp.stack([count, mean, spread])


def gather_plan(tiles):
    if tiles == 16:
        return {1: (0, 1), 2: (0, 2), 4: (0, 4), 6: (0, 6), 3: (1, 2), 5: (4, 1), 7: (6, 1)}
    return {mask: (0, mask) for mask in range(1, tiles // 2)}


def groups_of(tiles):
    if tiles == 16:
        return [[0, 1, 2], [4, 6, 3], [5, 7]]
    return [list(range(i, i + 4)) for i in range(0, tiles // 2, 4)]


def may_share(one, other, tiles, videos):
    low, high = min(one, other), max(one, other)
    quarter = tiles // 4
    return videos != 2 or high < tiles - quarter or low >= quarter


def shards(
    tiles,
    frames,
    latents,
    row_video,
    video_cols,
    first_gain,
    first_shift,
    conv_weight,
    conv_bias,
    second_gain,
    second_shift,
    triple_weight,
    triple_bias,
    output_weight,
    output_bias,
    upsample_weight,
    upsample_bias,
):
    row_count, frame_count, cols, channels = latents.shape
    assert frame_count == 1 and row_count % 2 == 0 and tiles % 4 == 0
    out_channels = upsample_weight.shape[-1]
    rows = row_count * tiles
    cells = row_count * cols
    padded = -(-(cols + 1) // 16) * 16
    near_rows = row_count + 2
    source = latents.reshape(row_count, cols, channels)
    tile = lax.axis_index("tile").astype(jnp.int32)
    info = jnp.concatenate([jnp.reshape(tile, (1,)), row_video, video_cols])

    def row(vector):
        return vector.reshape(1, -1)

    def shape(*dims, dtype=BF16):
        return jax.ShapeDtypeStruct(dims, dtype)

    def call(kernel, operands, out_shape, scratch=(), **kwargs):
        many = isinstance(out_shape, tuple)
        return pl.pallas_call(
            kernel,
            out_shape=out_shape,
            in_specs=[SMEM_SPEC] + [VMEM_SPEC] * len(operands),
            out_specs=(VMEM_SPEC,) * len(out_shape) if many else VMEM_SPEC,
            scratch_shapes=list(scratch),
            compiler_params=params(),
            **kwargs,
        )(info, *operands)

    before = lax.ppermute(source[row_count - 1 :], "tile", [(i, i + 1) for i in range(tiles - 1)])
    after = lax.ppermute(source[:1], "tile", [(i + 1, i) for i in range(tiles - 1)])
    stats_shape = shape(3, SLOTS, LANES, dtype=F32)
    stats = call(
        functools.partial(stats_kernel, rows), [source], stats_shape,
        cost_estimate=cost(cells * channels * 2, 2 * cells * channels), name="first_stats",
    )
    stats, before, after = lax.optimization_barrier((stats, before, after))

    def over_tiles(stats):
        bit = 1
        while bit < tiles:
            other = lax.ppermute(stats, "tile", [(i, i ^ bit) for i in range(tiles)])
            stats = merge_stats(stats, other)
            bit *= 2
        return stats

    stats = over_tiles(stats)
    hidden = call(
        functools.partial(hidden_kernel, rows),
        [before, source, after, stats, row(first_gain), row(first_shift)],
        shape(near_rows, cols, channels),
        cost_estimate=cost(cells * channels * 10, 5 * cells * channels, cells * channels),
        name="hidden",
    )

    taps = min(3, frames)
    context = [hidden] + [
        lax.ppermute(hidden, "frame", [(i, i + by) for i in range(frames - by)])
        for by in range(1, taps)
    ]

    pairs = row_count // 2
    pair_shape = shape(pairs, 2 * cols, channels)
    own, stats = pl.pallas_call(
        functools.partial(conv_kernel, rows, taps),
        out_shape=(pair_shape, stats_shape),
        in_specs=[SMEM_SPEC] + [VMEM_SPEC] * (taps + 2) + [HBM_SPEC],
        out_specs=(VMEM_SPEC, VMEM_SPEC),
        scratch_shapes=[
            pltpu.VMEM((taps, near_rows * padded, 3 * channels), BF16),
            pltpu.VMEM((3 * taps, 3 * channels, channels), BF16),
            pltpu.SemaphoreType.DMA((3 * taps,)),
        ],
        compiler_params=pltpu.CompilerParams(vmem_limit_bytes=CONV_VMEM_BYTES),
        cost_estimate=cost(
            9 * taps * cells * channels * channels, 18 * taps * channels * channels
        ),
        name="conv",
    )(info, *context, source, row(conv_bias), conv_weight.reshape(9, 3 * channels, channels))

    neighbour = [(i, i ^ 1) for i in range(tiles)]
    videos = video_cols.shape[0]
    blocks = {0: own}
    for mask, (parent, step) in gather_plan(tiles).items():
        moves = [(i, i ^ (2 * step)) for i in range(tiles)]
        moves = [(i, j) for i, j in moves if may_share(j, j ^ (2 * mask), tiles, videos)]
        blocks[mask] = lax.ppermute(blocks[parent], "tile", moves)
    other = lax.ppermute(own, "tile", neighbour)
    stats = over_tiles(stats)
    gain, shift = row(second_gain), row(second_shift)
    query_shapes = (shape(cells, channels), shape(cells, LANES, dtype=F32))
    mine_queries, mine_constant, queries, constant = call(
        functools.partial(query_kernel, rows),
        [own, other, stats, gain, shift, triple_weight, row(triple_bias)],
        query_shapes * 2,
        cost_estimate=cost(4 * cells * channels * channels, 4 * cells * channels),
        name="queries",
    )

    def attend(masks, queries, constant, state, yours, last):
        level_shape = shape(cells, LANES, dtype=F32)
        scratch = [pltpu.VMEM((cells, channels), BF16)]
        running = (level_shape, level_shape, shape(cells, channels, dtype=F32))
        if last:
            scratch += [pltpu.VMEM(each.shape, F32) for each in running]
            outs = shape(cells + 16, channels) if yours else (running[2], level_shape)
        else:
            outs = running
        macs = 2 * cells * len(masks) * cells * channels
        return call(
            functools.partial(attend_kernel, rows, tuple(masks), yours, not state, last),
            [stats, gain, shift, queries, constant] + [blocks[m] for m in masks] + list(state),
            outs,
            scratch=scratch,
            cost_estimate=cost(macs, 2 * cells * len(masks) * channels),
            name="attend_yours" if yours else "attend_mine",
        )

    groups = groups_of(tiles)
    state = ()
    for index, masks in enumerate(groups):
        state = attend(masks, queries, constant, state, True, index == len(groups) - 1)
    sent = state
    received = lax.ppermute(sent, "tile", neighbour)
    sent, mine_queries, upsample_weight = lax.optimization_barrier(
        (sent, mine_queries, upsample_weight)
    )
    mean, level = attend(
        [m for masks in groups for m in masks], mine_queries, mine_constant, (), False, True
    )
    folded = pl.pallas_call(
        fold_kernel,
        out_shape=shape(2, 2, 2, out_channels, 2 * channels),
        in_specs=[VMEM_SPEC],
        out_specs=VMEM_SPEC,
        compiler_params=params(),
        cost_estimate=cost(16 * channels * out_channels, 50 * channels * out_channels),
        name="fold",
    )(jnp.swapaxes(upsample_weight, 2, 3))

    rim_shape = shape(1, cols, channels)
    attended, first_row, last_row = call(
        functools.partial(finish_kernel, rows),
        [
            mean, level, received, own, triple_weight, row(triple_bias), output_weight,
            row(output_bias),
        ],
        (shape(row_count, cols, channels), rim_shape, rim_shape),
        cost_estimate=cost(2 * cells * channels * channels, 8 * cells * channels),
        name="finish",
    )
    before = lax.ppermute(last_row, "tile", [(i, i + 1) for i in range(tiles - 1)])
    after = lax.ppermute(first_row, "tile", [(i + 1, i) for i in range(tiles - 1)])
    decoded = call(
        functools.partial(upsample_kernel, rows),
        [before, attended, after, folded, row(upsample_bias)],
        shape(2 * row_count, 2 * cols, out_channels),
        scratch=[
            pltpu.VMEM((near_rows * padded, 3 * channels), BF16),
            pltpu.VMEM((-(-out_channels // LANES), 2 * row_count, 2 * cols, LANES), F32),
        ],
        cost_estimate=cost(16 * cells * channels * out_channels, 8 * cells * out_channels),
        name="upsample",
    )
    return decoded.reshape(2 * row_count, 1, 2 * cols, out_channels)


def solution(mesh):
    sizes = dict(mesh.shape)
    in_specs = (P("tile", "frame", None, None),) + (P(),) * 14
    out_specs = P("tile", "frame", None, None)
    body = functools.partial(shards, sizes["tile"], sizes["frame"])
    return jax.shard_map(body, mesh=mesh, in_specs=in_specs, out_specs=out_specs, check_vma=False)
```

```python
import functools
import math

import jax
import jax.numpy as jnp
from jax import lax
from jax.experimental import pallas as pl
from jax.experimental.pallas import tpu as pltpu
from jax.sharding import PartitionSpec as P

GROUPS = 32
EPSILON = 1e-05
MASKED = -1e30
LOWEST = -5e29
HIGHEST = lax.Precision.HIGHEST
SLOTS = 8
ROWS_OF_TILE = 4
LANES = 128
VMEM_BYTES = 24 * 1024 * 1024
CONV_VMEM_BYTES = 50 * 1024 * 1024
F32 = jnp.float32
BF16 = jnp.bfloat16

SMEM_SPEC = pl.BlockSpec(memory_space=pltpu.SMEM)
VMEM_SPEC = pl.BlockSpec(memory_space=pltpu.VMEM)
HBM_SPEC = pl.BlockSpec(memory_space=pltpu.HBM)


def cost(macs, nbytes, exps=0):
    return pl.CostEstimate(flops=2 * macs, bytes_accessed=nbytes, transcendentals=exps)


def params():
    return pltpu.CompilerParams(vmem_limit_bytes=VMEM_BYTES)


def member_matrix(channels):
    per_group = channels // GROUPS
    group = lax.broadcasted_iota(jnp.int32, (LANES, channels), 0) * per_group
    channel = lax.broadcasted_iota(jnp.int32, (LANES, channels), 1)
    return jnp.where((channel >= group) & (channel < group + per_group), 1.0, 0.0).astype(F32)


def to_groups(values, member):
    return lax.dot_general(
        values, member, (((1,), (1,)), ((), ())), precision=HIGHEST, preferred_element_type=F32
    )


def to_channels(values, member):
    return jnp.dot(values, member, precision=HIGHEST, preferred_element_type=F32)


class Info:
    def __init__(self, ref, rows):
        self.ref, self.rows = ref, rows
        self.videos = ref.shape[0] - 1 - rows

    def tile(self):
        return self.ref[0]

    def label(self, row):
        inside = (row >= 0) & (row < self.rows)
        return jnp.where(inside, self.ref[1 + jnp.clip(row, 0, self.rows - 1)], -1)

    def width(self, label):
        return jnp.where(label >= 0, self.ref[1 + self.rows + jnp.maximum(label, 0)], 0)

    def window(self, first, count):
        labels = [self.label(first + r) for r in range(count)]
        return labels, [self.width(label) for label in labels]


def pick(table, label, videos):
    chosen = table[0:1]
    for video in range(1, videos):
        chosen = jnp.where(label == video, table[video : video + 1], chosen)
    return chosen


def norm_tables(stats_ref, gain_ref):
    member = member_matrix(gain_ref.shape[1])
    counts = jnp.maximum(stats_ref[0], 1.0)
    scale = lax.rsqrt(stats_ref[2] / counts + EPSILON)
    return to_channels(stats_ref[1], member), to_channels(scale, member) * gain_ref[...]


def write_stats(out_ref, rows, labels, widths, videos, channels):
    member = member_matrix(channels)
    per_group = channels // GROUPS
    cols = rows[0].shape[0]
    slot = lax.broadcasted_iota(jnp.int32, (SLOTS, 1), 0)
    column = lax.broadcasted_iota(jnp.int32, (cols, 1), 0)
    sums = jnp.zeros((SLOTS, channels), F32)
    counts = jnp.zeros((SLOTS, 1), F32)
    for index, row in enumerate(rows):
        sums = jnp.where(slot == index, jnp.sum(row, axis=0, keepdims=True), sums)
        counts = jnp.where(slot == index, (widths[index] * per_group).astype(F32), counts)
    means = to_groups(sums, member) / jnp.maximum(counts, 1.0)
    means_wide = to_channels(means, member)
    squares = jnp.zeros((SLOTS, channels), F32)
    for index, row in enumerate(rows):
        centered = jnp.where(column < widths[index], row - means_wide[index : index + 1], 0.0)
        squares = jnp.where(
            slot == index, jnp.sum(centered * centered, axis=0, keepdims=True), squares
        )
    spreads = to_groups(squares, member)
    out_ref[...] = jnp.zeros(out_ref.shape, F32)
    for video in range(videos):
        total = jnp.zeros((1, LANES), F32)
        count = jnp.zeros((1, LANES), F32)
        for index in range(len(rows)):
            mine = labels[index] == video
            row_count = counts[index : index + 1]
            total = total + jnp.where(mine, means[index : index + 1] * row_count, 0.0)
            count = count + jnp.where(mine, row_count, 0.0)
        mean = total / jnp.maximum(count, 1.0)
        spread = jnp.zeros((1, LANES), F32)
        for index in range(len(rows)):
            off = means[index : index + 1] - mean
            part = spreads[index : index + 1] + counts[index : index + 1] * off * off
            spread = spread + jnp.where(labels[index] == video, part, 0.0)
        out_ref[0, video : video + 1, :] = count
        out_ref[1, video : video + 1, :] = mean
        out_ref[2, video : video + 1, :] = spread


def build_columns(columns_ref, row_refs):
    padded = columns_ref.shape[0] // len(row_refs)
    for index, row in enumerate(row_refs):
        cells = row().astype(F32)
        count, channels = cells.shape
        cells = jnp.concatenate([cells, jnp.zeros((padded - count, channels), F32)], axis=0)
        start = index * padded
        columns_ref[start : start + padded, 0:channels] = pltpu.roll(cells, 1, 0).astype(BF16)
        columns_ref[start : start + padded, channels : 2 * channels] = cells.astype(BF16)
        columns_ref[start : start + padded, 2 * channels : 3 * channels] = pltpu.roll(
            cells, padded - 1, 0
        ).astype(BF16)


def stats_kernel(rows, info_ref, latents_ref, out_ref):
    info = Info(info_ref, rows)
    row_count, cols, channels = latents_ref.shape
    labels, widths = info.window(info.tile() * row_count, row_count)
    column = lax.broadcasted_iota(jnp.int32, (cols, 1), 0)
    cells = [
        jnp.where(column < widths[r], latents_ref[r].astype(F32), 0.0) for r in range(row_count)
    ]
    write_stats(out_ref, cells, labels, widths, info.videos, channels)


def hidden_kernel(
    rows, info_ref, before_ref, latents_ref, after_ref, stats_ref, gain_ref, shift_ref, out_ref
):
    info = Info(info_ref, rows)
    row_count, cols, _ = latents_ref.shape
    labels, widths = info.window(info.tile() * row_count - 1, row_count + 2)
    means, scales = norm_tables(stats_ref, gain_ref)
    column = lax.broadcasted_iota(jnp.int32, (cols, 1), 0)
    for r in range(row_count + 2):
        if r == 0:
            source = before_ref[0]
        elif r == row_count + 1:
            source = after_ref[0]
        else:
            source = latents_ref[r - 1]
        mean = pick(means, labels[r], info.videos)
        scale = pick(scales, labels[r], info.videos)
        normed = (source.astype(F32) - mean) * scale + shift_ref[...]
        active = normed / (1.0 + jnp.exp(-normed))
        active = jnp.where(column < widths[r], active, 0.0)
        rest = jnp.zeros((out_ref.shape[1] - cols, active.shape[1]), F32)
        out_ref[r] = jnp.concatenate([active, rest], axis=0).astype(BF16)


def conv_kernel(rows, taps, info_ref, *rest):
    hidden_refs, rest = rest[:taps], rest[taps:]
    latents_ref, bias_ref, weight_ref, own_ref, stats_ref, inputs_ref, held_ref, sems = rest
    row_count, cols, channels = latents_ref.shape
    info = Info(info_ref, rows)
    padded = hidden_refs[0].shape[1]
    copies = [
        [
            pltpu.make_async_copy(
                weight_ref.at[2 - depth // 3, depth % 3, side],
                held_ref.at[
                    pl.ds(depth * channels, channels), pl.ds(side * channels, channels)
                ],
                sems.at[side, depth],
            )
            for depth in range(3 * taps)
        ]
        for side in range(3)
    ]
    for side in range(3):
        for copy in copies[side]:
            copy.start()
    labels, widths = info.window(info.tile() * row_count - 1, row_count + 2)
    for back, hidden_ref in enumerate(hidden_refs):
        for tap in range(3):
            lanes = slice((3 * back + tap) * channels, (3 * back + tap + 1) * channels)
            for r in range(row_count):
                block = hidden_ref[r + tap]
                if tap != 1:
                    same = labels[r + tap] == labels[r + 1]
                    block = jnp.where(same, block, jnp.zeros_like(block))
                inputs_ref[r * padded : (r + 1) * padded, lanes] = block
    for copy in copies[0] + copies[1]:
        copy.wait()
    near = jnp.dot(
        inputs_ref[...], held_ref[:, 0 : 2 * channels], preferred_element_type=F32
    )
    for copy in copies[2]:
        copy.wait()
    right = jnp.dot(inputs_ref[...], held_ref[:, 2 * channels :], preferred_element_type=F32)
    column = lax.broadcasted_iota(jnp.int32, (cols, 1), 0)
    cells = []
    for r in range(row_count):
        lines = slice(r * padded, (r + 1) * padded)
        branch = pltpu.roll(near[lines, 0:channels], 1, 0) + near[lines, channels:]
        branch = branch + pltpu.roll(right[lines], padded - 1, 0)
        value = latents_ref[r].astype(F32) + branch[:cols] + bias_ref[...]
        value = jnp.where(column < widths[r + 1], value, 0.0).astype(BF16)
        cells.append(value.astype(F32))
    for pair in range(row_count // 2):
        own_ref[pair] = jnp.concatenate(cells[2 * pair : 2 * pair + 2], axis=0).astype(BF16)
    write_stats(stats_ref, cells, labels[1:-1], widths[1:-1], info.videos, channels)


def split_rows(pairs_ref):
    cols = pairs_ref.shape[1] // 2
    cells = []
    for pair in range(pairs_ref.shape[0]):
        both = pairs_ref[pair].astype(F32)
        cells += [both[:cols], both[cols:]]
    return cells


def query_kernel(
    rows, info_ref, own_ref, other_ref, stats_ref, gain_ref, shift_ref, weight_ref, bias_ref,
    *out_refs,
):
    info = Info(info_ref, rows)
    pairs, double, channels = own_ref.shape
    cols = double // 2
    row_count = 2 * pairs
    span = row_count * cols
    means, scales = norm_tables(stats_ref, gain_ref)
    column = lax.broadcasted_iota(jnp.int32, (cols, 1), 0)
    cells = []
    for tile, pairs_ref in ((info.tile(), own_ref), (info.tile() ^ 1, other_ref)):
        labels, widths = info.window(tile * row_count, row_count)
        for r, values in enumerate(split_rows(pairs_ref)):
            mean = pick(means, labels[r], info.videos)
            scale = pick(scales, labels[r], info.videos)
            normed = (values - mean) * scale + shift_ref[...]
            cells.append(jnp.where(column < widths[r], normed, 0.0))
    cells = jnp.concatenate(cells, axis=0).astype(BF16)
    queries = (
        jnp.dot(cells, weight_ref[:, 0:channels], preferred_element_type=F32)
        + bias_ref[:, 0:channels]
    ).astype(BF16)
    factor = channels ** (-0.5) * math.log2(math.e)
    turned = lax.dot_general(
        queries, weight_ref[:, channels : 2 * channels], (((1,), (1,)), ((), ())),
        preferred_element_type=F32,
    )
    turned = (turned * factor).astype(BF16)
    constant = jnp.sum(
        queries.astype(F32) * bias_ref[:, channels : 2 * channels], axis=1, keepdims=True
    )
    constant = jnp.broadcast_to(constant * factor, (2 * span, LANES))
    for side in range(2):
        out_refs[2 * side][...] = turned[side * span : (side + 1) * span]
        out_refs[2 * side + 1][...] = constant[side * span : (side + 1) * span]


def attend_kernel(rows, masks, yours, first, last, info_ref, *rest):
    stats_ref, gain_ref, shift_ref, queries_ref, constant_ref, *rest = rest
    block_refs, rest = rest[: len(masks)], rest[len(masks) :]
    if not first:
        old_peak_ref, old_sum_ref, old_total_ref, *rest = rest
    if yours:
        key_refs, rest = rest[: len(masks)], rest[len(masks) :]
    else:
        key_refs = block_refs
    if last:
        *out_refs, peak_ref, sum_ref, total_ref = rest
    else:
        peak_ref, sum_ref, total_ref = rest
    info = Info(info_ref, rows)
    span, channels = queries_ref.shape
    double = block_refs[0].shape[1] if yours else 0
    cols = span // ROWS_OF_TILE
    row_count = ROWS_OF_TILE
    tile = info.tile()
    even = tile - lax.rem(tile, 2)
    labels = info.window((tile ^ 1 if yours else tile) * row_count, row_count)[0]
    if yours:
        lowest, highest = info.label(even * row_count), info.label((even + 2) * row_count - 1)
        means, scales = norm_tables(stats_ref, gain_ref)
    else:
        lowest, highest = labels[0], labels[-1]
    if first:
        peak_ref[...] = jnp.full(peak_ref.shape, LOWEST, F32)
        sum_ref[...] = jnp.zeros(sum_ref.shape, F32)
        total_ref[...] = jnp.zeros(total_ref.shape, F32)
    else:
        peak_ref[...] = old_peak_ref[...]
        sum_ref[...] = old_sum_ref[...]
        total_ref[...] = old_total_ref[...]
    query_label = jnp.concatenate(
        [jnp.zeros((cols, 1), F32) + label.astype(F32) for label in labels], axis=0
    )
    position = lax.broadcasted_iota(jnp.int32, (1, span), 1)

    for mask, block_ref, key_ref in zip(masks, block_refs, key_refs):
        near, widths = info.window((tile ^ (2 * mask)) * row_count, row_count)

        @pl.when((near[-1] >= lowest) & (near[0] <= highest))
        def _(near=near, widths=widths, block_ref=block_ref, key_ref=key_ref):
            code = jnp.full((1, span), -2.0, F32)
            for r in range(row_count):
                inside = (position >= r * cols) & (position < r * cols + widths[r])
                code = jnp.where(inside, near[r].astype(F32), code)
            if yours:
                for pair in range(row_count // 2):
                    both = block_ref[pair].astype(F32)
                    halves = []
                    for half in range(2):
                        label = near[2 * pair + half]
                        mean = pick(means, label, info.videos)
                        scale = pick(scales, label, info.videos)
                        values = both[half * cols : (half + 1) * cols]
                        halves.append((values - mean) * scale + shift_ref[...])
                    key_ref[pair * double : (pair + 1) * double, :] = jnp.concatenate(
                        halves, axis=0
                    ).astype(BF16)
            constant = constant_ref[:, 0:1]
            largest = peak_ref[:, 0:1]
            scores = lax.dot_general(
                queries_ref[...], key_ref[...], (((1,), (1,)), ((), ())),
                preferred_element_type=F32,
            )
            scores = jnp.where(code == query_label, scores, MASKED)
            peak = jnp.maximum(largest, jnp.max(scores, axis=1, keepdims=True) + constant)
            weights = jnp.exp2(scores - (peak - constant))
            factor = jnp.exp2(largest - peak)
            peak_ref[...] = jnp.broadcast_to(peak, peak_ref.shape)
            sums = sum_ref[:, 0:1] * factor + jnp.sum(weights, axis=1, keepdims=True)
            sum_ref[...] = jnp.broadcast_to(sums, sum_ref.shape)
            total_ref[...] = total_ref[...] * factor + jnp.dot(
                weights.astype(BF16), key_ref[...], preferred_element_type=F32
            )

    if not last:
        return
    denominator = sum_ref[:, 0:1]
    some = denominator > 0.0
    safe = jnp.where(some, denominator, 1.0)
    mean = total_ref[...] / safe
    level = jnp.where(some, peak_ref[:, 0:1] + jnp.log2(safe), LOWEST)
    if not yours:
        mean_ref, level_ref = out_refs
        mean_ref[...] = mean
        level_ref[...] = jnp.broadcast_to(level, level_ref.shape)
        return
    (sent_ref,) = out_refs
    sent_ref[0:span, :] = mean.astype(BF16)
    slots = sent_ref.shape[0] - span
    slot = lax.broadcasted_iota(jnp.int32, (slots, 1), 0)
    packed = jnp.zeros((slots, LANES), F32)
    for r in range(row_count):
        left = level[r * cols : (r + 1) * cols]
        left = jnp.sum(jnp.where(diagonal(cols), left, 0.0), axis=0, keepdims=True)
        for part in range(3):
            rounded = left.astype(BF16).astype(F32)
            packed = jnp.where(slot == 3 * r + part, rounded, packed)
            left = left - rounded
    sent_ref[span:, 0:LANES] = packed.astype(BF16)
    sent_ref[span:, LANES:] = jnp.zeros((slots, channels - LANES), BF16)


def diagonal(cols):
    return lax.broadcasted_iota(jnp.int32, (cols, LANES), 0) == lax.broadcasted_iota(
        jnp.int32, (cols, LANES), 1
    )


def finish_kernel(
    rows, info_ref, mean_ref, level_ref, received_ref, own_ref, triple_ref, triple_bias_ref,
    output_ref, output_bias_ref, out_ref, first_ref, last_ref,
):
    info = Info(info_ref, rows)
    row_count, cols, channels = out_ref.shape
    span = row_count * cols
    _, widths = info.window(info.tile() * row_count, row_count)
    received = received_ref[0:span, :].astype(F32)
    levels = received_ref[span:, 0:LANES].astype(F32)
    yours = []
    for r in range(row_count):
        level = levels[3 * r : 3 * r + 1] + levels[3 * r + 1 : 3 * r + 2]
        level = level + levels[3 * r + 2 : 3 * r + 3]
        yours.append(jnp.sum(jnp.where(diagonal(cols), level, 0.0), axis=1, keepdims=True))
    yours = jnp.concatenate(yours, axis=0)
    mine = level_ref[:, 0:1]
    peak = jnp.maximum(mine, yours)
    weight, other_weight = jnp.exp2(mine - peak), jnp.exp2(yours - peak)
    share = weight / (weight + other_weight)
    mean_cell = (mean_ref[...] * share + received * (1.0 - share)).astype(BF16)
    mixed = (
        jnp.dot(mean_cell, triple_ref[:, 2 * channels :], preferred_element_type=F32)
        + triple_bias_ref[:, 2 * channels :]
    ).astype(BF16)
    attended = jnp.dot(mixed, output_ref[...], preferred_element_type=F32) + output_bias_ref[...]
    column = lax.broadcasted_iota(jnp.int32, (cols, 1), 0)
    for r, before in enumerate(split_rows(own_ref)):
        value = before + attended[r * cols : (r + 1) * cols]
        value = jnp.where(column < widths[r], value, 0.0).astype(BF16)
        out_ref[r] = value
        if r == 0:
            first_ref[0] = value
        if r == row_count - 1:
            last_ref[0] = value


def fold_kernel(weight_ref, out_ref):
    channels = weight_ref.shape[-1]
    wide = [[weight_ref[a, b].astype(F32) for b in range(3)] for a in range(3)]

    def both(upper, lower):
        return [x + y for x, y in zip(upper, lower)]

    phases = [[wide[0], both(wide[1], wide[2])], [both(wide[0], wide[1]), wide[2]]]
    for down in range(2):
        for tap in range(2):
            left, middle, right = phases[down][tap]
            out_ref[down, tap, 0, :, 0:channels] = left.astype(BF16)
            out_ref[down, tap, 0, :, channels:] = (middle + right).astype(BF16)
            out_ref[down, tap, 1, :, 0:channels] = (left + middle).astype(BF16)
            out_ref[down, tap, 1, :, channels:] = right.astype(BF16)


def upsample_kernel(
    rows, info_ref, before_ref, own_ref, after_ref, weight_ref, bias_ref, out_ref, columns_ref,
    wide_ref,
):
    info = Info(info_ref, rows)
    row_count, cols, channels = own_ref.shape
    near_rows = row_count + 2
    padded = columns_ref.shape[0] // near_rows
    parts_out = wide_ref.shape[0]
    out_channels = out_ref.shape[-1]
    labels, widths = info.window(info.tile() * row_count - 1, near_rows)
    sources = [functools.partial(before_ref.__getitem__, 0)]
    sources += [functools.partial(own_ref.__getitem__, r) for r in range(row_count)]
    sources += [functools.partial(after_ref.__getitem__, 0)]
    build_columns(columns_ref, sources)
    span = row_count * padded
    wide_column = lax.broadcasted_iota(jnp.int32, (2 * cols, 1), 0)
    for down in range(2):
        for right in range(2):
            lanes = slice(right * channels, (right + 2) * channels)
            products = [
                lax.dot_general(
                    columns_ref[(down + tap) * padded : (down + tap) * padded + span, lanes],
                    weight_ref[down, tap, right],
                    (((1,), (1,)), ((), ())),
                    preferred_element_type=F32,
                )
                for tap in range(2)
            ]
            rim, same = products[down], products[1 - down]
            for r in range(row_count):
                lo, hi = r * padded, r * padded + cols
                near = labels[r + 2 * down]
                value = same[lo:hi] + jnp.where(near == labels[r + 1], rim[lo:hi], 0.0)
                for part in range(parts_out):
                    part_lo, part_hi = part * LANES, min((part + 1) * LANES, out_channels)
                    piece = value[:, part_lo:part_hi]
                    if part_hi - part_lo < LANES:
                        missing = LANES - (part_hi - part_lo)
                        piece = jnp.concatenate([piece, jnp.zeros((cols, missing), F32)], axis=1)
                    wide_ref[part, 2 * r + down, pl.ds(right, cols, 2), :] = piece
    for r in range(2 * row_count):
        valid = wide_column < 2 * widths[r // 2 + 1]
        for part in range(parts_out):
            lo, hi = part * LANES, min((part + 1) * LANES, out_channels)
            value = wide_ref[part, r, :, 0 : hi - lo] + bias_ref[:, lo:hi]
            out_ref[r, :, lo:hi] = jnp.where(valid, value, 0.0).astype(BF16)


def merge_stats(mine, other):
    count = mine[0] + other[0]
    safe = jnp.maximum(count, 1.0)
    off = other[1] - mine[1]
    mean = mine[1] + off * (other[0] / safe)
    spread = mine[2] + other[2] + off * off * (mine[0] * other[0] / safe)
    return jnp.stack([count, mean, spread])


def exchange(array, tiles, mask, among=None):
    moves = [(i, i ^ mask) for i in range(tiles) if among is None or among(i)]
    return lax.ppermute(array, "tile", moves)


def merge_round(stats, tiles, masks):
    parts = [stats] + [exchange(stats, tiles, mask) for mask in masks]
    while len(parts) > 1:
        parts = [merge_stats(*parts[i : i + 2]) for i in range(0, len(parts), 2)]
    return parts[0]


def merge_masks(tiles):
    bits = [1 << i for i in range(tiles.bit_length() - 1)]
    pairs = [bits[i : i + 2] for i in range(0, len(bits), 2)]
    return [[p[0], p[1], p[0] ^ p[1]] if len(p) == 2 else p for p in pairs]


def shards(
    tiles,
    frames,
    latents,
    row_video,
    video_cols,
    first_gain,
    first_shift,
    conv_weight,
    conv_bias,
    second_gain,
    second_shift,
    triple_weight,
    triple_bias,
    output_weight,
    output_bias,
    upsample_weight,
    upsample_bias,
):
    row_count, frame_count, cols, channels = latents.shape
    assert frame_count == 1 and row_count == ROWS_OF_TILE and tiles % 4 == 0
    out_channels = upsample_weight.shape[-1]
    rows = row_count * tiles
    cells = row_count * cols
    padded = -(-(cols + 1) // 16) * 16
    near_rows = row_count + 2
    source = latents.reshape(row_count, cols, channels)
    tile = lax.axis_index("tile").astype(jnp.int32)
    info = jnp.concatenate([jnp.reshape(tile, (1,)), row_video, video_cols])

    def row(vector):
        return vector.reshape(1, -1)

    def shape(*dims, dtype=BF16):
        return jax.ShapeDtypeStruct(dims, dtype)

    def call(kernel, operands, out_shape, scratch=(), **kwargs):
        many = isinstance(out_shape, tuple)
        return pl.pallas_call(
            kernel,
            out_shape=out_shape,
            in_specs=[SMEM_SPEC] + [VMEM_SPEC] * len(operands),
            out_specs=(VMEM_SPEC,) * len(out_shape) if many else VMEM_SPEC,
            scratch_shapes=list(scratch),
            compiler_params=params(),
            **kwargs,
        )(info, *operands)

    before = lax.ppermute(source[row_count - 1 :], "tile", [(i, i + 1) for i in range(tiles - 1)])
    after = lax.ppermute(source[:1], "tile", [(i + 1, i) for i in range(tiles - 1)])
    stats_shape = shape(3, SLOTS, LANES, dtype=F32)
    stats = call(
        functools.partial(stats_kernel, rows), [source], stats_shape,
        cost_estimate=cost(cells * channels * 2, 2 * cells * channels), name="first_stats",
    )
    rounds = merge_masks(tiles)
    for index, masks in enumerate(rounds):
        stats = merge_round(stats, tiles, masks)
        if index == 0:
            stats, before, after = lax.optimization_barrier((stats, before, after))
    hidden = call(
        functools.partial(hidden_kernel, rows),
        [before, source, after, stats, row(first_gain), row(first_shift)],
        shape(near_rows, padded, channels),
        cost_estimate=cost(cells * channels * 10, 5 * cells * channels, cells * channels),
        name="hidden",
    )

    taps = min(3, frames)
    context = [hidden] + [
        lax.ppermute(hidden, "frame", [(i, i + by) for i in range(frames - by)])
        for by in range(1, taps)
    ]

    pairs = row_count // 2
    pair_shape = shape(pairs, 2 * cols, channels)
    own, stats = pl.pallas_call(
        functools.partial(conv_kernel, rows, taps),
        out_shape=(pair_shape, stats_shape),
        in_specs=[SMEM_SPEC] + [VMEM_SPEC] * (taps + 2) + [HBM_SPEC],
        out_specs=(VMEM_SPEC, VMEM_SPEC),
        scratch_shapes=[
            pltpu.VMEM((row_count * padded, 3 * taps * channels), BF16),
            pltpu.VMEM((3 * taps * channels, 3 * channels), BF16),
            pltpu.SemaphoreType.DMA((3, 3 * taps)),
        ],
        compiler_params=pltpu.CompilerParams(vmem_limit_bytes=CONV_VMEM_BYTES),
        cost_estimate=cost(
            9 * taps * cells * channels * channels, 18 * taps * channels * channels
        ),
        name="conv",
    )(info, *context, source, row(conv_bias), conv_weight)

    blocks = {0: own}
    neighbour = [(i, i ^ 1) for i in range(tiles)]
    if tiles == 16 and video_cols.shape[0] == 2:
        def middle(t):
            return t // 4 in (1, 2)

        stats = merge_round(stats, tiles, rounds[1])
        other = exchange(own, tiles, 1)
        blocks[1] = exchange(own, tiles, 2)
        blocks[2] = exchange(own, tiles, 4)
        blocks[6] = exchange(own, tiles, 12, middle)
        stats, other, blocks[1], blocks[2], blocks[6] = lax.optimization_barrier(
            (stats, other, blocks[1], blocks[2], blocks[6])
        )
        stats = merge_round(stats, tiles, rounds[0])
        inward = exchange(blocks[2], tiles, 12, middle)
        outward = exchange(blocks[6], tiles, 4, middle)
        blocks[4] = jnp.where((tile // 4 == 1) | (tile // 4 == 2), inward, outward)
        blocks[7] = exchange(blocks[6], tiles, 2, middle)
        blocks[5] = exchange(blocks[4], tiles, 2)
        passed, blocks[4] = lax.optimization_barrier((blocks[1], blocks[4]))
        blocks[3] = exchange(passed, tiles, 4)
        groups = [[0, 1, 2, 6], [4], [7, 3, 5]]
    else:
        for masks in rounds:
            stats = merge_round(stats, tiles, masks)
        other = exchange(own, tiles, 1)
        for mask in range(1, tiles // 2):
            blocks[mask] = exchange(own, tiles, 2 * mask)
        groups = [list(range(i, i + 4)) for i in range(0, tiles // 2, 4)]
    gain, shift = row(second_gain), row(second_shift)
    query_shapes = (shape(cells, channels), shape(cells, LANES, dtype=F32))
    mine_queries, mine_constant, queries, constant = call(
        functools.partial(query_kernel, rows),
        [own, other, stats, gain, shift, triple_weight, row(triple_bias)],
        query_shapes * 2,
        cost_estimate=cost(4 * cells * channels * channels, 4 * cells * channels),
        name="queries",
    )

    keys = {}

    def attend(masks, queries, constant, state, yours, last):
        level_shape = shape(cells, LANES, dtype=F32)
        running = (level_shape, level_shape, shape(cells, channels, dtype=F32))
        scratch = []
        if last:
            scratch = [pltpu.VMEM(each.shape, F32) for each in running]
            outs = (shape(cells + 16, channels),) if yours else (running[2], level_shape)
        else:
            outs = running
        if yours:
            outs = (shape(cells, channels),) * len(masks) + outs
        macs = 2 * cells * len(masks) * cells * channels
        found = call(
            functools.partial(attend_kernel, rows, tuple(masks), yours, not state, last),
            [stats, gain, shift, queries, constant]
            + [blocks[m] if yours else keys[m] for m in masks]
            + list(state),
            outs,
            scratch=scratch,
            cost_estimate=cost(macs, 2 * cells * len(masks) * channels),
            name="attend_yours" if yours else "attend_mine",
        )
        if yours:
            keys.update(zip(masks, found))
            found = found[len(masks) :]
        return found

    state = ()
    for index, masks in enumerate(groups):
        state = attend(masks, queries, constant, state, True, index == len(groups) - 1)
    (sent,) = state
    received = lax.ppermute(sent, "tile", neighbour)
    sent, mine_queries, upsample_weight = lax.optimization_barrier(
        (sent, mine_queries, upsample_weight)
    )
    mean, level = attend(
        [m for masks in groups for m in masks], mine_queries, mine_constant, (), False, True
    )
    folded = pl.pallas_call(
        fold_kernel,
        out_shape=shape(2, 2, 2, out_channels, 2 * channels),
        in_specs=[VMEM_SPEC],
        out_specs=VMEM_SPEC,
        compiler_params=params(),
        cost_estimate=cost(16 * channels * out_channels, 50 * channels * out_channels),
        name="fold",
    )(jnp.swapaxes(upsample_weight, 2, 3))

    rim_shape = shape(1, cols, channels)
    attended, first_row, last_row = call(
        functools.partial(finish_kernel, rows),
        [
            mean, level, received, own, triple_weight, row(triple_bias), output_weight,
            row(output_bias),
        ],
        (shape(row_count, cols, channels), rim_shape, rim_shape),
        cost_estimate=cost(2 * cells * channels * channels, 8 * cells * channels),
        name="finish",
    )
    before = lax.ppermute(last_row, "tile", [(i, i + 1) for i in range(tiles - 1)])
    after = lax.ppermute(first_row, "tile", [(i + 1, i) for i in range(tiles - 1)])
    decoded = call(
        functools.partial(upsample_kernel, rows),
        [before, attended, after, folded, row(upsample_bias)],
        shape(2 * row_count, 2 * cols, out_channels),
        scratch=[
            pltpu.VMEM((near_rows * padded, 3 * channels), BF16),
            pltpu.VMEM((-(-out_channels // LANES), 2 * row_count, 2 * cols, LANES), F32),
        ],
        cost_estimate=cost(16 * cells * channels * out_channels, 8 * cells * out_channels),
        name="upsample",
    )
    return decoded.reshape(2 * row_count, 1, 2 * cols, out_channels)


def solution(mesh):
    sizes = dict(mesh.shape)
    in_specs = (P("tile", "frame", None, None),) + (P(),) * 14
    out_specs = P("tile", "frame", None, None)
    body = functools.partial(shards, sizes["tile"], sizes["frame"])
    return jax.shard_map(body, mesh=mesh, in_specs=in_specs, out_specs=out_specs, check_vma=False)
```

```python
import functools
import math

import jax
import jax.numpy as jnp
from jax import lax
from jax.experimental import pallas as pl
from jax.experimental.pallas import tpu as pltpu
from jax.sharding import PartitionSpec as P

GROUPS = 32
EPSILON = 1e-05
MASKED = -1e30
LOWEST = -5e29
HIGHEST = lax.Precision.HIGHEST
SLOTS = 8
ROWS_OF_TILE = 4
LANES = 128
VMEM_BYTES = 24 * 1024 * 1024
CONV_VMEM_BYTES = 50 * 1024 * 1024
F32 = jnp.float32
BF16 = jnp.bfloat16

SMEM_SPEC = pl.BlockSpec(memory_space=pltpu.SMEM)
VMEM_SPEC = pl.BlockSpec(memory_space=pltpu.VMEM)
HBM_SPEC = pl.BlockSpec(memory_space=pltpu.HBM)


def cost(microseconds):
    return pl.CostEstimate(
        flops=int(microseconds * 1.1e9), bytes_accessed=0, transcendentals=0
    )


def params():
    return pltpu.CompilerParams(vmem_limit_bytes=VMEM_BYTES)


def member_matrix(channels):
    per_group = channels // GROUPS
    group = lax.broadcasted_iota(jnp.int32, (LANES, channels), 0) * per_group
    channel = lax.broadcasted_iota(jnp.int32, (LANES, channels), 1)
    return jnp.where((channel >= group) & (channel < group + per_group), 1.0, 0.0).astype(F32)


def to_groups(values, member):
    return lax.dot_general(
        values, member, (((1,), (1,)), ((), ())), precision=HIGHEST, preferred_element_type=F32
    )


def to_channels(values, member):
    return jnp.dot(values, member, precision=HIGHEST, preferred_element_type=F32)


class Info:
    def __init__(self, ref, rows):
        self.ref, self.rows = ref, rows
        self.videos = ref.shape[0] - 1 - rows

    def tile(self):
        return self.ref[0]

    def label(self, row):
        inside = (row >= 0) & (row < self.rows)
        return jnp.where(inside, self.ref[1 + jnp.clip(row, 0, self.rows - 1)], -1)

    def width(self, label):
        return jnp.where(label >= 0, self.ref[1 + self.rows + jnp.maximum(label, 0)], 0)

    def window(self, first, count):
        labels = [self.label(first + r) for r in range(count)]
        return labels, [self.width(label) for label in labels]


def pick(table, label, videos):
    chosen = table[0:1]
    for video in range(1, videos):
        chosen = jnp.where(label == video, table[video : video + 1], chosen)
    return chosen


def norm_tables(stats_ref, gain_ref):
    member = member_matrix(gain_ref.shape[1])
    counts = jnp.maximum(stats_ref[0], 1.0)
    scale = lax.rsqrt(stats_ref[2] / counts + EPSILON)
    return to_channels(stats_ref[1], member), to_channels(scale, member) * gain_ref[...]


def write_stats(out_ref, rows, labels, widths, videos, channels):
    member = member_matrix(channels)
    per_group = channels // GROUPS
    cols = rows[0].shape[0]
    slot = lax.broadcasted_iota(jnp.int32, (SLOTS, 1), 0)
    column = lax.broadcasted_iota(jnp.int32, (cols, 1), 0)
    sums = jnp.zeros((SLOTS, channels), F32)
    counts = jnp.zeros((SLOTS, 1), F32)
    for index, row in enumerate(rows):
        sums = jnp.where(slot == index, jnp.sum(row, axis=0, keepdims=True), sums)
        counts = jnp.where(slot == index, (widths[index] * per_group).astype(F32), counts)
    means = to_groups(sums, member) / jnp.maximum(counts, 1.0)
    means_wide = to_channels(means, member)
    squares = jnp.zeros((SLOTS, channels), F32)
    for index, row in enumerate(rows):
        centered = jnp.where(column < widths[index], row - means_wide[index : index + 1], 0.0)
        squares = jnp.where(
            slot == index, jnp.sum(centered * centered, axis=0, keepdims=True), squares
        )
    spreads = to_groups(squares, member)
    out_ref[...] = jnp.zeros(out_ref.shape, F32)
    for video in range(videos):
        total = jnp.zeros((1, LANES), F32)
        count = jnp.zeros((1, LANES), F32)
        for index in range(len(rows)):
            mine = labels[index] == video
            row_count = counts[index : index + 1]
            total = total + jnp.where(mine, means[index : index + 1] * row_count, 0.0)
            count = count + jnp.where(mine, row_count, 0.0)
        mean = total / jnp.maximum(count, 1.0)
        spread = jnp.zeros((1, LANES), F32)
        for index in range(len(rows)):
            off = means[index : index + 1] - mean
            part = spreads[index : index + 1] + counts[index : index + 1] * off * off
            spread = spread + jnp.where(labels[index] == video, part, 0.0)
        out_ref[0, video : video + 1, :] = count
        out_ref[1, video : video + 1, :] = mean
        out_ref[2, video : video + 1, :] = spread


def build_columns(columns_ref, row_refs):
    padded = columns_ref.shape[0] // len(row_refs)
    for index, row in enumerate(row_refs):
        cells = row().astype(F32)
        count, channels = cells.shape
        cells = jnp.concatenate([cells, jnp.zeros((padded - count, channels), F32)], axis=0)
        start = index * padded
        columns_ref[start : start + padded, 0:channels] = pltpu.roll(cells, 1, 0).astype(BF16)
        columns_ref[start : start + padded, channels : 2 * channels] = cells.astype(BF16)
        columns_ref[start : start + padded, 2 * channels : 3 * channels] = pltpu.roll(
            cells, padded - 1, 0
        ).astype(BF16)


def stats_kernel(rows, info_ref, latents_ref, out_ref):
    info = Info(info_ref, rows)
    row_count, cols, channels = latents_ref.shape
    labels, widths = info.window(info.tile() * row_count, row_count)
    column = lax.broadcasted_iota(jnp.int32, (cols, 1), 0)
    cells = [
        jnp.where(column < widths[r], latents_ref[r].astype(F32), 0.0) for r in range(row_count)
    ]
    write_stats(out_ref, cells, labels, widths, info.videos, channels)


def rims(info, inner_ref, outer_ref):
    odd = lax.rem(info.tile(), 2) == 1
    inner, outer = inner_ref[0].astype(F32), outer_ref[0].astype(F32)
    return jnp.where(odd, inner, outer), jnp.where(odd, outer, inner)


def hidden_kernel(
    rows, info_ref, inner_ref, latents_ref, outer_ref, stats_ref, gain_ref, shift_ref, out_ref,
    source_ref,
):
    info = Info(info_ref, rows)
    row_count, cols, _ = latents_ref.shape
    labels, widths = info.window(info.tile() * row_count - 1, row_count + 2)
    means, scales = norm_tables(stats_ref, gain_ref)
    column = lax.broadcasted_iota(jnp.int32, (cols, 1), 0)
    above, below = rims(info, inner_ref, outer_ref)
    sources = [above] + [latents_ref[r].astype(F32) for r in range(row_count)] + [below]
    for r, source in enumerate(sources):
        mean = pick(means, labels[r], info.videos)
        scale = pick(scales, labels[r], info.videos)
        normed = (source - mean) * scale + shift_ref[...]
        active = normed / (1.0 + jnp.exp(-normed))
        active = jnp.where(column < widths[r], active, 0.0)
        rest = jnp.zeros((out_ref.shape[1] - cols, active.shape[1]), F32)
        out_ref[r] = jnp.concatenate([active, rest], axis=0).astype(BF16)
    source_ref[...] = latents_ref[...]


def hold_kernel(taps, weight_ref, held_ref, sems):
    channels = weight_ref.shape[-1]
    copies = [
        pltpu.make_async_copy(
            weight_ref.at[2 - depth // 3, depth % 3, side],
            held_ref.at[pl.ds(depth * channels, channels), pl.ds(side * channels, channels)],
            sems.at[side, depth],
        )
        for side in range(3)
        for depth in range(3 * taps)
    ]
    for copy in copies:
        copy.start()
    for copy in copies:
        copy.wait()


def conv_kernel(rows, taps, info_ref, *rest):
    hidden_refs, rest = rest[:taps], rest[taps:]
    latents_ref, bias_ref, held_ref, own_ref, stats_ref, inputs_ref = rest
    row_count, cols, channels = latents_ref.shape
    info = Info(info_ref, rows)
    padded = hidden_refs[0].shape[1]
    labels, widths = info.window(info.tile() * row_count - 1, row_count + 2)
    for back, hidden_ref in enumerate(hidden_refs):
        for tap in range(3):
            lanes = slice((3 * back + tap) * channels, (3 * back + tap + 1) * channels)
            for r in range(row_count):
                block = hidden_ref[r + tap]
                if tap != 1:
                    same = labels[r + tap] == labels[r + 1]
                    block = jnp.where(same, block, jnp.zeros_like(block))
                inputs_ref[r * padded : (r + 1) * padded, lanes] = block
    product = jnp.dot(inputs_ref[...], held_ref[...], preferred_element_type=F32)
    column = lax.broadcasted_iota(jnp.int32, (cols, 1), 0)
    cells = []
    for r in range(row_count):
        lines = slice(r * padded, (r + 1) * padded)
        branch = pltpu.roll(product[lines, 0:channels], 1, 0)
        branch = branch + product[lines, channels : 2 * channels]
        branch = branch + pltpu.roll(product[lines, 2 * channels :], padded - 1, 0)
        value = latents_ref[r].astype(F32) + branch[:cols] + bias_ref[...]
        value = jnp.where(column < widths[r + 1], value, 0.0).astype(BF16)
        cells.append(value.astype(F32))
    for pair in range(row_count // 2):
        own_ref[pair] = jnp.concatenate(cells[2 * pair : 2 * pair + 2], axis=0).astype(BF16)
    write_stats(stats_ref, cells, labels[1:-1], widths[1:-1], info.videos, channels)


def split_rows(pairs_ref):
    cols = pairs_ref.shape[1] // 2
    cells = []
    for pair in range(pairs_ref.shape[0]):
        both = pairs_ref[pair].astype(F32)
        cells += [both[:cols], both[cols:]]
    return cells


def query_kernel(
    rows, info_ref, own_ref, other_ref, stats_ref, gain_ref, shift_ref, weight_ref, bias_ref,
    *out_refs,
):
    info = Info(info_ref, rows)
    pairs, double, channels = own_ref.shape
    cols = double // 2
    row_count = 2 * pairs
    span = row_count * cols
    means, scales = norm_tables(stats_ref, gain_ref)
    column = lax.broadcasted_iota(jnp.int32, (cols, 1), 0)
    cells = []
    for tile, pairs_ref in ((info.tile(), own_ref), (info.tile() ^ 1, other_ref)):
        labels, widths = info.window(tile * row_count, row_count)
        for r, values in enumerate(split_rows(pairs_ref)):
            mean = pick(means, labels[r], info.videos)
            scale = pick(scales, labels[r], info.videos)
            normed = (values - mean) * scale + shift_ref[...]
            cells.append(jnp.where(column < widths[r], normed, 0.0))
    cells = jnp.concatenate(cells, axis=0).astype(BF16)
    queries = (
        jnp.dot(cells, weight_ref[:, 0:channels], preferred_element_type=F32)
        + bias_ref[:, 0:channels]
    ).astype(BF16)
    factor = channels ** (-0.5) * math.log2(math.e)
    turned = lax.dot_general(
        queries, weight_ref[:, channels : 2 * channels], (((1,), (1,)), ((), ())),
        preferred_element_type=F32,
    )
    turned = (turned * factor).astype(BF16)
    constant = jnp.sum(
        queries.astype(F32) * bias_ref[:, channels : 2 * channels], axis=1, keepdims=True
    )
    constant = jnp.broadcast_to(constant * factor, (2 * span, LANES))
    for side in range(2):
        out_refs[2 * side][...] = turned[side * span : (side + 1) * span]
        out_refs[2 * side + 1][...] = constant[side * span : (side + 1) * span]


def key_codes(info, masks, span, cols):
    row_count = span // cols
    position = lax.broadcasted_iota(jnp.int32, (1, len(masks) * span), 1)
    codes = jnp.full((1, len(masks) * span), -2.0, F32)
    for index, mask in enumerate(masks):
        near, widths = info.window((info.tile() ^ (2 * mask)) * row_count, row_count)
        for r in range(row_count):
            start = index * span + r * cols
            inside = (position >= start) & (position < start + widths[r])
            codes = jnp.where(inside, near[r].astype(F32), codes)
    return codes


def query_codes(info, tile, span, cols):
    row_count = span // cols
    labels, _ = info.window(tile * row_count, row_count)
    return jnp.concatenate(
        [jnp.zeros((cols, 1), F32) + label.astype(F32) for label in labels], axis=0
    )


def scores_of(queries, keys, codes, query_code):
    scores = lax.dot_general(
        queries, keys, (((1,), (1,)), ((), ())), preferred_element_type=F32
    )
    return jnp.where(codes == query_code, scores, MASKED)


def mean_and_level(peak, denominator, total):
    some = denominator > 0.0
    safe = jnp.where(some, denominator, 1.0)
    return total / safe, jnp.where(some, peak + jnp.log2(safe), LOWEST)


def attend_yours_kernel(rows, masks, first, last, info_ref, *rest):
    stats_ref, gain_ref, shift_ref, queries_ref, constant_ref, *rest = rest
    block_refs, rest = rest[: len(masks)], rest[len(masks) :]
    if not first:
        old_peak_ref, old_sum_ref, old_total_ref, *rest = rest
    keys_ref, *out_refs = rest
    info = Info(info_ref, rows)
    span, channels = queries_ref.shape
    pairs, double, _ = block_refs[0].shape
    cols = double // 2
    row_count = 2 * pairs
    tile = info.tile()
    means, scales = norm_tables(stats_ref, gain_ref)
    for index, (mask, block_ref) in enumerate(zip(masks, block_refs)):
        near, _ = info.window((tile ^ (2 * mask)) * row_count, row_count)
        for pair in range(pairs):
            both = block_ref[pair].astype(F32)
            halves = []
            for half in range(2):
                label = near[2 * pair + half]
                mean = pick(means, label, info.videos)
                scale = pick(scales, label, info.videos)
                values = both[half * cols : (half + 1) * cols]
                halves.append((values - mean) * scale + shift_ref[...])
            start = index * span + pair * double
            keys_ref[start : start + double, :] = jnp.concatenate(halves, axis=0).astype(BF16)
    constant = constant_ref[:, 0:1]
    scores = scores_of(
        queries_ref[...], keys_ref[...], key_codes(info, masks, span, cols),
        query_codes(info, tile ^ 1, span, cols),
    )
    peak = jnp.maximum(LOWEST, jnp.max(scores, axis=1, keepdims=True) + constant)
    if not first:
        largest = old_peak_ref[:, 0:1]
        peak = jnp.maximum(largest, peak)
    weights = jnp.exp2(scores - (peak - constant))
    denominator = jnp.sum(weights, axis=1, keepdims=True)
    total = jnp.dot(weights.astype(BF16), keys_ref[...], preferred_element_type=F32)
    if not first:
        factor = jnp.exp2(largest - peak)
        denominator = old_sum_ref[:, 0:1] * factor + denominator
        total = old_total_ref[...] * factor + total
    if not last:
        peak_ref, sum_ref, total_ref = out_refs
        peak_ref[...] = jnp.broadcast_to(peak, peak_ref.shape)
        sum_ref[...] = jnp.broadcast_to(denominator, sum_ref.shape)
        total_ref[...] = total
        return
    (sent_ref,) = out_refs
    mean, level = mean_and_level(peak, denominator, total)
    sent_ref[0:span, :] = mean.astype(BF16)
    slots = sent_ref.shape[0] - span
    slot = lax.broadcasted_iota(jnp.int32, (slots, 1), 0)
    packed = jnp.zeros((slots, LANES), F32)
    for r in range(row_count):
        left = level[r * cols : (r + 1) * cols]
        left = jnp.sum(jnp.where(diagonal(cols), left, 0.0), axis=0, keepdims=True)
        for part in range(3):
            rounded = left.astype(BF16).astype(F32)
            packed = jnp.where(slot == 3 * r + part, rounded, packed)
            left = left - rounded
    sent_ref[span:, 0:LANES] = packed.astype(BF16)
    sent_ref[span:, LANES:] = jnp.zeros((slots, channels - LANES), BF16)


def attend_mine_kernel(rows, groups, info_ref, queries_ref, constant_ref, *rest):
    key_refs, (mean_ref, level_ref) = rest[: len(groups)], rest[len(groups) :]
    info = Info(info_ref, rows)
    span = queries_ref.shape[0]
    cols = span // ROWS_OF_TILE
    query_code = query_codes(info, info.tile(), span, cols)
    constant = constant_ref[:, 0:1]
    peak = jnp.full((span, 1), LOWEST, F32)
    scores = []
    for masks, key_ref in zip(groups, key_refs):
        codes = key_codes(info, masks, span, cols)
        scores.append(scores_of(queries_ref[...], key_ref[...], codes, query_code))
        peak = jnp.maximum(peak, jnp.max(scores[-1], axis=1, keepdims=True) + constant)
    denominator, total = 0.0, 0.0
    for part, key_ref in zip(scores, key_refs):
        weights = jnp.exp2(part - (peak - constant))
        denominator = denominator + jnp.sum(weights, axis=1, keepdims=True)
        total = total + jnp.dot(
            weights.astype(BF16), key_ref[...], preferred_element_type=F32
        )
    mean, level = mean_and_level(peak, denominator, total)
    mean_ref[...] = mean
    level_ref[...] = jnp.broadcast_to(level, level_ref.shape)


def diagonal(cols):
    return lax.broadcasted_iota(jnp.int32, (cols, LANES), 0) == lax.broadcasted_iota(
        jnp.int32, (cols, LANES), 1
    )


def finish_kernel(
    rows, info_ref, mean_ref, level_ref, received_ref, own_ref, triple_ref, triple_bias_ref,
    output_ref, output_bias_ref, out_ref, inner_ref, outer_ref,
):
    info = Info(info_ref, rows)
    row_count, cols, channels = out_ref.shape
    span = row_count * cols
    _, widths = info.window(info.tile() * row_count, row_count)
    received = received_ref[0:span, :].astype(F32)
    levels = received_ref[span:, 0:LANES].astype(F32)
    yours = []
    for r in range(row_count):
        level = levels[3 * r : 3 * r + 1] + levels[3 * r + 1 : 3 * r + 2]
        level = level + levels[3 * r + 2 : 3 * r + 3]
        yours.append(jnp.sum(jnp.where(diagonal(cols), level, 0.0), axis=1, keepdims=True))
    yours = jnp.concatenate(yours, axis=0)
    mine = level_ref[:, 0:1]
    peak = jnp.maximum(mine, yours)
    weight, other_weight = jnp.exp2(mine - peak), jnp.exp2(yours - peak)
    share = weight / (weight + other_weight)
    mean_cell = (mean_ref[...] * share + received * (1.0 - share)).astype(BF16)
    mixed = (
        jnp.dot(mean_cell, triple_ref[:, 2 * channels :], preferred_element_type=F32)
        + triple_bias_ref[:, 2 * channels :]
    ).astype(BF16)
    attended = jnp.dot(mixed, output_ref[...], preferred_element_type=F32) + output_bias_ref[...]
    column = lax.broadcasted_iota(jnp.int32, (cols, 1), 0)
    for r, before in enumerate(split_rows(own_ref)):
        value = before + attended[r * cols : (r + 1) * cols]
        value = jnp.where(column < widths[r], value, 0.0)
        out_ref[r] = value.astype(BF16)
        if r == 0:
            top = value
    odd = lax.rem(info.tile(), 2) == 1
    inner_ref[0] = jnp.where(odd, top, value).astype(BF16)
    outer_ref[0] = jnp.where(odd, value, top).astype(BF16)


def fold_kernel(weight_ref, out_ref):
    channels = weight_ref.shape[-1]
    wide = [[weight_ref[a, b].astype(F32) for b in range(3)] for a in range(3)]

    def both(upper, lower):
        return [x + y for x, y in zip(upper, lower)]

    phases = [[wide[0], both(wide[1], wide[2])], [both(wide[0], wide[1]), wide[2]]]
    for down in range(2):
        for tap in range(2):
            left, middle, right = phases[down][tap]
            out_ref[down, tap, 0, :, 0:channels] = left.astype(BF16)
            out_ref[down, tap, 0, :, channels:] = (middle + right).astype(BF16)
            out_ref[down, tap, 1, :, 0:channels] = (left + middle).astype(BF16)
            out_ref[down, tap, 1, :, channels:] = right.astype(BF16)


def upsample_kernel(
    rows, info_ref, inner_ref, own_ref, outer_ref, weight_ref, bias_ref, out_ref, columns_ref,
    wide_ref,
):
    info = Info(info_ref, rows)
    row_count, cols, channels = own_ref.shape
    near_rows = row_count + 2
    padded = columns_ref.shape[0] // near_rows
    parts_out = wide_ref.shape[0]
    out_channels = out_ref.shape[-1]
    labels, widths = info.window(info.tile() * row_count - 1, near_rows)
    above, below = rims(info, inner_ref, outer_ref)
    sources = [lambda: above]
    sources += [functools.partial(own_ref.__getitem__, r) for r in range(row_count)]
    sources += [lambda: below]
    build_columns(columns_ref, sources)
    span = row_count * padded
    wide_column = lax.broadcasted_iota(jnp.int32, (2 * cols, 1), 0)
    for down in range(2):
        for right in range(2):
            lanes = slice(right * channels, (right + 2) * channels)
            products = [
                lax.dot_general(
                    columns_ref[(down + tap) * padded : (down + tap) * padded + span, lanes],
                    weight_ref[down, tap, right],
                    (((1,), (1,)), ((), ())),
                    preferred_element_type=F32,
                )
                for tap in range(2)
            ]
            rim, same = products[down], products[1 - down]
            for r in range(row_count):
                lo, hi = r * padded, r * padded + cols
                near = labels[r + 2 * down]
                value = same[lo:hi] + jnp.where(near == labels[r + 1], rim[lo:hi], 0.0)
                for part in range(parts_out):
                    part_lo, part_hi = part * LANES, min((part + 1) * LANES, out_channels)
                    piece = value[:, part_lo:part_hi]
                    if part_hi - part_lo < LANES:
                        missing = LANES - (part_hi - part_lo)
                        piece = jnp.concatenate([piece, jnp.zeros((cols, missing), F32)], axis=1)
                    wide_ref[part, 2 * r + down, pl.ds(right, cols, 2), :] = piece
    for r in range(2 * row_count):
        valid = wide_column < 2 * widths[r // 2 + 1]
        for part in range(parts_out):
            lo, hi = part * LANES, min((part + 1) * LANES, out_channels)
            value = wide_ref[part, r, :, 0 : hi - lo] + bias_ref[:, lo:hi]
            out_ref[r, :, lo:hi] = jnp.where(valid, value, 0.0).astype(BF16)


def merge_stats(mine, other):
    count = mine[0] + other[0]
    safe = jnp.maximum(count, 1.0)
    off = other[1] - mine[1]
    mean = mine[1] + off * (other[0] / safe)
    spread = mine[2] + other[2] + off * off * (mine[0] * other[0] / safe)
    return jnp.stack([count, mean, spread])


def exchange(array, tiles, mask, among=None):
    moves = [(i, i ^ mask) for i in range(tiles) if among is None or among(i)]
    return lax.ppermute(array, "tile", moves)


def merge_round(stats, tiles, masks):
    parts = [stats] + [exchange(stats, tiles, mask) for mask in masks]
    while len(parts) > 1:
        parts = [merge_stats(*parts[i : i + 2]) for i in range(0, len(parts), 2)]
    return parts[0]


def merge_masks(tiles):
    bits = [1 << i for i in range(tiles.bit_length() - 1)]
    pairs = [bits[i : i + 2] for i in range(0, len(bits), 2)]
    return [[p[0], p[1], p[0] ^ p[1]] if len(p) == 2 else p for p in pairs]


def shards(
    tiles,
    frames,
    latents,
    row_video,
    video_cols,
    first_gain,
    first_shift,
    conv_weight,
    conv_bias,
    second_gain,
    second_shift,
    triple_weight,
    triple_bias,
    output_weight,
    output_bias,
    upsample_weight,
    upsample_bias,
):
    row_count, frame_count, cols, channels = latents.shape
    assert frame_count == 1 and row_count == ROWS_OF_TILE and tiles % 4 == 0
    out_channels = upsample_weight.shape[-1]
    rows = row_count * tiles
    cells = row_count * cols
    padded = -(-(cols + 1) // 16) * 16
    near_rows = row_count + 2
    source = latents.reshape(row_count, cols, channels)
    tile = lax.axis_index("tile").astype(jnp.int32)
    info = jnp.concatenate([jnp.reshape(tile, (1,)), row_video, video_cols])

    def row(vector):
        return vector.reshape(1, -1)

    def shape(*dims, dtype=BF16):
        return jax.ShapeDtypeStruct(dims, dtype)

    def call(kernel, operands, out_shape, scratch=(), **kwargs):
        many = isinstance(out_shape, tuple)
        return pl.pallas_call(
            kernel,
            out_shape=out_shape,
            in_specs=[SMEM_SPEC] + [VMEM_SPEC] * len(operands),
            out_specs=(VMEM_SPEC,) * len(out_shape) if many else VMEM_SPEC,
            scratch_shapes=list(scratch),
            compiler_params=params(),
            **kwargs,
        )(info, *operands)

    outer_moves = [(i, i - 1 if i % 2 == 0 else i + 1) for i in range(tiles)]
    outer_moves = [(i, j) for i, j in outer_moves if 0 <= j < tiles]
    odd = tile % 2 == 1
    stats_shape = shape(3, SLOTS, LANES, dtype=F32)
    stats = call(
        functools.partial(stats_kernel, rows), [source], stats_shape,
        cost_estimate=cost(1.5), name="first_stats",
    )
    inner = exchange(jnp.where(odd, source[:1], source[row_count - 1 :]), tiles, 1)
    outer = lax.ppermute(
        jnp.where(odd, source[row_count - 1 :], source[:1]), "tile", outer_moves
    )
    taps = min(3, frames)
    held = pl.pallas_call(
        functools.partial(hold_kernel, taps),
        out_shape=shape(3 * taps * channels, 3 * channels),
        in_specs=[HBM_SPEC],
        out_specs=VMEM_SPEC,
        scratch_shapes=[pltpu.SemaphoreType.DMA((3, 3 * taps))],
        compiler_params=pltpu.CompilerParams(vmem_limit_bytes=CONV_VMEM_BYTES),
        cost_estimate=cost(1.0 * taps),
        name="hold",
    )(conv_weight)
    rounds = merge_masks(tiles)
    for index, masks in enumerate(rounds):
        stats = merge_round(stats, tiles, masks)
        if index == 0:
            stats, held = lax.optimization_barrier((stats, held))
    hidden, source = call(
        functools.partial(hidden_kernel, rows),
        [inner, source, outer, stats, row(first_gain), row(first_shift)],
        (shape(near_rows, padded, channels), shape(row_count, cols, channels)),
        cost_estimate=cost(1.3),
        name="hidden",
    )

    context = [hidden] + [
        lax.ppermute(hidden, "frame", [(i, i + by) for i in range(frames - by)])
        for by in range(1, taps)
    ]

    pairs = row_count // 2
    pair_shape = shape(pairs, 2 * cols, channels)
    own, stats = pl.pallas_call(
        functools.partial(conv_kernel, rows, taps),
        out_shape=(pair_shape, stats_shape),
        in_specs=[SMEM_SPEC] + [VMEM_SPEC] * (taps + 3),
        out_specs=(VMEM_SPEC, VMEM_SPEC),
        scratch_shapes=[
            pltpu.VMEM((row_count * padded, 3 * taps * channels), BF16),
        ],
        compiler_params=params(),
        cost_estimate=cost(2.5 * taps),
        name="conv",
    )(info, *context, source, row(conv_bias), held)

    blocks = {0: own}
    neighbour = [(i, i ^ 1) for i in range(tiles)]
    if tiles == 16 and video_cols.shape[0] == 2:
        def middle(t):
            return t // 4 in (1, 2)

        stats = merge_round(stats, tiles, rounds[1])
        other = exchange(own, tiles, 1)
        blocks[1] = exchange(own, tiles, 2)
        blocks[2] = exchange(own, tiles, 4)
        blocks[6] = exchange(own, tiles, 12, middle)
        stats, other, blocks[1], blocks[2], blocks[6] = lax.optimization_barrier(
            (stats, other, blocks[1], blocks[2], blocks[6])
        )
        stats = merge_round(stats, tiles, rounds[0])
        inward = exchange(blocks[2], tiles, 12, middle)
        outward = exchange(blocks[6], tiles, 4, middle)
        blocks[4] = jnp.where((tile // 4 == 1) | (tile // 4 == 2), inward, outward)
        blocks[7] = exchange(blocks[6], tiles, 2, middle)
        blocks[5] = exchange(blocks[4], tiles, 2)
        passed, blocks[4] = lax.optimization_barrier((blocks[1], blocks[4]))
        blocks[3] = exchange(passed, tiles, 4)
        groups = [[0, 1, 2, 6], [4], [7, 3, 5]]
    else:
        for masks in rounds:
            stats = merge_round(stats, tiles, masks)
        other = exchange(own, tiles, 1)
        for mask in range(1, tiles // 2):
            blocks[mask] = exchange(own, tiles, 2 * mask)
        groups = [list(range(i, i + 4)) for i in range(0, tiles // 2, 4)]
    gain, shift = row(second_gain), row(second_shift)
    query_shapes = (shape(cells, channels), shape(cells, LANES, dtype=F32))
    mine_queries, mine_constant, queries, constant = call(
        functools.partial(query_kernel, rows),
        [own, other, stats, gain, shift, triple_weight, row(triple_bias)],
        query_shapes * 2,
        cost_estimate=cost(1.9),
        name="queries",
    )

    level_shape = shape(cells, LANES, dtype=F32)
    total_shape = shape(cells, channels, dtype=F32)
    state, keys = (), []
    for index, masks in enumerate(groups):
        last = index == len(groups) - 1
        outs = (shape(len(masks) * cells, channels),)
        outs += (shape(cells + 16, channels),) if last else (level_shape, level_shape, total_shape)
        normed, *state = call(
            functools.partial(attend_yours_kernel, rows, tuple(masks), index == 0, last),
            [stats, gain, shift, queries, constant] + [blocks[m] for m in masks] + list(state),
            outs,
            cost_estimate=cost(1.0 * len(masks)),
            name="attend_yours",
        )
        keys.append(normed)
    (sent,) = state
    received = lax.ppermute(sent, "tile", neighbour)
    sent, mine_queries, upsample_weight = lax.optimization_barrier(
        (sent, mine_queries, upsample_weight)
    )
    mean, level = call(
        functools.partial(attend_mine_kernel, rows, tuple(tuple(masks) for masks in groups)),
        [mine_queries, mine_constant] + keys,
        (total_shape, level_shape),
        cost_estimate=cost(6.0),
        name="attend_mine",
    )
    folded = pl.pallas_call(
        fold_kernel,
        out_shape=shape(2, 2, 2, out_channels, 2 * channels),
        in_specs=[VMEM_SPEC],
        out_specs=VMEM_SPEC,
        compiler_params=params(),
        cost_estimate=cost(0.5),
        name="fold",
    )(jnp.swapaxes(upsample_weight, 2, 3))

    rim_shape = shape(1, cols, channels)
    attended, inner, outer = call(
        functools.partial(finish_kernel, rows),
        [
            mean, level, received, own, triple_weight, row(triple_bias), output_weight,
            row(output_bias),
        ],
        (shape(row_count, cols, channels), rim_shape, rim_shape),
        cost_estimate=cost(1.4),
        name="finish",
    )
    outer = lax.ppermute(outer, "tile", outer_moves)
    inner = exchange(inner, tiles, 1)
    decoded = call(
        functools.partial(upsample_kernel, rows),
        [inner, attended, outer, folded, row(upsample_bias)],
        shape(2 * row_count, 2 * cols, out_channels),
        scratch=[
            pltpu.VMEM((near_rows * padded, 3 * channels), BF16),
            pltpu.VMEM((-(-out_channels // LANES), 2 * row_count, 2 * cols, LANES), F32),
        ],
        cost_estimate=cost(2.3),
        name="upsample",
    )
    return decoded.reshape(2 * row_count, 1, 2 * cols, out_channels)


def solution(mesh):
    sizes = dict(mesh.shape)
    in_specs = (P("tile", "frame", None, None),) + (P(),) * 14
    out_specs = P("tile", "frame", None, None)
    body = functools.partial(shards, sizes["tile"], sizes["frame"])
    return jax.shard_map(body, mesh=mesh, in_specs=in_specs, out_specs=out_specs, check_vma=False)
```

```python
import functools
import math

import jax
import jax.numpy as jnp
from jax import lax
from jax.experimental import pallas as pl
from jax.experimental.pallas import tpu as pltpu
from jax.sharding import PartitionSpec as P

GROUPS = 32
EPSILON = 1e-05
MASKED = -1e30
LOWEST = -5e29
HIGHEST = lax.Precision.HIGHEST
SLOTS = 8
ROWS_OF_TILE = 4
LANES = 128
VMEM_BYTES = 24 * 1024 * 1024
F32 = jnp.float32
BF16 = jnp.bfloat16

SMEM_SPEC = pl.BlockSpec(memory_space=pltpu.SMEM)
VMEM_SPEC = pl.BlockSpec(memory_space=pltpu.VMEM)
HBM_SPEC = pl.BlockSpec(memory_space=pltpu.HBM)


def cost(microseconds):
    return pl.CostEstimate(
        flops=int(microseconds * 1.1e9), bytes_accessed=0, transcendentals=0
    )


def params():
    return pltpu.CompilerParams(vmem_limit_bytes=VMEM_BYTES)


def member_matrix(channels):
    per_group = channels // GROUPS
    group = lax.broadcasted_iota(jnp.int32, (LANES, channels), 0) * per_group
    channel = lax.broadcasted_iota(jnp.int32, (LANES, channels), 1)
    return jnp.where((channel >= group) & (channel < group + per_group), 1.0, 0.0).astype(F32)


def to_groups(values, member):
    return lax.dot_general(
        values, member, (((1,), (1,)), ((), ())), precision=HIGHEST, preferred_element_type=F32
    )


def to_channels(values, member):
    return jnp.dot(values, member, precision=HIGHEST, preferred_element_type=F32)


class Info:
    def __init__(self, ref, rows):
        self.ref, self.rows = ref, rows
        self.videos = ref.shape[0] - 1 - rows

    def tile(self):
        return self.ref[0]

    def label(self, row):
        inside = (row >= 0) & (row < self.rows)
        return jnp.where(inside, self.ref[1 + jnp.clip(row, 0, self.rows - 1)], -1)

    def width(self, label):
        return jnp.where(label >= 0, self.ref[1 + self.rows + jnp.maximum(label, 0)], 0)

    def window(self, first, count):
        labels = [self.label(first + r) for r in range(count)]
        return labels, [self.width(label) for label in labels]


def pick(table, label, videos):
    chosen = table[0:1]
    for video in range(1, videos):
        chosen = jnp.where(label == video, table[video : video + 1], chosen)
    return chosen


def norm_tables(stats_ref, gain_ref):
    member = member_matrix(gain_ref.shape[1])
    counts = jnp.maximum(stats_ref[0], 1.0)
    scale = lax.rsqrt(stats_ref[2] / counts + EPSILON)
    return to_channels(stats_ref[1], member), to_channels(scale, member) * gain_ref[...]


def write_stats(out_ref, rows, labels, widths, videos, channels):
    member = member_matrix(channels)
    per_group = channels // GROUPS
    cols = rows[0].shape[0]
    slot = lax.broadcasted_iota(jnp.int32, (SLOTS, 1), 0)
    column = lax.broadcasted_iota(jnp.int32, (cols, 1), 0)
    sums = jnp.zeros((SLOTS, channels), F32)
    counts = jnp.zeros((SLOTS, 1), F32)
    for index, row in enumerate(rows):
        sums = jnp.where(slot == index, jnp.sum(row, axis=0, keepdims=True), sums)
        counts = jnp.where(slot == index, (widths[index] * per_group).astype(F32), counts)
    means = to_groups(sums, member) / jnp.maximum(counts, 1.0)
    means_wide = to_channels(means, member)
    squares = jnp.zeros((SLOTS, channels), F32)
    for index, row in enumerate(rows):
        centered = jnp.where(column < widths[index], row - means_wide[index : index + 1], 0.0)
        squares = jnp.where(
            slot == index, jnp.sum(centered * centered, axis=0, keepdims=True), squares
        )
    spreads = to_groups(squares, member)
    out_ref[...] = jnp.zeros(out_ref.shape, F32)
    for video in range(videos):
        total = jnp.zeros((1, LANES), F32)
        count = jnp.zeros((1, LANES), F32)
        for index in range(len(rows)):
            mine = labels[index] == video
            row_count = counts[index : index + 1]
            total = total + jnp.where(mine, means[index : index + 1] * row_count, 0.0)
            count = count + jnp.where(mine, row_count, 0.0)
        mean = total / jnp.maximum(count, 1.0)
        spread = jnp.zeros((1, LANES), F32)
        for index in range(len(rows)):
            off = means[index : index + 1] - mean
            part = spreads[index : index + 1] + counts[index : index + 1] * off * off
            spread = spread + jnp.where(labels[index] == video, part, 0.0)
        out_ref[0, video : video + 1, :] = count
        out_ref[1, video : video + 1, :] = mean
        out_ref[2, video : video + 1, :] = spread


def build_columns(columns_ref, row_refs):
    padded = columns_ref.shape[0] // len(row_refs)
    for index, row in enumerate(row_refs):
        cells = row().astype(F32)
        count, channels = cells.shape
        cells = jnp.concatenate([cells, jnp.zeros((padded - count, channels), F32)], axis=0)
        start = index * padded
        columns_ref[start : start + padded, 0:channels] = pltpu.roll(cells, 1, 0).astype(BF16)
        columns_ref[start : start + padded, channels : 2 * channels] = cells.astype(BF16)
        columns_ref[start : start + padded, 2 * channels : 3 * channels] = pltpu.roll(
            cells, padded - 1, 0
        ).astype(BF16)


def stats_kernel(rows, info_ref, latents_ref, out_ref):
    info = Info(info_ref, rows)
    row_count, cols, channels = latents_ref.shape
    labels, widths = info.window(info.tile() * row_count, row_count)
    column = lax.broadcasted_iota(jnp.int32, (cols, 1), 0)
    cells = [
        jnp.where(column < widths[r], latents_ref[r].astype(F32), 0.0) for r in range(row_count)
    ]
    write_stats(out_ref, cells, labels, widths, info.videos, channels)


def rims(info, inner_ref, outer_ref):
    odd = lax.rem(info.tile(), 2) == 1
    inner, outer = inner_ref[0].astype(F32), outer_ref[0].astype(F32)
    return jnp.where(odd, inner, outer), jnp.where(odd, outer, inner)


def hidden_kernel(
    rows, info_ref, inner_ref, latents_ref, outer_ref, stats_ref, gain_ref, shift_ref, out_ref,
    source_ref,
):
    info = Info(info_ref, rows)
    row_count, cols, _ = latents_ref.shape
    labels, widths = info.window(info.tile() * row_count - 1, row_count + 2)
    means, scales = norm_tables(stats_ref, gain_ref)
    column = lax.broadcasted_iota(jnp.int32, (cols, 1), 0)
    above, below = rims(info, inner_ref, outer_ref)
    sources = [above] + [latents_ref[r].astype(F32) for r in range(row_count)] + [below]
    for r, source in enumerate(sources):
        mean = pick(means, labels[r], info.videos)
        scale = pick(scales, labels[r], info.videos)
        normed = (source - mean) * scale + shift_ref[...]
        active = normed / (1.0 + jnp.exp(-normed))
        active = jnp.where(column < widths[r], active, 0.0)
        rest = jnp.zeros((out_ref.shape[1] - cols, active.shape[1]), F32)
        out_ref[r] = jnp.concatenate([active, rest], axis=0).astype(BF16)
    source_ref[...] = latents_ref[...]


def conv_kernel(rows, taps, info_ref, *rest):
    hidden_refs, rest = rest[:taps], rest[taps:]
    latents_ref, bias_ref, weight_ref, own_ref, stats_ref, inputs_ref, held_ref = rest
    row_count, cols, channels = latents_ref.shape
    info = Info(info_ref, rows)
    padded = hidden_refs[0].shape[1]
    labels, widths = info.window(info.tile() * row_count - 1, row_count + 2)
    for back, hidden_ref in enumerate(hidden_refs):
        for tap in range(3):
            lanes = slice((3 * back + tap) * channels, (3 * back + tap + 1) * channels)
            for r in range(row_count):
                block = hidden_ref[r + tap]
                if tap != 1:
                    same = labels[r + tap] == labels[r + 1]
                    block = jnp.where(same, block, jnp.zeros_like(block))
                inputs_ref[r * padded : (r + 1) * padded, lanes] = block
    for depth in range(3 * taps):
        for side in range(3):
            held_ref[
                depth * channels : (depth + 1) * channels, side * channels : (side + 1) * channels
            ] = weight_ref[2 - depth // 3, depth % 3, side]
    product = jnp.dot(inputs_ref[...], held_ref[...], preferred_element_type=F32)
    column = lax.broadcasted_iota(jnp.int32, (cols, 1), 0)
    cells = []
    for r in range(row_count):
        lines = slice(r * padded, (r + 1) * padded)
        branch = pltpu.roll(product[lines, 0:channels], 1, 0)
        branch = branch + product[lines, channels : 2 * channels]
        branch = branch + pltpu.roll(product[lines, 2 * channels :], padded - 1, 0)
        value = latents_ref[r].astype(F32) + branch[:cols] + bias_ref[...]
        value = jnp.where(column < widths[r + 1], value, 0.0).astype(BF16)
        cells.append(value.astype(F32))
    for pair in range(row_count // 2):
        own_ref[pair] = jnp.concatenate(cells[2 * pair : 2 * pair + 2], axis=0).astype(BF16)
    write_stats(stats_ref, cells, labels[1:-1], widths[1:-1], info.videos, channels)


def split_rows(pairs_ref):
    cols = pairs_ref.shape[1] // 2
    cells = []
    for pair in range(pairs_ref.shape[0]):
        both = pairs_ref[pair].astype(F32)
        cells += [both[:cols], both[cols:]]
    return cells


def turned_queries(info, tile, pairs_ref, means, scales, shift_ref, weight_ref, bias_ref):
    pairs, double, channels = pairs_ref.shape
    cols = double // 2
    column = lax.broadcasted_iota(jnp.int32, (cols, 1), 0)
    labels, widths = info.window(tile * 2 * pairs, 2 * pairs)
    cells = []
    for r, values in enumerate(split_rows(pairs_ref)):
        mean = pick(means, labels[r], info.videos)
        scale = pick(scales, labels[r], info.videos)
        normed = (values - mean) * scale + shift_ref[...]
        cells.append(jnp.where(column < widths[r], normed, 0.0))
    cells = jnp.concatenate(cells, axis=0).astype(BF16)
    queries = (
        jnp.dot(cells, weight_ref[:, 0:channels], preferred_element_type=F32)
        + bias_ref[:, 0:channels]
    ).astype(BF16)
    factor = channels ** (-0.5) * math.log2(math.e)
    turned = lax.dot_general(
        queries, weight_ref[:, channels : 2 * channels], (((1,), (1,)), ((), ())),
        preferred_element_type=F32,
    )
    constant = jnp.sum(
        queries.astype(F32) * bias_ref[:, channels : 2 * channels], axis=1, keepdims=True
    )
    return (turned * factor).astype(BF16), constant * factor


def query_kernel(
    rows, info_ref, other_ref, stats_ref, gain_ref, shift_ref, weight_ref, bias_ref, queries_ref,
    constant_ref, means_ref, scales_ref,
):
    info = Info(info_ref, rows)
    means, scales = norm_tables(stats_ref, gain_ref)
    means_ref[...] = means
    scales_ref[...] = scales
    queries, constant = turned_queries(
        info, info.tile() ^ 1, other_ref, means, scales, shift_ref, weight_ref, bias_ref
    )
    queries_ref[...] = queries
    constant_ref[...] = jnp.broadcast_to(constant, constant_ref.shape)


def key_codes(info, masks, span, cols):
    row_count = span // cols
    position = lax.broadcasted_iota(jnp.int32, (1, len(masks) * span), 1)
    codes = jnp.full((1, len(masks) * span), -2.0, F32)
    for index, mask in enumerate(masks):
        near, widths = info.window((info.tile() ^ (2 * mask)) * row_count, row_count)
        for r in range(row_count):
            start = index * span + r * cols
            inside = (position >= start) & (position < start + widths[r])
            codes = jnp.where(inside, near[r].astype(F32), codes)
    return codes


def query_codes(info, tile, span, cols):
    row_count = span // cols
    labels, _ = info.window(tile * row_count, row_count)
    return jnp.concatenate(
        [jnp.zeros((cols, 1), F32) + label.astype(F32) for label in labels], axis=0
    )


def scores_of(queries, keys, codes, query_code):
    scores = lax.dot_general(
        queries, keys, (((1,), (1,)), ((), ())), preferred_element_type=F32
    )
    return jnp.where(codes == query_code, scores, MASKED)


def mean_and_level(peak, denominator, total):
    some = denominator > 0.0
    safe = jnp.where(some, denominator, 1.0)
    return total / safe, jnp.where(some, peak + jnp.log2(safe), LOWEST)


def attend_yours_kernel(rows, masks, first, last, info_ref, *rest):
    means_ref, scales_ref, shift_ref, queries_ref, constant_ref, *rest = rest
    block_refs, rest = rest[: len(masks)], rest[len(masks) :]
    if not first:
        old_peak_ref, old_sum_ref, old_total_ref, *rest = rest
    keys_ref, *out_refs = rest
    info = Info(info_ref, rows)
    span, channels = queries_ref.shape
    pairs, double, _ = block_refs[0].shape
    cols = double // 2
    row_count = 2 * pairs
    tile = info.tile()
    means, scales = means_ref[...], scales_ref[...]
    for index, (mask, block_ref) in enumerate(zip(masks, block_refs)):
        near, _ = info.window((tile ^ (2 * mask)) * row_count, row_count)
        for pair in range(pairs):
            both = block_ref[pair].astype(F32)
            halves = []
            for half in range(2):
                label = near[2 * pair + half]
                mean = pick(means, label, info.videos)
                scale = pick(scales, label, info.videos)
                values = both[half * cols : (half + 1) * cols]
                halves.append((values - mean) * scale + shift_ref[...])
            start = index * span + pair * double
            keys_ref[start : start + double, :] = jnp.concatenate(halves, axis=0).astype(BF16)
    constant = constant_ref[:, 0:1]
    scores = scores_of(
        queries_ref[...], keys_ref[...], key_codes(info, masks, span, cols),
        query_codes(info, tile ^ 1, span, cols),
    )
    peak = jnp.maximum(LOWEST, jnp.max(scores, axis=1, keepdims=True) + constant)
    if not first:
        largest = old_peak_ref[:, 0:1]
        peak = jnp.maximum(largest, peak)
    weights = jnp.exp2(scores - (peak - constant))
    denominator = jnp.sum(weights, axis=1, keepdims=True)
    total = jnp.dot(weights.astype(BF16), keys_ref[...], preferred_element_type=F32)
    if not first:
        factor = jnp.exp2(largest - peak)
        denominator = old_sum_ref[:, 0:1] * factor + denominator
        total = old_total_ref[...] * factor + total
    if not last:
        peak_ref, sum_ref, total_ref = out_refs
        peak_ref[...] = jnp.broadcast_to(peak, peak_ref.shape)
        sum_ref[...] = jnp.broadcast_to(denominator, sum_ref.shape)
        total_ref[...] = total
        return
    (sent_ref,) = out_refs
    mean, level = mean_and_level(peak, denominator, total)
    sent_ref[0:span, :] = mean.astype(BF16)
    slots = sent_ref.shape[0] - span
    slot = lax.broadcasted_iota(jnp.int32, (slots, 1), 0)
    packed = jnp.zeros((slots, LANES), F32)
    for r in range(row_count):
        left = level[r * cols : (r + 1) * cols]
        left = jnp.sum(jnp.where(diagonal(cols), left, 0.0), axis=0, keepdims=True)
        for part in range(3):
            rounded = left.astype(BF16).astype(F32)
            packed = jnp.where(slot == 3 * r + part, rounded, packed)
            left = left - rounded
    sent_ref[span:, 0:LANES] = packed.astype(BF16)
    sent_ref[span:, LANES:] = jnp.zeros((slots, channels - LANES), BF16)


def attend_mine_kernel(
    rows, groups, info_ref, own_ref, means_ref, scales_ref, shift_ref, weight_ref, bias_ref, *rest
):
    key_refs, (mean_ref, level_ref) = rest[: len(groups)], rest[len(groups) :]
    info = Info(info_ref, rows)
    span = mean_ref.shape[0]
    queries, constant = turned_queries(
        info, info.tile(), own_ref, means_ref[...], scales_ref[...], shift_ref, weight_ref,
        bias_ref,
    )
    cols = span // ROWS_OF_TILE
    query_code = query_codes(info, info.tile(), span, cols)
    peak = jnp.full((span, 1), LOWEST, F32)
    scores = []
    for masks, key_ref in zip(groups, key_refs):
        codes = key_codes(info, masks, span, cols)
        scores.append(scores_of(queries, key_ref[...], codes, query_code))
        peak = jnp.maximum(peak, jnp.max(scores[-1], axis=1, keepdims=True) + constant)
    denominator, total = 0.0, 0.0
    for part, key_ref in zip(scores, key_refs):
        weights = jnp.exp2(part - (peak - constant))
        denominator = denominator + jnp.sum(weights, axis=1, keepdims=True)
        total = total + jnp.dot(
            weights.astype(BF16), key_ref[...], preferred_element_type=F32
        )
    mean, level = mean_and_level(peak, denominator, total)
    mean_ref[...] = mean
    level_ref[...] = jnp.broadcast_to(level, level_ref.shape)


def diagonal(cols):
    return lax.broadcasted_iota(jnp.int32, (cols, LANES), 0) == lax.broadcasted_iota(
        jnp.int32, (cols, LANES), 1
    )


def finish_kernel(
    rows, info_ref, mean_ref, level_ref, received_ref, own_ref, triple_ref, triple_bias_ref,
    output_ref, output_bias_ref, out_ref, inner_ref, outer_ref,
):
    info = Info(info_ref, rows)
    row_count, cols, channels = out_ref.shape
    span = row_count * cols
    _, widths = info.window(info.tile() * row_count, row_count)
    received = received_ref[0:span, :].astype(F32)
    levels = received_ref[span:, 0:LANES].astype(F32)
    yours = []
    for r in range(row_count):
        level = levels[3 * r : 3 * r + 1] + levels[3 * r + 1 : 3 * r + 2]
        level = level + levels[3 * r + 2 : 3 * r + 3]
        yours.append(jnp.sum(jnp.where(diagonal(cols), level, 0.0), axis=1, keepdims=True))
    yours = jnp.concatenate(yours, axis=0)
    mine = level_ref[:, 0:1]
    peak = jnp.maximum(mine, yours)
    weight, other_weight = jnp.exp2(mine - peak), jnp.exp2(yours - peak)
    share = weight / (weight + other_weight)
    mean_cell = (mean_ref[...] * share + received * (1.0 - share)).astype(BF16)
    mixed = (
        jnp.dot(mean_cell, triple_ref[:, 2 * channels :], preferred_element_type=F32)
        + triple_bias_ref[:, 2 * channels :]
    ).astype(BF16)
    attended = jnp.dot(mixed, output_ref[...], preferred_element_type=F32) + output_bias_ref[...]
    column = lax.broadcasted_iota(jnp.int32, (cols, 1), 0)
    for r, before in enumerate(split_rows(own_ref)):
        value = before + attended[r * cols : (r + 1) * cols]
        value = jnp.where(column < widths[r], value, 0.0)
        out_ref[r] = value.astype(BF16)
        if r == 0:
            top = value
    odd = lax.rem(info.tile(), 2) == 1
    inner_ref[0] = jnp.where(odd, top, value).astype(BF16)
    outer_ref[0] = jnp.where(odd, value, top).astype(BF16)


def fold_kernel(weight_ref, out_ref):
    channels = weight_ref.shape[-1]
    wide = [[weight_ref[a, b].astype(F32) for b in range(3)] for a in range(3)]

    def both(upper, lower):
        return [x + y for x, y in zip(upper, lower)]

    phases = [[wide[0], both(wide[1], wide[2])], [both(wide[0], wide[1]), wide[2]]]
    for down in range(2):
        for tap in range(2):
            left, middle, right = phases[down][tap]
            out_ref[down, tap, 0, :, 0:channels] = left.astype(BF16)
            out_ref[down, tap, 0, :, channels:] = (middle + right).astype(BF16)
            out_ref[down, tap, 1, :, 0:channels] = (left + middle).astype(BF16)
            out_ref[down, tap, 1, :, channels:] = right.astype(BF16)


def upsample_kernel(
    rows, info_ref, inner_ref, own_ref, outer_ref, weight_ref, bias_ref, out_ref, columns_ref,
    wide_ref,
):
    info = Info(info_ref, rows)
    row_count, cols, channels = own_ref.shape
    near_rows = row_count + 2
    padded = columns_ref.shape[0] // near_rows
    parts_out = wide_ref.shape[0]
    out_channels = out_ref.shape[-1]
    labels, widths = info.window(info.tile() * row_count - 1, near_rows)
    above, below = rims(info, inner_ref, outer_ref)
    sources = [lambda: above]
    sources += [functools.partial(own_ref.__getitem__, r) for r in range(row_count)]
    sources += [lambda: below]
    build_columns(columns_ref, sources)
    span = row_count * padded
    wide_column = lax.broadcasted_iota(jnp.int32, (2 * cols, 1), 0)
    for down in range(2):
        for right in range(2):
            lanes = slice(right * channels, (right + 2) * channels)
            products = [
                lax.dot_general(
                    columns_ref[(down + tap) * padded : (down + tap) * padded + span, lanes],
                    weight_ref[down, tap, right],
                    (((1,), (1,)), ((), ())),
                    preferred_element_type=F32,
                )
                for tap in range(2)
            ]
            rim, same = products[down], products[1 - down]
            for r in range(row_count):
                lo, hi = r * padded, r * padded + cols
                near = labels[r + 2 * down]
                value = same[lo:hi] + jnp.where(near == labels[r + 1], rim[lo:hi], 0.0)
                for part in range(parts_out):
                    part_lo, part_hi = part * LANES, min((part + 1) * LANES, out_channels)
                    piece = value[:, part_lo:part_hi]
                    if part_hi - part_lo < LANES:
                        missing = LANES - (part_hi - part_lo)
                        piece = jnp.concatenate([piece, jnp.zeros((cols, missing), F32)], axis=1)
                    wide_ref[part, 2 * r + down, pl.ds(right, cols, 2), :] = piece
    for r in range(2 * row_count):
        valid = wide_column < 2 * widths[r // 2 + 1]
        for part in range(parts_out):
            lo, hi = part * LANES, min((part + 1) * LANES, out_channels)
            value = wide_ref[part, r, :, 0 : hi - lo] + bias_ref[:, lo:hi]
            out_ref[r, :, lo:hi] = jnp.where(valid, value, 0.0).astype(BF16)


def merge_stats(mine, other):
    count = mine[0] + other[0]
    safe = jnp.maximum(count, 1.0)
    off = other[1] - mine[1]
    mean = mine[1] + off * (other[0] / safe)
    spread = mine[2] + other[2] + off * off * (mine[0] * other[0] / safe)
    return jnp.stack([count, mean, spread])


def exchange(array, tiles, mask, among=None):
    moves = [(i, i ^ mask) for i in range(tiles) if among is None or among(i)]
    return lax.ppermute(array, "tile", moves)


def merge_round(stats, tiles, masks):
    parts = [stats] + [exchange(stats, tiles, mask) for mask in masks]
    while len(parts) > 1:
        parts = [merge_stats(*parts[i : i + 2]) for i in range(0, len(parts), 2)]
    return parts[0]


def merge_masks(tiles):
    bits = [1 << i for i in range(tiles.bit_length() - 1)]
    pairs = [bits[i : i + 2] for i in range(0, len(bits), 2)]
    return [[p[0], p[1], p[0] ^ p[1]] if len(p) == 2 else p for p in pairs]


def shards(
    tiles,
    frames,
    latents,
    row_video,
    video_cols,
    first_gain,
    first_shift,
    conv_weight,
    conv_bias,
    second_gain,
    second_shift,
    triple_weight,
    triple_bias,
    output_weight,
    output_bias,
    upsample_weight,
    upsample_bias,
):
    row_count, frame_count, cols, channels = latents.shape
    assert frame_count == 1 and row_count == ROWS_OF_TILE and tiles % 4 == 0
    out_channels = upsample_weight.shape[-1]
    rows = row_count * tiles
    cells = row_count * cols
    padded = -(-(cols + 1) // 16) * 16
    near_rows = row_count + 2
    source = latents.reshape(row_count, cols, channels)
    tile = lax.axis_index("tile").astype(jnp.int32)
    info = jnp.concatenate([jnp.reshape(tile, (1,)), row_video, video_cols])

    def row(vector):
        return vector.reshape(1, -1)

    def shape(*dims, dtype=BF16):
        return jax.ShapeDtypeStruct(dims, dtype)

    def call(kernel, operands, out_shape, scratch=(), **kwargs):
        many = isinstance(out_shape, tuple)
        return pl.pallas_call(
            kernel,
            out_shape=out_shape,
            in_specs=[SMEM_SPEC] + [VMEM_SPEC] * len(operands),
            out_specs=(VMEM_SPEC,) * len(out_shape) if many else VMEM_SPEC,
            scratch_shapes=list(scratch),
            compiler_params=params(),
            **kwargs,
        )(info, *operands)

    outer_moves = [(i, i - 1 if i % 2 == 0 else i + 1) for i in range(tiles)]
    outer_moves = [(i, j) for i, j in outer_moves if 0 <= j < tiles]
    odd = tile % 2 == 1
    stats_shape = shape(3, SLOTS, LANES, dtype=F32)
    stats = call(
        functools.partial(stats_kernel, rows), [source], stats_shape,
        cost_estimate=cost(1.5), name="first_stats",
    )
    inner = exchange(jnp.where(odd, source[:1], source[row_count - 1 :]), tiles, 1)
    outer = lax.ppermute(
        jnp.where(odd, source[row_count - 1 :], source[:1]), "tile", outer_moves
    )
    taps = min(3, frames)
    rounds = merge_masks(tiles)
    for index, masks in enumerate(rounds):
        stats = merge_round(stats, tiles, masks)
        if index == 0:
            stats, inner, outer = lax.optimization_barrier((stats, inner, outer))
    hidden, source = call(
        functools.partial(hidden_kernel, rows),
        [inner, source, outer, stats, row(first_gain), row(first_shift)],
        (shape(near_rows, padded, channels), shape(row_count, cols, channels)),
        cost_estimate=cost(1.3),
        name="hidden",
    )

    context = [hidden] + [
        lax.ppermute(hidden, "frame", [(i, i + by) for i in range(frames - by)])
        for by in range(1, taps)
    ]

    pairs = row_count // 2
    pair_shape = shape(pairs, 2 * cols, channels)
    own, stats = pl.pallas_call(
        functools.partial(conv_kernel, rows, taps),
        out_shape=(pair_shape, stats_shape),
        in_specs=[SMEM_SPEC] + [VMEM_SPEC] * (taps + 3),
        out_specs=(VMEM_SPEC, VMEM_SPEC),
        scratch_shapes=[
            pltpu.VMEM((row_count * padded, 3 * taps * channels), BF16),
            pltpu.VMEM((3 * taps * channels, 3 * channels), BF16),
        ],
        compiler_params=params(),
        cost_estimate=cost(2.5 * taps),
        name="conv",
    )(info, *context, source, row(conv_bias), conv_weight)

    blocks = {0: own}
    neighbour = [(i, i ^ 1) for i in range(tiles)]
    if tiles == 16 and video_cols.shape[0] == 2:
        def middle(t):
            return t // 4 in (1, 2)

        stats = merge_round(stats, tiles, rounds[1])
        blocks[2] = exchange(own, tiles, 4)
        blocks[6] = exchange(own, tiles, 12, middle)
        stats = merge_round(stats, tiles, rounds[0])
        own_xy, stats = lax.optimization_barrier((own, stats))
        other = exchange(own_xy, tiles, 1)
        blocks[1] = exchange(own_xy, tiles, 2)
        other, blocks[1] = lax.optimization_barrier((other, blocks[1]))
        inward = exchange(blocks[2], tiles, 12, middle)
        outward = exchange(blocks[6], tiles, 4, middle)
        blocks[4] = jnp.where((tile // 4 == 1) | (tile // 4 == 2), inward, outward)
        blocks[7] = exchange(blocks[6], tiles, 2, middle)
        blocks[5] = exchange(blocks[4], tiles, 2)
        passed, blocks[4] = lax.optimization_barrier((blocks[1], blocks[4]))
        blocks[3] = exchange(passed, tiles, 4)
        groups = [[0, 1, 2, 6], [4, 7, 3, 5]]
    else:
        for masks in rounds:
            stats = merge_round(stats, tiles, masks)
        other = exchange(own, tiles, 1)
        for mask in range(1, tiles // 2):
            blocks[mask] = exchange(own, tiles, 2 * mask)
        groups = [list(range(i, i + 4)) for i in range(0, tiles // 2, 4)]
    gain, shift = row(second_gain), row(second_shift)
    table_shape = shape(SLOTS, channels, dtype=F32)
    queries, constant, means, scales = call(
        functools.partial(query_kernel, rows),
        [other, stats, gain, shift, triple_weight, row(triple_bias)],
        (shape(cells, channels), shape(cells, LANES, dtype=F32), table_shape, table_shape),
        cost_estimate=cost(1.5),
        name="queries",
    )
    level_shape = shape(cells, LANES, dtype=F32)
    total_shape = shape(cells, channels, dtype=F32)
    state, keys = (), []
    for index, masks in enumerate(groups):
        last = index == len(groups) - 1
        outs = (shape(len(masks) * cells, channels),)
        outs += (shape(cells + 16, channels),) if last else (level_shape, level_shape, total_shape)
        normed, *state = call(
            functools.partial(attend_yours_kernel, rows, tuple(masks), index == 0, last),
            [means, scales, shift, queries, constant] + [blocks[m] for m in masks] + list(state),
            outs,
            cost_estimate=cost(0.9 * len(masks)),
            name="attend_yours",
        )
        keys.append(normed)
    (sent,) = state
    received = lax.ppermute(sent, "tile", neighbour)
    sent, own_late, upsample_weight = lax.optimization_barrier((sent, own, upsample_weight))
    mean, level = call(
        functools.partial(attend_mine_kernel, rows, tuple(tuple(masks) for masks in groups)),
        [own_late, means, scales, shift, triple_weight, row(triple_bias)] + keys,
        (total_shape, level_shape),
        cost_estimate=cost(6.0),
        name="attend_mine",
    )
    folded = pl.pallas_call(
        fold_kernel,
        out_shape=shape(2, 2, 2, out_channels, 2 * channels),
        in_specs=[VMEM_SPEC],
        out_specs=VMEM_SPEC,
        compiler_params=params(),
        cost_estimate=cost(0.5),
        name="fold",
    )(jnp.swapaxes(upsample_weight, 2, 3))

    rim_shape = shape(1, cols, channels)
    attended, inner, outer = call(
        functools.partial(finish_kernel, rows),
        [
            mean, level, received, own, triple_weight, row(triple_bias), output_weight,
            row(output_bias),
        ],
        (shape(row_count, cols, channels), rim_shape, rim_shape),
        cost_estimate=cost(1.4),
        name="finish",
    )
    outer = lax.ppermute(outer, "tile", outer_moves)
    inner = exchange(inner, tiles, 1)
    decoded = call(
        functools.partial(upsample_kernel, rows),
        [inner, attended, outer, folded, row(upsample_bias)],
        shape(2 * row_count, 2 * cols, out_channels),
        scratch=[
            pltpu.VMEM((near_rows * padded, 3 * channels), BF16),
            pltpu.VMEM((-(-out_channels // LANES), 2 * row_count, 2 * cols, LANES), F32),
        ],
        cost_estimate=cost(2.3),
        name="upsample",
    )
    return decoded.reshape(2 * row_count, 1, 2 * cols, out_channels)


def solution(mesh):
    sizes = dict(mesh.shape)
    in_specs = (P("tile", "frame", None, None),) + (P(),) * 14
    out_specs = P("tile", "frame", None, None)
    body = functools.partial(shards, sizes["tile"], sizes["frame"])
    return jax.shard_map(body, mesh=mesh, in_specs=in_specs, out_specs=out_specs, check_vma=False)
```

```python
import functools
import math

import jax
import jax.numpy as jnp
from jax import lax
from jax.experimental import pallas as pl
from jax.experimental.pallas import tpu as pltpu
from jax.sharding import PartitionSpec as P

GROUPS = 32
EPSILON = 1e-05
MASKED = -1e30
LOWEST = -5e29
HIGHEST = lax.Precision.HIGHEST
SLOTS = 8
ROWS_OF_TILE = 4
LANES = 128
VMEM_BYTES = 24 * 1024 * 1024
HIDDEN_VMEM_BYTES = 46 * 1024 * 1024
F32 = jnp.float32
BF16 = jnp.bfloat16

SMEM_SPEC = pl.BlockSpec(memory_space=pltpu.SMEM)
VMEM_SPEC = pl.BlockSpec(memory_space=pltpu.VMEM)
HBM_SPEC = pl.BlockSpec(memory_space=pltpu.HBM)


def cost(microseconds):
    return pl.CostEstimate(
        flops=int(microseconds * 1.1e9), bytes_accessed=0, transcendentals=0
    )


def params():
    return pltpu.CompilerParams(vmem_limit_bytes=VMEM_BYTES)


def member_matrix(channels):
    per_group = channels // GROUPS
    group = lax.broadcasted_iota(jnp.int32, (LANES, channels), 0) * per_group
    channel = lax.broadcasted_iota(jnp.int32, (LANES, channels), 1)
    return jnp.where((channel >= group) & (channel < group + per_group), 1.0, 0.0).astype(F32)


def to_groups(values, member):
    return lax.dot_general(
        values, member, (((1,), (1,)), ((), ())), precision=HIGHEST, preferred_element_type=F32
    )


def to_channels(values, member):
    return jnp.dot(values, member, precision=HIGHEST, preferred_element_type=F32)


class Info:
    def __init__(self, ref, rows):
        self.ref, self.rows = ref, rows
        self.videos = ref.shape[0] - 1 - rows

    def tile(self):
        return self.ref[0]

    def label(self, row):
        inside = (row >= 0) & (row < self.rows)
        return jnp.where(inside, self.ref[1 + jnp.clip(row, 0, self.rows - 1)], -1)

    def width(self, label):
        return jnp.where(label >= 0, self.ref[1 + self.rows + jnp.maximum(label, 0)], 0)

    def window(self, first, count):
        labels = [self.label(first + r) for r in range(count)]
        return labels, [self.width(label) for label in labels]


def pick(table, label, videos):
    chosen = table[0:1]
    for video in range(1, videos):
        chosen = jnp.where(label == video, table[video : video + 1], chosen)
    return chosen


def norm_tables(stats_ref, gain_ref):
    member = member_matrix(gain_ref.shape[1])
    counts = jnp.maximum(stats_ref[0], 1.0)
    scale = lax.rsqrt(stats_ref[2] / counts + EPSILON)
    return to_channels(stats_ref[1], member), to_channels(scale, member) * gain_ref[...]


def write_stats(out_ref, rows, labels, widths, videos, channels):
    member = member_matrix(channels)
    per_group = channels // GROUPS
    cols = rows[0].shape[0]
    slot = lax.broadcasted_iota(jnp.int32, (SLOTS, 1), 0)
    column = lax.broadcasted_iota(jnp.int32, (cols, 1), 0)
    sums = jnp.zeros((SLOTS, channels), F32)
    counts = jnp.zeros((SLOTS, 1), F32)
    for index, row in enumerate(rows):
        sums = jnp.where(slot == index, jnp.sum(row, axis=0, keepdims=True), sums)
        counts = jnp.where(slot == index, (widths[index] * per_group).astype(F32), counts)
    means = to_groups(sums, member) / jnp.maximum(counts, 1.0)
    means_wide = to_channels(means, member)
    squares = jnp.zeros((SLOTS, channels), F32)
    for index, row in enumerate(rows):
        centered = jnp.where(column < widths[index], row - means_wide[index : index + 1], 0.0)
        squares = jnp.where(
            slot == index, jnp.sum(centered * centered, axis=0, keepdims=True), squares
        )
    spreads = to_groups(squares, member)
    out_ref[...] = jnp.zeros(out_ref.shape, F32)
    for video in range(videos):
        total = jnp.zeros((1, LANES), F32)
        count = jnp.zeros((1, LANES), F32)
        for index in range(len(rows)):
            mine = labels[index] == video
            row_count = counts[index : index + 1]
            total = total + jnp.where(mine, means[index : index + 1] * row_count, 0.0)
            count = count + jnp.where(mine, row_count, 0.0)
        mean = total / jnp.maximum(count, 1.0)
        spread = jnp.zeros((1, LANES), F32)
        for index in range(len(rows)):
            off = means[index : index + 1] - mean
            part = spreads[index : index + 1] + counts[index : index + 1] * off * off
            spread = spread + jnp.where(labels[index] == video, part, 0.0)
        out_ref[0, video : video + 1, :] = count
        out_ref[1, video : video + 1, :] = mean
        out_ref[2, video : video + 1, :] = spread


def build_columns(columns_ref, row_refs):
    padded = columns_ref.shape[0] // len(row_refs)
    for index, row in enumerate(row_refs):
        cells = row().astype(F32)
        count, channels = cells.shape
        cells = jnp.concatenate([cells, jnp.zeros((padded - count, channels), F32)], axis=0)
        start = index * padded
        columns_ref[start : start + padded, 0:channels] = pltpu.roll(cells, 1, 0).astype(BF16)
        columns_ref[start : start + padded, channels : 2 * channels] = cells.astype(BF16)
        columns_ref[start : start + padded, 2 * channels : 3 * channels] = pltpu.roll(
            cells, padded - 1, 0
        ).astype(BF16)


def stats_kernel(rows, info_ref, latents_ref, out_ref):
    info = Info(info_ref, rows)
    row_count, cols, channels = latents_ref.shape
    labels, widths = info.window(info.tile() * row_count, row_count)
    column = lax.broadcasted_iota(jnp.int32, (cols, 1), 0)
    cells = [
        jnp.where(column < widths[r], latents_ref[r].astype(F32), 0.0) for r in range(row_count)
    ]
    write_stats(out_ref, cells, labels, widths, info.videos, channels)


def rims(info, inner_ref, outer_ref):
    odd = lax.rem(info.tile(), 2) == 1
    inner, outer = inner_ref[0].astype(F32), outer_ref[0].astype(F32)
    return jnp.where(odd, inner, outer), jnp.where(odd, outer, inner)


def hidden_kernel(
    rows, info_ref, inner_ref, latents_ref, outer_ref, stats_ref, gain_ref, shift_ref, weight_ref,
    out_ref, source_ref, held_ref, sems,
):
    channels = weight_ref.shape[-1]
    copies = [
        pltpu.make_async_copy(
            weight_ref.at[2 - depth // 3, depth % 3, side],
            held_ref.at[pl.ds(depth * channels, channels), pl.ds(side * channels, channels)],
            sems.at[side, depth],
        )
        for side in range(3)
        for depth in range(held_ref.shape[0] // channels)
    ]
    for copy in copies:
        copy.start()
    info = Info(info_ref, rows)
    row_count, cols, _ = latents_ref.shape
    labels, widths = info.window(info.tile() * row_count - 1, row_count + 2)
    means, scales = norm_tables(stats_ref, gain_ref)
    column = lax.broadcasted_iota(jnp.int32, (cols, 1), 0)
    above, below = rims(info, inner_ref, outer_ref)
    sources = [above] + [latents_ref[r].astype(F32) for r in range(row_count)] + [below]
    for r, source in enumerate(sources):
        mean = pick(means, labels[r], info.videos)
        scale = pick(scales, labels[r], info.videos)
        normed = (source - mean) * scale + shift_ref[...]
        active = normed / (1.0 + jnp.exp(-normed))
        active = jnp.where(column < widths[r], active, 0.0)
        rest = jnp.zeros((out_ref.shape[1] - cols, active.shape[1]), F32)
        out_ref[r] = jnp.concatenate([active, rest], axis=0).astype(BF16)
    source_ref[...] = latents_ref[...]
    for copy in copies:
        copy.wait()


def conv_kernel(rows, taps, info_ref, *rest):
    hidden_refs, rest = rest[:taps], rest[taps:]
    latents_ref, bias_ref, held_ref, own_ref, stats_ref, inputs_ref = rest
    row_count, cols, channels = latents_ref.shape
    info = Info(info_ref, rows)
    padded = hidden_refs[0].shape[1]
    labels, widths = info.window(info.tile() * row_count - 1, row_count + 2)
    for back, hidden_ref in enumerate(hidden_refs):
        for tap in range(3):
            lanes = slice((3 * back + tap) * channels, (3 * back + tap + 1) * channels)
            for r in range(row_count):
                block = hidden_ref[r + tap]
                if tap != 1:
                    same = labels[r + tap] == labels[r + 1]
                    block = jnp.where(same, block, jnp.zeros_like(block))
                inputs_ref[r * padded : (r + 1) * padded, lanes] = block
    product = jnp.dot(inputs_ref[...], held_ref[...], preferred_element_type=F32)
    column = lax.broadcasted_iota(jnp.int32, (cols, 1), 0)
    cells = []
    for r in range(row_count):
        lines = slice(r * padded, (r + 1) * padded)
        branch = pltpu.roll(product[lines, 0:channels], 1, 0)
        branch = branch + product[lines, channels : 2 * channels]
        branch = branch + pltpu.roll(product[lines, 2 * channels :], padded - 1, 0)
        value = latents_ref[r].astype(F32) + branch[:cols] + bias_ref[...]
        value = jnp.where(column < widths[r + 1], value, 0.0).astype(BF16)
        cells.append(value.astype(F32))
    for pair in range(row_count // 2):
        own_ref[pair] = jnp.concatenate(cells[2 * pair : 2 * pair + 2], axis=0).astype(BF16)
    write_stats(stats_ref, cells, labels[1:-1], widths[1:-1], info.videos, channels)


def split_rows(pairs_ref):
    cols = pairs_ref.shape[1] // 2
    cells = []
    for pair in range(pairs_ref.shape[0]):
        both = pairs_ref[pair].astype(F32)
        cells += [both[:cols], both[cols:]]
    return cells


def turned_queries(info, tile, pairs_ref, means, scales, shift_ref, weight_ref, bias_ref):
    pairs, double, channels = pairs_ref.shape
    cols = double // 2
    column = lax.broadcasted_iota(jnp.int32, (cols, 1), 0)
    labels, widths = info.window(tile * 2 * pairs, 2 * pairs)
    cells = []
    for r, values in enumerate(split_rows(pairs_ref)):
        mean = pick(means, labels[r], info.videos)
        scale = pick(scales, labels[r], info.videos)
        normed = (values - mean) * scale + shift_ref[...]
        cells.append(jnp.where(column < widths[r], normed, 0.0))
    cells = jnp.concatenate(cells, axis=0).astype(BF16)
    queries = (
        jnp.dot(cells, weight_ref[:, 0:channels], preferred_element_type=F32)
        + bias_ref[:, 0:channels]
    ).astype(BF16)
    factor = channels ** (-0.5) * math.log2(math.e)
    turned = lax.dot_general(
        queries, weight_ref[:, channels : 2 * channels], (((1,), (1,)), ((), ())),
        preferred_element_type=F32,
    )
    constant = jnp.sum(
        queries.astype(F32) * bias_ref[:, channels : 2 * channels], axis=1, keepdims=True
    )
    return (turned * factor).astype(BF16), constant * factor


def query_kernel(
    rows, info_ref, other_ref, stats_ref, gain_ref, shift_ref, weight_ref, bias_ref, queries_ref,
    constant_ref, means_ref, scales_ref,
):
    info = Info(info_ref, rows)
    means, scales = norm_tables(stats_ref, gain_ref)
    means_ref[...] = means
    scales_ref[...] = scales
    queries, constant = turned_queries(
        info, info.tile() ^ 1, other_ref, means, scales, shift_ref, weight_ref, bias_ref
    )
    queries_ref[...] = queries
    constant_ref[...] = jnp.broadcast_to(constant, constant_ref.shape)


def key_codes(info, masks, span, cols):
    row_count = span // cols
    position = lax.broadcasted_iota(jnp.int32, (1, len(masks) * span), 1)
    codes = jnp.full((1, len(masks) * span), -2.0, F32)
    for index, mask in enumerate(masks):
        near, widths = info.window((info.tile() ^ (2 * mask)) * row_count, row_count)
        for r in range(row_count):
            start = index * span + r * cols
            inside = (position >= start) & (position < start + widths[r])
            codes = jnp.where(inside, near[r].astype(F32), codes)
    return codes


def query_codes(info, tile, span, cols):
    row_count = span // cols
    labels, _ = info.window(tile * row_count, row_count)
    return jnp.concatenate(
        [jnp.zeros((cols, 1), F32) + label.astype(F32) for label in labels], axis=0
    )


def scores_of(queries, keys, codes, query_code):
    scores = lax.dot_general(
        queries, keys, (((1,), (1,)), ((), ())), preferred_element_type=F32
    )
    return jnp.where(codes == query_code, scores, MASKED)


def mean_and_level(peak, denominator, total):
    some = denominator > 0.0
    safe = jnp.where(some, denominator, 1.0)
    return total / safe, jnp.where(some, peak + jnp.log2(safe), LOWEST)


def attend_yours_kernel(rows, masks, first, last, info_ref, *rest):
    means_ref, scales_ref, shift_ref, queries_ref, constant_ref, *rest = rest
    block_refs, rest = rest[: len(masks)], rest[len(masks) :]
    if not first:
        old_peak_ref, old_sum_ref, old_total_ref, *rest = rest
    keys_ref, *out_refs = rest
    info = Info(info_ref, rows)
    span, channels = queries_ref.shape
    pairs, double, _ = block_refs[0].shape
    cols = double // 2
    row_count = 2 * pairs
    tile = info.tile()
    means, scales = means_ref[...], scales_ref[...]
    for index, (mask, block_ref) in enumerate(zip(masks, block_refs)):
        near, _ = info.window((tile ^ (2 * mask)) * row_count, row_count)
        for pair in range(pairs):
            both = block_ref[pair].astype(F32)
            halves = []
            for half in range(2):
                label = near[2 * pair + half]
                mean = pick(means, label, info.videos)
                scale = pick(scales, label, info.videos)
                values = both[half * cols : (half + 1) * cols]
                halves.append((values - mean) * scale + shift_ref[...])
            start = index * span + pair * double
            keys_ref[start : start + double, :] = jnp.concatenate(halves, axis=0).astype(BF16)
    constant = constant_ref[:, 0:1]
    scores = scores_of(
        queries_ref[...], keys_ref[...], key_codes(info, masks, span, cols),
        query_codes(info, tile ^ 1, span, cols),
    )
    peak = jnp.maximum(LOWEST, jnp.max(scores, axis=1, keepdims=True) + constant)
    if not first:
        largest = old_peak_ref[:, 0:1]
        peak = jnp.maximum(largest, peak)
    weights = jnp.exp2(scores - (peak - constant))
    denominator = jnp.sum(weights, axis=1, keepdims=True)
    total = jnp.dot(weights.astype(BF16), keys_ref[...], preferred_element_type=F32)
    if not first:
        factor = jnp.exp2(largest - peak)
        denominator = old_sum_ref[:, 0:1] * factor + denominator
        total = old_total_ref[...] * factor + total
    if not last:
        peak_ref, sum_ref, total_ref = out_refs
        peak_ref[...] = jnp.broadcast_to(peak, peak_ref.shape)
        sum_ref[...] = jnp.broadcast_to(denominator, sum_ref.shape)
        total_ref[...] = total
        return
    (sent_ref,) = out_refs
    mean, level = mean_and_level(peak, denominator, total)
    sent_ref[0:span, :] = mean.astype(BF16)
    slots = sent_ref.shape[0] - span
    slot = lax.broadcasted_iota(jnp.int32, (slots, 1), 0)
    packed = jnp.zeros((slots, LANES), F32)
    for r in range(row_count):
        left = level[r * cols : (r + 1) * cols]
        left = jnp.sum(jnp.where(diagonal(cols), left, 0.0), axis=0, keepdims=True)
        for part in range(3):
            rounded = left.astype(BF16).astype(F32)
            packed = jnp.where(slot == 3 * r + part, rounded, packed)
            left = left - rounded
    sent_ref[span:, 0:LANES] = packed.astype(BF16)
    sent_ref[span:, LANES:] = jnp.zeros((slots, channels - LANES), BF16)


def attend_mine_kernel(
    rows, groups, info_ref, own_ref, means_ref, scales_ref, shift_ref, weight_ref, bias_ref, *rest
):
    key_refs, (mean_ref, level_ref) = rest[: len(groups)], rest[len(groups) :]
    info = Info(info_ref, rows)
    span = mean_ref.shape[0]
    queries, constant = turned_queries(
        info, info.tile(), own_ref, means_ref[...], scales_ref[...], shift_ref, weight_ref,
        bias_ref,
    )
    cols = span // ROWS_OF_TILE
    query_code = query_codes(info, info.tile(), span, cols)
    peak = jnp.full((span, 1), LOWEST, F32)
    scores = []
    for masks, key_ref in zip(groups, key_refs):
        codes = key_codes(info, masks, span, cols)
        scores.append(scores_of(queries, key_ref[...], codes, query_code))
        peak = jnp.maximum(peak, jnp.max(scores[-1], axis=1, keepdims=True) + constant)
    denominator, total = 0.0, 0.0
    for part, key_ref in zip(scores, key_refs):
        weights = jnp.exp2(part - (peak - constant))
        denominator = denominator + jnp.sum(weights, axis=1, keepdims=True)
        total = total + jnp.dot(
            weights.astype(BF16), key_ref[...], preferred_element_type=F32
        )
    mean, level = mean_and_level(peak, denominator, total)
    mean_ref[...] = mean
    level_ref[...] = jnp.broadcast_to(level, level_ref.shape)


def diagonal(cols):
    return lax.broadcasted_iota(jnp.int32, (cols, LANES), 0) == lax.broadcasted_iota(
        jnp.int32, (cols, LANES), 1
    )


def finish_kernel(
    rows, info_ref, mean_ref, level_ref, received_ref, own_ref, triple_ref, triple_bias_ref,
    output_ref, output_bias_ref, out_ref, inner_ref, outer_ref,
):
    info = Info(info_ref, rows)
    row_count, cols, channels = out_ref.shape
    span = row_count * cols
    _, widths = info.window(info.tile() * row_count, row_count)
    received = received_ref[0:span, :].astype(F32)
    levels = received_ref[span:, 0:LANES].astype(F32)
    yours = []
    for r in range(row_count):
        level = levels[3 * r : 3 * r + 1] + levels[3 * r + 1 : 3 * r + 2]
        level = level + levels[3 * r + 2 : 3 * r + 3]
        yours.append(jnp.sum(jnp.where(diagonal(cols), level, 0.0), axis=1, keepdims=True))
    yours = jnp.concatenate(yours, axis=0)
    mine = level_ref[:, 0:1]
    peak = jnp.maximum(mine, yours)
    weight, other_weight = jnp.exp2(mine - peak), jnp.exp2(yours - peak)
    share = weight / (weight + other_weight)
    mean_cell = (mean_ref[...] * share + received * (1.0 - share)).astype(BF16)
    mixed = (
        jnp.dot(mean_cell, triple_ref[:, 2 * channels :], preferred_element_type=F32)
        + triple_bias_ref[:, 2 * channels :]
    ).astype(BF16)
    attended = jnp.dot(mixed, output_ref[...], preferred_element_type=F32) + output_bias_ref[...]
    column = lax.broadcasted_iota(jnp.int32, (cols, 1), 0)
    for r, before in enumerate(split_rows(own_ref)):
        value = before + attended[r * cols : (r + 1) * cols]
        value = jnp.where(column < widths[r], value, 0.0)
        out_ref[r] = value.astype(BF16)
        if r == 0:
            top = value
    odd = lax.rem(info.tile(), 2) == 1
    inner_ref[0] = jnp.where(odd, top, value).astype(BF16)
    outer_ref[0] = jnp.where(odd, value, top).astype(BF16)


def fold_kernel(weight_ref, out_ref):
    channels = weight_ref.shape[-1]
    wide = [[weight_ref[a, b].astype(F32) for b in range(3)] for a in range(3)]

    def both(upper, lower):
        return [x + y for x, y in zip(upper, lower)]

    phases = [[wide[0], both(wide[1], wide[2])], [both(wide[0], wide[1]), wide[2]]]
    for down in range(2):
        for tap in range(2):
            left, middle, right = phases[down][tap]
            out_ref[down, tap, 0, :, 0:channels] = left.astype(BF16)
            out_ref[down, tap, 0, :, channels:] = (middle + right).astype(BF16)
            out_ref[down, tap, 1, :, 0:channels] = (left + middle).astype(BF16)
            out_ref[down, tap, 1, :, channels:] = right.astype(BF16)


def upsample_kernel(
    rows, info_ref, inner_ref, own_ref, outer_ref, weight_ref, bias_ref, out_ref, columns_ref,
    wide_ref,
):
    info = Info(info_ref, rows)
    row_count, cols, channels = own_ref.shape
    near_rows = row_count + 2
    padded = columns_ref.shape[0] // near_rows
    parts_out = wide_ref.shape[0]
    out_channels = out_ref.shape[-1]
    labels, widths = info.window(info.tile() * row_count - 1, near_rows)
    above, below = rims(info, inner_ref, outer_ref)
    sources = [lambda: above]
    sources += [functools.partial(own_ref.__getitem__, r) for r in range(row_count)]
    sources += [lambda: below]
    build_columns(columns_ref, sources)
    span = row_count * padded
    wide_column = lax.broadcasted_iota(jnp.int32, (2 * cols, 1), 0)
    for down in range(2):
        for right in range(2):
            lanes = slice(right * channels, (right + 2) * channels)
            products = [
                lax.dot_general(
                    columns_ref[(down + tap) * padded : (down + tap) * padded + span, lanes],
                    weight_ref[down, tap, right],
                    (((1,), (1,)), ((), ())),
                    preferred_element_type=F32,
                )
                for tap in range(2)
            ]
            rim, same = products[down], products[1 - down]
            for r in range(row_count):
                lo, hi = r * padded, r * padded + cols
                near = labels[r + 2 * down]
                value = same[lo:hi] + jnp.where(near == labels[r + 1], rim[lo:hi], 0.0)
                for part in range(parts_out):
                    part_lo, part_hi = part * LANES, min((part + 1) * LANES, out_channels)
                    piece = value[:, part_lo:part_hi]
                    if part_hi - part_lo < LANES:
                        missing = LANES - (part_hi - part_lo)
                        piece = jnp.concatenate([piece, jnp.zeros((cols, missing), F32)], axis=1)
                    wide_ref[part, 2 * r + down, pl.ds(right, cols, 2), :] = piece
    for r in range(2 * row_count):
        valid = wide_column < 2 * widths[r // 2 + 1]
        for part in range(parts_out):
            lo, hi = part * LANES, min((part + 1) * LANES, out_channels)
            value = wide_ref[part, r, :, 0 : hi - lo] + bias_ref[:, lo:hi]
            out_ref[r, :, lo:hi] = jnp.where(valid, value, 0.0).astype(BF16)


def merge_stats(mine, other):
    count = mine[0] + other[0]
    safe = jnp.maximum(count, 1.0)
    off = other[1] - mine[1]
    mean = mine[1] + off * (other[0] / safe)
    spread = mine[2] + other[2] + off * off * (mine[0] * other[0] / safe)
    return jnp.stack([count, mean, spread])


def exchange(array, tiles, mask, among=None):
    moves = [(i, i ^ mask) for i in range(tiles) if among is None or among(i)]
    return lax.ppermute(array, "tile", moves)


def merge_round(stats, tiles, masks):
    parts = [stats] + [exchange(stats, tiles, mask) for mask in masks]
    while len(parts) > 1:
        parts = [merge_stats(*parts[i : i + 2]) for i in range(0, len(parts), 2)]
    return parts[0]


def merge_masks(tiles):
    bits = [1 << i for i in range(tiles.bit_length() - 1)]
    pairs = [bits[i : i + 2] for i in range(0, len(bits), 2)]
    return [[p[0], p[1], p[0] ^ p[1]] if len(p) == 2 else p for p in pairs]


def shards(
    tiles,
    frames,
    latents,
    row_video,
    video_cols,
    first_gain,
    first_shift,
    conv_weight,
    conv_bias,
    second_gain,
    second_shift,
    triple_weight,
    triple_bias,
    output_weight,
    output_bias,
    upsample_weight,
    upsample_bias,
):
    row_count, frame_count, cols, channels = latents.shape
    assert frame_count == 1 and row_count == ROWS_OF_TILE and tiles % 4 == 0
    out_channels = upsample_weight.shape[-1]
    rows = row_count * tiles
    cells = row_count * cols
    padded = -(-(cols + 1) // 16) * 16
    near_rows = row_count + 2
    source = latents.reshape(row_count, cols, channels)
    tile = lax.axis_index("tile").astype(jnp.int32)
    info = jnp.concatenate([jnp.reshape(tile, (1,)), row_video, video_cols])

    def row(vector):
        return vector.reshape(1, -1)

    def shape(*dims, dtype=BF16):
        return jax.ShapeDtypeStruct(dims, dtype)

    def call(kernel, operands, out_shape, scratch=(), **kwargs):
        many = isinstance(out_shape, tuple)
        return pl.pallas_call(
            kernel,
            out_shape=out_shape,
            in_specs=[SMEM_SPEC] + [VMEM_SPEC] * len(operands),
            out_specs=(VMEM_SPEC,) * len(out_shape) if many else VMEM_SPEC,
            scratch_shapes=list(scratch),
            compiler_params=params(),
            **kwargs,
        )(info, *operands)

    outer_moves = [(i, i - 1 if i % 2 == 0 else i + 1) for i in range(tiles)]
    outer_moves = [(i, j) for i, j in outer_moves if 0 <= j < tiles]
    odd = tile % 2 == 1
    stats_shape = shape(3, SLOTS, LANES, dtype=F32)
    stats = call(
        functools.partial(stats_kernel, rows), [source], stats_shape,
        cost_estimate=cost(1.5), name="first_stats",
    )
    inner = exchange(jnp.where(odd, source[:1], source[row_count - 1 :]), tiles, 1)
    outer = lax.ppermute(
        jnp.where(odd, source[row_count - 1 :], source[:1]), "tile", outer_moves
    )
    taps = min(3, frames)
    rounds = merge_masks(tiles)
    for index, masks in enumerate(reversed(rounds)):
        stats = merge_round(stats, tiles, masks)
        if index == 0:
            stats, inner, outer = lax.optimization_barrier((stats, inner, outer))
    hidden, source, held = pl.pallas_call(
        functools.partial(hidden_kernel, rows),
        out_shape=(
            shape(near_rows, padded, channels),
            shape(row_count, cols, channels),
            shape(3 * taps * channels, 3 * channels),
        ),
        in_specs=[SMEM_SPEC] + [VMEM_SPEC] * 6 + [HBM_SPEC],
        out_specs=(VMEM_SPEC,) * 3,
        scratch_shapes=[pltpu.SemaphoreType.DMA((3, 3 * taps))],
        compiler_params=pltpu.CompilerParams(vmem_limit_bytes=HIDDEN_VMEM_BYTES),
        cost_estimate=cost(2.0),
        name="hidden",
    )(info, inner, source, outer, stats, row(first_gain), row(first_shift), conv_weight)

    context = [hidden] + [
        lax.ppermute(hidden, "frame", [(i, i + by) for i in range(frames - by)])
        for by in range(1, taps)
    ]

    pairs = row_count // 2
    pair_shape = shape(pairs, 2 * cols, channels)
    own, stats = pl.pallas_call(
        functools.partial(conv_kernel, rows, taps),
        out_shape=(pair_shape, stats_shape),
        in_specs=[SMEM_SPEC] + [VMEM_SPEC] * (taps + 3),
        out_specs=(VMEM_SPEC, VMEM_SPEC),
        scratch_shapes=[
            pltpu.VMEM((row_count * padded, 3 * taps * channels), BF16),
        ],
        compiler_params=params(),
        cost_estimate=cost(2.5 * taps),
        name="conv",
    )(info, *context, source, row(conv_bias), held)

    blocks = {0: own}
    neighbour = [(i, i ^ 1) for i in range(tiles)]
    if tiles == 16 and video_cols.shape[0] == 2:
        def middle(t):
            return t // 4 in (1, 2)

        stats = merge_round(stats, tiles, rounds[1])
        blocks[2] = exchange(own, tiles, 4)
        blocks[6] = exchange(own, tiles, 12, middle)
        stats = merge_round(stats, tiles, rounds[0])
        own_xy, stats = lax.optimization_barrier((own, stats))
        other = exchange(own_xy, tiles, 1)
        blocks[1] = exchange(own_xy, tiles, 2)
        other, blocks[1] = lax.optimization_barrier((other, blocks[1]))
        inward = exchange(blocks[2], tiles, 12, middle)
        outward = exchange(blocks[6], tiles, 4, middle)
        blocks[4] = jnp.where((tile // 4 == 1) | (tile // 4 == 2), inward, outward)
        blocks[7] = exchange(blocks[6], tiles, 2, middle)
        blocks[5] = exchange(blocks[4], tiles, 2)
        passed, blocks[4] = lax.optimization_barrier((blocks[1], blocks[4]))
        blocks[3] = exchange(passed, tiles, 4)
        groups = [[0, 1, 2, 6], [4, 7, 3, 5]]
    else:
        for masks in rounds:
            stats = merge_round(stats, tiles, masks)
        other = exchange(own, tiles, 1)
        for mask in range(1, tiles // 2):
            blocks[mask] = exchange(own, tiles, 2 * mask)
        groups = [list(range(i, i + 4)) for i in range(0, tiles // 2, 4)]
    gain, shift = row(second_gain), row(second_shift)
    table_shape = shape(SLOTS, channels, dtype=F32)
    queries, constant, means, scales = call(
        functools.partial(query_kernel, rows),
        [other, stats, gain, shift, triple_weight, row(triple_bias)],
        (shape(cells, channels), shape(cells, LANES, dtype=F32), table_shape, table_shape),
        cost_estimate=cost(1.5),
        name="queries",
    )
    level_shape = shape(cells, LANES, dtype=F32)
    total_shape = shape(cells, channels, dtype=F32)
    state, keys = (), []
    for index, masks in enumerate(groups):
        last = index == len(groups) - 1
        outs = (shape(len(masks) * cells, channels),)
        outs += (shape(cells + 16, channels),) if last else (level_shape, level_shape, total_shape)
        normed, *state = call(
            functools.partial(attend_yours_kernel, rows, tuple(masks), index == 0, last),
            [means, scales, shift, queries, constant] + [blocks[m] for m in masks] + list(state),
            outs,
            cost_estimate=cost(0.9 * len(masks)),
            name="attend_yours",
        )
        keys.append(normed)
    (sent,) = state
    received = lax.ppermute(sent, "tile", neighbour)
    sent, own_late, upsample_weight = lax.optimization_barrier((sent, own, upsample_weight))
    mean, level = call(
        functools.partial(attend_mine_kernel, rows, tuple(tuple(masks) for masks in groups)),
        [own_late, means, scales, shift, triple_weight, row(triple_bias)] + keys,
        (total_shape, level_shape),
        cost_estimate=cost(6.0),
        name="attend_mine",
    )
    folded = pl.pallas_call(
        fold_kernel,
        out_shape=shape(2, 2, 2, out_channels, 2 * channels),
        in_specs=[VMEM_SPEC],
        out_specs=VMEM_SPEC,
        compiler_params=params(),
        cost_estimate=cost(0.5),
        name="fold",
    )(jnp.swapaxes(upsample_weight, 2, 3))

    rim_shape = shape(1, cols, channels)
    attended, inner, outer = call(
        functools.partial(finish_kernel, rows),
        [
            mean, level, received, own, triple_weight, row(triple_bias), output_weight,
            row(output_bias),
        ],
        (shape(row_count, cols, channels), rim_shape, rim_shape),
        cost_estimate=cost(1.4),
        name="finish",
    )
    outer = lax.ppermute(outer, "tile", outer_moves)
    inner = exchange(inner, tiles, 1)
    decoded = call(
        functools.partial(upsample_kernel, rows),
        [inner, attended, outer, folded, row(upsample_bias)],
        shape(2 * row_count, 2 * cols, out_channels),
        scratch=[
            pltpu.VMEM((near_rows * padded, 3 * channels), BF16),
            pltpu.VMEM((-(-out_channels // LANES), 2 * row_count, 2 * cols, LANES), F32),
        ],
        cost_estimate=cost(2.3),
        name="upsample",
    )
    return decoded.reshape(2 * row_count, 1, 2 * cols, out_channels)


def solution(mesh):
    sizes = dict(mesh.shape)
    in_specs = (P("tile", "frame", None, None),) + (P(),) * 14
    out_specs = P("tile", "frame", None, None)
    body = functools.partial(shards, sizes["tile"], sizes["frame"])
    return jax.shard_map(body, mesh=mesh, in_specs=in_specs, out_specs=out_specs, check_vma=False)
```

```python
import functools
import math

import jax
import jax.numpy as jnp
from jax import lax
from jax.experimental import pallas as pl
from jax.experimental.pallas import tpu as pltpu
from jax.sharding import PartitionSpec as P

GROUPS = 32
EPSILON = 1e-05
MASKED = -1e30
LOWEST = -5e29
HIGHEST = lax.Precision.HIGHEST
SLOTS = 8
ROWS_OF_TILE = 4
LANES = 128
VMEM_BYTES = 24 * 1024 * 1024
HOLD_VMEM_BYTES = 46 * 1024 * 1024
F32 = jnp.float32
BF16 = jnp.bfloat16

SMEM_SPEC = pl.BlockSpec(memory_space=pltpu.SMEM)
VMEM_SPEC = pl.BlockSpec(memory_space=pltpu.VMEM)
HBM_SPEC = pl.BlockSpec(memory_space=pltpu.HBM)


def cost(microseconds):
    return pl.CostEstimate(
        flops=int(microseconds * 1.1e9), bytes_accessed=0, transcendentals=0
    )


def params():
    return pltpu.CompilerParams(vmem_limit_bytes=VMEM_BYTES)


def member_matrix(channels):
    per_group = channels // GROUPS
    group = lax.broadcasted_iota(jnp.int32, (LANES, channels), 0) * per_group
    channel = lax.broadcasted_iota(jnp.int32, (LANES, channels), 1)
    return jnp.where((channel >= group) & (channel < group + per_group), 1.0, 0.0).astype(F32)


def to_groups(values, member):
    return lax.dot_general(
        values, member, (((1,), (1,)), ((), ())), precision=HIGHEST, preferred_element_type=F32
    )


def to_channels(values, member):
    return jnp.dot(values, member, precision=HIGHEST, preferred_element_type=F32)


class Info:
    def __init__(self, ref, rows):
        self.ref, self.rows = ref, rows
        self.videos = ref.shape[0] - 1 - rows

    def tile(self):
        return self.ref[0]

    def label(self, row):
        inside = (row >= 0) & (row < self.rows)
        return jnp.where(inside, self.ref[1 + jnp.clip(row, 0, self.rows - 1)], -1)

    def width(self, label):
        return jnp.where(label >= 0, self.ref[1 + self.rows + jnp.maximum(label, 0)], 0)

    def window(self, first, count):
        labels = [self.label(first + r) for r in range(count)]
        return labels, [self.width(label) for label in labels]


def pick(table, label, videos):
    chosen = table[0:1]
    for video in range(1, videos):
        chosen = jnp.where(label == video, table[video : video + 1], chosen)
    return chosen


def norm_tables(stats_ref, gain_ref):
    member = member_matrix(gain_ref.shape[1])
    counts = jnp.maximum(stats_ref[0], 1.0)
    scale = lax.rsqrt(stats_ref[2] / counts + EPSILON)
    return to_channels(stats_ref[1], member), to_channels(scale, member) * gain_ref[...]


def write_stats(out_ref, rows, labels, widths, videos, channels):
    member = member_matrix(channels)
    per_group = channels // GROUPS
    cols = rows[0].shape[0]
    slot = lax.broadcasted_iota(jnp.int32, (SLOTS, 1), 0)
    column = lax.broadcasted_iota(jnp.int32, (cols, 1), 0)
    sums = jnp.zeros((SLOTS, channels), F32)
    counts = jnp.zeros((SLOTS, 1), F32)
    for index, row in enumerate(rows):
        sums = jnp.where(slot == index, jnp.sum(row, axis=0, keepdims=True), sums)
        counts = jnp.where(slot == index, (widths[index] * per_group).astype(F32), counts)
    means = to_groups(sums, member) / jnp.maximum(counts, 1.0)
    means_wide = to_channels(means, member)
    squares = jnp.zeros((SLOTS, channels), F32)
    for index, row in enumerate(rows):
        centered = jnp.where(column < widths[index], row - means_wide[index : index + 1], 0.0)
        squares = jnp.where(
            slot == index, jnp.sum(centered * centered, axis=0, keepdims=True), squares
        )
    spreads = to_groups(squares, member)
    out_ref[...] = jnp.zeros(out_ref.shape, F32)
    for video in range(videos):
        total = jnp.zeros((1, LANES), F32)
        count = jnp.zeros((1, LANES), F32)
        for index in range(len(rows)):
            mine = labels[index] == video
            row_count = counts[index : index + 1]
            total = total + jnp.where(mine, means[index : index + 1] * row_count, 0.0)
            count = count + jnp.where(mine, row_count, 0.0)
        mean = total / jnp.maximum(count, 1.0)
        spread = jnp.zeros((1, LANES), F32)
        for index in range(len(rows)):
            off = means[index : index + 1] - mean
            part = spreads[index : index + 1] + counts[index : index + 1] * off * off
            spread = spread + jnp.where(labels[index] == video, part, 0.0)
        out_ref[0, video : video + 1, :] = count
        out_ref[1, video : video + 1, :] = mean
        out_ref[2, video : video + 1, :] = spread


def build_columns(columns_ref, row_refs):
    padded = columns_ref.shape[0] // len(row_refs)
    for index, row in enumerate(row_refs):
        cells = row().astype(F32)
        count, channels = cells.shape
        cells = jnp.concatenate([cells, jnp.zeros((padded - count, channels), F32)], axis=0)
        start = index * padded
        columns_ref[start : start + padded, 0:channels] = pltpu.roll(cells, 1, 0).astype(BF16)
        columns_ref[start : start + padded, channels : 2 * channels] = cells.astype(BF16)
        columns_ref[start : start + padded, 2 * channels : 3 * channels] = pltpu.roll(
            cells, padded - 1, 0
        ).astype(BF16)


def stats_kernel(rows, info_ref, latents_ref, out_ref):
    info = Info(info_ref, rows)
    row_count, cols, channels = latents_ref.shape
    labels, widths = info.window(info.tile() * row_count, row_count)
    column = lax.broadcasted_iota(jnp.int32, (cols, 1), 0)
    cells = [
        jnp.where(column < widths[r], latents_ref[r].astype(F32), 0.0) for r in range(row_count)
    ]
    write_stats(out_ref, cells, labels, widths, info.videos, channels)


def rims(info, inner_ref, outer_ref):
    odd = lax.rem(info.tile(), 2) == 1
    inner, outer = inner_ref[0].astype(F32), outer_ref[0].astype(F32)
    return jnp.where(odd, inner, outer), jnp.where(odd, outer, inner)


def hidden_kernel(
    rows, info_ref, outer_ref, inner_ref, latents_ref, stats_ref, gain_ref, shift_ref, out_ref,
    source_ref,
):
    info = Info(info_ref, rows)
    row_count, cols, _ = latents_ref.shape
    labels, widths = info.window(info.tile() * row_count - 1, row_count + 2)
    means, scales = norm_tables(stats_ref, gain_ref)
    column = lax.broadcasted_iota(jnp.int32, (cols, 1), 0)
    above, below = rims(info, inner_ref, outer_ref)
    sources = [above] + [latents_ref[r].astype(F32) for r in range(row_count)] + [below]
    for r, source in enumerate(sources):
        mean = pick(means, labels[r], info.videos)
        scale = pick(scales, labels[r], info.videos)
        normed = (source - mean) * scale + shift_ref[...]
        active = normed / (1.0 + jnp.exp(-normed))
        active = jnp.where(column < widths[r], active, 0.0)
        rest = jnp.zeros((out_ref.shape[1] - cols, active.shape[1]), F32)
        out_ref[r] = jnp.concatenate([active, rest], axis=0).astype(BF16)
    source_ref[...] = latents_ref[...]


def hold_kernel(taps, weight_ref, held_ref, sems):
    channels = weight_ref.shape[-1]
    copies = [
        pltpu.make_async_copy(
            weight_ref.at[2 - depth // 3, depth % 3, side],
            held_ref.at[pl.ds(depth * channels, channels), pl.ds(side * channels, channels)],
            sems.at[side, depth],
        )
        for side in range(3)
        for depth in range(3 * taps)
    ]
    for copy in copies:
        copy.start()
    for copy in copies:
        copy.wait()


def conv_kernel(rows, taps, info_ref, *rest):
    hidden_refs, rest = rest[:taps], rest[taps:]
    latents_ref, bias_ref, held_ref, own_ref, stats_ref, inputs_ref = rest
    row_count, cols, channels = latents_ref.shape
    info = Info(info_ref, rows)
    padded = hidden_refs[0].shape[1]
    labels, widths = info.window(info.tile() * row_count - 1, row_count + 2)
    for back, hidden_ref in enumerate(hidden_refs):
        for tap in range(3):
            lanes = slice((3 * back + tap) * channels, (3 * back + tap + 1) * channels)
            for r in range(row_count):
                block = hidden_ref[r + tap]
                if tap != 1:
                    same = labels[r + tap] == labels[r + 1]
                    block = jnp.where(same, block, jnp.zeros_like(block))
                inputs_ref[r * padded : (r + 1) * padded, lanes] = block
    product = jnp.dot(inputs_ref[...], held_ref[...], preferred_element_type=F32)
    column = lax.broadcasted_iota(jnp.int32, (cols, 1), 0)
    cells = []
    for r in range(row_count):
        lines = slice(r * padded, (r + 1) * padded)
        branch = pltpu.roll(product[lines, 0:channels], 1, 0)
        branch = branch + product[lines, channels : 2 * channels]
        branch = branch + pltpu.roll(product[lines, 2 * channels :], padded - 1, 0)
        value = latents_ref[r].astype(F32) + branch[:cols] + bias_ref[...]
        value = jnp.where(column < widths[r + 1], value, 0.0).astype(BF16)
        cells.append(value.astype(F32))
    for pair in range(row_count // 2):
        own_ref[pair] = jnp.concatenate(cells[2 * pair : 2 * pair + 2], axis=0).astype(BF16)
    write_stats(stats_ref, cells, labels[1:-1], widths[1:-1], info.videos, channels)


def split_rows(pairs_ref):
    cols = pairs_ref.shape[1] // 2
    cells = []
    for pair in range(pairs_ref.shape[0]):
        both = pairs_ref[pair].astype(F32)
        cells += [both[:cols], both[cols:]]
    return cells


def turned_queries(info, tile, pairs_ref, means, scales, shift_ref, weight_ref, bias_ref):
    pairs, double, channels = pairs_ref.shape
    cols = double // 2
    column = lax.broadcasted_iota(jnp.int32, (cols, 1), 0)
    labels, widths = info.window(tile * 2 * pairs, 2 * pairs)
    cells = []
    for r, values in enumerate(split_rows(pairs_ref)):
        mean = pick(means, labels[r], info.videos)
        scale = pick(scales, labels[r], info.videos)
        normed = (values - mean) * scale + shift_ref[...]
        cells.append(jnp.where(column < widths[r], normed, 0.0))
    cells = jnp.concatenate(cells, axis=0).astype(BF16)
    queries = (
        jnp.dot(cells, weight_ref[:, 0:channels], preferred_element_type=F32)
        + bias_ref[:, 0:channels]
    ).astype(BF16)
    factor = channels ** (-0.5) * math.log2(math.e)
    turned = lax.dot_general(
        queries, weight_ref[:, channels : 2 * channels], (((1,), (1,)), ((), ())),
        preferred_element_type=F32,
    )
    constant = jnp.sum(
        queries.astype(F32) * bias_ref[:, channels : 2 * channels], axis=1, keepdims=True
    )
    return (turned * factor).astype(BF16), constant * factor


def query_kernel(
    rows, info_ref, other_ref, stats_ref, gain_ref, shift_ref, weight_ref, bias_ref, queries_ref,
    constant_ref, means_ref, scales_ref,
):
    info = Info(info_ref, rows)
    means, scales = norm_tables(stats_ref, gain_ref)
    means_ref[...] = means
    scales_ref[...] = scales
    queries, constant = turned_queries(
        info, info.tile() ^ 1, other_ref, means, scales, shift_ref, weight_ref, bias_ref
    )
    queries_ref[...] = queries
    constant_ref[...] = jnp.broadcast_to(constant, constant_ref.shape)


def key_codes(info, masks, span, cols):
    row_count = span // cols
    position = lax.broadcasted_iota(jnp.int32, (1, len(masks) * span), 1)
    codes = jnp.full((1, len(masks) * span), -2.0, F32)
    for index, mask in enumerate(masks):
        near, widths = info.window((info.tile() ^ (2 * mask)) * row_count, row_count)
        for r in range(row_count):
            start = index * span + r * cols
            inside = (position >= start) & (position < start + widths[r])
            codes = jnp.where(inside, near[r].astype(F32), codes)
    return codes


def query_codes(info, tile, span, cols):
    row_count = span // cols
    labels, _ = info.window(tile * row_count, row_count)
    return jnp.concatenate(
        [jnp.zeros((cols, 1), F32) + label.astype(F32) for label in labels], axis=0
    )


def scores_of(queries, keys, codes, query_code):
    scores = lax.dot_general(
        queries, keys, (((1,), (1,)), ((), ())), preferred_element_type=F32
    )
    return jnp.where(codes == query_code, scores, MASKED)


def mean_and_level(peak, denominator, total):
    some = denominator > 0.0
    safe = jnp.where(some, denominator, 1.0)
    return total / safe, jnp.where(some, peak + jnp.log2(safe), LOWEST)


def attend_yours_kernel(rows, masks, first, last, info_ref, *rest):
    means_ref, scales_ref, shift_ref, queries_ref, constant_ref, *rest = rest
    block_refs, rest = rest[: len(masks)], rest[len(masks) :]
    if not first:
        old_peak_ref, old_sum_ref, old_total_ref, *rest = rest
    keys_ref, *out_refs = rest
    info = Info(info_ref, rows)
    span, channels = queries_ref.shape
    pairs, double, _ = block_refs[0].shape
    cols = double // 2
    row_count = 2 * pairs
    tile = info.tile()
    means, scales = means_ref[...], scales_ref[...]
    for index, (mask, block_ref) in enumerate(zip(masks, block_refs)):
        near, _ = info.window((tile ^ (2 * mask)) * row_count, row_count)
        for pair in range(pairs):
            both = block_ref[pair].astype(F32)
            halves = []
            for half in range(2):
                label = near[2 * pair + half]
                mean = pick(means, label, info.videos)
                scale = pick(scales, label, info.videos)
                values = both[half * cols : (half + 1) * cols]
                halves.append((values - mean) * scale + shift_ref[...])
            start = index * span + pair * double
            keys_ref[start : start + double, :] = jnp.concatenate(halves, axis=0).astype(BF16)
    constant = constant_ref[:, 0:1]
    scores = scores_of(
        queries_ref[...], keys_ref[...], key_codes(info, masks, span, cols),
        query_codes(info, tile ^ 1, span, cols),
    )
    peak = jnp.maximum(LOWEST, jnp.max(scores, axis=1, keepdims=True) + constant)
    if not first:
        largest = old_peak_ref[:, 0:1]
        peak = jnp.maximum(largest, peak)
    weights = jnp.exp2(scores - (peak - constant))
    denominator = jnp.sum(weights, axis=1, keepdims=True)
    total = jnp.dot(weights.astype(BF16), keys_ref[...], preferred_element_type=F32)
    if not first:
        factor = jnp.exp2(largest - peak)
        denominator = old_sum_ref[:, 0:1] * factor + denominator
        total = old_total_ref[...] * factor + total
    if not last:
        peak_ref, sum_ref, total_ref = out_refs
        peak_ref[...] = jnp.broadcast_to(peak, peak_ref.shape)
        sum_ref[...] = jnp.broadcast_to(denominator, sum_ref.shape)
        total_ref[...] = total
        return
    (sent_ref,) = out_refs
    mean, level = mean_and_level(peak, denominator, total)
    sent_ref[0:span, :] = mean.astype(BF16)
    slots = sent_ref.shape[0] - span
    slot = lax.broadcasted_iota(jnp.int32, (slots, 1), 0)
    packed = jnp.zeros((slots, LANES), F32)
    for r in range(row_count):
        left = level[r * cols : (r + 1) * cols]
        left = jnp.sum(jnp.where(diagonal(cols), left, 0.0), axis=0, keepdims=True)
        for part in range(3):
            rounded = left.astype(BF16).astype(F32)
            packed = jnp.where(slot == 3 * r + part, rounded, packed)
            left = left - rounded
    sent_ref[span:, 0:LANES] = packed.astype(BF16)
    sent_ref[span:, LANES:] = jnp.zeros((slots, channels - LANES), BF16)


def attend_mine_kernel(
    rows, groups, info_ref, own_ref, means_ref, scales_ref, shift_ref, weight_ref, bias_ref, *rest
):
    key_refs, (mean_ref, level_ref) = rest[: len(groups)], rest[len(groups) :]
    info = Info(info_ref, rows)
    span = mean_ref.shape[0]
    queries, constant = turned_queries(
        info, info.tile(), own_ref, means_ref[...], scales_ref[...], shift_ref, weight_ref,
        bias_ref,
    )
    cols = span // ROWS_OF_TILE
    query_code = query_codes(info, info.tile(), span, cols)
    peak = jnp.full((span, 1), LOWEST, F32)
    scores = []
    for masks, key_ref in zip(groups, key_refs):
        codes = key_codes(info, masks, span, cols)
        scores.append(scores_of(queries, key_ref[...], codes, query_code))
        peak = jnp.maximum(peak, jnp.max(scores[-1], axis=1, keepdims=True) + constant)
    denominator, total = 0.0, 0.0
    for part, key_ref in zip(scores, key_refs):
        weights = jnp.exp2(part - (peak - constant))
        denominator = denominator + jnp.sum(weights, axis=1, keepdims=True)
        total = total + jnp.dot(
            weights.astype(BF16), key_ref[...], preferred_element_type=F32
        )
    mean, level = mean_and_level(peak, denominator, total)
    mean_ref[...] = mean
    level_ref[...] = jnp.broadcast_to(level, level_ref.shape)


def diagonal(cols):
    return lax.broadcasted_iota(jnp.int32, (cols, LANES), 0) == lax.broadcasted_iota(
        jnp.int32, (cols, LANES), 1
    )


def finish_kernel(
    rows, info_ref, mean_ref, level_ref, received_ref, own_ref, triple_ref, triple_bias_ref,
    output_ref, output_bias_ref, out_ref, inner_ref, outer_ref,
):
    info = Info(info_ref, rows)
    row_count, cols, channels = out_ref.shape
    span = row_count * cols
    _, widths = info.window(info.tile() * row_count, row_count)
    received = received_ref[0:span, :].astype(F32)
    levels = received_ref[span:, 0:LANES].astype(F32)
    yours = []
    for r in range(row_count):
        level = levels[3 * r : 3 * r + 1] + levels[3 * r + 1 : 3 * r + 2]
        level = level + levels[3 * r + 2 : 3 * r + 3]
        yours.append(jnp.sum(jnp.where(diagonal(cols), level, 0.0), axis=1, keepdims=True))
    yours = jnp.concatenate(yours, axis=0)
    mine = level_ref[:, 0:1]
    peak = jnp.maximum(mine, yours)
    weight, other_weight = jnp.exp2(mine - peak), jnp.exp2(yours - peak)
    share = weight / (weight + other_weight)
    mean_cell = (mean_ref[...] * share + received * (1.0 - share)).astype(BF16)
    mixed = (
        jnp.dot(mean_cell, triple_ref[:, 2 * channels :], preferred_element_type=F32)
        + triple_bias_ref[:, 2 * channels :]
    ).astype(BF16)
    attended = jnp.dot(mixed, output_ref[...], preferred_element_type=F32) + output_bias_ref[...]
    column = lax.broadcasted_iota(jnp.int32, (cols, 1), 0)
    for r, before in enumerate(split_rows(own_ref)):
        value = before + attended[r * cols : (r + 1) * cols]
        value = jnp.where(column < widths[r], value, 0.0)
        out_ref[r] = value.astype(BF16)
        if r == 0:
            top = value
    odd = lax.rem(info.tile(), 2) == 1
    inner_ref[0] = jnp.where(odd, top, value).astype(BF16)
    outer_ref[0] = jnp.where(odd, value, top).astype(BF16)


def fold_kernel(weight_ref, out_ref):
    channels = weight_ref.shape[-1]
    wide = [[weight_ref[a, b].astype(F32) for b in range(3)] for a in range(3)]

    def both(upper, lower):
        return [x + y for x, y in zip(upper, lower)]

    phases = [[wide[0], both(wide[1], wide[2])], [both(wide[0], wide[1]), wide[2]]]
    for down in range(2):
        for tap in range(2):
            left, middle, right = phases[down][tap]
            out_ref[down, tap, 0, :, 0:channels] = left.astype(BF16)
            out_ref[down, tap, 0, :, channels:] = (middle + right).astype(BF16)
            out_ref[down, tap, 1, :, 0:channels] = (left + middle).astype(BF16)
            out_ref[down, tap, 1, :, channels:] = right.astype(BF16)


def upsample_kernel(
    rows, info_ref, outer_ref, inner_ref, own_ref, weight_ref, bias_ref, out_ref, columns_ref,
    wide_ref,
):
    info = Info(info_ref, rows)
    row_count, cols, channels = own_ref.shape
    near_rows = row_count + 2
    padded = columns_ref.shape[0] // near_rows
    parts_out = wide_ref.shape[0]
    out_channels = out_ref.shape[-1]
    labels, widths = info.window(info.tile() * row_count - 1, near_rows)
    above, below = rims(info, inner_ref, outer_ref)
    sources = [lambda: above]
    sources += [functools.partial(own_ref.__getitem__, r) for r in range(row_count)]
    sources += [lambda: below]
    build_columns(columns_ref, sources)
    span = row_count * padded
    wide_column = lax.broadcasted_iota(jnp.int32, (2 * cols, 1), 0)
    for down in range(2):
        for right in range(2):
            lanes = slice(right * channels, (right + 2) * channels)
            products = [
                lax.dot_general(
                    columns_ref[(down + tap) * padded : (down + tap) * padded + span, lanes],
                    weight_ref[down, tap, right],
                    (((1,), (1,)), ((), ())),
                    preferred_element_type=F32,
                )
                for tap in range(2)
            ]
            rim, same = products[down], products[1 - down]
            for r in range(row_count):
                lo, hi = r * padded, r * padded + cols
                near = labels[r + 2 * down]
                value = same[lo:hi] + jnp.where(near == labels[r + 1], rim[lo:hi], 0.0)
                for part in range(parts_out):
                    part_lo, part_hi = part * LANES, min((part + 1) * LANES, out_channels)
                    piece = value[:, part_lo:part_hi]
                    if part_hi - part_lo < LANES:
                        missing = LANES - (part_hi - part_lo)
                        piece = jnp.concatenate([piece, jnp.zeros((cols, missing), F32)], axis=1)
                    wide_ref[part, 2 * r + down, pl.ds(right, cols, 2), :] = piece
    for r in range(2 * row_count):
        valid = wide_column < 2 * widths[r // 2 + 1]
        for part in range(parts_out):
            lo, hi = part * LANES, min((part + 1) * LANES, out_channels)
            value = wide_ref[part, r, :, 0 : hi - lo] + bias_ref[:, lo:hi]
            out_ref[r, :, lo:hi] = jnp.where(valid, value, 0.0).astype(BF16)


def merge_stats(mine, other):
    count = mine[0] + other[0]
    safe = jnp.maximum(count, 1.0)
    off = other[1] - mine[1]
    mean = mine[1] + off * (other[0] / safe)
    spread = mine[2] + other[2] + off * off * (mine[0] * other[0] / safe)
    return jnp.stack([count, mean, spread])


def exchange(array, tiles, mask, among=None):
    moves = [(i, i ^ mask) for i in range(tiles) if among is None or among(i)]
    return lax.ppermute(array, "tile", moves)


def merge_round(stats, tiles, masks):
    parts = [stats] + [exchange(stats, tiles, mask) for mask in masks]
    while len(parts) > 1:
        parts = [merge_stats(*parts[i : i + 2]) for i in range(0, len(parts), 2)]
    return parts[0]


def merge_masks(tiles):
    bits = [1 << i for i in range(tiles.bit_length() - 1)]
    pairs = [bits[i : i + 2] for i in range(0, len(bits), 2)]
    return [[p[0], p[1], p[0] ^ p[1]] if len(p) == 2 else p for p in pairs]


def shards(
    tiles,
    frames,
    latents,
    row_video,
    video_cols,
    first_gain,
    first_shift,
    conv_weight,
    conv_bias,
    second_gain,
    second_shift,
    triple_weight,
    triple_bias,
    output_weight,
    output_bias,
    upsample_weight,
    upsample_bias,
):
    row_count, frame_count, cols, channels = latents.shape
    assert frame_count == 1 and row_count == ROWS_OF_TILE and tiles % 4 == 0
    out_channels = upsample_weight.shape[-1]
    rows = row_count * tiles
    cells = row_count * cols
    padded = -(-(cols + 1) // 16) * 16
    near_rows = row_count + 2
    source = latents.reshape(row_count, cols, channels)
    tile = lax.axis_index("tile").astype(jnp.int32)
    info = jnp.concatenate([jnp.reshape(tile, (1,)), row_video, video_cols])

    def row(vector):
        return vector.reshape(1, -1)

    def shape(*dims, dtype=BF16):
        return jax.ShapeDtypeStruct(dims, dtype)

    def call(kernel, operands, out_shape, scratch=(), **kwargs):
        many = isinstance(out_shape, tuple)
        return pl.pallas_call(
            kernel,
            out_shape=out_shape,
            in_specs=[SMEM_SPEC] + [VMEM_SPEC] * len(operands),
            out_specs=(VMEM_SPEC,) * len(out_shape) if many else VMEM_SPEC,
            scratch_shapes=list(scratch),
            compiler_params=params(),
            **kwargs,
        )(info, *operands)

    outer_moves = [(i, i - 1 if i % 2 == 0 else i + 1) for i in range(tiles)]
    outer_moves = [(i, j) for i, j in outer_moves if 0 <= j < tiles]
    odd = tile % 2 == 1
    stats_shape = shape(3, SLOTS, LANES, dtype=F32)
    stats = call(
        functools.partial(stats_kernel, rows), [source], stats_shape,
        cost_estimate=cost(1.5), name="first_stats",
    )
    outer = lax.ppermute(
        jnp.where(odd, source[row_count - 1 :], source[:1]), "tile", outer_moves
    )
    inner = exchange(jnp.where(odd, source[:1], source[row_count - 1 :]), tiles, 1)
    stats, outer, inner = lax.optimization_barrier((stats, outer, inner))
    taps = min(3, frames)
    held = pl.pallas_call(
        functools.partial(hold_kernel, taps),
        out_shape=shape(3 * taps * channels, 3 * channels),
        in_specs=[HBM_SPEC],
        out_specs=VMEM_SPEC,
        scratch_shapes=[pltpu.SemaphoreType.DMA((3, 3 * taps))],
        compiler_params=pltpu.CompilerParams(vmem_limit_bytes=HOLD_VMEM_BYTES),
        cost_estimate=cost(1.5 * taps),
        name="hold",
    )(conv_weight)
    rounds = merge_masks(tiles)
    for index, masks in enumerate(reversed(rounds)):
        stats = merge_round(stats, tiles, masks)
        if index == len(rounds) - 2:
            stats, held = lax.optimization_barrier((stats, held))
    hidden, source = call(
        functools.partial(hidden_kernel, rows),
        [outer, inner, source, stats, row(first_gain), row(first_shift)],
        (shape(near_rows, padded, channels), shape(row_count, cols, channels)),
        cost_estimate=cost(1.3),
        name="hidden",
    )

    context = [hidden] + [
        lax.ppermute(hidden, "frame", [(i, i + by) for i in range(frames - by)])
        for by in range(1, taps)
    ]

    pairs = row_count // 2
    pair_shape = shape(pairs, 2 * cols, channels)
    own, stats = pl.pallas_call(
        functools.partial(conv_kernel, rows, taps),
        out_shape=(pair_shape, stats_shape),
        in_specs=[SMEM_SPEC] + [VMEM_SPEC] * (taps + 3),
        out_specs=(VMEM_SPEC, VMEM_SPEC),
        scratch_shapes=[
            pltpu.VMEM((row_count * padded, 3 * taps * channels), BF16),
        ],
        compiler_params=params(),
        cost_estimate=cost(2.5 * taps),
        name="conv",
    )(info, *context, source, row(conv_bias), held)

    blocks = {0: own}
    neighbour = [(i, i ^ 1) for i in range(tiles)]
    if tiles == 16 and video_cols.shape[0] == 2:
        def middle(t):
            return t // 4 in (1, 2)

        stats = merge_round(stats, tiles, rounds[1])
        blocks[2] = exchange(own, tiles, 4)
        blocks[6] = exchange(own, tiles, 12, middle)
        stats = merge_round(stats, tiles, rounds[0])
        stats, own_xy = lax.optimization_barrier((stats, own))
        inward = exchange(blocks[2], tiles, 12, middle)
        outward = exchange(blocks[6], tiles, 4, middle)
        other = exchange(own_xy, tiles, 1)
        blocks[1] = exchange(own_xy, tiles, 2)
        other, blocks[1] = lax.optimization_barrier((other, blocks[1]))
        blocks[4] = jnp.where((tile // 4 == 1) | (tile // 4 == 2), inward, outward)
        passed, blocks[4] = lax.optimization_barrier((blocks[1], blocks[4]))
        blocks[5] = exchange(blocks[4], tiles, 2)
        blocks[3] = exchange(passed, tiles, 4)
        blocks[7] = exchange(passed, tiles, 12, middle)
        groups = [[0, 1, 2, 6], [4, 7, 3, 5]]
    else:
        for masks in rounds:
            stats = merge_round(stats, tiles, masks)
        other = exchange(own, tiles, 1)
        for mask in range(1, tiles // 2):
            blocks[mask] = exchange(own, tiles, 2 * mask)
        groups = [list(range(i, i + 4)) for i in range(0, tiles // 2, 4)]
    gain, shift = row(second_gain), row(second_shift)
    table_shape = shape(SLOTS, channels, dtype=F32)
    queries, constant, means, scales = call(
        functools.partial(query_kernel, rows),
        [other, stats, gain, shift, triple_weight, row(triple_bias)],
        (shape(cells, channels), shape(cells, LANES, dtype=F32), table_shape, table_shape),
        cost_estimate=cost(1.5),
        name="queries",
    )
    level_shape = shape(cells, LANES, dtype=F32)
    total_shape = shape(cells, channels, dtype=F32)
    state, keys = (), []
    for index, masks in enumerate(groups):
        last = index == len(groups) - 1
        outs = (shape(len(masks) * cells, channels),)
        outs += (shape(cells + 16, channels),) if last else (level_shape, level_shape, total_shape)
        normed, *state = call(
            functools.partial(attend_yours_kernel, rows, tuple(masks), index == 0, last),
            [means, scales, shift, queries, constant] + [blocks[m] for m in masks] + list(state),
            outs,
            cost_estimate=cost(0.9 * len(masks)),
            name="attend_yours",
        )
        keys.append(normed)
    (sent,) = state
    received = lax.ppermute(sent, "tile", neighbour)
    sent, own_late, upsample_weight = lax.optimization_barrier((sent, own, upsample_weight))
    mean, level = call(
        functools.partial(attend_mine_kernel, rows, tuple(tuple(masks) for masks in groups)),
        [own_late, means, scales, shift, triple_weight, row(triple_bias)] + keys,
        (total_shape, level_shape),
        cost_estimate=cost(6.0),
        name="attend_mine",
    )
    folded = pl.pallas_call(
        fold_kernel,
        out_shape=shape(2, 2, 2, out_channels, 2 * channels),
        in_specs=[VMEM_SPEC],
        out_specs=VMEM_SPEC,
        compiler_params=params(),
        cost_estimate=cost(0.5),
        name="fold",
    )(jnp.swapaxes(upsample_weight, 2, 3))

    rim_shape = shape(1, cols, channels)
    attended, inner, outer = call(
        functools.partial(finish_kernel, rows),
        [
            mean, level, received, own, triple_weight, row(triple_bias), output_weight,
            row(output_bias),
        ],
        (shape(row_count, cols, channels), rim_shape, rim_shape),
        cost_estimate=cost(1.4),
        name="finish",
    )
    outer = lax.ppermute(outer, "tile", outer_moves)
    inner = exchange(inner, tiles, 1)
    decoded = call(
        functools.partial(upsample_kernel, rows),
        [outer, inner, attended, folded, row(upsample_bias)],
        shape(2 * row_count, 2 * cols, out_channels),
        scratch=[
            pltpu.VMEM((near_rows * padded, 3 * channels), BF16),
            pltpu.VMEM((-(-out_channels // LANES), 2 * row_count, 2 * cols, LANES), F32),
        ],
        cost_estimate=cost(2.3),
        name="upsample",
    )
    return decoded.reshape(2 * row_count, 1, 2 * cols, out_channels)


def solution(mesh):
    sizes = dict(mesh.shape)
    in_specs = (P("tile", "frame", None, None),) + (P(),) * 14
    out_specs = P("tile", "frame", None, None)
    body = functools.partial(shards, sizes["tile"], sizes["frame"])
    return jax.shard_map(body, mesh=mesh, in_specs=in_specs, out_specs=out_specs, check_vma=False)
```

```python
import functools
import math

import jax
import jax.numpy as jnp
from jax import lax
from jax.experimental import pallas as pl
from jax.experimental.pallas import tpu as pltpu
from jax.sharding import PartitionSpec as P

GROUPS = 32
EPSILON = 1e-05
MASKED = -1e30
LOWEST = -5e29
HIGHEST = lax.Precision.HIGHEST
SLOTS = 8
ROWS_OF_TILE = 4
LANES = 128
VMEM_BYTES = 24 * 1024 * 1024
HOLD_VMEM_BYTES = 46 * 1024 * 1024
F32 = jnp.float32
BF16 = jnp.bfloat16

SMEM_SPEC = pl.BlockSpec(memory_space=pltpu.SMEM)
VMEM_SPEC = pl.BlockSpec(memory_space=pltpu.VMEM)
HBM_SPEC = pl.BlockSpec(memory_space=pltpu.HBM)


def cost(microseconds):
    return pl.CostEstimate(
        flops=int(microseconds * 1.1e9), bytes_accessed=0, transcendentals=0
    )


def params():
    return pltpu.CompilerParams(vmem_limit_bytes=VMEM_BYTES)


def member_matrix(channels):
    per_group = channels // GROUPS
    group = lax.broadcasted_iota(jnp.int32, (LANES, channels), 0) * per_group
    channel = lax.broadcasted_iota(jnp.int32, (LANES, channels), 1)
    return jnp.where((channel >= group) & (channel < group + per_group), 1.0, 0.0).astype(F32)


def to_groups(values, member):
    return lax.dot_general(
        values, member, (((1,), (1,)), ((), ())), precision=HIGHEST, preferred_element_type=F32
    )


def to_channels(values, member):
    return jnp.dot(values, member, precision=HIGHEST, preferred_element_type=F32)


class Info:
    def __init__(self, ref, rows):
        self.ref, self.rows = ref, rows
        self.videos = ref.shape[0] - 1 - rows

    def tile(self):
        return self.ref[0]

    def label(self, row):
        inside = (row >= 0) & (row < self.rows)
        return jnp.where(inside, self.ref[1 + jnp.clip(row, 0, self.rows - 1)], -1)

    def width(self, label):
        return jnp.where(label >= 0, self.ref[1 + self.rows + jnp.maximum(label, 0)], 0)

    def window(self, first, count):
        labels = [self.label(first + r) for r in range(count)]
        return labels, [self.width(label) for label in labels]


def pick(table, label, videos):
    chosen = table[0:1]
    for video in range(1, videos):
        chosen = jnp.where(label == video, table[video : video + 1], chosen)
    return chosen


def norm_tables(stats_ref, gain_ref):
    member = member_matrix(gain_ref.shape[1])
    counts = jnp.maximum(stats_ref[0], 1.0)
    scale = lax.rsqrt(stats_ref[2] / counts + EPSILON)
    return to_channels(stats_ref[1], member), to_channels(scale, member) * gain_ref[...]


def write_stats(out_ref, rows, labels, widths, videos, channels):
    member = member_matrix(channels)
    per_group = channels // GROUPS
    cols = rows[0].shape[0]
    slot = lax.broadcasted_iota(jnp.int32, (SLOTS, 1), 0)
    column = lax.broadcasted_iota(jnp.int32, (cols, 1), 0)
    sums = jnp.zeros((SLOTS, channels), F32)
    counts = jnp.zeros((SLOTS, 1), F32)
    for index, row in enumerate(rows):
        sums = jnp.where(slot == index, jnp.sum(row, axis=0, keepdims=True), sums)
        counts = jnp.where(slot == index, (widths[index] * per_group).astype(F32), counts)
    means = to_groups(sums, member) / jnp.maximum(counts, 1.0)
    means_wide = to_channels(means, member)
    squares = jnp.zeros((SLOTS, channels), F32)
    for index, row in enumerate(rows):
        centered = jnp.where(column < widths[index], row - means_wide[index : index + 1], 0.0)
        squares = jnp.where(
            slot == index, jnp.sum(centered * centered, axis=0, keepdims=True), squares
        )
    spreads = to_groups(squares, member)
    out_ref[...] = jnp.zeros(out_ref.shape, F32)
    for video in range(videos):
        total = jnp.zeros((1, LANES), F32)
        count = jnp.zeros((1, LANES), F32)
        for index in range(len(rows)):
            mine = labels[index] == video
            row_count = counts[index : index + 1]
            total = total + jnp.where(mine, means[index : index + 1] * row_count, 0.0)
            count = count + jnp.where(mine, row_count, 0.0)
        mean = total / jnp.maximum(count, 1.0)
        spread = jnp.zeros((1, LANES), F32)
        for index in range(len(rows)):
            off = means[index : index + 1] - mean
            part = spreads[index : index + 1] + counts[index : index + 1] * off * off
            spread = spread + jnp.where(labels[index] == video, part, 0.0)
        out_ref[0, video : video + 1, :] = count
        out_ref[1, video : video + 1, :] = mean
        out_ref[2, video : video + 1, :] = spread


def build_columns(columns_ref, row_refs):
    padded = columns_ref.shape[0] // len(row_refs)
    for index, row in enumerate(row_refs):
        cells = row().astype(F32)
        count, channels = cells.shape
        cells = jnp.concatenate([cells, jnp.zeros((padded - count, channels), F32)], axis=0)
        start = index * padded
        columns_ref[start : start + padded, 0:channels] = pltpu.roll(cells, 1, 0).astype(BF16)
        columns_ref[start : start + padded, channels : 2 * channels] = cells.astype(BF16)
        columns_ref[start : start + padded, 2 * channels : 3 * channels] = pltpu.roll(
            cells, padded - 1, 0
        ).astype(BF16)


def stats_kernel(rows, info_ref, latents_ref, out_ref):
    info = Info(info_ref, rows)
    row_count, cols, channels = latents_ref.shape
    labels, widths = info.window(info.tile() * row_count, row_count)
    column = lax.broadcasted_iota(jnp.int32, (cols, 1), 0)
    cells = [
        jnp.where(column < widths[r], latents_ref[r].astype(F32), 0.0) for r in range(row_count)
    ]
    write_stats(out_ref, cells, labels, widths, info.videos, channels)


def rims(info, outer_ref, inner_ref):
    odd = lax.rem(info.tile(), 2) == 1
    inner, outer = inner_ref[0].astype(F32), outer_ref[0].astype(F32)
    return jnp.where(odd, inner, outer), jnp.where(odd, outer, inner)


def hidden_kernel(
    rows, info_ref, outer_ref, inner_ref, latents_ref, stats_ref, gain_ref, shift_ref, out_ref,
    source_ref,
):
    info = Info(info_ref, rows)
    row_count, cols, _ = latents_ref.shape
    labels, widths = info.window(info.tile() * row_count - 1, row_count + 2)
    means, scales = norm_tables(stats_ref, gain_ref)
    column = lax.broadcasted_iota(jnp.int32, (cols, 1), 0)
    above, below = rims(info, outer_ref, inner_ref)
    sources = [above] + [latents_ref[r].astype(F32) for r in range(row_count)] + [below]
    for r, source in enumerate(sources):
        mean = pick(means, labels[r], info.videos)
        scale = pick(scales, labels[r], info.videos)
        normed = (source - mean) * scale + shift_ref[...]
        active = normed / (1.0 + jnp.exp(-normed))
        active = jnp.where(column < widths[r], active, 0.0)
        rest = jnp.zeros((out_ref.shape[1] - cols, active.shape[1]), F32)
        out_ref[r] = jnp.concatenate([active, rest], axis=0).astype(BF16)
    source_ref[...] = latents_ref[...]


def hold_kernel(taps, weight_ref, held_ref, sems):
    channels = weight_ref.shape[-1]
    copies = [
        pltpu.make_async_copy(
            weight_ref.at[2 - depth // 3, depth % 3, side],
            held_ref.at[pl.ds(depth * channels, channels), pl.ds(side * channels, channels)],
            sems.at[side, depth],
        )
        for side in range(3)
        for depth in range(3 * taps)
    ]
    for copy in copies:
        copy.start()
    for copy in copies:
        copy.wait()


def conv_kernel(rows, taps, info_ref, *rest):
    hidden_refs, rest = rest[:taps], rest[taps:]
    latents_ref, bias_ref, held_ref, own_ref, stats_ref, inputs_ref = rest
    row_count, cols, channels = latents_ref.shape
    info = Info(info_ref, rows)
    padded = hidden_refs[0].shape[1]
    labels, widths = info.window(info.tile() * row_count - 1, row_count + 2)
    for back, hidden_ref in enumerate(hidden_refs):
        for tap in range(3):
            lanes = slice((3 * back + tap) * channels, (3 * back + tap + 1) * channels)
            for r in range(row_count):
                block = hidden_ref[r + tap]
                if tap != 1:
                    same = labels[r + tap] == labels[r + 1]
                    block = jnp.where(same, block, jnp.zeros_like(block))
                inputs_ref[r * padded : (r + 1) * padded, lanes] = block
    product = jnp.dot(inputs_ref[...], held_ref[...], preferred_element_type=F32)
    column = lax.broadcasted_iota(jnp.int32, (cols, 1), 0)
    cells = []
    for r in range(row_count):
        lines = slice(r * padded, (r + 1) * padded)
        branch = pltpu.roll(product[lines, 0:channels], 1, 0)
        branch = branch + product[lines, channels : 2 * channels]
        branch = branch + pltpu.roll(product[lines, 2 * channels :], padded - 1, 0)
        value = latents_ref[r].astype(F32) + branch[:cols] + bias_ref[...]
        value = jnp.where(column < widths[r + 1], value, 0.0).astype(BF16)
        cells.append(value.astype(F32))
    for pair in range(row_count // 2):
        own_ref[pair] = jnp.concatenate(cells[2 * pair : 2 * pair + 2], axis=0).astype(BF16)
    write_stats(stats_ref, cells, labels[1:-1], widths[1:-1], info.videos, channels)


def split_rows(pairs_ref):
    cols = pairs_ref.shape[1] // 2
    cells = []
    for pair in range(pairs_ref.shape[0]):
        both = pairs_ref[pair].astype(F32)
        cells += [both[:cols], both[cols:]]
    return cells


def turned_queries(info, tile, pairs_ref, means, scales, shift_ref, weight_ref, bias_ref):
    pairs, double, channels = pairs_ref.shape
    cols = double // 2
    column = lax.broadcasted_iota(jnp.int32, (cols, 1), 0)
    labels, widths = info.window(tile * 2 * pairs, 2 * pairs)
    cells = []
    for r, values in enumerate(split_rows(pairs_ref)):
        mean = pick(means, labels[r], info.videos)
        scale = pick(scales, labels[r], info.videos)
        normed = (values - mean) * scale + shift_ref[...]
        cells.append(jnp.where(column < widths[r], normed, 0.0))
    cells = jnp.concatenate(cells, axis=0).astype(BF16)
    queries = (
        jnp.dot(cells, weight_ref[:, 0:channels], preferred_element_type=F32)
        + bias_ref[:, 0:channels]
    ).astype(BF16)
    factor = channels ** (-0.5) * math.log2(math.e)
    turned = lax.dot_general(
        queries, weight_ref[:, channels : 2 * channels], (((1,), (1,)), ((), ())),
        preferred_element_type=F32,
    )
    constant = jnp.sum(
        queries.astype(F32) * bias_ref[:, channels : 2 * channels], axis=1, keepdims=True
    )
    return (turned * factor).astype(BF16), constant * factor


def query_kernel(
    rows, info_ref, other_ref, stats_ref, gain_ref, shift_ref, weight_ref, bias_ref, queries_ref,
    constant_ref, means_ref, scales_ref,
):
    info = Info(info_ref, rows)
    means, scales = norm_tables(stats_ref, gain_ref)
    means_ref[...] = means
    scales_ref[...] = scales
    queries, constant = turned_queries(
        info, info.tile() ^ 1, other_ref, means, scales, shift_ref, weight_ref, bias_ref
    )
    queries_ref[...] = queries
    constant_ref[...] = jnp.broadcast_to(constant, constant_ref.shape)


def key_codes(info, masks, span, cols):
    row_count = span // cols
    position = lax.broadcasted_iota(jnp.int32, (1, len(masks) * span), 1)
    codes = jnp.full((1, len(masks) * span), -2.0, F32)
    for index, mask in enumerate(masks):
        near, widths = info.window((info.tile() ^ (2 * mask)) * row_count, row_count)
        for r in range(row_count):
            start = index * span + r * cols
            inside = (position >= start) & (position < start + widths[r])
            codes = jnp.where(inside, near[r].astype(F32), codes)
    return codes


def query_codes(info, tile, span, cols):
    row_count = span // cols
    labels, _ = info.window(tile * row_count, row_count)
    return jnp.concatenate(
        [jnp.zeros((cols, 1), F32) + label.astype(F32) for label in labels], axis=0
    )


def scores_of(queries, keys, codes, query_code):
    scores = lax.dot_general(
        queries, keys, (((1,), (1,)), ((), ())), preferred_element_type=F32
    )
    return jnp.where(codes == query_code, scores, MASKED)


def mean_and_level(peak, denominator, total):
    some = denominator > 0.0
    safe = jnp.where(some, denominator, 1.0)
    return total / safe, jnp.where(some, peak + jnp.log2(safe), LOWEST)


def attend_yours_kernel(rows, masks, first, last, info_ref, *rest):
    means_ref, scales_ref, shift_ref, queries_ref, constant_ref, *rest = rest
    block_refs, rest = rest[: len(masks)], rest[len(masks) :]
    if not first:
        old_peak_ref, old_sum_ref, old_total_ref, *rest = rest
    keys_ref, *out_refs = rest
    info = Info(info_ref, rows)
    span, channels = queries_ref.shape
    pairs, double, _ = block_refs[0].shape
    cols = double // 2
    row_count = 2 * pairs
    tile = info.tile()
    means, scales = means_ref[...], scales_ref[...]
    for index, (mask, block_ref) in enumerate(zip(masks, block_refs)):
        near, _ = info.window((tile ^ (2 * mask)) * row_count, row_count)
        for pair in range(pairs):
            both = block_ref[pair].astype(F32)
            halves = []
            for half in range(2):
                label = near[2 * pair + half]
                mean = pick(means, label, info.videos)
                scale = pick(scales, label, info.videos)
                values = both[half * cols : (half + 1) * cols]
                halves.append((values - mean) * scale + shift_ref[...])
            start = index * span + pair * double
            keys_ref[start : start + double, :] = jnp.concatenate(halves, axis=0).astype(BF16)
    constant = constant_ref[:, 0:1]
    scores = scores_of(
        queries_ref[...], keys_ref[...], key_codes(info, masks, span, cols),
        query_codes(info, tile ^ 1, span, cols),
    )
    peak = jnp.maximum(LOWEST, jnp.max(scores, axis=1, keepdims=True) + constant)
    if not first:
        largest = old_peak_ref[:, 0:1]
        peak = jnp.maximum(largest, peak)
    weights = jnp.exp2(scores - (peak - constant))
    denominator = jnp.sum(weights, axis=1, keepdims=True)
    total = jnp.dot(weights.astype(BF16), keys_ref[...], preferred_element_type=F32)
    if not first:
        factor = jnp.exp2(largest - peak)
        denominator = old_sum_ref[:, 0:1] * factor + denominator
        total = old_total_ref[...] * factor + total
    if not last:
        peak_ref, sum_ref, total_ref = out_refs
        peak_ref[...] = jnp.broadcast_to(peak, peak_ref.shape)
        sum_ref[...] = jnp.broadcast_to(denominator, sum_ref.shape)
        total_ref[...] = total
        return
    (sent_ref,) = out_refs
    mean, level = mean_and_level(peak, denominator, total)
    sent_ref[0:span, :] = mean.astype(BF16)
    slots = sent_ref.shape[0] - span
    slot = lax.broadcasted_iota(jnp.int32, (slots, 1), 0)
    packed = jnp.zeros((slots, LANES), F32)
    for r in range(row_count):
        left = level[r * cols : (r + 1) * cols]
        left = jnp.sum(jnp.where(diagonal(cols), left, 0.0), axis=0, keepdims=True)
        for part in range(3):
            rounded = left.astype(BF16).astype(F32)
            packed = jnp.where(slot == 3 * r + part, rounded, packed)
            left = left - rounded
    sent_ref[span:, 0:LANES] = packed.astype(BF16)
    sent_ref[span:, LANES:] = jnp.zeros((slots, channels - LANES), BF16)


def attend_mine_kernel(
    rows, groups, info_ref, own_ref, means_ref, scales_ref, shift_ref, weight_ref, bias_ref, *rest
):
    key_refs, (mean_ref, level_ref) = rest[: len(groups)], rest[len(groups) :]
    info = Info(info_ref, rows)
    span = mean_ref.shape[0]
    queries, constant = turned_queries(
        info, info.tile(), own_ref, means_ref[...], scales_ref[...], shift_ref, weight_ref,
        bias_ref,
    )
    cols = span // ROWS_OF_TILE
    query_code = query_codes(info, info.tile(), span, cols)
    peak = jnp.full((span, 1), LOWEST, F32)
    scores = []
    for masks, key_ref in zip(groups, key_refs):
        codes = key_codes(info, masks, span, cols)
        scores.append(scores_of(queries, key_ref[...], codes, query_code))
        peak = jnp.maximum(peak, jnp.max(scores[-1], axis=1, keepdims=True) + constant)
    denominator, total = 0.0, 0.0
    for part, key_ref in zip(scores, key_refs):
        weights = jnp.exp2(part - (peak - constant))
        denominator = denominator + jnp.sum(weights, axis=1, keepdims=True)
        total = total + jnp.dot(
            weights.astype(BF16), key_ref[...], preferred_element_type=F32
        )
    mean, level = mean_and_level(peak, denominator, total)
    mean_ref[...] = mean
    level_ref[...] = jnp.broadcast_to(level, level_ref.shape)


def diagonal(cols):
    return lax.broadcasted_iota(jnp.int32, (cols, LANES), 0) == lax.broadcasted_iota(
        jnp.int32, (cols, LANES), 1
    )


def finish_kernel(
    rows, info_ref, mean_ref, level_ref, received_ref, own_ref, triple_ref, triple_bias_ref,
    output_ref, output_bias_ref, out_ref, inner_ref, outer_ref,
):
    info = Info(info_ref, rows)
    row_count, cols, channels = out_ref.shape
    span = row_count * cols
    _, widths = info.window(info.tile() * row_count, row_count)
    received = received_ref[0:span, :].astype(F32)
    levels = received_ref[span:, 0:LANES].astype(F32)
    yours = []
    for r in range(row_count):
        level = levels[3 * r : 3 * r + 1] + levels[3 * r + 1 : 3 * r + 2]
        level = level + levels[3 * r + 2 : 3 * r + 3]
        yours.append(jnp.sum(jnp.where(diagonal(cols), level, 0.0), axis=1, keepdims=True))
    yours = jnp.concatenate(yours, axis=0)
    mine = level_ref[:, 0:1]
    peak = jnp.maximum(mine, yours)
    weight, other_weight = jnp.exp2(mine - peak), jnp.exp2(yours - peak)
    share = weight / (weight + other_weight)
    mean_cell = (mean_ref[...] * share + received * (1.0 - share)).astype(BF16)
    mixed = (
        jnp.dot(mean_cell, triple_ref[:, 2 * channels :], preferred_element_type=F32)
        + triple_bias_ref[:, 2 * channels :]
    ).astype(BF16)
    attended = jnp.dot(mixed, output_ref[...], preferred_element_type=F32) + output_bias_ref[...]
    column = lax.broadcasted_iota(jnp.int32, (cols, 1), 0)
    for r, before in enumerate(split_rows(own_ref)):
        value = before + attended[r * cols : (r + 1) * cols]
        value = jnp.where(column < widths[r], value, 0.0)
        out_ref[r] = value.astype(BF16)
        if r == 0:
            top = value
    odd = lax.rem(info.tile(), 2) == 1
    inner_ref[0] = jnp.where(odd, top, value).astype(BF16)
    outer_ref[0] = jnp.where(odd, value, top).astype(BF16)


def fold_kernel(weight_ref, out_ref):
    channels = weight_ref.shape[-1]
    wide = [[weight_ref[a, b].astype(F32) for b in range(3)] for a in range(3)]

    def both(upper, lower):
        return [x + y for x, y in zip(upper, lower)]

    phases = [[wide[0], both(wide[1], wide[2])], [both(wide[0], wide[1]), wide[2]]]
    for down in range(2):
        for tap in range(2):
            left, middle, right = phases[down][tap]
            out_ref[down, tap, 0, :, 0:channels] = left.astype(BF16)
            out_ref[down, tap, 0, :, channels:] = (middle + right).astype(BF16)
            out_ref[down, tap, 1, :, 0:channels] = (left + middle).astype(BF16)
            out_ref[down, tap, 1, :, channels:] = right.astype(BF16)


def spread_columns(wide_ref, value, row, right):
    cols, channels = value.shape
    for part in range(wide_ref.shape[0]):
        lo, hi = part * LANES, min((part + 1) * LANES, channels)
        piece = value[:, lo:hi]
        if hi - lo < LANES:
            piece = jnp.concatenate([piece, jnp.zeros((cols, LANES - hi + lo), F32)], axis=1)
        wide_ref[part, row, pl.ds(right, cols, 2), :] = piece


def phase_product(columns, weight):
    return lax.dot_general(
        columns, weight, (((1,), (1,)), ((), ())), preferred_element_type=F32
    )


def upsample_kernel(
    rows, info_ref, own_ref, weight_ref, bias_ref, out_ref, open_ref, columns_ref, wide_ref
):
    info = Info(info_ref, rows)
    row_count, cols, channels = own_ref.shape
    padded = columns_ref.shape[0] // row_count
    parts_out = wide_ref.shape[0]
    out_channels = out_ref.shape[-1]
    labels, widths = info.window(info.tile() * row_count, row_count)
    build_columns(
        columns_ref, [functools.partial(own_ref.__getitem__, r) for r in range(row_count)]
    )
    inner_rows = (row_count - 1) * padded
    wide_column = lax.broadcasted_iota(jnp.int32, (2 * cols, 1), 0)
    for down in range(2):
        for right in range(2):
            lanes = slice(right * channels, (right + 2) * channels)
            same = phase_product(columns_ref[:, lanes], weight_ref[down, 1 - down, right])
            start = down * padded
            rim = phase_product(
                columns_ref[start : start + inner_rows, lanes], weight_ref[down, down, right]
            )
            for r in range(row_count):
                value = same[r * padded : r * padded + cols]
                near = r - 1 + 2 * down
                if 0 <= near < row_count:
                    lo = (near - down) * padded
                    value = value + jnp.where(
                        labels[near] == labels[r], rim[lo : lo + cols], 0.0
                    )
                spread_columns(wide_ref, value, 2 * r + down, right)
    for part in range(parts_out):
        open_ref[part, 0] = wide_ref[part, 0]
        open_ref[part, 1] = wide_ref[part, 2 * row_count - 1]
    for r in range(1, 2 * row_count - 1):
        valid = wide_column < 2 * widths[r // 2]
        for part in range(parts_out):
            lo, hi = part * LANES, min((part + 1) * LANES, out_channels)
            value = wide_ref[part, r, :, 0 : hi - lo] + bias_ref[:, lo:hi]
            out_ref[r - 1, :, lo:hi] = jnp.where(valid, value, 0.0).astype(BF16)


def close_kernel(
    rows, info_ref, outer_ref, inner_ref, middle_ref, open_ref, weight_ref, bias_ref, out_ref,
    columns_ref, wide_ref,
):
    info = Info(info_ref, rows)
    wide_rows, wide_cols, out_channels = out_ref.shape
    row_count, cols = wide_rows // 2, wide_cols // 2
    channels = outer_ref.shape[-1]
    padded = columns_ref.shape[0] // 2
    labels, widths = info.window(info.tile() * row_count - 1, row_count + 2)
    above, below = rims(info, outer_ref, inner_ref)
    build_columns(columns_ref, [lambda: above, lambda: below])
    wide_column = lax.broadcasted_iota(jnp.int32, (wide_cols, 1), 0)
    for down in range(2):
        for right in range(2):
            lanes = slice(right * channels, (right + 2) * channels)
            rim = phase_product(
                columns_ref[down * padded : (down + 1) * padded, lanes],
                weight_ref[down, down, right],
            )
            spread_columns(wide_ref, rim[:cols], down, right)
    out_ref[1 : wide_rows - 1] = middle_ref[...]
    for down in range(2):
        rim_row, own_row = (row_count + 1, row_count) if down else (0, 1)
        valid = wide_column < 2 * widths[own_row]
        for part in range(wide_ref.shape[0]):
            lo, hi = part * LANES, min((part + 1) * LANES, out_channels)
            rim = jnp.where(
                labels[rim_row] == labels[own_row], wide_ref[part, down, :, 0 : hi - lo], 0.0
            )
            value = open_ref[part, down, :, 0 : hi - lo] + rim + bias_ref[:, lo:hi]
            value = jnp.where(valid, value, 0.0).astype(BF16)
            out_ref[down * (wide_rows - 1), :, lo:hi] = value


def merge_stats(mine, other):
    count = mine[0] + other[0]
    safe = jnp.maximum(count, 1.0)
    off = other[1] - mine[1]
    mean = mine[1] + off * (other[0] / safe)
    spread = mine[2] + other[2] + off * off * (mine[0] * other[0] / safe)
    return jnp.stack([count, mean, spread])


def exchange(array, tiles, mask, among=None):
    moves = [(i, i ^ mask) for i in range(tiles) if among is None or among(i)]
    return lax.ppermute(array, "tile", moves)


def merge_round(stats, tiles, masks, tied=()):
    parts = [stats] + [exchange(stats, tiles, mask) for mask in masks]
    if tied:
        parts[1], *tied = lax.optimization_barrier((parts[1], *tied))
    while len(parts) > 1:
        parts = [merge_stats(*parts[i : i + 2]) for i in range(0, len(parts), 2)]
    return (parts[0], *tied) if tied else parts[0]


def merge_masks(tiles):
    bits = [1 << i for i in range(tiles.bit_length() - 1)]
    pairs = [bits[i : i + 2] for i in range(0, len(bits), 2)]
    return [[p[0], p[1], p[0] ^ p[1]] if len(p) == 2 else p for p in pairs]


def shards(
    tiles,
    frames,
    latents,
    row_video,
    video_cols,
    first_gain,
    first_shift,
    conv_weight,
    conv_bias,
    second_gain,
    second_shift,
    triple_weight,
    triple_bias,
    output_weight,
    output_bias,
    upsample_weight,
    upsample_bias,
):
    row_count, frame_count, cols, channels = latents.shape
    assert frame_count == 1 and row_count == ROWS_OF_TILE and tiles % 4 == 0
    out_channels = upsample_weight.shape[-1]
    rows = row_count * tiles
    cells = row_count * cols
    padded = -(-(cols + 1) // 16) * 16
    near_rows = row_count + 2
    source = latents.reshape(row_count, cols, channels)
    tile = lax.axis_index("tile").astype(jnp.int32)
    info = jnp.concatenate([jnp.reshape(tile, (1,)), row_video, video_cols])

    def row(vector):
        return vector.reshape(1, -1)

    def shape(*dims, dtype=BF16):
        return jax.ShapeDtypeStruct(dims, dtype)

    def call(kernel, operands, out_shape, scratch=(), **kwargs):
        many = isinstance(out_shape, tuple)
        return pl.pallas_call(
            kernel,
            out_shape=out_shape,
            in_specs=[SMEM_SPEC] + [VMEM_SPEC] * len(operands),
            out_specs=(VMEM_SPEC,) * len(out_shape) if many else VMEM_SPEC,
            scratch_shapes=list(scratch),
            compiler_params=params(),
            **kwargs,
        )(info, *operands)

    outer_moves = [(i, i - 1 if i % 2 == 0 else i + 1) for i in range(tiles)]
    outer_moves = [(i, j) for i, j in outer_moves if 0 <= j < tiles]
    odd = tile % 2 == 1
    stats_shape = shape(3, SLOTS, LANES, dtype=F32)
    stats = call(
        functools.partial(stats_kernel, rows), [source], stats_shape,
        cost_estimate=cost(1.5), name="first_stats",
    )
    outer = lax.ppermute(
        jnp.where(odd, source[row_count - 1 :], source[:1]), "tile", outer_moves
    )
    inner = exchange(jnp.where(odd, source[:1], source[row_count - 1 :]), tiles, 1)
    stats, outer, inner = lax.optimization_barrier((stats, outer, inner))
    taps = min(3, frames)
    held = pl.pallas_call(
        functools.partial(hold_kernel, taps),
        out_shape=shape(3 * taps * channels, 3 * channels),
        in_specs=[HBM_SPEC],
        out_specs=VMEM_SPEC,
        scratch_shapes=[pltpu.SemaphoreType.DMA((3, 3 * taps))],
        compiler_params=pltpu.CompilerParams(vmem_limit_bytes=HOLD_VMEM_BYTES),
        cost_estimate=cost(1.5 * taps),
        name="hold",
    )(conv_weight)
    rounds = merge_masks(tiles)
    for index, masks in enumerate(reversed(rounds)):
        stats = merge_round(stats, tiles, masks)
        if index == len(rounds) - 2:
            stats, held = lax.optimization_barrier((stats, held))
    hidden, source = call(
        functools.partial(hidden_kernel, rows),
        [outer, inner, source, stats, row(first_gain), row(first_shift)],
        (shape(near_rows, padded, channels), shape(row_count, cols, channels)),
        cost_estimate=cost(1.3),
        name="hidden",
    )

    context = [hidden] + [
        lax.ppermute(hidden, "frame", [(i, i + by) for i in range(frames - by)])
        for by in range(1, taps)
    ]

    pairs = row_count // 2
    pair_shape = shape(pairs, 2 * cols, channels)
    own, stats = pl.pallas_call(
        functools.partial(conv_kernel, rows, taps),
        out_shape=(pair_shape, stats_shape),
        in_specs=[SMEM_SPEC] + [VMEM_SPEC] * (taps + 3),
        out_specs=(VMEM_SPEC, VMEM_SPEC),
        scratch_shapes=[
            pltpu.VMEM((row_count * padded, 3 * taps * channels), BF16),
        ],
        compiler_params=params(),
        cost_estimate=cost(2.5 * taps),
        name="conv",
    )(info, *context, source, row(conv_bias), held)

    blocks = {0: own}
    neighbour = [(i, i ^ 1) for i in range(tiles)]
    if tiles == 16 and video_cols.shape[0] == 2:
        def middle(t):
            return t // 4 in (1, 2)

        stats = merge_round(stats, tiles, rounds[1])
        blocks[2] = exchange(own, tiles, 4)
        blocks[6] = exchange(own, tiles, 12, middle)
        stats, blocks[2], blocks[6] = merge_round(
            stats, tiles, rounds[0], (blocks[2], blocks[6])
        )
        stats, own_xy = lax.optimization_barrier((stats, own))
        inward = exchange(blocks[2], tiles, 12, middle)
        outward = exchange(blocks[6], tiles, 4, middle)
        other = exchange(own_xy, tiles, 1)
        blocks[1] = exchange(own_xy, tiles, 2)
        blocks[4] = jnp.where((tile // 4 == 1) | (tile // 4 == 2), inward, outward)
        passed, blocks[4] = lax.optimization_barrier((blocks[1], blocks[4]))
        blocks[5] = exchange(blocks[4], tiles, 2)
        blocks[3] = exchange(passed, tiles, 4)
        blocks[7] = exchange(passed, tiles, 12, middle)
        groups = [[0, 1, 2, 6], [4, 7, 3, 5]]
    else:
        for masks in rounds:
            stats = merge_round(stats, tiles, masks)
        other = exchange(own, tiles, 1)
        for mask in range(1, tiles // 2):
            blocks[mask] = exchange(own, tiles, 2 * mask)
        groups = [list(range(i, i + 4)) for i in range(0, tiles // 2, 4)]
    gain, shift = row(second_gain), row(second_shift)
    table_shape = shape(SLOTS, channels, dtype=F32)
    queries, constant, means, scales = call(
        functools.partial(query_kernel, rows),
        [other, stats, gain, shift, triple_weight, row(triple_bias)],
        (shape(cells, channels), shape(cells, LANES, dtype=F32), table_shape, table_shape),
        cost_estimate=cost(1.5),
        name="queries",
    )
    level_shape = shape(cells, LANES, dtype=F32)
    total_shape = shape(cells, channels, dtype=F32)
    state, keys = (), []
    for index, masks in enumerate(groups):
        last = index == len(groups) - 1
        outs = (shape(len(masks) * cells, channels),)
        outs += (shape(cells + 16, channels),) if last else (level_shape, level_shape, total_shape)
        normed, *state = call(
            functools.partial(attend_yours_kernel, rows, tuple(masks), index == 0, last),
            [means, scales, shift, queries, constant] + [blocks[m] for m in masks] + list(state),
            outs,
            cost_estimate=cost(0.9 * len(masks)),
            name="attend_yours",
        )
        keys.append(normed)
    (sent,) = state
    received = lax.ppermute(sent, "tile", neighbour)
    sent, own_late, upsample_weight = lax.optimization_barrier((sent, own, upsample_weight))
    mean, level = call(
        functools.partial(attend_mine_kernel, rows, tuple(tuple(masks) for masks in groups)),
        [own_late, means, scales, shift, triple_weight, row(triple_bias)] + keys,
        (total_shape, level_shape),
        cost_estimate=cost(6.0),
        name="attend_mine",
    )
    folded = pl.pallas_call(
        fold_kernel,
        out_shape=shape(2, 2, 2, out_channels, 2 * channels),
        in_specs=[VMEM_SPEC],
        out_specs=VMEM_SPEC,
        compiler_params=params(),
        cost_estimate=cost(0.5),
        name="fold",
    )(jnp.swapaxes(upsample_weight, 2, 3))

    rim_shape = shape(1, cols, channels)
    attended, inner, outer = call(
        functools.partial(finish_kernel, rows),
        [
            mean, level, received, own, triple_weight, row(triple_bias), output_weight,
            row(output_bias),
        ],
        (shape(row_count, cols, channels), rim_shape, rim_shape),
        cost_estimate=cost(1.4),
        name="finish",
    )
    outer = lax.ppermute(outer, "tile", outer_moves)
    inner = exchange(inner, tiles, 1)
    parts_out = -(-out_channels // LANES)
    middle, open_rows = call(
        functools.partial(upsample_kernel, rows),
        [attended, folded, row(upsample_bias)],
        (
            shape(2 * row_count - 2, 2 * cols, out_channels),
            shape(parts_out, 2, 2 * cols, LANES, dtype=F32),
        ),
        scratch=[
            pltpu.VMEM((row_count * padded, 3 * channels), BF16),
            pltpu.VMEM((parts_out, 2 * row_count, 2 * cols, LANES), F32),
        ],
        cost_estimate=cost(2.0),
        name="upsample",
    )
    decoded = call(
        functools.partial(close_kernel, rows),
        [outer, inner, middle, open_rows, folded, row(upsample_bias)],
        shape(2 * row_count, 2 * cols, out_channels),
        scratch=[
            pltpu.VMEM((2 * padded, 3 * channels), BF16),
            pltpu.VMEM((parts_out, 2, 2 * cols, LANES), F32),
        ],
        cost_estimate=cost(1.0),
        name="close",
    )
    return decoded.reshape(2 * row_count, 1, 2 * cols, out_channels)


def solution(mesh):
    sizes = dict(mesh.shape)
    in_specs = (P("tile", "frame", None, None),) + (P(),) * 14
    out_specs = P("tile", "frame", None, None)
    body = functools.partial(shards, sizes["tile"], sizes["frame"])
    return jax.shard_map(body, mesh=mesh, in_specs=in_specs, out_specs=out_specs, check_vma=False)
```

```python
import functools
import math

import jax
import jax.numpy as jnp
from jax import lax
from jax.experimental import pallas as pl
from jax.experimental.pallas import tpu as pltpu
from jax.sharding import PartitionSpec as P

GROUPS = 32
EPSILON = 1e-05
MASKED = -1e30
LOWEST = -5e29
HIGHEST = lax.Precision.HIGHEST
SLOTS = 8
ROWS_OF_TILE = 4
LANES = 128
VMEM_BYTES = 24 * 1024 * 1024
HOLD_VMEM_BYTES = 46 * 1024 * 1024
F32 = jnp.float32
BF16 = jnp.bfloat16

SMEM_SPEC = pl.BlockSpec(memory_space=pltpu.SMEM)
VMEM_SPEC = pl.BlockSpec(memory_space=pltpu.VMEM)
HBM_SPEC = pl.BlockSpec(memory_space=pltpu.HBM)


def cost(microseconds):
    return pl.CostEstimate(
        flops=int(microseconds * 1.1e9), bytes_accessed=0, transcendentals=0
    )


def params():
    return pltpu.CompilerParams(vmem_limit_bytes=VMEM_BYTES)


def member_matrix(channels):
    per_group = channels // GROUPS
    group = lax.broadcasted_iota(jnp.int32, (LANES, channels), 0) * per_group
    channel = lax.broadcasted_iota(jnp.int32, (LANES, channels), 1)
    return jnp.where((channel >= group) & (channel < group + per_group), 1.0, 0.0).astype(F32)


def to_groups(values, member):
    return lax.dot_general(
        values, member, (((1,), (1,)), ((), ())), precision=HIGHEST, preferred_element_type=F32
    )


def to_channels(values, member):
    return jnp.dot(values, member, precision=HIGHEST, preferred_element_type=F32)


class Info:
    def __init__(self, ref, rows):
        self.ref, self.rows = ref, rows
        self.videos = ref.shape[0] - 2 - rows

    def tile(self):
        return self.ref[0]

    def frame(self):
        return self.ref[1]

    def label(self, row):
        inside = (row >= 0) & (row < self.rows)
        return jnp.where(inside, self.ref[2 + jnp.clip(row, 0, self.rows - 1)], -1)

    def width(self, label):
        return jnp.where(label >= 0, self.ref[2 + self.rows + jnp.maximum(label, 0)], 0)

    def window(self, first, count):
        labels = [self.label(first + r) for r in range(count)]
        return labels, [self.width(label) for label in labels]


def pick(table, label, videos):
    chosen = table[0:1]
    for video in range(1, videos):
        chosen = jnp.where(label == video, table[video : video + 1], chosen)
    return chosen


def norm_tables(stats_ref, gain_ref):
    member = member_matrix(gain_ref.shape[1])
    counts = jnp.maximum(stats_ref[0], 1.0)
    scale = lax.rsqrt(stats_ref[2] / counts + EPSILON)
    return to_channels(stats_ref[1], member), to_channels(scale, member) * gain_ref[...]


def write_stats(out_ref, rows, labels, widths, videos, channels):
    member = member_matrix(channels)
    per_group = channels // GROUPS
    cols = rows[0].shape[0]
    slot = lax.broadcasted_iota(jnp.int32, (SLOTS, 1), 0)
    column = lax.broadcasted_iota(jnp.int32, (cols, 1), 0)
    sums = jnp.zeros((SLOTS, channels), F32)
    counts = jnp.zeros((SLOTS, 1), F32)
    for index, row in enumerate(rows):
        sums = jnp.where(slot == index, jnp.sum(row, axis=0, keepdims=True), sums)
        counts = jnp.where(slot == index, (widths[index] * per_group).astype(F32), counts)
    means = to_groups(sums, member) / jnp.maximum(counts, 1.0)
    means_wide = to_channels(means, member)
    squares = jnp.zeros((SLOTS, channels), F32)
    for index, row in enumerate(rows):
        centered = jnp.where(column < widths[index], row - means_wide[index : index + 1], 0.0)
        squares = jnp.where(
            slot == index, jnp.sum(centered * centered, axis=0, keepdims=True), squares
        )
    spreads = to_groups(squares, member)
    out_ref[...] = jnp.zeros(out_ref.shape, F32)
    for video in range(videos):
        total = jnp.zeros((1, LANES), F32)
        count = jnp.zeros((1, LANES), F32)
        for index in range(len(rows)):
            mine = labels[index] == video
            row_count = counts[index : index + 1]
            total = total + jnp.where(mine, means[index : index + 1] * row_count, 0.0)
            count = count + jnp.where(mine, row_count, 0.0)
        mean = total / jnp.maximum(count, 1.0)
        spread = jnp.zeros((1, LANES), F32)
        for index in range(len(rows)):
            off = means[index : index + 1] - mean
            part = spreads[index : index + 1] + counts[index : index + 1] * off * off
            spread = spread + jnp.where(labels[index] == video, part, 0.0)
        out_ref[0, video : video + 1, :] = count
        out_ref[1, video : video + 1, :] = mean
        out_ref[2, video : video + 1, :] = spread


def build_columns(columns_ref, row_refs):
    padded = columns_ref.shape[0] // len(row_refs)
    for index, row in enumerate(row_refs):
        cells = row().astype(F32)
        count, channels = cells.shape
        cells = jnp.concatenate([cells, jnp.zeros((padded - count, channels), F32)], axis=0)
        start = index * padded
        columns_ref[start : start + padded, 0:channels] = pltpu.roll(cells, 1, 0).astype(BF16)
        columns_ref[start : start + padded, channels : 2 * channels] = cells.astype(BF16)
        columns_ref[start : start + padded, 2 * channels : 3 * channels] = pltpu.roll(
            cells, padded - 1, 0
        ).astype(BF16)


def stats_kernel(rows, info_ref, latents_ref, out_ref):
    info = Info(info_ref, rows)
    row_count, cols, channels = latents_ref.shape
    labels, widths = info.window(info.tile() * row_count, row_count)
    column = lax.broadcasted_iota(jnp.int32, (cols, 1), 0)
    cells = [
        jnp.where(column < widths[r], latents_ref[r].astype(F32), 0.0) for r in range(row_count)
    ]
    write_stats(out_ref, cells, labels, widths, info.videos, channels)


def rims(info, outer_ref, inner_ref):
    odd = lax.rem(info.tile(), 2) == 1
    inner, outer = inner_ref[0].astype(F32), outer_ref[0].astype(F32)
    return jnp.where(odd, inner, outer), jnp.where(odd, outer, inner)


def hidden_kernel(
    rows, info_ref, outer_ref, inner_ref, latents_ref, stats_ref, gain_ref, shift_ref, out_ref,
    source_ref,
):
    info = Info(info_ref, rows)
    row_count, cols, _ = latents_ref.shape
    labels, widths = info.window(info.tile() * row_count - 1, row_count + 2)
    means, scales = norm_tables(stats_ref, gain_ref)
    column = lax.broadcasted_iota(jnp.int32, (cols, 1), 0)
    above, below = rims(info, outer_ref, inner_ref)
    sources = [above] + [latents_ref[r].astype(F32) for r in range(row_count)] + [below]
    for r, source in enumerate(sources):
        mean = pick(means, labels[r], info.videos)
        scale = pick(scales, labels[r], info.videos)
        normed = (source - mean) * scale + shift_ref[...]
        active = normed / (1.0 + jnp.exp(-normed))
        active = jnp.where(column < widths[r], active, 0.0)
        rest = jnp.zeros((out_ref.shape[1] - cols, active.shape[1]), F32)
        out_ref[r] = jnp.concatenate([active, rest], axis=0).astype(BF16)
    source_ref[...] = latents_ref[...]


def hold_kernel(taps, weight_ref, held_ref, sems):
    channels = weight_ref.shape[-1]
    copies = [
        pltpu.make_async_copy(
            weight_ref.at[2 - depth // 3, depth % 3, side],
            held_ref.at[pl.ds(depth * channels, channels), pl.ds(side * channels, channels)],
            sems.at[side, depth],
        )
        for side in range(3)
        for depth in range(3 * taps)
    ]
    for copy in copies:
        copy.start()
    for copy in copies:
        copy.wait()


def conv_kernel(rows, taps, info_ref, *rest):
    hidden_refs, rest = rest[:taps], rest[taps:]
    latents_ref, bias_ref, held_ref, own_ref, stats_ref, inputs_ref, product_ref = rest
    row_count, cols, channels = latents_ref.shape
    info = Info(info_ref, rows)
    padded = hidden_refs[0].shape[1]
    labels, widths = info.window(info.tile() * row_count - 1, row_count + 2)
    for active in range(1, taps + 1):
        frames = info.frame() + 1

        @pl.when(frames == active if active < taps else frames >= active)
        def _(active=active):
            for back in range(active):
                for tap in range(3):
                    depth = 3 * back + tap
                    lanes = slice(depth * channels, (depth + 1) * channels)
                    for r in range(row_count):
                        block = hidden_refs[back][r + tap]
                        if tap != 1:
                            same = labels[r + tap] == labels[r + 1]
                            block = jnp.where(same, block, jnp.zeros_like(block))
                        inputs_ref[r * padded : (r + 1) * padded, lanes] = block
            deep = 3 * active * channels
            product_ref[...] = jnp.dot(
                inputs_ref[:, 0:deep], held_ref[0:deep, :], preferred_element_type=F32
            )

    column = lax.broadcasted_iota(jnp.int32, (cols, 1), 0)
    cells = []
    for r in range(row_count):
        lines = slice(r * padded, (r + 1) * padded)
        branch = pltpu.roll(product_ref[lines, 0:channels], 1, 0)
        branch = branch + product_ref[lines, channels : 2 * channels]
        branch = branch + pltpu.roll(product_ref[lines, 2 * channels :], padded - 1, 0)
        value = latents_ref[r].astype(F32) + branch[:cols] + bias_ref[...]
        value = jnp.where(column < widths[r + 1], value, 0.0).astype(BF16)
        cells.append(value.astype(F32))
    for pair in range(row_count // 2):
        own_ref[pair] = jnp.concatenate(cells[2 * pair : 2 * pair + 2], axis=0).astype(BF16)
    write_stats(stats_ref, cells, labels[1:-1], widths[1:-1], info.videos, channels)


def split_rows(pairs_ref):
    cols = pairs_ref.shape[1] // 2
    cells = []
    for pair in range(pairs_ref.shape[0]):
        both = pairs_ref[pair].astype(F32)
        cells += [both[:cols], both[cols:]]
    return cells


def turned_queries(info, tile, pairs_ref, means, scales, shift_ref, weight_ref, bias_ref):
    pairs, double, channels = pairs_ref.shape
    cols = double // 2
    column = lax.broadcasted_iota(jnp.int32, (cols, 1), 0)
    labels, widths = info.window(tile * 2 * pairs, 2 * pairs)
    cells = []
    for r, values in enumerate(split_rows(pairs_ref)):
        mean = pick(means, labels[r], info.videos)
        scale = pick(scales, labels[r], info.videos)
        normed = (values - mean) * scale + shift_ref[...]
        cells.append(jnp.where(column < widths[r], normed, 0.0))
    cells = jnp.concatenate(cells, axis=0).astype(BF16)
    queries = (
        jnp.dot(cells, weight_ref[:, 0:channels], preferred_element_type=F32)
        + bias_ref[:, 0:channels]
    ).astype(BF16)
    factor = channels ** (-0.5) * math.log2(math.e)
    turned = lax.dot_general(
        queries, weight_ref[:, channels : 2 * channels], (((1,), (1,)), ((), ())),
        preferred_element_type=F32,
    )
    constant = jnp.sum(
        queries.astype(F32) * bias_ref[:, channels : 2 * channels], axis=1, keepdims=True
    )
    return (turned * factor).astype(BF16), constant * factor


def query_kernel(
    rows, info_ref, other_ref, stats_ref, gain_ref, shift_ref, weight_ref, bias_ref, queries_ref,
    constant_ref, means_ref, scales_ref,
):
    info = Info(info_ref, rows)
    means, scales = norm_tables(stats_ref, gain_ref)
    means_ref[...] = means
    scales_ref[...] = scales
    queries, constant = turned_queries(
        info, info.tile() ^ 1, other_ref, means, scales, shift_ref, weight_ref, bias_ref
    )
    queries_ref[...] = queries
    constant_ref[...] = jnp.broadcast_to(constant, constant_ref.shape)


def key_codes(info, masks, span, cols):
    row_count = span // cols
    position = lax.broadcasted_iota(jnp.int32, (1, len(masks) * span), 1)
    codes = jnp.full((1, len(masks) * span), -2.0, F32)
    for index, mask in enumerate(masks):
        near, widths = info.window((info.tile() ^ (2 * mask)) * row_count, row_count)
        for r in range(row_count):
            start = index * span + r * cols
            inside = (position >= start) & (position < start + widths[r])
            codes = jnp.where(inside, near[r].astype(F32), codes)
    return codes


def query_codes(info, tile, span, cols):
    row_count = span // cols
    labels, _ = info.window(tile * row_count, row_count)
    return jnp.concatenate(
        [jnp.zeros((cols, 1), F32) + label.astype(F32) for label in labels], axis=0
    )


def scores_of(queries, keys, codes, query_code):
    scores = lax.dot_general(
        queries, keys, (((1,), (1,)), ((), ())), preferred_element_type=F32
    )
    return jnp.where(codes == query_code, scores, MASKED)


def mean_and_level(peak, denominator, total):
    some = denominator > 0.0
    safe = jnp.where(some, denominator, 1.0)
    return total / safe, jnp.where(some, peak + jnp.log2(safe), LOWEST)


def attend_yours_kernel(rows, masks, first, last, info_ref, *rest):
    means_ref, scales_ref, shift_ref, queries_ref, constant_ref, *rest = rest
    block_refs, rest = rest[: len(masks)], rest[len(masks) :]
    if not first:
        old_peak_ref, old_sum_ref, old_total_ref, *rest = rest
    keys_ref, *out_refs = rest
    info = Info(info_ref, rows)
    span, channels = queries_ref.shape
    pairs, double, _ = block_refs[0].shape
    cols = double // 2
    row_count = 2 * pairs
    tile = info.tile()
    means, scales = means_ref[...], scales_ref[...]
    for index, (mask, block_ref) in enumerate(zip(masks, block_refs)):
        near, _ = info.window((tile ^ (2 * mask)) * row_count, row_count)
        for pair in range(pairs):
            both = block_ref[pair].astype(F32)
            halves = []
            for half in range(2):
                label = near[2 * pair + half]
                mean = pick(means, label, info.videos)
                scale = pick(scales, label, info.videos)
                values = both[half * cols : (half + 1) * cols]
                halves.append((values - mean) * scale + shift_ref[...])
            start = index * span + pair * double
            keys_ref[start : start + double, :] = jnp.concatenate(halves, axis=0).astype(BF16)
    constant = constant_ref[:, 0:1]
    scores = scores_of(
        queries_ref[...], keys_ref[...], key_codes(info, masks, span, cols),
        query_codes(info, tile ^ 1, span, cols),
    )
    peak = jnp.maximum(LOWEST, jnp.max(scores, axis=1, keepdims=True) + constant)
    if not first:
        largest = old_peak_ref[:, 0:1]
        peak = jnp.maximum(largest, peak)
    weights = jnp.exp2(scores - (peak - constant))
    denominator = jnp.sum(weights, axis=1, keepdims=True)
    total = jnp.dot(weights.astype(BF16), keys_ref[...], preferred_element_type=F32)
    if not first:
        factor = jnp.exp2(largest - peak)
        denominator = old_sum_ref[:, 0:1] * factor + denominator
        total = old_total_ref[...] * factor + total
    if not last:
        peak_ref, sum_ref, total_ref = out_refs
        peak_ref[...] = jnp.broadcast_to(peak, peak_ref.shape)
        sum_ref[...] = jnp.broadcast_to(denominator, sum_ref.shape)
        total_ref[...] = total
        return
    (sent_ref,) = out_refs
    mean, level = mean_and_level(peak, denominator, total)
    sent_ref[0:span, :] = mean.astype(BF16)
    slots = sent_ref.shape[0] - span
    slot = lax.broadcasted_iota(jnp.int32, (slots, 1), 0)
    packed = jnp.zeros((slots, LANES), F32)
    for r in range(row_count):
        left = level[r * cols : (r + 1) * cols]
        left = jnp.sum(jnp.where(diagonal(cols), left, 0.0), axis=0, keepdims=True)
        for part in range(3):
            rounded = left.astype(BF16).astype(F32)
            packed = jnp.where(slot == 3 * r + part, rounded, packed)
            left = left - rounded
    sent_ref[span:, 0:LANES] = packed.astype(BF16)
    sent_ref[span:, LANES:] = jnp.zeros((slots, channels - LANES), BF16)


def attend_mine_kernel(
    rows, groups, info_ref, own_ref, means_ref, scales_ref, shift_ref, weight_ref, bias_ref, *rest
):
    key_refs, (mean_ref, level_ref) = rest[: len(groups)], rest[len(groups) :]
    info = Info(info_ref, rows)
    span = mean_ref.shape[0]
    queries, constant = turned_queries(
        info, info.tile(), own_ref, means_ref[...], scales_ref[...], shift_ref, weight_ref,
        bias_ref,
    )
    cols = span // ROWS_OF_TILE
    query_code = query_codes(info, info.tile(), span, cols)
    peak = jnp.full((span, 1), LOWEST, F32)
    scores = []
    for masks, key_ref in zip(groups, key_refs):
        codes = key_codes(info, masks, span, cols)
        scores.append(scores_of(queries, key_ref[...], codes, query_code))
        peak = jnp.maximum(peak, jnp.max(scores[-1], axis=1, keepdims=True) + constant)
    denominator, total = 0.0, 0.0
    for part, key_ref in zip(scores, key_refs):
        weights = jnp.exp2(part - (peak - constant))
        denominator = denominator + jnp.sum(weights, axis=1, keepdims=True)
        total = total + jnp.dot(
            weights.astype(BF16), key_ref[...], preferred_element_type=F32
        )
    mean, level = mean_and_level(peak, denominator, total)
    mean_ref[...] = mean
    level_ref[...] = jnp.broadcast_to(level, level_ref.shape)


def diagonal(cols):
    return lax.broadcasted_iota(jnp.int32, (cols, LANES), 0) == lax.broadcasted_iota(
        jnp.int32, (cols, LANES), 1
    )


def finish_kernel(
    rows, info_ref, mean_ref, level_ref, received_ref, own_ref, triple_ref, triple_bias_ref,
    output_ref, output_bias_ref, out_ref, inner_ref, outer_ref,
):
    info = Info(info_ref, rows)
    row_count, cols, channels = out_ref.shape
    span = row_count * cols
    _, widths = info.window(info.tile() * row_count, row_count)
    received = received_ref[0:span, :].astype(F32)
    levels = received_ref[span:, 0:LANES].astype(F32)
    yours = []
    for r in range(row_count):
        level = levels[3 * r : 3 * r + 1] + levels[3 * r + 1 : 3 * r + 2]
        level = level + levels[3 * r + 2 : 3 * r + 3]
        yours.append(jnp.sum(jnp.where(diagonal(cols), level, 0.0), axis=1, keepdims=True))
    yours = jnp.concatenate(yours, axis=0)
    mine = level_ref[:, 0:1]
    peak = jnp.maximum(mine, yours)
    weight, other_weight = jnp.exp2(mine - peak), jnp.exp2(yours - peak)
    share = weight / (weight + other_weight)
    mean_cell = (mean_ref[...] * share + received * (1.0 - share)).astype(BF16)
    mixed = (
        jnp.dot(mean_cell, triple_ref[:, 2 * channels :], preferred_element_type=F32)
        + triple_bias_ref[:, 2 * channels :]
    ).astype(BF16)
    attended = jnp.dot(mixed, output_ref[...], preferred_element_type=F32) + output_bias_ref[...]
    column = lax.broadcasted_iota(jnp.int32, (cols, 1), 0)
    for r, before in enumerate(split_rows(own_ref)):
        value = before + attended[r * cols : (r + 1) * cols]
        value = jnp.where(column < widths[r], value, 0.0)
        out_ref[r] = value.astype(BF16)
        if r == 0:
            top = value
    odd = lax.rem(info.tile(), 2) == 1
    inner_ref[0] = jnp.where(odd, top, value).astype(BF16)
    outer_ref[0] = jnp.where(odd, value, top).astype(BF16)


def fold_kernel(weight_ref, out_ref):
    channels = weight_ref.shape[-1]
    wide = [[weight_ref[a, b].astype(F32) for b in range(3)] for a in range(3)]

    def both(upper, lower):
        return [x + y for x, y in zip(upper, lower)]

    phases = [[wide[0], both(wide[1], wide[2])], [both(wide[0], wide[1]), wide[2]]]
    for down in range(2):
        for tap in range(2):
            left, middle, right = phases[down][tap]
            out_ref[down, tap, 0, :, 0:channels] = left.astype(BF16)
            out_ref[down, tap, 0, :, channels:] = (middle + right).astype(BF16)
            out_ref[down, tap, 1, :, 0:channels] = (left + middle).astype(BF16)
            out_ref[down, tap, 1, :, channels:] = right.astype(BF16)


def spread_columns(wide_ref, value, row, right):
    cols, channels = value.shape
    for part in range(wide_ref.shape[0]):
        lo, hi = part * LANES, min((part + 1) * LANES, channels)
        piece = value[:, lo:hi]
        if hi - lo < LANES:
            piece = jnp.concatenate([piece, jnp.zeros((cols, LANES - hi + lo), F32)], axis=1)
        wide_ref[part, row, pl.ds(right, cols, 2), :] = piece


def write_turned(out_ref, row, part, value, width):
    channels, cols = out_ref.shape[1:]
    lo, hi = part * LANES, min((part + 1) * LANES, channels)
    turned = value.T[0 : hi - lo, 0:cols]
    column = lax.broadcasted_iota(jnp.int32, (1, cols), 1)
    out_ref[row, lo:hi, :] = jnp.where(column < width, turned, 0.0).astype(BF16)


def phase_product(columns, weight):
    return lax.dot_general(
        columns, weight, (((1,), (1,)), ((), ())), preferred_element_type=F32
    )


def upsample_kernel(
    rows, info_ref, own_ref, weight_ref, bias_ref, out_ref, open_ref, columns_ref, wide_ref
):
    info = Info(info_ref, rows)
    row_count, cols, channels = own_ref.shape
    padded = columns_ref.shape[0] // row_count
    parts_out = wide_ref.shape[0]
    labels, widths = info.window(info.tile() * row_count, row_count)
    build_columns(
        columns_ref, [functools.partial(own_ref.__getitem__, r) for r in range(row_count)]
    )
    inner_rows = (row_count - 1) * padded
    for down in range(2):
        for right in range(2):
            lanes = slice(right * channels, (right + 2) * channels)
            same = phase_product(columns_ref[:, lanes], weight_ref[down, 1 - down, right])
            start = down * padded
            rim = phase_product(
                columns_ref[start : start + inner_rows, lanes], weight_ref[down, down, right]
            )
            for r in range(row_count):
                value = same[r * padded : r * padded + cols]
                near = r - 1 + 2 * down
                if 0 <= near < row_count:
                    lo = (near - down) * padded
                    value = value + jnp.where(
                        labels[near] == labels[r], rim[lo : lo + cols], 0.0
                    )
                spread_columns(wide_ref, value, 2 * r + down, right)
    for part in range(parts_out):
        open_ref[part, 0] = wide_ref[part, 0]
        open_ref[part, 1] = wide_ref[part, 2 * row_count - 1]
    for r in range(1, 2 * row_count - 1):
        for part in range(parts_out):
            value = wide_ref[part, r] + bias_ref[:, part * LANES : (part + 1) * LANES]
            write_turned(out_ref, r - 1, part, value, 2 * widths[r // 2])


def close_kernel(
    rows, info_ref, outer_ref, inner_ref, middle_ref, open_ref, weight_ref, bias_ref, out_ref,
    columns_ref, wide_ref,
):
    info = Info(info_ref, rows)
    wide_rows, _, wide_cols = out_ref.shape
    row_count, cols = wide_rows // 2, wide_cols // 2
    channels = outer_ref.shape[-1]
    padded = columns_ref.shape[0] // 2
    labels, widths = info.window(info.tile() * row_count - 1, row_count + 2)
    above, below = rims(info, outer_ref, inner_ref)
    build_columns(columns_ref, [lambda: above, lambda: below])
    for down in range(2):
        for right in range(2):
            lanes = slice(right * channels, (right + 2) * channels)
            rim = phase_product(
                columns_ref[down * padded : (down + 1) * padded, lanes],
                weight_ref[down, down, right],
            )
            spread_columns(wide_ref, rim[:cols], down, right)
    out_ref[1 : wide_rows - 1] = middle_ref[...]
    for down in range(2):
        rim_row, own_row = (row_count + 1, row_count) if down else (0, 1)
        for part in range(wide_ref.shape[0]):
            rim = jnp.where(labels[rim_row] == labels[own_row], wide_ref[part, down], 0.0)
            value = open_ref[part, down] + rim + bias_ref[:, part * LANES : (part + 1) * LANES]
            write_turned(
                out_ref, down * (wide_rows - 1), part, value, 2 * widths[own_row]
            )


def merge_stats(mine, other):
    count = mine[0] + other[0]
    safe = jnp.maximum(count, 1.0)
    off = other[1] - mine[1]
    mean = mine[1] + off * (other[0] / safe)
    spread = mine[2] + other[2] + off * off * (mine[0] * other[0] / safe)
    return jnp.stack([count, mean, spread])


def exchange(array, tiles, mask, among=None):
    moves = [(i, i ^ mask) for i in range(tiles) if among is None or among(i)]
    return lax.ppermute(array, "tile", moves)


def merge_round(stats, tiles, masks, tied=()):
    parts = [stats] + [exchange(stats, tiles, mask) for mask in masks]
    if tied:
        parts[1], *tied = lax.optimization_barrier((parts[1], *tied))
    while len(parts) > 1:
        parts = [merge_stats(*parts[i : i + 2]) for i in range(0, len(parts), 2)]
    return (parts[0], *tied) if tied else parts[0]


def merge_masks(tiles):
    bits = [1 << i for i in range(tiles.bit_length() - 1)]
    pairs = [bits[i : i + 2] for i in range(0, len(bits), 2)]
    return [[p[0], p[1], p[0] ^ p[1]] if len(p) == 2 else p for p in pairs]


def shards(
    tiles,
    frames,
    latents,
    row_video,
    video_cols,
    first_gain,
    first_shift,
    conv_weight,
    conv_bias,
    second_gain,
    second_shift,
    triple_weight,
    triple_bias,
    output_weight,
    output_bias,
    upsample_weight,
    upsample_bias,
):
    row_count, frame_count, cols, channels = latents.shape
    assert frame_count == 1 and row_count == ROWS_OF_TILE and tiles % 4 == 0
    out_channels = upsample_weight.shape[-1]
    rows = row_count * tiles
    cells = row_count * cols
    padded = -(-(cols + 1) // 16) * 16
    near_rows = row_count + 2
    source = latents.reshape(row_count, cols, channels)
    tile = lax.axis_index("tile").astype(jnp.int32)
    frame = lax.axis_index("frame").astype(jnp.int32)
    info = jnp.concatenate([jnp.stack([tile, frame]), row_video, video_cols])

    def row(vector):
        return vector.reshape(1, -1)

    def shape(*dims, dtype=BF16):
        return jax.ShapeDtypeStruct(dims, dtype)

    def call(kernel, operands, out_shape, scratch=(), **kwargs):
        many = isinstance(out_shape, tuple)
        return pl.pallas_call(
            kernel,
            out_shape=out_shape,
            in_specs=[SMEM_SPEC] + [VMEM_SPEC] * len(operands),
            out_specs=(VMEM_SPEC,) * len(out_shape) if many else VMEM_SPEC,
            scratch_shapes=list(scratch),
            compiler_params=params(),
            **kwargs,
        )(info, *operands)

    outer_moves = [(i, i - 1 if i % 2 == 0 else i + 1) for i in range(tiles)]
    outer_moves = [(i, j) for i, j in outer_moves if 0 <= j < tiles]
    odd = tile % 2 == 1
    stats_shape = shape(3, SLOTS, LANES, dtype=F32)
    stats = call(
        functools.partial(stats_kernel, rows), [source], stats_shape,
        cost_estimate=cost(1.5), name="first_stats",
    )
    outer = lax.ppermute(
        jnp.where(odd, source[row_count - 1 :], source[:1]), "tile", outer_moves
    )
    inner = exchange(jnp.where(odd, source[:1], source[row_count - 1 :]), tiles, 1)
    stats, outer, inner = lax.optimization_barrier((stats, outer, inner))
    taps = min(3, frames)
    held = pl.pallas_call(
        functools.partial(hold_kernel, taps),
        out_shape=shape(3 * taps * channels, 3 * channels),
        in_specs=[HBM_SPEC],
        out_specs=VMEM_SPEC,
        scratch_shapes=[pltpu.SemaphoreType.DMA((3, 3 * taps))],
        compiler_params=pltpu.CompilerParams(vmem_limit_bytes=HOLD_VMEM_BYTES),
        cost_estimate=cost(1.5 * taps),
        name="hold",
    )(conv_weight)
    rounds = merge_masks(tiles)
    for index, masks in enumerate(reversed(rounds)):
        stats = merge_round(stats, tiles, masks)
        if index == len(rounds) - 2:
            stats, held = lax.optimization_barrier((stats, held))
    hidden, source = call(
        functools.partial(hidden_kernel, rows),
        [outer, inner, source, stats, row(first_gain), row(first_shift)],
        (shape(near_rows, padded, channels), shape(row_count, cols, channels)),
        cost_estimate=cost(1.3),
        name="hidden",
    )

    context = [hidden] + [
        lax.ppermute(hidden, "frame", [(i, i + by) for i in range(frames - by)])
        for by in range(1, taps)
    ]

    pairs = row_count // 2
    pair_shape = shape(pairs, 2 * cols, channels)
    own, stats = pl.pallas_call(
        functools.partial(conv_kernel, rows, taps),
        out_shape=(pair_shape, stats_shape),
        in_specs=[SMEM_SPEC] + [VMEM_SPEC] * (taps + 3),
        out_specs=(VMEM_SPEC, VMEM_SPEC),
        scratch_shapes=[
            pltpu.VMEM((row_count * padded, 3 * taps * channels), BF16),
            pltpu.VMEM((row_count * padded, 3 * channels), F32),
        ],
        compiler_params=params(),
        cost_estimate=cost(2.5 * taps),
        name="conv",
    )(info, *context, source, row(conv_bias), held)

    blocks = {0: own}
    neighbour = [(i, i ^ 1) for i in range(tiles)]
    if tiles == 16 and video_cols.shape[0] == 2:
        def middle(t):
            return t // 4 in (1, 2)

        stats = merge_round(stats, tiles, rounds[1])
        blocks[2] = exchange(own, tiles, 4)
        blocks[6] = exchange(own, tiles, 12, middle)
        stats, blocks[2], blocks[6] = merge_round(
            stats, tiles, rounds[0], (blocks[2], blocks[6])
        )
        stats, own_xy = lax.optimization_barrier((stats, own))
        inward = exchange(blocks[2], tiles, 12, middle)
        outward = exchange(blocks[6], tiles, 4, middle)
        other = exchange(own_xy, tiles, 1)
        blocks[1] = exchange(own_xy, tiles, 2)
        blocks[4] = jnp.where((tile // 4 == 1) | (tile // 4 == 2), inward, outward)
        passed, blocks[4] = lax.optimization_barrier((blocks[1], blocks[4]))
        blocks[5] = exchange(blocks[4], tiles, 2)
        blocks[3] = exchange(passed, tiles, 4)
        blocks[7] = exchange(passed, tiles, 12, middle)
        groups = [[0, 1, 2, 6], [4, 7, 3, 5]]
    else:
        for masks in rounds:
            stats = merge_round(stats, tiles, masks)
        other = exchange(own, tiles, 1)
        for mask in range(1, tiles // 2):
            blocks[mask] = exchange(own, tiles, 2 * mask)
        groups = [list(range(i, i + 4)) for i in range(0, tiles // 2, 4)]
    gain, shift = row(second_gain), row(second_shift)
    table_shape = shape(SLOTS, channels, dtype=F32)
    queries, constant, means, scales = call(
        functools.partial(query_kernel, rows),
        [other, stats, gain, shift, triple_weight, row(triple_bias)],
        (shape(cells, channels), shape(cells, LANES, dtype=F32), table_shape, table_shape),
        cost_estimate=cost(1.5),
        name="queries",
    )
    level_shape = shape(cells, LANES, dtype=F32)
    total_shape = shape(cells, channels, dtype=F32)
    state, keys = (), []
    for index, masks in enumerate(groups):
        last = index == len(groups) - 1
        outs = (shape(len(masks) * cells, channels),)
        outs += (shape(cells + 16, channels),) if last else (level_shape, level_shape, total_shape)
        normed, *state = call(
            functools.partial(attend_yours_kernel, rows, tuple(masks), index == 0, last),
            [means, scales, shift, queries, constant] + [blocks[m] for m in masks] + list(state),
            outs,
            cost_estimate=cost(0.9 * len(masks)),
            name="attend_yours",
        )
        keys.append(normed)
    (sent,) = state
    received = lax.ppermute(sent, "tile", neighbour)
    sent, own_late, upsample_weight = lax.optimization_barrier((sent, own, upsample_weight))
    mean, level = call(
        functools.partial(attend_mine_kernel, rows, tuple(tuple(masks) for masks in groups)),
        [own_late, means, scales, shift, triple_weight, row(triple_bias)] + keys,
        (total_shape, level_shape),
        cost_estimate=cost(6.0),
        name="attend_mine",
    )
    folded = pl.pallas_call(
        fold_kernel,
        out_shape=shape(2, 2, 2, out_channels, 2 * channels),
        in_specs=[VMEM_SPEC],
        out_specs=VMEM_SPEC,
        compiler_params=params(),
        cost_estimate=cost(0.5),
        name="fold",
    )(jnp.swapaxes(upsample_weight, 2, 3))

    rim_shape = shape(1, cols, channels)
    attended, inner, outer = call(
        functools.partial(finish_kernel, rows),
        [
            mean, level, received, own, triple_weight, row(triple_bias), output_weight,
            row(output_bias),
        ],
        (shape(row_count, cols, channels), rim_shape, rim_shape),
        cost_estimate=cost(1.4),
        name="finish",
    )
    outer = lax.ppermute(outer, "tile", outer_moves)
    inner = exchange(inner, tiles, 1)
    parts_out = -(-out_channels // LANES)
    wide_cols = -(-2 * cols // LANES) * LANES
    wide_bias = jnp.pad(row(upsample_bias), ((0, 0), (0, -out_channels % LANES)))
    middle, open_rows = call(
        functools.partial(upsample_kernel, rows),
        [attended, folded, wide_bias],
        (
            shape(2 * row_count - 2, out_channels, 2 * cols),
            shape(parts_out, 2, wide_cols, LANES, dtype=F32),
        ),
        scratch=[
            pltpu.VMEM((row_count * padded, 3 * channels), BF16),
            pltpu.VMEM((parts_out, 2 * row_count, wide_cols, LANES), F32),
        ],
        cost_estimate=cost(2.0),
        name="upsample",
    )
    decoded = call(
        functools.partial(close_kernel, rows),
        [outer, inner, middle, open_rows, folded, wide_bias],
        shape(2 * row_count, out_channels, 2 * cols),
        scratch=[
            pltpu.VMEM((2 * padded, 3 * channels), BF16),
            pltpu.VMEM((parts_out, 2, wide_cols, LANES), F32),
        ],
        cost_estimate=cost(1.0),
        name="close",
    )
    return jnp.swapaxes(decoded, 1, 2).reshape(2 * row_count, 1, 2 * cols, out_channels)


def solution(mesh):
    sizes = dict(mesh.shape)
    in_specs = (P("tile", "frame", None, None),) + (P(),) * 14
    out_specs = P("tile", "frame", None, None)
    body = functools.partial(shards, sizes["tile"], sizes["frame"])
    return jax.shard_map(body, mesh=mesh, in_specs=in_specs, out_specs=out_specs, check_vma=False)
```

```python
import functools
import math

import jax
import jax.numpy as jnp
from jax import lax
from jax.experimental import pallas as pl
from jax.experimental.pallas import tpu as pltpu
from jax.sharding import PartitionSpec as P

GROUPS = 32
EPSILON = 1e-05
MASKED = -1e30
LOWEST = -5e29
HIGHEST = lax.Precision.HIGHEST
SLOTS = 8
ROWS_OF_TILE = 4
LANES = 128
VMEM_BYTES = 24 * 1024 * 1024
HOLD_VMEM_BYTES = 46 * 1024 * 1024
F32 = jnp.float32
BF16 = jnp.bfloat16

SMEM_SPEC = pl.BlockSpec(memory_space=pltpu.SMEM)
VMEM_SPEC = pl.BlockSpec(memory_space=pltpu.VMEM)
HBM_SPEC = pl.BlockSpec(memory_space=pltpu.HBM)


def cost(microseconds):
    return pl.CostEstimate(
        flops=int(microseconds * 1.1e9), bytes_accessed=0, transcendentals=0
    )


def params():
    return pltpu.CompilerParams(vmem_limit_bytes=VMEM_BYTES)


def member_matrix(channels):
    per_group = channels // GROUPS
    group = lax.broadcasted_iota(jnp.int32, (LANES, channels), 0) * per_group
    channel = lax.broadcasted_iota(jnp.int32, (LANES, channels), 1)
    return jnp.where((channel >= group) & (channel < group + per_group), 1.0, 0.0).astype(F32)


def to_groups(values, member):
    return lax.dot_general(
        values, member, (((1,), (1,)), ((), ())), precision=HIGHEST, preferred_element_type=F32
    )


def to_channels(values, member):
    return jnp.dot(values, member, precision=HIGHEST, preferred_element_type=F32)


class Info:
    def __init__(self, ref, rows):
        self.ref, self.rows = ref, rows
        self.videos = ref.shape[0] - 1 - rows

    def tile(self):
        return self.ref[0]

    def label(self, row):
        inside = (row >= 0) & (row < self.rows)
        return jnp.where(inside, self.ref[1 + jnp.clip(row, 0, self.rows - 1)], -1)

    def width(self, label):
        return jnp.where(label >= 0, self.ref[1 + self.rows + jnp.maximum(label, 0)], 0)

    def window(self, first, count):
        labels = [self.label(first + r) for r in range(count)]
        return labels, [self.width(label) for label in labels]


def pick(table, label, videos):
    chosen = table[0:1]
    for video in range(1, videos):
        chosen = jnp.where(label == video, table[video : video + 1], chosen)
    return chosen


def norm_tables(stats_ref, gain_ref):
    member = member_matrix(gain_ref.shape[1])
    counts = jnp.maximum(stats_ref[0], 1.0)
    scale = lax.rsqrt(stats_ref[2] / counts + EPSILON)
    return to_channels(stats_ref[1], member), to_channels(scale, member) * gain_ref[...]


def write_stats(out_ref, rows, labels, widths, videos, channels):
    member = member_matrix(channels)
    per_group = channels // GROUPS
    cols = rows[0].shape[0]
    slot = lax.broadcasted_iota(jnp.int32, (SLOTS, 1), 0)
    column = lax.broadcasted_iota(jnp.int32, (cols, 1), 0)
    sums = jnp.zeros((SLOTS, channels), F32)
    counts = jnp.zeros((SLOTS, 1), F32)
    for index, row in enumerate(rows):
        sums = jnp.where(slot == index, jnp.sum(row, axis=0, keepdims=True), sums)
        counts = jnp.where(slot == index, (widths[index] * per_group).astype(F32), counts)
    means = to_groups(sums, member) / jnp.maximum(counts, 1.0)
    means_wide = to_channels(means, member)
    squares = jnp.zeros((SLOTS, channels), F32)
    for index, row in enumerate(rows):
        centered = jnp.where(column < widths[index], row - means_wide[index : index + 1], 0.0)
        squares = jnp.where(
            slot == index, jnp.sum(centered * centered, axis=0, keepdims=True), squares
        )
    spreads = to_groups(squares, member)
    out_ref[...] = jnp.zeros(out_ref.shape, F32)
    for video in range(videos):
        total = jnp.zeros((1, LANES), F32)
        count = jnp.zeros((1, LANES), F32)
        for index in range(len(rows)):
            mine = labels[index] == video
            row_count = counts[index : index + 1]
            total = total + jnp.where(mine, means[index : index + 1] * row_count, 0.0)
            count = count + jnp.where(mine, row_count, 0.0)
        mean = total / jnp.maximum(count, 1.0)
        spread = jnp.zeros((1, LANES), F32)
        for index in range(len(rows)):
            off = means[index : index + 1] - mean
            part = spreads[index : index + 1] + counts[index : index + 1] * off * off
            spread = spread + jnp.where(labels[index] == video, part, 0.0)
        out_ref[0, video : video + 1, :] = count
        out_ref[1, video : video + 1, :] = mean
        out_ref[2, video : video + 1, :] = spread


def build_columns(columns_ref, row_refs):
    padded = columns_ref.shape[0] // len(row_refs)
    for index, row in enumerate(row_refs):
        cells = row().astype(F32)
        count, channels = cells.shape
        cells = jnp.concatenate([cells, jnp.zeros((padded - count, channels), F32)], axis=0)
        start = index * padded
        columns_ref[start : start + padded, 0:channels] = pltpu.roll(cells, 1, 0).astype(BF16)
        columns_ref[start : start + padded, channels : 2 * channels] = cells.astype(BF16)
        columns_ref[start : start + padded, 2 * channels : 3 * channels] = pltpu.roll(
            cells, padded - 1, 0
        ).astype(BF16)


def stats_kernel(rows, info_ref, latents_ref, out_ref):
    info = Info(info_ref, rows)
    row_count, cols, channels = latents_ref.shape
    labels, widths = info.window(info.tile() * row_count, row_count)
    column = lax.broadcasted_iota(jnp.int32, (cols, 1), 0)
    cells = [
        jnp.where(column < widths[r], latents_ref[r].astype(F32), 0.0) for r in range(row_count)
    ]
    write_stats(out_ref, cells, labels, widths, info.videos, channels)


def rims(info, outer_ref, inner_ref):
    odd = lax.rem(info.tile(), 2) == 1
    inner, outer = inner_ref[0].astype(F32), outer_ref[0].astype(F32)
    return jnp.where(odd, inner, outer), jnp.where(odd, outer, inner)


def hidden_kernel(
    rows, info_ref, outer_ref, inner_ref, latents_ref, stats_ref, gain_ref, shift_ref, out_ref,
    source_ref,
):
    info = Info(info_ref, rows)
    row_count, cols, _ = latents_ref.shape
    labels, widths = info.window(info.tile() * row_count - 1, row_count + 2)
    means, scales = norm_tables(stats_ref, gain_ref)
    column = lax.broadcasted_iota(jnp.int32, (cols, 1), 0)
    above, below = rims(info, outer_ref, inner_ref)
    sources = [above] + [latents_ref[r].astype(F32) for r in range(row_count)] + [below]
    for r, source in enumerate(sources):
        mean = pick(means, labels[r], info.videos)
        scale = pick(scales, labels[r], info.videos)
        normed = (source - mean) * scale + shift_ref[...]
        active = normed / (1.0 + jnp.exp(-normed))
        active = jnp.where(column < widths[r], active, 0.0)
        rest = jnp.zeros((out_ref.shape[1] - cols, active.shape[1]), F32)
        out_ref[r] = jnp.concatenate([active, rest], axis=0).astype(BF16)
    source_ref[...] = latents_ref[...]


def hold_kernel(taps, weight_ref, held_ref, sems):
    channels = weight_ref.shape[-1]
    copies = [
        pltpu.make_async_copy(
            weight_ref.at[2 - depth // 3, depth % 3, side],
            held_ref.at[pl.ds(depth * channels, channels), pl.ds(side * channels, channels)],
            sems.at[side, depth],
        )
        for side in range(3)
        for depth in range(3 * taps)
    ]
    for copy in copies:
        copy.start()
    for copy in copies:
        copy.wait()


def row_taps(info, hidden_refs, inputs_ref):
    near_rows, padded, channels = hidden_refs[0].shape
    row_count = near_rows - 2
    labels, _ = info.window(info.tile() * row_count - 1, near_rows)
    for back, hidden_ref in enumerate(hidden_refs):
        for tap in range(3):
            lanes = slice((3 * back + tap) * channels, (3 * back + tap + 1) * channels)
            for r in range(row_count):
                block = hidden_ref[r + tap]
                if tap != 1:
                    same = labels[r + tap] == labels[r + 1]
                    block = jnp.where(same, block, jnp.zeros_like(block))
                inputs_ref[r * padded : (r + 1) * padded, lanes] = block


def own_conv_kernel(rows, info_ref, hidden_ref, held_ref, product_ref, inputs_ref):
    row_taps(Info(info_ref, rows), [hidden_ref], inputs_ref)
    depth = inputs_ref.shape[1]
    product_ref[...] = jnp.dot(
        inputs_ref[...], held_ref[0:depth, :], preferred_element_type=F32
    )


def conv_kernel(rows, taps, info_ref, *rest):
    hidden_refs, rest = rest[: taps - 1], rest[taps - 1 :]
    product_ref, latents_ref, bias_ref, held_ref, own_ref, stats_ref, *inputs_refs = rest
    row_count, cols, channels = latents_ref.shape
    info = Info(info_ref, rows)
    padded = product_ref.shape[0] // row_count
    labels, widths = info.window(info.tile() * row_count - 1, row_count + 2)
    product = product_ref[...]
    if hidden_refs:
        (inputs_ref,) = inputs_refs
        row_taps(info, hidden_refs, inputs_ref)
        product = product + jnp.dot(
            inputs_ref[...], held_ref[3 * channels :, :], preferred_element_type=F32
        )
    column = lax.broadcasted_iota(jnp.int32, (cols, 1), 0)
    cells = []
    for r in range(row_count):
        lines = slice(r * padded, (r + 1) * padded)
        branch = pltpu.roll(product[lines, 0:channels], 1, 0)
        branch = branch + product[lines, channels : 2 * channels]
        branch = branch + pltpu.roll(product[lines, 2 * channels :], padded - 1, 0)
        value = latents_ref[r].astype(F32) + branch[:cols] + bias_ref[...]
        value = jnp.where(column < widths[r + 1], value, 0.0).astype(BF16)
        cells.append(value.astype(F32))
    for pair in range(row_count // 2):
        own_ref[pair] = jnp.concatenate(cells[2 * pair : 2 * pair + 2], axis=0).astype(BF16)
    write_stats(stats_ref, cells, labels[1:-1], widths[1:-1], info.videos, channels)


def split_rows(pairs_ref):
    cols = pairs_ref.shape[1] // 2
    cells = []
    for pair in range(pairs_ref.shape[0]):
        both = pairs_ref[pair].astype(F32)
        cells += [both[:cols], both[cols:]]
    return cells


def turned_queries(info, tile, pairs_ref, means, scales, shift_ref, weight_ref, bias_ref):
    pairs, double, channels = pairs_ref.shape
    cols = double // 2
    column = lax.broadcasted_iota(jnp.int32, (cols, 1), 0)
    labels, widths = info.window(tile * 2 * pairs, 2 * pairs)
    cells = []
    for r, values in enumerate(split_rows(pairs_ref)):
        mean = pick(means, labels[r], info.videos)
        scale = pick(scales, labels[r], info.videos)
        normed = (values - mean) * scale + shift_ref[...]
        cells.append(jnp.where(column < widths[r], normed, 0.0))
    cells = jnp.concatenate(cells, axis=0).astype(BF16)
    queries = (
        jnp.dot(cells, weight_ref[:, 0:channels], preferred_element_type=F32)
        + bias_ref[:, 0:channels]
    ).astype(BF16)
    factor = channels ** (-0.5) * math.log2(math.e)
    turned = lax.dot_general(
        queries, weight_ref[:, channels : 2 * channels], (((1,), (1,)), ((), ())),
        preferred_element_type=F32,
    )
    constant = jnp.sum(
        queries.astype(F32) * bias_ref[:, channels : 2 * channels], axis=1, keepdims=True
    )
    return (turned * factor).astype(BF16), constant * factor


def query_kernel(
    rows, info_ref, other_ref, stats_ref, gain_ref, shift_ref, weight_ref, bias_ref, queries_ref,
    constant_ref, means_ref, scales_ref,
):
    info = Info(info_ref, rows)
    means, scales = norm_tables(stats_ref, gain_ref)
    means_ref[...] = means
    scales_ref[...] = scales
    queries, constant = turned_queries(
        info, info.tile() ^ 1, other_ref, means, scales, shift_ref, weight_ref, bias_ref
    )
    queries_ref[...] = queries
    constant_ref[...] = jnp.broadcast_to(constant, constant_ref.shape)


def key_codes(info, masks, span, cols):
    row_count = span // cols
    position = lax.broadcasted_iota(jnp.int32, (1, len(masks) * span), 1)
    codes = jnp.full((1, len(masks) * span), -2.0, F32)
    for index, mask in enumerate(masks):
        near, widths = info.window((info.tile() ^ (2 * mask)) * row_count, row_count)
        for r in range(row_count):
            start = index * span + r * cols
            inside = (position >= start) & (position < start + widths[r])
            codes = jnp.where(inside, near[r].astype(F32), codes)
    return codes


def query_codes(info, tile, span, cols):
    row_count = span // cols
    labels, _ = info.window(tile * row_count, row_count)
    return jnp.concatenate(
        [jnp.zeros((cols, 1), F32) + label.astype(F32) for label in labels], axis=0
    )


def scores_of(queries, keys, codes, query_code):
    scores = lax.dot_general(
        queries, keys, (((1,), (1,)), ((), ())), preferred_element_type=F32
    )
    return jnp.where(codes == query_code, scores, MASKED)


def mean_and_level(peak, denominator, total):
    some = denominator > 0.0
    safe = jnp.where(some, denominator, 1.0)
    return total / safe, jnp.where(some, peak + jnp.log2(safe), LOWEST)


def attend_yours_kernel(rows, masks, first, last, info_ref, *rest):
    means_ref, scales_ref, shift_ref, queries_ref, constant_ref, *rest = rest
    block_refs, rest = rest[: len(masks)], rest[len(masks) :]
    if not first:
        old_peak_ref, old_sum_ref, old_total_ref, *rest = rest
    keys_ref, *out_refs = rest
    info = Info(info_ref, rows)
    span, channels = queries_ref.shape
    pairs, double, _ = block_refs[0].shape
    cols = double // 2
    row_count = 2 * pairs
    tile = info.tile()
    means, scales = means_ref[...], scales_ref[...]
    for index, (mask, block_ref) in enumerate(zip(masks, block_refs)):
        near, _ = info.window((tile ^ (2 * mask)) * row_count, row_count)
        for pair in range(pairs):
            both = block_ref[pair].astype(F32)
            halves = []
            for half in range(2):
                label = near[2 * pair + half]
                mean = pick(means, label, info.videos)
                scale = pick(scales, label, info.videos)
                values = both[half * cols : (half + 1) * cols]
                halves.append((values - mean) * scale + shift_ref[...])
            start = index * span + pair * double
            keys_ref[start : start + double, :] = jnp.concatenate(halves, axis=0).astype(BF16)
    constant = constant_ref[:, 0:1]
    scores = scores_of(
        queries_ref[...], keys_ref[...], key_codes(info, masks, span, cols),
        query_codes(info, tile ^ 1, span, cols),
    )
    peak = jnp.maximum(LOWEST, jnp.max(scores, axis=1, keepdims=True) + constant)
    if not first:
        largest = old_peak_ref[:, 0:1]
        peak = jnp.maximum(largest, peak)
    weights = jnp.exp2(scores - (peak - constant))
    denominator = jnp.sum(weights, axis=1, keepdims=True)
    total = jnp.dot(weights.astype(BF16), keys_ref[...], preferred_element_type=F32)
    if not first:
        factor = jnp.exp2(largest - peak)
        denominator = old_sum_ref[:, 0:1] * factor + denominator
        total = old_total_ref[...] * factor + total
    if not last:
        peak_ref, sum_ref, total_ref = out_refs
        peak_ref[...] = jnp.broadcast_to(peak, peak_ref.shape)
        sum_ref[...] = jnp.broadcast_to(denominator, sum_ref.shape)
        total_ref[...] = total
        return
    (sent_ref,) = out_refs
    mean, level = mean_and_level(peak, denominator, total)
    sent_ref[0:span, :] = mean.astype(BF16)
    slots = sent_ref.shape[0] - span
    slot = lax.broadcasted_iota(jnp.int32, (slots, 1), 0)
    packed = jnp.zeros((slots, LANES), F32)
    for r in range(row_count):
        left = level[r * cols : (r + 1) * cols]
        left = jnp.sum(jnp.where(diagonal(cols), left, 0.0), axis=0, keepdims=True)
        for part in range(3):
            rounded = left.astype(BF16).astype(F32)
            packed = jnp.where(slot == 3 * r + part, rounded, packed)
            left = left - rounded
    sent_ref[span:, 0:LANES] = packed.astype(BF16)
    sent_ref[span:, LANES:] = jnp.zeros((slots, channels - LANES), BF16)


def attend_mine_kernel(
    rows, groups, info_ref, own_ref, means_ref, scales_ref, shift_ref, weight_ref, bias_ref, *rest
):
    key_refs, (mean_ref, level_ref) = rest[: len(groups)], rest[len(groups) :]
    info = Info(info_ref, rows)
    span = mean_ref.shape[0]
    queries, constant = turned_queries(
        info, info.tile(), own_ref, means_ref[...], scales_ref[...], shift_ref, weight_ref,
        bias_ref,
    )
    cols = span // ROWS_OF_TILE
    query_code = query_codes(info, info.tile(), span, cols)
    peak = jnp.full((span, 1), LOWEST, F32)
    scores = []
    for masks, key_ref in zip(groups, key_refs):
        codes = key_codes(info, masks, span, cols)
        scores.append(scores_of(queries, key_ref[...], codes, query_code))
        peak = jnp.maximum(peak, jnp.max(scores[-1], axis=1, keepdims=True) + constant)
    denominator, total = 0.0, 0.0
    for part, key_ref in zip(scores, key_refs):
        weights = jnp.exp2(part - (peak - constant))
        denominator = denominator + jnp.sum(weights, axis=1, keepdims=True)
        total = total + jnp.dot(
            weights.astype(BF16), key_ref[...], preferred_element_type=F32
        )
    mean, level = mean_and_level(peak, denominator, total)
    mean_ref[...] = mean
    level_ref[...] = jnp.broadcast_to(level, level_ref.shape)


def diagonal(cols):
    return lax.broadcasted_iota(jnp.int32, (cols, LANES), 0) == lax.broadcasted_iota(
        jnp.int32, (cols, LANES), 1
    )


def finish_kernel(
    rows, info_ref, mean_ref, level_ref, received_ref, own_ref, triple_ref, triple_bias_ref,
    output_ref, output_bias_ref, out_ref, inner_ref, outer_ref,
):
    info = Info(info_ref, rows)
    row_count, cols, channels = out_ref.shape
    span = row_count * cols
    _, widths = info.window(info.tile() * row_count, row_count)
    received = received_ref[0:span, :].astype(F32)
    levels = received_ref[span:, 0:LANES].astype(F32)
    yours = []
    for r in range(row_count):
        level = levels[3 * r : 3 * r + 1] + levels[3 * r + 1 : 3 * r + 2]
        level = level + levels[3 * r + 2 : 3 * r + 3]
        yours.append(jnp.sum(jnp.where(diagonal(cols), level, 0.0), axis=1, keepdims=True))
    yours = jnp.concatenate(yours, axis=0)
    mine = level_ref[:, 0:1]
    peak = jnp.maximum(mine, yours)
    weight, other_weight = jnp.exp2(mine - peak), jnp.exp2(yours - peak)
    share = weight / (weight + other_weight)
    mean_cell = (mean_ref[...] * share + received * (1.0 - share)).astype(BF16)
    mixed = (
        jnp.dot(mean_cell, triple_ref[:, 2 * channels :], preferred_element_type=F32)
        + triple_bias_ref[:, 2 * channels :]
    ).astype(BF16)
    attended = jnp.dot(mixed, output_ref[...], preferred_element_type=F32) + output_bias_ref[...]
    column = lax.broadcasted_iota(jnp.int32, (cols, 1), 0)
    for r, before in enumerate(split_rows(own_ref)):
        value = before + attended[r * cols : (r + 1) * cols]
        value = jnp.where(column < widths[r], value, 0.0)
        out_ref[r] = value.astype(BF16)
        if r == 0:
            top = value
    odd = lax.rem(info.tile(), 2) == 1
    inner_ref[0] = jnp.where(odd, top, value).astype(BF16)
    outer_ref[0] = jnp.where(odd, value, top).astype(BF16)


def fold_kernel(weight_ref, out_ref):
    channels = weight_ref.shape[-1]
    wide = [[weight_ref[a, b].astype(F32) for b in range(3)] for a in range(3)]

    def both(upper, lower):
        return [x + y for x, y in zip(upper, lower)]

    phases = [[wide[0], both(wide[1], wide[2])], [both(wide[0], wide[1]), wide[2]]]
    for down in range(2):
        for tap in range(2):
            left, middle, right = phases[down][tap]
            out_ref[down, tap, 0, :, 0:channels] = left.astype(BF16)
            out_ref[down, tap, 0, :, channels:] = (middle + right).astype(BF16)
            out_ref[down, tap, 1, :, 0:channels] = (left + middle).astype(BF16)
            out_ref[down, tap, 1, :, channels:] = right.astype(BF16)


def spread_columns(wide_ref, value, row, right):
    cols, channels = value.shape
    for part in range(wide_ref.shape[0]):
        lo, hi = part * LANES, min((part + 1) * LANES, channels)
        piece = value[:, lo:hi]
        if hi - lo < LANES:
            piece = jnp.concatenate([piece, jnp.zeros((cols, LANES - hi + lo), F32)], axis=1)
        wide_ref[part, row, pl.ds(right, cols, 2), :] = piece


def write_turned(out_ref, row, part, value, width):
    channels, cols = out_ref.shape[1:]
    lo, hi = part * LANES, min((part + 1) * LANES, channels)
    turned = value.T[0 : hi - lo, 0:cols]
    column = lax.broadcasted_iota(jnp.int32, (1, cols), 1)
    out_ref[row, lo:hi, :] = jnp.where(column < width, turned, 0.0).astype(BF16)


def phase_product(columns, weight):
    return lax.dot_general(
        columns, weight, (((1,), (1,)), ((), ())), preferred_element_type=F32
    )


def upsample_kernel(
    rows, info_ref, own_ref, weight_ref, bias_ref, out_ref, open_ref, columns_ref, wide_ref
):
    info = Info(info_ref, rows)
    row_count, cols, channels = own_ref.shape
    padded = columns_ref.shape[0] // row_count
    parts_out = wide_ref.shape[0]
    labels, widths = info.window(info.tile() * row_count, row_count)
    build_columns(
        columns_ref, [functools.partial(own_ref.__getitem__, r) for r in range(row_count)]
    )
    inner_rows = (row_count - 1) * padded
    for down in range(2):
        for right in range(2):
            lanes = slice(right * channels, (right + 2) * channels)
            same = phase_product(columns_ref[:, lanes], weight_ref[down, 1 - down, right])
            start = down * padded
            rim = phase_product(
                columns_ref[start : start + inner_rows, lanes], weight_ref[down, down, right]
            )
            for r in range(row_count):
                value = same[r * padded : r * padded + cols]
                near = r - 1 + 2 * down
                if 0 <= near < row_count:
                    lo = (near - down) * padded
                    value = value + jnp.where(
                        labels[near] == labels[r], rim[lo : lo + cols], 0.0
                    )
                spread_columns(wide_ref, value, 2 * r + down, right)
    for part in range(parts_out):
        open_ref[part, 0] = wide_ref[part, 0]
        open_ref[part, 1] = wide_ref[part, 2 * row_count - 1]
    for r in range(1, 2 * row_count - 1):
        for part in range(parts_out):
            value = wide_ref[part, r] + bias_ref[:, part * LANES : (part + 1) * LANES]
            write_turned(out_ref, r - 1, part, value, 2 * widths[r // 2])


def close_kernel(
    rows, info_ref, outer_ref, inner_ref, middle_ref, open_ref, weight_ref, bias_ref, out_ref,
    columns_ref, wide_ref,
):
    info = Info(info_ref, rows)
    wide_rows, _, wide_cols = out_ref.shape
    row_count, cols = wide_rows // 2, wide_cols // 2
    channels = outer_ref.shape[-1]
    padded = columns_ref.shape[0] // 2
    labels, widths = info.window(info.tile() * row_count - 1, row_count + 2)
    above, below = rims(info, outer_ref, inner_ref)
    build_columns(columns_ref, [lambda: above, lambda: below])
    for down in range(2):
        for right in range(2):
            lanes = slice(right * channels, (right + 2) * channels)
            rim = phase_product(
                columns_ref[down * padded : (down + 1) * padded, lanes],
                weight_ref[down, down, right],
            )
            spread_columns(wide_ref, rim[:cols], down, right)
    out_ref[1 : wide_rows - 1] = middle_ref[...]
    for down in range(2):
        rim_row, own_row = (row_count + 1, row_count) if down else (0, 1)
        for part in range(wide_ref.shape[0]):
            rim = jnp.where(labels[rim_row] == labels[own_row], wide_ref[part, down], 0.0)
            value = open_ref[part, down] + rim + bias_ref[:, part * LANES : (part + 1) * LANES]
            write_turned(
                out_ref, down * (wide_rows - 1), part, value, 2 * widths[own_row]
            )


def merge_stats(mine, other):
    count = mine[0] + other[0]
    safe = jnp.maximum(count, 1.0)
    off = other[1] - mine[1]
    mean = mine[1] + off * (other[0] / safe)
    spread = mine[2] + other[2] + off * off * (mine[0] * other[0] / safe)
    return jnp.stack([count, mean, spread])


def exchange(array, tiles, mask, among=None):
    moves = [(i, i ^ mask) for i in range(tiles) if among is None or among(i)]
    return lax.ppermute(array, "tile", moves)


def merge_round(stats, tiles, masks, tied=()):
    parts = [stats] + [exchange(stats, tiles, mask) for mask in masks]
    if tied:
        parts[1], *tied = lax.optimization_barrier((parts[1], *tied))
    while len(parts) > 1:
        parts = [merge_stats(*parts[i : i + 2]) for i in range(0, len(parts), 2)]
    return (parts[0], *tied) if tied else parts[0]


def merge_masks(tiles):
    bits = [1 << i for i in range(tiles.bit_length() - 1)]
    pairs = [bits[i : i + 2] for i in range(0, len(bits), 2)]
    return [[p[0], p[1], p[0] ^ p[1]] if len(p) == 2 else p for p in pairs]


def shards(
    tiles,
    frames,
    latents,
    row_video,
    video_cols,
    first_gain,
    first_shift,
    conv_weight,
    conv_bias,
    second_gain,
    second_shift,
    triple_weight,
    triple_bias,
    output_weight,
    output_bias,
    upsample_weight,
    upsample_bias,
):
    row_count, frame_count, cols, channels = latents.shape
    assert frame_count == 1 and row_count == ROWS_OF_TILE and tiles % 4 == 0
    out_channels = upsample_weight.shape[-1]
    rows = row_count * tiles
    cells = row_count * cols
    padded = -(-(cols + 1) // 16) * 16
    near_rows = row_count + 2
    source = latents.reshape(row_count, cols, channels)
    tile = lax.axis_index("tile").astype(jnp.int32)
    info = jnp.concatenate([jnp.reshape(tile, (1,)), row_video, video_cols])

    def row(vector):
        return vector.reshape(1, -1)

    def shape(*dims, dtype=BF16):
        return jax.ShapeDtypeStruct(dims, dtype)

    def call(kernel, operands, out_shape, scratch=(), **kwargs):
        many = isinstance(out_shape, tuple)
        return pl.pallas_call(
            kernel,
            out_shape=out_shape,
            in_specs=[SMEM_SPEC] + [VMEM_SPEC] * len(operands),
            out_specs=(VMEM_SPEC,) * len(out_shape) if many else VMEM_SPEC,
            scratch_shapes=list(scratch),
            compiler_params=params(),
            **kwargs,
        )(info, *operands)

    outer_moves = [(i, i - 1 if i % 2 == 0 else i + 1) for i in range(tiles)]
    outer_moves = [(i, j) for i, j in outer_moves if 0 <= j < tiles]
    odd = tile % 2 == 1
    stats_shape = shape(3, SLOTS, LANES, dtype=F32)
    stats = call(
        functools.partial(stats_kernel, rows), [source], stats_shape,
        cost_estimate=cost(1.5), name="first_stats",
    )
    outer = lax.ppermute(
        jnp.where(odd, source[row_count - 1 :], source[:1]), "tile", outer_moves
    )
    inner = exchange(jnp.where(odd, source[:1], source[row_count - 1 :]), tiles, 1)
    stats, outer, inner = lax.optimization_barrier((stats, outer, inner))
    taps = min(3, frames)
    held = pl.pallas_call(
        functools.partial(hold_kernel, taps),
        out_shape=shape(3 * taps * channels, 3 * channels),
        in_specs=[HBM_SPEC],
        out_specs=VMEM_SPEC,
        scratch_shapes=[pltpu.SemaphoreType.DMA((3, 3 * taps))],
        compiler_params=pltpu.CompilerParams(vmem_limit_bytes=HOLD_VMEM_BYTES),
        cost_estimate=cost(1.5 * taps),
        name="hold",
    )(conv_weight)
    rounds = merge_masks(tiles)
    for index, masks in enumerate(reversed(rounds)):
        stats = merge_round(stats, tiles, masks)
        if index == len(rounds) - 2:
            stats, held = lax.optimization_barrier((stats, held))
    hidden, source = call(
        functools.partial(hidden_kernel, rows),
        [outer, inner, source, stats, row(first_gain), row(first_shift)],
        (shape(near_rows, padded, channels), shape(row_count, cols, channels)),
        cost_estimate=cost(1.3),
        name="hidden",
    )

    earlier = [
        lax.ppermute(hidden, "frame", [(i, i + by) for i in range(frames - by)])
        for by in range(1, taps)
    ]
    pairs = row_count // 2
    pair_shape = shape(pairs, 2 * cols, channels)
    product = call(
        functools.partial(own_conv_kernel, rows),
        [hidden, held],
        shape(row_count * padded, 3 * channels, dtype=F32),
        scratch=[pltpu.VMEM((row_count * padded, 3 * channels), BF16)],
        cost_estimate=cost(2.2),
        name="own_conv",
    )
    scratch = [pltpu.VMEM((row_count * padded, 3 * (taps - 1) * channels), BF16)]
    own, stats = call(
        functools.partial(conv_kernel, rows, taps),
        earlier + [product, source, row(conv_bias), held],
        (pair_shape, stats_shape),
        scratch=scratch if taps > 1 else [],
        cost_estimate=cost(1.5 + 2.0 * (taps - 1)),
        name="conv",
    )

    blocks = {0: own}
    neighbour = [(i, i ^ 1) for i in range(tiles)]
    if tiles == 16 and video_cols.shape[0] == 2:
        def middle(t):
            return t // 4 in (1, 2)

        stats = merge_round(stats, tiles, rounds[1])
        blocks[2] = exchange(own, tiles, 4)
        blocks[6] = exchange(own, tiles, 12, middle)
        stats, blocks[2], blocks[6] = merge_round(
            stats, tiles, rounds[0], (blocks[2], blocks[6])
        )
        stats, own_xy = lax.optimization_barrier((stats, own))
        inward = exchange(blocks[2], tiles, 12, middle)
        outward = exchange(blocks[6], tiles, 4, middle)
        other = exchange(own_xy, tiles, 1)
        blocks[1] = exchange(own_xy, tiles, 2)
        blocks[4] = jnp.where((tile // 4 == 1) | (tile // 4 == 2), inward, outward)
        passed, blocks[4] = lax.optimization_barrier((blocks[1], blocks[4]))
        blocks[5] = exchange(blocks[4], tiles, 2)
        blocks[3] = exchange(passed, tiles, 4)
        blocks[7] = exchange(passed, tiles, 12, middle)
        groups = [[0, 1, 2, 6], [4, 7, 3, 5]]
    else:
        for masks in rounds:
            stats = merge_round(stats, tiles, masks)
        other = exchange(own, tiles, 1)
        for mask in range(1, tiles // 2):
            blocks[mask] = exchange(own, tiles, 2 * mask)
        groups = [list(range(i, i + 4)) for i in range(0, tiles // 2, 4)]
    gain, shift = row(second_gain), row(second_shift)
    table_shape = shape(SLOTS, channels, dtype=F32)
    queries, constant, means, scales = call(
        functools.partial(query_kernel, rows),
        [other, stats, gain, shift, triple_weight, row(triple_bias)],
        (shape(cells, channels), shape(cells, LANES, dtype=F32), table_shape, table_shape),
        cost_estimate=cost(1.5),
        name="queries",
    )
    level_shape = shape(cells, LANES, dtype=F32)
    total_shape = shape(cells, channels, dtype=F32)
    state, keys = (), []
    for index, masks in enumerate(groups):
        last = index == len(groups) - 1
        outs = (shape(len(masks) * cells, channels),)
        outs += (shape(cells + 16, channels),) if last else (level_shape, level_shape, total_shape)
        normed, *state = call(
            functools.partial(attend_yours_kernel, rows, tuple(masks), index == 0, last),
            [means, scales, shift, queries, constant] + [blocks[m] for m in masks] + list(state),
            outs,
            cost_estimate=cost(0.9 * len(masks)),
            name="attend_yours",
        )
        keys.append(normed)
    (sent,) = state
    received = lax.ppermute(sent, "tile", neighbour)
    sent, own_late, upsample_weight = lax.optimization_barrier((sent, own, upsample_weight))
    mean, level = call(
        functools.partial(attend_mine_kernel, rows, tuple(tuple(masks) for masks in groups)),
        [own_late, means, scales, shift, triple_weight, row(triple_bias)] + keys,
        (total_shape, level_shape),
        cost_estimate=cost(6.0),
        name="attend_mine",
    )
    folded = pl.pallas_call(
        fold_kernel,
        out_shape=shape(2, 2, 2, out_channels, 2 * channels),
        in_specs=[VMEM_SPEC],
        out_specs=VMEM_SPEC,
        compiler_params=params(),
        cost_estimate=cost(0.5),
        name="fold",
    )(jnp.swapaxes(upsample_weight, 2, 3))

    rim_shape = shape(1, cols, channels)
    attended, inner, outer = call(
        functools.partial(finish_kernel, rows),
        [
            mean, level, received, own, triple_weight, row(triple_bias), output_weight,
            row(output_bias),
        ],
        (shape(row_count, cols, channels), rim_shape, rim_shape),
        cost_estimate=cost(1.4),
        name="finish",
    )
    outer = lax.ppermute(outer, "tile", outer_moves)
    inner = exchange(inner, tiles, 1)
    parts_out = -(-out_channels // LANES)
    wide_cols = -(-2 * cols // LANES) * LANES
    wide_bias = jnp.pad(row(upsample_bias), ((0, 0), (0, -out_channels % LANES)))
    middle, open_rows = call(
        functools.partial(upsample_kernel, rows),
        [attended, folded, wide_bias],
        (
            shape(2 * row_count - 2, out_channels, 2 * cols),
            shape(parts_out, 2, wide_cols, LANES, dtype=F32),
        ),
        scratch=[
            pltpu.VMEM((row_count * padded, 3 * channels), BF16),
            pltpu.VMEM((parts_out, 2 * row_count, wide_cols, LANES), F32),
        ],
        cost_estimate=cost(2.0),
        name="upsample",
    )
    decoded = call(
        functools.partial(close_kernel, rows),
        [outer, inner, middle, open_rows, folded, wide_bias],
        shape(2 * row_count, out_channels, 2 * cols),
        scratch=[
            pltpu.VMEM((2 * padded, 3 * channels), BF16),
            pltpu.VMEM((parts_out, 2, wide_cols, LANES), F32),
        ],
        cost_estimate=cost(1.0),
        name="close",
    )
    return jnp.swapaxes(decoded, 1, 2).reshape(2 * row_count, 1, 2 * cols, out_channels)


def solution(mesh):
    sizes = dict(mesh.shape)
    in_specs = (P("tile", "frame", None, None),) + (P(),) * 14
    out_specs = P("tile", "frame", None, None)
    body = functools.partial(shards, sizes["tile"], sizes["frame"])
    return jax.shard_map(body, mesh=mesh, in_specs=in_specs, out_specs=out_specs, check_vma=False)
```

```python
import functools
import math

import jax
import jax.numpy as jnp
from jax import lax
from jax.experimental import pallas as pl
from jax.experimental.pallas import tpu as pltpu
from jax.sharding import PartitionSpec as P

GROUPS = 32
EPSILON = 1e-05
MASKED = -1e30
LOWEST = -5e29
HIGHEST = lax.Precision.HIGHEST
SLOTS = 8
ROWS_OF_TILE = 4
LANES = 128
VMEM_BYTES = 24 * 1024 * 1024
HOLD_VMEM_BYTES = 46 * 1024 * 1024
F32 = jnp.float32
BF16 = jnp.bfloat16

SMEM_SPEC = pl.BlockSpec(memory_space=pltpu.SMEM)
VMEM_SPEC = pl.BlockSpec(memory_space=pltpu.VMEM)
HBM_SPEC = pl.BlockSpec(memory_space=pltpu.HBM)


def cost(microseconds):
    return pl.CostEstimate(
        flops=int(microseconds * 1.1e9), bytes_accessed=0, transcendentals=0
    )


def params():
    return pltpu.CompilerParams(vmem_limit_bytes=VMEM_BYTES)


def member_matrix(channels):
    per_group = channels // GROUPS
    group = lax.broadcasted_iota(jnp.int32, (LANES, channels), 0) * per_group
    channel = lax.broadcasted_iota(jnp.int32, (LANES, channels), 1)
    return jnp.where((channel >= group) & (channel < group + per_group), 1.0, 0.0).astype(F32)


def to_groups(values, member):
    return lax.dot_general(
        values, member, (((1,), (1,)), ((), ())), precision=HIGHEST, preferred_element_type=F32
    )


def to_channels(values, member):
    return jnp.dot(values, member, precision=HIGHEST, preferred_element_type=F32)


class Info:
    def __init__(self, ref, rows):
        self.ref, self.rows = ref, rows
        self.videos = ref.shape[0] - 1 - rows

    def tile(self):
        return self.ref[0]

    def label(self, row):
        inside = (row >= 0) & (row < self.rows)
        return jnp.where(inside, self.ref[1 + jnp.clip(row, 0, self.rows - 1)], -1)

    def width(self, label):
        return jnp.where(label >= 0, self.ref[1 + self.rows + jnp.maximum(label, 0)], 0)

    def window(self, first, count):
        labels = [self.label(first + r) for r in range(count)]
        return labels, [self.width(label) for label in labels]


def pick(table, label, videos):
    chosen = table[0:1]
    for video in range(1, videos):
        chosen = jnp.where(label == video, table[video : video + 1], chosen)
    return chosen


def norm_tables(stats_ref, gain_ref):
    member = member_matrix(gain_ref.shape[1])
    counts = jnp.maximum(stats_ref[0], 1.0)
    scale = lax.rsqrt(stats_ref[2] / counts + EPSILON)
    return to_channels(stats_ref[1], member), to_channels(scale, member) * gain_ref[...]


def write_stats(out_ref, rows, labels, widths, videos, channels):
    member = member_matrix(channels)
    per_group = channels // GROUPS
    cols = rows[0].shape[0]
    slot = lax.broadcasted_iota(jnp.int32, (SLOTS, 1), 0)
    column = lax.broadcasted_iota(jnp.int32, (cols, 1), 0)
    sums = jnp.zeros((SLOTS, channels), F32)
    counts = jnp.zeros((SLOTS, 1), F32)
    for index, row in enumerate(rows):
        sums = jnp.where(slot == index, jnp.sum(row, axis=0, keepdims=True), sums)
        counts = jnp.where(slot == index, (widths[index] * per_group).astype(F32), counts)
    means = to_groups(sums, member) / jnp.maximum(counts, 1.0)
    means_wide = to_channels(means, member)
    squares = jnp.zeros((SLOTS, channels), F32)
    for index, row in enumerate(rows):
        centered = jnp.where(column < widths[index], row - means_wide[index : index + 1], 0.0)
        squares = jnp.where(
            slot == index, jnp.sum(centered * centered, axis=0, keepdims=True), squares
        )
    spreads = to_groups(squares, member)
    out_ref[...] = jnp.zeros(out_ref.shape, F32)
    for video in range(videos):
        total = jnp.zeros((1, LANES), F32)
        count = jnp.zeros((1, LANES), F32)
        for index in range(len(rows)):
            mine = labels[index] == video
            row_count = counts[index : index + 1]
            total = total + jnp.where(mine, means[index : index + 1] * row_count, 0.0)
            count = count + jnp.where(mine, row_count, 0.0)
        mean = total / jnp.maximum(count, 1.0)
        spread = jnp.zeros((1, LANES), F32)
        for index in range(len(rows)):
            off = means[index : index + 1] - mean
            part = spreads[index : index + 1] + counts[index : index + 1] * off * off
            spread = spread + jnp.where(labels[index] == video, part, 0.0)
        out_ref[0, video : video + 1, :] = count
        out_ref[1, video : video + 1, :] = mean
        out_ref[2, video : video + 1, :] = spread


def build_columns(columns_ref, row_refs):
    padded = columns_ref.shape[0] // len(row_refs)
    for index, row in enumerate(row_refs):
        cells = row().astype(F32)
        count, channels = cells.shape
        cells = jnp.concatenate([cells, jnp.zeros((padded - count, channels), F32)], axis=0)
        start = index * padded
        columns_ref[start : start + padded, 0:channels] = pltpu.roll(cells, 1, 0).astype(BF16)
        columns_ref[start : start + padded, channels : 2 * channels] = cells.astype(BF16)
        columns_ref[start : start + padded, 2 * channels : 3 * channels] = pltpu.roll(
            cells, padded - 1, 0
        ).astype(BF16)


def stats_kernel(rows, info_ref, latents_ref, out_ref):
    info = Info(info_ref, rows)
    row_count, cols, channels = latents_ref.shape
    labels, widths = info.window(info.tile() * row_count, row_count)
    column = lax.broadcasted_iota(jnp.int32, (cols, 1), 0)
    cells = [
        jnp.where(column < widths[r], latents_ref[r].astype(F32), 0.0) for r in range(row_count)
    ]
    write_stats(out_ref, cells, labels, widths, info.videos, channels)


def rims(info, outer_ref, inner_ref):
    odd = lax.rem(info.tile(), 2) == 1
    inner, outer = inner_ref[0].astype(F32), outer_ref[0].astype(F32)
    return jnp.where(odd, inner, outer), jnp.where(odd, outer, inner)


def hidden_kernel(
    rows, info_ref, outer_ref, inner_ref, latents_ref, stats_ref, gain_ref, shift_ref, out_ref,
    source_ref,
):
    info = Info(info_ref, rows)
    row_count, cols, _ = latents_ref.shape
    labels, widths = info.window(info.tile() * row_count - 1, row_count + 2)
    means, scales = norm_tables(stats_ref, gain_ref)
    column = lax.broadcasted_iota(jnp.int32, (cols, 1), 0)
    above, below = rims(info, outer_ref, inner_ref)
    sources = [above] + [latents_ref[r].astype(F32) for r in range(row_count)] + [below]
    for r, source in enumerate(sources):
        mean = pick(means, labels[r], info.videos)
        scale = pick(scales, labels[r], info.videos)
        normed = (source - mean) * scale + shift_ref[...]
        active = normed / (1.0 + jnp.exp(-normed))
        active = jnp.where(column < widths[r], active, 0.0)
        rest = jnp.zeros((out_ref.shape[1] - cols, active.shape[1]), F32)
        out_ref[r] = jnp.concatenate([active, rest], axis=0).astype(BF16)
    source_ref[...] = latents_ref[...]


def hold_kernel(taps, weight_ref, held_ref, sems):
    channels = weight_ref.shape[-1]
    copies = [
        pltpu.make_async_copy(
            weight_ref.at[2 - depth // 3, depth % 3, side],
            held_ref.at[pl.ds(depth * channels, channels), pl.ds(side * channels, channels)],
            sems.at[side, depth],
        )
        for side in range(3)
        for depth in range(3 * taps)
    ]
    for copy in copies:
        copy.start()
    for copy in copies:
        copy.wait()


def row_taps(info, hidden_refs, inputs_ref):
    near_rows, padded, channels = hidden_refs[0].shape
    row_count = near_rows - 2
    labels, _ = info.window(info.tile() * row_count - 1, near_rows)
    for back, hidden_ref in enumerate(hidden_refs):
        for tap in range(3):
            lanes = slice((3 * back + tap) * channels, (3 * back + tap + 1) * channels)
            for r in range(row_count):
                block = hidden_ref[r + tap]
                if tap != 1:
                    same = labels[r + tap] == labels[r + 1]
                    block = jnp.where(same, block, jnp.zeros_like(block))
                inputs_ref[r * padded : (r + 1) * padded, lanes] = block


def own_conv_kernel(rows, info_ref, hidden_ref, held_ref, product_ref, inputs_ref):
    row_taps(Info(info_ref, rows), [hidden_ref], inputs_ref)
    depth = inputs_ref.shape[1]
    product_ref[...] = jnp.dot(
        inputs_ref[...], held_ref[0:depth, :], preferred_element_type=F32
    )


def conv_kernel(rows, taps, info_ref, *rest):
    hidden_refs, rest = rest[: taps - 1], rest[taps - 1 :]
    product_ref, latents_ref, bias_ref, held_ref, own_ref, stats_ref, *inputs_refs = rest
    row_count, cols, channels = latents_ref.shape
    info = Info(info_ref, rows)
    padded = product_ref.shape[0] // row_count
    labels, widths = info.window(info.tile() * row_count - 1, row_count + 2)
    product = product_ref[...]
    if hidden_refs:
        (inputs_ref,) = inputs_refs
        row_taps(info, hidden_refs, inputs_ref)
        product = product + jnp.dot(
            inputs_ref[...], held_ref[3 * channels :, :], preferred_element_type=F32
        )
    column = lax.broadcasted_iota(jnp.int32, (cols, 1), 0)
    cells = []
    for r in range(row_count):
        lines = slice(r * padded, (r + 1) * padded)
        branch = pltpu.roll(product[lines, 0:channels], 1, 0)
        branch = branch + product[lines, channels : 2 * channels]
        branch = branch + pltpu.roll(product[lines, 2 * channels :], padded - 1, 0)
        value = latents_ref[r].astype(F32) + branch[:cols] + bias_ref[...]
        value = jnp.where(column < widths[r + 1], value, 0.0).astype(BF16)
        cells.append(value.astype(F32))
    for pair in range(row_count // 2):
        own_ref[pair] = jnp.concatenate(cells[2 * pair : 2 * pair + 2], axis=0).astype(BF16)
    write_stats(stats_ref, cells, labels[1:-1], widths[1:-1], info.videos, channels)


def split_rows(pairs_ref):
    cols = pairs_ref.shape[1] // 2
    cells = []
    for pair in range(pairs_ref.shape[0]):
        both = pairs_ref[pair].astype(F32)
        cells += [both[:cols], both[cols:]]
    return cells


def turned_queries(info, tile, pairs_ref, means, scales, shift_ref, weight_ref, bias_ref):
    pairs, double, channels = pairs_ref.shape
    cols = double // 2
    column = lax.broadcasted_iota(jnp.int32, (cols, 1), 0)
    labels, widths = info.window(tile * 2 * pairs, 2 * pairs)
    cells = []
    for r, values in enumerate(split_rows(pairs_ref)):
        mean = pick(means, labels[r], info.videos)
        scale = pick(scales, labels[r], info.videos)
        normed = (values - mean) * scale + shift_ref[...]
        cells.append(jnp.where(column < widths[r], normed, 0.0))
    cells = jnp.concatenate(cells, axis=0).astype(BF16)
    queries = (
        jnp.dot(cells, weight_ref[:, 0:channels], preferred_element_type=F32)
        + bias_ref[:, 0:channels]
    ).astype(BF16)
    factor = channels ** (-0.5) * math.log2(math.e)
    turned = lax.dot_general(
        queries, weight_ref[:, channels : 2 * channels], (((1,), (1,)), ((), ())),
        preferred_element_type=F32,
    )
    constant = jnp.sum(
        queries.astype(F32) * bias_ref[:, channels : 2 * channels], axis=1, keepdims=True
    )
    return (turned * factor).astype(BF16), constant * factor


def query_kernel(
    rows, info_ref, own_ref, other_ref, stats_ref, gain_ref, shift_ref, weight_ref, bias_ref,
    means_ref, scales_ref, *out_refs,
):
    info = Info(info_ref, rows)
    means, scales = norm_tables(stats_ref, gain_ref)
    means_ref[...] = means
    scales_ref[...] = scales
    for side, (tile, pairs_ref) in enumerate(
        ((info.tile() ^ 1, other_ref), (info.tile(), own_ref))
    ):
        queries, constant = turned_queries(
            info, tile, pairs_ref, means, scales, shift_ref, weight_ref, bias_ref
        )
        queries_ref, constant_ref = out_refs[2 * side : 2 * side + 2]
        queries_ref[...] = queries
        constant_ref[...] = jnp.broadcast_to(constant, constant_ref.shape)


def key_codes(info, masks, span, cols):
    row_count = span // cols
    position = lax.broadcasted_iota(jnp.int32, (1, len(masks) * span), 1)
    codes = jnp.full((1, len(masks) * span), -2.0, F32)
    for index, mask in enumerate(masks):
        near, widths = info.window((info.tile() ^ (2 * mask)) * row_count, row_count)
        for r in range(row_count):
            start = index * span + r * cols
            inside = (position >= start) & (position < start + widths[r])
            codes = jnp.where(inside, near[r].astype(F32), codes)
    return codes


def query_codes(info, tile, span, cols):
    row_count = span // cols
    labels, _ = info.window(tile * row_count, row_count)
    return jnp.concatenate(
        [jnp.zeros((cols, 1), F32) + label.astype(F32) for label in labels], axis=0
    )


def scores_of(queries, keys, codes, query_code):
    scores = lax.dot_general(
        queries, keys, (((1,), (1,)), ((), ())), preferred_element_type=F32
    )
    return jnp.where(codes == query_code, scores, MASKED)


def mean_and_level(peak, denominator, total):
    some = denominator > 0.0
    safe = jnp.where(some, denominator, 1.0)
    return total / safe, jnp.where(some, peak + jnp.log2(safe), LOWEST)


def attend_yours_kernel(rows, masks, first, last, info_ref, *rest):
    means_ref, scales_ref, shift_ref, queries_ref, constant_ref, *rest = rest
    block_refs, rest = rest[: len(masks)], rest[len(masks) :]
    if not first:
        old_peak_ref, old_sum_ref, old_total_ref, *rest = rest
    keys_ref, *out_refs = rest
    info = Info(info_ref, rows)
    span, channels = queries_ref.shape
    pairs, double, _ = block_refs[0].shape
    cols = double // 2
    row_count = 2 * pairs
    tile = info.tile()
    means, scales = means_ref[...], scales_ref[...]
    for index, (mask, block_ref) in enumerate(zip(masks, block_refs)):
        near, _ = info.window((tile ^ (2 * mask)) * row_count, row_count)
        for pair in range(pairs):
            both = block_ref[pair].astype(F32)
            halves = []
            for half in range(2):
                label = near[2 * pair + half]
                mean = pick(means, label, info.videos)
                scale = pick(scales, label, info.videos)
                values = both[half * cols : (half + 1) * cols]
                halves.append((values - mean) * scale + shift_ref[...])
            start = index * span + pair * double
            keys_ref[start : start + double, :] = jnp.concatenate(halves, axis=0).astype(BF16)
    constant = constant_ref[:, 0:1]
    scores = scores_of(
        queries_ref[...], keys_ref[...], key_codes(info, masks, span, cols),
        query_codes(info, tile ^ 1, span, cols),
    )
    peak = jnp.maximum(LOWEST, jnp.max(scores, axis=1, keepdims=True) + constant)
    if not first:
        largest = old_peak_ref[:, 0:1]
        peak = jnp.maximum(largest, peak)
    weights = jnp.exp2(scores - (peak - constant))
    denominator = jnp.sum(weights, axis=1, keepdims=True)
    total = jnp.dot(weights.astype(BF16), keys_ref[...], preferred_element_type=F32)
    if not first:
        factor = jnp.exp2(largest - peak)
        denominator = old_sum_ref[:, 0:1] * factor + denominator
        total = old_total_ref[...] * factor + total
    if not last:
        peak_ref, sum_ref, total_ref = out_refs
        peak_ref[...] = jnp.broadcast_to(peak, peak_ref.shape)
        sum_ref[...] = jnp.broadcast_to(denominator, sum_ref.shape)
        total_ref[...] = total
        return
    (sent_ref,) = out_refs
    mean, level = mean_and_level(peak, denominator, total)
    sent_ref[0:span, :] = mean.astype(BF16)
    slots = sent_ref.shape[0] - span
    slot = lax.broadcasted_iota(jnp.int32, (slots, 1), 0)
    packed = jnp.zeros((slots, LANES), F32)
    for r in range(row_count):
        left = level[r * cols : (r + 1) * cols]
        left = jnp.sum(jnp.where(diagonal(cols), left, 0.0), axis=0, keepdims=True)
        for part in range(3):
            rounded = left.astype(BF16).astype(F32)
            packed = jnp.where(slot == 3 * r + part, rounded, packed)
            left = left - rounded
    sent_ref[span:, 0:LANES] = packed.astype(BF16)
    sent_ref[span:, LANES:] = jnp.zeros((slots, channels - LANES), BF16)


def attend_mine_kernel(
    rows, groups, info_ref, queries_ref, constant_ref, *rest
):
    key_refs, (mean_ref, level_ref) = rest[: len(groups)], rest[len(groups) :]
    info = Info(info_ref, rows)
    span = mean_ref.shape[0]
    queries, constant = queries_ref[...], constant_ref[:, 0:1]
    cols = span // ROWS_OF_TILE
    query_code = query_codes(info, info.tile(), span, cols)
    peak = jnp.full((span, 1), LOWEST, F32)
    scores = []
    for masks, key_ref in zip(groups, key_refs):
        codes = key_codes(info, masks, span, cols)
        scores.append(scores_of(queries, key_ref[...], codes, query_code))
        peak = jnp.maximum(peak, jnp.max(scores[-1], axis=1, keepdims=True) + constant)
    denominator, total = 0.0, 0.0
    for part, key_ref in zip(scores, key_refs):
        weights = jnp.exp2(part - (peak - constant))
        denominator = denominator + jnp.sum(weights, axis=1, keepdims=True)
        total = total + jnp.dot(
            weights.astype(BF16), key_ref[...], preferred_element_type=F32
        )
    mean, level = mean_and_level(peak, denominator, total)
    mean_ref[...] = mean
    level_ref[...] = jnp.broadcast_to(level, level_ref.shape)


def diagonal(cols):
    return lax.broadcasted_iota(jnp.int32, (cols, LANES), 0) == lax.broadcasted_iota(
        jnp.int32, (cols, LANES), 1
    )


def finish_kernel(
    rows, info_ref, mean_ref, level_ref, received_ref, own_ref, triple_ref, triple_bias_ref,
    output_ref, output_bias_ref, out_ref, inner_ref, outer_ref,
):
    info = Info(info_ref, rows)
    row_count, cols, channels = out_ref.shape
    span = row_count * cols
    _, widths = info.window(info.tile() * row_count, row_count)
    received = received_ref[0:span, :].astype(F32)
    levels = received_ref[span:, 0:LANES].astype(F32)
    yours = []
    for r in range(row_count):
        level = levels[3 * r : 3 * r + 1] + levels[3 * r + 1 : 3 * r + 2]
        level = level + levels[3 * r + 2 : 3 * r + 3]
        yours.append(jnp.sum(jnp.where(diagonal(cols), level, 0.0), axis=1, keepdims=True))
    yours = jnp.concatenate(yours, axis=0)
    mine = level_ref[:, 0:1]
    peak = jnp.maximum(mine, yours)
    weight, other_weight = jnp.exp2(mine - peak), jnp.exp2(yours - peak)
    share = weight / (weight + other_weight)
    mean_cell = (mean_ref[...] * share + received * (1.0 - share)).astype(BF16)
    mixed = (
        jnp.dot(mean_cell, triple_ref[:, 2 * channels :], preferred_element_type=F32)
        + triple_bias_ref[:, 2 * channels :]
    ).astype(BF16)
    attended = jnp.dot(mixed, output_ref[...], preferred_element_type=F32) + output_bias_ref[...]
    column = lax.broadcasted_iota(jnp.int32, (cols, 1), 0)
    for r, before in enumerate(split_rows(own_ref)):
        value = before + attended[r * cols : (r + 1) * cols]
        value = jnp.where(column < widths[r], value, 0.0)
        out_ref[r] = value.astype(BF16)
        if r == 0:
            top = value
    odd = lax.rem(info.tile(), 2) == 1
    inner_ref[0] = jnp.where(odd, top, value).astype(BF16)
    outer_ref[0] = jnp.where(odd, value, top).astype(BF16)


def fold_kernel(weight_ref, output_ref, out_ref, output_copy_ref):
    output_copy_ref[...] = output_ref[...]
    channels = weight_ref.shape[-1]
    wide = [[weight_ref[a, b].astype(F32) for b in range(3)] for a in range(3)]

    def both(upper, lower):
        return [x + y for x, y in zip(upper, lower)]

    phases = [[wide[0], both(wide[1], wide[2])], [both(wide[0], wide[1]), wide[2]]]
    for down in range(2):
        for tap in range(2):
            left, middle, right = phases[down][tap]
            out_ref[down, tap, 0, :, 0:channels] = left.astype(BF16)
            out_ref[down, tap, 0, :, channels:] = (middle + right).astype(BF16)
            out_ref[down, tap, 1, :, 0:channels] = (left + middle).astype(BF16)
            out_ref[down, tap, 1, :, channels:] = right.astype(BF16)


def spread_columns(wide_ref, value, row, right):
    cols, channels = value.shape
    for part in range(wide_ref.shape[0]):
        lo, hi = part * LANES, min((part + 1) * LANES, channels)
        piece = value[:, lo:hi]
        if hi - lo < LANES:
            piece = jnp.concatenate([piece, jnp.zeros((cols, LANES - hi + lo), F32)], axis=1)
        wide_ref[part, row, pl.ds(right, cols, 2), :] = piece


def write_turned(out_ref, row, part, value, width):
    channels, cols = out_ref.shape[1:]
    lo, hi = part * LANES, min((part + 1) * LANES, channels)
    turned = value.T[0 : hi - lo, 0:cols]
    column = lax.broadcasted_iota(jnp.int32, (1, cols), 1)
    out_ref[row, lo:hi, :] = jnp.where(column < width, turned, 0.0).astype(BF16)


def phase_product(columns, weight):
    return lax.dot_general(
        columns, weight, (((1,), (1,)), ((), ())), preferred_element_type=F32
    )


def upsample_kernel(
    rows, info_ref, own_ref, weight_ref, bias_ref, out_ref, open_ref, columns_ref, wide_ref,
    turned_ref, sem,
):
    info = Info(info_ref, rows)
    row_count, cols, channels = own_ref.shape
    padded = columns_ref.shape[0] // row_count
    parts_out = wide_ref.shape[0]
    labels, widths = info.window(info.tile() * row_count, row_count)
    build_columns(
        columns_ref, [functools.partial(own_ref.__getitem__, r) for r in range(row_count)]
    )
    inner_rows = (row_count - 1) * padded
    for down in range(2):
        for right in range(2):
            lanes = slice(right * channels, (right + 2) * channels)
            same = phase_product(columns_ref[:, lanes], weight_ref[down, 1 - down, right])
            start = down * padded
            rim = phase_product(
                columns_ref[start : start + inner_rows, lanes], weight_ref[down, down, right]
            )
            for r in range(row_count):
                value = same[r * padded : r * padded + cols]
                near = r - 1 + 2 * down
                if 0 <= near < row_count:
                    lo = (near - down) * padded
                    value = value + jnp.where(
                        labels[near] == labels[r], rim[lo : lo + cols], 0.0
                    )
                spread_columns(wide_ref, value, 2 * r + down, right)
    for part in range(parts_out):
        open_ref[part, 0] = wide_ref[part, 0]
        open_ref[part, 1] = wide_ref[part, 2 * row_count - 1]
    for r in range(1, 2 * row_count - 1):
        for part in range(parts_out):
            value = wide_ref[part, r] + bias_ref[:, part * LANES : (part + 1) * LANES]
            write_turned(turned_ref, r - 1, part, value, 2 * widths[r // 2])
    copy = pltpu.make_async_copy(turned_ref, out_ref.at[pl.ds(1, 2 * row_count - 2)], sem)
    copy.start()
    copy.wait()


def close_kernel(
    rows, info_ref, outer_ref, inner_ref, _, open_ref, weight_ref, bias_ref, out_ref, columns_ref,
    wide_ref, turned_ref, sems,
):
    info = Info(info_ref, rows)
    wide_rows, _, wide_cols = out_ref.shape
    row_count, cols = wide_rows // 2, wide_cols // 2
    channels = outer_ref.shape[-1]
    padded = columns_ref.shape[0] // 2
    labels, widths = info.window(info.tile() * row_count - 1, row_count + 2)
    above, below = rims(info, outer_ref, inner_ref)
    build_columns(columns_ref, [lambda: above, lambda: below])
    for down in range(2):
        for right in range(2):
            lanes = slice(right * channels, (right + 2) * channels)
            rim = phase_product(
                columns_ref[down * padded : (down + 1) * padded, lanes],
                weight_ref[down, down, right],
            )
            spread_columns(wide_ref, rim[:cols], down, right)
    copies = []
    for down in range(2):
        rim_row, own_row = (row_count + 1, row_count) if down else (0, 1)
        for part in range(wide_ref.shape[0]):
            rim = jnp.where(labels[rim_row] == labels[own_row], wide_ref[part, down], 0.0)
            value = open_ref[part, down] + rim + bias_ref[:, part * LANES : (part + 1) * LANES]
            write_turned(turned_ref, down, part, value, 2 * widths[own_row])
        copies.append(
            pltpu.make_async_copy(
                turned_ref.at[down], out_ref.at[down * (wide_rows - 1)], sems.at[down]
            )
        )
        copies[-1].start()
    for copy in copies:
        copy.wait()


def merge_stats(mine, other):
    count = mine[0] + other[0]
    safe = jnp.maximum(count, 1.0)
    off = other[1] - mine[1]
    mean = mine[1] + off * (other[0] / safe)
    spread = mine[2] + other[2] + off * off * (mine[0] * other[0] / safe)
    return jnp.stack([count, mean, spread])


def exchange(array, tiles, mask, among=None):
    moves = [(i, i ^ mask) for i in range(tiles) if among is None or among(i)]
    return lax.ppermute(array, "tile", moves)


def merge_round(stats, tiles, masks, tied=()):
    parts = [stats] + [exchange(stats, tiles, mask) for mask in masks]
    if tied:
        parts[1], *tied = lax.optimization_barrier((parts[1], *tied))
    while len(parts) > 1:
        parts = [merge_stats(*parts[i : i + 2]) for i in range(0, len(parts), 2)]
    return (parts[0], *tied) if tied else parts[0]


def merge_masks(tiles):
    bits = [1 << i for i in range(tiles.bit_length() - 1)]
    pairs = [bits[i : i + 2] for i in range(0, len(bits), 2)]
    return [[p[0], p[1], p[0] ^ p[1]] if len(p) == 2 else p for p in pairs]


def shards(
    tiles,
    frames,
    latents,
    row_video,
    video_cols,
    first_gain,
    first_shift,
    conv_weight,
    conv_bias,
    second_gain,
    second_shift,
    triple_weight,
    triple_bias,
    output_weight,
    output_bias,
    upsample_weight,
    upsample_bias,
):
    row_count, frame_count, cols, channels = latents.shape
    assert frame_count == 1 and row_count == ROWS_OF_TILE and tiles % 4 == 0
    out_channels = upsample_weight.shape[-1]
    rows = row_count * tiles
    cells = row_count * cols
    padded = -(-(cols + 1) // 16) * 16
    near_rows = row_count + 2
    source = latents.reshape(row_count, cols, channels)
    tile = lax.axis_index("tile").astype(jnp.int32)
    info = jnp.concatenate([jnp.reshape(tile, (1,)), row_video, video_cols])

    def row(vector):
        return vector.reshape(1, -1)

    def shape(*dims, dtype=BF16):
        return jax.ShapeDtypeStruct(dims, dtype)

    def call(kernel, operands, out_shape, scratch=(), **kwargs):
        many = isinstance(out_shape, tuple)
        return pl.pallas_call(
            kernel,
            out_shape=out_shape,
            in_specs=[SMEM_SPEC] + [VMEM_SPEC] * len(operands),
            out_specs=(VMEM_SPEC,) * len(out_shape) if many else VMEM_SPEC,
            scratch_shapes=list(scratch),
            compiler_params=params(),
            **kwargs,
        )(info, *operands)

    outer_moves = [(i, i - 1 if i % 2 == 0 else i + 1) for i in range(tiles)]
    outer_moves = [(i, j) for i, j in outer_moves if 0 <= j < tiles]
    odd = tile % 2 == 1
    stats_shape = shape(3, SLOTS, LANES, dtype=F32)
    stats = call(
        functools.partial(stats_kernel, rows), [source], stats_shape,
        cost_estimate=cost(1.5), name="first_stats",
    )
    outer = lax.ppermute(
        jnp.where(odd, source[row_count - 1 :], source[:1]), "tile", outer_moves
    )
    inner = exchange(jnp.where(odd, source[:1], source[row_count - 1 :]), tiles, 1)
    stats, outer, inner = lax.optimization_barrier((stats, outer, inner))
    taps = min(3, frames)
    held = pl.pallas_call(
        functools.partial(hold_kernel, taps),
        out_shape=shape(3 * taps * channels, 3 * channels),
        in_specs=[HBM_SPEC],
        out_specs=VMEM_SPEC,
        scratch_shapes=[pltpu.SemaphoreType.DMA((3, 3 * taps))],
        compiler_params=pltpu.CompilerParams(vmem_limit_bytes=HOLD_VMEM_BYTES),
        cost_estimate=cost(1.5 * taps),
        name="hold",
    )(conv_weight)
    rounds = merge_masks(tiles)
    for index, masks in enumerate(reversed(rounds)):
        stats = merge_round(stats, tiles, masks)
        if index == len(rounds) - 2:
            stats, held = lax.optimization_barrier((stats, held))
    hidden, source = call(
        functools.partial(hidden_kernel, rows),
        [outer, inner, source, stats, row(first_gain), row(first_shift)],
        (shape(near_rows, padded, channels), shape(row_count, cols, channels)),
        cost_estimate=cost(1.3),
        name="hidden",
    )

    earlier = [
        lax.ppermute(hidden, "frame", [(i, i + by) for i in range(frames - by)])
        for by in range(1, taps)
    ]
    pairs = row_count // 2
    pair_shape = shape(pairs, 2 * cols, channels)
    product = call(
        functools.partial(own_conv_kernel, rows),
        [hidden, held],
        shape(row_count * padded, 3 * channels, dtype=F32),
        scratch=[pltpu.VMEM((row_count * padded, 3 * channels), BF16)],
        cost_estimate=cost(2.2),
        name="own_conv",
    )
    scratch = [pltpu.VMEM((row_count * padded, 3 * (taps - 1) * channels), BF16)]
    own, stats = call(
        functools.partial(conv_kernel, rows, taps),
        earlier + [product, source, row(conv_bias), held],
        (pair_shape, stats_shape),
        scratch=scratch if taps > 1 else [],
        cost_estimate=cost(1.5 + 2.0 * (taps - 1)),
        name="conv",
    )

    blocks = {0: own}
    neighbour = [(i, i ^ 1) for i in range(tiles)]
    if tiles == 16 and video_cols.shape[0] == 2:
        def middle(t):
            return t // 4 in (1, 2)

        stats = merge_round(stats, tiles, rounds[1])
        blocks[2] = exchange(own, tiles, 4)
        blocks[6] = exchange(own, tiles, 12, middle)
        stats, blocks[2], blocks[6] = merge_round(
            stats, tiles, rounds[0], (blocks[2], blocks[6])
        )
        stats, own_xy = lax.optimization_barrier((stats, own))
        inward = exchange(blocks[2], tiles, 12, middle)
        outward = exchange(blocks[6], tiles, 4, middle)
        other = exchange(own_xy, tiles, 1)
        blocks[1] = exchange(own_xy, tiles, 2)
        blocks[4] = jnp.where((tile // 4 == 1) | (tile // 4 == 2), inward, outward)
        passed, blocks[4] = lax.optimization_barrier((blocks[1], blocks[4]))
        blocks[5] = exchange(blocks[4], tiles, 2)
        blocks[3] = exchange(passed, tiles, 4)
        blocks[7] = exchange(passed, tiles, 12, middle)
        groups = [[0, 1, 2, 6], [4, 7, 3, 5]]
    else:
        for masks in rounds:
            stats = merge_round(stats, tiles, masks)
        other = exchange(own, tiles, 1)
        for mask in range(1, tiles // 2):
            blocks[mask] = exchange(own, tiles, 2 * mask)
        groups = [list(range(i, i + 4)) for i in range(0, tiles // 2, 4)]
    gain, shift = row(second_gain), row(second_shift)
    table_shape = shape(SLOTS, channels, dtype=F32)
    folded, out_weight = pl.pallas_call(
        fold_kernel,
        out_shape=(shape(2, 2, 2, out_channels, 2 * channels), shape(channels, channels)),
        in_specs=[VMEM_SPEC, VMEM_SPEC],
        out_specs=(VMEM_SPEC, VMEM_SPEC),
        compiler_params=params(),
        cost_estimate=cost(0.6),
        name="fold",
    )(jnp.swapaxes(upsample_weight, 2, 3), output_weight)
    other, folded, out_weight = lax.optimization_barrier((other, folded, out_weight))
    query_shapes = (shape(cells, channels), shape(cells, LANES, dtype=F32))
    means, scales, queries, constant, mine_queries, mine_constant = call(
        functools.partial(query_kernel, rows),
        [own, other, stats, gain, shift, triple_weight, row(triple_bias)],
        (table_shape, table_shape) + query_shapes * 2,
        cost_estimate=cost(1.9),
        name="queries",
    )
    level_shape = shape(cells, LANES, dtype=F32)
    total_shape = shape(cells, channels, dtype=F32)
    state, keys = (), []
    for index, masks in enumerate(groups):
        last = index == len(groups) - 1
        outs = (shape(len(masks) * cells, channels),)
        outs += (shape(cells + 16, channels),) if last else (level_shape, level_shape, total_shape)
        normed, *state = call(
            functools.partial(attend_yours_kernel, rows, tuple(masks), index == 0, last),
            [means, scales, shift, queries, constant] + [blocks[m] for m in masks] + list(state),
            outs,
            cost_estimate=cost(0.9 * len(masks)),
            name="attend_yours",
        )
        keys.append(normed)
    (sent,) = state
    received = lax.ppermute(sent, "tile", neighbour)
    sent, mine_queries = lax.optimization_barrier((sent, mine_queries))
    mean, level = call(
        functools.partial(attend_mine_kernel, rows, tuple(tuple(masks) for masks in groups)),
        [mine_queries, mine_constant] + keys,
        (total_shape, level_shape),
        cost_estimate=cost(4.3),
        name="attend_mine",
    )

    rim_shape = shape(1, cols, channels)
    attended, inner, outer = call(
        functools.partial(finish_kernel, rows),
        [
            mean, level, received, own, triple_weight, row(triple_bias), out_weight,
            row(output_bias),
        ],
        (shape(row_count, cols, channels), rim_shape, rim_shape),
        cost_estimate=cost(1.4),
        name="finish",
    )
    outer = lax.ppermute(outer, "tile", outer_moves)
    inner = exchange(inner, tiles, 1)
    parts_out = -(-out_channels // LANES)
    wide_cols = -(-2 * cols // LANES) * LANES
    wide_bias = jnp.pad(row(upsample_bias), ((0, 0), (0, -out_channels % LANES)))
    out_shape = shape(2 * row_count, out_channels, 2 * cols)
    open_shape = shape(parts_out, 2, wide_cols, LANES, dtype=F32)
    decoded, open_rows = pl.pallas_call(
        functools.partial(upsample_kernel, rows),
        out_shape=(out_shape, open_shape),
        in_specs=[SMEM_SPEC] + [VMEM_SPEC] * 3,
        out_specs=(HBM_SPEC, VMEM_SPEC),
        scratch_shapes=[
            pltpu.VMEM((row_count * padded, 3 * channels), BF16),
            pltpu.VMEM((parts_out, 2 * row_count, wide_cols, LANES), F32),
            pltpu.VMEM((2 * row_count - 2, out_channels, 2 * cols), BF16),
            pltpu.SemaphoreType.DMA,
        ],
        compiler_params=params(),
        cost_estimate=cost(2.0),
        name="upsample",
    )(info, attended, folded, wide_bias)
    decoded = pl.pallas_call(
        functools.partial(close_kernel, rows),
        out_shape=out_shape,
        in_specs=[SMEM_SPEC] + [VMEM_SPEC] * 2 + [HBM_SPEC] + [VMEM_SPEC] * 3,
        out_specs=HBM_SPEC,
        scratch_shapes=[
            pltpu.VMEM((2 * padded, 3 * channels), BF16),
            pltpu.VMEM((parts_out, 2, wide_cols, LANES), F32),
            pltpu.VMEM((2, out_channels, 2 * cols), BF16),
            pltpu.SemaphoreType.DMA((2,)),
        ],
        input_output_aliases={3: 0},
        compiler_params=params(),
        cost_estimate=cost(1.0),
        name="close",
    )(info, outer, inner, decoded, open_rows, folded, wide_bias)
    return jnp.swapaxes(decoded, 1, 2).reshape(2 * row_count, 1, 2 * cols, out_channels)


def solution(mesh):
    sizes = dict(mesh.shape)
    in_specs = (P("tile", "frame", None, None),) + (P(),) * 14
    out_specs = P("tile", "frame", None, None)
    body = functools.partial(shards, sizes["tile"], sizes["frame"])
    return jax.shard_map(body, mesh=mesh, in_specs=in_specs, out_specs=out_specs, check_vma=False)
```

```python
import functools
import math

import jax
import jax.numpy as jnp
from jax import lax
from jax.experimental import pallas as pl
from jax.experimental.pallas import tpu as pltpu
from jax.sharding import PartitionSpec as P

GROUPS = 32
EPSILON = 1e-05
MASKED = -1e30
LOWEST = -5e29
HIGHEST = lax.Precision.HIGHEST
SLOTS = 8
ROWS_OF_TILE = 4
LANES = 128
VMEM_BYTES = 24 * 1024 * 1024
HOLD_VMEM_BYTES = 46 * 1024 * 1024
F32 = jnp.float32
BF16 = jnp.bfloat16

SMEM_SPEC = pl.BlockSpec(memory_space=pltpu.SMEM)
VMEM_SPEC = pl.BlockSpec(memory_space=pltpu.VMEM)
HBM_SPEC = pl.BlockSpec(memory_space=pltpu.HBM)


def cost(microseconds):
    return pl.CostEstimate(
        flops=int(microseconds * 1.1e9), bytes_accessed=0, transcendentals=0
    )


def params():
    return pltpu.CompilerParams(vmem_limit_bytes=VMEM_BYTES)


def member_matrix(channels):
    per_group = channels // GROUPS
    group = lax.broadcasted_iota(jnp.int32, (LANES, channels), 0) * per_group
    channel = lax.broadcasted_iota(jnp.int32, (LANES, channels), 1)
    return jnp.where((channel >= group) & (channel < group + per_group), 1.0, 0.0).astype(F32)


def to_groups(values, member):
    return lax.dot_general(
        values, member, (((1,), (1,)), ((), ())), precision=HIGHEST, preferred_element_type=F32
    )


def to_channels(values, member):
    return jnp.dot(values, member, precision=HIGHEST, preferred_element_type=F32)


class Info:
    def __init__(self, ref, rows):
        self.ref, self.rows = ref, rows
        self.videos = ref.shape[0] - 1 - rows

    def tile(self):
        return self.ref[0]

    def label(self, row):
        inside = (row >= 0) & (row < self.rows)
        return jnp.where(inside, self.ref[1 + jnp.clip(row, 0, self.rows - 1)], -1)

    def width(self, label):
        return jnp.where(label >= 0, self.ref[1 + self.rows + jnp.maximum(label, 0)], 0)

    def window(self, first, count):
        labels = [self.label(first + r) for r in range(count)]
        return labels, [self.width(label) for label in labels]


def pick(table, label, videos):
    chosen = table[0:1]
    for video in range(1, videos):
        chosen = jnp.where(label == video, table[video : video + 1], chosen)
    return chosen


def norm_tables(stats_ref, gain_ref):
    member = member_matrix(gain_ref.shape[1])
    counts = jnp.maximum(stats_ref[0], 1.0)
    scale = lax.rsqrt(stats_ref[2] / counts + EPSILON)
    return to_channels(stats_ref[1], member), to_channels(scale, member) * gain_ref[...]


def write_stats(out_ref, rows, labels, widths, videos, channels):
    member = member_matrix(channels)
    per_group = channels // GROUPS
    cols = rows[0].shape[0]
    slot = lax.broadcasted_iota(jnp.int32, (SLOTS, 1), 0)
    column = lax.broadcasted_iota(jnp.int32, (cols, 1), 0)
    sums = jnp.zeros((SLOTS, channels), F32)
    counts = jnp.zeros((SLOTS, 1), F32)
    for index, row in enumerate(rows):
        sums = jnp.where(slot == index, jnp.sum(row, axis=0, keepdims=True), sums)
        counts = jnp.where(slot == index, (widths[index] * per_group).astype(F32), counts)
    means = to_groups(sums, member) / jnp.maximum(counts, 1.0)
    means_wide = to_channels(means, member)
    squares = jnp.zeros((SLOTS, channels), F32)
    for index, row in enumerate(rows):
        centered = jnp.where(column < widths[index], row - means_wide[index : index + 1], 0.0)
        squares = jnp.where(
            slot == index, jnp.sum(centered * centered, axis=0, keepdims=True), squares
        )
    spreads = to_groups(squares, member)
    out_ref[...] = jnp.zeros(out_ref.shape, F32)
    for video in range(videos):
        total = jnp.zeros((1, LANES), F32)
        count = jnp.zeros((1, LANES), F32)
        for index in range(len(rows)):
            mine = labels[index] == video
            row_count = counts[index : index + 1]
            total = total + jnp.where(mine, means[index : index + 1] * row_count, 0.0)
            count = count + jnp.where(mine, row_count, 0.0)
        mean = total / jnp.maximum(count, 1.0)
        spread = jnp.zeros((1, LANES), F32)
        for index in range(len(rows)):
            off = means[index : index + 1] - mean
            part = spreads[index : index + 1] + counts[index : index + 1] * off * off
            spread = spread + jnp.where(labels[index] == video, part, 0.0)
        out_ref[0, video : video + 1, :] = count
        out_ref[1, video : video + 1, :] = mean
        out_ref[2, video : video + 1, :] = spread


def build_columns(columns_ref, row_refs):
    padded = columns_ref.shape[0] // len(row_refs)
    for index, row in enumerate(row_refs):
        cells = row().astype(F32)
        count, channels = cells.shape
        cells = jnp.concatenate([cells, jnp.zeros((padded - count, channels), F32)], axis=0)
        start = index * padded
        columns_ref[start : start + padded, 0:channels] = pltpu.roll(cells, 1, 0).astype(BF16)
        columns_ref[start : start + padded, channels : 2 * channels] = cells.astype(BF16)
        columns_ref[start : start + padded, 2 * channels : 3 * channels] = pltpu.roll(
            cells, padded - 1, 0
        ).astype(BF16)


def stats_kernel(rows, info_ref, latents_ref, out_ref):
    info = Info(info_ref, rows)
    row_count, cols, channels = latents_ref.shape
    labels, widths = info.window(info.tile() * row_count, row_count)
    column = lax.broadcasted_iota(jnp.int32, (cols, 1), 0)
    cells = [
        jnp.where(column < widths[r], latents_ref[r].astype(F32), 0.0) for r in range(row_count)
    ]
    write_stats(out_ref, cells, labels, widths, info.videos, channels)


def rims(info, outer_ref, inner_ref):
    odd = lax.rem(info.tile(), 2) == 1
    inner, outer = inner_ref[0].astype(F32), outer_ref[0].astype(F32)
    return jnp.where(odd, inner, outer), jnp.where(odd, outer, inner)


def hidden_kernel(
    rows, info_ref, outer_ref, inner_ref, latents_ref, stats_ref, gain_ref, shift_ref, out_ref,
    source_ref,
):
    info = Info(info_ref, rows)
    row_count, cols, _ = latents_ref.shape
    labels, widths = info.window(info.tile() * row_count - 1, row_count + 2)
    means, scales = norm_tables(stats_ref, gain_ref)
    column = lax.broadcasted_iota(jnp.int32, (cols, 1), 0)
    above, below = rims(info, outer_ref, inner_ref)
    sources = [above] + [latents_ref[r].astype(F32) for r in range(row_count)] + [below]
    for r, source in enumerate(sources):
        mean = pick(means, labels[r], info.videos)
        scale = pick(scales, labels[r], info.videos)
        normed = (source - mean) * scale + shift_ref[...]
        active = normed / (1.0 + jnp.exp(-normed))
        active = jnp.where(column < widths[r], active, 0.0)
        rest = jnp.zeros((out_ref.shape[1] - cols, active.shape[1]), F32)
        out_ref[r] = jnp.concatenate([active, rest], axis=0).astype(BF16)
    source_ref[...] = latents_ref[...]


def hold_kernel(taps, weight_ref, held_ref, sems):
    channels = weight_ref.shape[-1]
    copies = [
        pltpu.make_async_copy(
            weight_ref.at[2 - depth // 3, depth % 3, side],
            held_ref.at[pl.ds(depth * channels, channels), pl.ds(side * channels, channels)],
            sems.at[side, depth],
        )
        for side in range(3)
        for depth in range(3 * taps)
    ]
    for copy in copies:
        copy.start()
    for copy in copies:
        copy.wait()


def row_taps(info, hidden_refs, inputs_ref):
    near_rows, padded, channels = hidden_refs[0].shape
    row_count = near_rows - 2
    labels, _ = info.window(info.tile() * row_count - 1, near_rows)
    for back, hidden_ref in enumerate(hidden_refs):
        for tap in range(3):
            lanes = slice((3 * back + tap) * channels, (3 * back + tap + 1) * channels)
            for r in range(row_count):
                block = hidden_ref[r + tap]
                if tap != 1:
                    same = labels[r + tap] == labels[r + 1]
                    block = jnp.where(same, block, jnp.zeros_like(block))
                inputs_ref[r * padded : (r + 1) * padded, lanes] = block


def own_conv_kernel(rows, info_ref, hidden_ref, held_ref, product_ref, inputs_ref):
    row_taps(Info(info_ref, rows), [hidden_ref], inputs_ref)
    depth = inputs_ref.shape[1]
    product_ref[...] = jnp.dot(
        inputs_ref[...], held_ref[0:depth, :], preferred_element_type=F32
    )


def conv_kernel(rows, taps, info_ref, *rest):
    hidden_refs, rest = rest[: taps - 1], rest[taps - 1 :]
    product_ref, latents_ref, bias_ref, held_ref, own_ref, stats_ref, *inputs_refs = rest
    row_count, cols, channels = latents_ref.shape
    info = Info(info_ref, rows)
    padded = product_ref.shape[0] // row_count
    labels, widths = info.window(info.tile() * row_count - 1, row_count + 2)
    product = product_ref[...]
    if hidden_refs:
        (inputs_ref,) = inputs_refs
        row_taps(info, hidden_refs, inputs_ref)
        product = product + jnp.dot(
            inputs_ref[...], held_ref[3 * channels :, :], preferred_element_type=F32
        )
    column = lax.broadcasted_iota(jnp.int32, (cols, 1), 0)
    cells = []
    for r in range(row_count):
        lines = slice(r * padded, (r + 1) * padded)
        branch = pltpu.roll(product[lines, 0:channels], 1, 0)
        branch = branch + product[lines, channels : 2 * channels]
        branch = branch + pltpu.roll(product[lines, 2 * channels :], padded - 1, 0)
        value = latents_ref[r].astype(F32) + branch[:cols] + bias_ref[...]
        value = jnp.where(column < widths[r + 1], value, 0.0).astype(BF16)
        cells.append(value.astype(F32))
    for pair in range(row_count // 2):
        own_ref[pair] = jnp.concatenate(cells[2 * pair : 2 * pair + 2], axis=0).astype(BF16)
    write_stats(stats_ref, cells, labels[1:-1], widths[1:-1], info.videos, channels)


def split_rows(pairs_ref):
    cols = pairs_ref.shape[1] // 2
    cells = []
    for pair in range(pairs_ref.shape[0]):
        both = pairs_ref[pair].astype(F32)
        cells += [both[:cols], both[cols:]]
    return cells


def turned_queries(info, tile, pairs_ref, means, scales, shift_ref, weight_ref, bias_ref):
    pairs, double, channels = pairs_ref.shape
    cols = double // 2
    column = lax.broadcasted_iota(jnp.int32, (cols, 1), 0)
    labels, widths = info.window(tile * 2 * pairs, 2 * pairs)
    cells = []
    for r, values in enumerate(split_rows(pairs_ref)):
        mean = pick(means, labels[r], info.videos)
        scale = pick(scales, labels[r], info.videos)
        normed = (values - mean) * scale + shift_ref[...]
        cells.append(jnp.where(column < widths[r], normed, 0.0))
    cells = jnp.concatenate(cells, axis=0).astype(BF16)
    queries = (
        jnp.dot(cells, weight_ref[:, 0:channels], preferred_element_type=F32)
        + bias_ref[:, 0:channels]
    ).astype(BF16)
    factor = channels ** (-0.5) * math.log2(math.e)
    turned = lax.dot_general(
        queries, weight_ref[:, channels : 2 * channels], (((1,), (1,)), ((), ())),
        preferred_element_type=F32,
    )
    constant = jnp.sum(
        queries.astype(F32) * bias_ref[:, channels : 2 * channels], axis=1, keepdims=True
    )
    return (turned * factor).astype(BF16), constant * factor


def query_kernel(
    rows, info_ref, other_ref, stats_ref, gain_ref, shift_ref, weight_ref, bias_ref, queries_ref,
    constant_ref, means_ref, scales_ref,
):
    info = Info(info_ref, rows)
    means, scales = norm_tables(stats_ref, gain_ref)
    means_ref[...] = means
    scales_ref[...] = scales
    queries, constant = turned_queries(
        info, info.tile() ^ 1, other_ref, means, scales, shift_ref, weight_ref, bias_ref
    )
    queries_ref[...] = queries
    constant_ref[...] = jnp.broadcast_to(constant, constant_ref.shape)


def key_codes(info, masks, span, cols):
    row_count = span // cols
    position = lax.broadcasted_iota(jnp.int32, (1, len(masks) * span), 1)
    codes = jnp.full((1, len(masks) * span), -2.0, F32)
    for index, mask in enumerate(masks):
        near, widths = info.window((info.tile() ^ (2 * mask)) * row_count, row_count)
        for r in range(row_count):
            start = index * span + r * cols
            inside = (position >= start) & (position < start + widths[r])
            codes = jnp.where(inside, near[r].astype(F32), codes)
    return codes


def query_codes(info, tile, span, cols):
    row_count = span // cols
    labels, _ = info.window(tile * row_count, row_count)
    return jnp.concatenate(
        [jnp.zeros((cols, 1), F32) + label.astype(F32) for label in labels], axis=0
    )


def scores_of(queries, keys, codes, query_code):
    scores = lax.dot_general(
        queries, keys, (((1,), (1,)), ((), ())), preferred_element_type=F32
    )
    return jnp.where(codes == query_code, scores, MASKED)


def mean_and_level(peak, denominator, total):
    some = denominator > 0.0
    safe = jnp.where(some, denominator, 1.0)
    return total / safe, jnp.where(some, peak + jnp.log2(safe), LOWEST)


def attend_yours_kernel(rows, masks, first, last, info_ref, *rest):
    means_ref, scales_ref, shift_ref, queries_ref, constant_ref, *rest = rest
    block_refs, rest = rest[: len(masks)], rest[len(masks) :]
    if not first:
        old_peak_ref, old_sum_ref, old_total_ref, *rest = rest
    keys_ref, *out_refs = rest
    info = Info(info_ref, rows)
    span, channels = queries_ref.shape
    pairs, double, _ = block_refs[0].shape
    cols = double // 2
    row_count = 2 * pairs
    tile = info.tile()
    means, scales = means_ref[...], scales_ref[...]
    for index, (mask, block_ref) in enumerate(zip(masks, block_refs)):
        near, _ = info.window((tile ^ (2 * mask)) * row_count, row_count)
        for pair in range(pairs):
            both = block_ref[pair].astype(F32)
            halves = []
            for half in range(2):
                label = near[2 * pair + half]
                mean = pick(means, label, info.videos)
                scale = pick(scales, label, info.videos)
                values = both[half * cols : (half + 1) * cols]
                halves.append((values - mean) * scale + shift_ref[...])
            start = index * span + pair * double
            keys_ref[start : start + double, :] = jnp.concatenate(halves, axis=0).astype(BF16)
    constant = constant_ref[:, 0:1]
    scores = scores_of(
        queries_ref[...], keys_ref[...], key_codes(info, masks, span, cols),
        query_codes(info, tile ^ 1, span, cols),
    )
    peak = jnp.maximum(LOWEST, jnp.max(scores, axis=1, keepdims=True) + constant)
    if not first:
        largest = old_peak_ref[:, 0:1]
        peak = jnp.maximum(largest, peak)
    weights = jnp.exp2(scores - (peak - constant))
    denominator = jnp.sum(weights, axis=1, keepdims=True)
    total = jnp.dot(weights.astype(BF16), keys_ref[...], preferred_element_type=F32)
    if not first:
        factor = jnp.exp2(largest - peak)
        denominator = old_sum_ref[:, 0:1] * factor + denominator
        total = old_total_ref[...] * factor + total
    if not last:
        peak_ref, sum_ref, total_ref = out_refs
        peak_ref[...] = jnp.broadcast_to(peak, peak_ref.shape)
        sum_ref[...] = jnp.broadcast_to(denominator, sum_ref.shape)
        total_ref[...] = total
        return
    (sent_ref,) = out_refs
    mean, level = mean_and_level(peak, denominator, total)
    sent_ref[0:span, :] = mean.astype(BF16)
    slots = sent_ref.shape[0] - span
    slot = lax.broadcasted_iota(jnp.int32, (slots, 1), 0)
    packed = jnp.zeros((slots, LANES), F32)
    for r in range(row_count):
        left = level[r * cols : (r + 1) * cols]
        left = jnp.sum(jnp.where(diagonal(cols), left, 0.0), axis=0, keepdims=True)
        for part in range(3):
            rounded = left.astype(BF16).astype(F32)
            packed = jnp.where(slot == 3 * r + part, rounded, packed)
            left = left - rounded
    sent_ref[span:, 0:LANES] = packed.astype(BF16)
    sent_ref[span:, LANES:] = jnp.zeros((slots, channels - LANES), BF16)


def attend_mine_kernel(
    rows, groups, info_ref, own_ref, means_ref, scales_ref, shift_ref, weight_ref, bias_ref, *rest
):
    key_refs, (mean_ref, level_ref) = rest[: len(groups)], rest[len(groups) :]
    info = Info(info_ref, rows)
    span = mean_ref.shape[0]
    queries, constant = turned_queries(
        info, info.tile(), own_ref, means_ref[...], scales_ref[...], shift_ref, weight_ref,
        bias_ref,
    )
    cols = span // ROWS_OF_TILE
    query_code = query_codes(info, info.tile(), span, cols)
    peak = jnp.full((span, 1), LOWEST, F32)
    scores = []
    for masks, key_ref in zip(groups, key_refs):
        codes = key_codes(info, masks, span, cols)
        scores.append(scores_of(queries, key_ref[...], codes, query_code))
        peak = jnp.maximum(peak, jnp.max(scores[-1], axis=1, keepdims=True) + constant)
    denominator, total = 0.0, 0.0
    for part, key_ref in zip(scores, key_refs):
        weights = jnp.exp2(part - (peak - constant))
        denominator = denominator + jnp.sum(weights, axis=1, keepdims=True)
        total = total + jnp.dot(
            weights.astype(BF16), key_ref[...], preferred_element_type=F32
        )
    mean, level = mean_and_level(peak, denominator, total)
    mean_ref[...] = mean
    level_ref[...] = jnp.broadcast_to(level, level_ref.shape)


def diagonal(cols):
    return lax.broadcasted_iota(jnp.int32, (cols, LANES), 0) == lax.broadcasted_iota(
        jnp.int32, (cols, LANES), 1
    )


def finish_kernel(
    rows, info_ref, mean_ref, level_ref, received_ref, own_ref, triple_ref, triple_bias_ref,
    output_ref, output_bias_ref, out_ref, inner_ref, outer_ref,
):
    info = Info(info_ref, rows)
    row_count, cols, channels = out_ref.shape
    span = row_count * cols
    _, widths = info.window(info.tile() * row_count, row_count)
    received = received_ref[0:span, :].astype(F32)
    levels = received_ref[span:, 0:LANES].astype(F32)
    yours = []
    for r in range(row_count):
        level = levels[3 * r : 3 * r + 1] + levels[3 * r + 1 : 3 * r + 2]
        level = level + levels[3 * r + 2 : 3 * r + 3]
        yours.append(jnp.sum(jnp.where(diagonal(cols), level, 0.0), axis=1, keepdims=True))
    yours = jnp.concatenate(yours, axis=0)
    mine = level_ref[:, 0:1]
    peak = jnp.maximum(mine, yours)
    weight, other_weight = jnp.exp2(mine - peak), jnp.exp2(yours - peak)
    share = weight / (weight + other_weight)
    mean_cell = (mean_ref[...] * share + received * (1.0 - share)).astype(BF16)
    mixed = (
        jnp.dot(mean_cell, triple_ref[:, 2 * channels :], preferred_element_type=F32)
        + triple_bias_ref[:, 2 * channels :]
    ).astype(BF16)
    attended = jnp.dot(mixed, output_ref[...], preferred_element_type=F32) + output_bias_ref[...]
    column = lax.broadcasted_iota(jnp.int32, (cols, 1), 0)
    for r, before in enumerate(split_rows(own_ref)):
        value = before + attended[r * cols : (r + 1) * cols]
        value = jnp.where(column < widths[r], value, 0.0)
        out_ref[r] = value.astype(BF16)
        if r == 0:
            top = value
    odd = lax.rem(info.tile(), 2) == 1
    inner_ref[0] = jnp.where(odd, top, value).astype(BF16)
    outer_ref[0] = jnp.where(odd, value, top).astype(BF16)


def fold_kernel(weight_ref, out_ref):
    channels = weight_ref.shape[-1]
    wide = [[weight_ref[a, b].astype(F32) for b in range(3)] for a in range(3)]

    def both(upper, lower):
        return [x + y for x, y in zip(upper, lower)]

    phases = [[wide[0], both(wide[1], wide[2])], [both(wide[0], wide[1]), wide[2]]]
    for down in range(2):
        for tap in range(2):
            left, middle, right = phases[down][tap]
            out_ref[down, tap, 0, :, 0:channels] = left.astype(BF16)
            out_ref[down, tap, 0, :, channels:] = (middle + right).astype(BF16)
            out_ref[down, tap, 1, :, 0:channels] = (left + middle).astype(BF16)
            out_ref[down, tap, 1, :, channels:] = right.astype(BF16)


def spread_columns(wide_ref, value, row, right):
    cols, channels = value.shape
    for part in range(wide_ref.shape[0]):
        lo, hi = part * LANES, min((part + 1) * LANES, channels)
        piece = value[:, lo:hi]
        if hi - lo < LANES:
            piece = jnp.concatenate([piece, jnp.zeros((cols, LANES - hi + lo), F32)], axis=1)
        wide_ref[part, row, pl.ds(right, cols, 2), :] = piece


def write_turned(out_ref, row, part, value, width):
    channels, cols = out_ref.shape[1:]
    lo, hi = part * LANES, min((part + 1) * LANES, channels)
    turned = value.T[0 : hi - lo, 0:cols]
    column = lax.broadcasted_iota(jnp.int32, (1, cols), 1)
    out_ref[row, lo:hi, :] = jnp.where(column < width, turned, 0.0).astype(BF16)


def phase_product(columns, weight):
    return lax.dot_general(
        columns, weight, (((1,), (1,)), ((), ())), preferred_element_type=F32
    )


def upsample_kernel(
    rows, info_ref, own_ref, weight_ref, bias_ref, out_ref, open_ref, columns_ref, wide_ref
):
    info = Info(info_ref, rows)
    row_count, cols, channels = own_ref.shape
    padded = columns_ref.shape[0] // row_count
    parts_out = wide_ref.shape[0]
    labels, widths = info.window(info.tile() * row_count, row_count)
    build_columns(
        columns_ref, [functools.partial(own_ref.__getitem__, r) for r in range(row_count)]
    )
    inner_rows = (row_count - 1) * padded
    for down in range(2):
        for right in range(2):
            lanes = slice(right * channels, (right + 2) * channels)
            same = phase_product(columns_ref[:, lanes], weight_ref[down, 1 - down, right])
            start = down * padded
            rim = phase_product(
                columns_ref[start : start + inner_rows, lanes], weight_ref[down, down, right]
            )
            for r in range(row_count):
                value = same[r * padded : r * padded + cols]
                near = r - 1 + 2 * down
                if 0 <= near < row_count:
                    lo = (near - down) * padded
                    value = value + jnp.where(
                        labels[near] == labels[r], rim[lo : lo + cols], 0.0
                    )
                spread_columns(wide_ref, value, 2 * r + down, right)
    for part in range(parts_out):
        open_ref[part, 0] = wide_ref[part, 0]
        open_ref[part, 1] = wide_ref[part, 2 * row_count - 1]
    for r in range(1, 2 * row_count - 1):
        for part in range(parts_out):
            value = wide_ref[part, r] + bias_ref[:, part * LANES : (part + 1) * LANES]
            write_turned(out_ref, r - 1, part, value, 2 * widths[r // 2])


def close_kernel(
    rows, info_ref, outer_ref, inner_ref, middle_ref, open_ref, weight_ref, bias_ref, out_ref,
    columns_ref, wide_ref,
):
    info = Info(info_ref, rows)
    wide_rows, _, wide_cols = out_ref.shape
    row_count, cols = wide_rows // 2, wide_cols // 2
    channels = outer_ref.shape[-1]
    padded = columns_ref.shape[0] // 2
    labels, widths = info.window(info.tile() * row_count - 1, row_count + 2)
    above, below = rims(info, outer_ref, inner_ref)
    build_columns(columns_ref, [lambda: above, lambda: below])
    for down in range(2):
        for right in range(2):
            lanes = slice(right * channels, (right + 2) * channels)
            rim = phase_product(
                columns_ref[down * padded : (down + 1) * padded, lanes],
                weight_ref[down, down, right],
            )
            spread_columns(wide_ref, rim[:cols], down, right)
    out_ref[1 : wide_rows - 1] = middle_ref[...]
    for down in range(2):
        rim_row, own_row = (row_count + 1, row_count) if down else (0, 1)
        for part in range(wide_ref.shape[0]):
            rim = jnp.where(labels[rim_row] == labels[own_row], wide_ref[part, down], 0.0)
            value = open_ref[part, down] + rim + bias_ref[:, part * LANES : (part + 1) * LANES]
            write_turned(
                out_ref, down * (wide_rows - 1), part, value, 2 * widths[own_row]
            )


def merge_stats(mine, other):
    count = mine[0] + other[0]
    safe = jnp.maximum(count, 1.0)
    off = other[1] - mine[1]
    mean = mine[1] + off * (other[0] / safe)
    spread = mine[2] + other[2] + off * off * (mine[0] * other[0] / safe)
    return jnp.stack([count, mean, spread])


def exchange(array, tiles, mask, among=None):
    moves = [(i, i ^ mask) for i in range(tiles) if among is None or among(i)]
    return lax.ppermute(array, "tile", moves)


def merge_round(stats, tiles, masks, tied=(), after=None):
    parts = [stats] + [exchange(stats, tiles, mask) for mask in masks]
    free = ()
    if tied:
        *parts[2:], free = lax.optimization_barrier((*parts[2:], after))
        parts[1], *tied = lax.optimization_barrier((parts[1], *tied))
    while len(parts) > 1:
        parts = [merge_stats(*parts[i : i + 2]) for i in range(0, len(parts), 2)]
    return (parts[0], *tied, free) if tied else parts[0]


def merge_masks(tiles):
    bits = [1 << i for i in range(tiles.bit_length() - 1)]
    pairs = [bits[i : i + 2] for i in range(0, len(bits), 2)]
    return [[p[0], p[1], p[0] ^ p[1]] if len(p) == 2 else p for p in pairs]


def shards(
    tiles,
    frames,
    latents,
    row_video,
    video_cols,
    first_gain,
    first_shift,
    conv_weight,
    conv_bias,
    second_gain,
    second_shift,
    triple_weight,
    triple_bias,
    output_weight,
    output_bias,
    upsample_weight,
    upsample_bias,
):
    row_count, frame_count, cols, channels = latents.shape
    assert frame_count == 1 and row_count == ROWS_OF_TILE and tiles % 4 == 0
    out_channels = upsample_weight.shape[-1]
    rows = row_count * tiles
    cells = row_count * cols
    padded = -(-(cols + 1) // 16) * 16
    near_rows = row_count + 2
    source = latents.reshape(row_count, cols, channels)
    tile = lax.axis_index("tile").astype(jnp.int32)
    info = jnp.concatenate([jnp.reshape(tile, (1,)), row_video, video_cols])

    def row(vector):
        return vector.reshape(1, -1)

    def shape(*dims, dtype=BF16):
        return jax.ShapeDtypeStruct(dims, dtype)

    def call(kernel, operands, out_shape, scratch=(), **kwargs):
        many = isinstance(out_shape, tuple)
        return pl.pallas_call(
            kernel,
            out_shape=out_shape,
            in_specs=[SMEM_SPEC] + [VMEM_SPEC] * len(operands),
            out_specs=(VMEM_SPEC,) * len(out_shape) if many else VMEM_SPEC,
            scratch_shapes=list(scratch),
            compiler_params=params(),
            **kwargs,
        )(info, *operands)

    outer_moves = [(i, i - 1 if i % 2 == 0 else i + 1) for i in range(tiles)]
    outer_moves = [(i, j) for i, j in outer_moves if 0 <= j < tiles]
    odd = tile % 2 == 1
    stats_shape = shape(3, SLOTS, LANES, dtype=F32)
    stats = call(
        functools.partial(stats_kernel, rows), [source], stats_shape,
        cost_estimate=cost(1.5), name="first_stats",
    )
    outer = lax.ppermute(
        jnp.where(odd, source[row_count - 1 :], source[:1]), "tile", outer_moves
    )
    inner = exchange(jnp.where(odd, source[:1], source[row_count - 1 :]), tiles, 1)
    stats, outer, inner = lax.optimization_barrier((stats, outer, inner))
    taps = min(3, frames)
    held = pl.pallas_call(
        functools.partial(hold_kernel, taps),
        out_shape=shape(3 * taps * channels, 3 * channels),
        in_specs=[HBM_SPEC],
        out_specs=VMEM_SPEC,
        scratch_shapes=[pltpu.SemaphoreType.DMA((3, 3 * taps))],
        compiler_params=pltpu.CompilerParams(vmem_limit_bytes=HOLD_VMEM_BYTES),
        cost_estimate=cost(1.5 * taps),
        name="hold",
    )(conv_weight)
    rounds = merge_masks(tiles)
    for index, masks in enumerate(reversed(rounds)):
        stats = merge_round(stats, tiles, masks)
        if index == len(rounds) - 2:
            stats, held = lax.optimization_barrier((stats, held))
    hidden, source = call(
        functools.partial(hidden_kernel, rows),
        [outer, inner, source, stats, row(first_gain), row(first_shift)],
        (shape(near_rows, padded, channels), shape(row_count, cols, channels)),
        cost_estimate=cost(1.3),
        name="hidden",
    )

    earlier = [
        lax.ppermute(hidden, "frame", [(i, i + by) for i in range(frames - by)])
        for by in range(1, taps)
    ]
    pairs = row_count // 2
    pair_shape = shape(pairs, 2 * cols, channels)
    product = call(
        functools.partial(own_conv_kernel, rows),
        [hidden, held],
        shape(row_count * padded, 3 * channels, dtype=F32),
        scratch=[pltpu.VMEM((row_count * padded, 3 * channels), BF16)],
        cost_estimate=cost(2.2),
        name="own_conv",
    )
    scratch = [pltpu.VMEM((row_count * padded, 3 * (taps - 1) * channels), BF16)]
    own, stats = call(
        functools.partial(conv_kernel, rows, taps),
        earlier + [product, source, row(conv_bias), held],
        (pair_shape, stats_shape),
        scratch=scratch if taps > 1 else [],
        cost_estimate=cost(1.5 + 2.0 * (taps - 1)),
        name="conv",
    )

    blocks = {0: own}
    neighbour = [(i, i ^ 1) for i in range(tiles)]
    if tiles == 16 and video_cols.shape[0] == 2:
        def middle(t):
            return t // 4 in (1, 2)

        stats = merge_round(stats, tiles, rounds[1])
        blocks[2] = exchange(own, tiles, 4)
        blocks[6] = exchange(own, tiles, 12, middle)
        stats, blocks[2], blocks[6], own_xy = merge_round(
            stats, tiles, rounds[0], (blocks[2], blocks[6]), own
        )
        inward = exchange(blocks[2], tiles, 12, middle)
        outward = exchange(blocks[6], tiles, 4, middle)
        other = exchange(own_xy, tiles, 1)
        blocks[1] = exchange(own_xy, tiles, 2)
        blocks[4] = jnp.where((tile // 4 == 1) | (tile // 4 == 2), inward, outward)
        passed, blocks[4] = lax.optimization_barrier((blocks[1], blocks[4]))
        blocks[5] = exchange(blocks[4], tiles, 2)
        blocks[3] = exchange(passed, tiles, 4)
        blocks[7] = exchange(passed, tiles, 12, middle)
        groups = [[0, 1, 2, 6], [4, 7, 3, 5]]
    else:
        for masks in rounds:
            stats = merge_round(stats, tiles, masks)
        other = exchange(own, tiles, 1)
        for mask in range(1, tiles // 2):
            blocks[mask] = exchange(own, tiles, 2 * mask)
        groups = [list(range(i, i + 4)) for i in range(0, tiles // 2, 4)]
    gain, shift = row(second_gain), row(second_shift)
    table_shape = shape(SLOTS, channels, dtype=F32)
    queries, constant, means, scales = call(
        functools.partial(query_kernel, rows),
        [other, stats, gain, shift, triple_weight, row(triple_bias)],
        (shape(cells, channels), shape(cells, LANES, dtype=F32), table_shape, table_shape),
        cost_estimate=cost(1.5),
        name="queries",
    )
    level_shape = shape(cells, LANES, dtype=F32)
    total_shape = shape(cells, channels, dtype=F32)
    state, keys = (), []
    for index, masks in enumerate(groups):
        last = index == len(groups) - 1
        outs = (shape(len(masks) * cells, channels),)
        outs += (shape(cells + 16, channels),) if last else (level_shape, level_shape, total_shape)
        normed, *state = call(
            functools.partial(attend_yours_kernel, rows, tuple(masks), index == 0, last),
            [means, scales, shift, queries, constant] + [blocks[m] for m in masks] + list(state),
            outs,
            cost_estimate=cost(0.9 * len(masks)),
            name="attend_yours",
        )
        keys.append(normed)
    (sent,) = state
    received = lax.ppermute(sent, "tile", neighbour)
    sent, own_late, upsample_weight = lax.optimization_barrier((sent, own, upsample_weight))
    mean, level = call(
        functools.partial(attend_mine_kernel, rows, tuple(tuple(masks) for masks in groups)),
        [own_late, means, scales, shift, triple_weight, row(triple_bias)] + keys,
        (total_shape, level_shape),
        cost_estimate=cost(6.0),
        name="attend_mine",
    )
    folded = pl.pallas_call(
        fold_kernel,
        out_shape=shape(2, 2, 2, out_channels, 2 * channels),
        in_specs=[VMEM_SPEC],
        out_specs=VMEM_SPEC,
        compiler_params=params(),
        cost_estimate=cost(0.5),
        name="fold",
    )(jnp.swapaxes(upsample_weight, 2, 3))

    rim_shape = shape(1, cols, channels)
    attended, inner, outer = call(
        functools.partial(finish_kernel, rows),
        [
            mean, level, received, own, triple_weight, row(triple_bias), output_weight,
            row(output_bias),
        ],
        (shape(row_count, cols, channels), rim_shape, rim_shape),
        cost_estimate=cost(1.4),
        name="finish",
    )
    outer = lax.ppermute(outer, "tile", outer_moves)
    inner = exchange(inner, tiles, 1)
    parts_out = -(-out_channels // LANES)
    wide_cols = -(-2 * cols // LANES) * LANES
    wide_bias = jnp.pad(row(upsample_bias), ((0, 0), (0, -out_channels % LANES)))
    middle, open_rows = call(
        functools.partial(upsample_kernel, rows),
        [attended, folded, wide_bias],
        (
            shape(2 * row_count - 2, out_channels, 2 * cols),
            shape(parts_out, 2, wide_cols, LANES, dtype=F32),
        ),
        scratch=[
            pltpu.VMEM((row_count * padded, 3 * channels), BF16),
            pltpu.VMEM((parts_out, 2 * row_count, wide_cols, LANES), F32),
        ],
        cost_estimate=cost(2.0),
        name="upsample",
    )
    decoded = call(
        functools.partial(close_kernel, rows),
        [outer, inner, middle, open_rows, folded, wide_bias],
        shape(2 * row_count, out_channels, 2 * cols),
        scratch=[
            pltpu.VMEM((2 * padded, 3 * channels), BF16),
            pltpu.VMEM((parts_out, 2, wide_cols, LANES), F32),
        ],
        cost_estimate=cost(1.0),
        name="close",
    )
    return jnp.swapaxes(decoded, 1, 2).reshape(2 * row_count, 1, 2 * cols, out_channels)


def solution(mesh):
    sizes = dict(mesh.shape)
    in_specs = (P("tile", "frame", None, None),) + (P(),) * 14
    out_specs = P("tile", "frame", None, None)
    body = functools.partial(shards, sizes["tile"], sizes["frame"])
    return jax.shard_map(body, mesh=mesh, in_specs=in_specs, out_specs=out_specs, check_vma=False)
```

```python
import functools
import math

import jax
import jax.numpy as jnp
from jax import lax
from jax.experimental import pallas as pl
from jax.experimental.pallas import tpu as pltpu
from jax.sharding import PartitionSpec as P

GROUPS = 32
EPSILON = 1e-05
MASKED = -1e30
LOWEST = -5e29
HIGHEST = lax.Precision.HIGHEST
SLOTS = 8
ROWS_OF_TILE = 4
LANES = 128
VMEM_BYTES = 24 * 1024 * 1024
HOLD_VMEM_BYTES = 46 * 1024 * 1024
F32 = jnp.float32
BF16 = jnp.bfloat16

SMEM_SPEC = pl.BlockSpec(memory_space=pltpu.SMEM)
VMEM_SPEC = pl.BlockSpec(memory_space=pltpu.VMEM)
HBM_SPEC = pl.BlockSpec(memory_space=pltpu.HBM)


def cost(microseconds):
    return pl.CostEstimate(
        flops=int(microseconds * 1.1e9), bytes_accessed=0, transcendentals=0
    )


def params():
    return pltpu.CompilerParams(vmem_limit_bytes=VMEM_BYTES)


def member_matrix(channels):
    per_group = channels // GROUPS
    group = lax.broadcasted_iota(jnp.int32, (LANES, channels), 0) * per_group
    channel = lax.broadcasted_iota(jnp.int32, (LANES, channels), 1)
    return jnp.where((channel >= group) & (channel < group + per_group), 1.0, 0.0).astype(F32)


def to_groups(values, member):
    return lax.dot_general(
        values, member, (((1,), (1,)), ((), ())), precision=HIGHEST, preferred_element_type=F32
    )


def to_channels(values, member):
    return jnp.dot(values, member, precision=HIGHEST, preferred_element_type=F32)


class Info:
    def __init__(self, ref, rows):
        self.ref, self.rows = ref, rows
        self.videos = ref.shape[0] - 2 - rows

    def tile(self):
        return self.ref[0]

    def frame(self):
        return self.ref[1]

    def label(self, row):
        inside = (row >= 0) & (row < self.rows)
        return jnp.where(inside, self.ref[2 + jnp.clip(row, 0, self.rows - 1)], -1)

    def width(self, label):
        return jnp.where(label >= 0, self.ref[2 + self.rows + jnp.maximum(label, 0)], 0)

    def window(self, first, count):
        labels = [self.label(first + r) for r in range(count)]
        return labels, [self.width(label) for label in labels]


def pick(table, label, videos):
    chosen = table[0:1]
    for video in range(1, videos):
        chosen = jnp.where(label == video, table[video : video + 1], chosen)
    return chosen


def norm_tables(stats_ref, gain_ref):
    member = member_matrix(gain_ref.shape[1])
    counts = jnp.maximum(stats_ref[0], 1.0)
    scale = lax.rsqrt(stats_ref[2] / counts + EPSILON)
    return to_channels(stats_ref[1], member), to_channels(scale, member) * gain_ref[...]


def write_stats(out_ref, rows, labels, widths, videos, channels):
    member = member_matrix(channels)
    per_group = channels // GROUPS
    cols = rows[0].shape[0]
    slot = lax.broadcasted_iota(jnp.int32, (SLOTS, 1), 0)
    column = lax.broadcasted_iota(jnp.int32, (cols, 1), 0)
    sums = jnp.zeros((SLOTS, channels), F32)
    counts = jnp.zeros((SLOTS, 1), F32)
    for index, row in enumerate(rows):
        sums = jnp.where(slot == index, jnp.sum(row, axis=0, keepdims=True), sums)
        counts = jnp.where(slot == index, (widths[index] * per_group).astype(F32), counts)
    means = to_groups(sums, member) / jnp.maximum(counts, 1.0)
    means_wide = to_channels(means, member)
    squares = jnp.zeros((SLOTS, channels), F32)
    for index, row in enumerate(rows):
        centered = jnp.where(column < widths[index], row - means_wide[index : index + 1], 0.0)
        squares = jnp.where(
            slot == index, jnp.sum(centered * centered, axis=0, keepdims=True), squares
        )
    spreads = to_groups(squares, member)
    out_ref[...] = jnp.zeros(out_ref.shape, F32)
    for video in range(videos):
        total = jnp.zeros((1, LANES), F32)
        count = jnp.zeros((1, LANES), F32)
        for index in range(len(rows)):
            mine = labels[index] == video
            row_count = counts[index : index + 1]
            total = total + jnp.where(mine, means[index : index + 1] * row_count, 0.0)
            count = count + jnp.where(mine, row_count, 0.0)
        mean = total / jnp.maximum(count, 1.0)
        spread = jnp.zeros((1, LANES), F32)
        for index in range(len(rows)):
            off = means[index : index + 1] - mean
            part = spreads[index : index + 1] + counts[index : index + 1] * off * off
            spread = spread + jnp.where(labels[index] == video, part, 0.0)
        out_ref[0, video : video + 1, :] = count
        out_ref[1, video : video + 1, :] = mean
        out_ref[2, video : video + 1, :] = spread


def build_columns(columns_ref, row_refs):
    padded = columns_ref.shape[0] // len(row_refs)
    for index, row in enumerate(row_refs):
        cells = row().astype(F32)
        count, channels = cells.shape
        cells = jnp.concatenate([cells, jnp.zeros((padded - count, channels), F32)], axis=0)
        start = index * padded
        columns_ref[start : start + padded, 0:channels] = pltpu.roll(cells, 1, 0).astype(BF16)
        columns_ref[start : start + padded, channels : 2 * channels] = cells.astype(BF16)
        columns_ref[start : start + padded, 2 * channels : 3 * channels] = pltpu.roll(
            cells, padded - 1, 0
        ).astype(BF16)


def stats_kernel(rows, info_ref, latents_ref, out_ref):
    info = Info(info_ref, rows)
    row_count, cols, channels = latents_ref.shape
    labels, widths = info.window(info.tile() * row_count, row_count)
    column = lax.broadcasted_iota(jnp.int32, (cols, 1), 0)
    cells = [
        jnp.where(column < widths[r], latents_ref[r].astype(F32), 0.0) for r in range(row_count)
    ]
    write_stats(out_ref, cells, labels, widths, info.videos, channels)


def rims(info, outer_ref, inner_ref):
    odd = lax.rem(info.tile(), 2) == 1
    inner, outer = inner_ref[0].astype(F32), outer_ref[0].astype(F32)
    return jnp.where(odd, inner, outer), jnp.where(odd, outer, inner)


def hidden_kernel(
    rows, info_ref, outer_ref, inner_ref, latents_ref, stats_ref, gain_ref, shift_ref, out_ref,
    source_ref,
):
    info = Info(info_ref, rows)
    row_count, cols, _ = latents_ref.shape
    labels, widths = info.window(info.tile() * row_count - 1, row_count + 2)
    means, scales = norm_tables(stats_ref, gain_ref)
    column = lax.broadcasted_iota(jnp.int32, (cols, 1), 0)
    above, below = rims(info, outer_ref, inner_ref)
    sources = [above] + [latents_ref[r].astype(F32) for r in range(row_count)] + [below]
    for r, source in enumerate(sources):
        mean = pick(means, labels[r], info.videos)
        scale = pick(scales, labels[r], info.videos)
        normed = (source - mean) * scale + shift_ref[...]
        active = normed / (1.0 + jnp.exp(-normed))
        active = jnp.where(column < widths[r], active, 0.0)
        rest = jnp.zeros((out_ref.shape[1] - cols, active.shape[1]), F32)
        out_ref[r] = jnp.concatenate([active, rest], axis=0).astype(BF16)
    source_ref[...] = latents_ref[...]


def hold_kernel(taps, weight_ref, held_ref, sems):
    channels = weight_ref.shape[-1]
    copies = [
        pltpu.make_async_copy(
            weight_ref.at[2 - depth // 3, depth % 3, side],
            held_ref.at[pl.ds(depth * channels, channels), pl.ds(side * channels, channels)],
            sems.at[side, depth],
        )
        for side in range(3)
        for depth in range(3 * taps)
    ]
    for copy in copies:
        copy.start()
    for copy in copies:
        copy.wait()


def row_taps(info, hidden_refs, inputs_ref):
    near_rows, padded, channels = hidden_refs[0].shape
    row_count = near_rows - 2
    labels, _ = info.window(info.tile() * row_count - 1, near_rows)
    for back, hidden_ref in enumerate(hidden_refs):
        for tap in range(3):
            lanes = slice((3 * back + tap) * channels, (3 * back + tap + 1) * channels)
            for r in range(row_count):
                block = hidden_ref[r + tap]
                if tap != 1:
                    same = labels[r + tap] == labels[r + 1]
                    block = jnp.where(same, block, jnp.zeros_like(block))
                inputs_ref[r * padded : (r + 1) * padded, lanes] = block


def own_conv_kernel(rows, info_ref, hidden_ref, held_ref, product_ref, inputs_ref):
    row_taps(Info(info_ref, rows), [hidden_ref], inputs_ref)
    depth = inputs_ref.shape[1]
    product_ref[...] = jnp.dot(
        inputs_ref[...], held_ref[0:depth, :], preferred_element_type=F32
    )


def conv_kernel(rows, taps, info_ref, *rest):
    hidden_refs, rest = rest[: taps - 1], rest[taps - 1 :]
    product_ref, latents_ref, bias_ref, held_ref, own_ref, stats_ref, *rest = rest
    branch_ref, inputs_refs = rest[0], rest[1:]
    row_count, cols, channels = latents_ref.shape
    info = Info(info_ref, rows)
    padded = product_ref.shape[0] // row_count
    labels, widths = info.window(info.tile() * row_count - 1, row_count + 2)
    for active in range(taps):
        frame = info.frame()

        @pl.when(frame == active if active < taps - 1 else frame >= active)
        def _(active=active):
            product = product_ref[...]
            if active:
                depth = 3 * active * channels
                row_taps(info, hidden_refs[:active], inputs_refs[0])
                product = product + jnp.dot(
                    inputs_refs[0][:, 0:depth],
                    held_ref[3 * channels : 3 * channels + depth, :],
                    preferred_element_type=F32,
                )
            for r in range(row_count):
                lines = slice(r * padded, (r + 1) * padded)
                branch = pltpu.roll(product[lines, 0:channels], 1, 0)
                branch = branch + product[lines, channels : 2 * channels]
                branch = branch + pltpu.roll(product[lines, 2 * channels :], padded - 1, 0)
                branch_ref[r] = branch[:cols]

    column = lax.broadcasted_iota(jnp.int32, (cols, 1), 0)
    cells = []
    for r in range(row_count):
        value = latents_ref[r].astype(F32) + branch_ref[r] + bias_ref[...]
        value = jnp.where(column < widths[r + 1], value, 0.0).astype(BF16)
        cells.append(value.astype(F32))
    for pair in range(row_count // 2):
        own_ref[pair] = jnp.concatenate(cells[2 * pair : 2 * pair + 2], axis=0).astype(BF16)
    write_stats(stats_ref, cells, labels[1:-1], widths[1:-1], info.videos, channels)


def split_rows(pairs_ref):
    cols = pairs_ref.shape[1] // 2
    cells = []
    for pair in range(pairs_ref.shape[0]):
        both = pairs_ref[pair].astype(F32)
        cells += [both[:cols], both[cols:]]
    return cells


def turned_queries(info, tile, pairs_ref, means, scales, shift_ref, weight_ref, bias_ref):
    pairs, double, channels = pairs_ref.shape
    cols = double // 2
    column = lax.broadcasted_iota(jnp.int32, (cols, 1), 0)
    labels, widths = info.window(tile * 2 * pairs, 2 * pairs)
    cells = []
    for r, values in enumerate(split_rows(pairs_ref)):
        mean = pick(means, labels[r], info.videos)
        scale = pick(scales, labels[r], info.videos)
        normed = (values - mean) * scale + shift_ref[...]
        cells.append(jnp.where(column < widths[r], normed, 0.0))
    cells = jnp.concatenate(cells, axis=0).astype(BF16)
    queries = (
        jnp.dot(cells, weight_ref[:, 0:channels], preferred_element_type=F32)
        + bias_ref[:, 0:channels]
    ).astype(BF16)
    factor = channels ** (-0.5) * math.log2(math.e)
    turned = lax.dot_general(
        queries, weight_ref[:, channels : 2 * channels], (((1,), (1,)), ((), ())),
        preferred_element_type=F32,
    )
    constant = jnp.sum(
        queries.astype(F32) * bias_ref[:, channels : 2 * channels], axis=1, keepdims=True
    )
    return (turned * factor).astype(BF16), constant * factor


def query_kernel(
    rows, info_ref, other_ref, stats_ref, gain_ref, shift_ref, weight_ref, bias_ref, queries_ref,
    constant_ref, means_ref, scales_ref,
):
    info = Info(info_ref, rows)
    means, scales = norm_tables(stats_ref, gain_ref)
    means_ref[...] = means
    scales_ref[...] = scales
    queries, constant = turned_queries(
        info, info.tile() ^ 1, other_ref, means, scales, shift_ref, weight_ref, bias_ref
    )
    queries_ref[...] = queries
    constant_ref[...] = jnp.broadcast_to(constant, constant_ref.shape)


def key_codes(info, masks, span, cols):
    row_count = span // cols
    position = lax.broadcasted_iota(jnp.int32, (1, len(masks) * span), 1)
    codes = jnp.full((1, len(masks) * span), -2.0, F32)
    for index, mask in enumerate(masks):
        near, widths = info.window((info.tile() ^ (2 * mask)) * row_count, row_count)
        for r in range(row_count):
            start = index * span + r * cols
            inside = (position >= start) & (position < start + widths[r])
            codes = jnp.where(inside, near[r].astype(F32), codes)
    return codes


def query_codes(info, tile, span, cols):
    row_count = span // cols
    labels, _ = info.window(tile * row_count, row_count)
    return jnp.concatenate(
        [jnp.zeros((cols, 1), F32) + label.astype(F32) for label in labels], axis=0
    )


def scores_of(queries, keys, codes, query_code):
    scores = lax.dot_general(
        queries, keys, (((1,), (1,)), ((), ())), preferred_element_type=F32
    )
    return jnp.where(codes == query_code, scores, MASKED)


def mean_and_level(peak, denominator, total):
    some = denominator > 0.0
    safe = jnp.where(some, denominator, 1.0)
    return total / safe, jnp.where(some, peak + jnp.log2(safe), LOWEST)


def attend_yours_kernel(rows, masks, first, last, info_ref, *rest):
    means_ref, scales_ref, shift_ref, queries_ref, constant_ref, *rest = rest
    block_refs, rest = rest[: len(masks)], rest[len(masks) :]
    if not first:
        old_peak_ref, old_sum_ref, old_total_ref, *rest = rest
    keys_ref, *out_refs = rest
    info = Info(info_ref, rows)
    span, channels = queries_ref.shape
    pairs, double, _ = block_refs[0].shape
    cols = double // 2
    row_count = 2 * pairs
    tile = info.tile()
    means, scales = means_ref[...], scales_ref[...]
    for index, (mask, block_ref) in enumerate(zip(masks, block_refs)):
        near, _ = info.window((tile ^ (2 * mask)) * row_count, row_count)
        for pair in range(pairs):
            both = block_ref[pair].astype(F32)
            halves = []
            for half in range(2):
                label = near[2 * pair + half]
                mean = pick(means, label, info.videos)
                scale = pick(scales, label, info.videos)
                values = both[half * cols : (half + 1) * cols]
                halves.append((values - mean) * scale + shift_ref[...])
            start = index * span + pair * double
            keys_ref[start : start + double, :] = jnp.concatenate(halves, axis=0).astype(BF16)
    constant = constant_ref[:, 0:1]
    scores = scores_of(
        queries_ref[...], keys_ref[...], key_codes(info, masks, span, cols),
        query_codes(info, tile ^ 1, span, cols),
    )
    peak = jnp.maximum(LOWEST, jnp.max(scores, axis=1, keepdims=True) + constant)
    if not first:
        largest = old_peak_ref[:, 0:1]
        peak = jnp.maximum(largest, peak)
    weights = jnp.exp2(scores - (peak - constant))
    denominator = jnp.sum(weights, axis=1, keepdims=True)
    total = jnp.dot(weights.astype(BF16), keys_ref[...], preferred_element_type=F32)
    if not first:
        factor = jnp.exp2(largest - peak)
        denominator = old_sum_ref[:, 0:1] * factor + denominator
        total = old_total_ref[...] * factor + total
    if not last:
        peak_ref, sum_ref, total_ref = out_refs
        peak_ref[...] = jnp.broadcast_to(peak, peak_ref.shape)
        sum_ref[...] = jnp.broadcast_to(denominator, sum_ref.shape)
        total_ref[...] = total
        return
    (sent_ref,) = out_refs
    mean, level = mean_and_level(peak, denominator, total)
    sent_ref[0:span, :] = mean.astype(BF16)
    slots = sent_ref.shape[0] - span
    slot = lax.broadcasted_iota(jnp.int32, (slots, 1), 0)
    packed = jnp.zeros((slots, LANES), F32)
    for r in range(row_count):
        left = level[r * cols : (r + 1) * cols]
        left = jnp.sum(jnp.where(diagonal(cols), left, 0.0), axis=0, keepdims=True)
        for part in range(3):
            rounded = left.astype(BF16).astype(F32)
            packed = jnp.where(slot == 3 * r + part, rounded, packed)
            left = left - rounded
    sent_ref[span:, 0:LANES] = packed.astype(BF16)
    sent_ref[span:, LANES:] = jnp.zeros((slots, channels - LANES), BF16)


def attend_mine_kernel(
    rows, groups, info_ref, own_ref, means_ref, scales_ref, shift_ref, weight_ref, bias_ref, *rest
):
    key_refs, (mean_ref, level_ref) = rest[: len(groups)], rest[len(groups) :]
    info = Info(info_ref, rows)
    span = mean_ref.shape[0]
    queries, constant = turned_queries(
        info, info.tile(), own_ref, means_ref[...], scales_ref[...], shift_ref, weight_ref,
        bias_ref,
    )
    cols = span // ROWS_OF_TILE
    query_code = query_codes(info, info.tile(), span, cols)
    peak = jnp.full((span, 1), LOWEST, F32)
    scores = []
    for masks, key_ref in zip(groups, key_refs):
        codes = key_codes(info, masks, span, cols)
        scores.append(scores_of(queries, key_ref[...], codes, query_code))
        peak = jnp.maximum(peak, jnp.max(scores[-1], axis=1, keepdims=True) + constant)
    denominator, total = 0.0, 0.0
    for part, key_ref in zip(scores, key_refs):
        weights = jnp.exp2(part - (peak - constant))
        denominator = denominator + jnp.sum(weights, axis=1, keepdims=True)
        total = total + jnp.dot(
            weights.astype(BF16), key_ref[...], preferred_element_type=F32
        )
    mean, level = mean_and_level(peak, denominator, total)
    mean_ref[...] = mean
    level_ref[...] = jnp.broadcast_to(level, level_ref.shape)


def diagonal(cols):
    return lax.broadcasted_iota(jnp.int32, (cols, LANES), 0) == lax.broadcasted_iota(
        jnp.int32, (cols, LANES), 1
    )


def finish_kernel(
    rows, info_ref, mean_ref, level_ref, received_ref, own_ref, triple_ref, triple_bias_ref,
    output_ref, output_bias_ref, out_ref, inner_ref, outer_ref,
):
    info = Info(info_ref, rows)
    row_count, cols, channels = out_ref.shape
    span = row_count * cols
    _, widths = info.window(info.tile() * row_count, row_count)
    received = received_ref[0:span, :].astype(F32)
    levels = received_ref[span:, 0:LANES].astype(F32)
    yours = []
    for r in range(row_count):
        level = levels[3 * r : 3 * r + 1] + levels[3 * r + 1 : 3 * r + 2]
        level = level + levels[3 * r + 2 : 3 * r + 3]
        yours.append(jnp.sum(jnp.where(diagonal(cols), level, 0.0), axis=1, keepdims=True))
    yours = jnp.concatenate(yours, axis=0)
    mine = level_ref[:, 0:1]
    peak = jnp.maximum(mine, yours)
    weight, other_weight = jnp.exp2(mine - peak), jnp.exp2(yours - peak)
    share = weight / (weight + other_weight)
    mean_cell = (mean_ref[...] * share + received * (1.0 - share)).astype(BF16)
    mixed = (
        jnp.dot(mean_cell, triple_ref[:, 2 * channels :], preferred_element_type=F32)
        + triple_bias_ref[:, 2 * channels :]
    ).astype(BF16)
    attended = jnp.dot(mixed, output_ref[...], preferred_element_type=F32) + output_bias_ref[...]
    column = lax.broadcasted_iota(jnp.int32, (cols, 1), 0)
    for r, before in enumerate(split_rows(own_ref)):
        value = before + attended[r * cols : (r + 1) * cols]
        value = jnp.where(column < widths[r], value, 0.0)
        out_ref[r] = value.astype(BF16)
        if r == 0:
            top = value
    odd = lax.rem(info.tile(), 2) == 1
    inner_ref[0] = jnp.where(odd, top, value).astype(BF16)
    outer_ref[0] = jnp.where(odd, value, top).astype(BF16)


def fold_kernel(weight_ref, out_ref):
    channels = weight_ref.shape[-1]
    wide = [[weight_ref[a, b].astype(F32) for b in range(3)] for a in range(3)]

    def both(upper, lower):
        return [x + y for x, y in zip(upper, lower)]

    phases = [[wide[0], both(wide[1], wide[2])], [both(wide[0], wide[1]), wide[2]]]
    for down in range(2):
        for tap in range(2):
            left, middle, right = phases[down][tap]
            out_ref[down, tap, 0, :, 0:channels] = left.astype(BF16)
            out_ref[down, tap, 0, :, channels:] = (middle + right).astype(BF16)
            out_ref[down, tap, 1, :, 0:channels] = (left + middle).astype(BF16)
            out_ref[down, tap, 1, :, channels:] = right.astype(BF16)


def spread_columns(wide_ref, value, row, right):
    cols, channels = value.shape
    for part in range(wide_ref.shape[0]):
        lo, hi = part * LANES, min((part + 1) * LANES, channels)
        piece = value[:, lo:hi]
        if hi - lo < LANES:
            piece = jnp.concatenate([piece, jnp.zeros((cols, LANES - hi + lo), F32)], axis=1)
        wide_ref[part, row, pl.ds(right, cols, 2), :] = piece


def write_turned(out_ref, row, part, value, width):
    channels, cols = out_ref.shape[1:]
    lo, hi = part * LANES, min((part + 1) * LANES, channels)
    turned = value.T[0 : hi - lo, 0:cols]
    column = lax.broadcasted_iota(jnp.int32, (1, cols), 1)
    out_ref[row, lo:hi, :] = jnp.where(column < width, turned, 0.0).astype(BF16)


def phase_product(columns, weight):
    return lax.dot_general(
        columns, weight, (((1,), (1,)), ((), ())), preferred_element_type=F32
    )


def upsample_kernel(
    rows, info_ref, own_ref, weight_ref, bias_ref, out_ref, open_ref, columns_ref, wide_ref
):
    info = Info(info_ref, rows)
    row_count, cols, channels = own_ref.shape
    padded = columns_ref.shape[0] // row_count
    parts_out = wide_ref.shape[0]
    labels, widths = info.window(info.tile() * row_count, row_count)
    build_columns(
        columns_ref, [functools.partial(own_ref.__getitem__, r) for r in range(row_count)]
    )
    inner_rows = (row_count - 1) * padded
    for down in range(2):
        for right in range(2):
            lanes = slice(right * channels, (right + 2) * channels)
            same = phase_product(columns_ref[:, lanes], weight_ref[down, 1 - down, right])
            start = down * padded
            rim = phase_product(
                columns_ref[start : start + inner_rows, lanes], weight_ref[down, down, right]
            )
            for r in range(row_count):
                value = same[r * padded : r * padded + cols]
                near = r - 1 + 2 * down
                if 0 <= near < row_count:
                    lo = (near - down) * padded
                    value = value + jnp.where(
                        labels[near] == labels[r], rim[lo : lo + cols], 0.0
                    )
                spread_columns(wide_ref, value, 2 * r + down, right)
    for part in range(parts_out):
        open_ref[part, 0] = wide_ref[part, 0]
        open_ref[part, 1] = wide_ref[part, 2 * row_count - 1]
    for r in range(1, 2 * row_count - 1):
        for part in range(parts_out):
            value = wide_ref[part, r] + bias_ref[:, part * LANES : (part + 1) * LANES]
            write_turned(out_ref, r - 1, part, value, 2 * widths[r // 2])


def close_kernel(
    rows, info_ref, outer_ref, inner_ref, middle_ref, open_ref, weight_ref, bias_ref, out_ref,
    columns_ref, wide_ref,
):
    info = Info(info_ref, rows)
    wide_rows, _, wide_cols = out_ref.shape
    row_count, cols = wide_rows // 2, wide_cols // 2
    channels = outer_ref.shape[-1]
    padded = columns_ref.shape[0] // 2
    labels, widths = info.window(info.tile() * row_count - 1, row_count + 2)
    above, below = rims(info, outer_ref, inner_ref)
    build_columns(columns_ref, [lambda: above, lambda: below])
    for down in range(2):
        for right in range(2):
            lanes = slice(right * channels, (right + 2) * channels)
            rim = phase_product(
                columns_ref[down * padded : (down + 1) * padded, lanes],
                weight_ref[down, down, right],
            )
            spread_columns(wide_ref, rim[:cols], down, right)
    out_ref[1 : wide_rows - 1] = middle_ref[...]
    for down in range(2):
        rim_row, own_row = (row_count + 1, row_count) if down else (0, 1)
        for part in range(wide_ref.shape[0]):
            rim = jnp.where(labels[rim_row] == labels[own_row], wide_ref[part, down], 0.0)
            value = open_ref[part, down] + rim + bias_ref[:, part * LANES : (part + 1) * LANES]
            write_turned(
                out_ref, down * (wide_rows - 1), part, value, 2 * widths[own_row]
            )


def merge_stats(mine, other):
    count = mine[0] + other[0]
    safe = jnp.maximum(count, 1.0)
    off = other[1] - mine[1]
    mean = mine[1] + off * (other[0] / safe)
    spread = mine[2] + other[2] + off * off * (mine[0] * other[0] / safe)
    return jnp.stack([count, mean, spread])


def exchange(array, tiles, mask, among=None):
    moves = [(i, i ^ mask) for i in range(tiles) if among is None or among(i)]
    return lax.ppermute(array, "tile", moves)


def merge_round(stats, tiles, masks, tied=(), after=None):
    parts = [stats] + [exchange(stats, tiles, mask) for mask in masks]
    free = ()
    if tied:
        *parts[2:], free = lax.optimization_barrier((*parts[2:], after))
        parts[1], *tied = lax.optimization_barrier((parts[1], *tied))
    while len(parts) > 1:
        parts = [merge_stats(*parts[i : i + 2]) for i in range(0, len(parts), 2)]
    return (parts[0], *tied, free) if tied else parts[0]


def merge_masks(tiles):
    bits = [1 << i for i in range(tiles.bit_length() - 1)]
    pairs = [bits[i : i + 2] for i in range(0, len(bits), 2)]
    return [[p[0], p[1], p[0] ^ p[1]] if len(p) == 2 else p for p in pairs]


def shards(
    tiles,
    frames,
    latents,
    row_video,
    video_cols,
    first_gain,
    first_shift,
    conv_weight,
    conv_bias,
    second_gain,
    second_shift,
    triple_weight,
    triple_bias,
    output_weight,
    output_bias,
    upsample_weight,
    upsample_bias,
):
    row_count, frame_count, cols, channels = latents.shape
    assert frame_count == 1 and row_count == ROWS_OF_TILE and tiles % 4 == 0
    out_channels = upsample_weight.shape[-1]
    rows = row_count * tiles
    cells = row_count * cols
    padded = -(-(cols + 1) // 16) * 16
    near_rows = row_count + 2
    source = latents.reshape(row_count, cols, channels)
    tile = lax.axis_index("tile").astype(jnp.int32)
    frame = lax.axis_index("frame").astype(jnp.int32)
    info = jnp.concatenate([jnp.stack([tile, frame]), row_video, video_cols])

    def row(vector):
        return vector.reshape(1, -1)

    def shape(*dims, dtype=BF16):
        return jax.ShapeDtypeStruct(dims, dtype)

    def call(kernel, operands, out_shape, scratch=(), **kwargs):
        many = isinstance(out_shape, tuple)
        return pl.pallas_call(
            kernel,
            out_shape=out_shape,
            in_specs=[SMEM_SPEC] + [VMEM_SPEC] * len(operands),
            out_specs=(VMEM_SPEC,) * len(out_shape) if many else VMEM_SPEC,
            scratch_shapes=list(scratch),
            compiler_params=params(),
            **kwargs,
        )(info, *operands)

    outer_moves = [(i, i - 1 if i % 2 == 0 else i + 1) for i in range(tiles)]
    outer_moves = [(i, j) for i, j in outer_moves if 0 <= j < tiles]
    odd = tile % 2 == 1
    stats_shape = shape(3, SLOTS, LANES, dtype=F32)
    stats = call(
        functools.partial(stats_kernel, rows), [source], stats_shape,
        cost_estimate=cost(1.5), name="first_stats",
    )
    outer = lax.ppermute(
        jnp.where(odd, source[row_count - 1 :], source[:1]), "tile", outer_moves
    )
    inner = exchange(jnp.where(odd, source[:1], source[row_count - 1 :]), tiles, 1)
    stats, outer, inner = lax.optimization_barrier((stats, outer, inner))
    taps = min(3, frames)
    held = pl.pallas_call(
        functools.partial(hold_kernel, taps),
        out_shape=shape(3 * taps * channels, 3 * channels),
        in_specs=[HBM_SPEC],
        out_specs=VMEM_SPEC,
        scratch_shapes=[pltpu.SemaphoreType.DMA((3, 3 * taps))],
        compiler_params=pltpu.CompilerParams(vmem_limit_bytes=HOLD_VMEM_BYTES),
        cost_estimate=cost(1.5 * taps),
        name="hold",
    )(conv_weight)
    rounds = merge_masks(tiles)
    for index, masks in enumerate(reversed(rounds)):
        stats = merge_round(stats, tiles, masks)
        if index == len(rounds) - 2:
            stats, held = lax.optimization_barrier((stats, held))
    hidden, source = call(
        functools.partial(hidden_kernel, rows),
        [outer, inner, source, stats, row(first_gain), row(first_shift)],
        (shape(near_rows, padded, channels), shape(row_count, cols, channels)),
        cost_estimate=cost(1.3),
        name="hidden",
    )

    earlier = [
        lax.ppermute(hidden, "frame", [(i, i + by) for i in range(frames - by)])
        for by in range(1, taps)
    ]
    pairs = row_count // 2
    pair_shape = shape(pairs, 2 * cols, channels)
    product = call(
        functools.partial(own_conv_kernel, rows),
        [hidden, held],
        shape(row_count * padded, 3 * channels, dtype=F32),
        scratch=[pltpu.VMEM((row_count * padded, 3 * channels), BF16)],
        cost_estimate=cost(2.2),
        name="own_conv",
    )
    scratch = [pltpu.VMEM((row_count, cols, channels), F32)]
    if taps > 1:
        scratch.append(pltpu.VMEM((row_count * padded, 3 * (taps - 1) * channels), BF16))
    own, stats = call(
        functools.partial(conv_kernel, rows, taps),
        earlier + [product, source, row(conv_bias), held],
        (pair_shape, stats_shape),
        scratch=scratch,
        cost_estimate=cost(1.5 + 2.0 * (taps - 1)),
        name="conv",
    )

    blocks = {0: own}
    neighbour = [(i, i ^ 1) for i in range(tiles)]
    if tiles == 16 and video_cols.shape[0] == 2:
        def middle(t):
            return t // 4 in (1, 2)

        stats = merge_round(stats, tiles, rounds[1])
        blocks[2] = exchange(own, tiles, 4)
        blocks[6] = exchange(own, tiles, 12, middle)
        stats, blocks[2], blocks[6], own_xy = merge_round(
            stats, tiles, rounds[0], (blocks[2], blocks[6]), own
        )
        inward = exchange(blocks[2], tiles, 12, middle)
        outward = exchange(blocks[6], tiles, 4, middle)
        other = exchange(own_xy, tiles, 1)
        blocks[1] = exchange(own_xy, tiles, 2)
        blocks[4] = jnp.where((tile // 4 == 1) | (tile // 4 == 2), inward, outward)
        passed, blocks[4] = lax.optimization_barrier((blocks[1], blocks[4]))
        blocks[5] = exchange(blocks[4], tiles, 2)
        blocks[3] = exchange(passed, tiles, 4)
        blocks[7] = exchange(passed, tiles, 12, middle)
        groups = [[0, 1, 2, 6], [4, 7, 3, 5]]
    else:
        for masks in rounds:
            stats = merge_round(stats, tiles, masks)
        other = exchange(own, tiles, 1)
        for mask in range(1, tiles // 2):
            blocks[mask] = exchange(own, tiles, 2 * mask)
        groups = [list(range(i, i + 4)) for i in range(0, tiles // 2, 4)]
    gain, shift = row(second_gain), row(second_shift)
    table_shape = shape(SLOTS, channels, dtype=F32)
    queries, constant, means, scales = call(
        functools.partial(query_kernel, rows),
        [other, stats, gain, shift, triple_weight, row(triple_bias)],
        (shape(cells, channels), shape(cells, LANES, dtype=F32), table_shape, table_shape),
        cost_estimate=cost(1.5),
        name="queries",
    )
    level_shape = shape(cells, LANES, dtype=F32)
    total_shape = shape(cells, channels, dtype=F32)
    folded = pl.pallas_call(
        fold_kernel,
        out_shape=shape(2, 2, 2, out_channels, 2 * channels),
        in_specs=[VMEM_SPEC],
        out_specs=VMEM_SPEC,
        compiler_params=params(),
        cost_estimate=cost(0.5),
        name="fold",
    )(jnp.swapaxes(upsample_weight, 2, 3))
    state, keys = (), []
    for index, masks in enumerate(groups):
        last = index == len(groups) - 1
        outs = (shape(len(masks) * cells, channels),)
        outs += (shape(cells + 16, channels),) if last else (level_shape, level_shape, total_shape)
        normed, *state = call(
            functools.partial(attend_yours_kernel, rows, tuple(masks), index == 0, last),
            [means, scales, shift, queries, constant] + [blocks[m] for m in masks] + list(state),
            outs,
            cost_estimate=cost(0.9 * len(masks)),
            name="attend_yours",
        )
        keys.append(normed)
        if index == len(groups) - 2:
            *state, folded = lax.optimization_barrier((*state, folded))
    (sent,) = state
    received = lax.ppermute(sent, "tile", neighbour)
    sent, own_late = lax.optimization_barrier((sent, own))
    mean, level = call(
        functools.partial(attend_mine_kernel, rows, tuple(tuple(masks) for masks in groups)),
        [own_late, means, scales, shift, triple_weight, row(triple_bias)] + keys,
        (total_shape, level_shape),
        cost_estimate=cost(6.0),
        name="attend_mine",
    )
    rim_shape = shape(1, cols, channels)
    attended, inner, outer = call(
        functools.partial(finish_kernel, rows),
        [
            mean, level, received, own, triple_weight, row(triple_bias), output_weight,
            row(output_bias),
        ],
        (shape(row_count, cols, channels), rim_shape, rim_shape),
        cost_estimate=cost(1.4),
        name="finish",
    )
    outer = lax.ppermute(outer, "tile", outer_moves)
    inner = exchange(inner, tiles, 1)
    parts_out = -(-out_channels // LANES)
    wide_cols = -(-2 * cols // LANES) * LANES
    wide_bias = jnp.pad(row(upsample_bias), ((0, 0), (0, -out_channels % LANES)))
    middle, open_rows = call(
        functools.partial(upsample_kernel, rows),
        [attended, folded, wide_bias],
        (
            shape(2 * row_count - 2, out_channels, 2 * cols),
            shape(parts_out, 2, wide_cols, LANES, dtype=F32),
        ),
        scratch=[
            pltpu.VMEM((row_count * padded, 3 * channels), BF16),
            pltpu.VMEM((parts_out, 2 * row_count, wide_cols, LANES), F32),
        ],
        cost_estimate=cost(2.0),
        name="upsample",
    )
    decoded = call(
        functools.partial(close_kernel, rows),
        [outer, inner, middle, open_rows, folded, wide_bias],
        shape(2 * row_count, out_channels, 2 * cols),
        scratch=[
            pltpu.VMEM((2 * padded, 3 * channels), BF16),
            pltpu.VMEM((parts_out, 2, wide_cols, LANES), F32),
        ],
        cost_estimate=cost(1.0),
        name="close",
    )
    return jnp.swapaxes(decoded, 1, 2).reshape(2 * row_count, 1, 2 * cols, out_channels)


def solution(mesh):
    sizes = dict(mesh.shape)
    in_specs = (P("tile", "frame", None, None),) + (P(),) * 14
    out_specs = P("tile", "frame", None, None)
    body = functools.partial(shards, sizes["tile"], sizes["frame"])
    return jax.shard_map(body, mesh=mesh, in_specs=in_specs, out_specs=out_specs, check_vma=False)
```

```python
import functools
import math

import jax
import jax.numpy as jnp
from jax import lax
from jax.experimental import pallas as pl
from jax.experimental.pallas import tpu as pltpu
from jax.sharding import PartitionSpec as P

GROUPS = 32
EPSILON = 1e-05
MASKED = -1e30
LOWEST = -5e29
HIGHEST = lax.Precision.HIGHEST
SLOTS = 8
ROWS_OF_TILE = 4
LANES = 128
VMEM_BYTES = 24 * 1024 * 1024
HOLD_VMEM_BYTES = 46 * 1024 * 1024
F32 = jnp.float32
BF16 = jnp.bfloat16

SMEM_SPEC = pl.BlockSpec(memory_space=pltpu.SMEM)
VMEM_SPEC = pl.BlockSpec(memory_space=pltpu.VMEM)
HBM_SPEC = pl.BlockSpec(memory_space=pltpu.HBM)


def cost(microseconds):
    return pl.CostEstimate(
        flops=int(microseconds * 1.1e9), bytes_accessed=0, transcendentals=0
    )


def params():
    return pltpu.CompilerParams(vmem_limit_bytes=VMEM_BYTES)


def member_matrix(channels):
    per_group = channels // GROUPS
    group = lax.broadcasted_iota(jnp.int32, (LANES, channels), 0) * per_group
    channel = lax.broadcasted_iota(jnp.int32, (LANES, channels), 1)
    return jnp.where((channel >= group) & (channel < group + per_group), 1.0, 0.0).astype(F32)


def to_groups(values, member):
    return lax.dot_general(
        values, member, (((1,), (1,)), ((), ())), precision=HIGHEST, preferred_element_type=F32
    )


def to_channels(values, member):
    return jnp.dot(values, member, precision=HIGHEST, preferred_element_type=F32)


class Info:
    def __init__(self, ref, rows):
        self.ref, self.rows = ref, rows
        self.videos = ref.shape[0] - 1 - rows

    def tile(self):
        return self.ref[0]

    def label(self, row):
        inside = (row >= 0) & (row < self.rows)
        return jnp.where(inside, self.ref[1 + jnp.clip(row, 0, self.rows - 1)], -1)

    def width(self, label):
        return jnp.where(label >= 0, self.ref[1 + self.rows + jnp.maximum(label, 0)], 0)

    def window(self, first, count):
        labels = [self.label(first + r) for r in range(count)]
        return labels, [self.width(label) for label in labels]


def pick(table, label, videos):
    chosen = table[0:1]
    for video in range(1, videos):
        chosen = jnp.where(label == video, table[video : video + 1], chosen)
    return chosen


def norm_tables(stats_ref, gain_ref):
    member = member_matrix(gain_ref.shape[1])
    counts = jnp.maximum(stats_ref[0], 1.0)
    scale = lax.rsqrt(stats_ref[2] / counts + EPSILON)
    return to_channels(stats_ref[1], member), to_channels(scale, member) * gain_ref[...]


def write_stats(out_ref, rows, labels, widths, videos, channels):
    member = member_matrix(channels)
    per_group = channels // GROUPS
    cols = rows[0].shape[0]
    slot = lax.broadcasted_iota(jnp.int32, (SLOTS, 1), 0)
    column = lax.broadcasted_iota(jnp.int32, (cols, 1), 0)
    sums = jnp.zeros((SLOTS, channels), F32)
    counts = jnp.zeros((SLOTS, 1), F32)
    for index, row in enumerate(rows):
        sums = jnp.where(slot == index, jnp.sum(row, axis=0, keepdims=True), sums)
        counts = jnp.where(slot == index, (widths[index] * per_group).astype(F32), counts)
    means = to_groups(sums, member) / jnp.maximum(counts, 1.0)
    means_wide = to_channels(means, member)
    squares = jnp.zeros((SLOTS, channels), F32)
    for index, row in enumerate(rows):
        centered = jnp.where(column < widths[index], row - means_wide[index : index + 1], 0.0)
        squares = jnp.where(
            slot == index, jnp.sum(centered * centered, axis=0, keepdims=True), squares
        )
    spreads = to_groups(squares, member)
    out_ref[...] = jnp.zeros(out_ref.shape, F32)
    for video in range(videos):
        total = jnp.zeros((1, LANES), F32)
        count = jnp.zeros((1, LANES), F32)
        for index in range(len(rows)):
            mine = labels[index] == video
            row_count = counts[index : index + 1]
            total = total + jnp.where(mine, means[index : index + 1] * row_count, 0.0)
            count = count + jnp.where(mine, row_count, 0.0)
        mean = total / jnp.maximum(count, 1.0)
        spread = jnp.zeros((1, LANES), F32)
        for index in range(len(rows)):
            off = means[index : index + 1] - mean
            part = spreads[index : index + 1] + counts[index : index + 1] * off * off
            spread = spread + jnp.where(labels[index] == video, part, 0.0)
        out_ref[0, video : video + 1, :] = count
        out_ref[1, video : video + 1, :] = mean
        out_ref[2, video : video + 1, :] = spread


def build_columns(columns_ref, row_refs):
    padded = columns_ref.shape[0] // len(row_refs)
    for index, row in enumerate(row_refs):
        cells = row().astype(F32)
        count, channels = cells.shape
        cells = jnp.concatenate([cells, jnp.zeros((padded - count, channels), F32)], axis=0)
        start = index * padded
        columns_ref[start : start + padded, 0:channels] = pltpu.roll(cells, 1, 0).astype(BF16)
        columns_ref[start : start + padded, channels : 2 * channels] = cells.astype(BF16)
        columns_ref[start : start + padded, 2 * channels : 3 * channels] = pltpu.roll(
            cells, padded - 1, 0
        ).astype(BF16)


def stats_kernel(rows, info_ref, latents_ref, out_ref):
    info = Info(info_ref, rows)
    row_count, cols, channels = latents_ref.shape
    labels, widths = info.window(info.tile() * row_count, row_count)
    column = lax.broadcasted_iota(jnp.int32, (cols, 1), 0)
    cells = [
        jnp.where(column < widths[r], latents_ref[r].astype(F32), 0.0) for r in range(row_count)
    ]
    write_stats(out_ref, cells, labels, widths, info.videos, channels)


def rims(info, outer_ref, inner_ref):
    odd = lax.rem(info.tile(), 2) == 1
    inner, outer = inner_ref[0].astype(F32), outer_ref[0].astype(F32)
    return jnp.where(odd, inner, outer), jnp.where(odd, outer, inner)


def hidden_kernel(
    rows, info_ref, outer_ref, inner_ref, latents_ref, stats_ref, gain_ref, shift_ref, out_ref,
    source_ref,
):
    info = Info(info_ref, rows)
    row_count, cols, _ = latents_ref.shape
    labels, widths = info.window(info.tile() * row_count - 1, row_count + 2)
    means, scales = norm_tables(stats_ref, gain_ref)
    column = lax.broadcasted_iota(jnp.int32, (cols, 1), 0)
    above, below = rims(info, outer_ref, inner_ref)
    sources = [above] + [latents_ref[r].astype(F32) for r in range(row_count)] + [below]
    for r, source in enumerate(sources):
        mean = pick(means, labels[r], info.videos)
        scale = pick(scales, labels[r], info.videos)
        normed = (source - mean) * scale + shift_ref[...]
        active = normed / (1.0 + jnp.exp(-normed))
        active = jnp.where(column < widths[r], active, 0.0)
        rest = jnp.zeros((out_ref.shape[1] - cols, active.shape[1]), F32)
        out_ref[r] = jnp.concatenate([active, rest], axis=0).astype(BF16)
    source_ref[...] = latents_ref[...]


def hold_kernel(backs, weight_ref, held_ref, sems):
    channels = weight_ref.shape[-1]
    copies = [
        pltpu.make_async_copy(
            weight_ref.at[2 - back, tap, side],
            held_ref.at[
                pl.ds((3 * index + tap) * channels, channels), pl.ds(side * channels, channels)
            ],
            sems.at[index, tap, side],
        )
        for index, back in enumerate(backs)
        for tap in range(3)
        for side in range(3)
    ]
    for copy in copies:
        copy.start()
    for copy in copies:
        copy.wait()


def row_taps(info, hidden_refs, inputs_ref):
    near_rows, padded, channels = hidden_refs[0].shape
    row_count = near_rows - 2
    labels, _ = info.window(info.tile() * row_count - 1, near_rows)
    for back, hidden_ref in enumerate(hidden_refs):
        for tap in range(3):
            lanes = slice((3 * back + tap) * channels, (3 * back + tap + 1) * channels)
            for r in range(row_count):
                block = hidden_ref[r + tap]
                if tap != 1:
                    same = labels[r + tap] == labels[r + 1]
                    block = jnp.where(same, block, jnp.zeros_like(block))
                inputs_ref[r * padded : (r + 1) * padded, lanes] = block


def own_conv_kernel(rows, info_ref, hidden_ref, held_ref, product_ref, inputs_ref):
    row_taps(Info(info_ref, rows), [hidden_ref], inputs_ref)
    product_ref[...] = jnp.dot(inputs_ref[...], held_ref[...], preferred_element_type=F32)


def conv_kernel(rows, taps, info_ref, *rest):
    hidden_refs, rest = rest[: taps - 1], rest[taps - 1 :]
    product_ref, latents_ref, bias_ref, *rest = rest
    held_refs, (own_ref, stats_ref, *inputs_refs) = rest[: taps > 1], rest[taps > 1 :]
    row_count, cols, channels = latents_ref.shape
    info = Info(info_ref, rows)
    padded = product_ref.shape[0] // row_count
    labels, widths = info.window(info.tile() * row_count - 1, row_count + 2)
    product = product_ref[...]
    if hidden_refs:
        (inputs_ref,) = inputs_refs
        row_taps(info, hidden_refs, inputs_ref)
        product = product + jnp.dot(
            inputs_ref[...], held_refs[0][...], preferred_element_type=F32
        )
    column = lax.broadcasted_iota(jnp.int32, (cols, 1), 0)
    cells = []
    for r in range(row_count):
        lines = slice(r * padded, (r + 1) * padded)
        branch = pltpu.roll(product[lines, 0:channels], 1, 0)
        branch = branch + product[lines, channels : 2 * channels]
        branch = branch + pltpu.roll(product[lines, 2 * channels :], padded - 1, 0)
        value = latents_ref[r].astype(F32) + branch[:cols] + bias_ref[...]
        value = jnp.where(column < widths[r + 1], value, 0.0).astype(BF16)
        cells.append(value.astype(F32))
    for pair in range(row_count // 2):
        own_ref[pair] = jnp.concatenate(cells[2 * pair : 2 * pair + 2], axis=0).astype(BF16)
    write_stats(stats_ref, cells, labels[1:-1], widths[1:-1], info.videos, channels)


def split_rows(pairs_ref):
    cols = pairs_ref.shape[1] // 2
    cells = []
    for pair in range(pairs_ref.shape[0]):
        both = pairs_ref[pair].astype(F32)
        cells += [both[:cols], both[cols:]]
    return cells


def turned_queries(info, tile, pairs_ref, means, scales, shift_ref, weight_ref, bias_ref):
    pairs, double, channels = pairs_ref.shape
    cols = double // 2
    column = lax.broadcasted_iota(jnp.int32, (cols, 1), 0)
    labels, widths = info.window(tile * 2 * pairs, 2 * pairs)
    cells = []
    for r, values in enumerate(split_rows(pairs_ref)):
        mean = pick(means, labels[r], info.videos)
        scale = pick(scales, labels[r], info.videos)
        normed = (values - mean) * scale + shift_ref[...]
        cells.append(jnp.where(column < widths[r], normed, 0.0))
    cells = jnp.concatenate(cells, axis=0).astype(BF16)
    queries = (
        jnp.dot(cells, weight_ref[:, 0:channels], preferred_element_type=F32)
        + bias_ref[:, 0:channels]
    ).astype(BF16)
    factor = channels ** (-0.5) * math.log2(math.e)
    turned = lax.dot_general(
        queries, weight_ref[:, channels : 2 * channels], (((1,), (1,)), ((), ())),
        preferred_element_type=F32,
    )
    constant = jnp.sum(
        queries.astype(F32) * bias_ref[:, channels : 2 * channels], axis=1, keepdims=True
    )
    return (turned * factor).astype(BF16), constant * factor


def query_kernel(
    rows, info_ref, other_ref, stats_ref, gain_ref, shift_ref, weight_ref, bias_ref, queries_ref,
    constant_ref, means_ref, scales_ref,
):
    info = Info(info_ref, rows)
    means, scales = norm_tables(stats_ref, gain_ref)
    means_ref[...] = means
    scales_ref[...] = scales
    queries, constant = turned_queries(
        info, info.tile() ^ 1, other_ref, means, scales, shift_ref, weight_ref, bias_ref
    )
    queries_ref[...] = queries
    constant_ref[...] = jnp.broadcast_to(constant, constant_ref.shape)


def key_codes(info, masks, span, cols):
    row_count = span // cols
    position = lax.broadcasted_iota(jnp.int32, (1, len(masks) * span), 1)
    codes = jnp.full((1, len(masks) * span), -2.0, F32)
    for index, mask in enumerate(masks):
        near, widths = info.window((info.tile() ^ (2 * mask)) * row_count, row_count)
        for r in range(row_count):
            start = index * span + r * cols
            inside = (position >= start) & (position < start + widths[r])
            codes = jnp.where(inside, near[r].astype(F32), codes)
    return codes


def query_codes(info, tile, span, cols):
    row_count = span // cols
    labels, _ = info.window(tile * row_count, row_count)
    return jnp.concatenate(
        [jnp.zeros((cols, 1), F32) + label.astype(F32) for label in labels], axis=0
    )


def scores_of(queries, keys, codes, query_code):
    scores = lax.dot_general(
        queries, keys, (((1,), (1,)), ((), ())), preferred_element_type=F32
    )
    return jnp.where(codes == query_code, scores, MASKED)


def mean_and_level(peak, denominator, total):
    some = denominator > 0.0
    safe = jnp.where(some, denominator, 1.0)
    return total / safe, jnp.where(some, peak + jnp.log2(safe), LOWEST)


def attend_yours_kernel(rows, masks, first, last, info_ref, *rest):
    means_ref, scales_ref, shift_ref, queries_ref, constant_ref, *rest = rest
    block_refs, rest = rest[: len(masks)], rest[len(masks) :]
    if not first:
        old_peak_ref, old_sum_ref, old_total_ref, *rest = rest
    keys_ref, *out_refs = rest
    info = Info(info_ref, rows)
    span, channels = queries_ref.shape
    pairs, double, _ = block_refs[0].shape
    cols = double // 2
    row_count = 2 * pairs
    tile = info.tile()
    means, scales = means_ref[...], scales_ref[...]
    for index, (mask, block_ref) in enumerate(zip(masks, block_refs)):
        near, _ = info.window((tile ^ (2 * mask)) * row_count, row_count)
        for pair in range(pairs):
            both = block_ref[pair].astype(F32)
            halves = []
            for half in range(2):
                label = near[2 * pair + half]
                mean = pick(means, label, info.videos)
                scale = pick(scales, label, info.videos)
                values = both[half * cols : (half + 1) * cols]
                halves.append((values - mean) * scale + shift_ref[...])
            start = index * span + pair * double
            keys_ref[start : start + double, :] = jnp.concatenate(halves, axis=0).astype(BF16)
    constant = constant_ref[:, 0:1]
    scores = scores_of(
        queries_ref[...], keys_ref[...], key_codes(info, masks, span, cols),
        query_codes(info, tile ^ 1, span, cols),
    )
    peak = jnp.maximum(LOWEST, jnp.max(scores, axis=1, keepdims=True) + constant)
    if not first:
        largest = old_peak_ref[:, 0:1]
        peak = jnp.maximum(largest, peak)
    weights = jnp.exp2(scores - (peak - constant))
    denominator = jnp.sum(weights, axis=1, keepdims=True)
    total = jnp.dot(weights.astype(BF16), keys_ref[...], preferred_element_type=F32)
    if not first:
        factor = jnp.exp2(largest - peak)
        denominator = old_sum_ref[:, 0:1] * factor + denominator
        total = old_total_ref[...] * factor + total
    if not last:
        peak_ref, sum_ref, total_ref = out_refs
        peak_ref[...] = jnp.broadcast_to(peak, peak_ref.shape)
        sum_ref[...] = jnp.broadcast_to(denominator, sum_ref.shape)
        total_ref[...] = total
        return
    (sent_ref,) = out_refs
    mean, level = mean_and_level(peak, denominator, total)
    sent_ref[0:span, :] = mean.astype(BF16)
    slots = sent_ref.shape[0] - span
    slot = lax.broadcasted_iota(jnp.int32, (slots, 1), 0)
    packed = jnp.zeros((slots, LANES), F32)
    for r in range(row_count):
        left = level[r * cols : (r + 1) * cols]
        left = jnp.sum(jnp.where(diagonal(cols), left, 0.0), axis=0, keepdims=True)
        for part in range(3):
            rounded = left.astype(BF16).astype(F32)
            packed = jnp.where(slot == 3 * r + part, rounded, packed)
            left = left - rounded
    sent_ref[span:, 0:LANES] = packed.astype(BF16)
    sent_ref[span:, LANES:] = jnp.zeros((slots, channels - LANES), BF16)


def attend_mine_kernel(
    rows, groups, info_ref, own_ref, means_ref, scales_ref, shift_ref, weight_ref, bias_ref, *rest
):
    key_refs, (mean_ref, level_ref) = rest[: len(groups)], rest[len(groups) :]
    info = Info(info_ref, rows)
    span = mean_ref.shape[0]
    queries, constant = turned_queries(
        info, info.tile(), own_ref, means_ref[...], scales_ref[...], shift_ref, weight_ref,
        bias_ref,
    )
    cols = span // ROWS_OF_TILE
    query_code = query_codes(info, info.tile(), span, cols)
    peak = jnp.full((span, 1), LOWEST, F32)
    scores = []
    for masks, key_ref in zip(groups, key_refs):
        codes = key_codes(info, masks, span, cols)
        scores.append(scores_of(queries, key_ref[...], codes, query_code))
        peak = jnp.maximum(peak, jnp.max(scores[-1], axis=1, keepdims=True) + constant)
    denominator, total = 0.0, 0.0
    for part, key_ref in zip(scores, key_refs):
        weights = jnp.exp2(part - (peak - constant))
        denominator = denominator + jnp.sum(weights, axis=1, keepdims=True)
        total = total + jnp.dot(
            weights.astype(BF16), key_ref[...], preferred_element_type=F32
        )
    mean, level = mean_and_level(peak, denominator, total)
    mean_ref[...] = mean
    level_ref[...] = jnp.broadcast_to(level, level_ref.shape)


def diagonal(cols):
    return lax.broadcasted_iota(jnp.int32, (cols, LANES), 0) == lax.broadcasted_iota(
        jnp.int32, (cols, LANES), 1
    )


def finish_kernel(
    rows, info_ref, mean_ref, level_ref, received_ref, own_ref, triple_ref, triple_bias_ref,
    output_ref, output_bias_ref, out_ref, inner_ref, outer_ref,
):
    info = Info(info_ref, rows)
    row_count, cols, channels = out_ref.shape
    span = row_count * cols
    _, widths = info.window(info.tile() * row_count, row_count)
    received = received_ref[0:span, :].astype(F32)
    levels = received_ref[span:, 0:LANES].astype(F32)
    yours = []
    for r in range(row_count):
        level = levels[3 * r : 3 * r + 1] + levels[3 * r + 1 : 3 * r + 2]
        level = level + levels[3 * r + 2 : 3 * r + 3]
        yours.append(jnp.sum(jnp.where(diagonal(cols), level, 0.0), axis=1, keepdims=True))
    yours = jnp.concatenate(yours, axis=0)
    mine = level_ref[:, 0:1]
    peak = jnp.maximum(mine, yours)
    weight, other_weight = jnp.exp2(mine - peak), jnp.exp2(yours - peak)
    share = weight / (weight + other_weight)
    mean_cell = (mean_ref[...] * share + received * (1.0 - share)).astype(BF16)
    mixed = (
        jnp.dot(mean_cell, triple_ref[:, 2 * channels :], preferred_element_type=F32)
        + triple_bias_ref[:, 2 * channels :]
    ).astype(BF16)
    attended = jnp.dot(mixed, output_ref[...], preferred_element_type=F32) + output_bias_ref[...]
    column = lax.broadcasted_iota(jnp.int32, (cols, 1), 0)
    for r, before in enumerate(split_rows(own_ref)):
        value = before + attended[r * cols : (r + 1) * cols]
        value = jnp.where(column < widths[r], value, 0.0)
        out_ref[r] = value.astype(BF16)
        if r == 0:
            top = value
    odd = lax.rem(info.tile(), 2) == 1
    inner_ref[0] = jnp.where(odd, top, value).astype(BF16)
    outer_ref[0] = jnp.where(odd, value, top).astype(BF16)


def fold_kernel(weight_ref, out_ref):
    channels = weight_ref.shape[-1]
    wide = [[weight_ref[a, b].astype(F32) for b in range(3)] for a in range(3)]

    def both(upper, lower):
        return [x + y for x, y in zip(upper, lower)]

    phases = [[wide[0], both(wide[1], wide[2])], [both(wide[0], wide[1]), wide[2]]]
    for down in range(2):
        for tap in range(2):
            left, middle, right = phases[down][tap]
            out_ref[down, tap, 0, :, 0:channels] = left.astype(BF16)
            out_ref[down, tap, 0, :, channels:] = (middle + right).astype(BF16)
            out_ref[down, tap, 1, :, 0:channels] = (left + middle).astype(BF16)
            out_ref[down, tap, 1, :, channels:] = right.astype(BF16)


def spread_columns(wide_ref, value, row, right):
    cols, channels = value.shape
    for part in range(wide_ref.shape[0]):
        lo, hi = part * LANES, min((part + 1) * LANES, channels)
        piece = value[:, lo:hi]
        if hi - lo < LANES:
            piece = jnp.concatenate([piece, jnp.zeros((cols, LANES - hi + lo), F32)], axis=1)
        wide_ref[part, row, pl.ds(right, cols, 2), :] = piece


def write_turned(out_ref, row, part, value, width):
    channels, cols = out_ref.shape[1:]
    lo, hi = part * LANES, min((part + 1) * LANES, channels)
    turned = value.T[0 : hi - lo, 0:cols]
    column = lax.broadcasted_iota(jnp.int32, (1, cols), 1)
    out_ref[row, lo:hi, :] = jnp.where(column < width, turned, 0.0).astype(BF16)


def phase_product(columns, weight):
    return lax.dot_general(
        columns, weight, (((1,), (1,)), ((), ())), preferred_element_type=F32
    )


def upsample_kernel(
    rows, info_ref, own_ref, weight_ref, bias_ref, out_ref, open_ref, columns_ref, wide_ref
):
    info = Info(info_ref, rows)
    row_count, cols, channels = own_ref.shape
    padded = columns_ref.shape[0] // row_count
    parts_out = wide_ref.shape[0]
    labels, widths = info.window(info.tile() * row_count, row_count)
    build_columns(
        columns_ref, [functools.partial(own_ref.__getitem__, r) for r in range(row_count)]
    )
    inner_rows = (row_count - 1) * padded
    for down in range(2):
        for right in range(2):
            lanes = slice(right * channels, (right + 2) * channels)
            same = phase_product(columns_ref[:, lanes], weight_ref[down, 1 - down, right])
            start = down * padded
            rim = phase_product(
                columns_ref[start : start + inner_rows, lanes], weight_ref[down, down, right]
            )
            for r in range(row_count):
                value = same[r * padded : r * padded + cols]
                near = r - 1 + 2 * down
                if 0 <= near < row_count:
                    lo = (near - down) * padded
                    value = value + jnp.where(
                        labels[near] == labels[r], rim[lo : lo + cols], 0.0
                    )
                spread_columns(wide_ref, value, 2 * r + down, right)
    for part in range(parts_out):
        open_ref[part, 0] = wide_ref[part, 0]
        open_ref[part, 1] = wide_ref[part, 2 * row_count - 1]
    for r in range(1, 2 * row_count - 1):
        for part in range(parts_out):
            value = wide_ref[part, r] + bias_ref[:, part * LANES : (part + 1) * LANES]
            write_turned(out_ref, r - 1, part, value, 2 * widths[r // 2])


def close_kernel(
    rows, info_ref, outer_ref, inner_ref, middle_ref, open_ref, weight_ref, bias_ref, out_ref,
    columns_ref, wide_ref,
):
    info = Info(info_ref, rows)
    wide_rows, _, wide_cols = out_ref.shape
    row_count, cols = wide_rows // 2, wide_cols // 2
    channels = outer_ref.shape[-1]
    padded = columns_ref.shape[0] // 2
    labels, widths = info.window(info.tile() * row_count - 1, row_count + 2)
    above, below = rims(info, outer_ref, inner_ref)
    build_columns(columns_ref, [lambda: above, lambda: below])
    for down in range(2):
        for right in range(2):
            lanes = slice(right * channels, (right + 2) * channels)
            rim = phase_product(
                columns_ref[down * padded : (down + 1) * padded, lanes],
                weight_ref[down, down, right],
            )
            spread_columns(wide_ref, rim[:cols], down, right)
    out_ref[1 : wide_rows - 1] = middle_ref[...]
    for down in range(2):
        rim_row, own_row = (row_count + 1, row_count) if down else (0, 1)
        for part in range(wide_ref.shape[0]):
            rim = jnp.where(labels[rim_row] == labels[own_row], wide_ref[part, down], 0.0)
            value = open_ref[part, down] + rim + bias_ref[:, part * LANES : (part + 1) * LANES]
            write_turned(
                out_ref, down * (wide_rows - 1), part, value, 2 * widths[own_row]
            )


def merge_stats(mine, other):
    count = mine[0] + other[0]
    safe = jnp.maximum(count, 1.0)
    off = other[1] - mine[1]
    mean = mine[1] + off * (other[0] / safe)
    spread = mine[2] + other[2] + off * off * (mine[0] * other[0] / safe)
    return jnp.stack([count, mean, spread])


def exchange(array, tiles, mask, among=None):
    moves = [(i, i ^ mask) for i in range(tiles) if among is None or among(i)]
    return lax.ppermute(array, "tile", moves)


def merge_round(stats, tiles, masks, tied=(), after=None):
    parts = [stats] + [exchange(stats, tiles, mask) for mask in masks]
    free = ()
    if tied:
        *parts[2:], free = lax.optimization_barrier((*parts[2:], after))
        parts[1], *tied = lax.optimization_barrier((parts[1], *tied))
    while len(parts) > 1:
        parts = [merge_stats(*parts[i : i + 2]) for i in range(0, len(parts), 2)]
    return (parts[0], *tied, free) if tied else parts[0]


def merge_masks(tiles):
    bits = [1 << i for i in range(tiles.bit_length() - 1)]
    pairs = [bits[i : i + 2] for i in range(0, len(bits), 2)]
    return [[p[0], p[1], p[0] ^ p[1]] if len(p) == 2 else p for p in pairs]


def shards(
    tiles,
    frames,
    latents,
    row_video,
    video_cols,
    first_gain,
    first_shift,
    conv_weight,
    conv_bias,
    second_gain,
    second_shift,
    triple_weight,
    triple_bias,
    output_weight,
    output_bias,
    upsample_weight,
    upsample_bias,
):
    row_count, frame_count, cols, channels = latents.shape
    assert frame_count == 1 and row_count == ROWS_OF_TILE and tiles % 4 == 0
    out_channels = upsample_weight.shape[-1]
    rows = row_count * tiles
    cells = row_count * cols
    padded = -(-(cols + 1) // 16) * 16
    near_rows = row_count + 2
    source = latents.reshape(row_count, cols, channels)
    tile = lax.axis_index("tile").astype(jnp.int32)
    info = jnp.concatenate([jnp.reshape(tile, (1,)), row_video, video_cols])

    def row(vector):
        return vector.reshape(1, -1)

    def shape(*dims, dtype=BF16):
        return jax.ShapeDtypeStruct(dims, dtype)

    def call(kernel, operands, out_shape, scratch=(), **kwargs):
        many = isinstance(out_shape, tuple)
        return pl.pallas_call(
            kernel,
            out_shape=out_shape,
            in_specs=[SMEM_SPEC] + [VMEM_SPEC] * len(operands),
            out_specs=(VMEM_SPEC,) * len(out_shape) if many else VMEM_SPEC,
            scratch_shapes=list(scratch),
            compiler_params=params(),
            **kwargs,
        )(info, *operands)

    outer_moves = [(i, i - 1 if i % 2 == 0 else i + 1) for i in range(tiles)]
    outer_moves = [(i, j) for i, j in outer_moves if 0 <= j < tiles]
    odd = tile % 2 == 1
    stats_shape = shape(3, SLOTS, LANES, dtype=F32)
    stats = call(
        functools.partial(stats_kernel, rows), [source], stats_shape,
        cost_estimate=cost(1.5), name="first_stats",
    )
    outer = lax.ppermute(
        jnp.where(odd, source[row_count - 1 :], source[:1]), "tile", outer_moves
    )
    inner = exchange(jnp.where(odd, source[:1], source[row_count - 1 :]), tiles, 1)
    stats, outer, inner = lax.optimization_barrier((stats, outer, inner))
    taps = min(3, frames)
    held = [
        pl.pallas_call(
            functools.partial(hold_kernel, backs),
            out_shape=shape(3 * len(backs) * channels, 3 * channels),
            in_specs=[HBM_SPEC],
            out_specs=VMEM_SPEC,
            scratch_shapes=[pltpu.SemaphoreType.DMA((len(backs), 3, 3))],
            compiler_params=pltpu.CompilerParams(vmem_limit_bytes=HOLD_VMEM_BYTES),
            cost_estimate=cost(1.5 * len(backs)),
            name="hold",
        )(conv_weight)
        for backs in ((0,), tuple(range(1, taps)))
        if backs
    ]
    rounds = merge_masks(tiles)
    for index, masks in enumerate(reversed(rounds)):
        stats = merge_round(stats, tiles, masks)
        if index < len(held):
            stats, held[index] = lax.optimization_barrier((stats, held[index]))
    hidden, source = call(
        functools.partial(hidden_kernel, rows),
        [outer, inner, source, stats, row(first_gain), row(first_shift)],
        (shape(near_rows, padded, channels), shape(row_count, cols, channels)),
        cost_estimate=cost(1.3),
        name="hidden",
    )

    earlier = [
        lax.ppermute(hidden, "frame", [(i, i + by) for i in range(frames - by)])
        for by in range(1, taps)
    ]
    pairs = row_count // 2
    pair_shape = shape(pairs, 2 * cols, channels)
    product = call(
        functools.partial(own_conv_kernel, rows),
        [hidden, held[0]],
        shape(row_count * padded, 3 * channels, dtype=F32),
        scratch=[pltpu.VMEM((row_count * padded, 3 * channels), BF16)],
        cost_estimate=cost(2.2),
        name="own_conv",
    )
    scratch = [pltpu.VMEM((row_count * padded, 3 * (taps - 1) * channels), BF16)]
    own, stats = call(
        functools.partial(conv_kernel, rows, taps),
        earlier + [product, source, row(conv_bias)] + held[1:],
        (pair_shape, stats_shape),
        scratch=scratch if taps > 1 else [],
        cost_estimate=cost(1.5 + 2.0 * (taps - 1)),
        name="conv",
    )

    blocks = {0: own}
    neighbour = [(i, i ^ 1) for i in range(tiles)]
    if tiles == 16 and video_cols.shape[0] == 2:
        def middle(t):
            return t // 4 in (1, 2)

        stats = merge_round(stats, tiles, rounds[1])
        blocks[2] = exchange(own, tiles, 4)
        blocks[6] = exchange(own, tiles, 12, middle)
        stats, blocks[2], blocks[6], own_xy = merge_round(
            stats, tiles, rounds[0], (blocks[2], blocks[6]), own
        )
        inward = exchange(blocks[2], tiles, 12, middle)
        outward = exchange(blocks[6], tiles, 4, middle)
        other = exchange(own_xy, tiles, 1)
        blocks[1] = exchange(own_xy, tiles, 2)
        blocks[4] = jnp.where((tile // 4 == 1) | (tile // 4 == 2), inward, outward)
        passed, blocks[4] = lax.optimization_barrier((blocks[1], blocks[4]))
        blocks[5] = exchange(blocks[4], tiles, 2)
        blocks[3] = exchange(passed, tiles, 4)
        blocks[7] = exchange(passed, tiles, 12, middle)
        groups = [[0, 1, 2, 6], [4, 7, 3, 5]]
    else:
        for masks in rounds:
            stats = merge_round(stats, tiles, masks)
        other = exchange(own, tiles, 1)
        for mask in range(1, tiles // 2):
            blocks[mask] = exchange(own, tiles, 2 * mask)
        groups = [list(range(i, i + 4)) for i in range(0, tiles // 2, 4)]
    gain, shift = row(second_gain), row(second_shift)
    table_shape = shape(SLOTS, channels, dtype=F32)
    queries, constant, means, scales = call(
        functools.partial(query_kernel, rows),
        [other, stats, gain, shift, triple_weight, row(triple_bias)],
        (shape(cells, channels), shape(cells, LANES, dtype=F32), table_shape, table_shape),
        cost_estimate=cost(1.5),
        name="queries",
    )
    level_shape = shape(cells, LANES, dtype=F32)
    total_shape = shape(cells, channels, dtype=F32)
    state, keys = (), []
    for index, masks in enumerate(groups):
        last = index == len(groups) - 1
        outs = (shape(len(masks) * cells, channels),)
        outs += (shape(cells + 16, channels),) if last else (level_shape, level_shape, total_shape)
        normed, *state = call(
            functools.partial(attend_yours_kernel, rows, tuple(masks), index == 0, last),
            [means, scales, shift, queries, constant] + [blocks[m] for m in masks] + list(state),
            outs,
            cost_estimate=cost(0.9 * len(masks)),
            name="attend_yours",
        )
        keys.append(normed)
    (sent,) = state
    received = lax.ppermute(sent, "tile", neighbour)
    sent, own_late = lax.optimization_barrier((sent, own))
    mean, level = call(
        functools.partial(attend_mine_kernel, rows, tuple(tuple(masks) for masks in groups)),
        [own_late, means, scales, shift, triple_weight, row(triple_bias)] + keys,
        (total_shape, level_shape),
        cost_estimate=cost(6.0),
        name="attend_mine",
    )
    rim_shape = shape(1, cols, channels)
    attended, inner, outer = call(
        functools.partial(finish_kernel, rows),
        [
            mean, level, received, own, triple_weight, row(triple_bias), output_weight,
            row(output_bias),
        ],
        (shape(row_count, cols, channels), rim_shape, rim_shape),
        cost_estimate=cost(1.4),
        name="finish",
    )
    outer = lax.ppermute(outer, "tile", outer_moves)
    inner = exchange(inner, tiles, 1)
    attended, upsample_weight = lax.optimization_barrier((attended, upsample_weight))
    folded = pl.pallas_call(
        fold_kernel,
        out_shape=shape(2, 2, 2, out_channels, 2 * channels),
        in_specs=[VMEM_SPEC],
        out_specs=VMEM_SPEC,
        compiler_params=params(),
        cost_estimate=cost(0.5),
        name="fold",
    )(jnp.swapaxes(upsample_weight, 2, 3))
    parts_out = -(-out_channels // LANES)
    wide_cols = -(-2 * cols // LANES) * LANES
    wide_bias = jnp.pad(row(upsample_bias), ((0, 0), (0, -out_channels % LANES)))
    middle, open_rows = call(
        functools.partial(upsample_kernel, rows),
        [attended, folded, wide_bias],
        (
            shape(2 * row_count - 2, out_channels, 2 * cols),
            shape(parts_out, 2, wide_cols, LANES, dtype=F32),
        ),
        scratch=[
            pltpu.VMEM((row_count * padded, 3 * channels), BF16),
            pltpu.VMEM((parts_out, 2 * row_count, wide_cols, LANES), F32),
        ],
        cost_estimate=cost(2.0),
        name="upsample",
    )
    decoded = call(
        functools.partial(close_kernel, rows),
        [outer, inner, middle, open_rows, folded, wide_bias],
        shape(2 * row_count, out_channels, 2 * cols),
        scratch=[
            pltpu.VMEM((2 * padded, 3 * channels), BF16),
            pltpu.VMEM((parts_out, 2, wide_cols, LANES), F32),
        ],
        cost_estimate=cost(1.0),
        name="close",
    )
    return jnp.swapaxes(decoded, 1, 2).reshape(2 * row_count, 1, 2 * cols, out_channels)


def solution(mesh):
    sizes = dict(mesh.shape)
    in_specs = (P("tile", "frame", None, None),) + (P(),) * 14
    out_specs = P("tile", "frame", None, None)
    body = functools.partial(shards, sizes["tile"], sizes["frame"])
    return jax.shard_map(body, mesh=mesh, in_specs=in_specs, out_specs=out_specs, check_vma=False)
```

```python
import functools
import math

import jax
import jax.numpy as jnp
from jax import lax
from jax.experimental import pallas as pl
from jax.experimental.pallas import tpu as pltpu
from jax.sharding import PartitionSpec as P

GROUPS = 32
EPSILON = 1e-05
MASKED = -1e30
LOWEST = -5e29
HIGHEST = lax.Precision.HIGHEST
SLOTS = 8
ROWS_OF_TILE = 4
LANES = 128
VMEM_BYTES = 24 * 1024 * 1024
HOLD_VMEM_BYTES = 46 * 1024 * 1024
F32 = jnp.float32
BF16 = jnp.bfloat16

SMEM_SPEC = pl.BlockSpec(memory_space=pltpu.SMEM)
VMEM_SPEC = pl.BlockSpec(memory_space=pltpu.VMEM)
HBM_SPEC = pl.BlockSpec(memory_space=pltpu.HBM)


def cost(microseconds):
    return pl.CostEstimate(
        flops=int(microseconds * 1.1e9), bytes_accessed=0, transcendentals=0
    )


def params():
    return pltpu.CompilerParams(vmem_limit_bytes=VMEM_BYTES)


def member_matrix(channels):
    per_group = channels // GROUPS
    group = lax.broadcasted_iota(jnp.int32, (LANES, channels), 0) * per_group
    channel = lax.broadcasted_iota(jnp.int32, (LANES, channels), 1)
    return jnp.where((channel >= group) & (channel < group + per_group), 1.0, 0.0).astype(F32)


def to_groups(values, member):
    return lax.dot_general(
        values, member, (((1,), (1,)), ((), ())), precision=HIGHEST, preferred_element_type=F32
    )


def to_channels(values, member):
    return jnp.dot(values, member, precision=HIGHEST, preferred_element_type=F32)


class Info:
    def __init__(self, ref, rows):
        self.ref, self.rows = ref, rows
        self.videos = ref.shape[0] - 1 - rows

    def tile(self):
        return self.ref[0]

    def label(self, row):
        inside = (row >= 0) & (row < self.rows)
        return jnp.where(inside, self.ref[1 + jnp.clip(row, 0, self.rows - 1)], -1)

    def width(self, label):
        return jnp.where(label >= 0, self.ref[1 + self.rows + jnp.maximum(label, 0)], 0)

    def window(self, first, count):
        labels = [self.label(first + r) for r in range(count)]
        return labels, [self.width(label) for label in labels]


def pick(table, label, videos):
    chosen = table[0:1]
    for video in range(1, videos):
        chosen = jnp.where(label == video, table[video : video + 1], chosen)
    return chosen


def norm_tables(stats_ref, gain_ref):
    member = member_matrix(gain_ref.shape[1])
    counts = jnp.maximum(stats_ref[0], 1.0)
    scale = lax.rsqrt(stats_ref[2] / counts + EPSILON)
    return to_channels(stats_ref[1], member), to_channels(scale, member) * gain_ref[...]


def write_stats(out_ref, rows, labels, widths, videos, channels):
    member = member_matrix(channels)
    per_group = channels // GROUPS
    cols = rows[0].shape[0]
    slot = lax.broadcasted_iota(jnp.int32, (SLOTS, 1), 0)
    column = lax.broadcasted_iota(jnp.int32, (cols, 1), 0)
    sums = jnp.zeros((SLOTS, channels), F32)
    counts = jnp.zeros((SLOTS, 1), F32)
    for index, row in enumerate(rows):
        sums = jnp.where(slot == index, jnp.sum(row, axis=0, keepdims=True), sums)
        counts = jnp.where(slot == index, (widths[index] * per_group).astype(F32), counts)
    means = to_groups(sums, member) / jnp.maximum(counts, 1.0)
    means_wide = to_channels(means, member)
    squares = jnp.zeros((SLOTS, channels), F32)
    for index, row in enumerate(rows):
        centered = jnp.where(column < widths[index], row - means_wide[index : index + 1], 0.0)
        squares = jnp.where(
            slot == index, jnp.sum(centered * centered, axis=0, keepdims=True), squares
        )
    spreads = to_groups(squares, member)
    out_ref[...] = jnp.zeros(out_ref.shape, F32)
    for video in range(videos):
        total = jnp.zeros((1, LANES), F32)
        count = jnp.zeros((1, LANES), F32)
        for index in range(len(rows)):
            mine = labels[index] == video
            row_count = counts[index : index + 1]
            total = total + jnp.where(mine, means[index : index + 1] * row_count, 0.0)
            count = count + jnp.where(mine, row_count, 0.0)
        mean = total / jnp.maximum(count, 1.0)
        spread = jnp.zeros((1, LANES), F32)
        for index in range(len(rows)):
            off = means[index : index + 1] - mean
            part = spreads[index : index + 1] + counts[index : index + 1] * off * off
            spread = spread + jnp.where(labels[index] == video, part, 0.0)
        out_ref[0, video : video + 1, :] = count
        out_ref[1, video : video + 1, :] = mean
        out_ref[2, video : video + 1, :] = spread


def build_columns(columns_ref, row_refs):
    padded = columns_ref.shape[0] // len(row_refs)
    for index, row in enumerate(row_refs):
        cells = row().astype(F32)
        count, channels = cells.shape
        cells = jnp.concatenate([cells, jnp.zeros((padded - count, channels), F32)], axis=0)
        start = index * padded
        columns_ref[start : start + padded, 0:channels] = pltpu.roll(cells, 1, 0).astype(BF16)
        columns_ref[start : start + padded, channels : 2 * channels] = cells.astype(BF16)
        columns_ref[start : start + padded, 2 * channels : 3 * channels] = pltpu.roll(
            cells, padded - 1, 0
        ).astype(BF16)


def stats_kernel(rows, info_ref, latents_ref, out_ref):
    info = Info(info_ref, rows)
    row_count, cols, channels = latents_ref.shape
    labels, widths = info.window(info.tile() * row_count, row_count)
    column = lax.broadcasted_iota(jnp.int32, (cols, 1), 0)
    cells = [
        jnp.where(column < widths[r], latents_ref[r].astype(F32), 0.0) for r in range(row_count)
    ]
    write_stats(out_ref, cells, labels, widths, info.videos, channels)


def rims(info, outer_ref, inner_ref):
    odd = lax.rem(info.tile(), 2) == 1
    inner, outer = inner_ref[0].astype(F32), outer_ref[0].astype(F32)
    return jnp.where(odd, inner, outer), jnp.where(odd, outer, inner)


def hidden_kernel(
    rows, info_ref, outer_ref, inner_ref, latents_ref, stats_ref, gain_ref, shift_ref, out_ref,
    source_ref,
):
    info = Info(info_ref, rows)
    row_count, cols, _ = latents_ref.shape
    labels, widths = info.window(info.tile() * row_count - 1, row_count + 2)
    means, scales = norm_tables(stats_ref, gain_ref)
    column = lax.broadcasted_iota(jnp.int32, (cols, 1), 0)
    above, below = rims(info, outer_ref, inner_ref)
    sources = [above] + [latents_ref[r].astype(F32) for r in range(row_count)] + [below]
    for r, source in enumerate(sources):
        mean = pick(means, labels[r], info.videos)
        scale = pick(scales, labels[r], info.videos)
        normed = (source - mean) * scale + shift_ref[...]
        active = normed / (1.0 + jnp.exp(-normed))
        active = jnp.where(column < widths[r], active, 0.0)
        rest = jnp.zeros((out_ref.shape[1] - cols, active.shape[1]), F32)
        out_ref[r] = jnp.concatenate([active, rest], axis=0).astype(BF16)
    source_ref[...] = latents_ref[...]


def hold_kernel(backs, weight_ref, held_ref, sems):
    channels = weight_ref.shape[-1]
    copies = [
        pltpu.make_async_copy(
            weight_ref.at[2 - back, tap, side],
            held_ref.at[
                pl.ds((3 * index + tap) * channels, channels), pl.ds(side * channels, channels)
            ],
            sems.at[index, tap, side],
        )
        for index, back in enumerate(backs)
        for tap in range(3)
        for side in range(3)
    ]
    for copy in copies:
        copy.start()
    for copy in copies:
        copy.wait()


def row_taps(info, hidden_refs, inputs_ref):
    near_rows, padded, channels = hidden_refs[0].shape
    row_count = near_rows - 2
    labels, _ = info.window(info.tile() * row_count - 1, near_rows)
    for back, hidden_ref in enumerate(hidden_refs):
        for tap in range(3):
            lanes = slice((3 * back + tap) * channels, (3 * back + tap + 1) * channels)
            for r in range(row_count):
                block = hidden_ref[r + tap]
                if tap != 1:
                    same = labels[r + tap] == labels[r + 1]
                    block = jnp.where(same, block, jnp.zeros_like(block))
                inputs_ref[r * padded : (r + 1) * padded, lanes] = block


def own_conv_kernel(rows, info_ref, hidden_ref, held_ref, product_ref, inputs_ref):
    row_taps(Info(info_ref, rows), [hidden_ref], inputs_ref)
    product_ref[...] = jnp.dot(inputs_ref[...], held_ref[...], preferred_element_type=F32)


def conv_kernel(rows, taps, info_ref, *rest):
    hidden_refs, rest = rest[: taps - 1], rest[taps - 1 :]
    product_ref, latents_ref, bias_ref, *rest = rest
    held_refs, (own_ref, stats_ref, *inputs_refs) = rest[: taps > 1], rest[taps > 1 :]
    row_count, cols, channels = latents_ref.shape
    info = Info(info_ref, rows)
    padded = product_ref.shape[0] // row_count
    labels, widths = info.window(info.tile() * row_count - 1, row_count + 2)
    product = product_ref[...]
    if hidden_refs:
        (inputs_ref,) = inputs_refs
        row_taps(info, hidden_refs, inputs_ref)
        product = product + jnp.dot(
            inputs_ref[...], held_refs[0][...], preferred_element_type=F32
        )
    column = lax.broadcasted_iota(jnp.int32, (cols, 1), 0)
    cells = []
    for r in range(row_count):
        lines = slice(r * padded, (r + 1) * padded)
        branch = pltpu.roll(product[lines, 0:channels], 1, 0)
        branch = branch + product[lines, channels : 2 * channels]
        branch = branch + pltpu.roll(product[lines, 2 * channels :], padded - 1, 0)
        value = latents_ref[r].astype(F32) + branch[:cols] + bias_ref[...]
        value = jnp.where(column < widths[r + 1], value, 0.0).astype(BF16)
        cells.append(value.astype(F32))
    for pair in range(row_count // 2):
        own_ref[pair] = jnp.concatenate(cells[2 * pair : 2 * pair + 2], axis=0).astype(BF16)
    write_stats(stats_ref, cells, labels[1:-1], widths[1:-1], info.videos, channels)


def split_rows(pairs_ref):
    cols = pairs_ref.shape[1] // 2
    cells = []
    for pair in range(pairs_ref.shape[0]):
        both = pairs_ref[pair].astype(F32)
        cells += [both[:cols], both[cols:]]
    return cells


def turned_queries(info, tile, pairs_ref, means, scales, shift_ref, weight_ref, bias_ref):
    pairs, double, channels = pairs_ref.shape
    cols = double // 2
    column = lax.broadcasted_iota(jnp.int32, (cols, 1), 0)
    labels, widths = info.window(tile * 2 * pairs, 2 * pairs)
    cells = []
    for r, values in enumerate(split_rows(pairs_ref)):
        mean = pick(means, labels[r], info.videos)
        scale = pick(scales, labels[r], info.videos)
        normed = (values - mean) * scale + shift_ref[...]
        cells.append(jnp.where(column < widths[r], normed, 0.0))
    cells = jnp.concatenate(cells, axis=0).astype(BF16)
    queries = (
        jnp.dot(cells, weight_ref[:, 0:channels], preferred_element_type=F32)
        + bias_ref[:, 0:channels]
    ).astype(BF16)
    factor = channels ** (-0.5) * math.log2(math.e)
    turned = lax.dot_general(
        queries, weight_ref[:, channels : 2 * channels], (((1,), (1,)), ((), ())),
        preferred_element_type=F32,
    )
    constant = jnp.sum(
        queries.astype(F32) * bias_ref[:, channels : 2 * channels], axis=1, keepdims=True
    )
    return (turned * factor).astype(BF16), constant * factor


def query_kernel(
    rows, info_ref, other_ref, stats_ref, gain_ref, shift_ref, weight_ref, bias_ref, queries_ref,
    constant_ref, means_ref, scales_ref,
):
    info = Info(info_ref, rows)
    means, scales = norm_tables(stats_ref, gain_ref)
    means_ref[...] = means
    scales_ref[...] = scales
    queries, constant = turned_queries(
        info, info.tile() ^ 1, other_ref, means, scales, shift_ref, weight_ref, bias_ref
    )
    queries_ref[...] = queries
    constant_ref[...] = jnp.broadcast_to(constant, constant_ref.shape)


def key_codes(info, masks, span, cols):
    row_count = span // cols
    position = lax.broadcasted_iota(jnp.int32, (1, len(masks) * span), 1)
    codes = jnp.full((1, len(masks) * span), -2.0, F32)
    for index, mask in enumerate(masks):
        near, widths = info.window((info.tile() ^ (2 * mask)) * row_count, row_count)
        for r in range(row_count):
            start = index * span + r * cols
            inside = (position >= start) & (position < start + widths[r])
            codes = jnp.where(inside, near[r].astype(F32), codes)
    return codes


def query_codes(info, tile, span, cols):
    row_count = span // cols
    labels, _ = info.window(tile * row_count, row_count)
    return jnp.concatenate(
        [jnp.zeros((cols, 1), F32) + label.astype(F32) for label in labels], axis=0
    )


def scores_of(queries, keys, codes, query_code):
    scores = lax.dot_general(
        queries, keys, (((1,), (1,)), ((), ())), preferred_element_type=F32
    )
    return jnp.where(codes == query_code, scores, MASKED)


def mean_and_level(peak, denominator, total):
    some = denominator > 0.0
    safe = jnp.where(some, denominator, 1.0)
    return total / safe, jnp.where(some, peak + jnp.log2(safe), LOWEST)


def attend_yours_kernel(rows, masks, first, last, info_ref, *rest):
    means_ref, scales_ref, shift_ref, queries_ref, constant_ref, *rest = rest
    block_refs, rest = rest[: len(masks)], rest[len(masks) :]
    if not first:
        old_peak_ref, old_sum_ref, old_total_ref, *rest = rest
    keys_ref, *out_refs = rest
    info = Info(info_ref, rows)
    span, channels = queries_ref.shape
    pairs, double, _ = block_refs[0].shape
    cols = double // 2
    row_count = 2 * pairs
    tile = info.tile()
    means, scales = means_ref[...], scales_ref[...]
    for index, (mask, block_ref) in enumerate(zip(masks, block_refs)):
        near, _ = info.window((tile ^ (2 * mask)) * row_count, row_count)
        for pair in range(pairs):
            both = block_ref[pair].astype(F32)
            halves = []
            for half in range(2):
                label = near[2 * pair + half]
                mean = pick(means, label, info.videos)
                scale = pick(scales, label, info.videos)
                values = both[half * cols : (half + 1) * cols]
                halves.append((values - mean) * scale + shift_ref[...])
            start = index * span + pair * double
            keys_ref[start : start + double, :] = jnp.concatenate(halves, axis=0).astype(BF16)
    constant = constant_ref[:, 0:1]
    scores = scores_of(
        queries_ref[...], keys_ref[...], key_codes(info, masks, span, cols),
        query_codes(info, tile ^ 1, span, cols),
    )
    peak = jnp.maximum(LOWEST, jnp.max(scores, axis=1, keepdims=True) + constant)
    if not first:
        largest = old_peak_ref[:, 0:1]
        peak = jnp.maximum(largest, peak)
    weights = jnp.exp2(scores - (peak - constant))
    denominator = jnp.sum(weights, axis=1, keepdims=True)
    total = jnp.dot(weights.astype(BF16), keys_ref[...], preferred_element_type=F32)
    if not first:
        factor = jnp.exp2(largest - peak)
        denominator = old_sum_ref[:, 0:1] * factor + denominator
        total = old_total_ref[...] * factor + total
    if not last:
        peak_ref, sum_ref, total_ref = out_refs
        peak_ref[...] = jnp.broadcast_to(peak, peak_ref.shape)
        sum_ref[...] = jnp.broadcast_to(denominator, sum_ref.shape)
        total_ref[...] = total
        return
    (sent_ref,) = out_refs
    mean, level = mean_and_level(peak, denominator, total)
    sent_ref[0:span, :] = mean.astype(BF16)
    slots = sent_ref.shape[0] - span
    slot = lax.broadcasted_iota(jnp.int32, (slots, 1), 0)
    packed = jnp.zeros((slots, LANES), F32)
    for r in range(row_count):
        left = level[r * cols : (r + 1) * cols]
        left = jnp.sum(jnp.where(diagonal(cols), left, 0.0), axis=0, keepdims=True)
        for part in range(3):
            rounded = left.astype(BF16).astype(F32)
            packed = jnp.where(slot == 3 * r + part, rounded, packed)
            left = left - rounded
    sent_ref[span:, 0:LANES] = packed.astype(BF16)
    sent_ref[span:, LANES:] = jnp.zeros((slots, channels - LANES), BF16)


def attend_mine_kernel(
    rows, groups, info_ref, own_ref, means_ref, scales_ref, shift_ref, weight_ref, bias_ref, *rest
):
    key_refs, (mean_ref, level_ref) = rest[: len(groups)], rest[len(groups) :]
    info = Info(info_ref, rows)
    span = mean_ref.shape[0]
    queries, constant = turned_queries(
        info, info.tile(), own_ref, means_ref[...], scales_ref[...], shift_ref, weight_ref,
        bias_ref,
    )
    cols = span // ROWS_OF_TILE
    query_code = query_codes(info, info.tile(), span, cols)
    peak = jnp.full((span, 1), LOWEST, F32)
    scores = []
    for masks, key_ref in zip(groups, key_refs):
        codes = key_codes(info, masks, span, cols)
        scores.append(scores_of(queries, key_ref[...], codes, query_code))
        peak = jnp.maximum(peak, jnp.max(scores[-1], axis=1, keepdims=True) + constant)
    denominator, total = 0.0, 0.0
    for part, key_ref in zip(scores, key_refs):
        weights = jnp.exp2(part - (peak - constant))
        denominator = denominator + jnp.sum(weights, axis=1, keepdims=True)
        total = total + jnp.dot(
            weights.astype(BF16), key_ref[...], preferred_element_type=F32
        )
    mean, level = mean_and_level(peak, denominator, total)
    mean_ref[...] = mean
    level_ref[...] = jnp.broadcast_to(level, level_ref.shape)


def diagonal(cols):
    return lax.broadcasted_iota(jnp.int32, (cols, LANES), 0) == lax.broadcasted_iota(
        jnp.int32, (cols, LANES), 1
    )


def finish_kernel(
    rows, info_ref, mean_ref, level_ref, received_ref, own_ref, triple_ref, triple_bias_ref,
    output_ref, output_bias_ref, out_ref, inner_ref, outer_ref,
):
    info = Info(info_ref, rows)
    row_count, cols, channels = out_ref.shape
    span = row_count * cols
    _, widths = info.window(info.tile() * row_count, row_count)
    received = received_ref[0:span, :].astype(F32)
    levels = received_ref[span:, 0:LANES].astype(F32)
    yours = []
    for r in range(row_count):
        level = levels[3 * r : 3 * r + 1] + levels[3 * r + 1 : 3 * r + 2]
        level = level + levels[3 * r + 2 : 3 * r + 3]
        yours.append(jnp.sum(jnp.where(diagonal(cols), level, 0.0), axis=1, keepdims=True))
    yours = jnp.concatenate(yours, axis=0)
    mine = level_ref[:, 0:1]
    peak = jnp.maximum(mine, yours)
    weight, other_weight = jnp.exp2(mine - peak), jnp.exp2(yours - peak)
    share = weight / (weight + other_weight)
    mean_cell = (mean_ref[...] * share + received * (1.0 - share)).astype(BF16)
    mixed = (
        jnp.dot(mean_cell, triple_ref[:, 2 * channels :], preferred_element_type=F32)
        + triple_bias_ref[:, 2 * channels :]
    ).astype(BF16)
    attended = jnp.dot(mixed, output_ref[...], preferred_element_type=F32) + output_bias_ref[...]
    column = lax.broadcasted_iota(jnp.int32, (cols, 1), 0)
    for r, before in enumerate(split_rows(own_ref)):
        value = before + attended[r * cols : (r + 1) * cols]
        value = jnp.where(column < widths[r], value, 0.0)
        out_ref[r] = value.astype(BF16)
        if r == 0:
            top = value
    odd = lax.rem(info.tile(), 2) == 1
    inner_ref[0] = jnp.where(odd, top, value).astype(BF16)
    outer_ref[0] = jnp.where(odd, value, top).astype(BF16)


def fold_kernel(weight_ref, out_ref):
    channels = weight_ref.shape[-1]
    wide = [[weight_ref[a, b].astype(F32) for b in range(3)] for a in range(3)]

    def both(upper, lower):
        return [x + y for x, y in zip(upper, lower)]

    phases = [[wide[0], both(wide[1], wide[2])], [both(wide[0], wide[1]), wide[2]]]
    for down in range(2):
        for tap in range(2):
            left, middle, right = phases[down][tap]
            out_ref[down, tap, 0, :, 0:channels] = left.astype(BF16)
            out_ref[down, tap, 0, :, channels:] = (middle + right).astype(BF16)
            out_ref[down, tap, 1, :, 0:channels] = (left + middle).astype(BF16)
            out_ref[down, tap, 1, :, channels:] = right.astype(BF16)


def spread_columns(wide_ref, value, row, right):
    cols, channels = value.shape
    for part in range(wide_ref.shape[0]):
        lo, hi = part * LANES, min((part + 1) * LANES, channels)
        piece = value[:, lo:hi]
        if hi - lo < LANES:
            piece = jnp.concatenate([piece, jnp.zeros((cols, LANES - hi + lo), F32)], axis=1)
        wide_ref[part, row, pl.ds(right, cols, 2), :] = piece


def write_turned(out_ref, row, part, value, width):
    channels, cols = out_ref.shape[1:]
    lo, hi = part * LANES, min((part + 1) * LANES, channels)
    turned = value.T[0 : hi - lo, 0:cols]
    column = lax.broadcasted_iota(jnp.int32, (1, cols), 1)
    out_ref[row, lo:hi, :] = jnp.where(column < width, turned, 0.0).astype(BF16)


def phase_product(columns, weight):
    return lax.dot_general(
        columns, weight, (((1,), (1,)), ((), ())), preferred_element_type=F32
    )


def upsample_kernel(
    rows, info_ref, own_ref, weight_ref, bias_ref, out_ref, open_ref, columns_ref, wide_ref
):
    info = Info(info_ref, rows)
    row_count, cols, channels = own_ref.shape
    padded = columns_ref.shape[0] // row_count
    parts_out = wide_ref.shape[0]
    labels, widths = info.window(info.tile() * row_count, row_count)
    build_columns(
        columns_ref, [functools.partial(own_ref.__getitem__, r) for r in range(row_count)]
    )
    inner_rows = (row_count - 1) * padded
    for down in range(2):
        for right in range(2):
            lanes = slice(right * channels, (right + 2) * channels)
            same = phase_product(columns_ref[:, lanes], weight_ref[down, 1 - down, right])
            start = down * padded
            rim = phase_product(
                columns_ref[start : start + inner_rows, lanes], weight_ref[down, down, right]
            )
            for r in range(row_count):
                value = same[r * padded : r * padded + cols]
                near = r - 1 + 2 * down
                if 0 <= near < row_count:
                    lo = (near - down) * padded
                    value = value + jnp.where(
                        labels[near] == labels[r], rim[lo : lo + cols], 0.0
                    )
                spread_columns(wide_ref, value, 2 * r + down, right)
    for part in range(parts_out):
        open_ref[part, 0] = wide_ref[part, 0]
        open_ref[part, 1] = wide_ref[part, 2 * row_count - 1]
    for r in range(1, 2 * row_count - 1):
        for part in range(parts_out):
            value = wide_ref[part, r] + bias_ref[:, part * LANES : (part + 1) * LANES]
            write_turned(out_ref, r - 1, part, value, 2 * widths[r // 2])


def close_kernel(
    rows, info_ref, outer_ref, inner_ref, middle_ref, open_ref, weight_ref, bias_ref, out_ref,
    columns_ref, wide_ref,
):
    info = Info(info_ref, rows)
    wide_rows, _, wide_cols = out_ref.shape
    row_count, cols = wide_rows // 2, wide_cols // 2
    channels = outer_ref.shape[-1]
    padded = columns_ref.shape[0] // 2
    labels, widths = info.window(info.tile() * row_count - 1, row_count + 2)
    above, below = rims(info, outer_ref, inner_ref)
    build_columns(columns_ref, [lambda: above, lambda: below])
    for down in range(2):
        for right in range(2):
            lanes = slice(right * channels, (right + 2) * channels)
            rim = phase_product(
                columns_ref[down * padded : (down + 1) * padded, lanes],
                weight_ref[down, down, right],
            )
            spread_columns(wide_ref, rim[:cols], down, right)
    out_ref[1 : wide_rows - 1] = middle_ref[...]
    for down in range(2):
        rim_row, own_row = (row_count + 1, row_count) if down else (0, 1)
        for part in range(wide_ref.shape[0]):
            rim = jnp.where(labels[rim_row] == labels[own_row], wide_ref[part, down], 0.0)
            value = open_ref[part, down] + rim + bias_ref[:, part * LANES : (part + 1) * LANES]
            write_turned(
                out_ref, down * (wide_rows - 1), part, value, 2 * widths[own_row]
            )


def merge_stats(mine, other):
    count = mine[0] + other[0]
    safe = jnp.maximum(count, 1.0)
    off = other[1] - mine[1]
    mean = mine[1] + off * (other[0] / safe)
    spread = mine[2] + other[2] + off * off * (mine[0] * other[0] / safe)
    return jnp.stack([count, mean, spread])


def exchange(array, tiles, mask, among=None):
    moves = [(i, i ^ mask) for i in range(tiles) if among is None or among(i)]
    return lax.ppermute(array, "tile", moves)


def merge_round(stats, tiles, masks, tied=(), after=None):
    parts = [stats] + [exchange(stats, tiles, mask) for mask in masks]
    free = ()
    if tied:
        *parts[2:], free = lax.optimization_barrier((*parts[2:], after))
        parts[1], *tied = lax.optimization_barrier((parts[1], *tied))
    while len(parts) > 1:
        parts = [merge_stats(*parts[i : i + 2]) for i in range(0, len(parts), 2)]
    return (parts[0], *tied, free) if tied else parts[0]


def merge_masks(tiles):
    bits = [1 << i for i in range(tiles.bit_length() - 1)]
    pairs = [bits[i : i + 2] for i in range(0, len(bits), 2)]
    return [[p[0], p[1], p[0] ^ p[1]] if len(p) == 2 else p for p in pairs]


def shards(
    tiles,
    frames,
    latents,
    row_video,
    video_cols,
    first_gain,
    first_shift,
    conv_weight,
    conv_bias,
    second_gain,
    second_shift,
    triple_weight,
    triple_bias,
    output_weight,
    output_bias,
    upsample_weight,
    upsample_bias,
):
    row_count, frame_count, cols, channels = latents.shape
    assert frame_count == 1 and row_count == ROWS_OF_TILE and tiles % 4 == 0
    out_channels = upsample_weight.shape[-1]
    rows = row_count * tiles
    cells = row_count * cols
    padded = -(-(cols + 1) // 16) * 16
    near_rows = row_count + 2
    source = latents.reshape(row_count, cols, channels)
    tile = lax.axis_index("tile").astype(jnp.int32)
    info = jnp.concatenate([jnp.reshape(tile, (1,)), row_video, video_cols])

    def row(vector):
        return vector.reshape(1, -1)

    def shape(*dims, dtype=BF16):
        return jax.ShapeDtypeStruct(dims, dtype)

    def call(kernel, operands, out_shape, scratch=(), **kwargs):
        many = isinstance(out_shape, tuple)
        return pl.pallas_call(
            kernel,
            out_shape=out_shape,
            in_specs=[SMEM_SPEC] + [VMEM_SPEC] * len(operands),
            out_specs=(VMEM_SPEC,) * len(out_shape) if many else VMEM_SPEC,
            scratch_shapes=list(scratch),
            compiler_params=params(),
            **kwargs,
        )(info, *operands)

    outer_moves = [(i, i - 1 if i % 2 == 0 else i + 1) for i in range(tiles)]
    outer_moves = [(i, j) for i, j in outer_moves if 0 <= j < tiles]
    odd = tile % 2 == 1
    stats_shape = shape(3, SLOTS, LANES, dtype=F32)
    stats = call(
        functools.partial(stats_kernel, rows), [source], stats_shape,
        cost_estimate=cost(1.5), name="first_stats",
    )
    outer = lax.ppermute(
        jnp.where(odd, source[row_count - 1 :], source[:1]), "tile", outer_moves
    )
    inner = exchange(jnp.where(odd, source[:1], source[row_count - 1 :]), tiles, 1)
    stats, outer, inner = lax.optimization_barrier((stats, outer, inner))
    taps = min(3, frames)
    held = [
        pl.pallas_call(
            functools.partial(hold_kernel, backs),
            out_shape=shape(3 * len(backs) * channels, 3 * channels),
            in_specs=[HBM_SPEC],
            out_specs=VMEM_SPEC,
            scratch_shapes=[pltpu.SemaphoreType.DMA((len(backs), 3, 3))],
            compiler_params=pltpu.CompilerParams(vmem_limit_bytes=HOLD_VMEM_BYTES),
            cost_estimate=cost(1.5 * len(backs)),
            name="hold",
        )(conv_weight)
        for backs in ((0,), tuple(range(1, taps)))
        if backs
    ]
    rounds = merge_masks(tiles)
    for index, masks in enumerate(reversed(rounds)):
        stats = merge_round(stats, tiles, masks)
        if index < len(held):
            stats, held[index] = lax.optimization_barrier((stats, held[index]))
    hidden, source = call(
        functools.partial(hidden_kernel, rows),
        [outer, inner, source, stats, row(first_gain), row(first_shift)],
        (shape(near_rows, padded, channels), shape(row_count, cols, channels)),
        cost_estimate=cost(1.3),
        name="hidden",
    )

    earlier = [
        lax.ppermute(hidden, "frame", [(i, i + by) for i in range(frames - by)])
        for by in range(1, taps)
    ]
    pairs = row_count // 2
    pair_shape = shape(pairs, 2 * cols, channels)
    product = call(
        functools.partial(own_conv_kernel, rows),
        [hidden, held[0]],
        shape(row_count * padded, 3 * channels, dtype=F32),
        scratch=[pltpu.VMEM((row_count * padded, 3 * channels), BF16)],
        cost_estimate=cost(2.2),
        name="own_conv",
    )
    scratch = [pltpu.VMEM((row_count * padded, 3 * (taps - 1) * channels), BF16)]
    own, stats = call(
        functools.partial(conv_kernel, rows, taps),
        earlier + [product, source, row(conv_bias)] + held[1:],
        (pair_shape, stats_shape),
        scratch=scratch if taps > 1 else [],
        cost_estimate=cost(1.5 + 2.0 * (taps - 1)),
        name="conv",
    )

    blocks = {0: own}
    neighbour = [(i, i ^ 1) for i in range(tiles)]
    if tiles == 16 and video_cols.shape[0] == 2:
        def middle(t):
            return t // 4 in (1, 2)

        stats = merge_round(stats, tiles, rounds[1])
        blocks[2] = exchange(own, tiles, 4)
        blocks[6] = exchange(own, tiles, 12, middle)
        stats, blocks[2], blocks[6], own_xy = merge_round(
            stats, tiles, rounds[0], (blocks[2], blocks[6]), own
        )
        inward = exchange(blocks[2], tiles, 12, middle)
        outward = exchange(blocks[6], tiles, 4, middle)
        other = exchange(own_xy, tiles, 1)
        blocks[1] = exchange(own_xy, tiles, 2)
        blocks[4] = jnp.where((tile // 4 == 1) | (tile // 4 == 2), inward, outward)
        passed, blocks[4] = lax.optimization_barrier((blocks[1], blocks[4]))
        blocks[5] = exchange(blocks[4], tiles, 2)
        blocks[3] = exchange(passed, tiles, 4)
        blocks[7] = exchange(passed, tiles, 12, middle)
        groups = [[0, 1, 2, 6, 4], [7, 3, 5]]
    else:
        for masks in rounds:
            stats = merge_round(stats, tiles, masks)
        other = exchange(own, tiles, 1)
        for mask in range(1, tiles // 2):
            blocks[mask] = exchange(own, tiles, 2 * mask)
        groups = [list(range(i, i + 4)) for i in range(0, tiles // 2, 4)]
    gain, shift = row(second_gain), row(second_shift)
    table_shape = shape(SLOTS, channels, dtype=F32)
    queries, constant, means, scales = call(
        functools.partial(query_kernel, rows),
        [other, stats, gain, shift, triple_weight, row(triple_bias)],
        (shape(cells, channels), shape(cells, LANES, dtype=F32), table_shape, table_shape),
        cost_estimate=cost(1.5),
        name="queries",
    )
    level_shape = shape(cells, LANES, dtype=F32)
    total_shape = shape(cells, channels, dtype=F32)
    state, keys = (), []
    for index, masks in enumerate(groups):
        last = index == len(groups) - 1
        outs = (shape(len(masks) * cells, channels),)
        outs += (shape(cells + 16, channels),) if last else (level_shape, level_shape, total_shape)
        normed, *state = call(
            functools.partial(attend_yours_kernel, rows, tuple(masks), index == 0, last),
            [means, scales, shift, queries, constant] + [blocks[m] for m in masks] + list(state),
            outs,
            cost_estimate=cost(0.9 * len(masks)),
            name="attend_yours",
        )
        keys.append(normed)
    (sent,) = state
    received = lax.ppermute(sent, "tile", neighbour)
    sent, own_late, upsample_weight = lax.optimization_barrier((sent, own, upsample_weight))
    mean, level = call(
        functools.partial(attend_mine_kernel, rows, tuple(tuple(masks) for masks in groups)),
        [own_late, means, scales, shift, triple_weight, row(triple_bias)] + keys,
        (total_shape, level_shape),
        cost_estimate=cost(6.0),
        name="attend_mine",
    )
    folded = pl.pallas_call(
        fold_kernel,
        out_shape=shape(2, 2, 2, out_channels, 2 * channels),
        in_specs=[VMEM_SPEC],
        out_specs=VMEM_SPEC,
        compiler_params=params(),
        cost_estimate=cost(0.5),
        name="fold",
    )(jnp.swapaxes(upsample_weight, 2, 3))

    rim_shape = shape(1, cols, channels)
    attended, inner, outer = call(
        functools.partial(finish_kernel, rows),
        [
            mean, level, received, own, triple_weight, row(triple_bias), output_weight,
            row(output_bias),
        ],
        (shape(row_count, cols, channels), rim_shape, rim_shape),
        cost_estimate=cost(1.4),
        name="finish",
    )
    outer = lax.ppermute(outer, "tile", outer_moves)
    inner = exchange(inner, tiles, 1)
    parts_out = -(-out_channels // LANES)
    wide_cols = -(-2 * cols // LANES) * LANES
    wide_bias = jnp.pad(row(upsample_bias), ((0, 0), (0, -out_channels % LANES)))
    middle, open_rows = call(
        functools.partial(upsample_kernel, rows),
        [attended, folded, wide_bias],
        (
            shape(2 * row_count - 2, out_channels, 2 * cols),
            shape(parts_out, 2, wide_cols, LANES, dtype=F32),
        ),
        scratch=[
            pltpu.VMEM((row_count * padded, 3 * channels), BF16),
            pltpu.VMEM((parts_out, 2 * row_count, wide_cols, LANES), F32),
        ],
        cost_estimate=cost(2.0),
        name="upsample",
    )
    decoded = call(
        functools.partial(close_kernel, rows),
        [outer, inner, middle, open_rows, folded, wide_bias],
        shape(2 * row_count, out_channels, 2 * cols),
        scratch=[
            pltpu.VMEM((2 * padded, 3 * channels), BF16),
            pltpu.VMEM((parts_out, 2, wide_cols, LANES), F32),
        ],
        cost_estimate=cost(1.0),
        name="close",
    )
    return jnp.swapaxes(decoded, 1, 2).reshape(2 * row_count, 1, 2 * cols, out_channels)


def solution(mesh):
    sizes = dict(mesh.shape)
    in_specs = (P("tile", "frame", None, None),) + (P(),) * 14
    out_specs = P("tile", "frame", None, None)
    body = functools.partial(shards, sizes["tile"], sizes["frame"])
    return jax.shard_map(body, mesh=mesh, in_specs=in_specs, out_specs=out_specs, check_vma=False)
```

```python
import functools
import math

import jax
import jax.numpy as jnp
from jax import lax
from jax.experimental import pallas as pl
from jax.experimental.pallas import tpu as pltpu
from jax.sharding import PartitionSpec as P

GROUPS = 32
EPSILON = 1e-05
MASKED = -1e30
LOWEST = -5e29
SLOTS = 8
ROWS_OF_TILE = 4
LANES = 128
VMEM_BYTES = 24 * 1024 * 1024
HOLD_VMEM_BYTES = 46 * 1024 * 1024
F32 = jnp.float32
BF16 = jnp.bfloat16

SMEM_SPEC = pl.BlockSpec(memory_space=pltpu.SMEM)
VMEM_SPEC = pl.BlockSpec(memory_space=pltpu.VMEM)
HBM_SPEC = pl.BlockSpec(memory_space=pltpu.HBM)


def cost(microseconds):
    return pl.CostEstimate(
        flops=int(microseconds * 1.1e9), bytes_accessed=0, transcendentals=0
    )


def params():
    return pltpu.CompilerParams(vmem_limit_bytes=VMEM_BYTES)


def member_matrix(channels):
    per_group = channels // GROUPS
    group = lax.broadcasted_iota(jnp.int32, (LANES, channels), 0) * per_group
    channel = lax.broadcasted_iota(jnp.int32, (LANES, channels), 1)
    return jnp.where((channel >= group) & (channel < group + per_group), 1.0, 0.0).astype(BF16)


def thirds(values):
    parts = []
    for _ in range(3):
        parts.append(values.astype(BF16).astype(F32))
        values = values - parts[-1]
    return jnp.concatenate(parts, axis=0).astype(BF16)


def added(products):
    rows = products.shape[0] // 3
    return (products[2 * rows :] + products[rows : 2 * rows]) + products[:rows]


def to_groups(values, member):
    return added(
        lax.dot_general(
            thirds(values), member, (((1,), (1,)), ((), ())), preferred_element_type=F32
        )
    )


def to_channels(values, member):
    return added(jnp.dot(thirds(values), member, preferred_element_type=F32))


class Info:
    def __init__(self, ref, rows):
        self.ref, self.rows = ref, rows
        self.videos = ref.shape[0] - 1 - rows

    def tile(self):
        return self.ref[0]

    def label(self, row):
        inside = (row >= 0) & (row < self.rows)
        return jnp.where(inside, self.ref[1 + jnp.clip(row, 0, self.rows - 1)], -1)

    def width(self, label):
        return jnp.where(label >= 0, self.ref[1 + self.rows + jnp.maximum(label, 0)], 0)

    def window(self, first, count):
        labels = [self.label(first + r) for r in range(count)]
        return labels, [self.width(label) for label in labels]


def pick(table, label, videos):
    chosen = table[0:1]
    for video in range(1, videos):
        chosen = jnp.where(label == video, table[video : video + 1], chosen)
    return chosen


def norm_tables(stats_ref, gain_ref):
    member = member_matrix(gain_ref.shape[1])
    counts = jnp.maximum(stats_ref[0], 1.0)
    scale = lax.rsqrt(stats_ref[2] / counts + EPSILON)
    return to_channels(stats_ref[1], member), to_channels(scale, member) * gain_ref[...]


def write_stats(out_ref, rows, labels, widths, videos, channels):
    member = member_matrix(channels)
    per_group = channels // GROUPS
    cols = rows[0].shape[0]
    slot = lax.broadcasted_iota(jnp.int32, (SLOTS, 1), 0)
    column = lax.broadcasted_iota(jnp.int32, (cols, 1), 0)
    sums = jnp.zeros((SLOTS, channels), F32)
    counts = jnp.zeros((SLOTS, 1), F32)
    for index, row in enumerate(rows):
        sums = jnp.where(slot == index, jnp.sum(row, axis=0, keepdims=True), sums)
        counts = jnp.where(slot == index, (widths[index] * per_group).astype(F32), counts)
    means = to_groups(sums, member) / jnp.maximum(counts, 1.0)
    means_wide = to_channels(means, member)
    squares = jnp.zeros((SLOTS, channels), F32)
    for index, row in enumerate(rows):
        centered = jnp.where(column < widths[index], row - means_wide[index : index + 1], 0.0)
        squares = jnp.where(
            slot == index, jnp.sum(centered * centered, axis=0, keepdims=True), squares
        )
    spreads = to_groups(squares, member)
    out_ref[...] = jnp.zeros(out_ref.shape, F32)
    for video in range(videos):
        total = jnp.zeros((1, LANES), F32)
        count = jnp.zeros((1, LANES), F32)
        for index in range(len(rows)):
            mine = labels[index] == video
            row_count = counts[index : index + 1]
            total = total + jnp.where(mine, means[index : index + 1] * row_count, 0.0)
            count = count + jnp.where(mine, row_count, 0.0)
        mean = total / jnp.maximum(count, 1.0)
        spread = jnp.zeros((1, LANES), F32)
        for index in range(len(rows)):
            off = means[index : index + 1] - mean
            part = spreads[index : index + 1] + counts[index : index + 1] * off * off
            spread = spread + jnp.where(labels[index] == video, part, 0.0)
        out_ref[0, video : video + 1, :] = count
        out_ref[1, video : video + 1, :] = mean
        out_ref[2, video : video + 1, :] = spread


def build_columns(columns_ref, row_refs):
    padded = columns_ref.shape[0] // len(row_refs)
    for index, row in enumerate(row_refs):
        cells = row().astype(F32)
        count, channels = cells.shape
        cells = jnp.concatenate([cells, jnp.zeros((padded - count, channels), F32)], axis=0)
        start = index * padded
        columns_ref[start : start + padded, 0:channels] = pltpu.roll(cells, 1, 0).astype(BF16)
        columns_ref[start : start + padded, channels : 2 * channels] = cells.astype(BF16)
        columns_ref[start : start + padded, 2 * channels : 3 * channels] = pltpu.roll(
            cells, padded - 1, 0
        ).astype(BF16)


def stats_kernel(rows, info_ref, latents_ref, out_ref):
    info = Info(info_ref, rows)
    row_count, cols, channels = latents_ref.shape
    labels, widths = info.window(info.tile() * row_count, row_count)
    column = lax.broadcasted_iota(jnp.int32, (cols, 1), 0)
    cells = [
        jnp.where(column < widths[r], latents_ref[r].astype(F32), 0.0) for r in range(row_count)
    ]
    write_stats(out_ref, cells, labels, widths, info.videos, channels)


def rims(info, outer_ref, inner_ref):
    odd = lax.rem(info.tile(), 2) == 1
    inner, outer = inner_ref[0].astype(F32), outer_ref[0].astype(F32)
    return jnp.where(odd, inner, outer), jnp.where(odd, outer, inner)


def hidden_kernel(
    rows, info_ref, outer_ref, inner_ref, latents_ref, stats_ref, gain_ref, shift_ref, out_ref,
    source_ref,
):
    info = Info(info_ref, rows)
    row_count, cols, _ = latents_ref.shape
    labels, widths = info.window(info.tile() * row_count - 1, row_count + 2)
    means, scales = norm_tables(stats_ref, gain_ref)
    column = lax.broadcasted_iota(jnp.int32, (cols, 1), 0)
    above, below = rims(info, outer_ref, inner_ref)
    sources = [above] + [latents_ref[r].astype(F32) for r in range(row_count)] + [below]
    for r, source in enumerate(sources):
        mean = pick(means, labels[r], info.videos)
        scale = pick(scales, labels[r], info.videos)
        normed = (source - mean) * scale + shift_ref[...]
        active = normed / (1.0 + jnp.exp(-normed))
        active = jnp.where(column < widths[r], active, 0.0)
        rest = jnp.zeros((out_ref.shape[1] - cols, active.shape[1]), F32)
        out_ref[r] = jnp.concatenate([active, rest], axis=0).astype(BF16)
    source_ref[...] = latents_ref[...]


def hold_kernel(backs, weight_ref, held_ref, sems):
    channels = weight_ref.shape[-1]
    copies = [
        pltpu.make_async_copy(
            weight_ref.at[2 - back, tap, side],
            held_ref.at[
                pl.ds((3 * index + tap) * channels, channels), pl.ds(side * channels, channels)
            ],
            sems.at[index, tap, side],
        )
        for index, back in enumerate(backs)
        for tap in range(3)
        for side in range(3)
    ]
    for copy in copies:
        copy.start()
    for copy in copies:
        copy.wait()


def row_taps(info, hidden_refs, inputs_ref):
    near_rows, padded, channels = hidden_refs[0].shape
    row_count = near_rows - 2
    labels, _ = info.window(info.tile() * row_count - 1, near_rows)
    for back, hidden_ref in enumerate(hidden_refs):
        for tap in range(3):
            lanes = slice((3 * back + tap) * channels, (3 * back + tap + 1) * channels)
            for r in range(row_count):
                block = hidden_ref[r + tap]
                if tap != 1:
                    same = labels[r + tap] == labels[r + 1]
                    block = jnp.where(same, block, jnp.zeros_like(block))
                inputs_ref[r * padded : (r + 1) * padded, lanes] = block


def own_conv_kernel(rows, info_ref, hidden_ref, held_ref, product_ref, inputs_ref):
    row_taps(Info(info_ref, rows), [hidden_ref], inputs_ref)
    product_ref[...] = jnp.dot(inputs_ref[...], held_ref[...], preferred_element_type=F32)


def conv_kernel(rows, taps, info_ref, *rest):
    hidden_refs, rest = rest[: taps - 1], rest[taps - 1 :]
    product_ref, latents_ref, bias_ref, *rest = rest
    held_refs, (own_ref, stats_ref, *inputs_refs) = rest[: taps > 1], rest[taps > 1 :]
    row_count, cols, channels = latents_ref.shape
    info = Info(info_ref, rows)
    padded = product_ref.shape[0] // row_count
    labels, widths = info.window(info.tile() * row_count - 1, row_count + 2)
    product = product_ref[...]
    if hidden_refs:
        (inputs_ref,) = inputs_refs
        row_taps(info, hidden_refs, inputs_ref)
        product = product + jnp.dot(
            inputs_ref[...], held_refs[0][...], preferred_element_type=F32
        )
    column = lax.broadcasted_iota(jnp.int32, (cols, 1), 0)
    cells = []
    for r in range(row_count):
        lines = slice(r * padded, (r + 1) * padded)
        branch = pltpu.roll(product[lines, 0:channels], 1, 0)
        branch = branch + product[lines, channels : 2 * channels]
        branch = branch + pltpu.roll(product[lines, 2 * channels :], padded - 1, 0)
        value = latents_ref[r].astype(F32) + branch[:cols] + bias_ref[...]
        value = jnp.where(column < widths[r + 1], value, 0.0).astype(BF16)
        cells.append(value.astype(F32))
    for pair in range(row_count // 2):
        own_ref[pair] = jnp.concatenate(cells[2 * pair : 2 * pair + 2], axis=0).astype(BF16)
    write_stats(stats_ref, cells, labels[1:-1], widths[1:-1], info.videos, channels)


def split_rows(pairs_ref):
    cols = pairs_ref.shape[1] // 2
    cells = []
    for pair in range(pairs_ref.shape[0]):
        both = pairs_ref[pair].astype(F32)
        cells += [both[:cols], both[cols:]]
    return cells


def turned_queries(info, tile, pairs_ref, means, scales, shift_ref, weight_ref, bias_ref):
    pairs, double, channels = pairs_ref.shape
    cols = double // 2
    column = lax.broadcasted_iota(jnp.int32, (cols, 1), 0)
    labels, widths = info.window(tile * 2 * pairs, 2 * pairs)
    cells = []
    for r, values in enumerate(split_rows(pairs_ref)):
        mean = pick(means, labels[r], info.videos)
        scale = pick(scales, labels[r], info.videos)
        normed = (values - mean) * scale + shift_ref[...]
        cells.append(jnp.where(column < widths[r], normed, 0.0))
    cells = jnp.concatenate(cells, axis=0).astype(BF16)
    queries = (
        jnp.dot(cells, weight_ref[:, 0:channels], preferred_element_type=F32)
        + bias_ref[:, 0:channels]
    ).astype(BF16)
    factor = channels ** (-0.5) * math.log2(math.e)
    turned = lax.dot_general(
        queries, weight_ref[:, channels : 2 * channels], (((1,), (1,)), ((), ())),
        preferred_element_type=F32,
    )
    constant = jnp.sum(
        queries.astype(F32) * bias_ref[:, channels : 2 * channels], axis=1, keepdims=True
    )
    return (turned * factor).astype(BF16), constant * factor


def query_kernel(
    rows, info_ref, other_ref, stats_ref, gain_ref, shift_ref, weight_ref, bias_ref, queries_ref,
    constant_ref, means_ref, scales_ref,
):
    info = Info(info_ref, rows)
    means, scales = norm_tables(stats_ref, gain_ref)
    means_ref[...] = means
    scales_ref[...] = scales
    queries, constant = turned_queries(
        info, info.tile() ^ 1, other_ref, means, scales, shift_ref, weight_ref, bias_ref
    )
    queries_ref[...] = queries
    constant_ref[...] = jnp.broadcast_to(constant, constant_ref.shape)


def key_codes(info, masks, span, cols):
    row_count = span // cols
    position = lax.broadcasted_iota(jnp.int32, (1, len(masks) * span), 1)
    codes = jnp.full((1, len(masks) * span), -2.0, F32)
    for index, mask in enumerate(masks):
        near, widths = info.window((info.tile() ^ (2 * mask)) * row_count, row_count)
        for r in range(row_count):
            start = index * span + r * cols
            inside = (position >= start) & (position < start + widths[r])
            codes = jnp.where(inside, near[r].astype(F32), codes)
    return codes


def query_codes(info, tile, span, cols):
    row_count = span // cols
    labels, _ = info.window(tile * row_count, row_count)
    return jnp.concatenate(
        [jnp.zeros((cols, 1), F32) + label.astype(F32) for label in labels], axis=0
    )


def scores_of(queries, keys, codes, query_code):
    scores = lax.dot_general(
        queries, keys, (((1,), (1,)), ((), ())), preferred_element_type=F32
    )
    return jnp.where(codes == query_code, scores, MASKED)


def mean_and_level(peak, denominator, total):
    some = denominator > 0.0
    safe = jnp.where(some, denominator, 1.0)
    return total / safe, jnp.where(some, peak + jnp.log2(safe), LOWEST)


def attend_yours_kernel(rows, masks, first, last, info_ref, *rest):
    means_ref, scales_ref, shift_ref, queries_ref, constant_ref, *rest = rest
    block_refs, rest = rest[: len(masks)], rest[len(masks) :]
    if not first:
        old_peak_ref, old_sum_ref, old_total_ref, *rest = rest
    keys_ref, *out_refs = rest
    info = Info(info_ref, rows)
    span, channels = queries_ref.shape
    pairs, double, _ = block_refs[0].shape
    cols = double // 2
    row_count = 2 * pairs
    tile = info.tile()
    means, scales = means_ref[...], scales_ref[...]
    for index, (mask, block_ref) in enumerate(zip(masks, block_refs)):
        near, _ = info.window((tile ^ (2 * mask)) * row_count, row_count)
        for pair in range(pairs):
            both = block_ref[pair].astype(F32)
            halves = []
            for half in range(2):
                label = near[2 * pair + half]
                mean = pick(means, label, info.videos)
                scale = pick(scales, label, info.videos)
                values = both[half * cols : (half + 1) * cols]
                halves.append((values - mean) * scale + shift_ref[...])
            start = index * span + pair * double
            keys_ref[start : start + double, :] = jnp.concatenate(halves, axis=0).astype(BF16)
    constant = constant_ref[:, 0:1]
    scores = scores_of(
        queries_ref[...], keys_ref[...], key_codes(info, masks, span, cols),
        query_codes(info, tile ^ 1, span, cols),
    )
    peak = jnp.maximum(LOWEST, jnp.max(scores, axis=1, keepdims=True) + constant)
    if not first:
        largest = old_peak_ref[:, 0:1]
        peak = jnp.maximum(largest, peak)
    weights = jnp.exp2(scores - (peak - constant))
    denominator = jnp.sum(weights, axis=1, keepdims=True)
    total = jnp.dot(weights.astype(BF16), keys_ref[...], preferred_element_type=F32)
    if not first:
        factor = jnp.exp2(largest - peak)
        denominator = old_sum_ref[:, 0:1] * factor + denominator
        total = old_total_ref[...] * factor + total
    if not last:
        peak_ref, sum_ref, total_ref = out_refs
        peak_ref[...] = jnp.broadcast_to(peak, peak_ref.shape)
        sum_ref[...] = jnp.broadcast_to(denominator, sum_ref.shape)
        total_ref[...] = total
        return
    (sent_ref,) = out_refs
    mean, level = mean_and_level(peak, denominator, total)
    sent_ref[0:span, :] = mean.astype(BF16)
    slots = sent_ref.shape[0] - span
    slot = lax.broadcasted_iota(jnp.int32, (slots, 1), 0)
    packed = jnp.zeros((slots, LANES), F32)
    for r in range(row_count):
        left = level[r * cols : (r + 1) * cols]
        left = jnp.sum(jnp.where(diagonal(cols), left, 0.0), axis=0, keepdims=True)
        for part in range(3):
            rounded = left.astype(BF16).astype(F32)
            packed = jnp.where(slot == 3 * r + part, rounded, packed)
            left = left - rounded
    sent_ref[span:, 0:LANES] = packed.astype(BF16)
    sent_ref[span:, LANES:] = jnp.zeros((slots, channels - LANES), BF16)


def attend_mine_kernel(
    rows, groups, info_ref, own_ref, means_ref, scales_ref, shift_ref, weight_ref, bias_ref, *rest
):
    key_refs, (mean_ref, level_ref) = rest[: len(groups)], rest[len(groups) :]
    info = Info(info_ref, rows)
    span = mean_ref.shape[0]
    queries, constant = turned_queries(
        info, info.tile(), own_ref, means_ref[...], scales_ref[...], shift_ref, weight_ref,
        bias_ref,
    )
    cols = span // ROWS_OF_TILE
    query_code = query_codes(info, info.tile(), span, cols)
    peak = jnp.full((span, 1), LOWEST, F32)
    scores = []
    for masks, key_ref in zip(groups, key_refs):
        codes = key_codes(info, masks, span, cols)
        scores.append(scores_of(queries, key_ref[...], codes, query_code))
        peak = jnp.maximum(peak, jnp.max(scores[-1], axis=1, keepdims=True) + constant)
    denominator, total = 0.0, 0.0
    for part, key_ref in zip(scores, key_refs):
        weights = jnp.exp2(part - (peak - constant))
        denominator = denominator + jnp.sum(weights, axis=1, keepdims=True)
        total = total + jnp.dot(
            weights.astype(BF16), key_ref[...], preferred_element_type=F32
        )
    mean, level = mean_and_level(peak, denominator, total)
    mean_ref[...] = mean
    level_ref[...] = jnp.broadcast_to(level, level_ref.shape)


def diagonal(cols):
    return lax.broadcasted_iota(jnp.int32, (cols, LANES), 0) == lax.broadcasted_iota(
        jnp.int32, (cols, LANES), 1
    )


def finish_kernel(
    rows, info_ref, mean_ref, level_ref, received_ref, own_ref, triple_ref, triple_bias_ref,
    output_ref, output_bias_ref, out_ref, inner_ref, outer_ref,
):
    info = Info(info_ref, rows)
    row_count, cols, channels = out_ref.shape
    span = row_count * cols
    _, widths = info.window(info.tile() * row_count, row_count)
    received = received_ref[0:span, :].astype(F32)
    levels = received_ref[span:, 0:LANES].astype(F32)
    yours = []
    for r in range(row_count):
        level = levels[3 * r : 3 * r + 1] + levels[3 * r + 1 : 3 * r + 2]
        level = level + levels[3 * r + 2 : 3 * r + 3]
        yours.append(jnp.sum(jnp.where(diagonal(cols), level, 0.0), axis=1, keepdims=True))
    yours = jnp.concatenate(yours, axis=0)
    mine = level_ref[:, 0:1]
    peak = jnp.maximum(mine, yours)
    weight, other_weight = jnp.exp2(mine - peak), jnp.exp2(yours - peak)
    share = weight / (weight + other_weight)
    mean_cell = (mean_ref[...] * share + received * (1.0 - share)).astype(BF16)
    mixed = (
        jnp.dot(mean_cell, triple_ref[:, 2 * channels :], preferred_element_type=F32)
        + triple_bias_ref[:, 2 * channels :]
    ).astype(BF16)
    attended = jnp.dot(mixed, output_ref[...], preferred_element_type=F32) + output_bias_ref[...]
    column = lax.broadcasted_iota(jnp.int32, (cols, 1), 0)
    for r, before in enumerate(split_rows(own_ref)):
        value = before + attended[r * cols : (r + 1) * cols]
        value = jnp.where(column < widths[r], value, 0.0)
        out_ref[r] = value.astype(BF16)
        if r == 0:
            top = value
    odd = lax.rem(info.tile(), 2) == 1
    inner_ref[0] = jnp.where(odd, top, value).astype(BF16)
    outer_ref[0] = jnp.where(odd, value, top).astype(BF16)


def fold_kernel(weight_ref, out_ref):
    channels = weight_ref.shape[-1]
    wide = [[weight_ref[a, b].astype(F32) for b in range(3)] for a in range(3)]

    def both(upper, lower):
        return [x + y for x, y in zip(upper, lower)]

    phases = [[wide[0], both(wide[1], wide[2])], [both(wide[0], wide[1]), wide[2]]]
    for down in range(2):
        for tap in range(2):
            left, middle, right = phases[down][tap]
            out_ref[down, tap, 0, :, 0:channels] = left.astype(BF16)
            out_ref[down, tap, 0, :, channels:] = (middle + right).astype(BF16)
            out_ref[down, tap, 1, :, 0:channels] = (left + middle).astype(BF16)
            out_ref[down, tap, 1, :, channels:] = right.astype(BF16)


def spread_columns(wide_ref, value, row, right):
    cols, channels = value.shape
    for part in range(wide_ref.shape[0]):
        lo, hi = part * LANES, min((part + 1) * LANES, channels)
        piece = value[:, lo:hi]
        if hi - lo < LANES:
            piece = jnp.concatenate([piece, jnp.zeros((cols, LANES - hi + lo), F32)], axis=1)
        wide_ref[part, row, pl.ds(right, cols, 2), :] = piece


def write_turned(out_ref, row, part, value, width):
    channels, cols = out_ref.shape[1:]
    lo, hi = part * LANES, min((part + 1) * LANES, channels)
    turned = value.T[0 : hi - lo, 0:cols]
    column = lax.broadcasted_iota(jnp.int32, (1, cols), 1)
    out_ref[row, lo:hi, :] = jnp.where(column < width, turned, 0.0).astype(BF16)


def phase_product(columns, weight):
    return lax.dot_general(
        columns, weight, (((1,), (1,)), ((), ())), preferred_element_type=F32
    )


def upsample_kernel(
    rows, info_ref, own_ref, weight_ref, bias_ref, out_ref, open_ref, columns_ref, wide_ref
):
    info = Info(info_ref, rows)
    row_count, cols, channels = own_ref.shape
    padded = columns_ref.shape[0] // row_count
    parts_out = wide_ref.shape[0]
    labels, widths = info.window(info.tile() * row_count, row_count)
    build_columns(
        columns_ref, [functools.partial(own_ref.__getitem__, r) for r in range(row_count)]
    )
    inner_rows = (row_count - 1) * padded
    for down in range(2):
        for right in range(2):
            lanes = slice(right * channels, (right + 2) * channels)
            same = phase_product(columns_ref[:, lanes], weight_ref[down, 1 - down, right])
            start = down * padded
            rim = phase_product(
                columns_ref[start : start + inner_rows, lanes], weight_ref[down, down, right]
            )
            for r in range(row_count):
                value = same[r * padded : r * padded + cols]
                near = r - 1 + 2 * down
                if 0 <= near < row_count:
                    lo = (near - down) * padded
                    value = value + jnp.where(
                        labels[near] == labels[r], rim[lo : lo + cols], 0.0
                    )
                spread_columns(wide_ref, value, 2 * r + down, right)
    for part in range(parts_out):
        open_ref[part, 0] = wide_ref[part, 0]
        open_ref[part, 1] = wide_ref[part, 2 * row_count - 1]
    for r in range(1, 2 * row_count - 1):
        for part in range(parts_out):
            value = wide_ref[part, r] + bias_ref[:, part * LANES : (part + 1) * LANES]
            write_turned(out_ref, r - 1, part, value, 2 * widths[r // 2])


def close_kernel(
    rows, info_ref, outer_ref, inner_ref, middle_ref, open_ref, weight_ref, bias_ref, out_ref,
    columns_ref, wide_ref,
):
    info = Info(info_ref, rows)
    wide_rows, _, wide_cols = out_ref.shape
    row_count, cols = wide_rows // 2, wide_cols // 2
    channels = outer_ref.shape[-1]
    padded = columns_ref.shape[0] // 2
    labels, widths = info.window(info.tile() * row_count - 1, row_count + 2)
    above, below = rims(info, outer_ref, inner_ref)
    build_columns(columns_ref, [lambda: above, lambda: below])
    for down in range(2):
        for right in range(2):
            lanes = slice(right * channels, (right + 2) * channels)
            rim = phase_product(
                columns_ref[down * padded : (down + 1) * padded, lanes],
                weight_ref[down, down, right],
            )
            spread_columns(wide_ref, rim[:cols], down, right)
    out_ref[1 : wide_rows - 1] = middle_ref[...]
    for down in range(2):
        rim_row, own_row = (row_count + 1, row_count) if down else (0, 1)
        for part in range(wide_ref.shape[0]):
            rim = jnp.where(labels[rim_row] == labels[own_row], wide_ref[part, down], 0.0)
            value = open_ref[part, down] + rim + bias_ref[:, part * LANES : (part + 1) * LANES]
            write_turned(
                out_ref, down * (wide_rows - 1), part, value, 2 * widths[own_row]
            )


def merge_stats(mine, other):
    count = mine[0] + other[0]
    safe = jnp.maximum(count, 1.0)
    off = other[1] - mine[1]
    mean = mine[1] + off * (other[0] / safe)
    spread = mine[2] + other[2] + off * off * (mine[0] * other[0] / safe)
    return jnp.stack([count, mean, spread])


def exchange(array, tiles, mask, among=None):
    moves = [(i, i ^ mask) for i in range(tiles) if among is None or among(i)]
    return lax.ppermute(array, "tile", moves)


def merge_round(stats, tiles, masks, tied=(), after=None):
    parts = [stats] + [exchange(stats, tiles, mask) for mask in masks]
    free = ()
    if tied:
        *parts[2:], free = lax.optimization_barrier((*parts[2:], after))
        parts[1], *tied = lax.optimization_barrier((parts[1], *tied))
    while len(parts) > 1:
        parts = [merge_stats(*parts[i : i + 2]) for i in range(0, len(parts), 2)]
    return (parts[0], *tied, free) if tied else parts[0]


def merge_masks(tiles):
    bits = [1 << i for i in range(tiles.bit_length() - 1)]
    pairs = [bits[i : i + 2] for i in range(0, len(bits), 2)]
    return [[p[0], p[1], p[0] ^ p[1]] if len(p) == 2 else p for p in pairs]


def shards(
    tiles,
    frames,
    latents,
    row_video,
    video_cols,
    first_gain,
    first_shift,
    conv_weight,
    conv_bias,
    second_gain,
    second_shift,
    triple_weight,
    triple_bias,
    output_weight,
    output_bias,
    upsample_weight,
    upsample_bias,
):
    row_count, frame_count, cols, channels = latents.shape
    assert frame_count == 1 and row_count == ROWS_OF_TILE and tiles % 4 == 0
    out_channels = upsample_weight.shape[-1]
    rows = row_count * tiles
    cells = row_count * cols
    padded = -(-(cols + 1) // 16) * 16
    near_rows = row_count + 2
    source = latents.reshape(row_count, cols, channels)
    tile = lax.axis_index("tile").astype(jnp.int32)
    info = jnp.concatenate([jnp.reshape(tile, (1,)), row_video, video_cols])

    def row(vector):
        return vector.reshape(1, -1)

    def shape(*dims, dtype=BF16):
        return jax.ShapeDtypeStruct(dims, dtype)

    def call(kernel, operands, out_shape, scratch=(), **kwargs):
        many = isinstance(out_shape, tuple)
        return pl.pallas_call(
            kernel,
            out_shape=out_shape,
            in_specs=[SMEM_SPEC] + [VMEM_SPEC] * len(operands),
            out_specs=(VMEM_SPEC,) * len(out_shape) if many else VMEM_SPEC,
            scratch_shapes=list(scratch),
            compiler_params=params(),
            **kwargs,
        )(info, *operands)

    outer_moves = [(i, i - 1 if i % 2 == 0 else i + 1) for i in range(tiles)]
    outer_moves = [(i, j) for i, j in outer_moves if 0 <= j < tiles]
    odd = tile % 2 == 1
    stats_shape = shape(3, SLOTS, LANES, dtype=F32)
    stats = call(
        functools.partial(stats_kernel, rows), [source], stats_shape,
        cost_estimate=cost(1.5), name="first_stats",
    )
    outer = lax.ppermute(
        jnp.where(odd, source[row_count - 1 :], source[:1]), "tile", outer_moves
    )
    inner = exchange(jnp.where(odd, source[:1], source[row_count - 1 :]), tiles, 1)
    stats, outer, inner = lax.optimization_barrier((stats, outer, inner))
    taps = min(3, frames)
    held = [
        pl.pallas_call(
            functools.partial(hold_kernel, backs),
            out_shape=shape(3 * len(backs) * channels, 3 * channels),
            in_specs=[HBM_SPEC],
            out_specs=VMEM_SPEC,
            scratch_shapes=[pltpu.SemaphoreType.DMA((len(backs), 3, 3))],
            compiler_params=pltpu.CompilerParams(vmem_limit_bytes=HOLD_VMEM_BYTES),
            cost_estimate=cost(1.5 * len(backs)),
            name="hold",
        )(conv_weight)
        for backs in ((0,), tuple(range(1, taps)))
        if backs
    ]
    rounds = merge_masks(tiles)
    for index, masks in enumerate(reversed(rounds)):
        stats = merge_round(stats, tiles, masks)
        if index < len(held):
            stats, held[index] = lax.optimization_barrier((stats, held[index]))
    hidden, source = call(
        functools.partial(hidden_kernel, rows),
        [outer, inner, source, stats, row(first_gain), row(first_shift)],
        (shape(near_rows, padded, channels), shape(row_count, cols, channels)),
        cost_estimate=cost(1.3),
        name="hidden",
    )

    earlier = [
        lax.ppermute(hidden, "frame", [(i, i + by) for i in range(frames - by)])
        for by in range(1, taps)
    ]
    pairs = row_count // 2
    pair_shape = shape(pairs, 2 * cols, channels)
    product = call(
        functools.partial(own_conv_kernel, rows),
        [hidden, held[0]],
        shape(row_count * padded, 3 * channels, dtype=F32),
        scratch=[pltpu.VMEM((row_count * padded, 3 * channels), BF16)],
        cost_estimate=cost(2.2),
        name="own_conv",
    )
    scratch = [pltpu.VMEM((row_count * padded, 3 * (taps - 1) * channels), BF16)]
    own, stats = call(
        functools.partial(conv_kernel, rows, taps),
        earlier + [product, source, row(conv_bias)] + held[1:],
        (pair_shape, stats_shape),
        scratch=scratch if taps > 1 else [],
        cost_estimate=cost(1.5 + 2.0 * (taps - 1)),
        name="conv",
    )

    blocks = {0: own}
    neighbour = [(i, i ^ 1) for i in range(tiles)]
    if tiles == 16 and video_cols.shape[0] == 2:
        def middle(t):
            return t // 4 in (1, 2)

        stats = merge_round(stats, tiles, rounds[1])
        blocks[2] = exchange(own, tiles, 4)
        blocks[6] = exchange(own, tiles, 12, middle)
        stats, blocks[2], blocks[6], own_xy = merge_round(
            stats, tiles, rounds[0], (blocks[2], blocks[6]), own
        )
        inward = exchange(blocks[2], tiles, 12, middle)
        outward = exchange(blocks[6], tiles, 4, middle)
        other = exchange(own_xy, tiles, 1)
        blocks[1] = exchange(own_xy, tiles, 2)
        blocks[4] = jnp.where((tile // 4 == 1) | (tile // 4 == 2), inward, outward)
        passed, blocks[4] = lax.optimization_barrier((blocks[1], blocks[4]))
        blocks[5] = exchange(blocks[4], tiles, 2)
        blocks[3] = exchange(passed, tiles, 4)
        blocks[7] = exchange(passed, tiles, 12, middle)
        groups = [[0, 1, 2, 6, 4], [7, 3, 5]]
    else:
        for masks in rounds:
            stats = merge_round(stats, tiles, masks)
        other = exchange(own, tiles, 1)
        for mask in range(1, tiles // 2):
            blocks[mask] = exchange(own, tiles, 2 * mask)
        groups = [list(range(i, i + 4)) for i in range(0, tiles // 2, 4)]
    gain, shift = row(second_gain), row(second_shift)
    table_shape = shape(SLOTS, channels, dtype=F32)
    queries, constant, means, scales = call(
        functools.partial(query_kernel, rows),
        [other, stats, gain, shift, triple_weight, row(triple_bias)],
        (shape(cells, channels), shape(cells, LANES, dtype=F32), table_shape, table_shape),
        cost_estimate=cost(1.5),
        name="queries",
    )
    level_shape = shape(cells, LANES, dtype=F32)
    total_shape = shape(cells, channels, dtype=F32)
    state, keys = (), []
    for index, masks in enumerate(groups):
        last = index == len(groups) - 1
        outs = (shape(len(masks) * cells, channels),)
        outs += (shape(cells + 16, channels),) if last else (level_shape, level_shape, total_shape)
        normed, *state = call(
            functools.partial(attend_yours_kernel, rows, tuple(masks), index == 0, last),
            [means, scales, shift, queries, constant] + [blocks[m] for m in masks] + list(state),
            outs,
            cost_estimate=cost(0.9 * len(masks)),
            name="attend_yours",
        )
        keys.append(normed)
    (sent,) = state
    received = lax.ppermute(sent, "tile", neighbour)
    sent, own_late, upsample_weight = lax.optimization_barrier((sent, own, upsample_weight))
    mean, level = call(
        functools.partial(attend_mine_kernel, rows, tuple(tuple(masks) for masks in groups)),
        [own_late, means, scales, shift, triple_weight, row(triple_bias)] + keys,
        (total_shape, level_shape),
        cost_estimate=cost(6.0),
        name="attend_mine",
    )
    folded = pl.pallas_call(
        fold_kernel,
        out_shape=shape(2, 2, 2, out_channels, 2 * channels),
        in_specs=[VMEM_SPEC],
        out_specs=VMEM_SPEC,
        compiler_params=params(),
        cost_estimate=cost(0.5),
        name="fold",
    )(jnp.swapaxes(upsample_weight, 2, 3))

    rim_shape = shape(1, cols, channels)
    attended, inner, outer = call(
        functools.partial(finish_kernel, rows),
        [
            mean, level, received, own, triple_weight, row(triple_bias), output_weight,
            row(output_bias),
        ],
        (shape(row_count, cols, channels), rim_shape, rim_shape),
        cost_estimate=cost(1.4),
        name="finish",
    )
    outer = lax.ppermute(outer, "tile", outer_moves)
    inner = exchange(inner, tiles, 1)
    parts_out = -(-out_channels // LANES)
    wide_cols = -(-2 * cols // LANES) * LANES
    wide_bias = jnp.pad(row(upsample_bias), ((0, 0), (0, -out_channels % LANES)))
    middle, open_rows = call(
        functools.partial(upsample_kernel, rows),
        [attended, folded, wide_bias],
        (
            shape(2 * row_count - 2, out_channels, 2 * cols),
            shape(parts_out, 2, wide_cols, LANES, dtype=F32),
        ),
        scratch=[
            pltpu.VMEM((row_count * padded, 3 * channels), BF16),
            pltpu.VMEM((parts_out, 2 * row_count, wide_cols, LANES), F32),
        ],
        cost_estimate=cost(2.0),
        name="upsample",
    )
    decoded = call(
        functools.partial(close_kernel, rows),
        [outer, inner, middle, open_rows, folded, wide_bias],
        shape(2 * row_count, out_channels, 2 * cols),
        scratch=[
            pltpu.VMEM((2 * padded, 3 * channels), BF16),
            pltpu.VMEM((parts_out, 2, wide_cols, LANES), F32),
        ],
        cost_estimate=cost(1.0),
        name="close",
    )
    return jnp.swapaxes(decoded, 1, 2).reshape(2 * row_count, 1, 2 * cols, out_channels)


def solution(mesh):
    sizes = dict(mesh.shape)
    in_specs = (P("tile", "frame", None, None),) + (P(),) * 14
    out_specs = P("tile", "frame", None, None)
    body = functools.partial(shards, sizes["tile"], sizes["frame"])
    return jax.shard_map(body, mesh=mesh, in_specs=in_specs, out_specs=out_specs, check_vma=False)
```

```python
import functools
import math

import jax
import jax.numpy as jnp
from jax import lax
from jax.experimental import pallas as pl
from jax.experimental.pallas import tpu as pltpu
from jax.sharding import PartitionSpec as P

GROUPS = 32
EPSILON = 1e-05
MASKED = -1e30
LOWEST = -5e29
SLOTS = 8
ROWS_OF_TILE = 4
LANES = 128
VMEM_BYTES = 24 * 1024 * 1024
HOLD_VMEM_BYTES = 46 * 1024 * 1024
F32 = jnp.float32
BF16 = jnp.bfloat16

SMEM_SPEC = pl.BlockSpec(memory_space=pltpu.SMEM)
VMEM_SPEC = pl.BlockSpec(memory_space=pltpu.VMEM)
HBM_SPEC = pl.BlockSpec(memory_space=pltpu.HBM)


def cost(microseconds):
    return pl.CostEstimate(
        flops=int(microseconds * 1.1e9), bytes_accessed=0, transcendentals=0
    )


def params():
    return pltpu.CompilerParams(vmem_limit_bytes=VMEM_BYTES)


def member_matrix(channels):
    per_group = channels // GROUPS
    group = lax.broadcasted_iota(jnp.int32, (LANES, channels), 0) * per_group
    channel = lax.broadcasted_iota(jnp.int32, (LANES, channels), 1)
    return jnp.where((channel >= group) & (channel < group + per_group), 1.0, 0.0).astype(BF16)


def thirds(values):
    parts = []
    for _ in range(3):
        parts.append(values.astype(BF16).astype(F32))
        values = values - parts[-1]
    return jnp.concatenate(parts, axis=0).astype(BF16)


def added(products):
    rows = products.shape[0] // 3
    return (products[2 * rows :] + products[rows : 2 * rows]) + products[:rows]


def to_groups(values, member):
    return added(
        lax.dot_general(
            thirds(values), member, (((1,), (1,)), ((), ())), preferred_element_type=F32
        )
    )


def to_channels(values, member):
    return added(jnp.dot(thirds(values), member, preferred_element_type=F32))


class Info:
    def __init__(self, ref, rows):
        self.ref, self.rows = ref, rows
        self.videos = ref.shape[0] - 1 - rows

    def tile(self):
        return self.ref[0]

    def label(self, row):
        inside = (row >= 0) & (row < self.rows)
        return jnp.where(inside, self.ref[1 + jnp.clip(row, 0, self.rows - 1)], -1)

    def width(self, label):
        return jnp.where(label >= 0, self.ref[1 + self.rows + jnp.maximum(label, 0)], 0)

    def window(self, first, count):
        labels = [self.label(first + r) for r in range(count)]
        return labels, [self.width(label) for label in labels]


def pick(table, label, videos):
    chosen = table[0:1]
    for video in range(1, videos):
        chosen = jnp.where(label == video, table[video : video + 1], chosen)
    return chosen


def norm_tables(stats_ref, gain_ref):
    member = member_matrix(gain_ref.shape[1])
    counts = jnp.maximum(stats_ref[0], 1.0)
    scale = lax.rsqrt(stats_ref[2] / counts + EPSILON)
    return to_channels(stats_ref[1], member), to_channels(scale, member) * gain_ref[...]


def write_stats(out_ref, rows, labels, widths, videos, channels):
    member = member_matrix(channels)
    per_group = channels // GROUPS
    cols = rows[0].shape[0]
    slot = lax.broadcasted_iota(jnp.int32, (SLOTS, 1), 0)
    column = lax.broadcasted_iota(jnp.int32, (cols, 1), 0)
    sums = jnp.zeros((SLOTS, channels), F32)
    counts = jnp.zeros((SLOTS, 1), F32)
    for index, row in enumerate(rows):
        sums = jnp.where(slot == index, jnp.sum(row, axis=0, keepdims=True), sums)
        counts = jnp.where(slot == index, (widths[index] * per_group).astype(F32), counts)
    means = to_groups(sums, member) / jnp.maximum(counts, 1.0)
    means_wide = to_channels(means, member)
    squares = jnp.zeros((SLOTS, channels), F32)
    for index, row in enumerate(rows):
        centered = jnp.where(column < widths[index], row - means_wide[index : index + 1], 0.0)
        squares = jnp.where(
            slot == index, jnp.sum(centered * centered, axis=0, keepdims=True), squares
        )
    spreads = to_groups(squares, member)
    out_ref[...] = jnp.zeros(out_ref.shape, F32)
    for video in range(videos):
        total = jnp.zeros((1, LANES), F32)
        count = jnp.zeros((1, LANES), F32)
        for index in range(len(rows)):
            mine = labels[index] == video
            row_count = counts[index : index + 1]
            total = total + jnp.where(mine, means[index : index + 1] * row_count, 0.0)
            count = count + jnp.where(mine, row_count, 0.0)
        mean = total / jnp.maximum(count, 1.0)
        spread = jnp.zeros((1, LANES), F32)
        for index in range(len(rows)):
            off = means[index : index + 1] - mean
            part = spreads[index : index + 1] + counts[index : index + 1] * off * off
            spread = spread + jnp.where(labels[index] == video, part, 0.0)
        out_ref[0, video : video + 1, :] = count
        out_ref[1, video : video + 1, :] = mean
        out_ref[2, video : video + 1, :] = spread


def build_columns(columns_ref, row_refs):
    padded = columns_ref.shape[0] // len(row_refs)
    for index, row in enumerate(row_refs):
        cells = row().astype(F32)
        count, channels = cells.shape
        cells = jnp.concatenate([cells, jnp.zeros((padded - count, channels), F32)], axis=0)
        start = index * padded
        columns_ref[start : start + padded, 0:channels] = pltpu.roll(cells, 1, 0).astype(BF16)
        columns_ref[start : start + padded, channels : 2 * channels] = cells.astype(BF16)
        columns_ref[start : start + padded, 2 * channels : 3 * channels] = pltpu.roll(
            cells, padded - 1, 0
        ).astype(BF16)


def stats_kernel(rows, info_ref, latents_ref, out_ref):
    info = Info(info_ref, rows)
    row_count, cols, channels = latents_ref.shape
    labels, widths = info.window(info.tile() * row_count, row_count)
    column = lax.broadcasted_iota(jnp.int32, (cols, 1), 0)
    cells = [
        jnp.where(column < widths[r], latents_ref[r].astype(F32), 0.0) for r in range(row_count)
    ]
    write_stats(out_ref, cells, labels, widths, info.videos, channels)


def rims(info, outer_ref, inner_ref):
    odd = lax.rem(info.tile(), 2) == 1
    inner, outer = inner_ref[0].astype(F32), outer_ref[0].astype(F32)
    return jnp.where(odd, inner, outer), jnp.where(odd, outer, inner)


def hidden_kernel(
    rows, info_ref, outer_ref, inner_ref, latents_ref, stats_ref, gain_ref, shift_ref, out_ref,
    source_ref,
):
    info = Info(info_ref, rows)
    row_count, cols, _ = latents_ref.shape
    labels, widths = info.window(info.tile() * row_count - 1, row_count + 2)
    means, scales = norm_tables(stats_ref, gain_ref)
    column = lax.broadcasted_iota(jnp.int32, (cols, 1), 0)
    above, below = rims(info, outer_ref, inner_ref)
    sources = [above] + [latents_ref[r].astype(F32) for r in range(row_count)] + [below]
    for r, source in enumerate(sources):
        mean = pick(means, labels[r], info.videos)
        scale = pick(scales, labels[r], info.videos)
        normed = (source - mean) * scale + shift_ref[...]
        active = normed / (1.0 + jnp.exp(-normed))
        active = jnp.where(column < widths[r], active, 0.0)
        rest = jnp.zeros((out_ref.shape[1] - cols, active.shape[1]), F32)
        out_ref[r] = jnp.concatenate([active, rest], axis=0).astype(BF16)
    source_ref[...] = latents_ref[...]


def hold_kernel(backs, weight_ref, held_ref, sems):
    channels = weight_ref.shape[-1]
    copies = [
        pltpu.make_async_copy(
            weight_ref.at[2 - back, tap, side],
            held_ref.at[
                pl.ds((3 * index + tap) * channels, channels), pl.ds(side * channels, channels)
            ],
            sems.at[index, tap, side],
        )
        for index, back in enumerate(backs)
        for tap in range(3)
        for side in range(3)
    ]
    for copy in copies:
        copy.start()
    for copy in copies:
        copy.wait()


def row_taps(info, hidden_refs, inputs_ref):
    near_rows, padded, channels = hidden_refs[0].shape
    row_count = near_rows - 2
    labels, _ = info.window(info.tile() * row_count - 1, near_rows)
    for back, hidden_ref in enumerate(hidden_refs):
        for tap in range(3):
            lanes = slice((3 * back + tap) * channels, (3 * back + tap + 1) * channels)
            for r in range(row_count):
                block = hidden_ref[r + tap]
                if tap != 1:
                    same = labels[r + tap] == labels[r + 1]
                    block = jnp.where(same, block, jnp.zeros_like(block))
                inputs_ref[r * padded : (r + 1) * padded, lanes] = block


def own_conv_kernel(rows, info_ref, hidden_ref, held_ref, product_ref, inputs_ref):
    row_taps(Info(info_ref, rows), [hidden_ref], inputs_ref)
    product_ref[...] = jnp.dot(inputs_ref[...], held_ref[...], preferred_element_type=F32)


def conv_kernel(rows, taps, info_ref, *rest):
    hidden_refs, rest = rest[: taps - 1], rest[taps - 1 :]
    product_ref, latents_ref, bias_ref, *rest = rest
    held_refs, (own_ref, stats_ref, *inputs_refs) = rest[: taps > 1], rest[taps > 1 :]
    row_count, cols, channels = latents_ref.shape
    info = Info(info_ref, rows)
    padded = product_ref.shape[0] // row_count
    labels, widths = info.window(info.tile() * row_count - 1, row_count + 2)
    product = product_ref[...]
    if hidden_refs:
        (inputs_ref,) = inputs_refs
        row_taps(info, hidden_refs, inputs_ref)
        product = product + jnp.dot(
            inputs_ref[...], held_refs[0][...], preferred_element_type=F32
        )
    column = lax.broadcasted_iota(jnp.int32, (cols, 1), 0)
    cells = []
    for r in range(row_count):
        lines = slice(r * padded, (r + 1) * padded)
        branch = pltpu.roll(product[lines, 0:channels], 1, 0)
        branch = branch + product[lines, channels : 2 * channels]
        branch = branch + pltpu.roll(product[lines, 2 * channels :], padded - 1, 0)
        value = latents_ref[r].astype(F32) + branch[:cols] + bias_ref[...]
        value = jnp.where(column < widths[r + 1], value, 0.0).astype(BF16)
        cells.append(value.astype(F32))
    for pair in range(row_count // 2):
        own_ref[pair] = jnp.concatenate(cells[2 * pair : 2 * pair + 2], axis=0).astype(BF16)
    write_stats(stats_ref, cells, labels[1:-1], widths[1:-1], info.videos, channels)


def split_rows(pairs_ref):
    cols = pairs_ref.shape[1] // 2
    cells = []
    for pair in range(pairs_ref.shape[0]):
        both = pairs_ref[pair].astype(F32)
        cells += [both[:cols], both[cols:]]
    return cells


def turned_queries(info, tile, pairs_ref, means, scales, shift_ref, weight_ref, bias_ref):
    pairs, double, channels = pairs_ref.shape
    cols = double // 2
    column = lax.broadcasted_iota(jnp.int32, (cols, 1), 0)
    labels, widths = info.window(tile * 2 * pairs, 2 * pairs)
    cells = []
    for r, values in enumerate(split_rows(pairs_ref)):
        mean = pick(means, labels[r], info.videos)
        scale = pick(scales, labels[r], info.videos)
        normed = (values - mean) * scale + shift_ref[...]
        cells.append(jnp.where(column < widths[r], normed, 0.0))
    cells = jnp.concatenate(cells, axis=0).astype(BF16)
    queries = (
        jnp.dot(cells, weight_ref[:, 0:channels], preferred_element_type=F32)
        + bias_ref[:, 0:channels]
    ).astype(BF16)
    factor = channels ** (-0.5) * math.log2(math.e)
    turned = lax.dot_general(
        queries, weight_ref[:, channels : 2 * channels], (((1,), (1,)), ((), ())),
        preferred_element_type=F32,
    )
    constant = jnp.sum(
        queries.astype(F32) * bias_ref[:, channels : 2 * channels], axis=1, keepdims=True
    )
    return (turned * factor).astype(BF16), constant * factor


def query_kernel(
    rows, info_ref, other_ref, stats_ref, gain_ref, shift_ref, weight_ref, bias_ref, queries_ref,
    constant_ref, means_ref, scales_ref,
):
    info = Info(info_ref, rows)
    means, scales = norm_tables(stats_ref, gain_ref)
    means_ref[...] = means
    scales_ref[...] = scales
    queries, constant = turned_queries(
        info, info.tile() ^ 1, other_ref, means, scales, shift_ref, weight_ref, bias_ref
    )
    queries_ref[...] = queries
    constant_ref[...] = jnp.broadcast_to(constant, constant_ref.shape)


def key_codes(info, masks, span, cols):
    row_count = span // cols
    position = lax.broadcasted_iota(jnp.int32, (1, len(masks) * span), 1)
    codes = jnp.full((1, len(masks) * span), -2.0, F32)
    for index, mask in enumerate(masks):
        near, widths = info.window((info.tile() ^ (2 * mask)) * row_count, row_count)
        for r in range(row_count):
            start = index * span + r * cols
            inside = (position >= start) & (position < start + widths[r])
            codes = jnp.where(inside, near[r].astype(F32), codes)
    return codes


def query_codes(info, tile, span, cols):
    row_count = span // cols
    labels, _ = info.window(tile * row_count, row_count)
    return jnp.concatenate(
        [jnp.zeros((cols, 1), F32) + label.astype(F32) for label in labels], axis=0
    )


def scores_of(queries, keys, codes, query_code):
    scores = lax.dot_general(
        queries, keys, (((1,), (1,)), ((), ())), preferred_element_type=F32
    )
    return jnp.where(codes == query_code, scores, MASKED)


def mean_and_level(peak, denominator, total):
    some = denominator > 0.0
    safe = jnp.where(some, denominator, 1.0)
    return total / safe, jnp.where(some, peak + jnp.log2(safe), LOWEST)


def attend_yours_kernel(rows, masks, first, last, info_ref, *rest):
    means_ref, scales_ref, shift_ref, queries_ref, constant_ref, *rest = rest
    block_refs, rest = rest[: len(masks)], rest[len(masks) :]
    if not first:
        old_peak_ref, old_sum_ref, old_total_ref, *rest = rest
    keys_ref, *out_refs = rest
    info = Info(info_ref, rows)
    span, channels = queries_ref.shape
    pairs, double, _ = block_refs[0].shape
    cols = double // 2
    row_count = 2 * pairs
    tile = info.tile()
    means, scales = means_ref[...], scales_ref[...]
    for index, (mask, block_ref) in enumerate(zip(masks, block_refs)):
        near, _ = info.window((tile ^ (2 * mask)) * row_count, row_count)
        for pair in range(pairs):
            both = block_ref[pair].astype(F32)
            halves = []
            for half in range(2):
                label = near[2 * pair + half]
                mean = pick(means, label, info.videos)
                scale = pick(scales, label, info.videos)
                values = both[half * cols : (half + 1) * cols]
                halves.append((values - mean) * scale + shift_ref[...])
            start = index * span + pair * double
            keys_ref[start : start + double, :] = jnp.concatenate(halves, axis=0).astype(BF16)
    constant = constant_ref[:, 0:1]
    scores = scores_of(
        queries_ref[...], keys_ref[...], key_codes(info, masks, span, cols),
        query_codes(info, tile ^ 1, span, cols),
    )
    peak = jnp.maximum(LOWEST, jnp.max(scores, axis=1, keepdims=True) + constant)
    if not first:
        largest = old_peak_ref[:, 0:1]
        peak = jnp.maximum(largest, peak)
    weights = jnp.exp2(scores - (peak - constant))
    denominator = jnp.sum(weights, axis=1, keepdims=True)
    total = jnp.dot(weights.astype(BF16), keys_ref[...], preferred_element_type=F32)
    if not first:
        factor = jnp.exp2(largest - peak)
        denominator = old_sum_ref[:, 0:1] * factor + denominator
        total = old_total_ref[...] * factor + total
    if not last:
        peak_ref, sum_ref, total_ref = out_refs
        peak_ref[...] = jnp.broadcast_to(peak, peak_ref.shape)
        sum_ref[...] = jnp.broadcast_to(denominator, sum_ref.shape)
        total_ref[...] = total
        return
    (sent_ref,) = out_refs
    mean, level = mean_and_level(peak, denominator, total)
    sent_ref[0:span, :] = mean.astype(BF16)
    slots = sent_ref.shape[0] - span
    slot = lax.broadcasted_iota(jnp.int32, (slots, 1), 0)
    packed = jnp.zeros((slots, LANES), F32)
    for r in range(row_count):
        left = level[r * cols : (r + 1) * cols]
        left = jnp.sum(jnp.where(diagonal(cols), left, 0.0), axis=0, keepdims=True)
        for part in range(3):
            rounded = left.astype(BF16).astype(F32)
            packed = jnp.where(slot == 3 * r + part, rounded, packed)
            left = left - rounded
    sent_ref[span:, 0:LANES] = packed.astype(BF16)
    sent_ref[span:, LANES:] = jnp.zeros((slots, channels - LANES), BF16)


def attend_mine_kernel(
    rows, groups, info_ref, own_ref, means_ref, scales_ref, shift_ref, weight_ref, bias_ref, *rest
):
    key_refs, (mean_ref, level_ref) = rest[: len(groups)], rest[len(groups) :]
    info = Info(info_ref, rows)
    span = mean_ref.shape[0]
    queries, constant = turned_queries(
        info, info.tile(), own_ref, means_ref[...], scales_ref[...], shift_ref, weight_ref,
        bias_ref,
    )
    cols = span // ROWS_OF_TILE
    query_code = query_codes(info, info.tile(), span, cols)
    peak = jnp.full((span, 1), LOWEST, F32)
    scores = []
    for masks, key_ref in zip(groups, key_refs):
        codes = key_codes(info, masks, span, cols)
        scores.append(scores_of(queries, key_ref[...], codes, query_code))
        peak = jnp.maximum(peak, jnp.max(scores[-1], axis=1, keepdims=True) + constant)
    denominator, total = 0.0, 0.0
    for part, key_ref in zip(scores, key_refs):
        weights = jnp.exp2(part - (peak - constant))
        denominator = denominator + jnp.sum(weights, axis=1, keepdims=True)
        total = total + jnp.dot(
            weights.astype(BF16), key_ref[...], preferred_element_type=F32
        )
    mean, level = mean_and_level(peak, denominator, total)
    mean_ref[...] = mean
    level_ref[...] = jnp.broadcast_to(level, level_ref.shape)


def diagonal(cols):
    return lax.broadcasted_iota(jnp.int32, (cols, LANES), 0) == lax.broadcasted_iota(
        jnp.int32, (cols, LANES), 1
    )


def finish_kernel(
    rows, info_ref, mean_ref, level_ref, received_ref, own_ref, triple_ref, triple_bias_ref,
    output_ref, output_bias_ref, out_ref, inner_ref, outer_ref,
):
    info = Info(info_ref, rows)
    row_count, cols, channels = out_ref.shape
    span = row_count * cols
    _, widths = info.window(info.tile() * row_count, row_count)
    received = received_ref[0:span, :].astype(F32)
    levels = received_ref[span:, 0:LANES].astype(F32)
    yours = []
    for r in range(row_count):
        level = levels[3 * r : 3 * r + 1] + levels[3 * r + 1 : 3 * r + 2]
        level = level + levels[3 * r + 2 : 3 * r + 3]
        yours.append(jnp.sum(jnp.where(diagonal(cols), level, 0.0), axis=1, keepdims=True))
    yours = jnp.concatenate(yours, axis=0)
    mine = level_ref[:, 0:1]
    peak = jnp.maximum(mine, yours)
    weight, other_weight = jnp.exp2(mine - peak), jnp.exp2(yours - peak)
    share = weight / (weight + other_weight)
    mean_cell = (mean_ref[...] * share + received * (1.0 - share)).astype(BF16)
    mixed = (
        jnp.dot(mean_cell, triple_ref[:, 2 * channels :], preferred_element_type=F32)
        + triple_bias_ref[:, 2 * channels :]
    ).astype(BF16)
    attended = jnp.dot(mixed, output_ref[...], preferred_element_type=F32) + output_bias_ref[...]
    column = lax.broadcasted_iota(jnp.int32, (cols, 1), 0)
    for r, before in enumerate(split_rows(own_ref)):
        value = before + attended[r * cols : (r + 1) * cols]
        value = jnp.where(column < widths[r], value, 0.0)
        out_ref[r] = value.astype(BF16)
        if r == 0:
            top = value
    odd = lax.rem(info.tile(), 2) == 1
    inner_ref[0] = jnp.where(odd, top, value).astype(BF16)
    outer_ref[0] = jnp.where(odd, value, top).astype(BF16)


def fold_kernel(weight_ref, out_ref):
    channels = weight_ref.shape[-1]
    wide = [[weight_ref[a, b].astype(F32) for b in range(3)] for a in range(3)]

    def both(upper, lower):
        return [x + y for x, y in zip(upper, lower)]

    phases = [[wide[0], both(wide[1], wide[2])], [both(wide[0], wide[1]), wide[2]]]
    for down in range(2):
        for tap in range(2):
            left, middle, right = phases[down][tap]
            out_ref[down, tap, 0, :, 0:channels] = left.astype(BF16)
            out_ref[down, tap, 0, :, channels:] = (middle + right).astype(BF16)
            out_ref[down, tap, 1, :, 0:channels] = (left + middle).astype(BF16)
            out_ref[down, tap, 1, :, channels:] = right.astype(BF16)


def spread_columns(wide_ref, value, row, right):
    cols, channels = value.shape
    for part in range(wide_ref.shape[0]):
        lo, hi = part * LANES, min((part + 1) * LANES, channels)
        piece = value[:, lo:hi]
        if hi - lo < LANES:
            piece = jnp.concatenate([piece, jnp.zeros((cols, LANES - hi + lo), F32)], axis=1)
        wide_ref[part, row, pl.ds(right, cols, 2), :] = piece


def write_turned(out_ref, row, part, value, width):
    channels, cols = out_ref.shape[1:]
    lo, hi = part * LANES, min((part + 1) * LANES, channels)
    turned = value.T[0 : hi - lo, 0:cols]
    column = lax.broadcasted_iota(jnp.int32, (1, cols), 1)
    out_ref[row, lo:hi, :] = jnp.where(column < width, turned, 0.0).astype(BF16)


def phase_product(columns, weight):
    return lax.dot_general(
        columns, weight, (((1,), (1,)), ((), ())), preferred_element_type=F32
    )


def upsample_kernel(
    rows, info_ref, own_ref, weight_ref, bias_ref, out_ref, open_ref, columns_ref, wide_ref
):
    info = Info(info_ref, rows)
    row_count, cols, channels = own_ref.shape
    padded = columns_ref.shape[0] // row_count
    parts_out = wide_ref.shape[0]
    labels, widths = info.window(info.tile() * row_count, row_count)
    build_columns(
        columns_ref, [functools.partial(own_ref.__getitem__, r) for r in range(row_count)]
    )
    inner_rows = (row_count - 1) * padded
    for down in range(2):
        for right in range(2):
            lanes = slice(right * channels, (right + 2) * channels)
            same = phase_product(columns_ref[:, lanes], weight_ref[down, 1 - down, right])
            start = down * padded
            rim = phase_product(
                columns_ref[start : start + inner_rows, lanes], weight_ref[down, down, right]
            )
            for r in range(row_count):
                value = same[r * padded : r * padded + cols]
                near = r - 1 + 2 * down
                if 0 <= near < row_count:
                    lo = (near - down) * padded
                    value = value + jnp.where(
                        labels[near] == labels[r], rim[lo : lo + cols], 0.0
                    )
                spread_columns(wide_ref, value, 2 * r + down, right)
    for part in range(parts_out):
        open_ref[part, 0] = wide_ref[part, 0]
        open_ref[part, 1] = wide_ref[part, 2 * row_count - 1]
    for r in range(1, 2 * row_count - 1):
        for part in range(parts_out):
            value = wide_ref[part, r] + bias_ref[:, part * LANES : (part + 1) * LANES]
            write_turned(out_ref, r - 1, part, value, 2 * widths[r // 2])


def close_kernel(
    rows, info_ref, outer_ref, inner_ref, middle_ref, open_ref, weight_ref, bias_ref, out_ref,
    columns_ref, wide_ref,
):
    info = Info(info_ref, rows)
    wide_rows, _, wide_cols = out_ref.shape
    row_count, cols = wide_rows // 2, wide_cols // 2
    channels = outer_ref.shape[-1]
    padded = columns_ref.shape[0] // 2
    labels, widths = info.window(info.tile() * row_count - 1, row_count + 2)
    above, below = rims(info, outer_ref, inner_ref)
    build_columns(columns_ref, [lambda: above, lambda: below])
    for down in range(2):
        for right in range(2):
            lanes = slice(right * channels, (right + 2) * channels)
            rim = phase_product(
                columns_ref[down * padded : (down + 1) * padded, lanes],
                weight_ref[down, down, right],
            )
            spread_columns(wide_ref, rim[:cols], down, right)
    out_ref[1 : wide_rows - 1] = middle_ref[...]
    for down in range(2):
        rim_row, own_row = (row_count + 1, row_count) if down else (0, 1)
        for part in range(wide_ref.shape[0]):
            rim = jnp.where(labels[rim_row] == labels[own_row], wide_ref[part, down], 0.0)
            value = open_ref[part, down] + rim + bias_ref[:, part * LANES : (part + 1) * LANES]
            write_turned(
                out_ref, down * (wide_rows - 1), part, value, 2 * widths[own_row]
            )


def merge_stats(mine, other):
    count = mine[0] + other[0]
    safe = jnp.maximum(count, 1.0)
    off = other[1] - mine[1]
    mean = mine[1] + off * (other[0] / safe)
    spread = mine[2] + other[2] + off * off * (mine[0] * other[0] / safe)
    return jnp.stack([count, mean, spread])


def exchange(array, tiles, mask, among=None):
    moves = [(i, i ^ mask) for i in range(tiles) if among is None or among(i)]
    return lax.ppermute(array, "tile", moves)


def merge_round(stats, tiles, masks, tied=(), after=None, among=None):
    limits = among or {}
    parts = [stats] + [exchange(stats, tiles, mask, limits.get(mask)) for mask in masks]
    free = ()
    if tied:
        *parts[2:], free = lax.optimization_barrier((*parts[2:], after))
        parts[1], *tied = lax.optimization_barrier((parts[1], *tied))
    while len(parts) > 1:
        parts = [merge_stats(*parts[i : i + 2]) for i in range(0, len(parts), 2)]
    return (parts[0], *tied, free) if tied else parts[0]


def merge_masks(tiles):
    bits = [1 << i for i in range(tiles.bit_length() - 1)]
    pairs = [bits[i : i + 2] for i in range(0, len(bits), 2)]
    return [[p[0], p[1], p[0] ^ p[1]] if len(p) == 2 else p for p in pairs]


def shards(
    tiles,
    frames,
    latents,
    row_video,
    video_cols,
    first_gain,
    first_shift,
    conv_weight,
    conv_bias,
    second_gain,
    second_shift,
    triple_weight,
    triple_bias,
    output_weight,
    output_bias,
    upsample_weight,
    upsample_bias,
):
    row_count, frame_count, cols, channels = latents.shape
    assert frame_count == 1 and row_count == ROWS_OF_TILE and tiles % 4 == 0
    out_channels = upsample_weight.shape[-1]
    rows = row_count * tiles
    cells = row_count * cols
    padded = -(-(cols + 1) // 16) * 16
    near_rows = row_count + 2
    source = latents.reshape(row_count, cols, channels)
    tile = lax.axis_index("tile").astype(jnp.int32)
    info = jnp.concatenate([jnp.reshape(tile, (1,)), row_video, video_cols])

    def row(vector):
        return vector.reshape(1, -1)

    def shape(*dims, dtype=BF16):
        return jax.ShapeDtypeStruct(dims, dtype)

    def call(kernel, operands, out_shape, scratch=(), **kwargs):
        many = isinstance(out_shape, tuple)
        return pl.pallas_call(
            kernel,
            out_shape=out_shape,
            in_specs=[SMEM_SPEC] + [VMEM_SPEC] * len(operands),
            out_specs=(VMEM_SPEC,) * len(out_shape) if many else VMEM_SPEC,
            scratch_shapes=list(scratch),
            compiler_params=params(),
            **kwargs,
        )(info, *operands)

    outer_moves = [(i, i - 1 if i % 2 == 0 else i + 1) for i in range(tiles)]
    outer_moves = [(i, j) for i, j in outer_moves if 0 <= j < tiles]
    odd = tile % 2 == 1
    stats_shape = shape(3, SLOTS, LANES, dtype=F32)
    stats = call(
        functools.partial(stats_kernel, rows), [source], stats_shape,
        cost_estimate=cost(1.5), name="first_stats",
    )
    outer = lax.ppermute(
        jnp.where(odd, source[row_count - 1 :], source[:1]), "tile", outer_moves
    )
    inner = exchange(jnp.where(odd, source[:1], source[row_count - 1 :]), tiles, 1)
    stats, outer, inner = lax.optimization_barrier((stats, outer, inner))
    taps = min(3, frames)
    held = [
        pl.pallas_call(
            functools.partial(hold_kernel, backs),
            out_shape=shape(3 * len(backs) * channels, 3 * channels),
            in_specs=[HBM_SPEC],
            out_specs=VMEM_SPEC,
            scratch_shapes=[pltpu.SemaphoreType.DMA((len(backs), 3, 3))],
            compiler_params=pltpu.CompilerParams(vmem_limit_bytes=HOLD_VMEM_BYTES),
            cost_estimate=cost(1.5 * len(backs)),
            name="hold",
        )(conv_weight)
        for backs in ((0,), tuple(range(1, taps)))
        if backs
    ]
    rounds = merge_masks(tiles)
    layered = tiles == 16 and video_cols.shape[0] == 2

    def middle(t):
        return t // 4 in (1, 2)

    among = {12: middle} if layered else {}
    for index, masks in enumerate(reversed(rounds)):
        stats = merge_round(stats, tiles, masks, among=among)
        if index < len(held):
            stats, held[index] = lax.optimization_barrier((stats, held[index]))
    hidden, source = call(
        functools.partial(hidden_kernel, rows),
        [outer, inner, source, stats, row(first_gain), row(first_shift)],
        (shape(near_rows, padded, channels), shape(row_count, cols, channels)),
        cost_estimate=cost(1.3),
        name="hidden",
    )

    earlier = [
        lax.ppermute(hidden, "frame", [(i, i + by) for i in range(frames - by)])
        for by in range(1, taps)
    ]
    pairs = row_count // 2
    pair_shape = shape(pairs, 2 * cols, channels)
    product = call(
        functools.partial(own_conv_kernel, rows),
        [hidden, held[0]],
        shape(row_count * padded, 3 * channels, dtype=F32),
        scratch=[pltpu.VMEM((row_count * padded, 3 * channels), BF16)],
        cost_estimate=cost(2.2),
        name="own_conv",
    )
    scratch = [pltpu.VMEM((row_count * padded, 3 * (taps - 1) * channels), BF16)]
    own, stats = call(
        functools.partial(conv_kernel, rows, taps),
        earlier + [product, source, row(conv_bias)] + held[1:],
        (pair_shape, stats_shape),
        scratch=scratch if taps > 1 else [],
        cost_estimate=cost(1.5 + 2.0 * (taps - 1)),
        name="conv",
    )

    blocks = {0: own}
    neighbour = [(i, i ^ 1) for i in range(tiles)]
    if layered:
        stats = merge_round(stats, tiles, rounds[1], among=among)
        blocks[2] = exchange(own, tiles, 4)
        blocks[6] = exchange(own, tiles, 12, middle)
        stats, blocks[2], blocks[6], own_xy = merge_round(
            stats, tiles, rounds[0], (blocks[2], blocks[6]), own
        )
        inward = exchange(blocks[2], tiles, 12, middle)
        outward = exchange(blocks[6], tiles, 4, middle)
        other = exchange(own_xy, tiles, 1)
        blocks[1] = exchange(own_xy, tiles, 2)
        blocks[4] = jnp.where((tile // 4 == 1) | (tile // 4 == 2), inward, outward)
        passed, blocks[4] = lax.optimization_barrier((blocks[1], blocks[4]))
        blocks[5] = exchange(blocks[4], tiles, 2)
        blocks[3] = exchange(passed, tiles, 4)
        blocks[7] = exchange(passed, tiles, 12, middle)
        groups = [[0, 1, 2, 6, 4], [7, 3, 5]]
    else:
        for masks in rounds:
            stats = merge_round(stats, tiles, masks)
        other = exchange(own, tiles, 1)
        for mask in range(1, tiles // 2):
            blocks[mask] = exchange(own, tiles, 2 * mask)
        groups = [list(range(i, i + 4)) for i in range(0, tiles // 2, 4)]
    gain, shift = row(second_gain), row(second_shift)
    table_shape = shape(SLOTS, channels, dtype=F32)
    queries, constant, means, scales = call(
        functools.partial(query_kernel, rows),
        [other, stats, gain, shift, triple_weight, row(triple_bias)],
        (shape(cells, channels), shape(cells, LANES, dtype=F32), table_shape, table_shape),
        cost_estimate=cost(1.5),
        name="queries",
    )
    level_shape = shape(cells, LANES, dtype=F32)
    total_shape = shape(cells, channels, dtype=F32)
    state, keys = (), []
    for index, masks in enumerate(groups):
        last = index == len(groups) - 1
        outs = (shape(len(masks) * cells, channels),)
        outs += (shape(cells + 16, channels),) if last else (level_shape, level_shape, total_shape)
        normed, *state = call(
            functools.partial(attend_yours_kernel, rows, tuple(masks), index == 0, last),
            [means, scales, shift, queries, constant] + [blocks[m] for m in masks] + list(state),
            outs,
            cost_estimate=cost(0.9 * len(masks)),
            name="attend_yours",
        )
        keys.append(normed)
    (sent,) = state
    received = lax.ppermute(sent, "tile", neighbour)
    sent, own_late, upsample_weight = lax.optimization_barrier((sent, own, upsample_weight))
    mean, level = call(
        functools.partial(attend_mine_kernel, rows, tuple(tuple(masks) for masks in groups)),
        [own_late, means, scales, shift, triple_weight, row(triple_bias)] + keys,
        (total_shape, level_shape),
        cost_estimate=cost(6.0),
        name="attend_mine",
    )
    folded = pl.pallas_call(
        fold_kernel,
        out_shape=shape(2, 2, 2, out_channels, 2 * channels),
        in_specs=[VMEM_SPEC],
        out_specs=VMEM_SPEC,
        compiler_params=params(),
        cost_estimate=cost(0.5),
        name="fold",
    )(jnp.swapaxes(upsample_weight, 2, 3))

    rim_shape = shape(1, cols, channels)
    attended, inner, outer = call(
        functools.partial(finish_kernel, rows),
        [
            mean, level, received, own, triple_weight, row(triple_bias), output_weight,
            row(output_bias),
        ],
        (shape(row_count, cols, channels), rim_shape, rim_shape),
        cost_estimate=cost(1.4),
        name="finish",
    )
    outer = lax.ppermute(outer, "tile", outer_moves)
    inner = exchange(inner, tiles, 1)
    parts_out = -(-out_channels // LANES)
    wide_cols = -(-2 * cols // LANES) * LANES
    wide_bias = jnp.pad(row(upsample_bias), ((0, 0), (0, -out_channels % LANES)))
    middle, open_rows = call(
        functools.partial(upsample_kernel, rows),
        [attended, folded, wide_bias],
        (
            shape(2 * row_count - 2, out_channels, 2 * cols),
            shape(parts_out, 2, wide_cols, LANES, dtype=F32),
        ),
        scratch=[
            pltpu.VMEM((row_count * padded, 3 * channels), BF16),
            pltpu.VMEM((parts_out, 2 * row_count, wide_cols, LANES), F32),
        ],
        cost_estimate=cost(2.0),
        name="upsample",
    )
    decoded = call(
        functools.partial(close_kernel, rows),
        [outer, inner, middle, open_rows, folded, wide_bias],
        shape(2 * row_count, out_channels, 2 * cols),
        scratch=[
            pltpu.VMEM((2 * padded, 3 * channels), BF16),
            pltpu.VMEM((parts_out, 2, wide_cols, LANES), F32),
        ],
        cost_estimate=cost(1.0),
        name="close",
    )
    return jnp.swapaxes(decoded, 1, 2).reshape(2 * row_count, 1, 2 * cols, out_channels)


def solution(mesh):
    sizes = dict(mesh.shape)
    in_specs = (P("tile", "frame", None, None),) + (P(),) * 14
    out_specs = P("tile", "frame", None, None)
    body = functools.partial(shards, sizes["tile"], sizes["frame"])
    return jax.shard_map(body, mesh=mesh, in_specs=in_specs, out_specs=out_specs, check_vma=False)
```

```python
import functools
import math

import jax
import jax.numpy as jnp
from jax import lax
from jax.experimental import pallas as pl
from jax.experimental.pallas import tpu as pltpu
from jax.sharding import PartitionSpec as P

GROUPS = 32
EPSILON = 1e-05
MASKED = -1e30
LOWEST = -5e29
SLOTS = 8
ROWS_OF_TILE = 4
LANES = 128
VMEM_BYTES = 24 * 1024 * 1024
HOLD_VMEM_BYTES = 46 * 1024 * 1024
F32 = jnp.float32
BF16 = jnp.bfloat16

SMEM_SPEC = pl.BlockSpec(memory_space=pltpu.SMEM)
VMEM_SPEC = pl.BlockSpec(memory_space=pltpu.VMEM)
HBM_SPEC = pl.BlockSpec(memory_space=pltpu.HBM)


def cost(microseconds):
    return pl.CostEstimate(
        flops=int(microseconds * 1.1e9), bytes_accessed=0, transcendentals=0
    )


def params():
    return pltpu.CompilerParams(vmem_limit_bytes=VMEM_BYTES)


def member_matrix(channels):
    per_group = channels // GROUPS
    group = lax.broadcasted_iota(jnp.int32, (LANES, channels), 0) * per_group
    channel = lax.broadcasted_iota(jnp.int32, (LANES, channels), 1)
    return jnp.where((channel >= group) & (channel < group + per_group), 1.0, 0.0).astype(BF16)


def thirds(values):
    parts = []
    for _ in range(3):
        parts.append(values.astype(BF16).astype(F32))
        values = values - parts[-1]
    return jnp.concatenate(parts, axis=0).astype(BF16)


def added(products):
    rows = products.shape[0] // 3
    return (products[2 * rows :] + products[rows : 2 * rows]) + products[:rows]


def to_groups(values, member):
    return added(
        lax.dot_general(
            thirds(values), member, (((1,), (1,)), ((), ())), preferred_element_type=F32
        )
    )


def to_channels(values, member):
    return added(jnp.dot(thirds(values), member, preferred_element_type=F32))


class Info:
    def __init__(self, ref, rows):
        self.ref, self.rows = ref, rows
        self.videos = ref.shape[0] - 1 - rows

    def tile(self):
        return self.ref[0]

    def label(self, row):
        inside = (row >= 0) & (row < self.rows)
        return jnp.where(inside, self.ref[1 + jnp.clip(row, 0, self.rows - 1)], -1)

    def width(self, label):
        return jnp.where(label >= 0, self.ref[1 + self.rows + jnp.maximum(label, 0)], 0)

    def window(self, first, count):
        labels = [self.label(first + r) for r in range(count)]
        return labels, [self.width(label) for label in labels]


def pick(table, label, videos):
    chosen = table[0:1]
    for video in range(1, videos):
        chosen = jnp.where(label == video, table[video : video + 1], chosen)
    return chosen


def norm_tables(stats_ref, gain_ref):
    member = member_matrix(gain_ref.shape[1])
    counts = jnp.maximum(stats_ref[0], 1.0)
    scale = lax.rsqrt(stats_ref[2] / counts + EPSILON)
    return to_channels(stats_ref[1], member), to_channels(scale, member) * gain_ref[...]


def write_stats(out_ref, rows, labels, widths, videos, channels):
    member = member_matrix(channels)
    per_group = channels // GROUPS
    cols = rows[0].shape[0]
    slot = lax.broadcasted_iota(jnp.int32, (SLOTS, 1), 0)
    column = lax.broadcasted_iota(jnp.int32, (cols, 1), 0)
    sums = jnp.zeros((SLOTS, channels), F32)
    counts = jnp.zeros((SLOTS, 1), F32)
    for index, row in enumerate(rows):
        sums = jnp.where(slot == index, jnp.sum(row, axis=0, keepdims=True), sums)
        counts = jnp.where(slot == index, (widths[index] * per_group).astype(F32), counts)
    means = to_groups(sums, member) / jnp.maximum(counts, 1.0)
    means_wide = to_channels(means, member)
    squares = jnp.zeros((SLOTS, channels), F32)
    for index, row in enumerate(rows):
        centered = jnp.where(column < widths[index], row - means_wide[index : index + 1], 0.0)
        squares = jnp.where(
            slot == index, jnp.sum(centered * centered, axis=0, keepdims=True), squares
        )
    spreads = to_groups(squares, member)
    out_ref[...] = jnp.zeros(out_ref.shape, F32)
    for video in range(videos):
        total = jnp.zeros((1, LANES), F32)
        count = jnp.zeros((1, LANES), F32)
        for index in range(len(rows)):
            mine = labels[index] == video
            row_count = counts[index : index + 1]
            total = total + jnp.where(mine, means[index : index + 1] * row_count, 0.0)
            count = count + jnp.where(mine, row_count, 0.0)
        mean = total / jnp.maximum(count, 1.0)
        spread = jnp.zeros((1, LANES), F32)
        for index in range(len(rows)):
            off = means[index : index + 1] - mean
            part = spreads[index : index + 1] + counts[index : index + 1] * off * off
            spread = spread + jnp.where(labels[index] == video, part, 0.0)
        out_ref[0, video : video + 1, :] = count
        out_ref[1, video : video + 1, :] = mean
        out_ref[2, video : video + 1, :] = spread


def build_columns(columns_ref, row_refs):
    padded = columns_ref.shape[0] // len(row_refs)
    for index, row in enumerate(row_refs):
        cells = row().astype(F32)
        count, channels = cells.shape
        cells = jnp.concatenate([cells, jnp.zeros((padded - count, channels), F32)], axis=0)
        start = index * padded
        columns_ref[start : start + padded, 0:channels] = pltpu.roll(cells, 1, 0).astype(BF16)
        columns_ref[start : start + padded, channels : 2 * channels] = cells.astype(BF16)
        columns_ref[start : start + padded, 2 * channels : 3 * channels] = pltpu.roll(
            cells, padded - 1, 0
        ).astype(BF16)


def stats_kernel(rows, info_ref, latents_ref, out_ref):
    info = Info(info_ref, rows)
    row_count, cols, channels = latents_ref.shape
    labels, widths = info.window(info.tile() * row_count, row_count)
    column = lax.broadcasted_iota(jnp.int32, (cols, 1), 0)
    cells = [
        jnp.where(column < widths[r], latents_ref[r].astype(F32), 0.0) for r in range(row_count)
    ]
    write_stats(out_ref, cells, labels, widths, info.videos, channels)


def rims(info, outer_ref, inner_ref):
    odd = lax.rem(info.tile(), 2) == 1
    inner, outer = inner_ref[0].astype(F32), outer_ref[0].astype(F32)
    return jnp.where(odd, inner, outer), jnp.where(odd, outer, inner)


def hidden_kernel(
    rows, info_ref, outer_ref, inner_ref, latents_ref, stats_ref, gain_ref, shift_ref, out_ref,
    source_ref,
):
    info = Info(info_ref, rows)
    row_count, cols, _ = latents_ref.shape
    labels, widths = info.window(info.tile() * row_count - 1, row_count + 2)
    means, scales = norm_tables(stats_ref, gain_ref)
    column = lax.broadcasted_iota(jnp.int32, (cols, 1), 0)
    above, below = rims(info, outer_ref, inner_ref)
    sources = [above] + [latents_ref[r].astype(F32) for r in range(row_count)] + [below]
    for r, source in enumerate(sources):
        mean = pick(means, labels[r], info.videos)
        scale = pick(scales, labels[r], info.videos)
        normed = (source - mean) * scale + shift_ref[...]
        active = normed / (1.0 + jnp.exp(-normed))
        active = jnp.where(column < widths[r], active, 0.0)
        rest = jnp.zeros((out_ref.shape[1] - cols, active.shape[1]), F32)
        out_ref[r] = jnp.concatenate([active, rest], axis=0).astype(BF16)
    source_ref[...] = latents_ref[...]


def hold_kernel(backs, weight_ref, held_ref, sems):
    channels = weight_ref.shape[-1]
    copies = [
        pltpu.make_async_copy(
            weight_ref.at[2 - back, tap, side],
            held_ref.at[
                pl.ds((3 * index + tap) * channels, channels), pl.ds(side * channels, channels)
            ],
            sems.at[index, tap, side],
        )
        for index, back in enumerate(backs)
        for tap in range(3)
        for side in range(3)
    ]
    for copy in copies:
        copy.start()
    for copy in copies:
        copy.wait()


def row_taps(info, hidden_refs, inputs_ref):
    near_rows, padded, channels = hidden_refs[0].shape
    row_count = near_rows - 2
    labels, _ = info.window(info.tile() * row_count - 1, near_rows)
    for back, hidden_ref in enumerate(hidden_refs):
        for tap in range(3):
            lanes = slice((3 * back + tap) * channels, (3 * back + tap + 1) * channels)
            for r in range(row_count):
                block = hidden_ref[r + tap]
                if tap != 1:
                    same = labels[r + tap] == labels[r + 1]
                    block = jnp.where(same, block, jnp.zeros_like(block))
                inputs_ref[r * padded : (r + 1) * padded, lanes] = block


def own_conv_kernel(rows, info_ref, hidden_ref, held_ref, product_ref, inputs_ref):
    row_taps(Info(info_ref, rows), [hidden_ref], inputs_ref)
    product_ref[...] = jnp.dot(inputs_ref[...], held_ref[...], preferred_element_type=F32)


def conv_kernel(rows, taps, info_ref, *rest):
    hidden_refs, rest = rest[: taps - 1], rest[taps - 1 :]
    product_ref, latents_ref, bias_ref, *rest = rest
    held_refs, (own_ref, stats_ref, *inputs_refs) = rest[: taps > 1], rest[taps > 1 :]
    row_count, cols, channels = latents_ref.shape
    info = Info(info_ref, rows)
    padded = product_ref.shape[0] // row_count
    labels, widths = info.window(info.tile() * row_count - 1, row_count + 2)
    product = product_ref[...]
    if hidden_refs:
        (inputs_ref,) = inputs_refs
        row_taps(info, hidden_refs, inputs_ref)
        product = product + jnp.dot(
            inputs_ref[...], held_refs[0][...], preferred_element_type=F32
        )
    column = lax.broadcasted_iota(jnp.int32, (cols, 1), 0)
    cells = []
    for r in range(row_count):
        lines = slice(r * padded, (r + 1) * padded)
        branch = pltpu.roll(product[lines, 0:channels], 1, 0)
        branch = branch + product[lines, channels : 2 * channels]
        branch = branch + pltpu.roll(product[lines, 2 * channels :], padded - 1, 0)
        value = latents_ref[r].astype(F32) + branch[:cols] + bias_ref[...]
        value = jnp.where(column < widths[r + 1], value, 0.0).astype(BF16)
        cells.append(value.astype(F32))
    for pair in range(row_count // 2):
        own_ref[pair] = jnp.concatenate(cells[2 * pair : 2 * pair + 2], axis=0).astype(BF16)
    write_stats(stats_ref, cells, labels[1:-1], widths[1:-1], info.videos, channels)


def split_rows(pairs_ref):
    cols = pairs_ref.shape[1] // 2
    cells = []
    for pair in range(pairs_ref.shape[0]):
        both = pairs_ref[pair].astype(F32)
        cells += [both[:cols], both[cols:]]
    return cells


def turned_queries(info, tile, pairs_ref, means, scales, shift_ref, weight_ref, bias_ref):
    pairs, double, channels = pairs_ref.shape
    cols = double // 2
    column = lax.broadcasted_iota(jnp.int32, (cols, 1), 0)
    labels, widths = info.window(tile * 2 * pairs, 2 * pairs)
    cells = []
    for r, values in enumerate(split_rows(pairs_ref)):
        mean = pick(means, labels[r], info.videos)
        scale = pick(scales, labels[r], info.videos)
        normed = (values - mean) * scale + shift_ref[...]
        cells.append(jnp.where(column < widths[r], normed, 0.0))
    cells = jnp.concatenate(cells, axis=0).astype(BF16)
    queries = (
        jnp.dot(cells, weight_ref[:, 0:channels], preferred_element_type=F32)
        + bias_ref[:, 0:channels]
    ).astype(BF16)
    factor = channels ** (-0.5) * math.log2(math.e)
    turned = lax.dot_general(
        queries, weight_ref[:, channels : 2 * channels], (((1,), (1,)), ((), ())),
        preferred_element_type=F32,
    )
    constant = jnp.sum(
        queries.astype(F32) * bias_ref[:, channels : 2 * channels], axis=1, keepdims=True
    )
    return (turned * factor).astype(BF16), constant * factor


def query_kernel(
    rows, info_ref, other_ref, stats_ref, gain_ref, shift_ref, weight_ref, bias_ref, queries_ref,
    constant_ref, means_ref, scales_ref,
):
    info = Info(info_ref, rows)
    means, scales = norm_tables(stats_ref, gain_ref)
    means_ref[...] = means
    scales_ref[...] = scales
    queries, constant = turned_queries(
        info, info.tile() ^ 1, other_ref, means, scales, shift_ref, weight_ref, bias_ref
    )
    queries_ref[...] = queries
    constant_ref[...] = jnp.broadcast_to(constant, constant_ref.shape)


def key_codes(info, masks, span, cols):
    row_count = span // cols
    position = lax.broadcasted_iota(jnp.int32, (1, len(masks) * span), 1)
    codes = jnp.full((1, len(masks) * span), -2.0, F32)
    for index, mask in enumerate(masks):
        near, widths = info.window((info.tile() ^ (2 * mask)) * row_count, row_count)
        for r in range(row_count):
            start = index * span + r * cols
            inside = (position >= start) & (position < start + widths[r])
            codes = jnp.where(inside, near[r].astype(F32), codes)
    return codes


def query_codes(info, tile, span, cols):
    row_count = span // cols
    labels, _ = info.window(tile * row_count, row_count)
    return jnp.concatenate(
        [jnp.zeros((cols, 1), F32) + label.astype(F32) for label in labels], axis=0
    )


def scores_of(queries, keys, codes, query_code):
    scores = lax.dot_general(
        queries, keys, (((1,), (1,)), ((), ())), preferred_element_type=F32
    )
    return jnp.where(codes == query_code, scores, MASKED)


def mean_and_level(peak, denominator, total):
    some = denominator > 0.0
    safe = jnp.where(some, denominator, 1.0)
    return total / safe, jnp.where(some, peak + jnp.log2(safe), LOWEST)


def attend_yours_kernel(rows, masks, first, last, info_ref, *rest):
    means_ref, scales_ref, shift_ref, queries_ref, constant_ref, *rest = rest
    block_refs, rest = rest[: len(masks)], rest[len(masks) :]
    if not first:
        old_peak_ref, old_sum_ref, old_total_ref, *rest = rest
    keys_ref, *out_refs = rest
    info = Info(info_ref, rows)
    span, channels = queries_ref.shape
    pairs, double, _ = block_refs[0].shape
    cols = double // 2
    row_count = 2 * pairs
    tile = info.tile()
    means, scales = means_ref[...], scales_ref[...]
    for index, (mask, block_ref) in enumerate(zip(masks, block_refs)):
        near, _ = info.window((tile ^ (2 * mask)) * row_count, row_count)
        for pair in range(pairs):
            both = block_ref[pair].astype(F32)
            halves = []
            for half in range(2):
                label = near[2 * pair + half]
                mean = pick(means, label, info.videos)
                scale = pick(scales, label, info.videos)
                values = both[half * cols : (half + 1) * cols]
                halves.append((values - mean) * scale + shift_ref[...])
            start = index * span + pair * double
            keys_ref[start : start + double, :] = jnp.concatenate(halves, axis=0).astype(BF16)
    constant = constant_ref[:, 0:1]
    scores = scores_of(
        queries_ref[...], keys_ref[...], key_codes(info, masks, span, cols),
        query_codes(info, tile ^ 1, span, cols),
    )
    peak = jnp.maximum(LOWEST, jnp.max(scores, axis=1, keepdims=True) + constant)
    if not first:
        largest = old_peak_ref[:, 0:1]
        peak = jnp.maximum(largest, peak)
    weights = jnp.exp2(scores - (peak - constant))
    denominator = jnp.sum(weights, axis=1, keepdims=True)
    total = jnp.dot(weights.astype(BF16), keys_ref[...], preferred_element_type=F32)
    if not first:
        factor = jnp.exp2(largest - peak)
        denominator = old_sum_ref[:, 0:1] * factor + denominator
        total = old_total_ref[...] * factor + total
    if not last:
        peak_ref, sum_ref, total_ref = out_refs
        peak_ref[...] = jnp.broadcast_to(peak, peak_ref.shape)
        sum_ref[...] = jnp.broadcast_to(denominator, sum_ref.shape)
        total_ref[...] = total
        return
    (sent_ref,) = out_refs
    mean, level = mean_and_level(peak, denominator, total)
    sent_ref[0:span, :] = mean.astype(BF16)
    slots = sent_ref.shape[0] - span
    slot = lax.broadcasted_iota(jnp.int32, (slots, 1), 0)
    packed = jnp.zeros((slots, LANES), F32)
    for r in range(row_count):
        left = level[r * cols : (r + 1) * cols]
        left = jnp.sum(jnp.where(diagonal(cols), left, 0.0), axis=0, keepdims=True)
        for part in range(3):
            rounded = left.astype(BF16).astype(F32)
            packed = jnp.where(slot == 3 * r + part, rounded, packed)
            left = left - rounded
    sent_ref[span:, 0:LANES] = packed.astype(BF16)
    sent_ref[span:, LANES:] = jnp.zeros((slots, channels - LANES), BF16)


def attend_mine_kernel(
    rows, groups, info_ref, own_ref, means_ref, scales_ref, shift_ref, weight_ref, bias_ref, *rest
):
    key_refs, (mean_ref, level_ref) = rest[: len(groups)], rest[len(groups) :]
    info = Info(info_ref, rows)
    span = mean_ref.shape[0]
    queries, constant = turned_queries(
        info, info.tile(), own_ref, means_ref[...], scales_ref[...], shift_ref, weight_ref,
        bias_ref,
    )
    cols = span // ROWS_OF_TILE
    query_code = query_codes(info, info.tile(), span, cols)
    peak = jnp.full((span, 1), LOWEST, F32)
    scores = []
    for masks, key_ref in zip(groups, key_refs):
        codes = key_codes(info, masks, span, cols)
        scores.append(scores_of(queries, key_ref[...], codes, query_code))
        peak = jnp.maximum(peak, jnp.max(scores[-1], axis=1, keepdims=True) + constant)
    denominator, total = 0.0, 0.0
    for part, key_ref in zip(scores, key_refs):
        weights = jnp.exp2(part - (peak - constant))
        denominator = denominator + jnp.sum(weights, axis=1, keepdims=True)
        total = total + jnp.dot(
            weights.astype(BF16), key_ref[...], preferred_element_type=F32
        )
    mean, level = mean_and_level(peak, denominator, total)
    mean_ref[...] = mean
    level_ref[...] = jnp.broadcast_to(level, level_ref.shape)


def diagonal(cols):
    return lax.broadcasted_iota(jnp.int32, (cols, LANES), 0) == lax.broadcasted_iota(
        jnp.int32, (cols, LANES), 1
    )


def finish_kernel(
    rows, info_ref, mean_ref, level_ref, received_ref, own_ref, triple_ref, triple_bias_ref,
    output_ref, output_bias_ref, out_ref, inner_ref, outer_ref,
):
    info = Info(info_ref, rows)
    row_count, cols, channels = out_ref.shape
    span = row_count * cols
    _, widths = info.window(info.tile() * row_count, row_count)
    received = received_ref[0:span, :].astype(F32)
    levels = received_ref[span:, 0:LANES].astype(F32)
    yours = []
    for r in range(row_count):
        level = levels[3 * r : 3 * r + 1] + levels[3 * r + 1 : 3 * r + 2]
        level = level + levels[3 * r + 2 : 3 * r + 3]
        yours.append(jnp.sum(jnp.where(diagonal(cols), level, 0.0), axis=1, keepdims=True))
    yours = jnp.concatenate(yours, axis=0)
    mine = level_ref[:, 0:1]
    peak = jnp.maximum(mine, yours)
    weight, other_weight = jnp.exp2(mine - peak), jnp.exp2(yours - peak)
    share = weight / (weight + other_weight)
    mean_cell = (mean_ref[...] * share + received * (1.0 - share)).astype(BF16)
    mixed = (
        jnp.dot(mean_cell, triple_ref[:, 2 * channels :], preferred_element_type=F32)
        + triple_bias_ref[:, 2 * channels :]
    ).astype(BF16)
    attended = jnp.dot(mixed, output_ref[...], preferred_element_type=F32) + output_bias_ref[...]
    column = lax.broadcasted_iota(jnp.int32, (cols, 1), 0)
    for r, before in enumerate(split_rows(own_ref)):
        value = before + attended[r * cols : (r + 1) * cols]
        value = jnp.where(column < widths[r], value, 0.0)
        out_ref[r] = value.astype(BF16)
        if r == 0:
            top = value
    odd = lax.rem(info.tile(), 2) == 1
    inner_ref[0] = jnp.where(odd, top, value).astype(BF16)
    outer_ref[0] = jnp.where(odd, value, top).astype(BF16)


def fold_kernel(weight_ref, out_ref):
    channels = weight_ref.shape[-1]
    wide = [[weight_ref[a, b].astype(F32) for b in range(3)] for a in range(3)]

    def both(upper, lower):
        return [x + y for x, y in zip(upper, lower)]

    phases = [[wide[0], both(wide[1], wide[2])], [both(wide[0], wide[1]), wide[2]]]
    for down in range(2):
        for tap in range(2):
            left, middle, right = phases[down][tap]
            out_ref[down, tap, 0, :, 0:channels] = left.astype(BF16)
            out_ref[down, tap, 0, :, channels:] = (middle + right).astype(BF16)
            out_ref[down, tap, 1, :, 0:channels] = (left + middle).astype(BF16)
            out_ref[down, tap, 1, :, channels:] = right.astype(BF16)


def spread_columns(wide_ref, value, row, right):
    cols, channels = value.shape
    for part in range(wide_ref.shape[0]):
        lo, hi = part * LANES, min((part + 1) * LANES, channels)
        piece = value[:, lo:hi]
        if hi - lo < LANES:
            piece = jnp.concatenate([piece, jnp.zeros((cols, LANES - hi + lo), F32)], axis=1)
        wide_ref[part, row, pl.ds(right, cols, 2), :] = piece


def write_turned(out_ref, row, part, value, width):
    channels, cols = out_ref.shape[1:]
    lo, hi = part * LANES, min((part + 1) * LANES, channels)
    turned = value.T[0 : hi - lo, 0:cols]
    column = lax.broadcasted_iota(jnp.int32, (1, cols), 1)
    out_ref[row, lo:hi, :] = jnp.where(column < width, turned, 0.0).astype(BF16)


def phase_product(columns, weight):
    return lax.dot_general(
        columns, weight, (((1,), (1,)), ((), ())), preferred_element_type=F32
    )


def upsample_kernel(
    rows, info_ref, own_ref, weight_ref, bias_ref, out_ref, open_ref, columns_ref, wide_ref
):
    info = Info(info_ref, rows)
    row_count, cols, channels = own_ref.shape
    padded = columns_ref.shape[0] // row_count
    parts_out = wide_ref.shape[0]
    labels, widths = info.window(info.tile() * row_count, row_count)
    build_columns(
        columns_ref, [functools.partial(own_ref.__getitem__, r) for r in range(row_count)]
    )
    inner_rows = (row_count - 1) * padded
    for down in range(2):
        for right in range(2):
            lanes = slice(right * channels, (right + 2) * channels)
            same = phase_product(columns_ref[:, lanes], weight_ref[down, 1 - down, right])
            start = down * padded
            rim = phase_product(
                columns_ref[start : start + inner_rows, lanes], weight_ref[down, down, right]
            )
            for r in range(row_count):
                value = same[r * padded : r * padded + cols]
                near = r - 1 + 2 * down
                if 0 <= near < row_count:
                    lo = (near - down) * padded
                    value = value + jnp.where(
                        labels[near] == labels[r], rim[lo : lo + cols], 0.0
                    )
                spread_columns(wide_ref, value, 2 * r + down, right)
    for part in range(parts_out):
        open_ref[part, 0] = wide_ref[part, 0]
        open_ref[part, 1] = wide_ref[part, 2 * row_count - 1]
    for r in range(1, 2 * row_count - 1):
        for part in range(parts_out):
            value = wide_ref[part, r] + bias_ref[:, part * LANES : (part + 1) * LANES]
            write_turned(out_ref, r - 1, part, value, 2 * widths[r // 2])


def close_kernel(
    rows, info_ref, outer_ref, inner_ref, middle_ref, open_ref, weight_ref, bias_ref, out_ref,
    columns_ref, wide_ref,
):
    info = Info(info_ref, rows)
    wide_rows, _, wide_cols = out_ref.shape
    row_count, cols = wide_rows // 2, wide_cols // 2
    channels = outer_ref.shape[-1]
    padded = columns_ref.shape[0] // 2
    labels, widths = info.window(info.tile() * row_count - 1, row_count + 2)
    above, below = rims(info, outer_ref, inner_ref)
    build_columns(columns_ref, [lambda: above, lambda: below])
    for down in range(2):
        for right in range(2):
            lanes = slice(right * channels, (right + 2) * channels)
            rim = phase_product(
                columns_ref[down * padded : (down + 1) * padded, lanes],
                weight_ref[down, down, right],
            )
            spread_columns(wide_ref, rim[:cols], down, right)
    out_ref[1 : wide_rows - 1] = middle_ref[...]
    for down in range(2):
        rim_row, own_row = (row_count + 1, row_count) if down else (0, 1)
        for part in range(wide_ref.shape[0]):
            rim = jnp.where(labels[rim_row] == labels[own_row], wide_ref[part, down], 0.0)
            value = open_ref[part, down] + rim + bias_ref[:, part * LANES : (part + 1) * LANES]
            write_turned(
                out_ref, down * (wide_rows - 1), part, value, 2 * widths[own_row]
            )


def merge_stats(mine, other):
    count = mine[0] + other[0]
    safe = jnp.maximum(count, 1.0)
    off = other[1] - mine[1]
    mean = mine[1] + off * (other[0] / safe)
    spread = mine[2] + other[2] + off * off * (mine[0] * other[0] / safe)
    return jnp.stack([count, mean, spread])


def exchange(array, tiles, mask, among=None):
    moves = [(i, i ^ mask) for i in range(tiles) if among is None or among(i)]
    return lax.ppermute(array, "tile", moves)


def merge_round(stats, tiles, masks, tied=(), after=None, among=None):
    limits = among or {}
    parts = [stats] + [exchange(stats, tiles, mask, limits.get(mask)) for mask in masks]
    free = ()
    if tied:
        *parts[2:], free = lax.optimization_barrier((*parts[2:], after))
        parts[1], *tied = lax.optimization_barrier((parts[1], *tied))
    while len(parts) > 1:
        parts = [merge_stats(*parts[i : i + 2]) for i in range(0, len(parts), 2)]
    return (parts[0], *tied, free) if tied else parts[0]


def merge_masks(tiles):
    bits = [1 << i for i in range(tiles.bit_length() - 1)]
    pairs = [bits[i : i + 2] for i in range(0, len(bits), 2)]
    return [[p[0], p[1], p[0] ^ p[1]] if len(p) == 2 else p for p in pairs]


def shards(
    tiles,
    frames,
    latents,
    row_video,
    video_cols,
    first_gain,
    first_shift,
    conv_weight,
    conv_bias,
    second_gain,
    second_shift,
    triple_weight,
    triple_bias,
    output_weight,
    output_bias,
    upsample_weight,
    upsample_bias,
):
    row_count, frame_count, cols, channels = latents.shape
    assert frame_count == 1 and row_count == ROWS_OF_TILE and tiles % 4 == 0
    out_channels = upsample_weight.shape[-1]
    rows = row_count * tiles
    cells = row_count * cols
    padded = -(-(cols + 1) // 16) * 16
    near_rows = row_count + 2
    source = latents.reshape(row_count, cols, channels)
    tile = lax.axis_index("tile").astype(jnp.int32)
    info = jnp.concatenate([jnp.reshape(tile, (1,)), row_video, video_cols])

    def row(vector):
        return vector.reshape(1, -1)

    def shape(*dims, dtype=BF16):
        return jax.ShapeDtypeStruct(dims, dtype)

    def call(kernel, operands, out_shape, scratch=(), **kwargs):
        many = isinstance(out_shape, tuple)
        return pl.pallas_call(
            kernel,
            out_shape=out_shape,
            in_specs=[SMEM_SPEC] + [VMEM_SPEC] * len(operands),
            out_specs=(VMEM_SPEC,) * len(out_shape) if many else VMEM_SPEC,
            scratch_shapes=list(scratch),
            compiler_params=params(),
            **kwargs,
        )(info, *operands)

    outer_moves = [(i, i - 1 if i % 2 == 0 else i + 1) for i in range(tiles)]
    outer_moves = [(i, j) for i, j in outer_moves if 0 <= j < tiles]
    odd = tile % 2 == 1
    stats_shape = shape(3, SLOTS, LANES, dtype=F32)
    stats = call(
        functools.partial(stats_kernel, rows), [source], stats_shape,
        cost_estimate=cost(1.5), name="first_stats",
    )
    outer = lax.ppermute(
        jnp.where(odd, source[row_count - 1 :], source[:1]), "tile", outer_moves
    )
    inner = exchange(jnp.where(odd, source[:1], source[row_count - 1 :]), tiles, 1)
    stats, outer, inner = lax.optimization_barrier((stats, outer, inner))
    taps = min(3, frames)
    held = [
        pl.pallas_call(
            functools.partial(hold_kernel, backs),
            out_shape=shape(3 * len(backs) * channels, 3 * channels),
            in_specs=[HBM_SPEC],
            out_specs=VMEM_SPEC,
            scratch_shapes=[pltpu.SemaphoreType.DMA((len(backs), 3, 3))],
            compiler_params=pltpu.CompilerParams(vmem_limit_bytes=HOLD_VMEM_BYTES),
            cost_estimate=cost(1.5 * len(backs)),
            name="hold",
        )(conv_weight)
        for backs in ((0,), tuple(range(1, taps)))
        if backs
    ]
    rounds = merge_masks(tiles)
    layered = tiles == 16 and video_cols.shape[0] == 2

    def middle(t):
        return t // 4 in (1, 2)

    among = {12: middle} if layered else {}
    for index, masks in enumerate(reversed(rounds)):
        stats = merge_round(stats, tiles, masks)
        if index < len(held):
            stats, held[index] = lax.optimization_barrier((stats, held[index]))
    hidden, source = call(
        functools.partial(hidden_kernel, rows),
        [outer, inner, source, stats, row(first_gain), row(first_shift)],
        (shape(near_rows, padded, channels), shape(row_count, cols, channels)),
        cost_estimate=cost(1.3),
        name="hidden",
    )

    earlier = [
        lax.ppermute(hidden, "frame", [(i, i + by) for i in range(frames - by)])
        for by in range(1, taps)
    ]
    pairs = row_count // 2
    pair_shape = shape(pairs, 2 * cols, channels)
    product = call(
        functools.partial(own_conv_kernel, rows),
        [hidden, held[0]],
        shape(row_count * padded, 3 * channels, dtype=F32),
        scratch=[pltpu.VMEM((row_count * padded, 3 * channels), BF16)],
        cost_estimate=cost(2.2),
        name="own_conv",
    )
    scratch = [pltpu.VMEM((row_count * padded, 3 * (taps - 1) * channels), BF16)]
    own, stats = call(
        functools.partial(conv_kernel, rows, taps),
        earlier + [product, source, row(conv_bias)] + held[1:],
        (pair_shape, stats_shape),
        scratch=scratch if taps > 1 else [],
        cost_estimate=cost(1.5 + 2.0 * (taps - 1)),
        name="conv",
    )

    blocks = {0: own}
    neighbour = [(i, i ^ 1) for i in range(tiles)]
    if layered:
        stats = merge_round(stats, tiles, rounds[1], among=among)
        blocks[2] = exchange(own, tiles, 4)
        blocks[6] = exchange(own, tiles, 12, middle)
        stats, blocks[2], blocks[6], own_xy = merge_round(
            stats, tiles, rounds[0], (blocks[2], blocks[6]), own
        )
        inward = exchange(blocks[2], tiles, 12, middle)
        outward = exchange(blocks[6], tiles, 4, middle)
        other = exchange(own_xy, tiles, 1)
        blocks[1] = exchange(own_xy, tiles, 2)
        blocks[4] = jnp.where((tile // 4 == 1) | (tile // 4 == 2), inward, outward)
        passed, blocks[4] = lax.optimization_barrier((blocks[1], blocks[4]))
        blocks[5] = exchange(blocks[4], tiles, 2)
        blocks[3] = exchange(passed, tiles, 4)
        blocks[7] = exchange(passed, tiles, 12, middle)
        groups = [[0, 1, 2, 6, 4], [7, 3, 5]]
    else:
        for masks in rounds:
            stats = merge_round(stats, tiles, masks)
        other = exchange(own, tiles, 1)
        for mask in range(1, tiles // 2):
            blocks[mask] = exchange(own, tiles, 2 * mask)
        groups = [list(range(i, i + 4)) for i in range(0, tiles // 2, 4)]
    gain, shift = row(second_gain), row(second_shift)
    table_shape = shape(SLOTS, channels, dtype=F32)
    queries, constant, means, scales = call(
        functools.partial(query_kernel, rows),
        [other, stats, gain, shift, triple_weight, row(triple_bias)],
        (shape(cells, channels), shape(cells, LANES, dtype=F32), table_shape, table_shape),
        cost_estimate=cost(1.5),
        name="queries",
    )
    level_shape = shape(cells, LANES, dtype=F32)
    total_shape = shape(cells, channels, dtype=F32)
    state, keys = (), []
    for index, masks in enumerate(groups):
        last = index == len(groups) - 1
        outs = (shape(len(masks) * cells, channels),)
        outs += (shape(cells + 16, channels),) if last else (level_shape, level_shape, total_shape)
        normed, *state = call(
            functools.partial(attend_yours_kernel, rows, tuple(masks), index == 0, last),
            [means, scales, shift, queries, constant] + [blocks[m] for m in masks] + list(state),
            outs,
            cost_estimate=cost(0.9 * len(masks)),
            name="attend_yours",
        )
        keys.append(normed)
    (sent,) = state
    received = lax.ppermute(sent, "tile", neighbour)
    sent, own_late, upsample_weight = lax.optimization_barrier((sent, own, upsample_weight))
    mean, level = call(
        functools.partial(attend_mine_kernel, rows, tuple(tuple(masks) for masks in groups)),
        [own_late, means, scales, shift, triple_weight, row(triple_bias)] + keys,
        (total_shape, level_shape),
        cost_estimate=cost(6.0),
        name="attend_mine",
    )
    folded = pl.pallas_call(
        fold_kernel,
        out_shape=shape(2, 2, 2, out_channels, 2 * channels),
        in_specs=[VMEM_SPEC],
        out_specs=VMEM_SPEC,
        compiler_params=params(),
        cost_estimate=cost(0.5),
        name="fold",
    )(jnp.swapaxes(upsample_weight, 2, 3))

    rim_shape = shape(1, cols, channels)
    attended, inner, outer = call(
        functools.partial(finish_kernel, rows),
        [
            mean, level, received, own, triple_weight, row(triple_bias), output_weight,
            row(output_bias),
        ],
        (shape(row_count, cols, channels), rim_shape, rim_shape),
        cost_estimate=cost(1.4),
        name="finish",
    )
    outer = lax.ppermute(outer, "tile", outer_moves)
    inner = exchange(inner, tiles, 1)
    parts_out = -(-out_channels // LANES)
    wide_cols = -(-2 * cols // LANES) * LANES
    wide_bias = jnp.pad(row(upsample_bias), ((0, 0), (0, -out_channels % LANES)))
    middle, open_rows = call(
        functools.partial(upsample_kernel, rows),
        [attended, folded, wide_bias],
        (
            shape(2 * row_count - 2, out_channels, 2 * cols),
            shape(parts_out, 2, wide_cols, LANES, dtype=F32),
        ),
        scratch=[
            pltpu.VMEM((row_count * padded, 3 * channels), BF16),
            pltpu.VMEM((parts_out, 2 * row_count, wide_cols, LANES), F32),
        ],
        cost_estimate=cost(2.0),
        name="upsample",
    )
    decoded = call(
        functools.partial(close_kernel, rows),
        [outer, inner, middle, open_rows, folded, wide_bias],
        shape(2 * row_count, out_channels, 2 * cols),
        scratch=[
            pltpu.VMEM((2 * padded, 3 * channels), BF16),
            pltpu.VMEM((parts_out, 2, wide_cols, LANES), F32),
        ],
        cost_estimate=cost(1.0),
        name="close",
    )
    return jnp.swapaxes(decoded, 1, 2).reshape(2 * row_count, 1, 2 * cols, out_channels)


def solution(mesh):
    sizes = dict(mesh.shape)
    in_specs = (P("tile", "frame", None, None),) + (P(),) * 14
    out_specs = P("tile", "frame", None, None)
    body = functools.partial(shards, sizes["tile"], sizes["frame"])
    return jax.shard_map(body, mesh=mesh, in_specs=in_specs, out_specs=out_specs, check_vma=False)
```

```python
import functools
import math

import jax
import jax.numpy as jnp
from jax import lax
from jax.experimental import pallas as pl
from jax.experimental.pallas import tpu as pltpu
from jax.sharding import PartitionSpec as P

GROUPS = 32
EPSILON = 1e-05
MASKED = -1e30
LOWEST = -5e29
SLOTS = 8
ROWS_OF_TILE = 4
LANES = 128
VMEM_BYTES = 24 * 1024 * 1024
HOLD_VMEM_BYTES = 46 * 1024 * 1024
F32 = jnp.float32
BF16 = jnp.bfloat16

SMEM_SPEC = pl.BlockSpec(memory_space=pltpu.SMEM)
VMEM_SPEC = pl.BlockSpec(memory_space=pltpu.VMEM)
HBM_SPEC = pl.BlockSpec(memory_space=pltpu.HBM)


def cost(microseconds):
    return pl.CostEstimate(
        flops=int(microseconds * 1.1e9), bytes_accessed=0, transcendentals=0
    )


def params():
    return pltpu.CompilerParams(vmem_limit_bytes=VMEM_BYTES)


def member_matrix(channels):
    per_group = channels // GROUPS
    group = lax.broadcasted_iota(jnp.int32, (LANES, channels), 0) * per_group
    channel = lax.broadcasted_iota(jnp.int32, (LANES, channels), 1)
    return jnp.where((channel >= group) & (channel < group + per_group), 1.0, 0.0).astype(BF16)


def thirds(values):
    parts = []
    for _ in range(3):
        parts.append(values.astype(BF16).astype(F32))
        values = values - parts[-1]
    return jnp.concatenate(parts, axis=0).astype(BF16)


def added(products):
    rows = products.shape[0] // 3
    return (products[2 * rows :] + products[rows : 2 * rows]) + products[:rows]


def to_groups(values, member):
    return added(
        lax.dot_general(
            thirds(values), member, (((1,), (1,)), ((), ())), preferred_element_type=F32
        )
    )


def to_channels(values, member):
    return added(jnp.dot(thirds(values), member, preferred_element_type=F32))


class Info:
    def __init__(self, ref, rows):
        self.ref, self.rows = ref, rows
        self.videos = ref.shape[0] - 1 - rows

    def tile(self):
        return self.ref[0]

    def label(self, row):
        inside = (row >= 0) & (row < self.rows)
        return jnp.where(inside, self.ref[1 + jnp.clip(row, 0, self.rows - 1)], -1)

    def width(self, label):
        return jnp.where(label >= 0, self.ref[1 + self.rows + jnp.maximum(label, 0)], 0)

    def window(self, first, count):
        labels = [self.label(first + r) for r in range(count)]
        return labels, [self.width(label) for label in labels]


def pick(table, label, videos):
    chosen = table[0:1]
    for video in range(1, videos):
        chosen = jnp.where(label == video, table[video : video + 1], chosen)
    return chosen


def norm_tables(stats_ref, gain_ref):
    member = member_matrix(gain_ref.shape[1])
    counts = jnp.maximum(stats_ref[0], 1.0)
    scale = lax.rsqrt(stats_ref[2] / counts + EPSILON)
    return to_channels(stats_ref[1], member), to_channels(scale, member) * gain_ref[...]


def write_stats(out_ref, rows, labels, widths, videos, channels):
    member = member_matrix(channels)
    per_group = channels // GROUPS
    cols = rows[0].shape[0]
    slot = lax.broadcasted_iota(jnp.int32, (SLOTS, 1), 0)
    column = lax.broadcasted_iota(jnp.int32, (cols, 1), 0)
    sums = jnp.zeros((SLOTS, channels), F32)
    counts = jnp.zeros((SLOTS, 1), F32)
    for index, row in enumerate(rows):
        sums = jnp.where(slot == index, jnp.sum(row, axis=0, keepdims=True), sums)
        counts = jnp.where(slot == index, (widths[index] * per_group).astype(F32), counts)
    means = to_groups(sums, member) / jnp.maximum(counts, 1.0)
    means_wide = to_channels(means, member)
    squares = jnp.zeros((SLOTS, channels), F32)
    for index, row in enumerate(rows):
        centered = jnp.where(column < widths[index], row - means_wide[index : index + 1], 0.0)
        squares = jnp.where(
            slot == index, jnp.sum(centered * centered, axis=0, keepdims=True), squares
        )
    spreads = to_groups(squares, member)
    out_ref[...] = jnp.zeros(out_ref.shape, F32)
    for video in range(videos):
        total = jnp.zeros((1, LANES), F32)
        count = jnp.zeros((1, LANES), F32)
        for index in range(len(rows)):
            mine = labels[index] == video
            row_count = counts[index : index + 1]
            total = total + jnp.where(mine, means[index : index + 1] * row_count, 0.0)
            count = count + jnp.where(mine, row_count, 0.0)
        mean = total / jnp.maximum(count, 1.0)
        spread = jnp.zeros((1, LANES), F32)
        for index in range(len(rows)):
            off = means[index : index + 1] - mean
            part = spreads[index : index + 1] + counts[index : index + 1] * off * off
            spread = spread + jnp.where(labels[index] == video, part, 0.0)
        out_ref[0, video : video + 1, :] = count
        out_ref[1, video : video + 1, :] = mean
        out_ref[2, video : video + 1, :] = spread


def build_columns(columns_ref, row_refs):
    padded = columns_ref.shape[0] // len(row_refs)
    for index, row in enumerate(row_refs):
        cells = row().astype(F32)
        count, channels = cells.shape
        cells = jnp.concatenate([cells, jnp.zeros((padded - count, channels), F32)], axis=0)
        start = index * padded
        columns_ref[start : start + padded, 0:channels] = pltpu.roll(cells, 1, 0).astype(BF16)
        columns_ref[start : start + padded, channels : 2 * channels] = cells.astype(BF16)
        columns_ref[start : start + padded, 2 * channels : 3 * channels] = pltpu.roll(
            cells, padded - 1, 0
        ).astype(BF16)


def stats_kernel(rows, info_ref, latents_ref, out_ref):
    info = Info(info_ref, rows)
    row_count, cols, channels = latents_ref.shape
    labels, widths = info.window(info.tile() * row_count, row_count)
    column = lax.broadcasted_iota(jnp.int32, (cols, 1), 0)
    cells = [
        jnp.where(column < widths[r], latents_ref[r].astype(F32), 0.0) for r in range(row_count)
    ]
    write_stats(out_ref, cells, labels, widths, info.videos, channels)


def rims(info, outer_ref, inner_ref):
    odd = lax.rem(info.tile(), 2) == 1
    inner, outer = inner_ref[0].astype(F32), outer_ref[0].astype(F32)
    return jnp.where(odd, inner, outer), jnp.where(odd, outer, inner)


def hidden_kernel(
    rows, info_ref, outer_ref, inner_ref, latents_ref, stats_ref, gain_ref, shift_ref, out_ref,
    source_ref,
):
    info = Info(info_ref, rows)
    row_count, cols, _ = latents_ref.shape
    labels, widths = info.window(info.tile() * row_count - 1, row_count + 2)
    means, scales = norm_tables(stats_ref, gain_ref)
    column = lax.broadcasted_iota(jnp.int32, (cols, 1), 0)
    above, below = rims(info, outer_ref, inner_ref)
    sources = [above] + [latents_ref[r].astype(F32) for r in range(row_count)] + [below]
    for r, source in enumerate(sources):
        mean = pick(means, labels[r], info.videos)
        scale = pick(scales, labels[r], info.videos)
        normed = (source - mean) * scale + shift_ref[...]
        active = normed / (1.0 + jnp.exp(-normed))
        active = jnp.where(column < widths[r], active, 0.0)
        rest = jnp.zeros((out_ref.shape[1] - cols, active.shape[1]), F32)
        out_ref[r] = jnp.concatenate([active, rest], axis=0).astype(BF16)
    source_ref[...] = latents_ref[...]


def hold_kernel(backs, weight_ref, held_ref, sems):
    channels = weight_ref.shape[-1]
    copies = [
        pltpu.make_async_copy(
            weight_ref.at[2 - back, tap, side],
            held_ref.at[
                pl.ds((3 * index + tap) * channels, channels), pl.ds(side * channels, channels)
            ],
            sems.at[index, tap, side],
        )
        for index, back in enumerate(backs)
        for tap in range(3)
        for side in range(3)
    ]
    for copy in copies:
        copy.start()
    for copy in copies:
        copy.wait()


def row_taps(info, hidden_refs, inputs_ref):
    near_rows, padded, channels = hidden_refs[0].shape
    row_count = near_rows - 2
    labels, _ = info.window(info.tile() * row_count - 1, near_rows)
    for back, hidden_ref in enumerate(hidden_refs):
        for tap in range(3):
            lanes = slice((3 * back + tap) * channels, (3 * back + tap + 1) * channels)
            for r in range(row_count):
                block = hidden_ref[r + tap]
                if tap != 1:
                    same = labels[r + tap] == labels[r + 1]
                    block = jnp.where(same, block, jnp.zeros_like(block))
                inputs_ref[r * padded : (r + 1) * padded, lanes] = block


def own_conv_kernel(rows, info_ref, hidden_ref, held_ref, product_ref, inputs_ref):
    row_taps(Info(info_ref, rows), [hidden_ref], inputs_ref)
    product_ref[...] = jnp.dot(inputs_ref[...], held_ref[...], preferred_element_type=F32)


def conv_kernel(rows, taps, info_ref, *rest):
    hidden_refs, rest = rest[: taps - 1], rest[taps - 1 :]
    product_ref, latents_ref, bias_ref, *rest = rest
    held_refs, (own_ref, stats_ref, *inputs_refs) = rest[: taps > 1], rest[taps > 1 :]
    row_count, cols, channels = latents_ref.shape
    info = Info(info_ref, rows)
    padded = product_ref.shape[0] // row_count
    labels, widths = info.window(info.tile() * row_count - 1, row_count + 2)
    product = product_ref[...]
    if hidden_refs:
        (inputs_ref,) = inputs_refs
        row_taps(info, hidden_refs, inputs_ref)
        product = product + jnp.dot(
            inputs_ref[...], held_refs[0][...], preferred_element_type=F32
        )
    column = lax.broadcasted_iota(jnp.int32, (cols, 1), 0)
    cells = []
    for r in range(row_count):
        lines = slice(r * padded, (r + 1) * padded)
        branch = pltpu.roll(product[lines, 0:channels], 1, 0)
        branch = branch + product[lines, channels : 2 * channels]
        branch = branch + pltpu.roll(product[lines, 2 * channels :], padded - 1, 0)
        value = latents_ref[r].astype(F32) + branch[:cols] + bias_ref[...]
        value = jnp.where(column < widths[r + 1], value, 0.0).astype(BF16)
        cells.append(value.astype(F32))
    for pair in range(row_count // 2):
        own_ref[pair] = jnp.concatenate(cells[2 * pair : 2 * pair + 2], axis=0).astype(BF16)
    write_stats(stats_ref, cells, labels[1:-1], widths[1:-1], info.videos, channels)


def split_rows(pairs_ref):
    cols = pairs_ref.shape[1] // 2
    cells = []
    for pair in range(pairs_ref.shape[0]):
        both = pairs_ref[pair].astype(F32)
        cells += [both[:cols], both[cols:]]
    return cells


def turned_queries(info, tile, pairs_ref, means, scales, shift_ref, weight_ref, bias_ref):
    pairs, double, channels = pairs_ref.shape
    cols = double // 2
    column = lax.broadcasted_iota(jnp.int32, (cols, 1), 0)
    labels, widths = info.window(tile * 2 * pairs, 2 * pairs)
    cells = []
    for r, values in enumerate(split_rows(pairs_ref)):
        mean = pick(means, labels[r], info.videos)
        scale = pick(scales, labels[r], info.videos)
        normed = (values - mean) * scale + shift_ref[...]
        cells.append(jnp.where(column < widths[r], normed, 0.0))
    cells = jnp.concatenate(cells, axis=0).astype(BF16)
    queries = (
        jnp.dot(cells, weight_ref[:, 0:channels], preferred_element_type=F32)
        + bias_ref[:, 0:channels]
    ).astype(BF16)
    factor = channels ** (-0.5) * math.log2(math.e)
    turned = lax.dot_general(
        queries, weight_ref[:, channels : 2 * channels], (((1,), (1,)), ((), ())),
        preferred_element_type=F32,
    )
    constant = jnp.sum(
        queries.astype(F32) * bias_ref[:, channels : 2 * channels], axis=1, keepdims=True
    )
    return (turned * factor).astype(BF16), constant * factor


def query_kernel(
    rows, info_ref, other_ref, stats_ref, gain_ref, shift_ref, weight_ref, bias_ref, queries_ref,
    constant_ref, means_ref, scales_ref,
):
    info = Info(info_ref, rows)
    means, scales = norm_tables(stats_ref, gain_ref)
    means_ref[...] = means
    scales_ref[...] = scales
    queries, constant = turned_queries(
        info, info.tile() ^ 1, other_ref, means, scales, shift_ref, weight_ref, bias_ref
    )
    queries_ref[...] = queries
    constant_ref[...] = jnp.broadcast_to(constant, constant_ref.shape)


def key_codes(info, masks, span, cols):
    row_count = span // cols
    position = lax.broadcasted_iota(jnp.int32, (1, len(masks) * span), 1)
    codes = jnp.full((1, len(masks) * span), -2.0, F32)
    for index, mask in enumerate(masks):
        near, widths = info.window((info.tile() ^ (2 * mask)) * row_count, row_count)
        for r in range(row_count):
            start = index * span + r * cols
            inside = (position >= start) & (position < start + widths[r])
            codes = jnp.where(inside, near[r].astype(F32), codes)
    return codes


def query_codes(info, tile, span, cols):
    row_count = span // cols
    labels, _ = info.window(tile * row_count, row_count)
    return jnp.concatenate(
        [jnp.zeros((cols, 1), F32) + label.astype(F32) for label in labels], axis=0
    )


def scores_of(queries, keys, codes, query_code):
    scores = lax.dot_general(
        queries, keys, (((1,), (1,)), ((), ())), preferred_element_type=F32
    )
    return jnp.where(codes == query_code, scores, MASKED)


def mean_and_level(peak, denominator, total):
    some = denominator > 0.0
    safe = jnp.where(some, denominator, 1.0)
    return total / safe, jnp.where(some, peak + jnp.log2(safe), LOWEST)


def attend_yours_kernel(rows, masks, first, last, info_ref, *rest):
    means_ref, scales_ref, shift_ref, queries_ref, constant_ref, *rest = rest
    block_refs, rest = rest[: len(masks)], rest[len(masks) :]
    if not first:
        old_peak_ref, old_sum_ref, old_total_ref, *rest = rest
    keys_ref, *out_refs = rest
    info = Info(info_ref, rows)
    span, channels = queries_ref.shape
    pairs, double, _ = block_refs[0].shape
    cols = double // 2
    row_count = 2 * pairs
    tile = info.tile()
    means, scales = means_ref[...], scales_ref[...]
    for index, (mask, block_ref) in enumerate(zip(masks, block_refs)):
        near, _ = info.window((tile ^ (2 * mask)) * row_count, row_count)
        for pair in range(pairs):
            both = block_ref[pair].astype(F32)
            halves = []
            for half in range(2):
                label = near[2 * pair + half]
                mean = pick(means, label, info.videos)
                scale = pick(scales, label, info.videos)
                values = both[half * cols : (half + 1) * cols]
                halves.append((values - mean) * scale + shift_ref[...])
            start = index * span + pair * double
            keys_ref[start : start + double, :] = jnp.concatenate(halves, axis=0).astype(BF16)
    constant = constant_ref[:, 0:1]
    scores = scores_of(
        queries_ref[...], keys_ref[...], key_codes(info, masks, span, cols),
        query_codes(info, tile ^ 1, span, cols),
    )
    peak = jnp.maximum(LOWEST, jnp.max(scores, axis=1, keepdims=True) + constant)
    if not first:
        largest = old_peak_ref[:, 0:1]
        peak = jnp.maximum(largest, peak)
    weights = jnp.exp2(scores - (peak - constant))
    denominator = jnp.sum(weights, axis=1, keepdims=True)
    total = jnp.dot(weights.astype(BF16), keys_ref[...], preferred_element_type=F32)
    if not first:
        factor = jnp.exp2(largest - peak)
        denominator = old_sum_ref[:, 0:1] * factor + denominator
        total = old_total_ref[...] * factor + total
    if not last:
        peak_ref, sum_ref, total_ref = out_refs
        peak_ref[...] = jnp.broadcast_to(peak, peak_ref.shape)
        sum_ref[...] = jnp.broadcast_to(denominator, sum_ref.shape)
        total_ref[...] = total
        return
    (sent_ref,) = out_refs
    mean, level = mean_and_level(peak, denominator, total)
    sent_ref[0:span, :] = mean.astype(BF16)
    slots = sent_ref.shape[0] - span
    slot = lax.broadcasted_iota(jnp.int32, (slots, 1), 0)
    packed = jnp.zeros((slots, LANES), F32)
    for r in range(row_count):
        left = level[r * cols : (r + 1) * cols]
        left = jnp.sum(jnp.where(diagonal(cols), left, 0.0), axis=0, keepdims=True)
        for part in range(3):
            rounded = left.astype(BF16).astype(F32)
            packed = jnp.where(slot == 3 * r + part, rounded, packed)
            left = left - rounded
    sent_ref[span:, 0:LANES] = packed.astype(BF16)
    sent_ref[span:, LANES:] = jnp.zeros((slots, channels - LANES), BF16)


def attend_mine_kernel(
    rows, groups, info_ref, own_ref, means_ref, scales_ref, shift_ref, weight_ref, bias_ref, *rest
):
    key_refs, (mean_ref, level_ref) = rest[: len(groups)], rest[len(groups) :]
    info = Info(info_ref, rows)
    span = mean_ref.shape[0]
    queries, constant = turned_queries(
        info, info.tile(), own_ref, means_ref[...], scales_ref[...], shift_ref, weight_ref,
        bias_ref,
    )
    cols = span // ROWS_OF_TILE
    query_code = query_codes(info, info.tile(), span, cols)
    peak = jnp.full((span, 1), LOWEST, F32)
    scores = []
    for masks, key_ref in zip(groups, key_refs):
        codes = key_codes(info, masks, span, cols)
        scores.append(scores_of(queries, key_ref[...], codes, query_code))
        peak = jnp.maximum(peak, jnp.max(scores[-1], axis=1, keepdims=True) + constant)
    denominator, total = 0.0, 0.0
    for part, key_ref in zip(scores, key_refs):
        weights = jnp.exp2(part - (peak - constant))
        denominator = denominator + jnp.sum(weights, axis=1, keepdims=True)
        total = total + jnp.dot(
            weights.astype(BF16), key_ref[...], preferred_element_type=F32
        )
    mean, level = mean_and_level(peak, denominator, total)
    mean_ref[...] = mean
    level_ref[...] = jnp.broadcast_to(level, level_ref.shape)


def diagonal(cols):
    return lax.broadcasted_iota(jnp.int32, (cols, LANES), 0) == lax.broadcasted_iota(
        jnp.int32, (cols, LANES), 1
    )


def finish_kernel(
    rows, info_ref, mean_ref, level_ref, received_ref, own_ref, triple_ref, triple_bias_ref,
    output_ref, output_bias_ref, out_ref, inner_ref, outer_ref,
):
    info = Info(info_ref, rows)
    row_count, cols, channels = out_ref.shape
    span = row_count * cols
    _, widths = info.window(info.tile() * row_count, row_count)
    received = received_ref[0:span, :].astype(F32)
    levels = received_ref[span:, 0:LANES].astype(F32)
    yours = []
    for r in range(row_count):
        level = levels[3 * r : 3 * r + 1] + levels[3 * r + 1 : 3 * r + 2]
        level = level + levels[3 * r + 2 : 3 * r + 3]
        yours.append(jnp.sum(jnp.where(diagonal(cols), level, 0.0), axis=1, keepdims=True))
    yours = jnp.concatenate(yours, axis=0)
    mine = level_ref[:, 0:1]
    peak = jnp.maximum(mine, yours)
    weight, other_weight = jnp.exp2(mine - peak), jnp.exp2(yours - peak)
    share = weight / (weight + other_weight)
    mean_cell = (mean_ref[...] * share + received * (1.0 - share)).astype(BF16)
    mixed = (
        jnp.dot(mean_cell, triple_ref[:, 2 * channels :], preferred_element_type=F32)
        + triple_bias_ref[:, 2 * channels :]
    ).astype(BF16)
    attended = jnp.dot(mixed, output_ref[...], preferred_element_type=F32) + output_bias_ref[...]
    column = lax.broadcasted_iota(jnp.int32, (cols, 1), 0)
    for r, before in enumerate(split_rows(own_ref)):
        value = before + attended[r * cols : (r + 1) * cols]
        value = jnp.where(column < widths[r], value, 0.0)
        out_ref[r] = value.astype(BF16)
        if r == 0:
            top = value
    odd = lax.rem(info.tile(), 2) == 1
    inner_ref[0] = jnp.where(odd, top, value).astype(BF16)
    outer_ref[0] = jnp.where(odd, value, top).astype(BF16)


def fold_kernel(weight_ref, out_ref):
    channels = weight_ref.shape[-1]
    wide = [[weight_ref[a, b].astype(F32) for b in range(3)] for a in range(3)]

    def both(upper, lower):
        return [x + y for x, y in zip(upper, lower)]

    phases = [[wide[0], both(wide[1], wide[2])], [both(wide[0], wide[1]), wide[2]]]
    for down in range(2):
        for tap in range(2):
            left, middle, right = phases[down][tap]
            out_ref[down, tap, 0, :, 0:channels] = left.astype(BF16)
            out_ref[down, tap, 0, :, channels:] = (middle + right).astype(BF16)
            out_ref[down, tap, 1, :, 0:channels] = (left + middle).astype(BF16)
            out_ref[down, tap, 1, :, channels:] = right.astype(BF16)


def spread_columns(wide_ref, value, row, right):
    cols, channels = value.shape
    for part in range(wide_ref.shape[0]):
        lo, hi = part * LANES, min((part + 1) * LANES, channels)
        piece = value[:, lo:hi]
        if hi - lo < LANES:
            piece = jnp.concatenate([piece, jnp.zeros((cols, LANES - hi + lo), F32)], axis=1)
        wide_ref[part, row, pl.ds(right, cols, 2), :] = piece


def write_turned(out_ref, row, part, value, width):
    channels, cols = out_ref.shape[1:]
    lo, hi = part * LANES, min((part + 1) * LANES, channels)
    turned = value.T[0 : hi - lo, 0:cols]
    column = lax.broadcasted_iota(jnp.int32, (1, cols), 1)
    out_ref[row, lo:hi, :] = jnp.where(column < width, turned, 0.0).astype(BF16)


def phase_product(columns, weight):
    return lax.dot_general(
        columns, weight, (((1,), (1,)), ((), ())), preferred_element_type=F32
    )


def upsample_kernel(
    rows, info_ref, own_ref, weight_ref, bias_ref, out_ref, open_ref, columns_ref, wide_ref
):
    info = Info(info_ref, rows)
    row_count, cols, channels = own_ref.shape
    padded = columns_ref.shape[0] // row_count
    parts_out = wide_ref.shape[0]
    labels, widths = info.window(info.tile() * row_count, row_count)
    build_columns(
        columns_ref, [functools.partial(own_ref.__getitem__, r) for r in range(row_count)]
    )
    inner_rows = (row_count - 1) * padded
    for down in range(2):
        for right in range(2):
            lanes = slice(right * channels, (right + 2) * channels)
            same = phase_product(columns_ref[:, lanes], weight_ref[down, 1 - down, right])
            start = down * padded
            rim = phase_product(
                columns_ref[start : start + inner_rows, lanes], weight_ref[down, down, right]
            )
            for r in range(row_count):
                value = same[r * padded : r * padded + cols]
                near = r - 1 + 2 * down
                if 0 <= near < row_count:
                    lo = (near - down) * padded
                    value = value + jnp.where(
                        labels[near] == labels[r], rim[lo : lo + cols], 0.0
                    )
                spread_columns(wide_ref, value, 2 * r + down, right)
    for part in range(parts_out):
        open_ref[part, 0] = wide_ref[part, 0]
        open_ref[part, 1] = wide_ref[part, 2 * row_count - 1]
    for r in range(1, 2 * row_count - 1):
        for part in range(parts_out):
            value = wide_ref[part, r] + bias_ref[:, part * LANES : (part + 1) * LANES]
            write_turned(out_ref, r - 1, part, value, 2 * widths[r // 2])


def close_kernel(
    rows, info_ref, outer_ref, inner_ref, middle_ref, open_ref, weight_ref, bias_ref, out_ref,
    columns_ref, wide_ref,
):
    info = Info(info_ref, rows)
    wide_rows, _, wide_cols = out_ref.shape
    row_count, cols = wide_rows // 2, wide_cols // 2
    channels = outer_ref.shape[-1]
    padded = columns_ref.shape[0] // 2
    labels, widths = info.window(info.tile() * row_count - 1, row_count + 2)
    above, below = rims(info, outer_ref, inner_ref)
    build_columns(columns_ref, [lambda: above, lambda: below])
    for down in range(2):
        for right in range(2):
            lanes = slice(right * channels, (right + 2) * channels)
            rim = phase_product(
                columns_ref[down * padded : (down + 1) * padded, lanes],
                weight_ref[down, down, right],
            )
            spread_columns(wide_ref, rim[:cols], down, right)
    out_ref[1 : wide_rows - 1] = middle_ref[...]
    for down in range(2):
        rim_row, own_row = (row_count + 1, row_count) if down else (0, 1)
        for part in range(wide_ref.shape[0]):
            rim = jnp.where(labels[rim_row] == labels[own_row], wide_ref[part, down], 0.0)
            value = open_ref[part, down] + rim + bias_ref[:, part * LANES : (part + 1) * LANES]
            write_turned(
                out_ref, down * (wide_rows - 1), part, value, 2 * widths[own_row]
            )


def merge_stats(mine, other):
    count = mine[0] + other[0]
    safe = jnp.maximum(count, 1.0)
    off = other[1] - mine[1]
    mean = mine[1] + off * (other[0] / safe)
    spread = mine[2] + other[2] + off * off * (mine[0] * other[0] / safe)
    return jnp.stack([count, mean, spread])


def exchange(array, tiles, mask, among=None):
    moves = [(i, i ^ mask) for i in range(tiles) if among is None or among(i)]
    return lax.ppermute(array, "tile", moves)


def merge_round(stats, tiles, masks, tied=(), after=None):
    parts = [stats] + [exchange(stats, tiles, mask) for mask in masks]
    free = ()
    if tied:
        *parts[2:], free = lax.optimization_barrier((*parts[2:], after))
        parts[1], *tied = lax.optimization_barrier((parts[1], *tied))
    while len(parts) > 1:
        parts = [merge_stats(*parts[i : i + 2]) for i in range(0, len(parts), 2)]
    return (parts[0], *tied, free) if tied else parts[0]


def merge_masks(tiles):
    bits = [1 << i for i in range(tiles.bit_length() - 1)]
    pairs = [bits[i : i + 2] for i in range(0, len(bits), 2)]
    return [[p[0], p[1], p[0] ^ p[1]] if len(p) == 2 else p for p in pairs]


def shards(
    tiles,
    frames,
    latents,
    row_video,
    video_cols,
    first_gain,
    first_shift,
    conv_weight,
    conv_bias,
    second_gain,
    second_shift,
    triple_weight,
    triple_bias,
    output_weight,
    output_bias,
    upsample_weight,
    upsample_bias,
):
    row_count, frame_count, cols, channels = latents.shape
    assert frame_count == 1 and row_count == ROWS_OF_TILE and tiles % 4 == 0
    out_channels = upsample_weight.shape[-1]
    rows = row_count * tiles
    cells = row_count * cols
    padded = -(-(cols + 1) // 16) * 16
    near_rows = row_count + 2
    source = latents.reshape(row_count, cols, channels)
    tile = lax.axis_index("tile").astype(jnp.int32)
    info = jnp.concatenate([jnp.reshape(tile, (1,)), row_video, video_cols])

    def row(vector):
        return vector.reshape(1, -1)

    def shape(*dims, dtype=BF16):
        return jax.ShapeDtypeStruct(dims, dtype)

    def call(kernel, operands, out_shape, scratch=(), **kwargs):
        many = isinstance(out_shape, tuple)
        return pl.pallas_call(
            kernel,
            out_shape=out_shape,
            in_specs=[SMEM_SPEC] + [VMEM_SPEC] * len(operands),
            out_specs=(VMEM_SPEC,) * len(out_shape) if many else VMEM_SPEC,
            scratch_shapes=list(scratch),
            compiler_params=params(),
            **kwargs,
        )(info, *operands)

    outer_moves = [(i, i - 1 if i % 2 == 0 else i + 1) for i in range(tiles)]
    outer_moves = [(i, j) for i, j in outer_moves if 0 <= j < tiles]
    odd = tile % 2 == 1
    stats_shape = shape(3, SLOTS, LANES, dtype=F32)
    stats = call(
        functools.partial(stats_kernel, rows), [source], stats_shape,
        cost_estimate=cost(1.5), name="first_stats",
    )
    outer = lax.ppermute(
        jnp.where(odd, source[row_count - 1 :], source[:1]), "tile", outer_moves
    )
    inner = exchange(jnp.where(odd, source[:1], source[row_count - 1 :]), tiles, 1)
    stats, outer, inner = lax.optimization_barrier((stats, outer, inner))
    taps = min(3, frames)
    held = [
        pl.pallas_call(
            functools.partial(hold_kernel, backs),
            out_shape=shape(3 * len(backs) * channels, 3 * channels),
            in_specs=[HBM_SPEC],
            out_specs=VMEM_SPEC,
            scratch_shapes=[pltpu.SemaphoreType.DMA((len(backs), 3, 3))],
            compiler_params=pltpu.CompilerParams(vmem_limit_bytes=HOLD_VMEM_BYTES),
            cost_estimate=cost(1.5 * len(backs)),
            name="hold",
        )(conv_weight)
        for backs in ((0,), tuple(range(1, taps)))
        if backs
    ]
    rounds = merge_masks(tiles)
    for index, masks in enumerate(reversed(rounds)):
        stats = merge_round(stats, tiles, masks)
        if index < len(held):
            stats, held[index] = lax.optimization_barrier((stats, held[index]))
    hidden, source = call(
        functools.partial(hidden_kernel, rows),
        [outer, inner, source, stats, row(first_gain), row(first_shift)],
        (shape(near_rows, padded, channels), shape(row_count, cols, channels)),
        cost_estimate=cost(1.3),
        name="hidden",
    )

    earlier = [
        lax.ppermute(hidden, "frame", [(i, i + by) for i in range(frames - by)])
        for by in range(1, taps)
    ]
    pairs = row_count // 2
    pair_shape = shape(pairs, 2 * cols, channels)
    product = call(
        functools.partial(own_conv_kernel, rows),
        [hidden, held[0]],
        shape(row_count * padded, 3 * channels, dtype=F32),
        scratch=[pltpu.VMEM((row_count * padded, 3 * channels), BF16)],
        cost_estimate=cost(2.2),
        name="own_conv",
    )
    scratch = [pltpu.VMEM((row_count * padded, 3 * (taps - 1) * channels), BF16)]
    own, stats = call(
        functools.partial(conv_kernel, rows, taps),
        earlier + [product, source, row(conv_bias)] + held[1:],
        (pair_shape, stats_shape),
        scratch=scratch if taps > 1 else [],
        cost_estimate=cost(1.5 + 2.0 * (taps - 1)),
        name="conv",
    )

    blocks = {0: own}
    neighbour = [(i, i ^ 1) for i in range(tiles)]
    if tiles == 16 and video_cols.shape[0] == 2:
        def middle(t):
            return t // 4 in (1, 2)

        stats = merge_round(stats, tiles, rounds[1])
        blocks[2] = exchange(own, tiles, 4)
        blocks[6] = exchange(own, tiles, 12, middle)
        stats, blocks[2], blocks[6], own_xy = merge_round(
            stats, tiles, rounds[0], (blocks[2], blocks[6]), own
        )
        inward = exchange(blocks[2], tiles, 12, middle)
        outward = exchange(blocks[6], tiles, 4, middle)
        own_x, stats = lax.optimization_barrier((own, stats))
        other = exchange(own_x, tiles, 1)
        blocks[1] = exchange(own_xy, tiles, 2)
        blocks[4] = jnp.where((tile // 4 == 1) | (tile // 4 == 2), inward, outward)
        passed, blocks[4] = lax.optimization_barrier((blocks[1], blocks[4]))
        blocks[5] = exchange(blocks[4], tiles, 2)
        blocks[3] = exchange(passed, tiles, 4)
        blocks[7] = exchange(passed, tiles, 12, middle)
        groups = [[0, 1, 2, 6, 4], [7, 3, 5]]
    else:
        for masks in rounds:
            stats = merge_round(stats, tiles, masks)
        other = exchange(own, tiles, 1)
        for mask in range(1, tiles // 2):
            blocks[mask] = exchange(own, tiles, 2 * mask)
        groups = [list(range(i, i + 4)) for i in range(0, tiles // 2, 4)]
    gain, shift = row(second_gain), row(second_shift)
    table_shape = shape(SLOTS, channels, dtype=F32)
    queries, constant, means, scales = call(
        functools.partial(query_kernel, rows),
        [other, stats, gain, shift, triple_weight, row(triple_bias)],
        (shape(cells, channels), shape(cells, LANES, dtype=F32), table_shape, table_shape),
        cost_estimate=cost(1.5),
        name="queries",
    )
    level_shape = shape(cells, LANES, dtype=F32)
    total_shape = shape(cells, channels, dtype=F32)
    state, keys = (), []
    for index, masks in enumerate(groups):
        last = index == len(groups) - 1
        outs = (shape(len(masks) * cells, channels),)
        outs += (shape(cells + 16, channels),) if last else (level_shape, level_shape, total_shape)
        normed, *state = call(
            functools.partial(attend_yours_kernel, rows, tuple(masks), index == 0, last),
            [means, scales, shift, queries, constant] + [blocks[m] for m in masks] + list(state),
            outs,
            cost_estimate=cost(0.9 * len(masks)),
            name="attend_yours",
        )
        keys.append(normed)
    (sent,) = state
    received = lax.ppermute(sent, "tile", neighbour)
    sent, own_late, upsample_weight = lax.optimization_barrier((sent, own, upsample_weight))
    mean, level = call(
        functools.partial(attend_mine_kernel, rows, tuple(tuple(masks) for masks in groups)),
        [own_late, means, scales, shift, triple_weight, row(triple_bias)] + keys,
        (total_shape, level_shape),
        cost_estimate=cost(6.0),
        name="attend_mine",
    )
    folded = pl.pallas_call(
        fold_kernel,
        out_shape=shape(2, 2, 2, out_channels, 2 * channels),
        in_specs=[VMEM_SPEC],
        out_specs=VMEM_SPEC,
        compiler_params=params(),
        cost_estimate=cost(0.5),
        name="fold",
    )(jnp.swapaxes(upsample_weight, 2, 3))

    rim_shape = shape(1, cols, channels)
    attended, inner, outer = call(
        functools.partial(finish_kernel, rows),
        [
            mean, level, received, own, triple_weight, row(triple_bias), output_weight,
            row(output_bias),
        ],
        (shape(row_count, cols, channels), rim_shape, rim_shape),
        cost_estimate=cost(1.4),
        name="finish",
    )
    outer = lax.ppermute(outer, "tile", outer_moves)
    inner = exchange(inner, tiles, 1)
    parts_out = -(-out_channels // LANES)
    wide_cols = -(-2 * cols // LANES) * LANES
    wide_bias = jnp.pad(row(upsample_bias), ((0, 0), (0, -out_channels % LANES)))
    middle, open_rows = call(
        functools.partial(upsample_kernel, rows),
        [attended, folded, wide_bias],
        (
            shape(2 * row_count - 2, out_channels, 2 * cols),
            shape(parts_out, 2, wide_cols, LANES, dtype=F32),
        ),
        scratch=[
            pltpu.VMEM((row_count * padded, 3 * channels), BF16),
            pltpu.VMEM((parts_out, 2 * row_count, wide_cols, LANES), F32),
        ],
        cost_estimate=cost(2.0),
        name="upsample",
    )
    decoded = call(
        functools.partial(close_kernel, rows),
        [outer, inner, middle, open_rows, folded, wide_bias],
        shape(2 * row_count, out_channels, 2 * cols),
        scratch=[
            pltpu.VMEM((2 * padded, 3 * channels), BF16),
            pltpu.VMEM((parts_out, 2, wide_cols, LANES), F32),
        ],
        cost_estimate=cost(1.0),
        name="close",
    )
    return jnp.swapaxes(decoded, 1, 2).reshape(2 * row_count, 1, 2 * cols, out_channels)


def solution(mesh):
    sizes = dict(mesh.shape)
    in_specs = (P("tile", "frame", None, None),) + (P(),) * 14
    out_specs = P("tile", "frame", None, None)
    body = functools.partial(shards, sizes["tile"], sizes["frame"])
    return jax.shard_map(body, mesh=mesh, in_specs=in_specs, out_specs=out_specs, check_vma=False)
```

```python
import functools
import math

import jax
import jax.numpy as jnp
from jax import lax
from jax.experimental import pallas as pl
from jax.experimental.pallas import tpu as pltpu
from jax.sharding import PartitionSpec as P

GROUPS = 32
EPSILON = 1e-05
MASKED = -1e30
LOWEST = -5e29
SLOTS = 8
ROWS_OF_TILE = 4
LANES = 128
VMEM_BYTES = 24 * 1024 * 1024
HOLD_VMEM_BYTES = 46 * 1024 * 1024
F32 = jnp.float32
BF16 = jnp.bfloat16

SMEM_SPEC = pl.BlockSpec(memory_space=pltpu.SMEM)
VMEM_SPEC = pl.BlockSpec(memory_space=pltpu.VMEM)
HBM_SPEC = pl.BlockSpec(memory_space=pltpu.HBM)


def cost(microseconds):
    return pl.CostEstimate(
        flops=int(microseconds * 1.1e9), bytes_accessed=0, transcendentals=0
    )


def params():
    return pltpu.CompilerParams(vmem_limit_bytes=VMEM_BYTES)


def member_matrix(channels):
    per_group = channels // GROUPS
    group = lax.broadcasted_iota(jnp.int32, (LANES, channels), 0) * per_group
    channel = lax.broadcasted_iota(jnp.int32, (LANES, channels), 1)
    return jnp.where((channel >= group) & (channel < group + per_group), 1.0, 0.0).astype(BF16)


def thirds(values):
    parts = []
    for _ in range(3):
        parts.append(values.astype(BF16).astype(F32))
        values = values - parts[-1]
    return jnp.concatenate(parts, axis=0).astype(BF16)


def added(products):
    rows = products.shape[0] // 3
    return (products[2 * rows :] + products[rows : 2 * rows]) + products[:rows]


def to_groups(values, member):
    return added(
        lax.dot_general(
            thirds(values), member, (((1,), (1,)), ((), ())), preferred_element_type=F32
        )
    )


def to_channels(values, member):
    return added(jnp.dot(thirds(values), member, preferred_element_type=F32))


class Info:
    def __init__(self, ref, rows):
        self.ref, self.rows = ref, rows
        self.videos = ref.shape[0] - 1 - rows

    def tile(self):
        return self.ref[0]

    def label(self, row):
        inside = (row >= 0) & (row < self.rows)
        return jnp.where(inside, self.ref[1 + jnp.clip(row, 0, self.rows - 1)], -1)

    def width(self, label):
        return jnp.where(label >= 0, self.ref[1 + self.rows + jnp.maximum(label, 0)], 0)

    def window(self, first, count):
        labels = [self.label(first + r) for r in range(count)]
        return labels, [self.width(label) for label in labels]


def pick(table, label, videos):
    chosen = table[0:1]
    for video in range(1, videos):
        chosen = jnp.where(label == video, table[video : video + 1], chosen)
    return chosen


def norm_tables(stats_ref, gain_ref):
    member = member_matrix(gain_ref.shape[1])
    counts = jnp.maximum(stats_ref[0], 1.0)
    scale = lax.rsqrt(stats_ref[2] / counts + EPSILON)
    return to_channels(stats_ref[1], member), to_channels(scale, member) * gain_ref[...]


def write_stats(out_ref, rows, labels, widths, videos, channels):
    member = member_matrix(channels)
    per_group = channels // GROUPS
    cols = rows[0].shape[0]
    slot = lax.broadcasted_iota(jnp.int32, (SLOTS, 1), 0)
    column = lax.broadcasted_iota(jnp.int32, (cols, 1), 0)
    sums = jnp.zeros((SLOTS, channels), F32)
    counts = jnp.zeros((SLOTS, 1), F32)
    for index, row in enumerate(rows):
        sums = jnp.where(slot == index, jnp.sum(row, axis=0, keepdims=True), sums)
        counts = jnp.where(slot == index, (widths[index] * per_group).astype(F32), counts)
    means = to_groups(sums, member) / jnp.maximum(counts, 1.0)
    means_wide = to_channels(means, member)
    squares = jnp.zeros((SLOTS, channels), F32)
    for index, row in enumerate(rows):
        centered = jnp.where(column < widths[index], row - means_wide[index : index + 1], 0.0)
        squares = jnp.where(
            slot == index, jnp.sum(centered * centered, axis=0, keepdims=True), squares
        )
    spreads = to_groups(squares, member)
    out_ref[...] = jnp.zeros(out_ref.shape, F32)
    for video in range(videos):
        total = jnp.zeros((1, LANES), F32)
        count = jnp.zeros((1, LANES), F32)
        for index in range(len(rows)):
            mine = labels[index] == video
            row_count = counts[index : index + 1]
            total = total + jnp.where(mine, means[index : index + 1] * row_count, 0.0)
            count = count + jnp.where(mine, row_count, 0.0)
        mean = total / jnp.maximum(count, 1.0)
        spread = jnp.zeros((1, LANES), F32)
        for index in range(len(rows)):
            off = means[index : index + 1] - mean
            part = spreads[index : index + 1] + counts[index : index + 1] * off * off
            spread = spread + jnp.where(labels[index] == video, part, 0.0)
        out_ref[0, video : video + 1, :] = count
        out_ref[1, video : video + 1, :] = mean
        out_ref[2, video : video + 1, :] = spread


def build_columns(columns_ref, row_refs):
    padded = columns_ref.shape[0] // len(row_refs)
    for index, row in enumerate(row_refs):
        cells = row().astype(F32)
        count, channels = cells.shape
        cells = jnp.concatenate([cells, jnp.zeros((padded - count, channels), F32)], axis=0)
        start = index * padded
        columns_ref[start : start + padded, 0:channels] = pltpu.roll(cells, 1, 0).astype(BF16)
        columns_ref[start : start + padded, channels : 2 * channels] = cells.astype(BF16)
        columns_ref[start : start + padded, 2 * channels : 3 * channels] = pltpu.roll(
            cells, padded - 1, 0
        ).astype(BF16)


def stats_kernel(rows, info_ref, latents_ref, out_ref):
    info = Info(info_ref, rows)
    row_count, cols, channels = latents_ref.shape
    labels, widths = info.window(info.tile() * row_count, row_count)
    column = lax.broadcasted_iota(jnp.int32, (cols, 1), 0)
    cells = [
        jnp.where(column < widths[r], latents_ref[r].astype(F32), 0.0) for r in range(row_count)
    ]
    write_stats(out_ref, cells, labels, widths, info.videos, channels)


def rims(info, outer_ref, inner_ref):
    odd = lax.rem(info.tile(), 2) == 1
    inner, outer = inner_ref[0].astype(F32), outer_ref[0].astype(F32)
    return jnp.where(odd, inner, outer), jnp.where(odd, outer, inner)


def hidden_kernel(
    rows, info_ref, outer_ref, inner_ref, latents_ref, stats_ref, gain_ref, shift_ref, out_ref,
    source_ref,
):
    info = Info(info_ref, rows)
    row_count, cols, _ = latents_ref.shape
    labels, widths = info.window(info.tile() * row_count - 1, row_count + 2)
    means, scales = norm_tables(stats_ref, gain_ref)
    column = lax.broadcasted_iota(jnp.int32, (cols, 1), 0)
    above, below = rims(info, outer_ref, inner_ref)
    sources = [above] + [latents_ref[r].astype(F32) for r in range(row_count)] + [below]
    for r, source in enumerate(sources):
        mean = pick(means, labels[r], info.videos)
        scale = pick(scales, labels[r], info.videos)
        normed = (source - mean) * scale + shift_ref[...]
        active = normed / (1.0 + jnp.exp(-normed))
        active = jnp.where(column < widths[r], active, 0.0)
        rest = jnp.zeros((out_ref.shape[1] - cols, active.shape[1]), F32)
        out_ref[r] = jnp.concatenate([active, rest], axis=0).astype(BF16)
    source_ref[...] = latents_ref[...]


def hold_kernel(backs, weight_ref, held_ref, sems):
    channels = weight_ref.shape[-1]
    copies = [
        pltpu.make_async_copy(
            weight_ref.at[2 - back, tap, side],
            held_ref.at[
                pl.ds((3 * index + tap) * channels, channels), pl.ds(side * channels, channels)
            ],
            sems.at[index, tap, side],
        )
        for index, back in enumerate(backs)
        for tap in range(3)
        for side in range(3)
    ]
    for copy in copies:
        copy.start()
    for copy in copies:
        copy.wait()


def row_taps(info, hidden_refs, inputs_ref):
    near_rows, padded, channels = hidden_refs[0].shape
    row_count = near_rows - 2
    labels, _ = info.window(info.tile() * row_count - 1, near_rows)
    for back, hidden_ref in enumerate(hidden_refs):
        for tap in range(3):
            lanes = slice((3 * back + tap) * channels, (3 * back + tap + 1) * channels)
            for r in range(row_count):
                block = hidden_ref[r + tap]
                if tap != 1:
                    same = labels[r + tap] == labels[r + 1]
                    block = jnp.where(same, block, jnp.zeros_like(block))
                inputs_ref[r * padded : (r + 1) * padded, lanes] = block


def own_conv_kernel(rows, info_ref, hidden_ref, held_ref, product_ref, inputs_ref):
    row_taps(Info(info_ref, rows), [hidden_ref], inputs_ref)
    product_ref[...] = jnp.dot(inputs_ref[...], held_ref[...], preferred_element_type=F32)


def conv_kernel(rows, taps, info_ref, *rest):
    hidden_refs, rest = rest[: taps - 1], rest[taps - 1 :]
    product_ref, latents_ref, bias_ref, *rest = rest
    held_refs, (own_ref, stats_ref, *inputs_refs) = rest[: taps > 1], rest[taps > 1 :]
    row_count, cols, channels = latents_ref.shape
    info = Info(info_ref, rows)
    padded = product_ref.shape[0] // row_count
    labels, widths = info.window(info.tile() * row_count - 1, row_count + 2)
    product = product_ref[...]
    if hidden_refs:
        (inputs_ref,) = inputs_refs
        row_taps(info, hidden_refs, inputs_ref)
        product = product + jnp.dot(
            inputs_ref[...], held_refs[0][...], preferred_element_type=F32
        )
    column = lax.broadcasted_iota(jnp.int32, (cols, 1), 0)
    cells = []
    for r in range(row_count):
        lines = slice(r * padded, (r + 1) * padded)
        branch = pltpu.roll(product[lines, 0:channels], 1, 0)
        branch = branch + product[lines, channels : 2 * channels]
        branch = branch + pltpu.roll(product[lines, 2 * channels :], padded - 1, 0)
        value = latents_ref[r].astype(F32) + branch[:cols] + bias_ref[...]
        value = jnp.where(column < widths[r + 1], value, 0.0).astype(BF16)
        cells.append(value.astype(F32))
    for pair in range(row_count // 2):
        own_ref[pair] = jnp.concatenate(cells[2 * pair : 2 * pair + 2], axis=0).astype(BF16)
    write_stats(stats_ref, cells, labels[1:-1], widths[1:-1], info.videos, channels)


def split_rows(pairs_ref):
    cols = pairs_ref.shape[1] // 2
    cells = []
    for pair in range(pairs_ref.shape[0]):
        both = pairs_ref[pair].astype(F32)
        cells += [both[:cols], both[cols:]]
    return cells


def turned_queries(info, tile, pairs_ref, means, scales, shift_ref, weight_ref, bias_ref):
    pairs, double, channels = pairs_ref.shape
    cols = double // 2
    column = lax.broadcasted_iota(jnp.int32, (cols, 1), 0)
    labels, widths = info.window(tile * 2 * pairs, 2 * pairs)
    cells = []
    for r, values in enumerate(split_rows(pairs_ref)):
        mean = pick(means, labels[r], info.videos)
        scale = pick(scales, labels[r], info.videos)
        normed = (values - mean) * scale + shift_ref[...]
        cells.append(jnp.where(column < widths[r], normed, 0.0))
    cells = jnp.concatenate(cells, axis=0).astype(BF16)
    queries = (
        jnp.dot(cells, weight_ref[:, 0:channels], preferred_element_type=F32)
        + bias_ref[:, 0:channels]
    ).astype(BF16)
    factor = channels ** (-0.5) * math.log2(math.e)
    turned = lax.dot_general(
        queries, weight_ref[:, channels : 2 * channels], (((1,), (1,)), ((), ())),
        preferred_element_type=F32,
    )
    constant = jnp.sum(
        queries.astype(F32) * bias_ref[:, channels : 2 * channels], axis=1, keepdims=True
    )
    return (turned * factor).astype(BF16), constant * factor


def query_kernel(
    rows, info_ref, other_ref, stats_ref, gain_ref, shift_ref, weight_ref, bias_ref, queries_ref,
    constant_ref, means_ref, scales_ref,
):
    info = Info(info_ref, rows)
    means, scales = norm_tables(stats_ref, gain_ref)
    means_ref[...] = means
    scales_ref[...] = scales
    queries, constant = turned_queries(
        info, info.tile() ^ 1, other_ref, means, scales, shift_ref, weight_ref, bias_ref
    )
    queries_ref[...] = queries
    constant_ref[...] = jnp.broadcast_to(constant, constant_ref.shape)


def key_codes(info, masks, span, cols):
    row_count = span // cols
    position = lax.broadcasted_iota(jnp.int32, (1, len(masks) * span), 1)
    codes = jnp.full((1, len(masks) * span), -2.0, F32)
    for index, mask in enumerate(masks):
        near, widths = info.window((info.tile() ^ (2 * mask)) * row_count, row_count)
        for r in range(row_count):
            start = index * span + r * cols
            inside = (position >= start) & (position < start + widths[r])
            codes = jnp.where(inside, near[r].astype(F32), codes)
    return codes


def query_codes(info, tile, span, cols):
    row_count = span // cols
    labels, _ = info.window(tile * row_count, row_count)
    return jnp.concatenate(
        [jnp.zeros((cols, 1), F32) + label.astype(F32) for label in labels], axis=0
    )


def scores_of(queries, keys, codes, query_code):
    scores = lax.dot_general(
        queries, keys, (((1,), (1,)), ((), ())), preferred_element_type=F32
    )
    return jnp.where(codes == query_code, scores, MASKED)


def mean_and_level(peak, denominator, total):
    some = denominator > 0.0
    safe = jnp.where(some, denominator, 1.0)
    return total / safe, jnp.where(some, peak + jnp.log2(safe), LOWEST)


def attend_yours_kernel(rows, masks, first, last, info_ref, *rest):
    means_ref, scales_ref, shift_ref, queries_ref, constant_ref, *rest = rest
    block_refs, rest = rest[: len(masks)], rest[len(masks) :]
    if not first:
        old_peak_ref, old_sum_ref, old_total_ref, *rest = rest
    keys_ref, *out_refs = rest
    info = Info(info_ref, rows)
    span, channels = queries_ref.shape
    pairs, double, _ = block_refs[0].shape
    cols = double // 2
    row_count = 2 * pairs
    tile = info.tile()
    means, scales = means_ref[...], scales_ref[...]
    for index, (mask, block_ref) in enumerate(zip(masks, block_refs)):
        near, _ = info.window((tile ^ (2 * mask)) * row_count, row_count)
        for pair in range(pairs):
            both = block_ref[pair].astype(F32)
            halves = []
            for half in range(2):
                label = near[2 * pair + half]
                mean = pick(means, label, info.videos)
                scale = pick(scales, label, info.videos)
                values = both[half * cols : (half + 1) * cols]
                halves.append((values - mean) * scale + shift_ref[...])
            start = index * span + pair * double
            keys_ref[start : start + double, :] = jnp.concatenate(halves, axis=0).astype(BF16)
    constant = constant_ref[:, 0:1]
    scores = scores_of(
        queries_ref[...], keys_ref[...], key_codes(info, masks, span, cols),
        query_codes(info, tile ^ 1, span, cols),
    )
    peak = jnp.maximum(LOWEST, jnp.max(scores, axis=1, keepdims=True) + constant)
    if not first:
        largest = old_peak_ref[:, 0:1]
        peak = jnp.maximum(largest, peak)
    weights = jnp.exp2(scores - (peak - constant))
    denominator = jnp.sum(weights, axis=1, keepdims=True)
    total = jnp.dot(weights.astype(BF16), keys_ref[...], preferred_element_type=F32)
    if not first:
        factor = jnp.exp2(largest - peak)
        denominator = old_sum_ref[:, 0:1] * factor + denominator
        total = old_total_ref[...] * factor + total
    if not last:
        peak_ref, sum_ref, total_ref = out_refs
        peak_ref[...] = jnp.broadcast_to(peak, peak_ref.shape)
        sum_ref[...] = jnp.broadcast_to(denominator, sum_ref.shape)
        total_ref[...] = total
        return
    (sent_ref,) = out_refs
    mean, level = mean_and_level(peak, denominator, total)
    sent_ref[0:span, :] = mean.astype(BF16)
    slots = sent_ref.shape[0] - span
    slot = lax.broadcasted_iota(jnp.int32, (slots, 1), 0)
    packed = jnp.zeros((slots, LANES), F32)
    for r in range(row_count):
        left = level[r * cols : (r + 1) * cols]
        left = jnp.sum(jnp.where(diagonal(cols), left, 0.0), axis=0, keepdims=True)
        for part in range(3):
            rounded = left.astype(BF16).astype(F32)
            packed = jnp.where(slot == 3 * r + part, rounded, packed)
            left = left - rounded
    sent_ref[span:, 0:LANES] = packed.astype(BF16)
    sent_ref[span:, LANES:] = jnp.zeros((slots, channels - LANES), BF16)


def attend_mine_kernel(
    rows, groups, info_ref, own_ref, means_ref, scales_ref, shift_ref, weight_ref, bias_ref, *rest
):
    key_refs, (mean_ref, level_ref) = rest[: len(groups)], rest[len(groups) :]
    info = Info(info_ref, rows)
    span = mean_ref.shape[0]
    queries, constant = turned_queries(
        info, info.tile(), own_ref, means_ref[...], scales_ref[...], shift_ref, weight_ref,
        bias_ref,
    )
    cols = span // ROWS_OF_TILE
    query_code = query_codes(info, info.tile(), span, cols)
    peak = jnp.full((span, 1), LOWEST, F32)
    scores = []
    for masks, key_ref in zip(groups, key_refs):
        codes = key_codes(info, masks, span, cols)
        scores.append(scores_of(queries, key_ref[...], codes, query_code))
        peak = jnp.maximum(peak, jnp.max(scores[-1], axis=1, keepdims=True) + constant)
    denominator, total = 0.0, 0.0
    for part, key_ref in zip(scores, key_refs):
        weights = jnp.exp2(part - (peak - constant))
        denominator = denominator + jnp.sum(weights, axis=1, keepdims=True)
        total = total + jnp.dot(
            weights.astype(BF16), key_ref[...], preferred_element_type=F32
        )
    mean, level = mean_and_level(peak, denominator, total)
    mean_ref[...] = mean
    level_ref[...] = jnp.broadcast_to(level, level_ref.shape)


def diagonal(cols):
    return lax.broadcasted_iota(jnp.int32, (cols, LANES), 0) == lax.broadcasted_iota(
        jnp.int32, (cols, LANES), 1
    )


def finish_kernel(
    rows, info_ref, mean_ref, level_ref, received_ref, own_ref, triple_ref, triple_bias_ref,
    output_ref, output_bias_ref, out_ref, inner_ref, outer_ref,
):
    info = Info(info_ref, rows)
    row_count, cols, channels = out_ref.shape
    span = row_count * cols
    _, widths = info.window(info.tile() * row_count, row_count)
    received = received_ref[0:span, :].astype(F32)
    levels = received_ref[span:, 0:LANES].astype(F32)
    yours = []
    for r in range(row_count):
        level = levels[3 * r : 3 * r + 1] + levels[3 * r + 1 : 3 * r + 2]
        level = level + levels[3 * r + 2 : 3 * r + 3]
        yours.append(jnp.sum(jnp.where(diagonal(cols), level, 0.0), axis=1, keepdims=True))
    yours = jnp.concatenate(yours, axis=0)
    mine = level_ref[:, 0:1]
    peak = jnp.maximum(mine, yours)
    weight, other_weight = jnp.exp2(mine - peak), jnp.exp2(yours - peak)
    share = weight / (weight + other_weight)
    mean_cell = (mean_ref[...] * share + received * (1.0 - share)).astype(BF16)
    mixed = (
        jnp.dot(mean_cell, triple_ref[:, 2 * channels :], preferred_element_type=F32)
        + triple_bias_ref[:, 2 * channels :]
    ).astype(BF16)
    attended = jnp.dot(mixed, output_ref[...], preferred_element_type=F32) + output_bias_ref[...]
    column = lax.broadcasted_iota(jnp.int32, (cols, 1), 0)
    for r, before in enumerate(split_rows(own_ref)):
        value = before + attended[r * cols : (r + 1) * cols]
        value = jnp.where(column < widths[r], value, 0.0)
        out_ref[r] = value.astype(BF16)
        if r == 0:
            top = value
    odd = lax.rem(info.tile(), 2) == 1
    inner_ref[0] = jnp.where(odd, top, value).astype(BF16)
    outer_ref[0] = jnp.where(odd, value, top).astype(BF16)


def fold_kernel(weight_ref, out_ref):
    channels = weight_ref.shape[-1]
    wide = [[weight_ref[a, b].astype(F32) for b in range(3)] for a in range(3)]

    def both(upper, lower):
        return [x + y for x, y in zip(upper, lower)]

    phases = [[wide[0], both(wide[1], wide[2])], [both(wide[0], wide[1]), wide[2]]]
    for down in range(2):
        for tap in range(2):
            left, middle, right = phases[down][tap]
            out_ref[down, tap, 0, :, 0:channels] = left.astype(BF16)
            out_ref[down, tap, 0, :, channels:] = (middle + right).astype(BF16)
            out_ref[down, tap, 1, :, 0:channels] = (left + middle).astype(BF16)
            out_ref[down, tap, 1, :, channels:] = right.astype(BF16)


def spread_columns(wide_ref, value, row, right):
    cols, channels = value.shape
    for part in range(wide_ref.shape[0]):
        lo, hi = part * LANES, min((part + 1) * LANES, channels)
        piece = value[:, lo:hi]
        if hi - lo < LANES:
            piece = jnp.concatenate([piece, jnp.zeros((cols, LANES - hi + lo), F32)], axis=1)
        wide_ref[part, row, pl.ds(right, cols, 2), :] = piece


def write_turned(out_ref, row, part, value, width):
    channels, cols = out_ref.shape[1:]
    lo, hi = part * LANES, min((part + 1) * LANES, channels)
    turned = value.T[0 : hi - lo, 0:cols]
    column = lax.broadcasted_iota(jnp.int32, (1, cols), 1)
    out_ref[row, lo:hi, :] = jnp.where(column < width, turned, 0.0).astype(BF16)


def phase_product(columns, weight):
    return lax.dot_general(
        columns, weight, (((1,), (1,)), ((), ())), preferred_element_type=F32
    )


def upsample_kernel(
    rows, info_ref, own_ref, weight_ref, bias_ref, out_ref, open_ref, columns_ref, wide_ref
):
    info = Info(info_ref, rows)
    row_count, cols, channels = own_ref.shape
    padded = columns_ref.shape[0] // row_count
    parts_out = wide_ref.shape[0]
    labels, widths = info.window(info.tile() * row_count, row_count)
    build_columns(
        columns_ref, [functools.partial(own_ref.__getitem__, r) for r in range(row_count)]
    )
    inner_rows = (row_count - 1) * padded
    for down in range(2):
        for right in range(2):
            lanes = slice(right * channels, (right + 2) * channels)
            same = phase_product(columns_ref[:, lanes], weight_ref[down, 1 - down, right])
            start = down * padded
            rim = phase_product(
                columns_ref[start : start + inner_rows, lanes], weight_ref[down, down, right]
            )
            for r in range(row_count):
                value = same[r * padded : r * padded + cols]
                near = r - 1 + 2 * down
                if 0 <= near < row_count:
                    lo = (near - down) * padded
                    value = value + jnp.where(
                        labels[near] == labels[r], rim[lo : lo + cols], 0.0
                    )
                spread_columns(wide_ref, value, 2 * r + down, right)
    for part in range(parts_out):
        open_ref[part, 0] = wide_ref[part, 0]
        open_ref[part, 1] = wide_ref[part, 2 * row_count - 1]
    for r in range(1, 2 * row_count - 1):
        for part in range(parts_out):
            value = wide_ref[part, r] + bias_ref[:, part * LANES : (part + 1) * LANES]
            write_turned(out_ref, r - 1, part, value, 2 * widths[r // 2])


def close_kernel(
    rows, info_ref, outer_ref, inner_ref, middle_ref, open_ref, weight_ref, bias_ref, out_ref,
    columns_ref, wide_ref,
):
    info = Info(info_ref, rows)
    wide_rows, _, wide_cols = out_ref.shape
    row_count, cols = wide_rows // 2, wide_cols // 2
    channels = outer_ref.shape[-1]
    padded = columns_ref.shape[0] // 2
    labels, widths = info.window(info.tile() * row_count - 1, row_count + 2)
    above, below = rims(info, outer_ref, inner_ref)
    build_columns(columns_ref, [lambda: above, lambda: below])
    for down in range(2):
        for right in range(2):
            lanes = slice(right * channels, (right + 2) * channels)
            rim = phase_product(
                columns_ref[down * padded : (down + 1) * padded, lanes],
                weight_ref[down, down, right],
            )
            spread_columns(wide_ref, rim[:cols], down, right)
    out_ref[1 : wide_rows - 1] = middle_ref[...]
    for down in range(2):
        rim_row, own_row = (row_count + 1, row_count) if down else (0, 1)
        for part in range(wide_ref.shape[0]):
            rim = jnp.where(labels[rim_row] == labels[own_row], wide_ref[part, down], 0.0)
            value = open_ref[part, down] + rim + bias_ref[:, part * LANES : (part + 1) * LANES]
            write_turned(
                out_ref, down * (wide_rows - 1), part, value, 2 * widths[own_row]
            )


def merge_stats(mine, other):
    count = mine[0] + other[0]
    safe = jnp.maximum(count, 1.0)
    off = other[1] - mine[1]
    mean = mine[1] + off * (other[0] / safe)
    spread = mine[2] + other[2] + off * off * (mine[0] * other[0] / safe)
    return jnp.stack([count, mean, spread])


def exchange(array, tiles, mask, among=None):
    moves = [(i, i ^ mask) for i in range(tiles) if among is None or among(i)]
    return lax.ppermute(array, "tile", moves)


def merge_round(stats, tiles, masks, tied=(), after=None):
    parts = [stats] + [exchange(stats, tiles, mask) for mask in masks]
    free = ()
    if tied:
        *parts[2:], free = lax.optimization_barrier((*parts[2:], after))
        parts[1], *tied = lax.optimization_barrier((parts[1], *tied))
    while len(parts) > 1:
        parts = [merge_stats(*parts[i : i + 2]) for i in range(0, len(parts), 2)]
    return (parts[0], *tied, free) if tied else parts[0]


def merge_masks(tiles):
    bits = [1 << i for i in range(tiles.bit_length() - 1)]
    pairs = [bits[i : i + 2] for i in range(0, len(bits), 2)]
    return [[p[0], p[1], p[0] ^ p[1]] if len(p) == 2 else p for p in pairs]


def shards(
    tiles,
    frames,
    latents,
    row_video,
    video_cols,
    first_gain,
    first_shift,
    conv_weight,
    conv_bias,
    second_gain,
    second_shift,
    triple_weight,
    triple_bias,
    output_weight,
    output_bias,
    upsample_weight,
    upsample_bias,
):
    row_count, frame_count, cols, channels = latents.shape
    assert frame_count == 1 and row_count == ROWS_OF_TILE and tiles % 4 == 0
    out_channels = upsample_weight.shape[-1]
    rows = row_count * tiles
    cells = row_count * cols
    padded = -(-(cols + 1) // 16) * 16
    near_rows = row_count + 2
    source = latents.reshape(row_count, cols, channels)
    tile = lax.axis_index("tile").astype(jnp.int32)
    info = jnp.concatenate([jnp.reshape(tile, (1,)), row_video, video_cols])

    def row(vector):
        return vector.reshape(1, -1)

    def shape(*dims, dtype=BF16):
        return jax.ShapeDtypeStruct(dims, dtype)

    def call(kernel, operands, out_shape, scratch=(), **kwargs):
        many = isinstance(out_shape, tuple)
        return pl.pallas_call(
            kernel,
            out_shape=out_shape,
            in_specs=[SMEM_SPEC] + [VMEM_SPEC] * len(operands),
            out_specs=(VMEM_SPEC,) * len(out_shape) if many else VMEM_SPEC,
            scratch_shapes=list(scratch),
            compiler_params=params(),
            **kwargs,
        )(info, *operands)

    outer_moves = [(i, i - 1 if i % 2 == 0 else i + 1) for i in range(tiles)]
    outer_moves = [(i, j) for i, j in outer_moves if 0 <= j < tiles]
    odd = tile % 2 == 1
    stats_shape = shape(3, SLOTS, LANES, dtype=F32)
    stats = call(
        functools.partial(stats_kernel, rows), [source], stats_shape,
        cost_estimate=cost(1.5), name="first_stats",
    )
    outer = lax.ppermute(
        jnp.where(odd, source[row_count - 1 :], source[:1]), "tile", outer_moves
    )
    inner = exchange(jnp.where(odd, source[:1], source[row_count - 1 :]), tiles, 1)
    stats, outer, inner = lax.optimization_barrier((stats, outer, inner))
    taps = min(3, frames)
    held = [
        pl.pallas_call(
            functools.partial(hold_kernel, backs),
            out_shape=shape(3 * len(backs) * channels, 3 * channels),
            in_specs=[HBM_SPEC],
            out_specs=VMEM_SPEC,
            scratch_shapes=[pltpu.SemaphoreType.DMA((len(backs), 3, 3))],
            compiler_params=pltpu.CompilerParams(vmem_limit_bytes=HOLD_VMEM_BYTES),
            cost_estimate=cost(1.5 * len(backs)),
            name="hold",
        )(conv_weight)
        for backs in ((0,), tuple(range(1, taps)))
        if backs
    ]
    rounds = merge_masks(tiles)
    for index, masks in enumerate(reversed(rounds)):
        stats = merge_round(stats, tiles, masks)
        if index < len(held):
            stats, held[index] = lax.optimization_barrier((stats, held[index]))
    hidden, source = call(
        functools.partial(hidden_kernel, rows),
        [outer, inner, source, stats, row(first_gain), row(first_shift)],
        (shape(near_rows, padded, channels), shape(row_count, cols, channels)),
        cost_estimate=cost(1.3),
        name="hidden",
    )

    earlier = [
        lax.ppermute(hidden, "frame", [(i, i + by) for i in range(frames - by)])
        for by in range(1, taps)
    ]
    pairs = row_count // 2
    pair_shape = shape(pairs, 2 * cols, channels)
    product = call(
        functools.partial(own_conv_kernel, rows),
        [hidden, held[0]],
        shape(row_count * padded, 3 * channels, dtype=F32),
        scratch=[pltpu.VMEM((row_count * padded, 3 * channels), BF16)],
        cost_estimate=cost(2.2),
        name="own_conv",
    )
    scratch = [pltpu.VMEM((row_count * padded, 3 * (taps - 1) * channels), BF16)]
    own, stats = call(
        functools.partial(conv_kernel, rows, taps),
        earlier + [product, source, row(conv_bias)] + held[1:],
        (pair_shape, stats_shape),
        scratch=scratch if taps > 1 else [],
        cost_estimate=cost(1.5 + 2.0 * (taps - 1)),
        name="conv",
    )

    blocks = {0: own}
    neighbour = [(i, i ^ 1) for i in range(tiles)]
    if tiles == 16 and video_cols.shape[0] == 2:
        def middle(t):
            return t // 4 in (1, 2)

        stats = merge_round(stats, tiles, rounds[1])
        blocks[2] = exchange(own, tiles, 4)
        blocks[6] = exchange(own, tiles, 12, middle)
        stats, blocks[2], blocks[6], own_xy = merge_round(
            stats, tiles, rounds[0], (blocks[2], blocks[6]), own
        )
        inward = exchange(blocks[2], tiles, 12, middle)
        outward = exchange(blocks[6], tiles, 4, middle)
        own_x, stats = lax.optimization_barrier((own, stats))
        other = exchange(own_x, tiles, 1)
        blocks[1] = exchange(own_xy, tiles, 2)
        blocks[4] = jnp.where((tile // 4 == 1) | (tile // 4 == 2), inward, outward)
        passed, blocks[4] = lax.optimization_barrier((blocks[1], blocks[4]))
        blocks[5] = exchange(blocks[4], tiles, 2)
        blocks[3] = exchange(passed, tiles, 4)
        blocks[7] = exchange(passed, tiles, 12, middle)
        groups = [[0, 1, 2, 6, 4], [7, 3, 5]]
    else:
        for masks in rounds:
            stats = merge_round(stats, tiles, masks)
        other = exchange(own, tiles, 1)
        for mask in range(1, tiles // 2):
            blocks[mask] = exchange(own, tiles, 2 * mask)
        groups = [list(range(i, i + 4)) for i in range(0, tiles // 2, 4)]
    gain, shift = row(second_gain), row(second_shift)
    table_shape = shape(SLOTS, channels, dtype=F32)
    queries, constant, means, scales = call(
        functools.partial(query_kernel, rows),
        [other, stats, gain, shift, triple_weight, row(triple_bias)],
        (shape(cells, channels), shape(cells, LANES, dtype=F32), table_shape, table_shape),
        cost_estimate=cost(1.5),
        name="queries",
    )
    level_shape = shape(cells, LANES, dtype=F32)
    total_shape = shape(cells, channels, dtype=F32)
    state, keys = (), []
    for index, masks in enumerate(groups):
        last = index == len(groups) - 1
        outs = (shape(len(masks) * cells, channels),)
        outs += (shape(cells + 16, channels),) if last else (level_shape, level_shape, total_shape)
        normed, *state = call(
            functools.partial(attend_yours_kernel, rows, tuple(masks), index == 0, last),
            [means, scales, shift, queries, constant] + [blocks[m] for m in masks] + list(state),
            outs,
            cost_estimate=cost(0.9 * len(masks)),
            name="attend_yours",
        )
        keys.append(normed)
    (sent,) = state
    received = lax.ppermute(sent, "tile", neighbour)
    sent, own_late = lax.optimization_barrier((sent, own))
    mean, level = call(
        functools.partial(attend_mine_kernel, rows, tuple(tuple(masks) for masks in groups)),
        [own_late, means, scales, shift, triple_weight, row(triple_bias)] + keys,
        (total_shape, level_shape),
        cost_estimate=cost(6.0),
        name="attend_mine",
    )
    rim_shape = shape(1, cols, channels)
    attended, inner, outer = call(
        functools.partial(finish_kernel, rows),
        [
            mean, level, received, own, triple_weight, row(triple_bias), output_weight,
            row(output_bias),
        ],
        (shape(row_count, cols, channels), rim_shape, rim_shape),
        cost_estimate=cost(1.4),
        name="finish",
    )
    outer = lax.ppermute(outer, "tile", outer_moves)
    inner = exchange(inner, tiles, 1)
    attended, upsample_weight = lax.optimization_barrier((attended, upsample_weight))
    folded = pl.pallas_call(
        fold_kernel,
        out_shape=shape(2, 2, 2, out_channels, 2 * channels),
        in_specs=[VMEM_SPEC],
        out_specs=VMEM_SPEC,
        compiler_params=params(),
        cost_estimate=cost(0.1),
        name="fold",
    )(jnp.swapaxes(upsample_weight, 2, 3))
    parts_out = -(-out_channels // LANES)
    wide_cols = -(-2 * cols // LANES) * LANES
    wide_bias = jnp.pad(row(upsample_bias), ((0, 0), (0, -out_channels % LANES)))
    middle, open_rows = call(
        functools.partial(upsample_kernel, rows),
        [attended, folded, wide_bias],
        (
            shape(2 * row_count - 2, out_channels, 2 * cols),
            shape(parts_out, 2, wide_cols, LANES, dtype=F32),
        ),
        scratch=[
            pltpu.VMEM((row_count * padded, 3 * channels), BF16),
            pltpu.VMEM((parts_out, 2 * row_count, wide_cols, LANES), F32),
        ],
        cost_estimate=cost(0.2),
        name="upsample",
    )
    decoded = call(
        functools.partial(close_kernel, rows),
        [outer, inner, middle, open_rows, folded, wide_bias],
        shape(2 * row_count, out_channels, 2 * cols),
        scratch=[
            pltpu.VMEM((2 * padded, 3 * channels), BF16),
            pltpu.VMEM((parts_out, 2, wide_cols, LANES), F32),
        ],
        cost_estimate=cost(1.0),
        name="close",
    )
    return jnp.swapaxes(decoded, 1, 2).reshape(2 * row_count, 1, 2 * cols, out_channels)


def solution(mesh):
    sizes = dict(mesh.shape)
    in_specs = (P("tile", "frame", None, None),) + (P(),) * 14
    out_specs = P("tile", "frame", None, None)
    body = functools.partial(shards, sizes["tile"], sizes["frame"])
    return jax.shard_map(body, mesh=mesh, in_specs=in_specs, out_specs=out_specs, check_vma=False)
```

```python
import functools
import math

import jax
import jax.numpy as jnp
from jax import lax
from jax.experimental import pallas as pl
from jax.experimental.pallas import tpu as pltpu
from jax.sharding import PartitionSpec as P

GROUPS = 32
EPSILON = 1e-05
MASKED = -1e30
LOWEST = -5e29
SLOTS = 8
ROWS_OF_TILE = 4
LANES = 128
VMEM_BYTES = 24 * 1024 * 1024
HOLD_VMEM_BYTES = 46 * 1024 * 1024
F32 = jnp.float32
BF16 = jnp.bfloat16

SMEM_SPEC = pl.BlockSpec(memory_space=pltpu.SMEM)
VMEM_SPEC = pl.BlockSpec(memory_space=pltpu.VMEM)
HBM_SPEC = pl.BlockSpec(memory_space=pltpu.HBM)


def cost(microseconds):
    return pl.CostEstimate(
        flops=int(microseconds * 1.1e9), bytes_accessed=0, transcendentals=0
    )


def params():
    return pltpu.CompilerParams(vmem_limit_bytes=VMEM_BYTES)


def member_matrix(channels):
    per_group = channels // GROUPS
    group = lax.broadcasted_iota(jnp.int32, (LANES, channels), 0) * per_group
    channel = lax.broadcasted_iota(jnp.int32, (LANES, channels), 1)
    return jnp.where((channel >= group) & (channel < group + per_group), 1.0, 0.0).astype(BF16)


def thirds(values):
    parts = []
    for _ in range(3):
        parts.append(values.astype(BF16).astype(F32))
        values = values - parts[-1]
    return jnp.concatenate(parts, axis=0).astype(BF16)


def added(products):
    rows = products.shape[0] // 3
    return (products[2 * rows :] + products[rows : 2 * rows]) + products[:rows]


def to_groups(values, member):
    return added(
        lax.dot_general(
            thirds(values), member, (((1,), (1,)), ((), ())), preferred_element_type=F32
        )
    )


def to_channels(values, member):
    return added(jnp.dot(thirds(values), member, preferred_element_type=F32))


class Info:
    def __init__(self, ref, rows):
        self.ref, self.rows = ref, rows
        self.videos = ref.shape[0] - 1 - rows

    def tile(self):
        return self.ref[0]

    def label(self, row):
        inside = (row >= 0) & (row < self.rows)
        return jnp.where(inside, self.ref[1 + jnp.clip(row, 0, self.rows - 1)], -1)

    def width(self, label):
        return jnp.where(label >= 0, self.ref[1 + self.rows + jnp.maximum(label, 0)], 0)

    def window(self, first, count):
        labels = [self.label(first + r) for r in range(count)]
        return labels, [self.width(label) for label in labels]


def pick(table, label, videos):
    chosen = table[0:1]
    for video in range(1, videos):
        chosen = jnp.where(label == video, table[video : video + 1], chosen)
    return chosen


def norm_tables(stats_ref, gain_ref):
    member = member_matrix(gain_ref.shape[1])
    counts = jnp.maximum(stats_ref[0], 1.0)
    scale = lax.rsqrt(stats_ref[2] / counts + EPSILON)
    return to_channels(stats_ref[1], member), to_channels(scale, member) * gain_ref[...]


def write_stats(out_ref, rows, labels, widths, videos, channels):
    member = member_matrix(channels)
    per_group = channels // GROUPS
    cols = rows[0].shape[0]
    slot = lax.broadcasted_iota(jnp.int32, (SLOTS, 1), 0)
    column = lax.broadcasted_iota(jnp.int32, (cols, 1), 0)
    sums = jnp.zeros((SLOTS, channels), F32)
    counts = jnp.zeros((SLOTS, 1), F32)
    for index, row in enumerate(rows):
        sums = jnp.where(slot == index, jnp.sum(row, axis=0, keepdims=True), sums)
        counts = jnp.where(slot == index, (widths[index] * per_group).astype(F32), counts)
    means = to_groups(sums, member) / jnp.maximum(counts, 1.0)
    means_wide = to_channels(means, member)
    squares = jnp.zeros((SLOTS, channels), F32)
    for index, row in enumerate(rows):
        centered = jnp.where(column < widths[index], row - means_wide[index : index + 1], 0.0)
        squares = jnp.where(
            slot == index, jnp.sum(centered * centered, axis=0, keepdims=True), squares
        )
    spreads = to_groups(squares, member)
    out_ref[...] = jnp.zeros(out_ref.shape, F32)
    for video in range(videos):
        total = jnp.zeros((1, LANES), F32)
        count = jnp.zeros((1, LANES), F32)
        for index in range(len(rows)):
            mine = labels[index] == video
            row_count = counts[index : index + 1]
            total = total + jnp.where(mine, means[index : index + 1] * row_count, 0.0)
            count = count + jnp.where(mine, row_count, 0.0)
        mean = total / jnp.maximum(count, 1.0)
        spread = jnp.zeros((1, LANES), F32)
        for index in range(len(rows)):
            off = means[index : index + 1] - mean
            part = spreads[index : index + 1] + counts[index : index + 1] * off * off
            spread = spread + jnp.where(labels[index] == video, part, 0.0)
        out_ref[0, video : video + 1, :] = count
        out_ref[1, video : video + 1, :] = mean
        out_ref[2, video : video + 1, :] = spread


def build_columns(columns_ref, row_refs):
    padded = columns_ref.shape[0] // len(row_refs)
    for index, row in enumerate(row_refs):
        cells = row().astype(F32)
        count, channels = cells.shape
        cells = jnp.concatenate([cells, jnp.zeros((padded - count, channels), F32)], axis=0)
        start = index * padded
        columns_ref[start : start + padded, 0:channels] = pltpu.roll(cells, 1, 0).astype(BF16)
        columns_ref[start : start + padded, channels : 2 * channels] = cells.astype(BF16)
        columns_ref[start : start + padded, 2 * channels : 3 * channels] = pltpu.roll(
            cells, padded - 1, 0
        ).astype(BF16)


def stats_kernel(rows, info_ref, latents_ref, out_ref):
    info = Info(info_ref, rows)
    row_count, cols, channels = latents_ref.shape
    labels, widths = info.window(info.tile() * row_count, row_count)
    column = lax.broadcasted_iota(jnp.int32, (cols, 1), 0)
    cells = [
        jnp.where(column < widths[r], latents_ref[r].astype(F32), 0.0) for r in range(row_count)
    ]
    write_stats(out_ref, cells, labels, widths, info.videos, channels)


def rims(info, outer_ref, inner_ref):
    odd = lax.rem(info.tile(), 2) == 1
    inner, outer = inner_ref[0].astype(F32), outer_ref[0].astype(F32)
    return jnp.where(odd, inner, outer), jnp.where(odd, outer, inner)


def hidden_kernel(
    rows, info_ref, outer_ref, inner_ref, latents_ref, stats_ref, gain_ref, shift_ref, out_ref,
    source_ref,
):
    info = Info(info_ref, rows)
    row_count, cols, _ = latents_ref.shape
    labels, widths = info.window(info.tile() * row_count - 1, row_count + 2)
    means, scales = norm_tables(stats_ref, gain_ref)
    column = lax.broadcasted_iota(jnp.int32, (cols, 1), 0)
    above, below = rims(info, outer_ref, inner_ref)
    sources = [above] + [latents_ref[r].astype(F32) for r in range(row_count)] + [below]
    for r, source in enumerate(sources):
        mean = pick(means, labels[r], info.videos)
        scale = pick(scales, labels[r], info.videos)
        normed = (source - mean) * scale + shift_ref[...]
        active = normed / (1.0 + jnp.exp(-normed))
        active = jnp.where(column < widths[r], active, 0.0)
        rest = jnp.zeros((out_ref.shape[1] - cols, active.shape[1]), F32)
        out_ref[r] = jnp.concatenate([active, rest], axis=0).astype(BF16)
    source_ref[...] = latents_ref[...]


def hold_kernel(backs, weight_ref, held_ref, sems):
    channels = weight_ref.shape[-1]
    copies = [
        pltpu.make_async_copy(
            weight_ref.at[2 - back, tap, side],
            held_ref.at[
                pl.ds((3 * index + tap) * channels, channels), pl.ds(side * channels, channels)
            ],
            sems.at[index, tap, side],
        )
        for index, back in enumerate(backs)
        for tap in range(3)
        for side in range(3)
    ]
    for copy in copies:
        copy.start()
    for copy in copies:
        copy.wait()


def row_taps(info, hidden_refs, inputs_ref):
    near_rows, padded, channels = hidden_refs[0].shape
    row_count = near_rows - 2
    labels, _ = info.window(info.tile() * row_count - 1, near_rows)
    for back, hidden_ref in enumerate(hidden_refs):
        for tap in range(3):
            lanes = slice((3 * back + tap) * channels, (3 * back + tap + 1) * channels)
            for r in range(row_count):
                block = hidden_ref[r + tap]
                if tap != 1:
                    same = labels[r + tap] == labels[r + 1]
                    block = jnp.where(same, block, jnp.zeros_like(block))
                inputs_ref[r * padded : (r + 1) * padded, lanes] = block


def own_conv_kernel(rows, info_ref, hidden_ref, held_ref, product_ref, inputs_ref):
    row_taps(Info(info_ref, rows), [hidden_ref], inputs_ref)
    product_ref[...] = jnp.dot(inputs_ref[...], held_ref[...], preferred_element_type=F32)


def conv_kernel(rows, taps, info_ref, *rest):
    hidden_refs, rest = rest[: taps - 1], rest[taps - 1 :]
    product_ref, latents_ref, bias_ref, *rest = rest
    held_refs, (own_ref, stats_ref, *inputs_refs) = rest[: taps > 1], rest[taps > 1 :]
    row_count, cols, channels = latents_ref.shape
    info = Info(info_ref, rows)
    padded = product_ref.shape[0] // row_count
    labels, widths = info.window(info.tile() * row_count - 1, row_count + 2)
    product = product_ref[...]
    if hidden_refs:
        (inputs_ref,) = inputs_refs
        row_taps(info, hidden_refs, inputs_ref)
        product = product + jnp.dot(
            inputs_ref[...], held_refs[0][...], preferred_element_type=F32
        )
    column = lax.broadcasted_iota(jnp.int32, (cols, 1), 0)
    cells = []
    for r in range(row_count):
        lines = slice(r * padded, (r + 1) * padded)
        branch = pltpu.roll(product[lines, 0:channels], 1, 0)
        branch = branch + product[lines, channels : 2 * channels]
        branch = branch + pltpu.roll(product[lines, 2 * channels :], padded - 1, 0)
        value = latents_ref[r].astype(F32) + branch[:cols] + bias_ref[...]
        value = jnp.where(column < widths[r + 1], value, 0.0).astype(BF16)
        cells.append(value.astype(F32))
    for pair in range(row_count // 2):
        own_ref[pair] = jnp.concatenate(cells[2 * pair : 2 * pair + 2], axis=0).astype(BF16)
    write_stats(stats_ref, cells, labels[1:-1], widths[1:-1], info.videos, channels)


def split_rows(pairs_ref):
    cols = pairs_ref.shape[1] // 2
    cells = []
    for pair in range(pairs_ref.shape[0]):
        both = pairs_ref[pair].astype(F32)
        cells += [both[:cols], both[cols:]]
    return cells


def turned_queries(info, tile, pairs_ref, means, scales, shift_ref, weight_ref, bias_ref):
    pairs, double, channels = pairs_ref.shape
    cols = double // 2
    column = lax.broadcasted_iota(jnp.int32, (cols, 1), 0)
    labels, widths = info.window(tile * 2 * pairs, 2 * pairs)
    cells = []
    for r, values in enumerate(split_rows(pairs_ref)):
        mean = pick(means, labels[r], info.videos)
        scale = pick(scales, labels[r], info.videos)
        normed = (values - mean) * scale + shift_ref[...]
        cells.append(jnp.where(column < widths[r], normed, 0.0))
    cells = jnp.concatenate(cells, axis=0).astype(BF16)
    queries = (
        jnp.dot(cells, weight_ref[:, 0:channels], preferred_element_type=F32)
        + bias_ref[:, 0:channels]
    ).astype(BF16)
    factor = channels ** (-0.5) * math.log2(math.e)
    turned = lax.dot_general(
        queries, weight_ref[:, channels : 2 * channels], (((1,), (1,)), ((), ())),
        preferred_element_type=F32,
    )
    constant = jnp.sum(
        queries.astype(F32) * bias_ref[:, channels : 2 * channels], axis=1, keepdims=True
    )
    return (turned * factor).astype(BF16), constant * factor


def query_kernel(
    rows, info_ref, own_ref, other_ref, stats_ref, gain_ref, shift_ref, weight_ref, bias_ref,
    means_ref, scales_ref, *out_refs,
):
    info = Info(info_ref, rows)
    means, scales = norm_tables(stats_ref, gain_ref)
    means_ref[...] = means
    scales_ref[...] = scales
    for side, (tile, pairs_ref) in enumerate(
        ((info.tile() ^ 1, other_ref), (info.tile(), own_ref))
    ):
        queries, constant = turned_queries(
            info, tile, pairs_ref, means, scales, shift_ref, weight_ref, bias_ref
        )
        queries_ref, constant_ref = out_refs[2 * side : 2 * side + 2]
        queries_ref[...] = queries
        constant_ref[...] = jnp.broadcast_to(constant, constant_ref.shape)


def key_codes(info, masks, span, cols):
    row_count = span // cols
    position = lax.broadcasted_iota(jnp.int32, (1, len(masks) * span), 1)
    codes = jnp.full((1, len(masks) * span), -2.0, F32)
    for index, mask in enumerate(masks):
        near, widths = info.window((info.tile() ^ (2 * mask)) * row_count, row_count)
        for r in range(row_count):
            start = index * span + r * cols
            inside = (position >= start) & (position < start + widths[r])
            codes = jnp.where(inside, near[r].astype(F32), codes)
    return codes


def query_codes(info, tile, span, cols):
    row_count = span // cols
    labels, _ = info.window(tile * row_count, row_count)
    return jnp.concatenate(
        [jnp.zeros((cols, 1), F32) + label.astype(F32) for label in labels], axis=0
    )


def scores_of(queries, keys, codes, query_code):
    scores = lax.dot_general(
        queries, keys, (((1,), (1,)), ((), ())), preferred_element_type=F32
    )
    return jnp.where(codes == query_code, scores, MASKED)


def mean_and_level(peak, denominator, total):
    some = denominator > 0.0
    safe = jnp.where(some, denominator, 1.0)
    return total / safe, jnp.where(some, peak + jnp.log2(safe), LOWEST)


def attend_yours_kernel(rows, masks, first, last, info_ref, *rest):
    means_ref, scales_ref, shift_ref, queries_ref, constant_ref, *rest = rest
    block_refs, rest = rest[: len(masks)], rest[len(masks) :]
    if not first:
        old_peak_ref, old_sum_ref, old_total_ref, *rest = rest
    keys_ref, *out_refs = rest
    info = Info(info_ref, rows)
    span, channels = queries_ref.shape
    pairs, double, _ = block_refs[0].shape
    cols = double // 2
    row_count = 2 * pairs
    tile = info.tile()
    means, scales = means_ref[...], scales_ref[...]
    for index, (mask, block_ref) in enumerate(zip(masks, block_refs)):
        near, _ = info.window((tile ^ (2 * mask)) * row_count, row_count)
        for pair in range(pairs):
            both = block_ref[pair].astype(F32)
            halves = []
            for half in range(2):
                label = near[2 * pair + half]
                mean = pick(means, label, info.videos)
                scale = pick(scales, label, info.videos)
                values = both[half * cols : (half + 1) * cols]
                halves.append((values - mean) * scale + shift_ref[...])
            start = index * span + pair * double
            keys_ref[start : start + double, :] = jnp.concatenate(halves, axis=0).astype(BF16)
    constant = constant_ref[:, 0:1]
    scores = scores_of(
        queries_ref[...], keys_ref[...], key_codes(info, masks, span, cols),
        query_codes(info, tile ^ 1, span, cols),
    )
    peak = jnp.maximum(LOWEST, jnp.max(scores, axis=1, keepdims=True) + constant)
    if not first:
        largest = old_peak_ref[:, 0:1]
        peak = jnp.maximum(largest, peak)
    weights = jnp.exp2(scores - (peak - constant))
    denominator = jnp.sum(weights, axis=1, keepdims=True)
    total = jnp.dot(weights.astype(BF16), keys_ref[...], preferred_element_type=F32)
    if not first:
        factor = jnp.exp2(largest - peak)
        denominator = old_sum_ref[:, 0:1] * factor + denominator
        total = old_total_ref[...] * factor + total
    if not last:
        peak_ref, sum_ref, total_ref = out_refs
        peak_ref[...] = jnp.broadcast_to(peak, peak_ref.shape)
        sum_ref[...] = jnp.broadcast_to(denominator, sum_ref.shape)
        total_ref[...] = total
        return
    (sent_ref,) = out_refs
    mean, level = mean_and_level(peak, denominator, total)
    sent_ref[0:span, :] = mean.astype(BF16)
    slots = sent_ref.shape[0] - span
    slot = lax.broadcasted_iota(jnp.int32, (slots, 1), 0)
    packed = jnp.zeros((slots, LANES), F32)
    for r in range(row_count):
        left = level[r * cols : (r + 1) * cols]
        left = jnp.sum(jnp.where(diagonal(cols), left, 0.0), axis=0, keepdims=True)
        for part in range(3):
            rounded = left.astype(BF16).astype(F32)
            packed = jnp.where(slot == 3 * r + part, rounded, packed)
            left = left - rounded
    sent_ref[span:, 0:LANES] = packed.astype(BF16)
    sent_ref[span:, LANES:] = jnp.zeros((slots, channels - LANES), BF16)


def attend_mine_kernel(
    rows, groups, info_ref, queries_ref, constant_ref, *rest
):
    key_refs, (mean_ref, level_ref) = rest[: len(groups)], rest[len(groups) :]
    info = Info(info_ref, rows)
    span = mean_ref.shape[0]
    queries, constant = queries_ref[...], constant_ref[:, 0:1]
    cols = span // ROWS_OF_TILE
    query_code = query_codes(info, info.tile(), span, cols)
    peak = jnp.full((span, 1), LOWEST, F32)
    scores = []
    for masks, key_ref in zip(groups, key_refs):
        codes = key_codes(info, masks, span, cols)
        scores.append(scores_of(queries, key_ref[...], codes, query_code))
        peak = jnp.maximum(peak, jnp.max(scores[-1], axis=1, keepdims=True) + constant)
    denominator, total = 0.0, 0.0
    for part, key_ref in zip(scores, key_refs):
        weights = jnp.exp2(part - (peak - constant))
        denominator = denominator + jnp.sum(weights, axis=1, keepdims=True)
        total = total + jnp.dot(
            weights.astype(BF16), key_ref[...], preferred_element_type=F32
        )
    mean, level = mean_and_level(peak, denominator, total)
    mean_ref[...] = mean
    level_ref[...] = jnp.broadcast_to(level, level_ref.shape)


def diagonal(cols):
    return lax.broadcasted_iota(jnp.int32, (cols, LANES), 0) == lax.broadcasted_iota(
        jnp.int32, (cols, LANES), 1
    )


def finish_kernel(
    rows, info_ref, mean_ref, level_ref, received_ref, own_ref, triple_ref, triple_bias_ref,
    output_ref, output_bias_ref, out_ref, inner_ref, outer_ref,
):
    info = Info(info_ref, rows)
    row_count, cols, channels = out_ref.shape
    span = row_count * cols
    _, widths = info.window(info.tile() * row_count, row_count)
    received = received_ref[0:span, :].astype(F32)
    levels = received_ref[span:, 0:LANES].astype(F32)
    yours = []
    for r in range(row_count):
        level = levels[3 * r : 3 * r + 1] + levels[3 * r + 1 : 3 * r + 2]
        level = level + levels[3 * r + 2 : 3 * r + 3]
        yours.append(jnp.sum(jnp.where(diagonal(cols), level, 0.0), axis=1, keepdims=True))
    yours = jnp.concatenate(yours, axis=0)
    mine = level_ref[:, 0:1]
    peak = jnp.maximum(mine, yours)
    weight, other_weight = jnp.exp2(mine - peak), jnp.exp2(yours - peak)
    share = weight / (weight + other_weight)
    mean_cell = (mean_ref[...] * share + received * (1.0 - share)).astype(BF16)
    mixed = (
        jnp.dot(mean_cell, triple_ref[:, 2 * channels :], preferred_element_type=F32)
        + triple_bias_ref[:, 2 * channels :]
    ).astype(BF16)
    attended = jnp.dot(mixed, output_ref[...], preferred_element_type=F32) + output_bias_ref[...]
    column = lax.broadcasted_iota(jnp.int32, (cols, 1), 0)
    for r, before in enumerate(split_rows(own_ref)):
        value = before + attended[r * cols : (r + 1) * cols]
        value = jnp.where(column < widths[r], value, 0.0)
        out_ref[r] = value.astype(BF16)
        if r == 0:
            top = value
    odd = lax.rem(info.tile(), 2) == 1
    inner_ref[0] = jnp.where(odd, top, value).astype(BF16)
    outer_ref[0] = jnp.where(odd, value, top).astype(BF16)


def fold_kernel(weight_ref, out_ref):
    channels = weight_ref.shape[-1]
    wide = [[weight_ref[a, b].astype(F32) for b in range(3)] for a in range(3)]

    def both(upper, lower):
        return [x + y for x, y in zip(upper, lower)]

    phases = [[wide[0], both(wide[1], wide[2])], [both(wide[0], wide[1]), wide[2]]]
    for down in range(2):
        for tap in range(2):
            left, middle, right = phases[down][tap]
            out_ref[down, tap, 0, :, 0:channels] = left.astype(BF16)
            out_ref[down, tap, 0, :, channels:] = (middle + right).astype(BF16)
            out_ref[down, tap, 1, :, 0:channels] = (left + middle).astype(BF16)
            out_ref[down, tap, 1, :, channels:] = right.astype(BF16)


def spread_columns(wide_ref, value, row, right):
    cols, channels = value.shape
    for part in range(wide_ref.shape[0]):
        lo, hi = part * LANES, min((part + 1) * LANES, channels)
        piece = value[:, lo:hi]
        if hi - lo < LANES:
            piece = jnp.concatenate([piece, jnp.zeros((cols, LANES - hi + lo), F32)], axis=1)
        wide_ref[part, row, pl.ds(right, cols, 2), :] = piece


def write_turned(out_ref, row, part, value, width):
    channels, cols = out_ref.shape[1:]
    lo, hi = part * LANES, min((part + 1) * LANES, channels)
    turned = value.T[0 : hi - lo, 0:cols]
    column = lax.broadcasted_iota(jnp.int32, (1, cols), 1)
    out_ref[row, lo:hi, :] = jnp.where(column < width, turned, 0.0).astype(BF16)


def phase_product(columns, weight):
    return lax.dot_general(
        columns, weight, (((1,), (1,)), ((), ())), preferred_element_type=F32
    )


def upsample_kernel(
    rows, info_ref, own_ref, weight_ref, bias_ref, out_ref, open_ref, columns_ref, wide_ref
):
    info = Info(info_ref, rows)
    row_count, cols, channels = own_ref.shape
    padded = columns_ref.shape[0] // row_count
    parts_out = wide_ref.shape[0]
    labels, widths = info.window(info.tile() * row_count, row_count)
    build_columns(
        columns_ref, [functools.partial(own_ref.__getitem__, r) for r in range(row_count)]
    )
    inner_rows = (row_count - 1) * padded
    for down in range(2):
        for right in range(2):
            lanes = slice(right * channels, (right + 2) * channels)
            same = phase_product(columns_ref[:, lanes], weight_ref[down, 1 - down, right])
            start = down * padded
            rim = phase_product(
                columns_ref[start : start + inner_rows, lanes], weight_ref[down, down, right]
            )
            for r in range(row_count):
                value = same[r * padded : r * padded + cols]
                near = r - 1 + 2 * down
                if 0 <= near < row_count:
                    lo = (near - down) * padded
                    value = value + jnp.where(
                        labels[near] == labels[r], rim[lo : lo + cols], 0.0
                    )
                spread_columns(wide_ref, value, 2 * r + down, right)
    for part in range(parts_out):
        open_ref[part, 0] = wide_ref[part, 0]
        open_ref[part, 1] = wide_ref[part, 2 * row_count - 1]
    for r in range(1, 2 * row_count - 1):
        for part in range(parts_out):
            value = wide_ref[part, r] + bias_ref[:, part * LANES : (part + 1) * LANES]
            write_turned(out_ref, r - 1, part, value, 2 * widths[r // 2])


def close_kernel(
    rows, info_ref, outer_ref, inner_ref, middle_ref, open_ref, weight_ref, bias_ref, out_ref,
    columns_ref, wide_ref,
):
    info = Info(info_ref, rows)
    wide_rows, _, wide_cols = out_ref.shape
    row_count, cols = wide_rows // 2, wide_cols // 2
    channels = outer_ref.shape[-1]
    padded = columns_ref.shape[0] // 2
    labels, widths = info.window(info.tile() * row_count - 1, row_count + 2)
    above, below = rims(info, outer_ref, inner_ref)
    build_columns(columns_ref, [lambda: above, lambda: below])
    for down in range(2):
        for right in range(2):
            lanes = slice(right * channels, (right + 2) * channels)
            rim = phase_product(
                columns_ref[down * padded : (down + 1) * padded, lanes],
                weight_ref[down, down, right],
            )
            spread_columns(wide_ref, rim[:cols], down, right)
    out_ref[1 : wide_rows - 1] = middle_ref[...]
    for down in range(2):
        rim_row, own_row = (row_count + 1, row_count) if down else (0, 1)
        for part in range(wide_ref.shape[0]):
            rim = jnp.where(labels[rim_row] == labels[own_row], wide_ref[part, down], 0.0)
            value = open_ref[part, down] + rim + bias_ref[:, part * LANES : (part + 1) * LANES]
            write_turned(
                out_ref, down * (wide_rows - 1), part, value, 2 * widths[own_row]
            )


def merge_stats(mine, other):
    count = mine[0] + other[0]
    safe = jnp.maximum(count, 1.0)
    off = other[1] - mine[1]
    mean = mine[1] + off * (other[0] / safe)
    spread = mine[2] + other[2] + off * off * (mine[0] * other[0] / safe)
    return jnp.stack([count, mean, spread])


def exchange(array, tiles, mask, among=None):
    moves = [(i, i ^ mask) for i in range(tiles) if among is None or among(i)]
    return lax.ppermute(array, "tile", moves)


def merge_round(stats, tiles, masks, tied=(), after=None):
    parts = [stats] + [exchange(stats, tiles, mask) for mask in masks]
    free = ()
    if tied:
        *parts[2:], free = lax.optimization_barrier((*parts[2:], after))
        parts[1], *tied = lax.optimization_barrier((parts[1], *tied))
    while len(parts) > 1:
        parts = [merge_stats(*parts[i : i + 2]) for i in range(0, len(parts), 2)]
    return (parts[0], *tied, free) if tied else parts[0]


def merge_masks(tiles):
    bits = [1 << i for i in range(tiles.bit_length() - 1)]
    pairs = [bits[i : i + 2] for i in range(0, len(bits), 2)]
    return [[p[0], p[1], p[0] ^ p[1]] if len(p) == 2 else p for p in pairs]


def shards(
    tiles,
    frames,
    latents,
    row_video,
    video_cols,
    first_gain,
    first_shift,
    conv_weight,
    conv_bias,
    second_gain,
    second_shift,
    triple_weight,
    triple_bias,
    output_weight,
    output_bias,
    upsample_weight,
    upsample_bias,
):
    row_count, frame_count, cols, channels = latents.shape
    assert frame_count == 1 and row_count == ROWS_OF_TILE and tiles % 4 == 0
    out_channels = upsample_weight.shape[-1]
    rows = row_count * tiles
    cells = row_count * cols
    padded = -(-(cols + 1) // 16) * 16
    near_rows = row_count + 2
    source = latents.reshape(row_count, cols, channels)
    tile = lax.axis_index("tile").astype(jnp.int32)
    info = jnp.concatenate([jnp.reshape(tile, (1,)), row_video, video_cols])

    def row(vector):
        return vector.reshape(1, -1)

    def shape(*dims, dtype=BF16):
        return jax.ShapeDtypeStruct(dims, dtype)

    def call(kernel, operands, out_shape, scratch=(), **kwargs):
        many = isinstance(out_shape, tuple)
        return pl.pallas_call(
            kernel,
            out_shape=out_shape,
            in_specs=[SMEM_SPEC] + [VMEM_SPEC] * len(operands),
            out_specs=(VMEM_SPEC,) * len(out_shape) if many else VMEM_SPEC,
            scratch_shapes=list(scratch),
            compiler_params=params(),
            **kwargs,
        )(info, *operands)

    outer_moves = [(i, i - 1 if i % 2 == 0 else i + 1) for i in range(tiles)]
    outer_moves = [(i, j) for i, j in outer_moves if 0 <= j < tiles]
    odd = tile % 2 == 1
    stats_shape = shape(3, SLOTS, LANES, dtype=F32)
    stats = call(
        functools.partial(stats_kernel, rows), [source], stats_shape,
        cost_estimate=cost(1.5), name="first_stats",
    )
    outer = lax.ppermute(
        jnp.where(odd, source[row_count - 1 :], source[:1]), "tile", outer_moves
    )
    inner = exchange(jnp.where(odd, source[:1], source[row_count - 1 :]), tiles, 1)
    stats, outer, inner = lax.optimization_barrier((stats, outer, inner))
    taps = min(3, frames)
    held = [
        pl.pallas_call(
            functools.partial(hold_kernel, backs),
            out_shape=shape(3 * len(backs) * channels, 3 * channels),
            in_specs=[HBM_SPEC],
            out_specs=VMEM_SPEC,
            scratch_shapes=[pltpu.SemaphoreType.DMA((len(backs), 3, 3))],
            compiler_params=pltpu.CompilerParams(vmem_limit_bytes=HOLD_VMEM_BYTES),
            cost_estimate=cost(1.5 * len(backs)),
            name="hold",
        )(conv_weight)
        for backs in ((0,), tuple(range(1, taps)))
        if backs
    ]
    rounds = merge_masks(tiles)
    for index, masks in enumerate(reversed(rounds)):
        stats = merge_round(stats, tiles, masks)
        if index < len(held):
            stats, held[index] = lax.optimization_barrier((stats, held[index]))
    hidden, source = call(
        functools.partial(hidden_kernel, rows),
        [outer, inner, source, stats, row(first_gain), row(first_shift)],
        (shape(near_rows, padded, channels), shape(row_count, cols, channels)),
        cost_estimate=cost(1.3),
        name="hidden",
    )

    earlier = [
        lax.ppermute(hidden, "frame", [(i, i + by) for i in range(frames - by)])
        for by in range(1, taps)
    ]
    pairs = row_count // 2
    pair_shape = shape(pairs, 2 * cols, channels)
    product = call(
        functools.partial(own_conv_kernel, rows),
        [hidden, held[0]],
        shape(row_count * padded, 3 * channels, dtype=F32),
        scratch=[pltpu.VMEM((row_count * padded, 3 * channels), BF16)],
        cost_estimate=cost(2.2),
        name="own_conv",
    )
    scratch = [pltpu.VMEM((row_count * padded, 3 * (taps - 1) * channels), BF16)]
    own, stats = call(
        functools.partial(conv_kernel, rows, taps),
        earlier + [product, source, row(conv_bias)] + held[1:],
        (pair_shape, stats_shape),
        scratch=scratch if taps > 1 else [],
        cost_estimate=cost(1.5 + 2.0 * (taps - 1)),
        name="conv",
    )

    blocks = {0: own}
    neighbour = [(i, i ^ 1) for i in range(tiles)]
    if tiles == 16 and video_cols.shape[0] == 2:
        def middle(t):
            return t // 4 in (1, 2)

        stats = merge_round(stats, tiles, rounds[1])
        blocks[2] = exchange(own, tiles, 4)
        blocks[6] = exchange(own, tiles, 12, middle)
        stats, blocks[2], blocks[6], own_xy = merge_round(
            stats, tiles, rounds[0], (blocks[2], blocks[6]), own
        )
        inward = exchange(blocks[2], tiles, 12, middle)
        outward = exchange(blocks[6], tiles, 4, middle)
        own_x, stats = lax.optimization_barrier((own, stats))
        other = exchange(own_x, tiles, 1)
        blocks[1] = exchange(own_xy, tiles, 2)
        blocks[4] = jnp.where((tile // 4 == 1) | (tile // 4 == 2), inward, outward)
        passed, blocks[4] = lax.optimization_barrier((blocks[1], blocks[4]))
        blocks[5] = exchange(blocks[4], tiles, 2)
        blocks[3] = exchange(passed, tiles, 4)
        blocks[7] = exchange(passed, tiles, 12, middle)
        groups = [[0, 1, 2, 6, 4], [7, 3, 5]]
    else:
        for masks in rounds:
            stats = merge_round(stats, tiles, masks)
        other = exchange(own, tiles, 1)
        for mask in range(1, tiles // 2):
            blocks[mask] = exchange(own, tiles, 2 * mask)
        groups = [list(range(i, i + 4)) for i in range(0, tiles // 2, 4)]
    gain, shift = row(second_gain), row(second_shift)
    table_shape = shape(SLOTS, channels, dtype=F32)
    query_shapes = (shape(cells, channels), shape(cells, LANES, dtype=F32))
    means, scales, queries, constant, mine_queries, mine_constant = call(
        functools.partial(query_kernel, rows),
        [own, other, stats, gain, shift, triple_weight, row(triple_bias)],
        (table_shape, table_shape) + query_shapes * 2,
        cost_estimate=cost(1.9),
        name="queries",
    )
    level_shape = shape(cells, LANES, dtype=F32)
    total_shape = shape(cells, channels, dtype=F32)
    state, keys = (), []
    for index, masks in enumerate(groups):
        last = index == len(groups) - 1
        outs = (shape(len(masks) * cells, channels),)
        outs += (shape(cells + 16, channels),) if last else (level_shape, level_shape, total_shape)
        normed, *state = call(
            functools.partial(attend_yours_kernel, rows, tuple(masks), index == 0, last),
            [means, scales, shift, queries, constant] + [blocks[m] for m in masks] + list(state),
            outs,
            cost_estimate=cost(0.9 * len(masks)),
            name="attend_yours",
        )
        keys.append(normed)
    (sent,) = state
    received = lax.ppermute(sent, "tile", neighbour)
    sent, mine_queries = lax.optimization_barrier((sent, mine_queries))
    mean, level = call(
        functools.partial(attend_mine_kernel, rows, tuple(tuple(masks) for masks in groups)),
        [mine_queries, mine_constant] + keys,
        (total_shape, level_shape),
        cost_estimate=cost(6.0),
        name="attend_mine",
    )
    rim_shape = shape(1, cols, channels)
    attended, inner, outer = call(
        functools.partial(finish_kernel, rows),
        [
            mean, level, received, own, triple_weight, row(triple_bias), output_weight,
            row(output_bias),
        ],
        (shape(row_count, cols, channels), rim_shape, rim_shape),
        cost_estimate=cost(1.4),
        name="finish",
    )
    outer = lax.ppermute(outer, "tile", outer_moves)
    inner = exchange(inner, tiles, 1)
    attended, upsample_weight = lax.optimization_barrier((attended, upsample_weight))
    folded = pl.pallas_call(
        fold_kernel,
        out_shape=shape(2, 2, 2, out_channels, 2 * channels),
        in_specs=[VMEM_SPEC],
        out_specs=VMEM_SPEC,
        compiler_params=params(),
        cost_estimate=cost(0.1),
        name="fold",
    )(jnp.swapaxes(upsample_weight, 2, 3))
    parts_out = -(-out_channels // LANES)
    wide_cols = -(-2 * cols // LANES) * LANES
    wide_bias = jnp.pad(row(upsample_bias), ((0, 0), (0, -out_channels % LANES)))
    middle, open_rows = call(
        functools.partial(upsample_kernel, rows),
        [attended, folded, wide_bias],
        (
            shape(2 * row_count - 2, out_channels, 2 * cols),
            shape(parts_out, 2, wide_cols, LANES, dtype=F32),
        ),
        scratch=[
            pltpu.VMEM((row_count * padded, 3 * channels), BF16),
            pltpu.VMEM((parts_out, 2 * row_count, wide_cols, LANES), F32),
        ],
        cost_estimate=cost(0.2),
        name="upsample",
    )
    decoded = call(
        functools.partial(close_kernel, rows),
        [outer, inner, middle, open_rows, folded, wide_bias],
        shape(2 * row_count, out_channels, 2 * cols),
        scratch=[
            pltpu.VMEM((2 * padded, 3 * channels), BF16),
            pltpu.VMEM((parts_out, 2, wide_cols, LANES), F32),
        ],
        cost_estimate=cost(1.0),
        name="close",
    )
    return jnp.swapaxes(decoded, 1, 2).reshape(2 * row_count, 1, 2 * cols, out_channels)


def solution(mesh):
    sizes = dict(mesh.shape)
    in_specs = (P("tile", "frame", None, None),) + (P(),) * 14
    out_specs = P("tile", "frame", None, None)
    body = functools.partial(shards, sizes["tile"], sizes["frame"])
    return jax.shard_map(body, mesh=mesh, in_specs=in_specs, out_specs=out_specs, check_vma=False)
```

```python
import functools
import math

import jax
import jax.numpy as jnp
from jax import lax
from jax.experimental import pallas as pl
from jax.experimental.pallas import tpu as pltpu
from jax.sharding import PartitionSpec as P

GROUPS = 32
EPSILON = 1e-05
MASKED = -1e30
LOWEST = -5e29
SLOTS = 8
ROWS_OF_TILE = 4
LANES = 128
VMEM_BYTES = 24 * 1024 * 1024
HOLD_VMEM_BYTES = 46 * 1024 * 1024
F32 = jnp.float32
BF16 = jnp.bfloat16

SMEM_SPEC = pl.BlockSpec(memory_space=pltpu.SMEM)
VMEM_SPEC = pl.BlockSpec(memory_space=pltpu.VMEM)
HBM_SPEC = pl.BlockSpec(memory_space=pltpu.HBM)


def cost(microseconds):
    return pl.CostEstimate(
        flops=int(microseconds * 1.1e9), bytes_accessed=0, transcendentals=0
    )


def params():
    return pltpu.CompilerParams(vmem_limit_bytes=VMEM_BYTES)


def member_matrix(channels):
    per_group = channels // GROUPS
    group = lax.broadcasted_iota(jnp.int32, (LANES, channels), 0) * per_group
    channel = lax.broadcasted_iota(jnp.int32, (LANES, channels), 1)
    return jnp.where((channel >= group) & (channel < group + per_group), 1.0, 0.0).astype(BF16)


def thirds(values):
    parts = []
    for _ in range(3):
        parts.append(values.astype(BF16).astype(F32))
        values = values - parts[-1]
    return jnp.concatenate(parts, axis=0).astype(BF16)


def added(products):
    rows = products.shape[0] // 3
    return (products[2 * rows :] + products[rows : 2 * rows]) + products[:rows]


def to_groups(values, member):
    return added(
        lax.dot_general(
            thirds(values), member, (((1,), (1,)), ((), ())), preferred_element_type=F32
        )
    )


def to_channels(values, member):
    return added(jnp.dot(thirds(values), member, preferred_element_type=F32))


class Info:
    def __init__(self, ref, rows):
        self.ref, self.rows = ref, rows
        self.videos = ref.shape[0] - 1 - rows

    def tile(self):
        return self.ref[0]

    def label(self, row):
        inside = (row >= 0) & (row < self.rows)
        return jnp.where(inside, self.ref[1 + jnp.clip(row, 0, self.rows - 1)], -1)

    def width(self, label):
        return jnp.where(label >= 0, self.ref[1 + self.rows + jnp.maximum(label, 0)], 0)

    def window(self, first, count):
        labels = [self.label(first + r) for r in range(count)]
        return labels, [self.width(label) for label in labels]


def pick(table, label, videos):
    chosen = table[0:1]
    for video in range(1, videos):
        chosen = jnp.where(label == video, table[video : video + 1], chosen)
    return chosen


def norm_tables(stats_ref, gain_ref):
    member = member_matrix(gain_ref.shape[1])
    counts = jnp.maximum(stats_ref[0], 1.0)
    scale = lax.rsqrt(stats_ref[2] / counts + EPSILON)
    return to_channels(stats_ref[1], member), to_channels(scale, member) * gain_ref[...]


def write_stats(out_ref, rows, labels, widths, videos, channels):
    member = member_matrix(channels)
    per_group = channels // GROUPS
    cols = rows[0].shape[0]
    slot = lax.broadcasted_iota(jnp.int32, (SLOTS, 1), 0)
    column = lax.broadcasted_iota(jnp.int32, (cols, 1), 0)
    sums = jnp.zeros((SLOTS, channels), F32)
    counts = jnp.zeros((SLOTS, 1), F32)
    for index, row in enumerate(rows):
        sums = jnp.where(slot == index, jnp.sum(row, axis=0, keepdims=True), sums)
        counts = jnp.where(slot == index, (widths[index] * per_group).astype(F32), counts)
    means = to_groups(sums, member) / jnp.maximum(counts, 1.0)
    means_wide = to_channels(means, member)
    squares = jnp.zeros((SLOTS, channels), F32)
    for index, row in enumerate(rows):
        centered = jnp.where(column < widths[index], row - means_wide[index : index + 1], 0.0)
        squares = jnp.where(
            slot == index, jnp.sum(centered * centered, axis=0, keepdims=True), squares
        )
    spreads = to_groups(squares, member)
    out_ref[...] = jnp.zeros(out_ref.shape, F32)
    for video in range(videos):
        total = jnp.zeros((1, LANES), F32)
        count = jnp.zeros((1, LANES), F32)
        for index in range(len(rows)):
            mine = labels[index] == video
            row_count = counts[index : index + 1]
            total = total + jnp.where(mine, means[index : index + 1] * row_count, 0.0)
            count = count + jnp.where(mine, row_count, 0.0)
        mean = total / jnp.maximum(count, 1.0)
        spread = jnp.zeros((1, LANES), F32)
        for index in range(len(rows)):
            off = means[index : index + 1] - mean
            part = spreads[index : index + 1] + counts[index : index + 1] * off * off
            spread = spread + jnp.where(labels[index] == video, part, 0.0)
        out_ref[0, video : video + 1, :] = count
        out_ref[1, video : video + 1, :] = mean
        out_ref[2, video : video + 1, :] = spread


def build_columns(columns_ref, row_refs):
    padded = columns_ref.shape[0] // len(row_refs)
    for index, row in enumerate(row_refs):
        cells = row().astype(F32)
        count, channels = cells.shape
        cells = jnp.concatenate([cells, jnp.zeros((padded - count, channels), F32)], axis=0)
        start = index * padded
        columns_ref[start : start + padded, 0:channels] = pltpu.roll(cells, 1, 0).astype(BF16)
        columns_ref[start : start + padded, channels : 2 * channels] = cells.astype(BF16)
        columns_ref[start : start + padded, 2 * channels : 3 * channels] = pltpu.roll(
            cells, padded - 1, 0
        ).astype(BF16)


def stats_kernel(rows, info_ref, latents_ref, out_ref):
    info = Info(info_ref, rows)
    row_count, cols, channels = latents_ref.shape
    labels, widths = info.window(info.tile() * row_count, row_count)
    column = lax.broadcasted_iota(jnp.int32, (cols, 1), 0)
    cells = [
        jnp.where(column < widths[r], latents_ref[r].astype(F32), 0.0) for r in range(row_count)
    ]
    write_stats(out_ref, cells, labels, widths, info.videos, channels)


def rims(info, outer_ref, inner_ref):
    odd = lax.rem(info.tile(), 2) == 1
    inner, outer = inner_ref[0].astype(F32), outer_ref[0].astype(F32)
    return jnp.where(odd, inner, outer), jnp.where(odd, outer, inner)


def hidden_kernel(
    rows, info_ref, outer_ref, inner_ref, latents_ref, stats_ref, gain_ref, shift_ref, out_ref,
    source_ref,
):
    info = Info(info_ref, rows)
    row_count, cols, _ = latents_ref.shape
    labels, widths = info.window(info.tile() * row_count - 1, row_count + 2)
    means, scales = norm_tables(stats_ref, gain_ref)
    column = lax.broadcasted_iota(jnp.int32, (cols, 1), 0)
    above, below = rims(info, outer_ref, inner_ref)
    sources = [above] + [latents_ref[r].astype(F32) for r in range(row_count)] + [below]
    for r, source in enumerate(sources):
        mean = pick(means, labels[r], info.videos)
        scale = pick(scales, labels[r], info.videos)
        normed = (source - mean) * scale + shift_ref[...]
        active = normed / (1.0 + jnp.exp(-normed))
        active = jnp.where(column < widths[r], active, 0.0)
        rest = jnp.zeros((out_ref.shape[1] - cols, active.shape[1]), F32)
        out_ref[r] = jnp.concatenate([active, rest], axis=0).astype(BF16)
    source_ref[...] = latents_ref[...]


def hold_kernel(backs, weight_ref, held_ref, sems):
    channels = weight_ref.shape[-1]
    copies = [
        pltpu.make_async_copy(
            weight_ref.at[2 - back, tap, side],
            held_ref.at[
                pl.ds((3 * index + tap) * channels, channels), pl.ds(side * channels, channels)
            ],
            sems.at[index, tap, side],
        )
        for index, back in enumerate(backs)
        for tap in range(3)
        for side in range(3)
    ]
    for copy in copies:
        copy.start()
    for copy in copies:
        copy.wait()


def row_taps(info, hidden_refs, inputs_ref):
    near_rows, padded, channels = hidden_refs[0].shape
    row_count = near_rows - 2
    labels, _ = info.window(info.tile() * row_count - 1, near_rows)
    for back, hidden_ref in enumerate(hidden_refs):
        for tap in range(3):
            lanes = slice((3 * back + tap) * channels, (3 * back + tap + 1) * channels)
            for r in range(row_count):
                block = hidden_ref[r + tap]
                if tap != 1:
                    same = labels[r + tap] == labels[r + 1]
                    block = jnp.where(same, block, jnp.zeros_like(block))
                inputs_ref[r * padded : (r + 1) * padded, lanes] = block


def own_conv_kernel(rows, info_ref, hidden_ref, held_ref, product_ref, inputs_ref):
    row_taps(Info(info_ref, rows), [hidden_ref], inputs_ref)
    product_ref[...] = jnp.dot(inputs_ref[...], held_ref[...], preferred_element_type=F32)


def conv_kernel(rows, taps, info_ref, *rest):
    hidden_refs, rest = rest[: taps - 1], rest[taps - 1 :]
    product_ref, latents_ref, bias_ref, *rest = rest
    held_refs, (own_ref, stats_ref, *inputs_refs) = rest[: taps > 1], rest[taps > 1 :]
    row_count, cols, channels = latents_ref.shape
    info = Info(info_ref, rows)
    padded = product_ref.shape[0] // row_count
    labels, widths = info.window(info.tile() * row_count - 1, row_count + 2)
    product = product_ref[...]
    if hidden_refs:
        (inputs_ref,) = inputs_refs
        row_taps(info, hidden_refs, inputs_ref)
        product = product + jnp.dot(
            inputs_ref[...], held_refs[0][...], preferred_element_type=F32
        )
    column = lax.broadcasted_iota(jnp.int32, (cols, 1), 0)
    cells = []
    for r in range(row_count):
        lines = slice(r * padded, (r + 1) * padded)
        branch = pltpu.roll(product[lines, 0:channels], 1, 0)
        branch = branch + product[lines, channels : 2 * channels]
        branch = branch + pltpu.roll(product[lines, 2 * channels :], padded - 1, 0)
        value = latents_ref[r].astype(F32) + branch[:cols] + bias_ref[...]
        value = jnp.where(column < widths[r + 1], value, 0.0).astype(BF16)
        cells.append(value.astype(F32))
    for pair in range(row_count // 2):
        own_ref[pair] = jnp.concatenate(cells[2 * pair : 2 * pair + 2], axis=0).astype(BF16)
    write_stats(stats_ref, cells, labels[1:-1], widths[1:-1], info.videos, channels)


def split_rows(pairs_ref):
    cols = pairs_ref.shape[1] // 2
    cells = []
    for pair in range(pairs_ref.shape[0]):
        both = pairs_ref[pair].astype(F32)
        cells += [both[:cols], both[cols:]]
    return cells


def turned_queries(info, tile, pairs_ref, means, scales, shift_ref, weight_ref, bias_ref):
    pairs, double, channels = pairs_ref.shape
    cols = double // 2
    column = lax.broadcasted_iota(jnp.int32, (cols, 1), 0)
    labels, widths = info.window(tile * 2 * pairs, 2 * pairs)
    cells = []
    for r, values in enumerate(split_rows(pairs_ref)):
        mean = pick(means, labels[r], info.videos)
        scale = pick(scales, labels[r], info.videos)
        normed = (values - mean) * scale + shift_ref[...]
        cells.append(jnp.where(column < widths[r], normed, 0.0))
    cells = jnp.concatenate(cells, axis=0).astype(BF16)
    queries = (
        jnp.dot(cells, weight_ref[:, 0:channels], preferred_element_type=F32)
        + bias_ref[:, 0:channels]
    ).astype(BF16)
    factor = channels ** (-0.5) * math.log2(math.e)
    turned = lax.dot_general(
        queries, weight_ref[:, channels : 2 * channels], (((1,), (1,)), ((), ())),
        preferred_element_type=F32,
    )
    constant = jnp.sum(
        queries.astype(F32) * bias_ref[:, channels : 2 * channels], axis=1, keepdims=True
    )
    return (turned * factor).astype(BF16), constant * factor


def query_kernel(
    rows, info_ref, own_ref, other_ref, stats_ref, gain_ref, shift_ref, weight_ref, bias_ref,
    means_ref, scales_ref, *out_refs,
):
    info = Info(info_ref, rows)
    means, scales = norm_tables(stats_ref, gain_ref)
    means_ref[...] = means
    scales_ref[...] = scales
    for side, (tile, pairs_ref) in enumerate(
        ((info.tile() ^ 1, other_ref), (info.tile(), own_ref))
    ):
        queries, constant = turned_queries(
            info, tile, pairs_ref, means, scales, shift_ref, weight_ref, bias_ref
        )
        queries_ref, constant_ref = out_refs[2 * side : 2 * side + 2]
        queries_ref[...] = queries
        constant_ref[...] = jnp.broadcast_to(constant, constant_ref.shape)


def key_codes(info, masks, span, cols):
    row_count = span // cols
    position = lax.broadcasted_iota(jnp.int32, (1, len(masks) * span), 1)
    codes = jnp.full((1, len(masks) * span), -2.0, F32)
    for index, mask in enumerate(masks):
        near, widths = info.window((info.tile() ^ (2 * mask)) * row_count, row_count)
        for r in range(row_count):
            start = index * span + r * cols
            inside = (position >= start) & (position < start + widths[r])
            codes = jnp.where(inside, near[r].astype(F32), codes)
    return codes


def query_codes(info, tile, span, cols):
    row_count = span // cols
    labels, _ = info.window(tile * row_count, row_count)
    return jnp.concatenate(
        [jnp.zeros((cols, 1), F32) + label.astype(F32) for label in labels], axis=0
    )


def scores_of(queries, keys, codes, query_code):
    scores = lax.dot_general(
        queries, keys, (((1,), (1,)), ((), ())), preferred_element_type=F32
    )
    return jnp.where(codes == query_code, scores, MASKED)


def mean_and_level(peak, denominator, total):
    some = denominator > 0.0
    safe = jnp.where(some, denominator, 1.0)
    return total / safe, jnp.where(some, peak + jnp.log2(safe), LOWEST)


def attend_yours_kernel(rows, masks, first, last, info_ref, *rest):
    means_ref, scales_ref, shift_ref, queries_ref, constant_ref, *rest = rest
    block_refs, rest = rest[: len(masks)], rest[len(masks) :]
    if not first:
        old_peak_ref, old_sum_ref, old_total_ref, *rest = rest
    keys_ref, *out_refs = rest
    info = Info(info_ref, rows)
    span, channels = queries_ref.shape
    pairs, double, _ = block_refs[0].shape
    cols = double // 2
    row_count = 2 * pairs
    tile = info.tile()
    means, scales = means_ref[...], scales_ref[...]
    for index, (mask, block_ref) in enumerate(zip(masks, block_refs)):
        near, _ = info.window((tile ^ (2 * mask)) * row_count, row_count)
        for pair in range(pairs):
            both = block_ref[pair].astype(F32)
            halves = []
            for half in range(2):
                label = near[2 * pair + half]
                mean = pick(means, label, info.videos)
                scale = pick(scales, label, info.videos)
                values = both[half * cols : (half + 1) * cols]
                halves.append((values - mean) * scale + shift_ref[...])
            start = index * span + pair * double
            keys_ref[start : start + double, :] = jnp.concatenate(halves, axis=0).astype(BF16)
    constant = constant_ref[:, 0:1]
    scores = scores_of(
        queries_ref[...], keys_ref[...], key_codes(info, masks, span, cols),
        query_codes(info, tile ^ 1, span, cols),
    )
    peak = jnp.maximum(LOWEST, jnp.max(scores, axis=1, keepdims=True) + constant)
    if not first:
        largest = old_peak_ref[:, 0:1]
        peak = jnp.maximum(largest, peak)
    weights = jnp.exp2(scores - (peak - constant))
    denominator = jnp.sum(weights, axis=1, keepdims=True)
    total = jnp.dot(weights.astype(BF16), keys_ref[...], preferred_element_type=F32)
    if not first:
        factor = jnp.exp2(largest - peak)
        denominator = old_sum_ref[:, 0:1] * factor + denominator
        total = old_total_ref[...] * factor + total
    if not last:
        peak_ref, sum_ref, total_ref = out_refs
        peak_ref[...] = jnp.broadcast_to(peak, peak_ref.shape)
        sum_ref[...] = jnp.broadcast_to(denominator, sum_ref.shape)
        total_ref[...] = total
        return
    (sent_ref,) = out_refs
    mean, level = mean_and_level(peak, denominator, total)
    sent_ref[0:span, :] = mean.astype(BF16)
    slots = sent_ref.shape[0] - span
    slot = lax.broadcasted_iota(jnp.int32, (slots, 1), 0)
    packed = jnp.zeros((slots, LANES), F32)
    for r in range(row_count):
        left = level[r * cols : (r + 1) * cols]
        left = jnp.sum(jnp.where(diagonal(cols), left, 0.0), axis=0, keepdims=True)
        for part in range(3):
            rounded = left.astype(BF16).astype(F32)
            packed = jnp.where(slot == 3 * r + part, rounded, packed)
            left = left - rounded
    sent_ref[span:, 0:LANES] = packed.astype(BF16)
    sent_ref[span:, LANES:] = jnp.zeros((slots, channels - LANES), BF16)


def attend_mine_kernel(
    rows, groups, info_ref, queries_ref, constant_ref, *rest
):
    key_refs, (mean_ref, level_ref) = rest[: len(groups)], rest[len(groups) :]
    info = Info(info_ref, rows)
    span = mean_ref.shape[0]
    queries, constant = queries_ref[...], constant_ref[:, 0:1]
    cols = span // ROWS_OF_TILE
    query_code = query_codes(info, info.tile(), span, cols)
    peak = jnp.full((span, 1), LOWEST, F32)
    scores = []
    for masks, key_ref in zip(groups, key_refs):
        codes = key_codes(info, masks, span, cols)
        scores.append(scores_of(queries, key_ref[...], codes, query_code))
        peak = jnp.maximum(peak, jnp.max(scores[-1], axis=1, keepdims=True) + constant)
    denominator, total = 0.0, 0.0
    for part, key_ref in zip(scores, key_refs):
        weights = jnp.exp2(part - (peak - constant))
        denominator = denominator + jnp.sum(weights, axis=1, keepdims=True)
        total = total + jnp.dot(
            weights.astype(BF16), key_ref[...], preferred_element_type=F32
        )
    mean, level = mean_and_level(peak, denominator, total)
    mean_ref[...] = mean
    level_ref[...] = jnp.broadcast_to(level, level_ref.shape)


def diagonal(cols):
    return lax.broadcasted_iota(jnp.int32, (cols, LANES), 0) == lax.broadcasted_iota(
        jnp.int32, (cols, LANES), 1
    )


def finish_kernel(
    rows, info_ref, mean_ref, level_ref, received_ref, own_ref, triple_ref, triple_bias_ref,
    output_ref, output_bias_ref, out_ref, inner_ref, outer_ref,
):
    info = Info(info_ref, rows)
    row_count, cols, channels = out_ref.shape
    span = row_count * cols
    _, widths = info.window(info.tile() * row_count, row_count)
    received = received_ref[0:span, :].astype(F32)
    levels = received_ref[span:, 0:LANES].astype(F32)
    yours = []
    for r in range(row_count):
        level = levels[3 * r : 3 * r + 1] + levels[3 * r + 1 : 3 * r + 2]
        level = level + levels[3 * r + 2 : 3 * r + 3]
        yours.append(jnp.sum(jnp.where(diagonal(cols), level, 0.0), axis=1, keepdims=True))
    yours = jnp.concatenate(yours, axis=0)
    mine = level_ref[:, 0:1]
    peak = jnp.maximum(mine, yours)
    weight, other_weight = jnp.exp2(mine - peak), jnp.exp2(yours - peak)
    share = weight / (weight + other_weight)
    mean_cell = (mean_ref[...] * share + received * (1.0 - share)).astype(BF16)
    mixed = (
        jnp.dot(mean_cell, triple_ref[:, 2 * channels :], preferred_element_type=F32)
        + triple_bias_ref[:, 2 * channels :]
    ).astype(BF16)
    attended = jnp.dot(mixed, output_ref[...], preferred_element_type=F32) + output_bias_ref[...]
    column = lax.broadcasted_iota(jnp.int32, (cols, 1), 0)
    for r, before in enumerate(split_rows(own_ref)):
        value = before + attended[r * cols : (r + 1) * cols]
        value = jnp.where(column < widths[r], value, 0.0)
        out_ref[r] = value.astype(BF16)
        if r == 0:
            top = value
    odd = lax.rem(info.tile(), 2) == 1
    inner_ref[0] = jnp.where(odd, top, value).astype(BF16)
    outer_ref[0] = jnp.where(odd, value, top).astype(BF16)


def fold_kernel(weight_ref, out_ref):
    channels = weight_ref.shape[-1]
    wide = [[weight_ref[a, b].astype(F32) for b in range(3)] for a in range(3)]

    def both(upper, lower):
        return [x + y for x, y in zip(upper, lower)]

    phases = [[wide[0], both(wide[1], wide[2])], [both(wide[0], wide[1]), wide[2]]]
    for down in range(2):
        for tap in range(2):
            left, middle, right = phases[down][tap]
            out_ref[down, tap, 0, :, 0:channels] = left.astype(BF16)
            out_ref[down, tap, 0, :, channels:] = (middle + right).astype(BF16)
            out_ref[down, tap, 1, :, 0:channels] = (left + middle).astype(BF16)
            out_ref[down, tap, 1, :, channels:] = right.astype(BF16)


def spread_columns(wide_ref, value, row, right):
    cols, channels = value.shape
    for part in range(wide_ref.shape[0]):
        lo, hi = part * LANES, min((part + 1) * LANES, channels)
        piece = value[:, lo:hi]
        if hi - lo < LANES:
            piece = jnp.concatenate([piece, jnp.zeros((cols, LANES - hi + lo), F32)], axis=1)
        wide_ref[part, row, pl.ds(right, cols, 2), :] = piece


def write_turned(out_ref, row, part, value, width):
    channels, cols = out_ref.shape[1:]
    lo, hi = part * LANES, min((part + 1) * LANES, channels)
    turned = value.T[0 : hi - lo, 0:cols]
    column = lax.broadcasted_iota(jnp.int32, (1, cols), 1)
    out_ref[row, lo:hi, :] = jnp.where(column < width, turned, 0.0).astype(BF16)


def phase_product(columns, weight):
    return lax.dot_general(
        columns, weight, (((1,), (1,)), ((), ())), preferred_element_type=F32
    )


def upsample_kernel(
    rows, info_ref, own_ref, weight_ref, bias_ref, out_ref, open_ref, columns_ref, wide_ref,
    turned_ref, sem,
):
    info = Info(info_ref, rows)
    row_count, cols, channels = own_ref.shape
    padded = columns_ref.shape[0] // row_count
    parts_out = wide_ref.shape[0]
    labels, widths = info.window(info.tile() * row_count, row_count)
    build_columns(
        columns_ref, [functools.partial(own_ref.__getitem__, r) for r in range(row_count)]
    )
    inner_rows = (row_count - 1) * padded
    for down in range(2):
        for right in range(2):
            lanes = slice(right * channels, (right + 2) * channels)
            same = phase_product(columns_ref[:, lanes], weight_ref[down, 1 - down, right])
            start = down * padded
            rim = phase_product(
                columns_ref[start : start + inner_rows, lanes], weight_ref[down, down, right]
            )
            for r in range(row_count):
                value = same[r * padded : r * padded + cols]
                near = r - 1 + 2 * down
                if 0 <= near < row_count:
                    lo = (near - down) * padded
                    value = value + jnp.where(
                        labels[near] == labels[r], rim[lo : lo + cols], 0.0
                    )
                spread_columns(wide_ref, value, 2 * r + down, right)
    for part in range(parts_out):
        open_ref[part, 0] = wide_ref[part, 0]
        open_ref[part, 1] = wide_ref[part, 2 * row_count - 1]
    for r in range(1, 2 * row_count - 1):
        for part in range(parts_out):
            value = wide_ref[part, r] + bias_ref[:, part * LANES : (part + 1) * LANES]
            write_turned(turned_ref, r - 1, part, value, 2 * widths[r // 2])
    copy = pltpu.make_async_copy(turned_ref, out_ref.at[pl.ds(1, 2 * row_count - 2)], sem)
    copy.start()
    copy.wait()


def close_kernel(
    rows, info_ref, outer_ref, inner_ref, _, open_ref, weight_ref, bias_ref, out_ref, columns_ref,
    wide_ref, turned_ref, sems,
):
    info = Info(info_ref, rows)
    wide_rows, _, wide_cols = out_ref.shape
    row_count, cols = wide_rows // 2, wide_cols // 2
    channels = outer_ref.shape[-1]
    padded = columns_ref.shape[0] // 2
    labels, widths = info.window(info.tile() * row_count - 1, row_count + 2)
    above, below = rims(info, outer_ref, inner_ref)
    build_columns(columns_ref, [lambda: above, lambda: below])
    for down in range(2):
        for right in range(2):
            lanes = slice(right * channels, (right + 2) * channels)
            rim = phase_product(
                columns_ref[down * padded : (down + 1) * padded, lanes],
                weight_ref[down, down, right],
            )
            spread_columns(wide_ref, rim[:cols], down, right)
    copies = []
    for down in range(2):
        rim_row, own_row = (row_count + 1, row_count) if down else (0, 1)
        for part in range(wide_ref.shape[0]):
            rim = jnp.where(labels[rim_row] == labels[own_row], wide_ref[part, down], 0.0)
            value = open_ref[part, down] + rim + bias_ref[:, part * LANES : (part + 1) * LANES]
            write_turned(turned_ref, down, part, value, 2 * widths[own_row])
        copies.append(
            pltpu.make_async_copy(
                turned_ref.at[down], out_ref.at[down * (wide_rows - 1)], sems.at[down]
            )
        )
        copies[-1].start()
    for copy in copies:
        copy.wait()


def merge_stats(mine, other):
    count = mine[0] + other[0]
    safe = jnp.maximum(count, 1.0)
    off = other[1] - mine[1]
    mean = mine[1] + off * (other[0] / safe)
    spread = mine[2] + other[2] + off * off * (mine[0] * other[0] / safe)
    return jnp.stack([count, mean, spread])


def exchange(array, tiles, mask, among=None):
    moves = [(i, i ^ mask) for i in range(tiles) if among is None or among(i)]
    return lax.ppermute(array, "tile", moves)


def merge_round(stats, tiles, masks, tied=(), after=None):
    parts = [stats] + [exchange(stats, tiles, mask) for mask in masks]
    free = ()
    if tied:
        *parts[2:], free = lax.optimization_barrier((*parts[2:], after))
        parts[1], *tied = lax.optimization_barrier((parts[1], *tied))
    while len(parts) > 1:
        parts = [merge_stats(*parts[i : i + 2]) for i in range(0, len(parts), 2)]
    return (parts[0], *tied, free) if tied else parts[0]


def merge_masks(tiles):
    bits = [1 << i for i in range(tiles.bit_length() - 1)]
    pairs = [bits[i : i + 2] for i in range(0, len(bits), 2)]
    return [[p[0], p[1], p[0] ^ p[1]] if len(p) == 2 else p for p in pairs]


def shards(
    tiles,
    frames,
    latents,
    row_video,
    video_cols,
    first_gain,
    first_shift,
    conv_weight,
    conv_bias,
    second_gain,
    second_shift,
    triple_weight,
    triple_bias,
    output_weight,
    output_bias,
    upsample_weight,
    upsample_bias,
):
    row_count, frame_count, cols, channels = latents.shape
    assert frame_count == 1 and row_count == ROWS_OF_TILE and tiles % 4 == 0
    out_channels = upsample_weight.shape[-1]
    rows = row_count * tiles
    cells = row_count * cols
    padded = -(-(cols + 1) // 16) * 16
    near_rows = row_count + 2
    source = latents.reshape(row_count, cols, channels)
    tile = lax.axis_index("tile").astype(jnp.int32)
    info = jnp.concatenate([jnp.reshape(tile, (1,)), row_video, video_cols])

    def row(vector):
        return vector.reshape(1, -1)

    def shape(*dims, dtype=BF16):
        return jax.ShapeDtypeStruct(dims, dtype)

    def call(kernel, operands, out_shape, scratch=(), **kwargs):
        many = isinstance(out_shape, tuple)
        return pl.pallas_call(
            kernel,
            out_shape=out_shape,
            in_specs=[SMEM_SPEC] + [VMEM_SPEC] * len(operands),
            out_specs=(VMEM_SPEC,) * len(out_shape) if many else VMEM_SPEC,
            scratch_shapes=list(scratch),
            compiler_params=params(),
            **kwargs,
        )(info, *operands)

    outer_moves = [(i, i - 1 if i % 2 == 0 else i + 1) for i in range(tiles)]
    outer_moves = [(i, j) for i, j in outer_moves if 0 <= j < tiles]
    odd = tile % 2 == 1
    stats_shape = shape(3, SLOTS, LANES, dtype=F32)
    stats = call(
        functools.partial(stats_kernel, rows), [source], stats_shape,
        cost_estimate=cost(1.5), name="first_stats",
    )
    outer = lax.ppermute(
        jnp.where(odd, source[row_count - 1 :], source[:1]), "tile", outer_moves
    )
    inner = exchange(jnp.where(odd, source[:1], source[row_count - 1 :]), tiles, 1)
    stats, outer, inner = lax.optimization_barrier((stats, outer, inner))
    taps = min(3, frames)
    held = [
        pl.pallas_call(
            functools.partial(hold_kernel, backs),
            out_shape=shape(3 * len(backs) * channels, 3 * channels),
            in_specs=[HBM_SPEC],
            out_specs=VMEM_SPEC,
            scratch_shapes=[pltpu.SemaphoreType.DMA((len(backs), 3, 3))],
            compiler_params=pltpu.CompilerParams(vmem_limit_bytes=HOLD_VMEM_BYTES),
            cost_estimate=cost(1.5 * len(backs)),
            name="hold",
        )(conv_weight)
        for backs in ((0,), tuple(range(1, taps)))
        if backs
    ]
    rounds = merge_masks(tiles)
    for index, masks in enumerate(reversed(rounds)):
        stats = merge_round(stats, tiles, masks)
        if index < len(held):
            stats, held[index] = lax.optimization_barrier((stats, held[index]))
    hidden, source = call(
        functools.partial(hidden_kernel, rows),
        [outer, inner, source, stats, row(first_gain), row(first_shift)],
        (shape(near_rows, padded, channels), shape(row_count, cols, channels)),
        cost_estimate=cost(1.3),
        name="hidden",
    )

    earlier = [
        lax.ppermute(hidden, "frame", [(i, i + by) for i in range(frames - by)])
        for by in range(1, taps)
    ]
    pairs = row_count // 2
    pair_shape = shape(pairs, 2 * cols, channels)
    product = call(
        functools.partial(own_conv_kernel, rows),
        [hidden, held[0]],
        shape(row_count * padded, 3 * channels, dtype=F32),
        scratch=[pltpu.VMEM((row_count * padded, 3 * channels), BF16)],
        cost_estimate=cost(2.2),
        name="own_conv",
    )
    scratch = [pltpu.VMEM((row_count * padded, 3 * (taps - 1) * channels), BF16)]
    own, stats = call(
        functools.partial(conv_kernel, rows, taps),
        earlier + [product, source, row(conv_bias)] + held[1:],
        (pair_shape, stats_shape),
        scratch=scratch if taps > 1 else [],
        cost_estimate=cost(1.5 + 2.0 * (taps - 1)),
        name="conv",
    )

    blocks = {0: own}
    neighbour = [(i, i ^ 1) for i in range(tiles)]
    if tiles == 16 and video_cols.shape[0] == 2:
        def middle(t):
            return t // 4 in (1, 2)

        stats = merge_round(stats, tiles, rounds[1])
        blocks[2] = exchange(own, tiles, 4)
        blocks[6] = exchange(own, tiles, 12, middle)
        stats, blocks[2], blocks[6], own_xy = merge_round(
            stats, tiles, rounds[0], (blocks[2], blocks[6]), own
        )
        inward = exchange(blocks[2], tiles, 12, middle)
        outward = exchange(blocks[6], tiles, 4, middle)
        own_x, stats = lax.optimization_barrier((own, stats))
        other = exchange(own_x, tiles, 1)
        blocks[1] = exchange(own_xy, tiles, 2)
        blocks[4] = jnp.where((tile // 4 == 1) | (tile // 4 == 2), inward, outward)
        passed, blocks[4] = lax.optimization_barrier((blocks[1], blocks[4]))
        blocks[5] = exchange(blocks[4], tiles, 2)
        blocks[3] = exchange(passed, tiles, 4)
        blocks[7] = exchange(passed, tiles, 12, middle)
        groups = [[0, 1, 2, 6, 4], [7, 3, 5]]
    else:
        for masks in rounds:
            stats = merge_round(stats, tiles, masks)
        other = exchange(own, tiles, 1)
        for mask in range(1, tiles // 2):
            blocks[mask] = exchange(own, tiles, 2 * mask)
        groups = [list(range(i, i + 4)) for i in range(0, tiles // 2, 4)]
    gain, shift = row(second_gain), row(second_shift)
    table_shape = shape(SLOTS, channels, dtype=F32)
    query_shapes = (shape(cells, channels), shape(cells, LANES, dtype=F32))
    means, scales, queries, constant, mine_queries, mine_constant = call(
        functools.partial(query_kernel, rows),
        [own, other, stats, gain, shift, triple_weight, row(triple_bias)],
        (table_shape, table_shape) + query_shapes * 2,
        cost_estimate=cost(1.9),
        name="queries",
    )
    level_shape = shape(cells, LANES, dtype=F32)
    total_shape = shape(cells, channels, dtype=F32)
    state, keys = (), []
    for index, masks in enumerate(groups):
        last = index == len(groups) - 1
        outs = (shape(len(masks) * cells, channels),)
        outs += (shape(cells + 16, channels),) if last else (level_shape, level_shape, total_shape)
        normed, *state = call(
            functools.partial(attend_yours_kernel, rows, tuple(masks), index == 0, last),
            [means, scales, shift, queries, constant] + [blocks[m] for m in masks] + list(state),
            outs,
            cost_estimate=cost(0.9 * len(masks)),
            name="attend_yours",
        )
        keys.append(normed)
    (sent,) = state
    received = lax.ppermute(sent, "tile", neighbour)
    sent, mine_queries = lax.optimization_barrier((sent, mine_queries))
    mean, level = call(
        functools.partial(attend_mine_kernel, rows, tuple(tuple(masks) for masks in groups)),
        [mine_queries, mine_constant] + keys,
        (total_shape, level_shape),
        cost_estimate=cost(6.0),
        name="attend_mine",
    )
    rim_shape = shape(1, cols, channels)
    attended, inner, outer = call(
        functools.partial(finish_kernel, rows),
        [
            mean, level, received, own, triple_weight, row(triple_bias), output_weight,
            row(output_bias),
        ],
        (shape(row_count, cols, channels), rim_shape, rim_shape),
        cost_estimate=cost(1.4),
        name="finish",
    )
    outer = lax.ppermute(outer, "tile", outer_moves)
    inner = exchange(inner, tiles, 1)
    attended, upsample_weight = lax.optimization_barrier((attended, upsample_weight))
    folded = pl.pallas_call(
        fold_kernel,
        out_shape=shape(2, 2, 2, out_channels, 2 * channels),
        in_specs=[VMEM_SPEC],
        out_specs=VMEM_SPEC,
        compiler_params=params(),
        cost_estimate=cost(0.1),
        name="fold",
    )(jnp.swapaxes(upsample_weight, 2, 3))
    parts_out = -(-out_channels // LANES)
    wide_cols = -(-2 * cols // LANES) * LANES
    wide_bias = jnp.pad(row(upsample_bias), ((0, 0), (0, -out_channels % LANES)))
    out_shape = shape(2 * row_count, out_channels, 2 * cols)
    open_shape = shape(parts_out, 2, wide_cols, LANES, dtype=F32)
    decoded, open_rows = pl.pallas_call(
        functools.partial(upsample_kernel, rows),
        out_shape=(out_shape, open_shape),
        in_specs=[SMEM_SPEC] + [VMEM_SPEC] * 3,
        out_specs=(HBM_SPEC, VMEM_SPEC),
        scratch_shapes=[
            pltpu.VMEM((row_count * padded, 3 * channels), BF16),
            pltpu.VMEM((parts_out, 2 * row_count, wide_cols, LANES), F32),
            pltpu.VMEM((2 * row_count - 2, out_channels, 2 * cols), BF16),
            pltpu.SemaphoreType.DMA,
        ],
        compiler_params=params(),
        cost_estimate=cost(0.2),
        name="upsample",
    )(info, attended, folded, wide_bias)
    decoded = pl.pallas_call(
        functools.partial(close_kernel, rows),
        out_shape=out_shape,
        in_specs=[SMEM_SPEC] + [VMEM_SPEC] * 2 + [HBM_SPEC] + [VMEM_SPEC] * 3,
        out_specs=HBM_SPEC,
        scratch_shapes=[
            pltpu.VMEM((2 * padded, 3 * channels), BF16),
            pltpu.VMEM((parts_out, 2, wide_cols, LANES), F32),
            pltpu.VMEM((2, out_channels, 2 * cols), BF16),
            pltpu.SemaphoreType.DMA((2,)),
        ],
        input_output_aliases={3: 0},
        compiler_params=params(),
        cost_estimate=cost(1.0),
        name="close",
    )(info, outer, inner, decoded, open_rows, folded, wide_bias)
    return jnp.swapaxes(decoded, 1, 2).reshape(2 * row_count, 1, 2 * cols, out_channels)


def solution(mesh):
    sizes = dict(mesh.shape)
    in_specs = (P("tile", "frame", None, None),) + (P(),) * 14
    out_specs = P("tile", "frame", None, None)
    body = functools.partial(shards, sizes["tile"], sizes["frame"])
    return jax.shard_map(body, mesh=mesh, in_specs=in_specs, out_specs=out_specs, check_vma=False)
```
